32 devices in a mesh: dp: 4 (over y, x), expert: 8 (over z, core).
Axes of the slice: x: 2, y: 2, z: 4, core: 2. Of those that a mesh axis runs over, the one named last changes fastest.
Arguments:
- inputs: bfloat16 [2, 4, 1536, 2048], P(None, 'dp', 'expert'), may hold values from -6 to 6
- cotangent: bfloat16 [2, 4, 1536, 2048], P(None, 'dp', 'expert'), may hold values from -6 to 6
- membership: int32 [2, 4, 1536], P(None, 'dp'), may hold values from 0 to 8, as said below
- routes: int32 [2, 4, 1536, 8], P(None, 'dp', 'expert'), may hold values from 0 to 15, all different within a row
- gate_weights: float32 [2, 4, 1536, 8], P(None, 'dp', 'expert'), may hold values from 0.06 to 0.19
- pair_order: int32 [2, 4, 8, 1536], P(None, 'dp', 'expert'), may hold values from 0 to 1535, each once within a row
- w_query: bfloat16 [2048, 4096], P(None, ('dp', 'expert')), may hold values from -0.125 to 0.125
- w_key: bfloat16 [2048, 512], P(None, ('dp', 'expert')), may hold values from -0.125 to 0.125
- w_value: bfloat16 [2048, 512], P(None, ('dp', 'expert')), may hold values from -0.125 to 0.125
- w_output: bfloat16 [4096, 2048], P(('dp', 'expert')), may hold values from -0.5 to 0.5
- norm_gains: bfloat16 [4352], P(('dp', 'expert')), may hold values from 0.5 to 1.5
- w_gate: bfloat16 [16, 2048, 768], P('expert', 'dp'), may hold values from -0.125 to 0.125
- w_up: bfloat16 [16, 2048, 768], P('expert', 'dp'), may hold values from -0.125 to 0.125
- w_down: bfloat16 [16, 768, 2048], P('expert', None, 'dp'), may hold values from -0.625 to 0.625
Outputs:
- output: bfloat16 [2, 4, 1536, 2048], P(None, 'dp', 'expert')
- input_grad: float32 [2, 4, 1536, 2048], P(None, 'dp', 'expert')
- grad_query: float32 [2048, 4096], P(None, ('dp', 'expert'))
- grad_key: float32 [2048, 512], P(None, ('dp', 'expert'))
- grad_value: float32 [2048, 512], P(None, ('dp', 'expert'))
- grad_output: float32 [4096, 2048], P(('dp', 'expert'))
- grad_gains: float32 [4352], P(('dp', 'expert'))
- grad_gate: float32 [16, 2048, 768], P('expert', 'dp')
- grad_up: float32 [16, 2048, 768], P('expert', 'dp')
- grad_down: float32 [16, 768, 2048], P('expert', None, 'dp')
The draws below stay inside these ranges and needn't reach their ends.
Inputs may be any that keep to these rules, and one draw needn't show every extreme that they name: `membership`: the first 1024 tokens of each group are its prompt (0); then continuations 1 to 8 follow in order, each of half to three halves of 64 tokens, together 8 * 64 tokens. `routes`: each token names 8 different experts. `pair_order`: within each block of 192 tokens the 1536 pairs carry each priority once.
All inputs are finite; a program needn't handle non-finite values.
Results may differ from the reference program's by a relative error of at most 0.019.
Values may be sent and summed in bfloat16 or wider, within the bound.
A program may use at most 384 MiB of HBM per device.

```python
import jax
import jax.numpy as jnp
from jax import lax

D = 2048
H = 32
KVH = 4
HD = 128
FF = 768
TOPK = 8
CONTS = 8
PROMPT = 1024
MICRO = 2
CONT_LEN = 64
EXPERTS = 16
GROUPS = 4
GROUP_TOK = 1536
PAIRS = 1536
CAP = 96
GAIN_LEN = 4352
N_EXPERT = 8


def draw_membership(key, part):
    key = jax.random.fold_in(key, 11)
    half_len = CONT_LEN // 2
    shifts = jax.random.randint(key, (MICRO, GROUPS, CONTS // 2), -half_len, half_len + 1)
    lengths = jnp.stack([CONT_LEN + shifts, CONT_LEN - shifts], axis=-1).reshape(MICRO, GROUPS, CONTS)
    bounds = PROMPT + jnp.cumsum(lengths, axis=-1)
    index = jnp.arange(GROUP_TOK, dtype=jnp.int32)
    passed = jnp.sum((index[None, None, :, None] >= bounds[:, :, None, :]).astype(jnp.int32), axis=-1)
    return jnp.where(index[None, None, :] < PROMPT, 0, 1 + passed).astype(jnp.int32)


def block_levels(own_key, shape, cuts, least, top_value):
    factor_of, own = 1.0, jax.random.fold_in(own_key, 6)
    for axis_at, blocks in cuts:
        draws = jnp.exp(jax.random.uniform(jax.random.fold_in(own, axis_at), (blocks,), jnp.float32, least / len(cuts), top_value / len(cuts)))
        factor_of = factor_of * jnp.repeat(draws, shape[axis_at] // blocks).reshape([-1 if axis == axis_at else 1 for axis in range(len(shape))])
    return factor_of


def choose_distinct(stream_key, rows, number_of, top, lift):
    sequence = jax.random.permutation(jax.random.fold_in(stream_key, 1), number_of)
    favour = sequence
    for power in range(3):
        favour = favour * favour // number_of
    favour = favour * lift // number_of
    lots = jax.random.randint(jax.random.fold_in(stream_key, 2), (rows, number_of), 0, 4096) + favour
    holders = jax.random.permutation(jax.random.fold_in(stream_key, 3), rows)[jnp.arange(number_of) % rows]
    lots = jnp.where(jnp.arange(rows)[:, None] == holders[None, :], 1 << 14, lots)
    priority = lots * number_of + jnp.arange(number_of)
    return lax.top_k(priority.astype(jnp.int32), top)[1].astype(jnp.int32)


def centred(own_key, shape, scale, reach, pieces=(), kind=jnp.bfloat16):
    values = scale * jax.random.normal(own_key, shape, jnp.float32)
    if pieces:
        values = values * block_levels(own_key, shape, pieces, -0.22, 0.18)
    return jnp.clip(values, -reach, reach).astype(kind)


def setup_inputs(seed: int = 0) -> dict:
    arg_keys = jax.random.split(jax.random.key(seed), 15)
    inputs = centred(arg_keys[0], (MICRO, GROUPS, GROUP_TOK, D), 1.0, 6.0, ((1, 4), (2, 8)))
    cotangent = centred(arg_keys[1], (MICRO, GROUPS, GROUP_TOK, D), 1.0, 6.0, ((1, 4), (2, 8)))
    membership = draw_membership(jax.random.fold_in(arg_keys[14], 71), 0)
    routes = choose_distinct(arg_keys[3], MICRO * GROUPS * GROUP_TOK, EXPERTS, TOPK, 4096).reshape((MICRO, GROUPS, GROUP_TOK, TOPK))
    gate_weights = jnp.clip(0.06 + 0.13 * jax.random.uniform(arg_keys[4], (MICRO, GROUPS, GROUP_TOK, TOPK), jnp.float32) ** block_levels(arg_keys[4], (MICRO, GROUPS, GROUP_TOK, TOPK), ((1, 4), (2, 8)), -0.2, 0.2), 0.06, 0.19)
    pair_order = jax.vmap(lambda own: jax.random.permutation(own, PAIRS))(jax.random.split(arg_keys[5], MICRO * GROUPS * N_EXPERT)).reshape((MICRO, GROUPS, N_EXPERT, PAIRS)).astype(jnp.int32)
    w_query = centred(arg_keys[6], (D, H * HD), D ** -0.5, 0.125, ((1, 32),))
    w_key = centred(arg_keys[7], (D, KVH * HD), D ** -0.5, 0.125, ((1, 32),))
    w_value = centred(arg_keys[8], (D, KVH * HD), D ** -0.5, 0.125, ((1, 32),))
    w_output = centred(arg_keys[9], (H * HD, D), (H * HD // 32) ** -0.5, 0.5, ((0, 32),))
    norm_gains = jnp.clip(1.0 + 0.1 * jax.random.normal(arg_keys[10], (GAIN_LEN,), jnp.float32), 0.5, 1.5).astype(jnp.bfloat16)
    w_gate = centred(arg_keys[11], (EXPERTS, D, FF), D ** -0.5, 0.125, ((0, 8), (1, 4)))
    w_up = centred(arg_keys[12], (EXPERTS, D, FF), D ** -0.5, 0.125, ((0, 8), (1, 4)))
    w_down = centred(arg_keys[13], (EXPERTS, FF, D), (FF // 8) ** -0.5, 0.625, ((0, 8), (2, 4)))
    return {"inputs": inputs, "cotangent": cotangent, "membership": membership, "routes": routes, "gate_weights": gate_weights, "pair_order": pair_order, "w_query": w_query, "w_key": w_key, "w_value": w_value, "w_output": w_output, "norm_gains": norm_gains, "w_gate": w_gate, "w_up": w_up, "w_down": w_down}


EPSILON = 1e-06
ROPE_BASE = 1000000.0
MASKED = -1e+30
HIGHEST = lax.Precision.HIGHEST

@jax.custom_vjp
def low(v):
    return lax.optimization_barrier(v.astype(jnp.bfloat16)).astype(jnp.float32)

@jax.custom_vjp
def low_back(v):
    return v

def low_keep(v):
    return (low(v), None)

def low_pass(kept, grad):
    return (grad,)

def back_keep(v):
    return (v, None)

def back_low(kept, grad):
    return (low(grad),)
low.defvjp(low_keep, low_pass)
low_back.defvjp(back_keep, back_low)

def rms_norm(values, norm_gain):
    return values * lax.rsqrt(lax.optimization_barrier(jnp.mean(values * values, axis=-1, keepdims=True)) + EPSILON) * norm_gain

def rotate(values, cosine, sine_part):
    half_dim = values.shape[-1] // 2
    first_half = values[..., :half_dim]
    second_half = values[..., half_dim:]
    return jnp.concatenate([first_half * cosine - second_half * sine_part, second_half * cosine + first_half * sine_part], axis=-1)

def layout(segment):
    index = jnp.arange(GROUP_TOK, dtype=jnp.int32)
    before = lax.optimization_barrier(jnp.sum((segment[None, :] < segment[:, None]).astype(jnp.int32), axis=1))
    position = jnp.where(segment == 0, index, PROMPT + index - before)
    allowed = (index[None, :] <= index[:, None]) & ((segment[None, :] == 0) | (segment[None, :] == segment[:, None]))
    return (position, allowed)

def attend_head(query_h, key_h, value_h, allowed):
    scores = jnp.einsum('tgd,sd->tgs', query_h, key_h, precision=HIGHEST) * HD ** (-0.5)
    scores = low_back(scores)
    scores = jnp.where(allowed[:, None, :], scores, MASKED)
    row_max = lax.optimization_barrier(jnp.max(scores, axis=-1, keepdims=True))
    scaled = jnp.exp(scores - row_max)
    attn_prob = low(scaled / lax.optimization_barrier(jnp.sum(scaled, axis=-1, keepdims=True)))
    return jnp.einsum('tgs,sd->tgd', attn_prob, value_h, precision=HIGHEST)

def assign(route_ids, gate_vals, ranking):
    pair_experts = route_ids.reshape(N_EXPERT, PAIRS)

    def slots(experts_row, ranks_row):
        earlier = (experts_row[None, :] == experts_row[:, None]) & (ranks_row[None, :] < ranks_row[:, None])
        return lax.optimization_barrier(jnp.sum(earlier.astype(jnp.int32), axis=1))
    slot_of = jax.vmap(slots)(pair_experts, ranking)
    kept_pair = slot_of < CAP
    local_col = pair_experts * CAP + slot_of
    block_base = jnp.arange(N_EXPERT, dtype=jnp.int32)[:, None] * (EXPERTS * CAP)
    flat_ids = jnp.where(kept_pair, block_base + local_col, N_EXPERT * EXPERTS * CAP).reshape(-1)
    pick_ids = (block_base + jnp.minimum(local_col, EXPERTS * CAP - 1)).reshape(-1)
    pair_weight = gate_vals * kept_pair.reshape(GROUP_TOK, TOPK).astype(jnp.float32)
    return (flat_ids, pick_ids, pair_weight)

def layer(params, hidden, segment, flat_ids, pick_ids, pair_weight):
    w_query, w_key, w_value, w_output, norm_gains, w_gate, w_up, w_down = params
    gain_in = norm_gains[:D]
    gain_mid = norm_gains[D:2 * D]
    gain_q = norm_gains[2 * D:2 * D + HD]
    gain_k = norm_gains[2 * D + HD:]
    position, allowed = layout(segment)
    frequency = ROPE_BASE ** (-(jnp.arange(HD // 2, dtype=jnp.float32) * 2.0 / HD))
    angles = position.astype(jnp.float32)[:, None] * frequency[None, :]
    cosine = jnp.cos(angles)[:, None, :]
    sine_part = jnp.sin(angles)[:, None, :]
    normed = low(rms_norm(hidden, gain_in))
    queries = low_back(jnp.dot(normed, w_query, precision=HIGHEST)).reshape(GROUP_TOK, H, HD)
    keys_pre = low_back(jnp.dot(normed, w_key, precision=HIGHEST)).reshape(GROUP_TOK, KVH, HD)
    values = low(low_back(jnp.dot(normed, w_value, precision=HIGHEST))).reshape(GROUP_TOK, KVH, HD)
    queries = low(low_back(rotate(rms_norm(queries, gain_q), cosine, sine_part)))
    keys = low(low_back(rotate(rms_norm(keys_pre, gain_k), cosine, sine_part)))
    q_heads = jnp.transpose(queries.reshape(GROUP_TOK, KVH, H // KVH, HD), (1, 0, 2, 3))
    k_heads = jnp.transpose(keys, (1, 0, 2))
    v_heads = jnp.transpose(values, (1, 0, 2))

    def head_fn(operands):
        return attend_head(operands[0], operands[1], operands[2], allowed)
    mixed_heads = lax.map(jax.checkpoint(head_fn), (q_heads, k_heads, v_heads))
    mixed_heads = jnp.transpose(mixed_heads, (1, 0, 2, 3)).reshape(GROUP_TOK, H * HD)
    mixed_heads = low(low_back(mixed_heads))
    branch = low_back(jnp.dot(mixed_heads, w_output, precision=HIGHEST))
    middle = hidden + branch
    routed = low(rms_norm(middle, gain_mid))
    pair_rows = jnp.repeat(routed, TOPK, axis=0)
    buffer_rows = jax.ops.segment_sum(pair_rows, flat_ids, num_segments=N_EXPERT * EXPERTS * CAP + 1)[:-1]
    buffer_rows = buffer_rows.reshape(N_EXPERT, EXPERTS, CAP, D).transpose(1, 0, 2, 3).reshape(EXPERTS, N_EXPERT * CAP, D)
    buffer_rows = low_back(buffer_rows)
    gate_pre = low_back(jnp.einsum('erd,edf->erf', buffer_rows, w_gate, precision=HIGHEST))
    up_pre = low_back(jnp.einsum('erd,edf->erf', buffer_rows, w_up, precision=HIGHEST))
    hidden_low = low(jax.nn.silu(gate_pre) * up_pre)
    result = low(low_back(jnp.einsum('erf,efd->erd', hidden_low, w_down, precision=HIGHEST)))
    result = result.reshape(EXPERTS, N_EXPERT, CAP, D).transpose(1, 0, 2, 3).reshape(N_EXPERT * EXPERTS * CAP, D)
    picked = jnp.take(result, pick_ids, axis=0).reshape(GROUP_TOK, TOPK, D)
    expert_mix = lax.optimization_barrier(jnp.sum(picked * pair_weight[:, :, None], axis=1))
    return middle + expert_mix

def reference(inputs, cotangent, membership, routes, gate_weights, pair_order, w_query, w_key, w_value, w_output, norm_gains, w_gate, w_up, w_down):
    params = tuple((weight.astype(jnp.float32) for weight in (w_query, w_key, w_value, w_output, norm_gains, w_gate, w_up, w_down)))
    group_count = MICRO * GROUPS

    def flatten(array):
        return array.reshape((group_count,) + array.shape[2:])
    stacked = (flatten(inputs), flatten(cotangent), flatten(membership), flatten(routes), flatten(gate_weights), flatten(pair_order))

    def one_group(totals, item_data):
        hidden, cot_rows, segment, route_ids, gate_vals, ranking = item_data
        flat_ids, pick_ids, pair_weight = assign(route_ids, gate_vals, ranking)

        def group_fn(param_set, hidden_rows):
            return layer(param_set, hidden_rows, segment, flat_ids, pick_ids, pair_weight)
        result, pullback = jax.vjp(group_fn, params, hidden.astype(jnp.float32))
        grad_params, grad_hidden = pullback(cot_rows.astype(jnp.float32))
        totals = jax.tree.map(jnp.add, totals, grad_params)
        return (totals, (result.astype(jnp.bfloat16), grad_hidden))
    zeros = tuple((jnp.zeros_like(param) for param in params))
    totals, (results, grads) = lax.scan(one_group, zeros, stacked)
    full_shape = (MICRO, GROUPS, GROUP_TOK, D)
    return (results.reshape(full_shape), grads.reshape(full_shape), totals[0], totals[1], totals[2], totals[3], totals[4], totals[5], totals[6], totals[7])
```

```python
import functools
import math

import jax
import jax.numpy as jnp
from jax import lax
from jax.experimental import pallas as pl
from jax.experimental.pallas import tpu as pltpu
from jax.sharding import PartitionSpec as P

H = 32
KVH = 4
HD = 128
FF = 768
TOPK = 8
PROMPT = 1024
PER_KV = H // KVH

EPSILON = 1e-06
ROPE_BASE = 1000000.0
MASKED = -1e30
LOG2E = math.log2(math.e)
SCALE = HD ** (-0.5)

bf16 = jnp.bfloat16
f32 = jnp.float32
NT = (((1,), (1,)), ((), ()))
TN = (((0,), (0,)), ((), ()))
NN = (((1,), (0,)), ((), ()))
BOTH = ("dp", "expert")
VMEM_LIMIT = 56 * 1024 * 1024


def mm(a, b, dims=NN):
    return lax.dot_general(a, b, dims, preferred_element_type=f32)


def rms_scale(values):
    return lax.rsqrt(jnp.mean(values * values, axis=-1, keepdims=True) + EPSILON)


def norm_back(upstream, values, inv_rms, norm_gain):
    lifted = upstream * norm_gain
    inner_dot = jnp.mean(lifted * values, axis=-1, keepdims=True)
    back_grad = inv_rms * lifted - values * (inv_rms * inv_rms * inv_rms) * inner_dot
    gain_grad = jnp.sum((upstream * values * inv_rms).reshape(-1, values.shape[-1]), axis=0)
    return (back_grad, gain_grad)


def rotate(values, cosine, sine_part):
    half_dim = values.shape[-1] // 2
    first_half = values[..., :half_dim]
    second_half = values[..., half_dim:]
    return jnp.concatenate(
        [
            first_half * cosine - second_half * sine_part,
            second_half * cosine + first_half * sine_part,
        ],
        axis=-1,
    )


def attend_forward(step_heads, chunk, q_ref, kv_ref, bias_ref, o_ref, log_ref):
    group_len = bias_ref.shape[1]
    keys = kv_ref[:, 0, :, :HD].reshape(group_len, HD)
    values_t = kv_ref[:, 0, :, HD:].reshape(group_len, HD).T
    rows = q_ref.shape[1]
    for step in range(PER_KV // step_heads):
        heads = range(step * step_heads, (step + 1) * step_heads)
        query = jnp.concatenate([q_ref[0, :, h * HD : (h + 1) * HD] for h in heads], axis=0)
        mixed, row_sum = 0.0, 0.0
        for at in range(0, group_len, chunk):
            scores = mm(keys[at : at + chunk], query, NT)
            prob = jnp.exp2(scores + bias_ref[0, at : at + chunk, :])
            row_sum += jnp.sum(prob, axis=0, keepdims=True)
            mixed += mm(values_t[:, at : at + chunk], prob.astype(bf16))
        out = (mixed / row_sum).T.astype(bf16)
        for i, h in enumerate(heads):
            o_ref[0, :, h * HD : (h + 1) * HD] = out[i * rows : (i + 1) * rows]
        log_ref[0, 0, step : step + 1, :] = jnp.log2(row_sum)


def attend_backward(
    step_heads, chunk, q_ref, kv_ref, bias_ref, o_ref, do_ref, log_ref, dq_ref, dkv_ref, dk_acc, dv_acc
):
    group_len = bias_ref.shape[1]
    keys = kv_ref[:, 0, :, :HD].reshape(group_len, HD)
    values = kv_ref[:, 0, :, HD:].reshape(group_len, HD)
    keys_t = keys.T
    rows = q_ref.shape[1]
    dk_acc[...] = jnp.zeros_like(dk_acc)
    dv_acc[...] = jnp.zeros_like(dv_acc)
    for step in range(PER_KV // step_heads):
        heads = range(step * step_heads, (step + 1) * step_heads)
        query = jnp.concatenate([q_ref[0, :, h * HD : (h + 1) * HD] for h in heads], axis=0)
        grad = jnp.concatenate([do_ref[0, :, h * HD : (h + 1) * HD] for h in heads], axis=0)
        mixed = jnp.concatenate([o_ref[0, :, h * HD : (h + 1) * HD] for h in heads], axis=0)
        row_dot = jnp.sum((grad.astype(f32) * mixed.astype(f32)).T, axis=0, keepdims=True)
        log_sum = log_ref[0, 0, step : step + 1, :]
        dq_t = 0.0
        for at in range(0, group_len, chunk):
            part = slice(at, at + chunk)
            scores = mm(keys[part], query, NT)
            prob = jnp.exp2(scores + (bias_ref[0, part, :] - log_sum))
            d_prob = mm(values[part], grad, NT)
            d_score = (prob * (d_prob - row_dot)).astype(bf16)
            dv_acc[part] += mm(prob.astype(bf16), grad)
            dk_acc[part] += mm(d_score, query)
            dq_t += mm(keys_t[:, part], d_score)
        out = (dq_t * SCALE).T.astype(bf16)
        for i, h in enumerate(heads):
            dq_ref[0, :, h * HD : (h + 1) * HD] = out[i * rows : (i + 1) * rows]
    blocks = dkv_ref.shape[0]
    dkv_ref[:, 0, :, :HD] = (dk_acc[...] * (1.0 / LOG2E)).astype(bf16).reshape(blocks, rows, HD)
    dkv_ref[:, 0, :, HD:] = dv_acc[...].astype(bf16).reshape(blocks, rows, HD)


def attention_specs(micro, rows, group_len, blocks, step_heads):
    wide = PER_KV * HD
    q_spec = pl.BlockSpec((1, rows, wide), lambda b, g: (b, 0, g))
    kv_spec = pl.BlockSpec((blocks, 1, rows, 2 * HD), lambda b, g: (0, b, 0, g))
    bias_spec = pl.BlockSpec((1, group_len, step_heads * rows), lambda b, g: (b, 0, 0))
    log_spec = pl.BlockSpec((1, 1, PER_KV // step_heads, step_heads * rows), lambda b, g: (b, g, 0, 0))
    return q_spec, kv_spec, bias_spec, log_spec


def run_forward(query, kv_all, bias, step_heads, chunk):
    micro, rows, _ = query.shape
    blocks = kv_all.shape[0]
    group_len = bias.shape[1]
    q_spec, kv_spec, bias_spec, log_spec = attention_specs(micro, rows, group_len, blocks, step_heads)
    flops = 4 * micro * rows * H * HD * group_len
    return pl.pallas_call(
        functools.partial(attend_forward, step_heads, chunk),
        grid=(micro, KVH),
        in_specs=[q_spec, kv_spec, bias_spec],
        out_specs=[q_spec, log_spec],
        out_shape=[
            jax.ShapeDtypeStruct(query.shape, bf16),
            jax.ShapeDtypeStruct((micro, KVH, PER_KV // step_heads, step_heads * rows), f32),
        ],
        compiler_params=pltpu.CompilerParams(vmem_limit_bytes=VMEM_LIMIT),
        cost_estimate=pl.CostEstimate(
            flops=flops, bytes_accessed=20_000_000, transcendentals=flops // (4 * HD)
        ),
    )(query, kv_all, bias)


def run_backward(query, kv_all, bias, mixed, grad, logs, step_heads, chunk):
    micro, rows, _ = query.shape
    blocks = kv_all.shape[0]
    group_len = bias.shape[1]
    q_spec, kv_spec, bias_spec, log_spec = attention_specs(micro, rows, group_len, blocks, step_heads)
    flops = 10 * micro * rows * H * HD * group_len
    return pl.pallas_call(
        functools.partial(attend_backward, step_heads, chunk),
        grid=(micro, KVH),
        in_specs=[q_spec, kv_spec, bias_spec, q_spec, q_spec, log_spec],
        out_specs=[q_spec, kv_spec],
        out_shape=[
            jax.ShapeDtypeStruct(query.shape, bf16),
            jax.ShapeDtypeStruct(kv_all.shape, bf16),
        ],
        scratch_shapes=[pltpu.VMEM((group_len, HD), f32), pltpu.VMEM((group_len, HD), f32)],
        compiler_params=pltpu.CompilerParams(vmem_limit_bytes=VMEM_LIMIT),
        cost_estimate=pl.CostEstimate(
            flops=flops, bytes_accessed=30_000_000, transcendentals=flops // (10 * HD)
        ),
    )(query, kv_all, bias, mixed, grad, logs)


def slots_of(route_ids, gate_vals, ranking, capacity, experts):
    rows = route_ids.shape[0]
    pair_experts = route_ids.reshape(-1)
    earlier = (pair_experts[None, :] == pair_experts[:, None]) & (
        ranking[None, :] < ranking[:, None]
    )
    slot = jnp.sum(earlier.astype(jnp.int32), axis=1).reshape(rows, -1)
    kept = slot < capacity
    chosen = route_ids[:, :, None] == jnp.arange(experts, dtype=jnp.int32)[None, None, :]
    chosen = chosen & kept[:, :, None]
    slot_map = jnp.sum(jnp.where(chosen, slot[:, :, None] + 1, 0), axis=1).astype(f32) - 1.0
    weight_map = jnp.sum(jnp.where(chosen, gate_vals[:, :, None], 0.0), axis=1)
    return slot_map, weight_map


def body(
    inputs,
    cotangent,
    membership,
    routes,
    gate_weights,
    pair_order,
    w_query,
    w_key,
    w_value,
    w_output,
    norm_gains,
    w_gate,
    w_up,
    w_down,
):
    micro = inputs.shape[0]
    rows = inputs.shape[2]
    width = inputs.shape[3]
    group_len = membership.shape[2]
    member = lax.axis_index("expert")
    blocks = lax.axis_size("expert")
    shards = blocks * lax.axis_size("dp")
    shard_at = lax.axis_index("dp") * blocks + member
    local_experts = w_gate.shape[0]
    experts = local_experts * blocks
    capacity = rows * TOPK // experts
    step_heads = max(1, 384 // rows)
    total = micro * rows
    q_part, k_part, v_part = w_query.shape[1], w_key.shape[1], w_value.shape[1]

    gain_len = norm_gains.shape[0]
    gain_shard = jnp.zeros((2048,), bf16).at[:gain_len].set(norm_gains).reshape(16, 128)
    gain_full = lax.all_gather(gain_shard, BOTH, axis=0, tiled=True)
    gains = gain_full.reshape(shards, 2048)[:, :gain_len].reshape(-1).astype(f32)
    gain_in = gains[:width]
    gain_mid = gains[width : 2 * width]
    gain_q = gains[2 * width : 2 * width + HD]
    gain_k = gains[2 * width + HD :]

    qkv_w = lax.all_gather(
        jnp.concatenate([w_query.T, w_key.T, w_value.T], axis=0), BOTH, axis=0, tiled=True
    )
    out_w = lax.all_gather(w_output, BOTH, axis=0, tiled=True)
    wg = lax.all_gather(w_gate, "dp", axis=1, tiled=True)
    wu = lax.all_gather(w_up, "dp", axis=1, tiled=True)
    wd = lax.all_gather(w_down, "dp", axis=2, tiled=True)

    slot_map, weight_map = jax.vmap(
        lambda r, g, o: slots_of(r, g, o, capacity, experts)
    )(routes[:, 0], gate_weights[:, 0], pair_order[:, 0, 0])
    routing = jnp.concatenate([slot_map, weight_map], axis=-1)
    routing = lax.all_gather(routing, "expert", axis=0, tiled=False)
    mine = member * local_experts
    slot_mine = lax.dynamic_slice_in_dim(routing, mine, local_experts, axis=3)
    weight_mine = lax.dynamic_slice_in_dim(routing, experts + mine, local_experts, axis=3)
    slot_mine = jnp.transpose(slot_mine, (1, 3, 0, 2))
    weight_mine = jnp.transpose(weight_mine, (1, 3, 0, 2))
    slot_ids = jnp.arange(capacity, dtype=f32)
    hit = slot_mine[:, :, :, None, :] == slot_ids[None, None, None, :, None]
    pick = hit.astype(bf16)
    weighted = jnp.where(hit, weight_mine[:, :, :, None, :], 0.0)
    slot_weight = jnp.sum(weighted, axis=-1)
    weighted = weighted.astype(bf16)

    key_index = jnp.arange(group_len, dtype=jnp.int32)
    start_row = member * rows
    segment = membership[:, 0]
    row_index = start_row + jnp.arange(rows, dtype=jnp.int32)
    seg_rows = lax.dynamic_slice_in_dim(segment, start_row, rows, axis=1)
    before = jnp.sum((segment[:, None, :] < seg_rows[:, :, None]).astype(jnp.int32), axis=2)
    position = jnp.where(seg_rows == 0, row_index[None], PROMPT + row_index[None] - before)
    allowed = (key_index[None, :, None] <= row_index[None, None, :]) & (
        (segment[:, :, None] == 0) | (segment[:, :, None] == seg_rows[:, None, :])
    )
    bias = jnp.tile(jnp.where(allowed, 0.0, MASKED).astype(f32), (1, 1, step_heads))
    frequency = ROPE_BASE ** (-(jnp.arange(HD // 2, dtype=f32) * 2.0 / HD))
    angles = position.astype(f32).reshape(total)[:, None] * frequency[None, :]
    cosine = jnp.cos(angles)[:, None, :]
    sine_part = jnp.sin(angles)[:, None, :]

    hidden = inputs[:, 0].astype(f32).reshape(total, width)
    scale_in = rms_scale(hidden)
    normed = (hidden * scale_in * gain_in).astype(bf16)
    proj = mm(normed, qkv_w, NT).reshape(total, shards, q_part + k_part + v_part)
    queries = proj[:, :, :q_part].reshape(total, H, HD)
    key_pre = proj[:, :, q_part : q_part + k_part].reshape(total, KVH, HD)
    value = proj[:, :, q_part + k_part :].reshape(total, KVH, HD).astype(bf16)
    scale_q = rms_scale(queries)
    scale_k = rms_scale(key_pre)
    q_low = rotate(queries * scale_q * (gain_q * (SCALE * LOG2E)), cosine, sine_part).astype(bf16)
    q_low = q_low.reshape(micro, rows, H * HD)
    k_low = rotate(key_pre * scale_k * gain_k, cosine, sine_part).astype(bf16)
    kv_own = jnp.concatenate([k_low, value], axis=-1).reshape(micro, rows, KVH * 2 * HD)
    kv_all = lax.all_gather(kv_own, "expert", axis=0, tiled=False)
    chunk = 256
    mixed, logs = run_forward(q_low, kv_all, bias, step_heads, chunk)

    branch = mm(mixed.reshape(total, H * HD), out_w)
    middle = hidden + branch
    scale_mid = rms_scale(middle)
    routed = (middle * scale_mid * gain_mid).astype(bf16).reshape(micro, rows, width)
    middle = middle.reshape(micro, rows, width)
    scale_mid = scale_mid.reshape(micro, rows, 1)

    outputs, d_branches, d_middles = [], [], []
    acc_gate = acc_up = acc_down = 0.0
    grad_mid = 0.0
    slots = blocks * capacity
    for at in range(micro):
        d_out = lax.all_gather(cotangent[at, 0], "expert", axis=0, tiled=False)
        tokens = lax.all_gather(routed[at], "expert", axis=0, tiled=False)
        picked = jnp.einsum("ebst,btd->ebsd", pick[at], tokens, preferred_element_type=f32)
        picked = picked.astype(bf16).reshape(local_experts, slots, width)
        d_result = jnp.einsum("ebst,btd->ebsd", pick[at], d_out, preferred_element_type=f32)
        d_result = (d_result * slot_weight[at][..., None]).astype(bf16)
        d_result = d_result.reshape(local_experts, slots, width)
        gate_pre = jnp.einsum("erd,edf->erf", picked, wg, preferred_element_type=f32)
        up_pre = jnp.einsum("erd,edf->erf", picked, wu, preferred_element_type=f32)
        d_hidden = jnp.einsum("erd,efd->erf", d_result, wd, preferred_element_type=f32)
        sigmoid_g = jax.nn.sigmoid(gate_pre)
        silu_g = gate_pre * sigmoid_g
        hidden_low = (silu_g * up_pre).astype(bf16)
        d_gate = (d_hidden * up_pre * sigmoid_g * (1.0 + gate_pre * (1.0 - sigmoid_g))).astype(bf16)
        d_up = (d_hidden * silu_g).astype(bf16)
        d_rows = jnp.einsum("erf,edf->erd", d_gate, wg, preferred_element_type=f32)
        d_rows = d_rows + jnp.einsum("erf,edf->erd", d_up, wu, preferred_element_type=f32)
        d_rows = d_rows.astype(bf16).reshape(local_experts, blocks, capacity, width)
        d_part = jnp.einsum("ebst,ebsd->btd", pick[at], d_rows, preferred_element_type=f32)
        d_part = d_part.astype(bf16).reshape(group_len, width)
        d_routed = lax.psum_scatter(d_part, "expert", scatter_dimension=0, tiled=True).astype(f32)
        result = jnp.einsum("erf,efd->erd", hidden_low, wd, preferred_element_type=f32)
        result = result.astype(bf16).reshape(local_experts, blocks, capacity, width)
        part = jnp.einsum("ebst,ebsd->btd", weighted[at], result, preferred_element_type=f32)
        part = part.astype(bf16).reshape(group_len, width)
        expert_mix = lax.psum_scatter(part, "expert", scatter_dimension=0, tiled=True).astype(f32)
        outputs.append((middle[at] + expert_mix).astype(bf16))

        acc_down += jnp.einsum("erf,erd->efd", hidden_low, d_result, preferred_element_type=f32)
        acc_gate += jnp.einsum("erd,erf->edf", picked, d_gate, preferred_element_type=f32)
        acc_up += jnp.einsum("erd,erf->edf", picked, d_up, preferred_element_type=f32)

        d_mid_norm, mid_gain_grad = norm_back(d_routed, middle[at], scale_mid[at], gain_mid)
        grad_mid = grad_mid + mid_gain_grad
        d_middle = cotangent[at, 0].astype(f32) + d_mid_norm
        d_middles.append(d_middle)
        d_branches.append(d_middle.astype(bf16))

    grad_gate = lax.psum_scatter(acc_gate.astype(bf16), "dp", scatter_dimension=1, tiled=True)
    grad_up = lax.psum_scatter(acc_up.astype(bf16), "dp", scatter_dimension=1, tiled=True)
    grad_down = lax.psum_scatter(acc_down.astype(bf16), "dp", scatter_dimension=2, tiled=True)

    d_branch = jnp.concatenate(d_branches, axis=0)
    d_middle = jnp.concatenate(d_middles, axis=0)
    grad_output = mm(mixed.reshape(total, H * HD), d_branch, TN).astype(bf16)
    grad_output = lax.psum_scatter(grad_output, BOTH, scatter_dimension=0, tiled=True)
    d_mixed = mm(d_branch, out_w, NT).astype(bf16).reshape(micro, rows, H * HD)
    dq_low, dkv_all = run_backward(q_low, kv_all, bias, mixed, d_mixed, logs, step_heads, chunk)
    dkv = lax.psum_scatter(dkv_all, "expert", scatter_dimension=0, tiled=False)
    dkv = dkv.reshape(total, KVH, 2 * HD)
    d_query = rotate(dq_low.reshape(total, H, HD).astype(f32), cosine, -sine_part)
    d_query, grad_qn = norm_back(d_query, queries, scale_q, gain_q)
    d_key = rotate(dkv[:, :, :HD].astype(f32), cosine, -sine_part)
    d_key, grad_kn = norm_back(d_key, key_pre, scale_k, gain_k)
    d_proj = jnp.concatenate(
        [
            d_query.astype(bf16).reshape(total, shards, q_part),
            d_key.astype(bf16).reshape(total, shards, k_part),
            dkv[:, :, HD:].reshape(total, shards, v_part),
        ],
        axis=-1,
    ).reshape(total, -1)
    grad_qkv = mm(d_proj, normed, TN).astype(bf16)
    grad_qkv = lax.psum_scatter(grad_qkv, BOTH, scatter_dimension=0, tiled=True).astype(f32)
    d_normed = mm(d_proj, qkv_w)
    d_in_norm, grad_in = norm_back(d_normed, hidden, scale_in, gain_in)
    input_grad = d_middle + d_in_norm

    gain_grads = jnp.concatenate([grad_in, grad_mid, grad_qn, grad_kn]).reshape(shards, gain_len)
    gain_grads = jnp.pad(gain_grads, ((0, 0), (0, 256 - gain_len % 256)))
    gain_all = lax.all_gather(gain_grads, BOTH, axis=0, tiled=False)
    grad_gains = jnp.sum(lax.dynamic_index_in_dim(gain_all, shard_at, axis=1, keepdims=False), axis=0)
    return (
        jnp.stack(outputs)[:, None],
        input_grad.reshape(micro, 1, rows, width),
        grad_qkv[:q_part].T,
        grad_qkv[q_part : q_part + k_part].T,
        grad_qkv[q_part + k_part :].T,
        grad_output.astype(f32),
        grad_gains[:gain_len],
        grad_gate.astype(f32),
        grad_up.astype(f32),
        grad_down.astype(f32),
    )


def solution(mesh):
    return jax.shard_map(
        body,
        mesh=mesh,
        in_specs=(
            P(None, "dp", "expert", None),
            P(None, "dp", "expert", None),
            P(None, "dp", None),
            P(None, "dp", "expert", None),
            P(None, "dp", "expert", None),
            P(None, "dp", "expert", None),
            P(None, ("dp", "expert")),
            P(None, ("dp", "expert")),
            P(None, ("dp", "expert")),
            P(("dp", "expert"), None),
            P(("dp", "expert")),
            P("expert", "dp", None),
            P("expert", "dp", None),
            P("expert", None, "dp"),
        ),
        out_specs=(
            P(None, "dp", "expert", None),
            P(None, "dp", "expert", None),
            P(None, ("dp", "expert")),
            P(None, ("dp", "expert")),
            P(None, ("dp", "expert")),
            P(("dp", "expert"), None),
            P(("dp", "expert")),
            P("expert", "dp", None),
            P("expert", "dp", None),
            P("expert", None, "dp"),
        ),
        check_vma=False,
    )
```

```python
import functools
import math

import jax
import jax.numpy as jnp
from jax import lax
from jax.experimental import pallas as pl
from jax.experimental.pallas import tpu as pltpu
from jax.sharding import PartitionSpec as P

H = 32
KVH = 4
HD = 128
FF = 768
TOPK = 8
PROMPT = 1024
PER_KV = H // KVH

EPSILON = 1e-06
ROPE_BASE = 1000000.0
MASKED = -1e30
LOG2E = math.log2(math.e)
SCALE = HD ** (-0.5)

bf16 = jnp.bfloat16
f32 = jnp.float32
NT = (((1,), (1,)), ((), ()))
TN = (((0,), (0,)), ((), ()))
NN = (((1,), (0,)), ((), ()))
BOTH = ("dp", "expert")
VMEM_LIMIT = 56 * 1024 * 1024


def mm(a, b, dims=NN):
    return lax.dot_general(a, b, dims, preferred_element_type=f32)


def rms_scale(values):
    return lax.rsqrt(jnp.mean(values * values, axis=-1, keepdims=True) + EPSILON)


def norm_back(upstream, values, inv_rms, norm_gain):
    lifted = upstream * norm_gain
    inner_dot = jnp.mean(lifted * values, axis=-1, keepdims=True)
    back_grad = inv_rms * lifted - values * (inv_rms * inv_rms * inv_rms) * inner_dot
    gain_grad = jnp.sum((upstream * values * inv_rms).reshape(-1, values.shape[-1]), axis=0)
    return (back_grad, gain_grad)


def rotate(values, cosine, sine_part):
    half_dim = values.shape[-1] // 2
    first_half = values[..., :half_dim]
    second_half = values[..., half_dim:]
    return jnp.concatenate(
        [
            first_half * cosine - second_half * sine_part,
            second_half * cosine + first_half * sine_part,
        ],
        axis=-1,
    )


def attend_forward(step_heads, chunk, q_ref, kv_ref, bias_ref, o_ref, log_ref):
    group_len = bias_ref.shape[1]
    keys = kv_ref[:, 0, :, :HD].reshape(group_len, HD)
    values_t = kv_ref[:, 0, :, HD:].reshape(group_len, HD).T
    rows = q_ref.shape[1]
    for step in range(PER_KV // step_heads):
        heads = range(step * step_heads, (step + 1) * step_heads)
        query = jnp.concatenate([q_ref[0, :, h * HD : (h + 1) * HD] for h in heads], axis=0)
        mixed, row_sum = 0.0, 0.0
        for at in range(0, group_len, chunk):
            scores = mm(keys[at : at + chunk], query, NT)
            prob = jnp.exp2(scores + bias_ref[0, at : at + chunk, :])
            row_sum += jnp.sum(prob, axis=0, keepdims=True)
            mixed += mm(values_t[:, at : at + chunk], prob.astype(bf16))
        out = (mixed / row_sum).T.astype(bf16)
        for i, h in enumerate(heads):
            o_ref[0, :, h * HD : (h + 1) * HD] = out[i * rows : (i + 1) * rows]
        log_ref[0, 0, step : step + 1, :] = jnp.log2(row_sum)


def attend_backward(
    step_heads, chunk, q_ref, kv_ref, bias_ref, o_ref, do_ref, log_ref, dq_ref, dkv_ref, dk_acc, dv_acc
):
    group_len = bias_ref.shape[1]
    keys = kv_ref[:, 0, :, :HD].reshape(group_len, HD)
    values = kv_ref[:, 0, :, HD:].reshape(group_len, HD)
    keys_t = keys.T
    rows = q_ref.shape[1]
    dk_acc[...] = jnp.zeros_like(dk_acc)
    dv_acc[...] = jnp.zeros_like(dv_acc)
    for step in range(PER_KV // step_heads):
        heads = range(step * step_heads, (step + 1) * step_heads)
        query = jnp.concatenate([q_ref[0, :, h * HD : (h + 1) * HD] for h in heads], axis=0)
        grad = jnp.concatenate([do_ref[0, :, h * HD : (h + 1) * HD] for h in heads], axis=0)
        mixed = jnp.concatenate([o_ref[0, :, h * HD : (h + 1) * HD] for h in heads], axis=0)
        row_dot = jnp.sum((grad.astype(f32) * mixed.astype(f32)).T, axis=0, keepdims=True)
        log_sum = log_ref[0, 0, step : step + 1, :]
        dq_t = 0.0
        for at in range(0, group_len, chunk):
            part = slice(at, at + chunk)
            scores = mm(keys[part], query, NT)
            prob = jnp.exp2(scores + (bias_ref[0, part, :] - log_sum))
            d_prob = mm(values[part], grad, NT)
            d_score = (prob * (d_prob - row_dot)).astype(bf16)
            dv_acc[part] += mm(prob.astype(bf16), grad)
            dk_acc[part] += mm(d_score, query)
            dq_t += mm(keys_t[:, part], d_score)
        out = (dq_t * SCALE).T.astype(bf16)
        for i, h in enumerate(heads):
            dq_ref[0, :, h * HD : (h + 1) * HD] = out[i * rows : (i + 1) * rows]
    blocks = dkv_ref.shape[0]
    dkv_ref[:, 0, :, :HD] = (dk_acc[...] * (1.0 / LOG2E)).astype(bf16).reshape(blocks, rows, HD)
    dkv_ref[:, 0, :, HD:] = dv_acc[...].astype(bf16).reshape(blocks, rows, HD)


def attention_specs(micro, rows, group_len, blocks, step_heads):
    wide = PER_KV * HD
    q_spec = pl.BlockSpec((1, rows, wide), lambda b, g: (b, 0, g))
    kv_spec = pl.BlockSpec((blocks, 1, rows, 2 * HD), lambda b, g: (0, b, 0, g))
    bias_spec = pl.BlockSpec((1, group_len, step_heads * rows), lambda b, g: (b, 0, 0))
    log_spec = pl.BlockSpec((1, 1, PER_KV // step_heads, step_heads * rows), lambda b, g: (b, g, 0, 0))
    return q_spec, kv_spec, bias_spec, log_spec


def run_forward(query, kv_all, bias, step_heads, chunk):
    micro, rows, _ = query.shape
    blocks = kv_all.shape[0]
    group_len = bias.shape[1]
    q_spec, kv_spec, bias_spec, log_spec = attention_specs(micro, rows, group_len, blocks, step_heads)
    flops = 4 * micro * rows * H * HD * group_len
    return pl.pallas_call(
        functools.partial(attend_forward, step_heads, chunk),
        grid=(micro, KVH),
        in_specs=[q_spec, kv_spec, bias_spec],
        out_specs=[q_spec, log_spec],
        out_shape=[
            jax.ShapeDtypeStruct(query.shape, bf16),
            jax.ShapeDtypeStruct((micro, KVH, PER_KV // step_heads, step_heads * rows), f32),
        ],
        compiler_params=pltpu.CompilerParams(vmem_limit_bytes=VMEM_LIMIT),
        cost_estimate=pl.CostEstimate(
            flops=flops, bytes_accessed=20_000_000, transcendentals=flops // (4 * HD)
        ),
    )(query, kv_all, bias)


def run_backward(query, kv_all, bias, mixed, grad, logs, step_heads, chunk):
    micro, rows, _ = query.shape
    blocks = kv_all.shape[0]
    group_len = bias.shape[1]
    q_spec, kv_spec, bias_spec, log_spec = attention_specs(micro, rows, group_len, blocks, step_heads)
    flops = 10 * micro * rows * H * HD * group_len
    return pl.pallas_call(
        functools.partial(attend_backward, step_heads, chunk),
        grid=(micro, KVH),
        in_specs=[q_spec, kv_spec, bias_spec, q_spec, q_spec, log_spec],
        out_specs=[q_spec, kv_spec],
        out_shape=[
            jax.ShapeDtypeStruct(query.shape, bf16),
            jax.ShapeDtypeStruct(kv_all.shape, bf16),
        ],
        scratch_shapes=[pltpu.VMEM((group_len, HD), f32), pltpu.VMEM((group_len, HD), f32)],
        compiler_params=pltpu.CompilerParams(vmem_limit_bytes=VMEM_LIMIT),
        cost_estimate=pl.CostEstimate(
            flops=flops, bytes_accessed=30_000_000, transcendentals=flops // (10 * HD)
        ),
    )(query, kv_all, bias, mixed, grad, logs)


MESH = pl.DeviceIdType.MESH


def gather_kernel(phases, count, *refs):
    ins, outs, sems = refs[:count], refs[count : 2 * count], refs[2 * count :]
    dp = lax.axis_index("dp"); member = lax.axis_index("expert")
    blocks = lax.axis_size("expert")
    core = member % 2; z = member // 2
    depth = blocks // 2
    sibling = (dp, member + 1 - 2 * core)
    by_x = (dp + 1 - 2 * (dp % 2), member)
    by_y = ((dp + 2) % 4, member)
    x_at, y_at, far_at = by_x[0], by_y[0], 3 - dp
    above, below = (dp, member + 2), (dp, member - 2)
    barrier = pltpu.get_barrier_semaphore()
    peers = [(sibling, None), (by_x, None), (by_y, None), (above, z < depth - 1), (below, z > 0)]
    for peer, ok in peers:
        if ok is None:
            pl.semaphore_signal(barrier, inc=1, device_id=peer, device_id_type=MESH)
        else:
            @pl.when(ok)
            def _(peer=peer):
                pl.semaphore_signal(barrier, inc=1, device_id=peer, device_id_type=MESH)
    @pl.when((z == 0) | (z == depth - 1))
    def _(): pl.semaphore_wait(barrier, 4)
    @pl.when((z > 0) & (z < depth - 1))
    def _(): pl.semaphore_wait(barrier, 5)

    def guarded(ok, run):
        if ok is None: run()
        else: pl.when(ok)(run)

    class Item:
        pass

    def make(i):
        src, out = ins[i], outs[i]
        rows = src.shape[0]
        half = rows // 2
        (own_sem, sz, rz, sxy, rxy, sc, rc) = sems[i * 7 : (i + 1) * 7]
        def at(d, s, lo=0, n=rows):
            return out.at[pl.ds(pl.multiple_of((d * blocks + s * 2 + core) * rows + lo, 16 if half % 16 == 0 else 8), n)]
        def copy(a, b, ss, rs, to):
            return pltpu.make_async_remote_copy(src_ref=a, dst_ref=b, send_sem=ss, recv_sem=rs, device_id=to, device_id_type=MESH)
        def block(d, s):
            return at(d, s)
        it = Item()
        def local():
            return pltpu.make_async_copy(src, at(dp, z), own_sem)
        def up(s, ref): return copy(ref, at(dp, s), sz.at[0, s], rz.at[s], above)
        def down(s, ref): return copy(ref, at(dp, s), sz.at[1, s], rz.at[s], below)
        def to_x(s, ref): return copy(ref, at(dp, s), sxy.at[0, s], rxy.at[0, s], by_x)
        def to_y(s, ref): return copy(ref, at(dp, s), sxy.at[1, s], rxy.at[1, s], by_y)
        def half_y(s):
            return copy(at(x_at, s, 0, half), at(x_at, s, 0, half), sxy.at[2, s], rxy.at[2, s], by_y)
        def half_x(s):
            return copy(at(y_at, s, half, half), at(y_at, s, half, half), sxy.at[3, s], rxy.at[3, s], by_x)
        def to_core(r, d, s, ref): return copy(ref, at(d, s), sc.at[r, s], rc.at[r, s], sibling)
        def spread(s, ref):
            to_x(s, ref).start(); to_y(s, ref).start(); to_core(0, dp, s, ref).start()
        def start():
            local().start()
            guarded(z < depth - 1, lambda: up(z, src).start())
            guarded(z > 0, lambda: down(z, src).start())
            spread(z, src)
        def z_event(s, ok, rising):
            def run():
                up(s, at(dp, s)).wait_recv()
                if rising: guarded(z < depth - 1, lambda: up(s, at(dp, s)).start())
                else: guarded(z > 0, lambda: down(s, at(dp, s)).start())
                spread(s, at(dp, s))
            pl.when(ok)(run)
        def near_event(s, ok):
            def run():
                to_x(s, at(dp, s)).wait_recv()
                half_y(s).start()
                to_core(1, x_at, s, at(x_at, s)).start()
                to_y(s, at(dp, s)).wait_recv()
                half_x(s).start()
                to_core(2, y_at, s, at(y_at, s)).start()
            guarded(ok, run)
        def far_event(s, ok):
            def run():
                half_y(s).wait_recv(); half_x(s).wait_recv()
                to_core(3, far_at, s, at(far_at, s)).start()
            guarded(ok, run)
        def core_wait(s):
            for r, d in enumerate((dp, x_at, y_at, far_at)):
                to_core(r, d, s, at(d, s)).wait_recv()
        def finish():
            local().wait()
            for s in range(depth):
                for c in (to_x(s, at(dp, s)), to_y(s, at(dp, s)), half_y(s), half_x(s)): c.wait_send()
                for r, d in enumerate((dp, x_at, y_at, far_at)): to_core(r, d, s, at(d, s)).wait_send()
                guarded((z >= s) & (z < depth - 1), lambda: up(s, at(dp, s)).wait_send())
                guarded((z <= s) & (z > 0), lambda: down(s, at(dp, s)).wait_send())
        it.start, it.z_event, it.near_event, it.far_event, it.core_wait, it.finish = start, z_event, near_event, far_event, core_wait, finish
        return it
    items = [make(i) for i in range(count)]
    def around(d):
        if d == 0: return [(z, None, True)]
        return [(z - d, z >= d, True), (z + d, z + d < depth, False)]
    for n, phase in enumerate(phases):
        its = [items[i] for i in phase]
        for it in its: it.start()
        for d in range(1, depth + 2):
            if d < depth:
                for s, ok, rising in around(d):
                    for it in its: it.z_event(s, ok, rising)
            if d - 1 < depth:
                for s, ok, _ in around(d - 1):
                    for it in its: it.near_event(s, ok)
            if d - 2 >= 0:
                for s, ok, _ in around(d - 2):
                    for it in its: it.far_event(s, ok)
            if n + 1 < len(phases) and d == depth: pass
    for it in items:
        for s in range(depth): it.core_wait(s)
    for it in items: it.finish()

def gather_rows(arrays, phases, cid):
    shards = lax.axis_size("dp") * lax.axis_size("expert")
    depth = lax.axis_size("expert") // 2
    D = pltpu.SemaphoreType.DMA
    sems = []
    for _ in arrays:
        sems += [D, D((2, depth)), D((depth,)), D((4, depth)), D((4, depth)), D((4, depth)), D((4, depth))]
    return pl.pallas_call(
        functools.partial(gather_kernel, phases, len(arrays)),
        out_shape=[jax.ShapeDtypeStruct((shards * a.shape[0],) + a.shape[1:], a.dtype) for a in arrays],
        in_specs=[pl.BlockSpec(memory_space=pl.ANY)] * len(arrays),
        out_specs=[pl.BlockSpec(memory_space=pl.ANY)] * len(arrays),
        scratch_shapes=sems,
        compiler_params=pltpu.CompilerParams(collective_id=cid, has_side_effects=True),
        cost_estimate=pl.CostEstimate(flops=0, bytes_accessed=400_000_000, transcendentals=0),
    )(*arrays)


def reduce_kernel(rows, cuts, a_ref, b_ref, o_ref, sib, got, own, far, near, plane, got_z,
                  s0, r0, s1, r1, s2, r2, s3, r3):
    dp = lax.axis_index("dp"); member = lax.axis_index("expert")
    core = member % 2; z = member // 2
    sibling = (dp, member + 1 - 2 * core)
    by_x = (dp + 1 - 2 * (dp % 2), member)
    by_y = ((dp + 2) % 4, member)
    x_at, y_at = by_x[0], by_y[0]
    far_at = 3 - dp
    half = rows // 2
    depth = lax.axis_size("expert") // 2
    barrier = pltpu.get_barrier_semaphore()
    peers = [sibling, by_x, by_y] + [(dp, ((z + d) % depth) * 2 + core) for d in range(1, depth)]
    for peer in peers:
        pl.semaphore_signal(barrier, inc=1, device_id=peer, device_id_type=MESH)
    pl.semaphore_wait(barrier, len(peers))

    def pick(table):
        at = table[depth-1]
        for i in range(depth - 1):
            at = jnp.where(z == i, table[i], at)
        return at
    orders = [[3, 3, 0, 0], [2, 0, 3, 1], [1, 2, 1, 2], [0, 1, 2, 3]]
    targets = [pick(t) for t in orders]
    wide = 4 * rows
    cols = b_ref.shape[1] // cuts

    def copy(src, dst, ssem, rsem, to):
        return pltpu.make_async_remote_copy(src_ref=src, dst_ref=dst, send_sem=ssem, recv_sem=rsem, device_id=to, device_id_type=MESH)

    def product(half_of, k, put):
        base = (half_of * depth + targets[k]) * wide
        def step(i, _):
            at = (i // cuts) * rows
            col = pl.multiple_of((i % cuts) * cols, cols)
            part = jnp.dot(a_ref[pl.ds(pl.multiple_of(base + at, 16), rows), :], b_ref[:, pl.ds(col, cols)], preferred_element_type=f32)
            put(pl.ds(pl.multiple_of(at, 16), rows), pl.ds(col, cols), part)
            return 0
        lax.fori_loop(0, 4 * cuts, step, 0)

    sib_copies, far_copies, near_copies, z_copies = {}, {}, {}, {}
    def sib_step(k):
        slot = k % 2
        if k >= 2:
            sib_copies[k - 2].wait_send()
        def put(r, c, part):
            sib[slot, r, c] = part.astype(bf16)
        product(1 - core, k, put)
        sib_copies[k] = copy(sib.at[slot], got.at[k], s0.at[slot], r0.at[k], sibling)
        sib_copies[k].start()
    def blk(at):
        return pl.ds(pl.multiple_of(at * rows, 16), rows)
    def own_step(k):
        sib_copies[k].wait_recv()
        def put(r, c, part):
            own[k, r, c] = (part + got[k, r, c].astype(f32)).astype(bf16)
        product(core, k, put)
        base = pl.multiple_of(far_at * rows, 16)
        far_copies[k] = (
            copy(own.at[k, pl.ds(base, half)], far.at[k, 0], s1.at[k, 0], r1.at[k, 0], by_x),
            copy(own.at[k, pl.ds(pl.multiple_of(base + half, 16), half)], far.at[k, 1], s1.at[k, 1], r1.at[k, 1], by_y),
        )
        for c in far_copies[k]: c.start()
    def near_step(k):
        a, b = far_copies[k]
        a.wait_recv()
        rng = pl.ds(pl.multiple_of(y_at * rows, 16), half)
        own[k, rng] = (own[k, rng].astype(f32) + far[k, 0].astype(f32)).astype(bf16)
        to_y = copy(own.at[k, blk(y_at)], near.at[k, 1], s2.at[k, 1], r2.at[k, 1], by_y)
        to_y.start()
        b.wait_recv()
        rng = pl.ds(pl.multiple_of(x_at * rows + half, 16), half)
        own[k, rng] = (own[k, rng].astype(f32) + far[k, 1].astype(f32)).astype(bf16)
        to_x = copy(own.at[k, blk(x_at)], near.at[k, 0], s2.at[k, 0], r2.at[k, 0], by_x)
        to_x.start()
        near_copies[k] = (to_x, to_y)
    def plane_step(k):
        for c in near_copies[k]: c.wait_recv()
        total = own[k, blk(dp)].astype(f32) + near[k, 0].astype(f32) + near[k, 1].astype(f32)
        if k < depth - 1:
            plane[k] = total.astype(bf16)
            to = (dp, targets[k] * 2 + core)
            z_copies[k] = copy(plane.at[k], got_z.at[z], s3.at[k], r3.at[z], to)
            z_copies[k].start()
        else:
            o_ref[...] = total
    sib_step(0); sib_step(1)
    own_step(0)
    sib_step(2)
    own_step(1)
    near_step(0)
    sib_step(3)
    own_step(2)
    near_step(1)
    plane_step(0)
    own_step(3)
    near_step(2)
    plane_step(1)
    near_step(3)
    plane_step(2)
    plane_step(3)
    for d in range(1, depth):
        src = (z + d) % depth
        copy(plane.at[0], got_z.at[src], s3.at[0], r3.at[src], sibling).wait_recv()
        o_ref[...] += got_z[src].astype(f32)
    for k in range(depth):
        if k >= 2: sib_copies[k].wait_send()
        for c in far_copies[k]: c.wait_send()
        for c in near_copies[k]: c.wait_send()
        if k < depth - 1: z_copies[k].wait_send()

def reduce_rows(a, b, rows, cid, special):
    if not special:
        part = mm(a, b, TN).astype(bf16)
        return lax.psum_scatter(part, BOTH, scatter_dimension=0, tiled=True).astype(f32)
    tokens, width = b.shape
    depth = 4
    at = a.reshape(tokens, 4, depth, 2, rows).transpose(3, 2, 1, 4, 0).reshape(-1, tokens)
    D = pltpu.SemaphoreType.DMA
    return pl.pallas_call(
        functools.partial(reduce_kernel, rows, 4),
        out_shape=jax.ShapeDtypeStruct((rows, width), f32),
        in_specs=[pl.BlockSpec(memory_space=pltpu.VMEM)] * 2,
        out_specs=pl.BlockSpec(memory_space=pltpu.VMEM),
        scratch_shapes=[
            pltpu.VMEM((2, 4 * rows, width), bf16),
            pltpu.VMEM((depth, 4 * rows, width), bf16),
            pltpu.VMEM((depth, 4 * rows, width), bf16),
            pltpu.VMEM((depth, 2, rows // 2, width), bf16),
            pltpu.VMEM((depth, 2, rows, width), bf16),
            pltpu.VMEM((depth - 1, rows, width), bf16),
            pltpu.VMEM((depth, rows, width), bf16),
            D((2,)), D((depth,)), D((depth, 2)), D((depth, 2)), D((depth, 2)), D((depth, 2)), D((depth - 1,)), D((depth,)),
        ],
        compiler_params=pltpu.CompilerParams(vmem_limit_bytes=60*1024*1024, collective_id=cid, has_side_effects=True),
        cost_estimate=pl.CostEstimate(flops=2*tokens*32*rows*width, bytes_accessed=10_000_000, transcendentals=0),
    )(at, b)


def slots_of(route_ids, gate_vals, ranking, capacity, experts):
    rows = route_ids.shape[0]
    pair_experts = route_ids.reshape(-1)
    earlier = (pair_experts[None, :] == pair_experts[:, None]) & (
        ranking[None, :] < ranking[:, None]
    )
    slot = jnp.sum(earlier.astype(jnp.int32), axis=1).reshape(rows, -1)
    kept = slot < capacity
    chosen = route_ids[:, :, None] == jnp.arange(experts, dtype=jnp.int32)[None, None, :]
    chosen = chosen & kept[:, :, None]
    slot_map = jnp.sum(jnp.where(chosen, slot[:, :, None] + 1, 0), axis=1).astype(f32) - 1.0
    weight_map = jnp.sum(jnp.where(chosen, gate_vals[:, :, None], 0.0), axis=1)
    return slot_map, weight_map


def swap(values, bit):
    return lax.ppermute(values, "dp", [(i, i ^ bit) for i in range(lax.axis_size("dp"))])


def gather_parts(own, axis):
    if lax.axis_size("dp") != 4:
        return lax.all_gather(own, "dp", axis=axis, tiled=True)
    at = lax.axis_index("dp")
    size = own.shape[axis]
    by_x, by_y = swap(own, 1), swap(own, 2)
    far_0, far_1 = swap(by_x[:1], 2), swap(by_y[1:], 1)
    shape = list(own.shape)
    shape[axis] *= 4
    full = jnp.zeros(tuple(shape), own.dtype)
    for part, expert, bits in ((own, 0, 0), (by_x, 0, 1), (by_y, 0, 2), (far_0, 0, 3), (far_1, 1, 3)):
        start = [expert, 0, 0]
        start[axis] = (at ^ bits) * size
        full = lax.dynamic_update_slice(full, part, tuple(start))
    return full


def scatter_far(total, axis):
    if lax.axis_size("dp") != 4:
        low = total.astype(bf16)
        return [lax.psum_scatter(low, "dp", scatter_dimension=axis, tiled=True)]
    at = lax.axis_index("dp")
    size = total.shape[axis] // 4

    def part(bits):
        return lax.dynamic_slice_in_dim(total, (at ^ bits) * size, size, axis=axis)

    far = part(3).astype(bf16)
    return [swap(far[:1], 1), swap(far[1:], 2), part(1), part(2), part(0)]


def scatter_near(for_y, for_x=None, near_x=None, near_y=None, own=None):
    if for_x is None:
        return for_y.astype(f32)
    near_y = jnp.concatenate([near_y[:1] + for_y.astype(f32), near_y[1:]], axis=0).astype(bf16)
    near_x = jnp.concatenate([near_x[:1], near_x[1:] + for_x.astype(f32)], axis=0).astype(bf16)
    by_x, by_y = swap(near_x, 1), swap(near_y, 2)
    return own + by_x.astype(f32) + by_y.astype(f32)


def body(
    inputs,
    cotangent,
    membership,
    routes,
    gate_weights,
    pair_order,
    w_query,
    w_key,
    w_value,
    w_output,
    norm_gains,
    w_gate,
    w_up,
    w_down,
):
    micro = inputs.shape[0]
    rows = inputs.shape[2]
    width = inputs.shape[3]
    group_len = membership.shape[2]
    member = lax.axis_index("expert")
    blocks = lax.axis_size("expert")
    shards = blocks * lax.axis_size("dp")
    shard_at = lax.axis_index("dp") * blocks + member
    local_experts = w_gate.shape[0]
    experts = local_experts * blocks
    capacity = rows * TOPK // experts
    step_heads = max(1, 384 // rows)
    total = micro * rows
    q_part, k_part, v_part = w_query.shape[1], w_key.shape[1], w_value.shape[1]

    special = blocks == 8 and shards == 32

    gain_len = norm_gains.shape[0]
    gain_shard = jnp.zeros((2048,), bf16).at[:gain_len].set(norm_gains).reshape(16, 128)
    qkv_w = jnp.concatenate([w_query.T, w_key.T, w_value.T], axis=0)
    if special:
        qkv_w, out_w, gain_full = gather_rows([qkv_w, w_output, gain_shard], [(2, 0, 1)], 1)
    else:
        qkv_w, out_w, gain_full = (
            lax.all_gather(part, BOTH, axis=0, tiled=True) for part in (qkv_w, w_output, gain_shard)
        )
    d_out_all = lax.all_gather(cotangent[:, 0], "expert", axis=0, tiled=False)
    qkv_w, d_out_all = lax.optimization_barrier((qkv_w, d_out_all))
    gains = gain_full.reshape(shards, 2048)[:, :gain_len].reshape(-1).astype(f32)
    gain_in = gains[:width]
    gain_mid = gains[width : 2 * width]
    gain_q = gains[2 * width : 2 * width + HD]
    gain_k = gains[2 * width + HD :]

    w_gate, w_up, w_down, qkv_w = lax.optimization_barrier((w_gate, w_up, w_down, qkv_w))
    wg = gather_parts(w_gate, 1)
    wu = gather_parts(w_up, 1)
    wd = gather_parts(w_down, 2)

    slot_map, weight_map = jax.vmap(
        lambda r, g, o: slots_of(r, g, o, capacity, experts)
    )(routes[:, 0], gate_weights[:, 0], pair_order[:, 0, 0])
    routing = jnp.concatenate([slot_map, weight_map], axis=-1)
    routing = lax.all_gather(routing, "expert", axis=0, tiled=False)
    mine = member * local_experts
    slot_mine = lax.dynamic_slice_in_dim(routing, mine, local_experts, axis=3)
    weight_mine = lax.dynamic_slice_in_dim(routing, experts + mine, local_experts, axis=3)
    slot_mine = jnp.transpose(slot_mine, (1, 3, 0, 2))
    weight_mine = jnp.transpose(weight_mine, (1, 3, 0, 2))
    slot_ids = jnp.arange(capacity, dtype=f32)
    hit = slot_mine[:, :, :, None, :] == slot_ids[None, None, None, :, None]
    pick = hit.astype(bf16)
    weighted = jnp.where(hit, weight_mine[:, :, :, None, :], 0.0)
    slot_weight = jnp.sum(weighted, axis=-1)
    weighted = weighted.astype(bf16)

    key_index = jnp.arange(group_len, dtype=jnp.int32)
    start_row = member * rows
    segment = membership[:, 0]
    row_index = start_row + jnp.arange(rows, dtype=jnp.int32)
    seg_rows = lax.dynamic_slice_in_dim(segment, start_row, rows, axis=1)
    before = jnp.sum((segment[:, None, :] < seg_rows[:, :, None]).astype(jnp.int32), axis=2)
    position = jnp.where(seg_rows == 0, row_index[None], PROMPT + row_index[None] - before)
    allowed = (key_index[None, :, None] <= row_index[None, None, :]) & (
        (segment[:, :, None] == 0) | (segment[:, :, None] == seg_rows[:, None, :])
    )
    bias = jnp.tile(jnp.where(allowed, 0.0, MASKED).astype(f32), (1, 1, step_heads))
    frequency = ROPE_BASE ** (-(jnp.arange(HD // 2, dtype=f32) * 2.0 / HD))
    angles = position.astype(f32).reshape(total)[:, None] * frequency[None, :]
    cosine = jnp.cos(angles)[:, None, :]
    sine_part = jnp.sin(angles)[:, None, :]

    hidden = inputs[:, 0].astype(f32).reshape(total, width)
    scale_in = rms_scale(hidden)
    normed = (hidden * scale_in * gain_in).astype(bf16)
    proj = mm(normed, qkv_w, NT).reshape(total, shards, q_part + k_part + v_part)
    queries = proj[:, :, :q_part].reshape(total, H, HD)
    key_pre = proj[:, :, q_part : q_part + k_part].reshape(total, KVH, HD)
    value = proj[:, :, q_part + k_part :].reshape(total, KVH, HD).astype(bf16)
    scale_q = rms_scale(queries)
    scale_k = rms_scale(key_pre)
    q_low = rotate(queries * scale_q * (gain_q * (SCALE * LOG2E)), cosine, sine_part).astype(bf16)
    q_low = q_low.reshape(micro, rows, H * HD)
    k_low = rotate(key_pre * scale_k * gain_k, cosine, sine_part).astype(bf16)
    kv_own = jnp.concatenate([k_low, value], axis=-1).reshape(micro, rows, KVH * 2 * HD)
    kv_all = lax.all_gather(kv_own, "expert", axis=0, tiled=False)
    chunk = 256
    mixed, logs = run_forward(q_low, kv_all, bias, step_heads, chunk)

    branch = mm(mixed.reshape(total, H * HD), out_w)
    middle = hidden + branch
    scale_mid = rms_scale(middle)
    routed = (middle * scale_mid * gain_mid).astype(bf16).reshape(micro, rows, width)
    middle = middle.reshape(micro, rows, width)
    scale_mid = scale_mid.reshape(micro, rows, 1)

    mix_parts, d_routeds, d_branches, d_middles = [], [], [], []
    acc_gate = acc_up = acc_down = 0.0
    grad_mid = 0.0
    slots = blocks * capacity
    for at in range(micro):
        d_out = d_out_all[:, at]
        tokens = lax.all_gather(routed[at], "expert", axis=0, tiled=False)
        picked = jnp.einsum("ebst,btd->ebsd", pick[at], tokens, preferred_element_type=f32)
        picked = picked.astype(bf16).reshape(local_experts, slots, width)
        d_result = jnp.einsum("ebst,btd->ebsd", pick[at], d_out, preferred_element_type=f32)
        d_result = (d_result * slot_weight[at][..., None]).astype(bf16)
        d_result = d_result.reshape(local_experts, slots, width)
        gate_pre = jnp.einsum("erd,edf->erf", picked, wg, preferred_element_type=f32)
        up_pre = jnp.einsum("erd,edf->erf", picked, wu, preferred_element_type=f32)
        d_hidden = jnp.einsum("erd,efd->erf", d_result, wd, preferred_element_type=f32)
        sigmoid_g = jax.nn.sigmoid(gate_pre)
        silu_g = gate_pre * sigmoid_g
        hidden_low = (silu_g * up_pre).astype(bf16)
        d_gate = (d_hidden * up_pre * sigmoid_g * (1.0 + gate_pre * (1.0 - sigmoid_g))).astype(bf16)
        d_up = (d_hidden * silu_g).astype(bf16)
        d_rows = jnp.einsum("erf,edf->erd", d_gate, wg, preferred_element_type=f32)
        d_rows = d_rows + jnp.einsum("erf,edf->erd", d_up, wu, preferred_element_type=f32)
        d_rows = d_rows.astype(bf16).reshape(local_experts, blocks, capacity, width)
        d_part = jnp.einsum("ebst,ebsd->btd", pick[at], d_rows, preferred_element_type=f32)
        d_part = d_part.astype(bf16).reshape(group_len, width)
        d_routed = lax.psum_scatter(d_part, "expert", scatter_dimension=0, tiled=True).astype(f32)
        result = jnp.einsum("erf,efd->erd", hidden_low, wd, preferred_element_type=f32)
        result = result.astype(bf16).reshape(local_experts, blocks, capacity, width)
        part = jnp.einsum("ebst,ebsd->btd", weighted[at], result, preferred_element_type=f32)
        mix_parts.append(part.astype(bf16).reshape(group_len, width))
        d_routeds.append(d_routed)

        acc_down += jnp.einsum("erf,erd->efd", hidden_low, d_result, preferred_element_type=f32)
        acc_gate += jnp.einsum("erd,erf->edf", picked, d_gate, preferred_element_type=f32)
        acc_up += jnp.einsum("erd,erf->edf", picked, d_up, preferred_element_type=f32)

    scattering = [scatter_far(acc, axis) for acc, axis in ((acc_gate, 1), (acc_up, 1), (acc_down, 2))]
    d_routeds[-1], scattering = lax.optimization_barrier((d_routeds[-1], scattering))
    expert_grads = [scatter_near(*parts) for parts in scattering]
    for at in range(micro):
        d_mid_norm, mid_gain_grad = norm_back(d_routeds[at], middle[at], scale_mid[at], gain_mid)
        grad_mid = grad_mid + mid_gain_grad
        d_middle = cotangent[at, 0].astype(f32) + d_mid_norm
        d_middles.append(d_middle)
        d_branches.append(d_middle.astype(bf16))

    d_branch = jnp.concatenate(d_branches, axis=0)
    d_middle = jnp.concatenate(d_middles, axis=0)
    d_mixed = mm(d_branch, out_w, NT).astype(bf16).reshape(micro, rows, H * HD)
    dq_low, dkv_all = run_backward(q_low, kv_all, bias, mixed, d_mixed, logs, step_heads, chunk)
    mixed_after, dq_low, dkv_all, expert_grads = lax.optimization_barrier(
        (mixed, dq_low, dkv_all, expert_grads)
    )
    grad_output = reduce_rows(mixed_after.reshape(total, H * HD), d_branch, w_output.shape[0], 2, special)
    dkv = lax.psum_scatter(dkv_all, "expert", scatter_dimension=0, tiled=False)
    mix_parts, dkv, grad_output = lax.optimization_barrier((mix_parts, dkv, grad_output))
    outputs = []
    for at in range(micro):
        mix = lax.psum_scatter(mix_parts[at], "expert", scatter_dimension=0, tiled=True)
        outputs.append((middle[at] + mix.astype(f32)).astype(bf16))
    dkv = dkv.reshape(total, KVH, 2 * HD)
    d_query = rotate(dq_low.reshape(total, H, HD).astype(f32), cosine, -sine_part)
    d_query, grad_qn = norm_back(d_query, queries, scale_q, gain_q)
    d_key = rotate(dkv[:, :, :HD].astype(f32), cosine, -sine_part)
    d_key, grad_kn = norm_back(d_key, key_pre, scale_k, gain_k)
    d_proj = jnp.concatenate(
        [
            d_query.astype(bf16).reshape(total, shards, q_part),
            d_key.astype(bf16).reshape(total, shards, k_part),
            dkv[:, :, HD:].reshape(total, shards, v_part),
        ],
        axis=-1,
    ).reshape(total, -1)
    grad_qkv = reduce_rows(d_proj, normed, q_part + k_part + v_part, 3, special)
    d_normed = mm(d_proj, qkv_w)
    d_in_norm, grad_in = norm_back(d_normed, hidden, scale_in, gain_in)
    input_grad = d_middle + d_in_norm

    gain_grads = jnp.concatenate([grad_in, grad_mid, grad_qn, grad_kn]).reshape(shards, gain_len)
    gain_grads = jnp.pad(gain_grads, ((0, 0), (0, 256 - gain_len % 256)))
    gain_all = lax.all_gather(gain_grads, BOTH, axis=0, tiled=False)
    grad_gains = jnp.sum(lax.dynamic_index_in_dim(gain_all, shard_at, axis=1, keepdims=False), axis=0)
    return (
        jnp.stack(outputs)[:, None],
        input_grad.reshape(micro, 1, rows, width),
        grad_qkv[:q_part].T,
        grad_qkv[q_part : q_part + k_part].T,
        grad_qkv[q_part + k_part :].T,
        grad_output,
        grad_gains[:gain_len],
        *expert_grads,
    )


def solution(mesh):
    return jax.shard_map(
        body,
        mesh=mesh,
        in_specs=(
            P(None, "dp", "expert", None),
            P(None, "dp", "expert", None),
            P(None, "dp", None),
            P(None, "dp", "expert", None),
            P(None, "dp", "expert", None),
            P(None, "dp", "expert", None),
            P(None, ("dp", "expert")),
            P(None, ("dp", "expert")),
            P(None, ("dp", "expert")),
            P(("dp", "expert"), None),
            P(("dp", "expert")),
            P("expert", "dp", None),
            P("expert", "dp", None),
            P("expert", None, "dp"),
        ),
        out_specs=(
            P(None, "dp", "expert", None),
            P(None, "dp", "expert", None),
            P(None, ("dp", "expert")),
            P(None, ("dp", "expert")),
            P(None, ("dp", "expert")),
            P(("dp", "expert"), None),
            P(("dp", "expert")),
            P("expert", "dp", None),
            P("expert", "dp", None),
            P("expert", None, "dp"),
        ),
        check_vma=False,
    )
```

```python
import functools
import math

import jax
import jax.numpy as jnp
from jax import lax
from jax.experimental import pallas as pl
from jax.experimental.pallas import tpu as pltpu
from jax.sharding import PartitionSpec as P

H = 32
KVH = 4
HD = 128
FF = 768
TOPK = 8
PROMPT = 1024
PER_KV = H // KVH

EPSILON = 1e-06
ROPE_BASE = 1000000.0
MASKED = -1e30
LOG2E = math.log2(math.e)
SCALE = HD ** (-0.5)

bf16 = jnp.bfloat16
f32 = jnp.float32
NT = (((1,), (1,)), ((), ()))
TN = (((0,), (0,)), ((), ()))
NN = (((1,), (0,)), ((), ()))
BOTH = ("dp", "expert")
VMEM_LIMIT = 56 * 1024 * 1024


def mm(a, b, dims=NN):
    return lax.dot_general(a, b, dims, preferred_element_type=f32)


def rms_scale(values):
    return lax.rsqrt(jnp.mean(values * values, axis=-1, keepdims=True) + EPSILON)


def norm_back(upstream, values, inv_rms, norm_gain):
    lifted = upstream * norm_gain
    inner_dot = jnp.mean(lifted * values, axis=-1, keepdims=True)
    back_grad = inv_rms * lifted - values * (inv_rms * inv_rms * inv_rms) * inner_dot
    gain_grad = jnp.sum((upstream * values * inv_rms).reshape(-1, values.shape[-1]), axis=0)
    return (back_grad, gain_grad)


def rotate(values, cosine, sine_part):
    half_dim = values.shape[-1] // 2
    first_half = values[..., :half_dim]
    second_half = values[..., half_dim:]
    return jnp.concatenate(
        [
            first_half * cosine - second_half * sine_part,
            second_half * cosine + first_half * sine_part,
        ],
        axis=-1,
    )


def attend_forward(step_heads, chunk, q_ref, kv_ref, bias_ref, o_ref, log_ref):
    group_len = bias_ref.shape[1]
    keys = kv_ref[:, 0, :, :HD].reshape(group_len, HD)
    values_t = kv_ref[:, 0, :, HD:].reshape(group_len, HD).T
    rows = q_ref.shape[1]
    for step in range(PER_KV // step_heads):
        heads = range(step * step_heads, (step + 1) * step_heads)
        query = jnp.concatenate([q_ref[0, :, h * HD : (h + 1) * HD] for h in heads], axis=0)
        mixed, row_sum = 0.0, 0.0
        for at in range(0, group_len, chunk):
            scores = mm(keys[at : at + chunk], query, NT)
            prob = jnp.exp2(scores + bias_ref[0, at : at + chunk, :])
            row_sum += jnp.sum(prob, axis=0, keepdims=True)
            mixed += mm(values_t[:, at : at + chunk], prob.astype(bf16))
        out = (mixed / row_sum).T.astype(bf16)
        for i, h in enumerate(heads):
            o_ref[0, :, h * HD : (h + 1) * HD] = out[i * rows : (i + 1) * rows]
        log_ref[0, 0, step : step + 1, :] = jnp.log2(row_sum)


def attend_backward(
    step_heads, chunk, q_ref, kv_ref, bias_ref, o_ref, do_ref, log_ref, dq_ref, dkv_ref, dk_acc, dv_acc
):
    group_len = bias_ref.shape[1]
    keys = kv_ref[:, 0, :, :HD].reshape(group_len, HD)
    values = kv_ref[:, 0, :, HD:].reshape(group_len, HD)
    keys_t = keys.T
    rows = q_ref.shape[1]
    dk_acc[...] = jnp.zeros_like(dk_acc)
    dv_acc[...] = jnp.zeros_like(dv_acc)
    for step in range(PER_KV // step_heads):
        heads = range(step * step_heads, (step + 1) * step_heads)
        query = jnp.concatenate([q_ref[0, :, h * HD : (h + 1) * HD] for h in heads], axis=0)
        grad = jnp.concatenate([do_ref[0, :, h * HD : (h + 1) * HD] for h in heads], axis=0)
        mixed = jnp.concatenate([o_ref[0, :, h * HD : (h + 1) * HD] for h in heads], axis=0)
        row_dot = jnp.sum((grad.astype(f32) * mixed.astype(f32)).T, axis=0, keepdims=True)
        log_sum = log_ref[0, 0, step : step + 1, :]
        dq_t = 0.0
        for at in range(0, group_len, chunk):
            part = slice(at, at + chunk)
            scores = mm(keys[part], query, NT)
            prob = jnp.exp2(scores + (bias_ref[0, part, :] - log_sum))
            d_prob = mm(values[part], grad, NT)
            d_score = (prob * (d_prob - row_dot)).astype(bf16)
            dv_acc[part] += mm(prob.astype(bf16), grad)
            dk_acc[part] += mm(d_score, query)
            dq_t += mm(keys_t[:, part], d_score)
        out = (dq_t * SCALE).T.astype(bf16)
        for i, h in enumerate(heads):
            dq_ref[0, :, h * HD : (h + 1) * HD] = out[i * rows : (i + 1) * rows]
    blocks = dkv_ref.shape[0]
    dkv_ref[:, 0, :, :HD] = (dk_acc[...] * (1.0 / LOG2E)).astype(bf16).reshape(blocks, rows, HD)
    dkv_ref[:, 0, :, HD:] = dv_acc[...].astype(bf16).reshape(blocks, rows, HD)


def attention_specs(micro, rows, group_len, blocks, step_heads):
    wide = PER_KV * HD
    q_spec = pl.BlockSpec((1, rows, wide), lambda b, g: (b, 0, g))
    kv_spec = pl.BlockSpec((blocks, 1, rows, 2 * HD), lambda b, g: (0, b, 0, g))
    bias_spec = pl.BlockSpec((1, group_len, step_heads * rows), lambda b, g: (b, 0, 0))
    log_spec = pl.BlockSpec((1, 1, PER_KV // step_heads, step_heads * rows), lambda b, g: (b, g, 0, 0))
    return q_spec, kv_spec, bias_spec, log_spec


def run_forward(query, kv_all, bias, step_heads, chunk):
    micro, rows, _ = query.shape
    blocks = kv_all.shape[0]
    group_len = bias.shape[1]
    q_spec, kv_spec, bias_spec, log_spec = attention_specs(micro, rows, group_len, blocks, step_heads)
    flops = 4 * micro * rows * H * HD * group_len
    return pl.pallas_call(
        functools.partial(attend_forward, step_heads, chunk),
        grid=(micro, KVH),
        in_specs=[q_spec, kv_spec, bias_spec],
        out_specs=[q_spec, log_spec],
        out_shape=[
            jax.ShapeDtypeStruct(query.shape, bf16),
            jax.ShapeDtypeStruct((micro, KVH, PER_KV // step_heads, step_heads * rows), f32),
        ],
        compiler_params=pltpu.CompilerParams(vmem_limit_bytes=VMEM_LIMIT),
        cost_estimate=pl.CostEstimate(
            flops=flops, bytes_accessed=20_000_000, transcendentals=flops // (4 * HD)
        ),
    )(query, kv_all, bias)


def run_backward(query, kv_all, bias, mixed, grad, logs, step_heads, chunk):
    micro, rows, _ = query.shape
    blocks = kv_all.shape[0]
    group_len = bias.shape[1]
    q_spec, kv_spec, bias_spec, log_spec = attention_specs(micro, rows, group_len, blocks, step_heads)
    flops = 10 * micro * rows * H * HD * group_len
    return pl.pallas_call(
        functools.partial(attend_backward, step_heads, chunk),
        grid=(micro, KVH),
        in_specs=[q_spec, kv_spec, bias_spec, q_spec, q_spec, log_spec],
        out_specs=[q_spec, kv_spec],
        out_shape=[
            jax.ShapeDtypeStruct(query.shape, bf16),
            jax.ShapeDtypeStruct(kv_all.shape, bf16),
        ],
        scratch_shapes=[pltpu.VMEM((group_len, HD), f32), pltpu.VMEM((group_len, HD), f32)],
        compiler_params=pltpu.CompilerParams(vmem_limit_bytes=VMEM_LIMIT),
        cost_estimate=pl.CostEstimate(
            flops=flops, bytes_accessed=30_000_000, transcendentals=flops // (10 * HD)
        ),
    )(query, kv_all, bias, mixed, grad, logs)


MESH = pl.DeviceIdType.MESH


def gather_kernel(phases, count, *refs):
    ins, outs, sems = refs[:count], refs[count : 2 * count], refs[2 * count :]
    dp = lax.axis_index("dp"); member = lax.axis_index("expert")
    blocks = lax.axis_size("expert")
    core = member % 2; z = member // 2
    depth = blocks // 2
    sibling = (dp, member + 1 - 2 * core)
    by_x = (dp + 1 - 2 * (dp % 2), member)
    by_y = ((dp + 2) % 4, member)
    x_at, y_at, far_at = by_x[0], by_y[0], 3 - dp
    above, below = (dp, member + 2), (dp, member - 2)
    barrier = pltpu.get_barrier_semaphore()
    peers = [(sibling, None), (by_x, None), (by_y, None), (above, z < depth - 1), (below, z > 0)]
    for peer, ok in peers:
        if ok is None:
            pl.semaphore_signal(barrier, inc=1, device_id=peer, device_id_type=MESH)
        else:
            @pl.when(ok)
            def _(peer=peer):
                pl.semaphore_signal(barrier, inc=1, device_id=peer, device_id_type=MESH)
    @pl.when((z == 0) | (z == depth - 1))
    def _(): pl.semaphore_wait(barrier, 4)
    @pl.when((z > 0) & (z < depth - 1))
    def _(): pl.semaphore_wait(barrier, 5)

    def guarded(ok, run):
        if ok is None: run()
        else: pl.when(ok)(run)

    class Item:
        pass

    def make(i):
        src, out = ins[i], outs[i]
        rows = src.shape[0]
        half = rows // 2
        (own_sem, sz, rz, sxy, rxy, sc, rc) = sems[i * 7 : (i + 1) * 7]
        def at(d, s, lo=0, n=rows):
            return out.at[pl.ds(pl.multiple_of((d * blocks + s * 2 + core) * rows + lo, 16 if half % 16 == 0 else 8), n)]
        def copy(a, b, ss, rs, to):
            return pltpu.make_async_remote_copy(src_ref=a, dst_ref=b, send_sem=ss, recv_sem=rs, device_id=to, device_id_type=MESH)
        def block(d, s):
            return at(d, s)
        it = Item()
        def local():
            return pltpu.make_async_copy(src, at(dp, z), own_sem)
        def up(s, ref): return copy(ref, at(dp, s), sz.at[0, s], rz.at[s], above)
        def down(s, ref): return copy(ref, at(dp, s), sz.at[1, s], rz.at[s], below)
        def to_x(s, ref): return copy(ref, at(dp, s), sxy.at[0, s], rxy.at[0, s], by_x)
        def to_y(s, ref): return copy(ref, at(dp, s), sxy.at[1, s], rxy.at[1, s], by_y)
        def half_y(s):
            return copy(at(x_at, s, 0, half), at(x_at, s, 0, half), sxy.at[2, s], rxy.at[2, s], by_y)
        def half_x(s):
            return copy(at(y_at, s, half, half), at(y_at, s, half, half), sxy.at[3, s], rxy.at[3, s], by_x)
        def to_core(r, d, s, ref): return copy(ref, at(d, s), sc.at[r, s], rc.at[r, s], sibling)
        def spread(s, ref):
            to_x(s, ref).start(); to_y(s, ref).start(); to_core(0, dp, s, ref).start()
        def start():
            local().start()
            guarded(z < depth - 1, lambda: up(z, src).start())
            guarded(z > 0, lambda: down(z, src).start())
            spread(z, src)
        def z_event(s, ok, rising):
            def run():
                up(s, at(dp, s)).wait_recv()
                if rising: guarded(z < depth - 1, lambda: up(s, at(dp, s)).start())
                else: guarded(z > 0, lambda: down(s, at(dp, s)).start())
                spread(s, at(dp, s))
            pl.when(ok)(run)
        def near_event(s, ok):
            def run():
                to_x(s, at(dp, s)).wait_recv()
                half_y(s).start()
                to_core(1, x_at, s, at(x_at, s)).start()
                to_y(s, at(dp, s)).wait_recv()
                half_x(s).start()
                to_core(2, y_at, s, at(y_at, s)).start()
            guarded(ok, run)
        def far_event(s, ok):
            def run():
                half_y(s).wait_recv(); half_x(s).wait_recv()
                to_core(3, far_at, s, at(far_at, s)).start()
            guarded(ok, run)
        def core_wait(s):
            for r, d in enumerate((dp, x_at, y_at, far_at)):
                to_core(r, d, s, at(d, s)).wait_recv()
        def finish():
            local().wait()
            for s in range(depth):
                for c in (to_x(s, at(dp, s)), to_y(s, at(dp, s)), half_y(s), half_x(s)): c.wait_send()
                for r, d in enumerate((dp, x_at, y_at, far_at)): to_core(r, d, s, at(d, s)).wait_send()
                guarded((z >= s) & (z < depth - 1), lambda: up(s, at(dp, s)).wait_send())
                guarded((z <= s) & (z > 0), lambda: down(s, at(dp, s)).wait_send())
        it.start, it.z_event, it.near_event, it.far_event, it.core_wait, it.finish = start, z_event, near_event, far_event, core_wait, finish
        return it
    items = [make(i) for i in range(count)]
    def around(d):
        if d == 0: return [(z, None, True)]
        return [(z - d, z >= d, True), (z + d, z + d < depth, False)]
    for n, phase in enumerate(phases):
        its = [items[i] for i in phase]
        for it in its: it.start()
        for d in range(1, depth + 2):
            if d < depth:
                for s, ok, rising in around(d):
                    for it in its: it.z_event(s, ok, rising)
            if d - 1 < depth:
                for s, ok, _ in around(d - 1):
                    for it in its: it.near_event(s, ok)
            if d - 2 >= 0:
                for s, ok, _ in around(d - 2):
                    for it in its: it.far_event(s, ok)
            if n + 1 < len(phases) and d == depth: pass
    for it in items:
        for s in range(depth): it.core_wait(s)
    for it in items: it.finish()

def gather_rows(arrays, phases, cid):
    shards = lax.axis_size("dp") * lax.axis_size("expert")
    depth = lax.axis_size("expert") // 2
    D = pltpu.SemaphoreType.DMA
    sems = []
    for _ in arrays:
        sems += [D, D((2, depth)), D((depth,)), D((4, depth)), D((4, depth)), D((4, depth)), D((4, depth))]
    return pl.pallas_call(
        functools.partial(gather_kernel, phases, len(arrays)),
        out_shape=[jax.ShapeDtypeStruct((shards * a.shape[0],) + a.shape[1:], a.dtype) for a in arrays],
        in_specs=[pl.BlockSpec(memory_space=pl.ANY)] * len(arrays),
        out_specs=[pl.BlockSpec(memory_space=pl.ANY)] * len(arrays),
        scratch_shapes=sems,
        compiler_params=pltpu.CompilerParams(collective_id=cid, has_side_effects=True),
        cost_estimate=pl.CostEstimate(flops=0, bytes_accessed=400_000_000, transcendentals=0),
    )(*arrays)


def reduce_kernel(rows, cuts, a_ref, b_ref, g_ref, o_ref, go_ref, sib, got, own, far, near, plane, got_z,
                  s0, r0, s1, r1, s2, r2, s3, r3, g_acc, g_got, g_z, gs, gr, gsz, grz):
    dp = lax.axis_index("dp"); member = lax.axis_index("expert")
    core = member % 2; z = member // 2
    sibling = (dp, member + 1 - 2 * core)
    by_x = (dp + 1 - 2 * (dp % 2), member)
    by_y = ((dp + 2) % 4, member)
    x_at, y_at = by_x[0], by_y[0]
    far_at = 3 - dp
    half = rows // 2
    depth = lax.axis_size("expert") // 2
    barrier = pltpu.get_barrier_semaphore()
    peers = [sibling, by_x, by_y] + [(dp, ((z + d) % depth) * 2 + core) for d in range(1, depth)]
    for peer in peers:
        pl.semaphore_signal(barrier, inc=1, device_id=peer, device_id_type=MESH)
    pl.semaphore_wait(barrier, len(peers))

    def pick(table):
        at = table[depth-1]
        for i in range(depth - 1):
            at = jnp.where(z == i, table[i], at)
        return at
    orders = [[3, 3, 0, 0], [2, 0, 3, 1], [1, 2, 1, 2], [0, 1, 2, 3]]
    targets = [pick(t) for t in orders]
    wide = 4 * rows
    cols = b_ref.shape[1] // cuts

    def copy(src, dst, ssem, rsem, to):
        return pltpu.make_async_remote_copy(src_ref=src, dst_ref=dst, send_sem=ssem, recv_sem=rsem, device_id=to, device_id_type=MESH)

    def product(half_of, k, put):
        base = (half_of * depth + targets[k]) * wide
        def step(i, _):
            at = (i // cuts) * rows
            col = pl.multiple_of((i % cuts) * cols, cols)
            part = jnp.dot(a_ref[pl.ds(pl.multiple_of(base + at, 16), rows), :], b_ref[:, pl.ds(col, cols)], preferred_element_type=f32)
            put(pl.ds(pl.multiple_of(at, 16), rows), pl.ds(col, cols), part)
            return 0
        lax.fori_loop(0, 4 * cuts, step, 0)

    def gain_hop(i, src, to):
        return copy(src, g_got.at[i, pl.ds(0, src.shape[0])], gs.at[i], gr.at[i], to)
    hops = {}
    def gain_step(i):
        rows4 = lambda at: pl.ds(pl.multiple_of(at * 8, 8), 8)
        if i == 0:
            hops[0] = gain_hop(0, g_ref.at[pl.ds(pl.multiple_of((1 - core) * 32, 32), 32)], sibling)
        elif i == 1:
            hops[0].wait_recv()
            g_acc[...] = g_ref[pl.ds(pl.multiple_of(core * 32, 32), 32)] + g_got[0]
            hops[1] = gain_hop(1, g_acc.at[pl.ds(pl.multiple_of((1 - dp // 2) * 16, 16), 16)], by_y)
        elif i == 2:
            hops[1].wait_recv()
            mine = pl.ds(pl.multiple_of((dp // 2) * 16, 16), 16)
            g_acc[mine] += g_got[1, :16]
            hops[2] = gain_hop(2, g_acc.at[rows4(x_at)], by_x)
        elif i == 3:
            hops[2].wait_recv()
            g_acc[rows4(dp)] += g_got[2, :8]
            for d in range(1, depth):
                to = (z + d) % depth
                hops[2 + d] = copy(g_acc.at[pl.ds(dp * 8 + to, 1)], g_z.at[z], gsz.at[d - 1], grz.at[z], (dp, to * 2 + core))
        if i < 3:
            hops[i].start()
        else:
            for d in range(1, depth):
                hops[2 + d].start()
    def gain_end():
        total = g_acc[pl.ds(dp * 8 + z, 1)]
        for d in range(1, depth):
            src = (z + d) % depth
            copy(g_acc.at[pl.ds(dp * 8, 1)], g_z.at[src], gsz.at[0], grz.at[src], sibling).wait_recv()
            total += g_z[src]
        go_ref[...] = total
        for i in hops:
            hops[i].wait_send()
    sib_copies, far_copies, near_copies, z_copies = {}, {}, {}, {}
    def sib_step(k):
        slot = k % 2
        if k >= 2:
            sib_copies[k - 2].wait_send()
        def put(r, c, part):
            sib[slot, r, c] = part.astype(bf16)
        product(1 - core, k, put)
        sib_copies[k] = copy(sib.at[slot], got.at[k], s0.at[slot], r0.at[k], sibling)
        sib_copies[k].start()
    def blk(at):
        return pl.ds(pl.multiple_of(at * rows, 16), rows)
    def own_step(k):
        sib_copies[k].wait_recv()
        def put(r, c, part):
            own[k, r, c] = (part + got[k, r, c].astype(f32)).astype(bf16)
        product(core, k, put)
        base = pl.multiple_of(far_at * rows, 16)
        far_copies[k] = (
            copy(own.at[k, pl.ds(base, half)], far.at[k, 0], s1.at[k, 0], r1.at[k, 0], by_x),
            copy(own.at[k, pl.ds(pl.multiple_of(base + half, 16), half)], far.at[k, 1], s1.at[k, 1], r1.at[k, 1], by_y),
        )
        for c in far_copies[k]: c.start()
    def near_step(k):
        a, b = far_copies[k]
        a.wait_recv()
        rng = pl.ds(pl.multiple_of(y_at * rows, 16), half)
        own[k, rng] = (own[k, rng].astype(f32) + far[k, 0].astype(f32)).astype(bf16)
        to_y = copy(own.at[k, blk(y_at)], near.at[k, 1], s2.at[k, 1], r2.at[k, 1], by_y)
        to_y.start()
        b.wait_recv()
        rng = pl.ds(pl.multiple_of(x_at * rows + half, 16), half)
        own[k, rng] = (own[k, rng].astype(f32) + far[k, 1].astype(f32)).astype(bf16)
        to_x = copy(own.at[k, blk(x_at)], near.at[k, 0], s2.at[k, 0], r2.at[k, 0], by_x)
        to_x.start()
        near_copies[k] = (to_x, to_y)
    def plane_step(k):
        for c in near_copies[k]: c.wait_recv()
        total = own[k, blk(dp)].astype(f32) + near[k, 0].astype(f32) + near[k, 1].astype(f32)
        if k < depth - 1:
            plane[k] = total.astype(bf16)
            to = (dp, targets[k] * 2 + core)
            z_copies[k] = copy(plane.at[k], got_z.at[z], s3.at[k], r3.at[z], to)
            z_copies[k].start()
        else:
            o_ref[...] = total
    gain_step(0)
    sib_step(0); sib_step(1)
    own_step(0)
    gain_step(1)
    sib_step(2)
    own_step(1)
    gain_step(2)
    near_step(0)
    sib_step(3)
    own_step(2)
    gain_step(3)
    near_step(1)
    plane_step(0)
    own_step(3)
    near_step(2)
    plane_step(1)
    near_step(3)
    plane_step(2)
    plane_step(3)
    for d in range(1, depth):
        src = (z + d) % depth
        copy(plane.at[0], got_z.at[src], s3.at[0], r3.at[src], sibling).wait_recv()
        o_ref[...] += got_z[src].astype(f32)
    gain_end()
    for k in range(depth):
        if k >= 2: sib_copies[k].wait_send()
        for c in far_copies[k]: c.wait_send()
        for c in near_copies[k]: c.wait_send()
        if k < depth - 1: z_copies[k].wait_send()

def reduce_rows(a, b, rows, cid, gains=None):
    tokens, width = b.shape
    depth = 4
    at = a.reshape(tokens, 4, depth, 2, rows).transpose(3, 2, 1, 4, 0).reshape(-1, tokens)
    D = pltpu.SemaphoreType.DMA
    lanes = 256
    padded = jnp.zeros((32, lanes), f32)
    if gains is not None:
        padded = jnp.pad(gains, ((0, 0), (0, lanes - gains.shape[1])))
    padded = padded.reshape(4, depth, 2, lanes).transpose(2, 0, 1, 3)
    padded = jnp.pad(padded, ((0, 0), (0, 0), (0, 8 - depth), (0, 0))).reshape(64, lanes)
    return pl.pallas_call(
        functools.partial(reduce_kernel, rows, 4),
        out_shape=[jax.ShapeDtypeStruct((rows, width), f32), jax.ShapeDtypeStruct((1, lanes), f32)],
        in_specs=[pl.BlockSpec(memory_space=pltpu.VMEM)] * 3,
        out_specs=[pl.BlockSpec(memory_space=pltpu.VMEM)] * 2,
        scratch_shapes=[
            pltpu.VMEM((2, 4 * rows, width), bf16),
            pltpu.VMEM((depth, 4 * rows, width), bf16),
            pltpu.VMEM((depth, 4 * rows, width), bf16),
            pltpu.VMEM((depth, 2, rows // 2, width), bf16),
            pltpu.VMEM((depth, 2, rows, width), bf16),
            pltpu.VMEM((depth - 1, rows, width), bf16),
            pltpu.VMEM((depth, rows, width), bf16),
            D((2,)), D((depth,)), D((depth, 2)), D((depth, 2)), D((depth, 2)), D((depth, 2)), D((depth - 1,)), D((depth,)),
            pltpu.VMEM((32, lanes), f32), pltpu.VMEM((3, 32, lanes), f32), pltpu.VMEM((depth, 1, lanes), f32),
            D((3,)), D((3,)), D((depth - 1,)), D((depth,)),
        ],
        compiler_params=pltpu.CompilerParams(vmem_limit_bytes=60*1024*1024, collective_id=cid, has_side_effects=True),
        cost_estimate=pl.CostEstimate(flops=2*tokens*32*rows*width, bytes_accessed=10_000_000, transcendentals=0),
    )(at, b, padded)


ROUTE_LANES = 128


def picks_of(routing, first, local_experts, capacity):
    rows = routing.shape[0]
    lanes = lax.broadcasted_iota(jnp.int32, (rows, ROUTE_LANES), 1)
    places = lax.broadcasted_iota(jnp.int32, (rows, local_experts * capacity), 1)
    hit, weighted = None, 0.0
    for e in range(local_experts):

        def column(base):
            return jnp.sum(jnp.where(lanes == base + first + e, routing, 0.0), axis=1, keepdims=True)

        slot = column(0).astype(jnp.int32)
        here = places == jnp.where(slot >= 0, slot + e * capacity, -1)
        hit = here if hit is None else hit | here
        weighted = weighted + jnp.where(here, column(32) + column(64), 0.0)
    return jnp.where(hit, 1.0, 0.0).astype(bf16), weighted.astype(bf16)


def pick_kernel(capacity, local_experts, n_alias, tok_ref, cot_ref, *refs):
    x_ref, dy_ref = refs[n_alias:]
    width = tok_ref.shape[2]
    first = lax.axis_index("expert") * local_experts
    routing = cot_ref[0, :, width:]
    hit, _ = picks_of(routing.astype(f32), first, local_experts, capacity)
    x = mm(hit, tok_ref[0], TN).astype(bf16)
    rows = mm(hit, routing, TN)
    lanes = lax.broadcasted_iota(jnp.int32, rows.shape, 1)
    owner = lax.broadcasted_iota(jnp.int32, rows.shape, 0) // capacity
    at = lanes - first - owner
    weight = jnp.sum(jnp.where((at == 32) | (at == 64), rows, 0.0), axis=1, keepdims=True)
    dy = (mm(hit, cot_ref[0, :, :width], TN) * weight).astype(bf16)
    for e in range(local_experts):
        x_ref[e, 0, 0] = x[e * capacity : (e + 1) * capacity]
        dy_ref[e, 0, 0] = dy[e * capacity : (e + 1) * capacity]


def expert_kernel(n_alias, *refs):
    x_ref, dy_ref = refs[:2]
    parts = (refs[2:7], refs[7:12], refs[12:17])
    z_ref, dg_ref, du_ref, y_ref, dx_ref, wg, wu, wd, sems = refs[17 + n_alias :]
    local_experts, width, _ = wg.shape
    at = lax.axis_index("dp")
    size = width // 4
    places = (at, at + 1 - 2 * (at % 2), (at + 2) % 4, 3 - at, 3 - at)

    def copies(e):
        out = []
        for m, full in enumerate((wg, wu, wd)):
            for p in range(4):
                part = parts[m][p] if p < 3 else parts[m][3 + e]
                src = part.at[e] if p < 3 else part.at[0]
                where = pl.ds(pl.multiple_of(places[p] * size, size), size)
                dst = full.at[e, where, :] if m < 2 else full.at[e, :, where]
                out.append(pltpu.make_async_copy(src, dst, sems.at[e, m, p]))
        return out

    expert, chunk = pl.program_id(0), pl.program_id(1)

    @pl.when((expert == 0) & (chunk == 0))
    def _():
        for e in range(local_experts):
            for c in copies(e):
                c.start()

    for e in range(local_experts):

        @pl.when((expert == e) & (chunk == 0))
        def _(e=e):
            for c in copies(e):
                c.wait()

    x, dy = x_ref[0, 0], dy_ref[0, 0]
    gate = mm(x, wg[expert])
    up = mm(x, wu[expert])
    d_hidden = mm(dy, wd[expert], NT)
    sig = 1.0 / (1.0 + jnp.exp(-gate))
    silu = gate * sig
    z = (silu * up).astype(bf16)
    d_gate = (d_hidden * up * sig * (1.0 + gate * (1.0 - sig))).astype(bf16)
    d_up = (d_hidden * silu).astype(bf16)
    z_ref[0, 0] = z
    dg_ref[0, 0] = d_gate
    du_ref[0, 0] = d_up
    dx_ref[0] = (mm(d_gate, wg[expert], NT) + mm(d_up, wu[expert], NT)).astype(bf16)
    y_ref[0] = mm(z, wd[expert]).astype(bf16)


def sum_kernel(capacity, routing_ref, y_ref, dx_ref, mix_ref, da_ref):
    local_experts, _, _, width = y_ref.shape
    first = lax.axis_index("expert") * local_experts
    hit, weighted = picks_of(routing_ref[0].astype(f32), first, local_experts, capacity)
    da_ref[...] = mm(hit, dx_ref[...].reshape(local_experts * capacity, width)).astype(bf16)
    mix_ref[...] = mm(weighted, y_ref[...].reshape(local_experts * capacity, width)).astype(bf16)


def run_experts(tokens, cot, parts, capacity, batch_at, micro, earlier):
    blocks, rows, width = tokens.shape
    local_experts, _, hidden = parts[0][0].shape
    flat = [p for group in parts for p in group]
    any_spec = pl.BlockSpec(memory_space=pl.ANY)
    params = pltpu.CompilerParams(vmem_limit_bytes=VMEM_LIMIT)
    slots = blocks * capacity
    picked_spec = pl.BlockSpec((local_experts, 1, 1, capacity, width), lambda b: (0, batch_at, b, 0, 0))
    picked = jax.ShapeDtypeStruct((local_experts, micro, blocks, capacity, width), bf16)
    x, dy = pl.pallas_call(
        functools.partial(pick_kernel, capacity, local_experts, len(earlier[:2])),
        grid=(blocks,),
        in_specs=[
            pl.BlockSpec((1, rows, width), lambda b: (b, 0, 0)),
            pl.BlockSpec((1, rows, cot.shape[2]), lambda b: (b, 0, 0)),
        ]
        + [any_spec] * len(earlier[:2]),
        out_specs=[picked_spec] * 2,
        out_shape=[picked] * 2,
        input_output_aliases={2 + i: i for i in range(len(earlier[:2]))},
        compiler_params=params,
        cost_estimate=pl.CostEstimate(
            flops=4 * slots * local_experts * rows * width, bytes_accessed=25_000_000, transcendentals=0
        ),
    )(tokens, cot, *[a.reshape(picked.shape) for a in earlier[:2]])
    x, dy = (a.reshape(local_experts, micro, slots, width) for a in (x, dy))
    chunk = slots // 2
    row_spec = pl.BlockSpec((1, 1, chunk, width), lambda e, i: (e, batch_at, i, 0))
    hid_spec = pl.BlockSpec((1, 1, chunk, hidden), lambda e, i: (e, batch_at, i, 0))
    out_spec = pl.BlockSpec((1, chunk, width), lambda e, i: (e, i, 0))
    hid = jax.ShapeDtypeStruct((local_experts, micro, slots, hidden), bf16)
    out = jax.ShapeDtypeStruct((local_experts, slots, width), bf16)
    z, dg, du, y, dx = pl.pallas_call(
        functools.partial(expert_kernel, len(earlier[2:])),
        grid=(local_experts, 2),
        in_specs=[row_spec, row_spec] + [any_spec] * (len(flat) + len(earlier[2:])),
        out_specs=[hid_spec] * 3 + [out_spec] * 2,
        out_shape=[hid] * 3 + [out] * 2,
        input_output_aliases={2 + len(flat) + i: i for i in range(len(earlier[2:]))},
        scratch_shapes=[
            pltpu.VMEM((local_experts, width, hidden), bf16),
            pltpu.VMEM((local_experts, width, hidden), bf16),
            pltpu.VMEM((local_experts, hidden, width), bf16),
            pltpu.SemaphoreType.DMA((local_experts, 3, 4)),
        ],
        compiler_params=params,
        cost_estimate=pl.CostEstimate(
            flops=12 * local_experts * slots * width * hidden, bytes_accessed=50_000_000, transcendentals=0
        ),
    )(x, dy, *flat, *earlier[2:])
    y, dx = (a.reshape(local_experts, blocks, capacity, width) for a in (y, dx))
    part_spec = pl.BlockSpec((local_experts, 1, capacity, width), lambda b: (0, b, 0, 0))
    sums = jax.ShapeDtypeStruct((blocks * rows, width), bf16)
    sums_spec = pl.BlockSpec((rows, width), lambda b: (b, 0))
    mix, da = pl.pallas_call(
        functools.partial(sum_kernel, capacity),
        grid=(blocks,),
        in_specs=[
            pl.BlockSpec((1, rows, ROUTE_LANES), lambda b: (b, 0, width // ROUTE_LANES)),
            part_spec,
            part_spec,
        ],
        out_specs=[sums_spec] * 2,
        out_shape=[sums] * 2,
        compiler_params=params,
        cost_estimate=pl.CostEstimate(
            flops=4 * slots * local_experts * rows * width, bytes_accessed=25_000_000, transcendentals=0
        ),
    )(cot, y, dx)
    return [x, dy, z, dg, du], mix, da


def slots_of(route_ids, gate_vals, ranking, capacity, experts):
    rows = route_ids.shape[0]
    pair_experts = route_ids.reshape(-1)
    earlier = (pair_experts[None, :] == pair_experts[:, None]) & (
        ranking[None, :] < ranking[:, None]
    )
    slot = jnp.sum(earlier.astype(jnp.int32), axis=1).reshape(rows, -1)
    kept = slot < capacity
    chosen = route_ids[:, :, None] == jnp.arange(experts, dtype=jnp.int32)[None, None, :]
    chosen = chosen & kept[:, :, None]
    slot_map = jnp.sum(jnp.where(chosen, slot[:, :, None] + 1, 0), axis=1).astype(f32) - 1.0
    weight_map = jnp.sum(jnp.where(chosen, gate_vals[:, :, None], 0.0), axis=1)
    return slot_map, weight_map


def swap(values, bit):
    return lax.ppermute(values, "dp", [(i, i ^ bit) for i in range(lax.axis_size("dp"))])


def scatter_far(total, axis):
    at = lax.axis_index("dp")
    size = total.shape[axis] // 4

    def part(bits):
        return lax.dynamic_slice_in_dim(total, (at ^ bits) * size, size, axis=axis)

    far = part(3)
    return [swap(far[:1], 1), swap(far[1:], 2), part(1), part(2), part(0)]


def scatter_near(for_y, for_x, near_x, near_y, own):
    half_y = (near_y[:1].astype(f32) + for_y.astype(f32)).astype(bf16)
    half_x = (near_x[1:].astype(f32) + for_x.astype(f32)).astype(bf16)
    near_y = jnp.concatenate([half_y, near_y[1:]], axis=0)
    near_x = jnp.concatenate([near_x[:1], half_x], axis=0)
    by_x, by_y = swap(near_x, 1), swap(near_y, 2)
    return own.astype(f32) + by_x.astype(f32) + by_y.astype(f32)


def body_plain(
    inputs,
    cotangent,
    membership,
    routes,
    gate_weights,
    pair_order,
    w_query,
    w_key,
    w_value,
    w_output,
    norm_gains,
    w_gate,
    w_up,
    w_down,
):
    micro = inputs.shape[0]
    rows = inputs.shape[2]
    width = inputs.shape[3]
    group_len = membership.shape[2]
    member = lax.axis_index("expert")
    blocks = lax.axis_size("expert")
    shards = blocks * lax.axis_size("dp")
    shard_at = lax.axis_index("dp") * blocks + member
    local_experts = w_gate.shape[0]
    experts = local_experts * blocks
    capacity = rows * TOPK // experts
    step_heads = max(1, 384 // rows)
    total = micro * rows
    q_part, k_part, v_part = w_query.shape[1], w_key.shape[1], w_value.shape[1]

    gain_len = norm_gains.shape[0]
    gain_shard = jnp.zeros((2048,), bf16).at[:gain_len].set(norm_gains).reshape(16, 128)
    gain_full = lax.all_gather(gain_shard, BOTH, axis=0, tiled=True)
    gains = gain_full.reshape(shards, 2048)[:, :gain_len].reshape(-1).astype(f32)
    gain_in = gains[:width]
    gain_mid = gains[width : 2 * width]
    gain_q = gains[2 * width : 2 * width + HD]
    gain_k = gains[2 * width + HD :]

    qkv_w = lax.all_gather(
        jnp.concatenate([w_query.T, w_key.T, w_value.T], axis=0), BOTH, axis=0, tiled=True
    )
    out_w = lax.all_gather(w_output, BOTH, axis=0, tiled=True)
    wg = lax.all_gather(w_gate, "dp", axis=1, tiled=True)
    wu = lax.all_gather(w_up, "dp", axis=1, tiled=True)
    wd = lax.all_gather(w_down, "dp", axis=2, tiled=True)

    slot_map, weight_map = jax.vmap(
        lambda r, g, o: slots_of(r, g, o, capacity, experts)
    )(routes[:, 0], gate_weights[:, 0], pair_order[:, 0, 0])
    routing = jnp.concatenate([slot_map, weight_map], axis=-1)
    routing = lax.all_gather(routing, "expert", axis=0, tiled=False)
    mine = member * local_experts
    slot_mine = lax.dynamic_slice_in_dim(routing, mine, local_experts, axis=3)
    weight_mine = lax.dynamic_slice_in_dim(routing, experts + mine, local_experts, axis=3)
    slot_mine = jnp.transpose(slot_mine, (1, 3, 0, 2))
    weight_mine = jnp.transpose(weight_mine, (1, 3, 0, 2))
    slot_ids = jnp.arange(capacity, dtype=f32)
    hit = slot_mine[:, :, :, None, :] == slot_ids[None, None, None, :, None]
    pick = hit.astype(bf16)
    weighted = jnp.where(hit, weight_mine[:, :, :, None, :], 0.0)
    slot_weight = jnp.sum(weighted, axis=-1)
    weighted = weighted.astype(bf16)

    key_index = jnp.arange(group_len, dtype=jnp.int32)
    start_row = member * rows
    segment = membership[:, 0]
    row_index = start_row + jnp.arange(rows, dtype=jnp.int32)
    seg_rows = lax.dynamic_slice_in_dim(segment, start_row, rows, axis=1)
    before = jnp.sum((segment[:, None, :] < seg_rows[:, :, None]).astype(jnp.int32), axis=2)
    position = jnp.where(seg_rows == 0, row_index[None], PROMPT + row_index[None] - before)
    allowed = (key_index[None, :, None] <= row_index[None, None, :]) & (
        (segment[:, :, None] == 0) | (segment[:, :, None] == seg_rows[:, None, :])
    )
    bias = jnp.tile(jnp.where(allowed, 0.0, MASKED).astype(f32), (1, 1, step_heads))
    frequency = ROPE_BASE ** (-(jnp.arange(HD // 2, dtype=f32) * 2.0 / HD))
    angles = position.astype(f32).reshape(total)[:, None] * frequency[None, :]
    cosine = jnp.cos(angles)[:, None, :]
    sine_part = jnp.sin(angles)[:, None, :]

    hidden = inputs[:, 0].astype(f32).reshape(total, width)
    scale_in = rms_scale(hidden)
    normed = (hidden * scale_in * gain_in).astype(bf16)
    proj = mm(normed, qkv_w, NT).reshape(total, shards, q_part + k_part + v_part)
    queries = proj[:, :, :q_part].reshape(total, H, HD)
    key_pre = proj[:, :, q_part : q_part + k_part].reshape(total, KVH, HD)
    value = proj[:, :, q_part + k_part :].reshape(total, KVH, HD).astype(bf16)
    scale_q = rms_scale(queries)
    scale_k = rms_scale(key_pre)
    q_low = rotate(queries * scale_q * (gain_q * (SCALE * LOG2E)), cosine, sine_part).astype(bf16)
    q_low = q_low.reshape(micro, rows, H * HD)
    k_low = rotate(key_pre * scale_k * gain_k, cosine, sine_part).astype(bf16)
    kv_own = jnp.concatenate([k_low, value], axis=-1).reshape(micro, rows, KVH * 2 * HD)
    kv_all = lax.all_gather(kv_own, "expert", axis=0, tiled=False)
    chunk = 256
    mixed, logs = run_forward(q_low, kv_all, bias, step_heads, chunk)

    branch = mm(mixed.reshape(total, H * HD), out_w)
    middle = hidden + branch
    scale_mid = rms_scale(middle)
    routed = (middle * scale_mid * gain_mid).astype(bf16).reshape(micro, rows, width)
    middle = middle.reshape(micro, rows, width)
    scale_mid = scale_mid.reshape(micro, rows, 1)

    outputs, d_branches, d_middles = [], [], []
    acc_gate = acc_up = acc_down = 0.0
    grad_mid = 0.0
    slots = blocks * capacity
    for at in range(micro):
        d_out = lax.all_gather(cotangent[at, 0], "expert", axis=0, tiled=False)
        tokens = lax.all_gather(routed[at], "expert", axis=0, tiled=False)
        picked = jnp.einsum("ebst,btd->ebsd", pick[at], tokens, preferred_element_type=f32)
        picked = picked.astype(bf16).reshape(local_experts, slots, width)
        d_result = jnp.einsum("ebst,btd->ebsd", pick[at], d_out, preferred_element_type=f32)
        d_result = (d_result * slot_weight[at][..., None]).astype(bf16)
        d_result = d_result.reshape(local_experts, slots, width)
        gate_pre = jnp.einsum("erd,edf->erf", picked, wg, preferred_element_type=f32)
        up_pre = jnp.einsum("erd,edf->erf", picked, wu, preferred_element_type=f32)
        d_hidden = jnp.einsum("erd,efd->erf", d_result, wd, preferred_element_type=f32)
        sigmoid_g = jax.nn.sigmoid(gate_pre)
        silu_g = gate_pre * sigmoid_g
        hidden_low = (silu_g * up_pre).astype(bf16)
        d_gate = (d_hidden * up_pre * sigmoid_g * (1.0 + gate_pre * (1.0 - sigmoid_g))).astype(bf16)
        d_up = (d_hidden * silu_g).astype(bf16)
        d_rows = jnp.einsum("erf,edf->erd", d_gate, wg, preferred_element_type=f32)
        d_rows = d_rows + jnp.einsum("erf,edf->erd", d_up, wu, preferred_element_type=f32)
        d_rows = d_rows.astype(bf16).reshape(local_experts, blocks, capacity, width)
        d_part = jnp.einsum("ebst,ebsd->btd", pick[at], d_rows, preferred_element_type=f32)
        d_part = d_part.astype(bf16).reshape(group_len, width)
        d_routed = lax.psum_scatter(d_part, "expert", scatter_dimension=0, tiled=True).astype(f32)
        result = jnp.einsum("erf,efd->erd", hidden_low, wd, preferred_element_type=f32)
        result = result.astype(bf16).reshape(local_experts, blocks, capacity, width)
        part = jnp.einsum("ebst,ebsd->btd", weighted[at], result, preferred_element_type=f32)
        part = part.astype(bf16).reshape(group_len, width)
        expert_mix = lax.psum_scatter(part, "expert", scatter_dimension=0, tiled=True).astype(f32)
        outputs.append((middle[at] + expert_mix).astype(bf16))

        acc_down += jnp.einsum("erf,erd->efd", hidden_low, d_result, preferred_element_type=f32)
        acc_gate += jnp.einsum("erd,erf->edf", picked, d_gate, preferred_element_type=f32)
        acc_up += jnp.einsum("erd,erf->edf", picked, d_up, preferred_element_type=f32)

        d_mid_norm, mid_gain_grad = norm_back(d_routed, middle[at], scale_mid[at], gain_mid)
        grad_mid = grad_mid + mid_gain_grad
        d_middle = cotangent[at, 0].astype(f32) + d_mid_norm
        d_middles.append(d_middle)
        d_branches.append(d_middle.astype(bf16))

    grad_gate = lax.psum_scatter(acc_gate.astype(bf16), "dp", scatter_dimension=1, tiled=True)
    grad_up = lax.psum_scatter(acc_up.astype(bf16), "dp", scatter_dimension=1, tiled=True)
    grad_down = lax.psum_scatter(acc_down.astype(bf16), "dp", scatter_dimension=2, tiled=True)

    d_branch = jnp.concatenate(d_branches, axis=0)
    d_middle = jnp.concatenate(d_middles, axis=0)
    grad_output = mm(mixed.reshape(total, H * HD), d_branch, TN).astype(bf16)
    grad_output = lax.psum_scatter(grad_output, BOTH, scatter_dimension=0, tiled=True)
    d_mixed = mm(d_branch, out_w, NT).astype(bf16).reshape(micro, rows, H * HD)
    dq_low, dkv_all = run_backward(q_low, kv_all, bias, mixed, d_mixed, logs, step_heads, chunk)
    dkv = lax.psum_scatter(dkv_all, "expert", scatter_dimension=0, tiled=False)
    dkv = dkv.reshape(total, KVH, 2 * HD)
    d_query = rotate(dq_low.reshape(total, H, HD).astype(f32), cosine, -sine_part)
    d_query, grad_qn = norm_back(d_query, queries, scale_q, gain_q)
    d_key = rotate(dkv[:, :, :HD].astype(f32), cosine, -sine_part)
    d_key, grad_kn = norm_back(d_key, key_pre, scale_k, gain_k)
    d_proj = jnp.concatenate(
        [
            d_query.astype(bf16).reshape(total, shards, q_part),
            d_key.astype(bf16).reshape(total, shards, k_part),
            dkv[:, :, HD:].reshape(total, shards, v_part),
        ],
        axis=-1,
    ).reshape(total, -1)
    grad_qkv = mm(d_proj, normed, TN).astype(bf16)
    grad_qkv = lax.psum_scatter(grad_qkv, BOTH, scatter_dimension=0, tiled=True).astype(f32)
    d_normed = mm(d_proj, qkv_w)
    d_in_norm, grad_in = norm_back(d_normed, hidden, scale_in, gain_in)
    input_grad = d_middle + d_in_norm

    gain_grads = jnp.concatenate([grad_in, grad_mid, grad_qn, grad_kn]).reshape(shards, gain_len)
    gain_grads = jnp.pad(gain_grads, ((0, 0), (0, 256 - gain_len % 256)))
    gain_all = lax.all_gather(gain_grads, BOTH, axis=0, tiled=False)
    grad_gains = jnp.sum(lax.dynamic_index_in_dim(gain_all, shard_at, axis=1, keepdims=False), axis=0)
    return (
        jnp.stack(outputs)[:, None],
        input_grad.reshape(micro, 1, rows, width),
        grad_qkv[:q_part].T,
        grad_qkv[q_part : q_part + k_part].T,
        grad_qkv[q_part + k_part :].T,
        grad_output.astype(f32),
        grad_gains[:gain_len],
        grad_gate.astype(f32),
        grad_up.astype(f32),
        grad_down.astype(f32),
    )


def body_fast(
    inputs,
    cotangent,
    membership,
    routes,
    gate_weights,
    pair_order,
    w_query,
    w_key,
    w_value,
    w_output,
    norm_gains,
    w_gate,
    w_up,
    w_down,
):
    micro = inputs.shape[0]
    rows = inputs.shape[2]
    width = inputs.shape[3]
    group_len = membership.shape[2]
    member = lax.axis_index("expert")
    blocks = lax.axis_size("expert")
    shards = blocks * lax.axis_size("dp")
    local_experts = w_gate.shape[0]
    experts = local_experts * blocks
    capacity = rows * TOPK // experts
    step_heads = max(1, 384 // rows)
    total = micro * rows
    q_part, k_part, v_part = w_query.shape[1], w_key.shape[1], w_value.shape[1]
    tie = lax.optimization_barrier

    slot_map, weight_map = jax.vmap(
        lambda r, g, o: slots_of(r, g, o, capacity, experts)
    )(routes[:, 0], gate_weights[:, 0], pair_order[:, 0, 0])
    weight_high = tie(weight_map.astype(bf16))
    weight_low = (weight_map - weight_high.astype(f32)).astype(bf16)

    def padded(values, lanes):
        return jnp.pad(values, ((0, 0), (0, 0), (0, lanes - experts)))

    cot_rows = jnp.concatenate(
        [
            cotangent[:, 0],
            padded(slot_map.astype(bf16), 32),
            padded(weight_high, 32),
            padded(weight_low, ROUTE_LANES - 64),
        ],
        axis=-1,
    )

    gain_len = norm_gains.shape[0]
    gain_shard = jnp.zeros((2048,), bf16).at[:gain_len].set(norm_gains).reshape(16, 128)
    qkv_w = jnp.concatenate([w_query.T, w_key.T, w_value.T], axis=0)
    qkv_w, out_w, gain_full = gather_rows([qkv_w, w_output, gain_shard], [(2, 0, 1)], 1)
    qkv_w, cot_0, cot_1, w_gate, w_up, w_down = tie(
        (qkv_w, cot_rows[0], cot_rows[1], w_gate, w_up, w_down)
    )
    gains = gain_full.reshape(shards, 2048)[:, :gain_len].reshape(-1).astype(f32)
    gain_in = gains[:width]
    gain_mid = gains[width : 2 * width]
    gain_q = gains[2 * width : 2 * width + HD]
    gain_k = gains[2 * width + HD :]
    cot_0 = lax.all_gather(cot_0, "expert", axis=0, tiled=False)
    cot_1 = lax.all_gather(cot_1, "expert", axis=0, tiled=False)
    gate_near, up_near, down_near = ((swap(w, 1), swap(w, 2)) for w in (w_gate, w_up, w_down))

    key_index = jnp.arange(group_len, dtype=jnp.int32)
    start_row = member * rows
    segment = membership[:, 0]
    row_index = start_row + jnp.arange(rows, dtype=jnp.int32)
    seg_rows = lax.dynamic_slice_in_dim(segment, start_row, rows, axis=1)
    before = jnp.sum((segment[:, None, :] < seg_rows[:, :, None]).astype(jnp.int32), axis=2)
    position = jnp.where(seg_rows == 0, row_index[None], PROMPT + row_index[None] - before)
    allowed = (key_index[None, :, None] <= row_index[None, None, :]) & (
        (segment[:, :, None] == 0) | (segment[:, :, None] == seg_rows[:, None, :])
    )
    bias = jnp.tile(jnp.where(allowed, 0.0, MASKED).astype(f32), (1, 1, step_heads))
    frequency = ROPE_BASE ** (-(jnp.arange(HD // 2, dtype=f32) * 2.0 / HD))
    angles = position.astype(f32).reshape(total)[:, None] * frequency[None, :]
    cosine = jnp.cos(angles)[:, None, :]
    sine_part = jnp.sin(angles)[:, None, :]

    hidden = inputs[:, 0].astype(f32).reshape(total, width)
    scale_in = rms_scale(hidden)
    normed = (hidden * scale_in * gain_in).astype(bf16)
    proj = mm(normed, qkv_w, NT).reshape(total, shards, q_part + k_part + v_part)
    queries = proj[:, :, :q_part].reshape(total, H, HD)
    key_pre = proj[:, :, q_part : q_part + k_part].reshape(total, KVH, HD)
    value = proj[:, :, q_part + k_part :].reshape(total, KVH, HD).astype(bf16)
    scale_q = rms_scale(queries)
    scale_k = rms_scale(key_pre)
    q_low = rotate(queries * scale_q * (gain_q * (SCALE * LOG2E)), cosine, sine_part).astype(bf16)
    q_low = q_low.reshape(micro, rows, H * HD)
    k_low = rotate(key_pre * scale_k * gain_k, cosine, sine_part).astype(bf16)
    kv_own = jnp.concatenate([k_low, value], axis=-1).reshape(micro, rows, KVH * 2 * HD)
    kv_own, cot_0, gate_near = tie((kv_own, cot_0, gate_near))
    kv_all = lax.all_gather(kv_own, "expert", axis=0, tiled=False)
    kv_all, up_near, down_near = tie((kv_all, up_near, down_near))
    parts = [
        (own, near[0], near[1], swap(near[0][:1], 2), swap(near[1][1:], 1))
        for own, near in ((w_gate, gate_near), (w_up, up_near), (w_down, down_near))
    ]
    chunk = 256
    mixed, logs = run_forward(q_low, kv_all, bias, step_heads, chunk)

    branch = mm(mixed.reshape(total, H * HD), out_w)
    middle = hidden + branch
    scale_mid = rms_scale(middle)
    routed = (middle * scale_mid * gain_mid).astype(bf16).reshape(micro, rows, width)
    routed, parts, cot_1 = tie((routed, parts, cot_1))
    middle = middle.reshape(micro, rows, width)
    scale_mid = scale_mid.reshape(micro, rows, 1)

    mix_parts, d_routeds, d_branches, d_middles = [], [], [], []
    kept = []
    for at, cot in enumerate((cot_0, cot_1)):
        tokens = lax.all_gather(routed[at], "expert", axis=0, tiled=False)
        kept, mix, d_part = run_experts(tokens, cot, parts, capacity, at, micro, kept)
        kept, d_part, mix = tie((kept, d_part, mix))
        mix_parts.append(mix)
        d_routed = lax.psum_scatter(d_part, "expert", scatter_dimension=0, tiled=True)
        d_routeds.append(d_routed)
    picked, d_result, hidden_low, d_gate, d_up = (
        a.reshape(local_experts, -1, a.shape[-1]) for a in kept
    )

    def weight_grad(rows_in, rows_out):
        return jnp.einsum("era,erb->eab", rows_in, rows_out, preferred_element_type=f32).astype(bf16)

    scattering = [
        scatter_far(weight_grad(hidden_low, d_result), 2),
        scatter_far(weight_grad(picked, d_gate), 1),
        scatter_far(weight_grad(picked, d_up), 1),
    ]
    d_routeds[-1], scattering = tie((d_routeds[-1], scattering))
    expert_grads = [scatter_near(*pieces) for pieces in scattering]
    grad_mid = 0.0
    for at in range(micro):
        d_mid_norm, mid_gain_grad = norm_back(
            d_routeds[at].astype(f32), middle[at], scale_mid[at], gain_mid
        )
        grad_mid = grad_mid + mid_gain_grad
        d_middle = cotangent[at, 0].astype(f32) + d_mid_norm
        d_middles.append(d_middle)
        d_branches.append(d_middle.astype(bf16))

    d_branch = jnp.concatenate(d_branches, axis=0)
    d_middle = jnp.concatenate(d_middles, axis=0)
    d_mixed = mm(d_branch, out_w, NT).astype(bf16).reshape(micro, rows, H * HD)
    dq_low, dkv_all = run_backward(q_low, kv_all, bias, mixed, d_mixed, logs, step_heads, chunk)
    mixed_after, dq_low, dkv_all, expert_grads = tie((mixed, dq_low, dkv_all, expert_grads))
    grad_output, _ = reduce_rows(mixed_after.reshape(total, H * HD), d_branch, w_output.shape[0], 2)
    dkv = lax.psum_scatter(dkv_all, "expert", scatter_dimension=0, tiled=False)
    dkv, grad_output, dq_low = tie((dkv, grad_output, dq_low))
    dkv = dkv.reshape(total, KVH, 2 * HD)
    mix_parts, dkv = tie((mix_parts, dkv))
    outputs = []
    for at in range(micro):
        mix = lax.psum_scatter(mix_parts[at], "expert", scatter_dimension=0, tiled=True)
        outputs.append((middle[at] + mix.astype(f32)).astype(bf16))
    d_query = rotate(dq_low.reshape(total, H, HD).astype(f32), cosine, -sine_part)
    d_query, grad_qn = norm_back(d_query, queries, scale_q, gain_q)
    d_key = rotate(dkv[:, :, :HD].astype(f32), cosine, -sine_part)
    d_key, grad_kn = norm_back(d_key, key_pre, scale_k, gain_k)
    d_proj = jnp.concatenate(
        [
            d_query.astype(bf16).reshape(total, shards, q_part),
            d_key.astype(bf16).reshape(total, shards, k_part),
            dkv[:, :, HD:].reshape(total, shards, v_part),
        ],
        axis=-1,
    ).reshape(total, -1)
    d_normed = mm(d_proj, qkv_w)
    d_in_norm, grad_in = norm_back(d_normed, hidden, scale_in, gain_in)
    input_grad = d_middle + d_in_norm
    gain_grads = jnp.concatenate([grad_in, grad_mid, grad_qn, grad_kn]).reshape(shards, gain_len)
    grad_qkv, grad_gains = reduce_rows(d_proj, normed, q_part + k_part + v_part, 3, gain_grads)
    return (
        jnp.stack(outputs)[:, None],
        input_grad.reshape(micro, 1, rows, width),
        grad_qkv[:q_part].T,
        grad_qkv[q_part : q_part + k_part].T,
        grad_qkv[q_part + k_part :].T,
        grad_output,
        grad_gains[0, :gain_len],
        expert_grads[1],
        expert_grads[2],
        expert_grads[0],
    )


def solution(mesh):
    fast = mesh.shape["dp"] == 4 and mesh.shape["expert"] == 8
    return jax.shard_map(
        body_fast if fast else body_plain,
        mesh=mesh,
        in_specs=(
            P(None, "dp", "expert", None),
            P(None, "dp", "expert", None),
            P(None, "dp", None),
            P(None, "dp", "expert", None),
            P(None, "dp", "expert", None),
            P(None, "dp", "expert", None),
            P(None, ("dp", "expert")),
            P(None, ("dp", "expert")),
            P(None, ("dp", "expert")),
            P(("dp", "expert"), None),
            P(("dp", "expert")),
            P("expert", "dp", None),
            P("expert", "dp", None),
            P("expert", None, "dp"),
        ),
        out_specs=(
            P(None, "dp", "expert", None),
            P(None, "dp", "expert", None),
            P(None, ("dp", "expert")),
            P(None, ("dp", "expert")),
            P(None, ("dp", "expert")),
            P(("dp", "expert"), None),
            P(("dp", "expert")),
            P("expert", "dp", None),
            P("expert", "dp", None),
            P("expert", None, "dp"),
        ),
        check_vma=False,
    )
```

```python
import functools
import math

import jax
import jax.numpy as jnp
from jax import lax
from jax.experimental import pallas as pl
from jax.experimental.pallas import tpu as pltpu
from jax.sharding import PartitionSpec as P

H = 32
KVH = 4
HD = 128
FF = 768
TOPK = 8
PROMPT = 1024
PER_KV = H // KVH

EPSILON = 1e-06
ROPE_BASE = 1000000.0
MASKED = -1e30
LOG2E = math.log2(math.e)
SCALE = HD ** (-0.5)

bf16 = jnp.bfloat16
f32 = jnp.float32
NT = (((1,), (1,)), ((), ()))
TN = (((0,), (0,)), ((), ()))
NN = (((1,), (0,)), ((), ()))
BOTH = ("dp", "expert")
VMEM_LIMIT = 56 * 1024 * 1024


def mm(a, b, dims=NN):
    return lax.dot_general(a, b, dims, preferred_element_type=f32)


def rms_scale(values):
    return lax.rsqrt(jnp.mean(values * values, axis=-1, keepdims=True) + EPSILON)


def norm_back(upstream, values, inv_rms, norm_gain):
    lifted = upstream * norm_gain
    inner_dot = jnp.mean(lifted * values, axis=-1, keepdims=True)
    back_grad = inv_rms * lifted - values * (inv_rms * inv_rms * inv_rms) * inner_dot
    gain_grad = jnp.sum((upstream * values * inv_rms).reshape(-1, values.shape[-1]), axis=0)
    return (back_grad, gain_grad)


def rotate(values, cosine, sine_part):
    half_dim = values.shape[-1] // 2
    first_half = values[..., :half_dim]
    second_half = values[..., half_dim:]
    return jnp.concatenate(
        [
            first_half * cosine - second_half * sine_part,
            second_half * cosine + first_half * sine_part,
        ],
        axis=-1,
    )


def turn(values, cosine, sine):
    return values * cosine + pltpu.roll(values, HD // 2, 1) * sine


def project(x_ref, wq_ref, wkv_ref, cos_ref, sin_ref, gq_ref, gk_ref, q_ref, qraw_ref, kv_ref, kraw_ref, wkv_out):
    x = x_ref[...]
    cosine, sine = cos_ref[...], sin_ref[...]
    for at in range(0, PER_KV * HD, 2 * HD):
        raw = mm(x, wq_ref[at : at + 2 * HD], NT)
        qraw_ref[:, at : at + 2 * HD] = raw
        for lane in (0, HD):
            head = raw[:, lane : lane + HD]
            normed = head * rms_scale(head) * gq_ref[...]
            q_ref[:, at + lane : at + lane + HD] = turn(normed, cosine, sine).astype(bf16)
    piece = HD // PER_KV
    w_k = [wkv_ref[2 * piece * i : 2 * piece * i + piece] for i in range(PER_KV)]
    w_v = [wkv_ref[2 * piece * i + piece : 2 * piece * (i + 1)] for i in range(PER_KV)]
    w_kv = jnp.concatenate(w_k + w_v, axis=0)
    wkv_out[...] = w_kv
    raw = mm(x, w_kv, NT)
    key = raw[:, :HD]
    kraw_ref[...] = key
    normed = key * rms_scale(key) * gk_ref[...]
    kv_ref[:, :HD] = turn(normed, cosine, sine).astype(bf16)
    kv_ref[:, HD:] = raw[:, HD:].astype(bf16)


def run_project(x, wq, wkv, cosine, sine, gain_q, gain_k):
    tokens, width = x.shape
    wide = PER_KV * HD
    whole = lambda a: pl.BlockSpec(a.shape, lambda g: (0, 0))
    cols = lambda n: pl.BlockSpec((tokens, n), lambda g: (0, g))
    rows = lambda n: pl.BlockSpec((n, width), lambda g: (g, 0))
    return pl.pallas_call(
        project,
        grid=(KVH,),
        in_specs=[whole(x), rows(wide), rows(2 * HD), whole(cosine), whole(sine), whole(gain_q), whole(gain_k)],
        out_specs=[cols(wide), cols(wide), cols(2 * HD), cols(HD), rows(2 * HD)],
        out_shape=[
            jax.ShapeDtypeStruct((tokens, H * HD), bf16),
            jax.ShapeDtypeStruct((tokens, H * HD), f32),
            jax.ShapeDtypeStruct((tokens, KVH * 2 * HD), bf16),
            jax.ShapeDtypeStruct((tokens, KVH * HD), f32),
            jax.ShapeDtypeStruct((KVH * 2 * HD, width), bf16),
        ],
        compiler_params=pltpu.CompilerParams(vmem_limit_bytes=VMEM_LIMIT),
        cost_estimate=pl.CostEstimate(
            flops=2 * tokens * width * (H + 2 * KVH) * HD, bytes_accessed=40_000_000, transcendentals=0
        ),
    )(x, wq, wkv, cosine, sine, gain_q, gain_k)


def norm_turn_back(grad, raw, cosine, sine, gain):
    grad = turn(grad, cosine, -sine)
    scale = rms_scale(raw)
    lifted = grad * gain
    inner = jnp.mean(lifted * raw, axis=-1, keepdims=True)
    back = scale * lifted - raw * (scale * scale * scale) * inner
    return back, jnp.sum(grad * raw * scale, axis=0, keepdims=True)


def key_back(dkv_ref, kraw_ref, cos_ref, sin_ref, gk_ref, out_ref, out_t_ref, gain_ref):
    gain_sum = 0.0
    for g in range(KVH):
        key = slice(2 * g * HD, (2 * g + 1) * HD)
        value = slice((2 * g + 1) * HD, (2 * g + 2) * HD)
        grad = dkv_ref[:, key].astype(f32)
        back, part = norm_turn_back(
            grad, kraw_ref[:, g * HD : (g + 1) * HD], cos_ref[...], sin_ref[...], gk_ref[...]
        )
        gain_sum += part
        low = back.astype(bf16)
        out_ref[:, key] = low
        out_t_ref[key] = low.T
        out_ref[:, value] = dkv_ref[:, value]
        out_t_ref[value] = dkv_ref[:, value].T
    gain_ref[...] = gain_sum


def run_key_back(dkv, key_raw, cosine, sine, gain):
    tokens, wide = dkv.shape
    return pl.pallas_call(
        key_back,
        out_shape=[
            jax.ShapeDtypeStruct((tokens, wide), bf16),
            jax.ShapeDtypeStruct((wide, tokens), bf16),
            jax.ShapeDtypeStruct((1, HD), f32),
        ],
        compiler_params=pltpu.CompilerParams(vmem_limit_bytes=VMEM_LIMIT),
    )(dkv, key_raw, cosine, sine, gain)


def attend_forward(step_heads, chunk, q_ref, kv_ref, bias_ref, o_ref, log_ref):
    group_len = bias_ref.shape[1]
    keys = kv_ref[:, 0, :, :HD].reshape(group_len, HD)
    values_t = kv_ref[:, 0, :, HD:].reshape(group_len, HD).T
    rows = q_ref.shape[1]
    for step in range(PER_KV // step_heads):
        heads = range(step * step_heads, (step + 1) * step_heads)
        query = jnp.concatenate([q_ref[0, :, h * HD : (h + 1) * HD] for h in heads], axis=0)
        mixed, row_sum = 0.0, 0.0
        for at in range(0, group_len, chunk):
            scores = mm(keys[at : at + chunk], query, NT)
            prob = jnp.exp2(scores + bias_ref[0, at : at + chunk, :])
            row_sum += jnp.sum(prob, axis=0, keepdims=True)
            mixed += mm(values_t[:, at : at + chunk], prob.astype(bf16))
        out = (mixed / row_sum).T.astype(bf16)
        for i, h in enumerate(heads):
            o_ref[0, :, h * HD : (h + 1) * HD] = out[i * rows : (i + 1) * rows]
        log_ref[0, 0, step : step + 1, :] = jnp.log2(row_sum)


def attend_backward(
    step_heads, chunk, q_ref, kv_ref, bias_ref, o_ref, do_ref, log_ref, raw_ref, cos_ref, sin_ref, gain_ref,
    dq_ref, dkv_ref, gain_out, dk_acc, dv_acc
):
    group_len = bias_ref.shape[1]
    keys = kv_ref[:, 0, :, :HD].reshape(group_len, HD)
    values = kv_ref[:, 0, :, HD:].reshape(group_len, HD)
    keys_t = keys.T
    rows = q_ref.shape[1]
    cosine, sine, gain = cos_ref[0], sin_ref[0], gain_ref[...]

    @pl.when((pl.program_id(0) == 0) & (pl.program_id(1) == 0))
    def _():
        gain_out[...] = jnp.zeros_like(gain_out)

    gain_sum = 0.0
    dk_acc[...] = jnp.zeros_like(dk_acc)
    dv_acc[...] = jnp.zeros_like(dv_acc)
    for step in range(PER_KV // step_heads):
        heads = range(step * step_heads, (step + 1) * step_heads)
        query = jnp.concatenate([q_ref[0, :, h * HD : (h + 1) * HD] for h in heads], axis=0)
        grad = jnp.concatenate([do_ref[0, :, h * HD : (h + 1) * HD] for h in heads], axis=0)
        mixed = jnp.concatenate([o_ref[0, :, h * HD : (h + 1) * HD] for h in heads], axis=0)
        row_dot = jnp.sum((grad.astype(f32) * mixed.astype(f32)).T, axis=0, keepdims=True)
        log_sum = log_ref[0, 0, step : step + 1, :]
        dq_t = 0.0
        for at in range(0, group_len, chunk):
            part = slice(at, at + chunk)
            scores = mm(keys[part], query, NT)
            prob = jnp.exp2(scores + (bias_ref[0, part, :] - log_sum))
            d_prob = mm(values[part], grad, NT)
            d_score = (prob * (d_prob - row_dot)).astype(bf16)
            dv_acc[part] += mm(prob.astype(bf16), grad)
            dk_acc[part] += mm(d_score, query)
            dq_t += mm(keys_t[:, part], d_score)
        out = (dq_t * SCALE).T.astype(bf16).astype(f32)
        for i, h in enumerate(heads):
            head = slice(h * HD, (h + 1) * HD)
            back, part = norm_turn_back(
                out[i * rows : (i + 1) * rows], raw_ref[0, :, head], cosine, sine, gain
            )
            dq_ref[0, :, head] = back.astype(bf16)
            gain_sum += part
    gain_out[...] += gain_sum
    blocks = dkv_ref.shape[0]
    dkv_ref[:, 0, :, :HD] = (dk_acc[...] * (1.0 / LOG2E)).astype(bf16).reshape(blocks, rows, HD)
    dkv_ref[:, 0, :, HD:] = dv_acc[...].astype(bf16).reshape(blocks, rows, HD)


def attention_specs(micro, rows, group_len, blocks, step_heads):
    wide = PER_KV * HD
    q_spec = pl.BlockSpec((1, rows, wide), lambda b, g: (b, 0, g))
    kv_spec = pl.BlockSpec((blocks, 1, rows, 2 * HD), lambda b, g: (0, b, 0, g))
    bias_spec = pl.BlockSpec((1, group_len, step_heads * rows), lambda b, g: (b, 0, 0))
    log_spec = pl.BlockSpec((1, 1, PER_KV // step_heads, step_heads * rows), lambda b, g: (b, g, 0, 0))
    return q_spec, kv_spec, bias_spec, log_spec


def run_forward(query, kv_all, bias, step_heads, chunk):
    micro, rows, _ = query.shape
    blocks = kv_all.shape[0]
    group_len = bias.shape[1]
    q_spec, kv_spec, bias_spec, log_spec = attention_specs(micro, rows, group_len, blocks, step_heads)
    flops = 4 * micro * rows * H * HD * group_len
    return pl.pallas_call(
        functools.partial(attend_forward, step_heads, chunk),
        grid=(micro, KVH),
        in_specs=[q_spec, kv_spec, bias_spec],
        out_specs=[q_spec, log_spec],
        out_shape=[
            jax.ShapeDtypeStruct(query.shape, bf16),
            jax.ShapeDtypeStruct((micro, KVH, PER_KV // step_heads, step_heads * rows), f32),
        ],
        compiler_params=pltpu.CompilerParams(vmem_limit_bytes=VMEM_LIMIT),
        cost_estimate=pl.CostEstimate(
            flops=flops, bytes_accessed=20_000_000, transcendentals=flops // (4 * HD)
        ),
    )(query, kv_all, bias)


def run_backward(query, kv_all, bias, mixed, grad, logs, raw, cosine, sine, gain, step_heads, chunk):
    micro, rows, _ = query.shape
    blocks = kv_all.shape[0]
    group_len = bias.shape[1]
    q_spec, kv_spec, bias_spec, log_spec = attention_specs(micro, rows, group_len, blocks, step_heads)
    flops = 10 * micro * rows * H * HD * group_len
    return pl.pallas_call(
        functools.partial(attend_backward, step_heads, chunk),
        grid=(micro, KVH),
        in_specs=[q_spec, kv_spec, bias_spec, q_spec, q_spec, log_spec, q_spec]
        + [pl.BlockSpec((1, rows, HD), lambda b, g: (b, 0, 0))] * 2
        + [pl.BlockSpec((1, HD), lambda b, g: (0, 0))],
        out_specs=[q_spec, kv_spec, pl.BlockSpec((1, HD), lambda b, g: (0, 0))],
        out_shape=[
            jax.ShapeDtypeStruct(query.shape, bf16),
            jax.ShapeDtypeStruct(kv_all.shape, bf16),
            jax.ShapeDtypeStruct((1, HD), f32),
        ],
        scratch_shapes=[pltpu.VMEM((group_len, HD), f32), pltpu.VMEM((group_len, HD), f32)],
        compiler_params=pltpu.CompilerParams(vmem_limit_bytes=VMEM_LIMIT),
        cost_estimate=pl.CostEstimate(
            flops=flops, bytes_accessed=30_000_000, transcendentals=flops // (10 * HD)
        ),
    )(query, kv_all, bias, mixed, grad, logs, raw, cosine, sine, gain)


MESH = pl.DeviceIdType.MESH


def gather_kernel(phases, count, *refs):
    ins, outs, sems = refs[:count], refs[count : 2 * count], refs[2 * count :]
    dp = lax.axis_index("dp"); member = lax.axis_index("expert")
    blocks = lax.axis_size("expert")
    core = member % 2; z = member // 2
    depth = blocks // 2
    sibling = (dp, member + 1 - 2 * core)
    by_x = (dp + 1 - 2 * (dp % 2), member)
    by_y = ((dp + 2) % 4, member)
    x_at, y_at, far_at = by_x[0], by_y[0], 3 - dp
    above, below = (dp, member + 2), (dp, member - 2)
    barrier = pltpu.get_barrier_semaphore()
    peers = [(sibling, None), (by_x, None), (by_y, None), (above, z < depth - 1), (below, z > 0)]
    for peer, ok in peers:
        if ok is None:
            pl.semaphore_signal(barrier, inc=1, device_id=peer, device_id_type=MESH)
        else:
            @pl.when(ok)
            def _(peer=peer):
                pl.semaphore_signal(barrier, inc=1, device_id=peer, device_id_type=MESH)
    @pl.when((z == 0) | (z == depth - 1))
    def _(): pl.semaphore_wait(barrier, 4)
    @pl.when((z > 0) & (z < depth - 1))
    def _(): pl.semaphore_wait(barrier, 5)

    def guarded(ok, run):
        if ok is None: run()
        else: pl.when(ok)(run)

    class Item:
        pass

    def make(i):
        src, out = ins[i], outs[i]
        rows = src.shape[0]
        half = rows // 2
        (own_sem, sz, rz, sxy, rxy, sc, rc) = sems[i * 7 : (i + 1) * 7]
        def at(d, s, lo=0, n=rows):
            return out.at[pl.ds(pl.multiple_of((d * blocks + s * 2 + core) * rows + lo, 16 if half % 16 == 0 else 8), n)]
        def copy(a, b, ss, rs, to):
            return pltpu.make_async_remote_copy(src_ref=a, dst_ref=b, send_sem=ss, recv_sem=rs, device_id=to, device_id_type=MESH)
        def block(d, s):
            return at(d, s)
        it = Item()
        def local():
            return pltpu.make_async_copy(src, at(dp, z), own_sem)
        def up(s, ref): return copy(ref, at(dp, s), sz.at[0, s], rz.at[s], above)
        def down(s, ref): return copy(ref, at(dp, s), sz.at[1, s], rz.at[s], below)
        def to_x(s, ref): return copy(ref, at(dp, s), sxy.at[0, s], rxy.at[0, s], by_x)
        def to_y(s, ref): return copy(ref, at(dp, s), sxy.at[1, s], rxy.at[1, s], by_y)
        def half_y(s):
            return copy(at(x_at, s, 0, half), at(x_at, s, 0, half), sxy.at[2, s], rxy.at[2, s], by_y)
        def half_x(s):
            return copy(at(y_at, s, half, half), at(y_at, s, half, half), sxy.at[3, s], rxy.at[3, s], by_x)
        def to_core(r, d, s, ref): return copy(ref, at(d, s), sc.at[r, s], rc.at[r, s], sibling)
        def spread(s, ref):
            to_x(s, ref).start(); to_y(s, ref).start(); to_core(0, dp, s, ref).start()
        def start():
            local().start()
            guarded(z < depth - 1, lambda: up(z, src).start())
            guarded(z > 0, lambda: down(z, src).start())
            spread(z, src)
        def z_event(s, ok, rising):
            def run():
                up(s, at(dp, s)).wait_recv()
                if rising: guarded(z < depth - 1, lambda: up(s, at(dp, s)).start())
                else: guarded(z > 0, lambda: down(s, at(dp, s)).start())
                spread(s, at(dp, s))
            pl.when(ok)(run)
        def near_event(s, ok):
            def run():
                to_x(s, at(dp, s)).wait_recv()
                half_y(s).start()
                to_core(1, x_at, s, at(x_at, s)).start()
                to_y(s, at(dp, s)).wait_recv()
                half_x(s).start()
                to_core(2, y_at, s, at(y_at, s)).start()
            guarded(ok, run)
        def far_event(s, ok):
            def run():
                half_y(s).wait_recv(); half_x(s).wait_recv()
                to_core(3, far_at, s, at(far_at, s)).start()
            guarded(ok, run)
        def core_wait(s):
            for r, d in enumerate((dp, x_at, y_at, far_at)):
                to_core(r, d, s, at(d, s)).wait_recv()
        def finish():
            local().wait()
            for s in range(depth):
                for c in (to_x(s, at(dp, s)), to_y(s, at(dp, s)), half_y(s), half_x(s)): c.wait_send()
                for r, d in enumerate((dp, x_at, y_at, far_at)): to_core(r, d, s, at(d, s)).wait_send()
                guarded((z >= s) & (z < depth - 1), lambda: up(s, at(dp, s)).wait_send())
                guarded((z <= s) & (z > 0), lambda: down(s, at(dp, s)).wait_send())
        it.start, it.z_event, it.near_event, it.far_event, it.core_wait, it.finish = start, z_event, near_event, far_event, core_wait, finish
        return it
    items = [make(i) for i in range(count)]
    def around(d):
        if d == 0: return [(z, None, True)]
        return [(z - d, z >= d, True), (z + d, z + d < depth, False)]
    for n, phase in enumerate(phases):
        its = [items[i] for i in phase]
        for it in its: it.start()
        for d in range(1, depth + 2):
            if d < depth:
                for s, ok, rising in around(d):
                    for it in its: it.z_event(s, ok, rising)
            if d - 1 < depth:
                for s, ok, _ in around(d - 1):
                    for it in its: it.near_event(s, ok)
            if d - 2 >= 0:
                for s, ok, _ in around(d - 2):
                    for it in its: it.far_event(s, ok)
            if n + 1 < len(phases) and d == depth: pass
    for it in items:
        for s in range(depth): it.core_wait(s)
    for it in items: it.finish()

def gather_rows(arrays, phases, cid):
    shards = lax.axis_size("dp") * lax.axis_size("expert")
    depth = lax.axis_size("expert") // 2
    D = pltpu.SemaphoreType.DMA
    sems = []
    for _ in arrays:
        sems += [D, D((2, depth)), D((depth,)), D((4, depth)), D((4, depth)), D((4, depth)), D((4, depth))]
    return pl.pallas_call(
        functools.partial(gather_kernel, phases, len(arrays)),
        out_shape=[jax.ShapeDtypeStruct((shards * a.shape[0],) + a.shape[1:], a.dtype) for a in arrays],
        in_specs=[pl.BlockSpec(memory_space=pl.ANY)] * len(arrays),
        out_specs=[pl.BlockSpec(memory_space=pl.ANY)] * len(arrays),
        scratch_shapes=sems,
        compiler_params=pltpu.CompilerParams(collective_id=cid, has_side_effects=True),
        cost_estimate=pl.CostEstimate(flops=0, bytes_accessed=400_000_000, transcendentals=0),
    )(*arrays)


def reduce_kernel(rows, cuts, a_ref, extra_ref, b_ref, g_ref, o_ref, go_ref, sib, got, own, far, near, plane, got_z,
                  s0, r0, s1, r1, s2, r2, s3, r3, g_acc, g_got, g_z, gs, gr, gsz, grz):
    dp = lax.axis_index("dp"); member = lax.axis_index("expert")
    core = member % 2; z = member // 2
    sibling = (dp, member + 1 - 2 * core)
    by_x = (dp + 1 - 2 * (dp % 2), member)
    by_y = ((dp + 2) % 4, member)
    x_at, y_at = by_x[0], by_y[0]
    far_at = 3 - dp
    half = rows // 2
    depth = lax.axis_size("expert") // 2
    barrier = pltpu.get_barrier_semaphore()
    peers = [sibling, by_x, by_y] + [(dp, ((z + d) % depth) * 2 + core) for d in range(1, depth)]
    for peer in peers:
        pl.semaphore_signal(barrier, inc=1, device_id=peer, device_id_type=MESH)
    pl.semaphore_wait(barrier, len(peers))

    def pick(table):
        at = table[depth-1]
        for i in range(depth - 1):
            at = jnp.where(z == i, table[i], at)
        return at
    orders = [[3, 3, 0, 0], [2, 0, 3, 1], [1, 2, 1, 2], [0, 1, 2, 3]]
    targets = [pick(t) for t in orders]
    cols = b_ref.shape[1] // cuts

    def copy(src, dst, ssem, rsem, to):
        return pltpu.make_async_remote_copy(src_ref=src, dst_ref=dst, send_sem=ssem, recv_sem=rsem, device_id=to, device_id_type=MESH)

    blocks = 2 * depth
    piece = (rows - HD) // 2

    def product(half_of, k, put):
        spot = targets[k] * 2 + half_of

        def step(i, _):
            shard = (i // cuts) * blocks + spot
            at = (i // cuts) * rows
            col = pl.ds(pl.multiple_of((i % cuts) * cols, cols), cols)
            part = mm(a_ref[:, pl.ds(pl.multiple_of(shard * HD, HD), HD)], b_ref[:, col], TN)
            put(pl.ds(pl.multiple_of(at, 16), HD), col, part)
            if piece:
                base = (shard // PER_KV) * (2 * HD) + (shard % PER_KV) * piece
                small = jnp.concatenate(
                    [
                        extra_ref[pl.ds(pl.multiple_of(base, 16), piece), :],
                        extra_ref[pl.ds(pl.multiple_of(base + HD, 16), piece), :],
                    ],
                    axis=0,
                )
                put(pl.ds(pl.multiple_of(at + HD, 16), 2 * piece), col, mm(small, b_ref[:, col]))
            return 0

        lax.fori_loop(0, 4 * cuts, step, 0)

    def gain_hop(i, src, to):
        return copy(src, g_got.at[i, pl.ds(0, src.shape[0])], gs.at[i], gr.at[i], to)
    hops = {}
    def gain_step(i):
        rows4 = lambda at: pl.ds(pl.multiple_of(at * 8, 8), 8)
        if i == 0:
            hops[0] = gain_hop(0, g_ref.at[pl.ds(pl.multiple_of((1 - core) * 32, 32), 32)], sibling)
        elif i == 1:
            hops[0].wait_recv()
            g_acc[...] = g_ref[pl.ds(pl.multiple_of(core * 32, 32), 32)] + g_got[0]
            hops[1] = gain_hop(1, g_acc.at[pl.ds(pl.multiple_of((1 - dp // 2) * 16, 16), 16)], by_y)
        elif i == 2:
            hops[1].wait_recv()
            mine = pl.ds(pl.multiple_of((dp // 2) * 16, 16), 16)
            g_acc[mine] += g_got[1, :16]
            hops[2] = gain_hop(2, g_acc.at[rows4(x_at)], by_x)
        elif i == 3:
            hops[2].wait_recv()
            g_acc[rows4(dp)] += g_got[2, :8]
            for d in range(1, depth):
                to = (z + d) % depth
                hops[2 + d] = copy(g_acc.at[pl.ds(dp * 8 + to, 1)], g_z.at[z], gsz.at[d - 1], grz.at[z], (dp, to * 2 + core))
        if i < 3:
            hops[i].start()
        else:
            for d in range(1, depth):
                hops[2 + d].start()
    def gain_end():
        total = g_acc[pl.ds(dp * 8 + z, 1)]
        for d in range(1, depth):
            src = (z + d) % depth
            copy(g_acc.at[pl.ds(dp * 8, 1)], g_z.at[src], gsz.at[0], grz.at[src], sibling).wait_recv()
            total += g_z[src]
        go_ref[...] = total
        for i in hops:
            hops[i].wait_send()
    sib_copies, far_copies, near_copies, z_copies = {}, {}, {}, {}
    def sib_step(k):
        slot = k % 2
        if k >= 2:
            sib_copies[k - 2].wait_send()
        def put(r, c, part):
            sib[slot, r, c] = part.astype(bf16)
        product(1 - core, k, put)
        sib_copies[k] = copy(sib.at[slot], got.at[k], s0.at[slot], r0.at[k], sibling)
        sib_copies[k].start()
    def blk(at):
        return pl.ds(pl.multiple_of(at * rows, 16), rows)
    def own_step(k):
        sib_copies[k].wait_recv()
        def put(r, c, part):
            own[k, r, c] = (part + got[k, r, c].astype(f32)).astype(bf16)
        product(core, k, put)
        base = pl.multiple_of(far_at * rows, 16)
        far_copies[k] = (
            copy(own.at[k, pl.ds(base, half)], far.at[k, 0], s1.at[k, 0], r1.at[k, 0], by_x),
            copy(own.at[k, pl.ds(pl.multiple_of(base + half, 16), half)], far.at[k, 1], s1.at[k, 1], r1.at[k, 1], by_y),
        )
        for c in far_copies[k]: c.start()
    def near_step(k):
        a, b = far_copies[k]
        a.wait_recv()
        rng = pl.ds(pl.multiple_of(y_at * rows, 16), half)
        own[k, rng] = (own[k, rng].astype(f32) + far[k, 0].astype(f32)).astype(bf16)
        to_y = copy(own.at[k, blk(y_at)], near.at[k, 1], s2.at[k, 1], r2.at[k, 1], by_y)
        to_y.start()
        b.wait_recv()
        rng = pl.ds(pl.multiple_of(x_at * rows + half, 16), half)
        own[k, rng] = (own[k, rng].astype(f32) + far[k, 1].astype(f32)).astype(bf16)
        to_x = copy(own.at[k, blk(x_at)], near.at[k, 0], s2.at[k, 0], r2.at[k, 0], by_x)
        to_x.start()
        near_copies[k] = (to_x, to_y)
    def plane_step(k):
        for c in near_copies[k]: c.wait_recv()
        total = own[k, blk(dp)].astype(f32) + near[k, 0].astype(f32) + near[k, 1].astype(f32)
        if k < depth - 1:
            plane[k] = total.astype(bf16)
            to = (dp, targets[k] * 2 + core)
            z_copies[k] = copy(plane.at[k], got_z.at[z], s3.at[k], r3.at[z], to)
            z_copies[k].start()
        else:
            o_ref[...] = total
    gain_step(0)
    sib_step(0); sib_step(1)
    own_step(0)
    gain_step(1)
    sib_step(2)
    own_step(1)
    gain_step(2)
    near_step(0)
    sib_step(3)
    own_step(2)
    gain_step(3)
    near_step(1)
    plane_step(0)
    own_step(3)
    near_step(2)
    plane_step(1)
    near_step(3)
    plane_step(2)
    plane_step(3)
    for d in range(1, depth):
        src = (z + d) % depth
        copy(plane.at[0], got_z.at[src], s3.at[0], r3.at[src], sibling).wait_recv()
        o_ref[...] += got_z[src].astype(f32)
    gain_end()
    for k in range(depth):
        if k >= 2: sib_copies[k].wait_send()
        for c in far_copies[k]: c.wait_send()
        for c in near_copies[k]: c.wait_send()
        if k < depth - 1: z_copies[k].wait_send()

def reduce_rows(a, extra, b, cid, gains=None):
    tokens, width = b.shape
    depth = 4
    rows = HD + (0 if extra is None else extra.shape[0] // 32)
    if extra is None:
        extra = jnp.zeros((16, 128), bf16)
    D = pltpu.SemaphoreType.DMA
    lanes = 256
    padded = jnp.zeros((32, lanes), f32)
    if gains is not None:
        padded = jnp.pad(gains, ((0, 0), (0, lanes - gains.shape[1])))
    padded = padded.reshape(4, depth, 2, lanes).transpose(2, 0, 1, 3)
    padded = jnp.pad(padded, ((0, 0), (0, 0), (0, 8 - depth), (0, 0))).reshape(64, lanes)
    return pl.pallas_call(
        functools.partial(reduce_kernel, rows, 4),
        out_shape=[jax.ShapeDtypeStruct((rows, width), f32), jax.ShapeDtypeStruct((1, lanes), f32)],
        in_specs=[pl.BlockSpec(memory_space=pltpu.VMEM)] * 4,
        out_specs=[pl.BlockSpec(memory_space=pltpu.VMEM)] * 2,
        scratch_shapes=[
            pltpu.VMEM((2, 4 * rows, width), bf16),
            pltpu.VMEM((depth, 4 * rows, width), bf16),
            pltpu.VMEM((depth, 4 * rows, width), bf16),
            pltpu.VMEM((depth, 2, rows // 2, width), bf16),
            pltpu.VMEM((depth, 2, rows, width), bf16),
            pltpu.VMEM((depth - 1, rows, width), bf16),
            pltpu.VMEM((depth, rows, width), bf16),
            D((2,)), D((depth,)), D((depth, 2)), D((depth, 2)), D((depth, 2)), D((depth, 2)), D((depth - 1,)), D((depth,)),
            pltpu.VMEM((32, lanes), f32), pltpu.VMEM((3, 32, lanes), f32), pltpu.VMEM((depth, 1, lanes), f32),
            D((3,)), D((3,)), D((depth - 1,)), D((depth,)),
        ],
        compiler_params=pltpu.CompilerParams(vmem_limit_bytes=60*1024*1024, collective_id=cid, has_side_effects=True),
        cost_estimate=pl.CostEstimate(flops=2*tokens*32*rows*width, bytes_accessed=10_000_000, transcendentals=0),
    )(a, extra, b, padded)


ROUTE_LANES = 128


def picks_of(routing, first, local_experts, capacity):
    rows = routing.shape[0]
    lanes = lax.broadcasted_iota(jnp.int32, (rows, ROUTE_LANES), 1)
    places = lax.broadcasted_iota(jnp.int32, (rows, local_experts * capacity), 1)
    hit, weighted = None, 0.0
    for e in range(local_experts):

        def column(base):
            return jnp.sum(jnp.where(lanes == base + first + e, routing, 0.0), axis=1, keepdims=True)

        slot = column(0).astype(jnp.int32)
        here = places == jnp.where(slot >= 0, slot + e * capacity, -1)
        hit = here if hit is None else hit | here
        weighted = weighted + jnp.where(here, column(32) + column(64), 0.0)
    return jnp.where(hit, 1.0, 0.0).astype(bf16), weighted.astype(bf16)


def pick_kernel(capacity, local_experts, n_alias, tok_ref, cot_ref, *refs):
    x_ref, dy_ref = refs[n_alias:]
    width = cot_ref.shape[2]
    first = lax.axis_index("expert") * local_experts
    routing = tok_ref[0, :, width:]
    hit, _ = picks_of(routing.astype(f32), first, local_experts, capacity)
    x = mm(hit, tok_ref[0, :, :width], TN).astype(bf16)
    rows = mm(hit, routing, TN)
    lanes = lax.broadcasted_iota(jnp.int32, rows.shape, 1)
    owner = lax.broadcasted_iota(jnp.int32, rows.shape, 0) // capacity
    at = lanes - first - owner
    weight = jnp.sum(jnp.where((at == 32) | (at == 64), rows, 0.0), axis=1, keepdims=True)
    dy = (mm(hit, cot_ref[0], TN) * weight).astype(bf16)
    for e in range(local_experts):
        x_ref[e, 0, 0] = x[e * capacity : (e + 1) * capacity]
        dy_ref[e, 0, 0] = dy[e * capacity : (e + 1) * capacity]


def expert_kernel(n_alias, *refs):
    x_ref, dy_ref = refs[:2]
    parts = (refs[2:7], refs[7:12], refs[12:17])
    z_ref, dg_ref, du_ref, y_ref, dx_ref, wg, wu, wd, sems = refs[17 + n_alias :]
    local_experts, width, _ = wg.shape
    at = lax.axis_index("dp")
    size = width // 4
    places = (at, at + 1 - 2 * (at % 2), (at + 2) % 4, 3 - at, 3 - at)

    def copies(e):
        out = []
        for m, full in enumerate((wg, wu, wd)):
            for p in range(4):
                part = parts[m][p] if p < 3 else parts[m][3 + e]
                src = part.at[e] if p < 3 else part.at[0]
                where = pl.ds(pl.multiple_of(places[p] * size, size), size)
                dst = full.at[e, where, :] if m < 2 else full.at[e, :, where]
                out.append(pltpu.make_async_copy(src, dst, sems.at[e, m, p]))
        return out

    expert, chunk = pl.program_id(0), pl.program_id(1)

    @pl.when((expert == 0) & (chunk == 0))
    def _():
        for e in range(local_experts):
            for c in copies(e):
                c.start()

    for e in range(local_experts):

        @pl.when((expert == e) & (chunk == 0))
        def _(e=e):
            for c in copies(e):
                c.wait()

    x, dy = x_ref[0, 0], dy_ref[0, 0]
    gate = mm(x, wg[expert])
    up = mm(x, wu[expert])
    d_hidden = mm(dy, wd[expert], NT)
    sig = 1.0 / (1.0 + jnp.exp(-gate))
    silu = gate * sig
    z = (silu * up).astype(bf16)
    d_gate = (d_hidden * up * sig * (1.0 + gate * (1.0 - sig))).astype(bf16)
    d_up = (d_hidden * silu).astype(bf16)
    z_ref[0, 0] = z
    dg_ref[0, 0] = d_gate
    du_ref[0, 0] = d_up
    dx_ref[0] = (mm(d_gate, wg[expert], NT) + mm(d_up, wu[expert], NT)).astype(bf16)
    y_ref[0] = mm(z, wd[expert]).astype(bf16)


def sum_kernel(capacity, routing_ref, y_ref, dx_ref, mix_ref, da_ref):
    local_experts, _, _, width = y_ref.shape
    first = lax.axis_index("expert") * local_experts
    hit, weighted = picks_of(routing_ref[0].astype(f32), first, local_experts, capacity)
    da_ref[...] = mm(hit, dx_ref[...].reshape(local_experts * capacity, width)).astype(bf16)
    mix_ref[...] = mm(weighted, y_ref[...].reshape(local_experts * capacity, width)).astype(bf16)


def run_experts(tokens, cot, parts, capacity, batch_at, micro, earlier):
    blocks, rows, width = cot.shape
    local_experts, _, hidden = parts[0][0].shape
    flat = [p for group in parts for p in group]
    any_spec = pl.BlockSpec(memory_space=pl.ANY)
    params = pltpu.CompilerParams(vmem_limit_bytes=VMEM_LIMIT)
    slots = blocks * capacity
    picked_spec = pl.BlockSpec((local_experts, 1, 1, capacity, width), lambda b: (0, batch_at, b, 0, 0))
    picked = jax.ShapeDtypeStruct((local_experts, micro, blocks, capacity, width), bf16)
    x, dy = pl.pallas_call(
        functools.partial(pick_kernel, capacity, local_experts, len(earlier[:2])),
        grid=(blocks,),
        in_specs=[
            pl.BlockSpec((1, rows, tokens.shape[2]), lambda b: (b, 0, 0)),
            pl.BlockSpec((1, rows, width), lambda b: (b, 0, 0)),
        ]
        + [any_spec] * len(earlier[:2]),
        out_specs=[picked_spec] * 2,
        out_shape=[picked] * 2,
        input_output_aliases={2 + i: i for i in range(len(earlier[:2]))},
        compiler_params=params,
        cost_estimate=pl.CostEstimate(
            flops=4 * slots * local_experts * rows * width, bytes_accessed=25_000_000, transcendentals=0
        ),
    )(tokens, cot, *[a.reshape(picked.shape) for a in earlier[:2]])
    x, dy = (a.reshape(local_experts, micro, slots, width) for a in (x, dy))
    chunk = slots // 2
    row_spec = pl.BlockSpec((1, 1, chunk, width), lambda e, i: (e, batch_at, i, 0))
    hid_spec = pl.BlockSpec((1, 1, chunk, hidden), lambda e, i: (e, batch_at, i, 0))
    out_spec = pl.BlockSpec((1, chunk, width), lambda e, i: (e, i, 0))
    hid = jax.ShapeDtypeStruct((local_experts, micro, slots, hidden), bf16)
    out = jax.ShapeDtypeStruct((local_experts, slots, width), bf16)
    z, dg, du, y, dx = pl.pallas_call(
        functools.partial(expert_kernel, len(earlier[2:])),
        grid=(local_experts, 2),
        in_specs=[row_spec, row_spec] + [any_spec] * (len(flat) + len(earlier[2:])),
        out_specs=[hid_spec] * 3 + [out_spec] * 2,
        out_shape=[hid] * 3 + [out] * 2,
        input_output_aliases={2 + len(flat) + i: i for i in range(len(earlier[2:]))},
        scratch_shapes=[
            pltpu.VMEM((local_experts, width, hidden), bf16),
            pltpu.VMEM((local_experts, width, hidden), bf16),
            pltpu.VMEM((local_experts, hidden, width), bf16),
            pltpu.SemaphoreType.DMA((local_experts, 3, 4)),
        ],
        compiler_params=params,
        cost_estimate=pl.CostEstimate(
            flops=12 * local_experts * slots * width * hidden, bytes_accessed=50_000_000, transcendentals=0
        ),
    )(x, dy, *flat, *earlier[2:])
    y, dx = (a.reshape(local_experts, blocks, capacity, width) for a in (y, dx))
    part_spec = pl.BlockSpec((local_experts, 1, capacity, width), lambda b: (0, b, 0, 0))
    sums = jax.ShapeDtypeStruct((blocks * rows, width), bf16)
    sums_spec = pl.BlockSpec((rows, width), lambda b: (b, 0))
    mix, da = pl.pallas_call(
        functools.partial(sum_kernel, capacity),
        grid=(blocks,),
        in_specs=[
            pl.BlockSpec((1, rows, ROUTE_LANES), lambda b: (b, 0, width // ROUTE_LANES)),
            part_spec,
            part_spec,
        ],
        out_specs=[sums_spec] * 2,
        out_shape=[sums] * 2,
        compiler_params=params,
        cost_estimate=pl.CostEstimate(
            flops=4 * slots * local_experts * rows * width, bytes_accessed=25_000_000, transcendentals=0
        ),
    )(tokens, y, dx)
    return [x, dy, z, dg, du], mix, da


def slots_of(route_ids, gate_vals, ranking, capacity, experts):
    rows = route_ids.shape[0]
    pair_experts = route_ids.reshape(-1)
    earlier = (pair_experts[None, :] == pair_experts[:, None]) & (
        ranking[None, :] < ranking[:, None]
    )
    slot = jnp.sum(earlier.astype(jnp.int32), axis=1).reshape(rows, -1)
    kept = slot < capacity
    chosen = route_ids[:, :, None] == jnp.arange(experts, dtype=jnp.int32)[None, None, :]
    chosen = chosen & kept[:, :, None]
    slot_map = jnp.sum(jnp.where(chosen, slot[:, :, None] + 1, 0), axis=1).astype(f32) - 1.0
    weight_map = jnp.sum(jnp.where(chosen, gate_vals[:, :, None], 0.0), axis=1)
    return slot_map, weight_map


def swap(values, bit):
    return lax.ppermute(values, "dp", [(i, i ^ bit) for i in range(lax.axis_size("dp"))])


def scatter_far(total, axis):
    at = lax.axis_index("dp")
    size = total.shape[axis] // 4

    def part(bits):
        return lax.dynamic_slice_in_dim(total, (at ^ bits) * size, size, axis=axis)

    far = part(3)
    return [swap(far[:1], 1), swap(far[1:], 2), part(1), part(2), part(0)]


def scatter_near(for_y, for_x, near_x, near_y, own):
    half_y = (near_y[:1].astype(f32) + for_y.astype(f32)).astype(bf16)
    half_x = (near_x[1:].astype(f32) + for_x.astype(f32)).astype(bf16)
    near_y = jnp.concatenate([half_y, near_y[1:]], axis=0)
    near_x = jnp.concatenate([near_x[:1], half_x], axis=0)
    by_x, by_y = swap(near_x, 1), swap(near_y, 2)
    return own.astype(f32) + by_x.astype(f32) + by_y.astype(f32)


def body_plain(
    inputs,
    cotangent,
    membership,
    routes,
    gate_weights,
    pair_order,
    w_query,
    w_key,
    w_value,
    w_output,
    norm_gains,
    w_gate,
    w_up,
    w_down,
):
    micro = inputs.shape[0]
    rows = inputs.shape[2]
    width = inputs.shape[3]
    group_len = membership.shape[2]
    member = lax.axis_index("expert")
    blocks = lax.axis_size("expert")
    shards = blocks * lax.axis_size("dp")
    shard_at = lax.axis_index("dp") * blocks + member
    local_experts = w_gate.shape[0]
    experts = local_experts * blocks
    capacity = rows * TOPK // experts
    step_heads = max(1, 384 // rows)
    total = micro * rows
    q_part, k_part, v_part = w_query.shape[1], w_key.shape[1], w_value.shape[1]

    gain_len = norm_gains.shape[0]
    gain_shard = jnp.zeros((2048,), bf16).at[:gain_len].set(norm_gains).reshape(16, 128)
    gain_full = lax.all_gather(gain_shard, BOTH, axis=0, tiled=True)
    gains = gain_full.reshape(shards, 2048)[:, :gain_len].reshape(-1).astype(f32)
    gain_in = gains[:width]
    gain_mid = gains[width : 2 * width]
    gain_q = gains[2 * width : 2 * width + HD]
    gain_k = gains[2 * width + HD :]

    qkv_w = lax.all_gather(
        jnp.concatenate([w_query.T, w_key.T, w_value.T], axis=0), BOTH, axis=0, tiled=True
    )
    out_w = lax.all_gather(w_output, BOTH, axis=0, tiled=True)
    wg = lax.all_gather(w_gate, "dp", axis=1, tiled=True)
    wu = lax.all_gather(w_up, "dp", axis=1, tiled=True)
    wd = lax.all_gather(w_down, "dp", axis=2, tiled=True)

    slot_map, weight_map = jax.vmap(
        lambda r, g, o: slots_of(r, g, o, capacity, experts)
    )(routes[:, 0], gate_weights[:, 0], pair_order[:, 0, 0])
    routing = jnp.concatenate([slot_map, weight_map], axis=-1)
    routing = lax.all_gather(routing, "expert", axis=0, tiled=False)
    mine = member * local_experts
    slot_mine = lax.dynamic_slice_in_dim(routing, mine, local_experts, axis=3)
    weight_mine = lax.dynamic_slice_in_dim(routing, experts + mine, local_experts, axis=3)
    slot_mine = jnp.transpose(slot_mine, (1, 3, 0, 2))
    weight_mine = jnp.transpose(weight_mine, (1, 3, 0, 2))
    slot_ids = jnp.arange(capacity, dtype=f32)
    hit = slot_mine[:, :, :, None, :] == slot_ids[None, None, None, :, None]
    pick = hit.astype(bf16)
    weighted = jnp.where(hit, weight_mine[:, :, :, None, :], 0.0)
    slot_weight = jnp.sum(weighted, axis=-1)
    weighted = weighted.astype(bf16)

    key_index = jnp.arange(group_len, dtype=jnp.int32)
    start_row = member * rows
    segment = membership[:, 0]
    row_index = start_row + jnp.arange(rows, dtype=jnp.int32)
    seg_rows = lax.dynamic_slice_in_dim(segment, start_row, rows, axis=1)
    before = jnp.sum((segment[:, None, :] < seg_rows[:, :, None]).astype(jnp.int32), axis=2)
    position = jnp.where(seg_rows == 0, row_index[None], PROMPT + row_index[None] - before)
    allowed = (key_index[None, :, None] <= row_index[None, None, :]) & (
        (segment[:, :, None] == 0) | (segment[:, :, None] == seg_rows[:, None, :])
    )
    bias = jnp.tile(jnp.where(allowed, 0.0, MASKED).astype(f32), (1, 1, step_heads))
    frequency = ROPE_BASE ** (-(jnp.arange(HD // 2, dtype=f32) * 2.0 / HD))
    angles = position.astype(f32).reshape(total)[:, None] * frequency[None, :]
    cosine = jnp.cos(angles)[:, None, :]
    sine_part = jnp.sin(angles)[:, None, :]

    hidden = inputs[:, 0].astype(f32).reshape(total, width)
    scale_in = rms_scale(hidden)
    normed = (hidden * scale_in * gain_in).astype(bf16)
    proj = mm(normed, qkv_w, NT).reshape(total, shards, q_part + k_part + v_part)
    queries = proj[:, :, :q_part].reshape(total, H, HD)
    key_pre = proj[:, :, q_part : q_part + k_part].reshape(total, KVH, HD)
    value = proj[:, :, q_part + k_part :].reshape(total, KVH, HD).astype(bf16)
    scale_q = rms_scale(queries)
    scale_k = rms_scale(key_pre)
    q_low = rotate(queries * scale_q * (gain_q * (SCALE * LOG2E)), cosine, sine_part).astype(bf16)
    q_low = q_low.reshape(micro, rows, H * HD)
    k_low = rotate(key_pre * scale_k * gain_k, cosine, sine_part).astype(bf16)
    kv_own = jnp.concatenate([k_low, value], axis=-1).reshape(micro, rows, KVH * 2 * HD)
    kv_all = lax.all_gather(kv_own, "expert", axis=0, tiled=False)
    chunk = 256
    mixed, logs = run_forward(q_low, kv_all, bias, step_heads, chunk)

    branch = mm(mixed.reshape(total, H * HD), out_w)
    middle = hidden + branch
    scale_mid = rms_scale(middle)
    routed = (middle * scale_mid * gain_mid).astype(bf16).reshape(micro, rows, width)
    middle = middle.reshape(micro, rows, width)
    scale_mid = scale_mid.reshape(micro, rows, 1)

    outputs, d_branches, d_middles = [], [], []
    acc_gate = acc_up = acc_down = 0.0
    grad_mid = 0.0
    slots = blocks * capacity
    for at in range(micro):
        d_out = lax.all_gather(cotangent[at, 0], "expert", axis=0, tiled=False)
        tokens = lax.all_gather(routed[at], "expert", axis=0, tiled=False)
        picked = jnp.einsum("ebst,btd->ebsd", pick[at], tokens, preferred_element_type=f32)
        picked = picked.astype(bf16).reshape(local_experts, slots, width)
        d_result = jnp.einsum("ebst,btd->ebsd", pick[at], d_out, preferred_element_type=f32)
        d_result = (d_result * slot_weight[at][..., None]).astype(bf16)
        d_result = d_result.reshape(local_experts, slots, width)
        gate_pre = jnp.einsum("erd,edf->erf", picked, wg, preferred_element_type=f32)
        up_pre = jnp.einsum("erd,edf->erf", picked, wu, preferred_element_type=f32)
        d_hidden = jnp.einsum("erd,efd->erf", d_result, wd, preferred_element_type=f32)
        sigmoid_g = jax.nn.sigmoid(gate_pre)
        silu_g = gate_pre * sigmoid_g
        hidden_low = (silu_g * up_pre).astype(bf16)
        d_gate = (d_hidden * up_pre * sigmoid_g * (1.0 + gate_pre * (1.0 - sigmoid_g))).astype(bf16)
        d_up = (d_hidden * silu_g).astype(bf16)
        d_rows = jnp.einsum("erf,edf->erd", d_gate, wg, preferred_element_type=f32)
        d_rows = d_rows + jnp.einsum("erf,edf->erd", d_up, wu, preferred_element_type=f32)
        d_rows = d_rows.astype(bf16).reshape(local_experts, blocks, capacity, width)
        d_part = jnp.einsum("ebst,ebsd->btd", pick[at], d_rows, preferred_element_type=f32)
        d_part = d_part.astype(bf16).reshape(group_len, width)
        d_routed = lax.psum_scatter(d_part, "expert", scatter_dimension=0, tiled=True).astype(f32)
        result = jnp.einsum("erf,efd->erd", hidden_low, wd, preferred_element_type=f32)
        result = result.astype(bf16).reshape(local_experts, blocks, capacity, width)
        part = jnp.einsum("ebst,ebsd->btd", weighted[at], result, preferred_element_type=f32)
        part = part.astype(bf16).reshape(group_len, width)
        expert_mix = lax.psum_scatter(part, "expert", scatter_dimension=0, tiled=True).astype(f32)
        outputs.append((middle[at] + expert_mix).astype(bf16))

        acc_down += jnp.einsum("erf,erd->efd", hidden_low, d_result, preferred_element_type=f32)
        acc_gate += jnp.einsum("erd,erf->edf", picked, d_gate, preferred_element_type=f32)
        acc_up += jnp.einsum("erd,erf->edf", picked, d_up, preferred_element_type=f32)

        d_mid_norm, mid_gain_grad = norm_back(d_routed, middle[at], scale_mid[at], gain_mid)
        grad_mid = grad_mid + mid_gain_grad
        d_middle = cotangent[at, 0].astype(f32) + d_mid_norm
        d_middles.append(d_middle)
        d_branches.append(d_middle.astype(bf16))

    grad_gate = lax.psum_scatter(acc_gate.astype(bf16), "dp", scatter_dimension=1, tiled=True)
    grad_up = lax.psum_scatter(acc_up.astype(bf16), "dp", scatter_dimension=1, tiled=True)
    grad_down = lax.psum_scatter(acc_down.astype(bf16), "dp", scatter_dimension=2, tiled=True)

    d_branch = jnp.concatenate(d_branches, axis=0)
    d_middle = jnp.concatenate(d_middles, axis=0)
    grad_output = mm(mixed.reshape(total, H * HD), d_branch, TN).astype(bf16)
    grad_output = lax.psum_scatter(grad_output, BOTH, scatter_dimension=0, tiled=True)
    d_mixed = mm(d_branch, out_w, NT).astype(bf16).reshape(micro, rows, H * HD)
    cos_rows = jnp.concatenate([cosine, cosine], axis=-1).reshape(micro, rows, HD)
    sine_rows = jnp.concatenate([-sine_part, sine_part], axis=-1).reshape(micro, rows, HD)
    q_raw = queries.reshape(micro, rows, H * HD)
    d_query, dkv_all, grad_qn = run_backward(
        q_low, kv_all, bias, mixed, d_mixed, logs, q_raw, cos_rows, sine_rows, gain_q[None, :], step_heads, chunk
    )
    grad_qn = grad_qn[0]
    dkv = lax.psum_scatter(dkv_all, "expert", scatter_dimension=0, tiled=False)
    dkv = dkv.reshape(total, KVH, 2 * HD)
    d_key = rotate(dkv[:, :, :HD].astype(f32), cosine, -sine_part)
    d_key, grad_kn = norm_back(d_key, key_pre, scale_k, gain_k)
    d_proj = jnp.concatenate(
        [
            d_query.reshape(total, shards, q_part),
            d_key.astype(bf16).reshape(total, shards, k_part),
            dkv[:, :, HD:].reshape(total, shards, v_part),
        ],
        axis=-1,
    ).reshape(total, -1)
    grad_qkv = mm(d_proj, normed, TN).astype(bf16)
    grad_qkv = lax.psum_scatter(grad_qkv, BOTH, scatter_dimension=0, tiled=True).astype(f32)
    d_normed = mm(d_proj, qkv_w)
    d_in_norm, grad_in = norm_back(d_normed, hidden, scale_in, gain_in)
    input_grad = d_middle + d_in_norm

    gain_grads = jnp.concatenate([grad_in, grad_mid, grad_qn, grad_kn]).reshape(shards, gain_len)
    gain_grads = jnp.pad(gain_grads, ((0, 0), (0, 256 - gain_len % 256)))
    gain_all = lax.all_gather(gain_grads, BOTH, axis=0, tiled=False)
    grad_gains = jnp.sum(lax.dynamic_index_in_dim(gain_all, shard_at, axis=1, keepdims=False), axis=0)
    return (
        jnp.stack(outputs)[:, None],
        input_grad.reshape(micro, 1, rows, width),
        grad_qkv[:q_part].T,
        grad_qkv[q_part : q_part + k_part].T,
        grad_qkv[q_part + k_part :].T,
        grad_output.astype(f32),
        grad_gains[:gain_len],
        grad_gate.astype(f32),
        grad_up.astype(f32),
        grad_down.astype(f32),
    )


def body_fast(
    inputs,
    cotangent,
    membership,
    routes,
    gate_weights,
    pair_order,
    w_query,
    w_key,
    w_value,
    w_output,
    norm_gains,
    w_gate,
    w_up,
    w_down,
):
    micro = inputs.shape[0]
    rows = inputs.shape[2]
    width = inputs.shape[3]
    group_len = membership.shape[2]
    member = lax.axis_index("expert")
    blocks = lax.axis_size("expert")
    shards = blocks * lax.axis_size("dp")
    local_experts = w_gate.shape[0]
    experts = local_experts * blocks
    capacity = rows * TOPK // experts
    step_heads = max(1, 384 // rows)
    total = micro * rows
    q_part, k_part, v_part = w_query.shape[1], w_key.shape[1], w_value.shape[1]
    tie = lax.optimization_barrier

    slot_map, weight_map = jax.vmap(
        lambda r, g, o: slots_of(r, g, o, capacity, experts)
    )(routes[:, 0], gate_weights[:, 0], pair_order[:, 0, 0])
    weight_high = tie(weight_map.astype(bf16))
    weight_low = (weight_map - weight_high.astype(f32)).astype(bf16)

    def padded(values, lanes):
        return jnp.pad(values, ((0, 0), (0, 0), (0, lanes - experts)))

    routing = jnp.concatenate(
        [
            padded(slot_map.astype(bf16), 32),
            padded(weight_high, 32),
            padded(weight_low, ROUTE_LANES - 64),
        ],
        axis=-1,
    )

    gain_len = norm_gains.shape[0]
    gain_shard = jnp.zeros((2048,), bf16).at[:gain_len].set(norm_gains).reshape(16, 128)
    kv_w = jnp.concatenate([w_key.T, w_value.T], axis=0)
    q_w, kv_w, out_w, gain_full = gather_rows(
        [w_query.T, kv_w, w_output, gain_shard], [(3, 0, 1, 2)], 1
    )
    cot_0 = lax.all_gather(cotangent[0, 0], "expert", axis=0, tiled=False)
    q_w, cot_0, cot_1, w_gate, w_up, w_down = tie(
        (q_w, cot_0, cotangent[1, 0], w_gate, w_up, w_down)
    )
    gains = gain_full.reshape(shards, 2048)[:, :gain_len].reshape(-1).astype(f32)
    gain_in = gains[:width]
    gain_mid = gains[width : 2 * width]
    gain_q = gains[2 * width : 2 * width + HD]
    gain_k = gains[2 * width + HD :]
    cot_1 = lax.all_gather(cot_1, "expert", axis=0, tiled=False)
    gate_near, up_near, down_near = ((swap(w, 1), swap(w, 2)) for w in (w_gate, w_up, w_down))

    key_index = jnp.arange(group_len, dtype=jnp.int32)
    start_row = member * rows
    segment = membership[:, 0]
    row_index = start_row + jnp.arange(rows, dtype=jnp.int32)
    seg_rows = lax.dynamic_slice_in_dim(segment, start_row, rows, axis=1)
    before = jnp.sum((segment[:, None, :] < seg_rows[:, :, None]).astype(jnp.int32), axis=2)
    position = jnp.where(seg_rows == 0, row_index[None], PROMPT + row_index[None] - before)
    allowed = (key_index[None, :, None] <= row_index[None, None, :]) & (
        (segment[:, :, None] == 0) | (segment[:, :, None] == seg_rows[:, None, :])
    )
    bias = jnp.tile(jnp.where(allowed, 0.0, MASKED).astype(f32), (1, 1, step_heads))
    frequency = ROPE_BASE ** (-(jnp.arange(HD // 2, dtype=f32) * 2.0 / HD))
    angles = position.astype(f32).reshape(total)[:, None] * frequency[None, :]
    cosine, sine = jnp.cos(angles), jnp.sin(angles)
    cosine = jnp.concatenate([cosine, cosine], axis=-1)
    sine = jnp.concatenate([-sine, sine], axis=-1)
    gain_q, gain_k = gain_q[None, :], gain_k[None, :]

    hidden = inputs[:, 0].astype(f32).reshape(total, width)
    scale_in = rms_scale(hidden)
    normed = (hidden * scale_in * gain_in).astype(bf16)
    q_low, q_raw, kv_own, k_raw, kv_w = run_project(
        normed, q_w, kv_w, cosine, sine, gain_q * (SCALE * LOG2E), gain_k
    )
    q_low, q_raw = (a.reshape(micro, rows, H * HD) for a in (q_low, q_raw))
    kv_own = kv_own.reshape(micro, rows, KVH * 2 * HD)
    kv_all = lax.all_gather(kv_own, "expert", axis=0, tiled=False)
    kv_all, gate_near = tie((kv_all, gate_near))
    chunk = 256
    mixed, logs = run_forward(q_low, kv_all, bias, step_heads, chunk)
    mixed, up_near, down_near = tie((mixed, up_near, down_near))
    parts = [
        (own, near[0], near[1], swap(near[0][:1], 2), swap(near[1][1:], 1))
        for own, near in ((w_gate, gate_near), (w_up, up_near), (w_down, down_near))
    ]

    branch = mm(mixed.reshape(total, H * HD), out_w)
    middle = hidden + branch
    scale_mid = rms_scale(middle)
    routed = (middle * scale_mid * gain_mid).astype(bf16).reshape(micro, rows, width)
    routed = jnp.concatenate([routed, routing], axis=-1)
    routed, cot_1 = tie((routed, cot_1))
    middle = middle.reshape(micro, rows, width)
    scale_mid = scale_mid.reshape(micro, rows, 1)

    mix_parts, d_routeds, d_branches, d_middles = [], [], [], []
    kept = []
    for at, cot in enumerate((cot_0, cot_1)):
        tokens = lax.all_gather(routed[at], "expert", axis=0, tiled=False)
        tokens, parts = tie((tokens, parts))
        kept, mix, d_part = run_experts(tokens, cot, parts, capacity, at, micro, kept)
        kept, d_part, mix, d_routeds = tie((kept, d_part, mix, d_routeds))
        mix_parts.append(mix)
        d_routed = lax.psum_scatter(d_part, "expert", scatter_dimension=0, tiled=True)
        d_routeds.append(d_routed)
    picked, d_result, hidden_low, d_gate, d_up = (
        a.reshape(local_experts, -1, a.shape[-1]) for a in kept
    )

    def weight_grad(rows_in, rows_out):
        return jnp.einsum("era,erb->eab", rows_in, rows_out, preferred_element_type=f32).astype(bf16)

    scattering = [
        scatter_far(weight_grad(hidden_low, d_result), 2),
        scatter_far(weight_grad(picked, d_gate), 1),
        scatter_far(weight_grad(picked, d_up), 1),
    ]
    d_routeds[-1], scattering = tie((d_routeds[-1], scattering))
    expert_grads = [scatter_near(*pieces) for pieces in scattering]
    grad_mid = 0.0
    for at in range(micro):
        d_mid_norm, mid_gain_grad = norm_back(
            d_routeds[at].astype(f32), middle[at], scale_mid[at], gain_mid
        )
        grad_mid = grad_mid + mid_gain_grad
        d_middle = cotangent[at, 0].astype(f32) + d_mid_norm
        d_middles.append(d_middle)
        d_branches.append(d_middle.astype(bf16))

    d_branch = jnp.concatenate(d_branches, axis=0)
    d_middle = jnp.concatenate(d_middles, axis=0)
    d_mixed = mm(d_branch, out_w, NT).astype(bf16).reshape(micro, rows, H * HD)
    cos_rows, sine_rows = (a.reshape(micro, rows, HD) for a in (cosine, sine))
    d_query, dkv_all, grad_qn = run_backward(
        q_low, kv_all, bias, mixed, d_mixed, logs, q_raw, cos_rows, sine_rows, gain_q, step_heads, chunk
    )
    mixed_after, d_query, dkv_all, expert_grads = tie((mixed, d_query, dkv_all, expert_grads))
    grad_output, _ = reduce_rows(mixed_after.reshape(total, H * HD), None, d_branch, 2)
    dkv = lax.psum_scatter(dkv_all, "expert", scatter_dimension=0, tiled=False)
    dkv, grad_output, d_query = tie((dkv, grad_output, d_query))
    d_query = d_query.reshape(total, H * HD)
    dkv = dkv.reshape(total, KVH * 2 * HD)
    mix_parts, dkv = tie((mix_parts, dkv))
    outputs = []
    for at in range(micro):
        mix = lax.psum_scatter(mix_parts[at], "expert", scatter_dimension=0, tiled=True)
        outputs.append((middle[at] + mix.astype(f32)).astype(bf16))
    dkv, dkv_t, grad_kn = run_key_back(dkv, k_raw, cosine, sine, gain_k)
    d_normed = mm(d_query, q_w) + mm(dkv, kv_w)
    d_in_norm, grad_in = norm_back(d_normed, hidden, scale_in, gain_in)
    input_grad = d_middle + d_in_norm
    gain_grads = jnp.concatenate([grad_in, grad_mid, grad_qn[0], grad_kn[0]]).reshape(shards, gain_len)
    grad_qkv, grad_gains = reduce_rows(d_query, dkv_t, normed, 3, gain_grads)
    return (
        jnp.stack(outputs)[:, None],
        input_grad.reshape(micro, 1, rows, width),
        grad_qkv[:q_part].T,
        grad_qkv[q_part : q_part + k_part].T,
        grad_qkv[q_part + k_part :].T,
        grad_output,
        grad_gains[0, :gain_len],
        expert_grads[1],
        expert_grads[2],
        expert_grads[0],
    )


def solution(mesh):
    fast = mesh.shape["dp"] == 4 and mesh.shape["expert"] == 8
    return jax.shard_map(
        body_fast if fast else body_plain,
        mesh=mesh,
        in_specs=(
            P(None, "dp", "expert", None),
            P(None, "dp", "expert", None),
            P(None, "dp", None),
            P(None, "dp", "expert", None),
            P(None, "dp", "expert", None),
            P(None, "dp", "expert", None),
            P(None, ("dp", "expert")),
            P(None, ("dp", "expert")),
            P(None, ("dp", "expert")),
            P(("dp", "expert"), None),
            P(("dp", "expert")),
            P("expert", "dp", None),
            P("expert", "dp", None),
            P("expert", None, "dp"),
        ),
        out_specs=(
            P(None, "dp", "expert", None),
            P(None, "dp", "expert", None),
            P(None, ("dp", "expert")),
            P(None, ("dp", "expert")),
            P(None, ("dp", "expert")),
            P(("dp", "expert"), None),
            P(("dp", "expert")),
            P("expert", "dp", None),
            P("expert", "dp", None),
            P("expert", None, "dp"),
        ),
        check_vma=False,
    )
```

```python
import functools
import math

import jax
import jax.numpy as jnp
from jax import lax
from jax.experimental import pallas as pl
from jax.experimental.pallas import tpu as pltpu
from jax.sharding import PartitionSpec as P

H = 32
KVH = 4
HD = 128
FF = 768
TOPK = 8
PROMPT = 1024
PER_KV = H // KVH

EPSILON = 1e-06
ROPE_BASE = 1000000.0
MASKED = -1e30
LOG2E = math.log2(math.e)
SCALE = HD ** (-0.5)

bf16 = jnp.bfloat16
f32 = jnp.float32
NT = (((1,), (1,)), ((), ()))
TN = (((0,), (0,)), ((), ()))
NN = (((1,), (0,)), ((), ()))
BOTH = ("dp", "expert")
VMEM_LIMIT = 56 * 1024 * 1024


def mm(a, b, dims=NN):
    return lax.dot_general(a, b, dims, preferred_element_type=f32)


def rms_scale(values):
    return lax.rsqrt(jnp.mean(values * values, axis=-1, keepdims=True) + EPSILON)


def norm_back(upstream, values, inv_rms, norm_gain):
    lifted = upstream * norm_gain
    inner_dot = jnp.mean(lifted * values, axis=-1, keepdims=True)
    back_grad = inv_rms * lifted - values * (inv_rms * inv_rms * inv_rms) * inner_dot
    gain_grad = jnp.sum((upstream * values * inv_rms).reshape(-1, values.shape[-1]), axis=0)
    return (back_grad, gain_grad)


def rotate(values, cosine, sine_part):
    half_dim = values.shape[-1] // 2
    first_half = values[..., :half_dim]
    second_half = values[..., half_dim:]
    return jnp.concatenate(
        [
            first_half * cosine - second_half * sine_part,
            second_half * cosine + first_half * sine_part,
        ],
        axis=-1,
    )


def turn(values, cosine, sine):
    return values * cosine + pltpu.roll(values, HD // 2, 1) * sine


def project(x_ref, wq_ref, wkv_ref, cos_ref, sin_ref, gq_ref, gk_ref, q_ref, qraw_ref, kv_ref, kraw_ref, wkv_out):
    x = x_ref[...]
    cosine, sine = cos_ref[...], sin_ref[...]
    for at in range(0, PER_KV * HD, 2 * HD):
        raw = mm(x, wq_ref[at : at + 2 * HD], NT)
        qraw_ref[:, at : at + 2 * HD] = raw
        for lane in (0, HD):
            head = raw[:, lane : lane + HD]
            normed = head * rms_scale(head) * gq_ref[...]
            q_ref[:, at + lane : at + lane + HD] = turn(normed, cosine, sine).astype(bf16)
    piece = HD // PER_KV
    w_k = [wkv_ref[2 * piece * i : 2 * piece * i + piece] for i in range(PER_KV)]
    w_v = [wkv_ref[2 * piece * i + piece : 2 * piece * (i + 1)] for i in range(PER_KV)]
    w_kv = jnp.concatenate(w_k + w_v, axis=0)
    wkv_out[...] = w_kv
    raw = mm(x, w_kv, NT)
    key = raw[:, :HD]
    kraw_ref[...] = key
    normed = key * rms_scale(key) * gk_ref[...]
    kv_ref[:, :HD] = turn(normed, cosine, sine).astype(bf16)
    kv_ref[:, HD:] = raw[:, HD:].astype(bf16)


def run_project(x, wq, wkv, cosine, sine, gain_q, gain_k):
    tokens, width = x.shape
    wide = PER_KV * HD
    whole = lambda a: pl.BlockSpec(a.shape, lambda g: (0, 0))
    cols = lambda n: pl.BlockSpec((tokens, n), lambda g: (0, g))
    rows = lambda n: pl.BlockSpec((n, width), lambda g: (g, 0))
    return pl.pallas_call(
        project,
        grid=(KVH,),
        in_specs=[whole(x), rows(wide), rows(2 * HD), whole(cosine), whole(sine), whole(gain_q), whole(gain_k)],
        out_specs=[cols(wide), cols(wide), cols(2 * HD), cols(HD), rows(2 * HD)],
        out_shape=[
            jax.ShapeDtypeStruct((tokens, H * HD), bf16),
            jax.ShapeDtypeStruct((tokens, H * HD), f32),
            jax.ShapeDtypeStruct((tokens, KVH * 2 * HD), bf16),
            jax.ShapeDtypeStruct((tokens, KVH * HD), f32),
            jax.ShapeDtypeStruct((KVH * 2 * HD, width), bf16),
        ],
        compiler_params=pltpu.CompilerParams(vmem_limit_bytes=VMEM_LIMIT),
        cost_estimate=pl.CostEstimate(
            flops=2 * tokens * width * (H + 2 * KVH) * HD, bytes_accessed=40_000_000, transcendentals=0
        ),
    )(x, wq, wkv, cosine, sine, gain_q, gain_k)


def norm_turn_back(grad, raw, cosine, sine, gain):
    grad = turn(grad, cosine, -sine)
    scale = rms_scale(raw)
    lifted = grad * gain
    inner = jnp.mean(lifted * raw, axis=-1, keepdims=True)
    back = scale * lifted - raw * (scale * scale * scale) * inner
    return back, jnp.sum(grad * raw * scale, axis=0, keepdims=True)


def key_back(dkv_ref, kraw_ref, cos_ref, sin_ref, gk_ref, out_ref, out_t_ref, gain_ref):
    gain_sum = 0.0
    for g in range(KVH):
        key = slice(2 * g * HD, (2 * g + 1) * HD)
        value = slice((2 * g + 1) * HD, (2 * g + 2) * HD)
        grad = dkv_ref[:, key].astype(f32)
        back, part = norm_turn_back(
            grad, kraw_ref[:, g * HD : (g + 1) * HD], cos_ref[...], sin_ref[...], gk_ref[...]
        )
        gain_sum += part
        low = back.astype(bf16)
        out_ref[:, key] = low
        out_t_ref[key] = low.T
        out_ref[:, value] = dkv_ref[:, value]
        out_t_ref[value] = dkv_ref[:, value].T
    gain_ref[...] = gain_sum


def run_key_back(dkv, key_raw, cosine, sine, gain):
    tokens, wide = dkv.shape
    return pl.pallas_call(
        key_back,
        out_shape=[
            jax.ShapeDtypeStruct((tokens, wide), bf16),
            jax.ShapeDtypeStruct((wide, tokens), bf16),
            jax.ShapeDtypeStruct((1, HD), f32),
        ],
        compiler_params=pltpu.CompilerParams(vmem_limit_bytes=VMEM_LIMIT),
    )(dkv, key_raw, cosine, sine, gain)


def attend_forward(step_heads, chunk, q_ref, kv_ref, bias_ref, o_ref, log_ref):
    group_len = bias_ref.shape[1]
    keys = kv_ref[:, 0, :, :HD].reshape(group_len, HD)
    values_t = kv_ref[:, 0, :, HD:].reshape(group_len, HD).T
    rows = q_ref.shape[1]
    for step in range(PER_KV // step_heads):
        heads = range(step * step_heads, (step + 1) * step_heads)
        query = jnp.concatenate([q_ref[0, :, h * HD : (h + 1) * HD] for h in heads], axis=0)
        mixed, row_sum = 0.0, 0.0
        for at in range(0, group_len, chunk):
            scores = mm(keys[at : at + chunk], query, NT)
            prob = jnp.exp2(scores + bias_ref[0, at : at + chunk, :])
            row_sum += jnp.sum(prob, axis=0, keepdims=True)
            mixed += mm(values_t[:, at : at + chunk], prob.astype(bf16))
        out = (mixed / row_sum).T.astype(bf16)
        for i, h in enumerate(heads):
            o_ref[0, :, h * HD : (h + 1) * HD] = out[i * rows : (i + 1) * rows]
        log_ref[0, 0, step : step + 1, :] = jnp.log2(row_sum)


def attend_backward(
    step_heads, chunk, q_ref, kv_ref, bias_ref, o_ref, do_ref, log_ref, raw_ref, cos_ref, sin_ref, gain_ref,
    dq_ref, dkv_ref, gain_out, dk_acc, dv_acc
):
    group_len = bias_ref.shape[1]
    keys = kv_ref[:, 0, :, :HD].reshape(group_len, HD)
    values = kv_ref[:, 0, :, HD:].reshape(group_len, HD)
    keys_t = keys.T
    rows = q_ref.shape[1]
    cosine, sine, gain = cos_ref[0], sin_ref[0], gain_ref[...]

    @pl.when((pl.program_id(0) == 0) & (pl.program_id(1) == 0))
    def _():
        gain_out[...] = jnp.zeros_like(gain_out)

    gain_sum = 0.0
    dk_acc[...] = jnp.zeros_like(dk_acc)
    dv_acc[...] = jnp.zeros_like(dv_acc)
    for step in range(PER_KV // step_heads):
        heads = range(step * step_heads, (step + 1) * step_heads)
        query = jnp.concatenate([q_ref[0, :, h * HD : (h + 1) * HD] for h in heads], axis=0)
        grad = jnp.concatenate([do_ref[0, :, h * HD : (h + 1) * HD] for h in heads], axis=0)
        mixed = jnp.concatenate([o_ref[0, :, h * HD : (h + 1) * HD] for h in heads], axis=0)
        row_dot = jnp.sum((grad.astype(f32) * mixed.astype(f32)).T, axis=0, keepdims=True)
        log_sum = log_ref[0, 0, step : step + 1, :]
        dq_t = 0.0
        for at in range(0, group_len, chunk):
            part = slice(at, at + chunk)
            scores = mm(keys[part], query, NT)
            prob = jnp.exp2(scores + (bias_ref[0, part, :] - log_sum))
            d_prob = mm(values[part], grad, NT)
            d_score = (prob * (d_prob - row_dot)).astype(bf16)
            dv_acc[part] += mm(prob.astype(bf16), grad)
            dk_acc[part] += mm(d_score, query)
            dq_t += mm(keys_t[:, part], d_score)
        out = (dq_t * SCALE).T.astype(bf16).astype(f32)
        for i, h in enumerate(heads):
            head = slice(h * HD, (h + 1) * HD)
            back, part = norm_turn_back(
                out[i * rows : (i + 1) * rows], raw_ref[0, :, head], cosine, sine, gain
            )
            dq_ref[0, :, head] = back.astype(bf16)
            gain_sum += part
    gain_out[...] += gain_sum
    blocks = dkv_ref.shape[0]
    dkv_ref[:, 0, :, :HD] = (dk_acc[...] * (1.0 / LOG2E)).astype(bf16).reshape(blocks, rows, HD)
    dkv_ref[:, 0, :, HD:] = dv_acc[...].astype(bf16).reshape(blocks, rows, HD)


def attention_specs(micro, rows, group_len, blocks, step_heads):
    wide = PER_KV * HD
    q_spec = pl.BlockSpec((1, rows, wide), lambda b, g: (b, 0, g))
    kv_spec = pl.BlockSpec((blocks, 1, rows, 2 * HD), lambda b, g: (0, b, 0, g))
    bias_spec = pl.BlockSpec((1, group_len, step_heads * rows), lambda b, g: (b, 0, 0))
    log_spec = pl.BlockSpec((1, 1, PER_KV // step_heads, step_heads * rows), lambda b, g: (b, g, 0, 0))
    return q_spec, kv_spec, bias_spec, log_spec


def run_forward(query, kv_all, bias, step_heads, chunk):
    micro, rows, _ = query.shape
    blocks = kv_all.shape[0]
    group_len = bias.shape[1]
    q_spec, kv_spec, bias_spec, log_spec = attention_specs(micro, rows, group_len, blocks, step_heads)
    flops = 4 * micro * rows * H * HD * group_len
    return pl.pallas_call(
        functools.partial(attend_forward, step_heads, chunk),
        grid=(micro, KVH),
        in_specs=[q_spec, kv_spec, bias_spec],
        out_specs=[q_spec, log_spec],
        out_shape=[
            jax.ShapeDtypeStruct(query.shape, bf16),
            jax.ShapeDtypeStruct((micro, KVH, PER_KV // step_heads, step_heads * rows), f32),
        ],
        compiler_params=pltpu.CompilerParams(vmem_limit_bytes=VMEM_LIMIT),
        cost_estimate=pl.CostEstimate(
            flops=flops, bytes_accessed=20_000_000, transcendentals=flops // (4 * HD)
        ),
    )(query, kv_all, bias)


def run_backward(query, kv_all, bias, mixed, grad, logs, raw, cosine, sine, gain, step_heads, chunk):
    micro, rows, _ = query.shape
    blocks = kv_all.shape[0]
    group_len = bias.shape[1]
    q_spec, kv_spec, bias_spec, log_spec = attention_specs(micro, rows, group_len, blocks, step_heads)
    flops = 10 * micro * rows * H * HD * group_len
    return pl.pallas_call(
        functools.partial(attend_backward, step_heads, chunk),
        grid=(micro, KVH),
        in_specs=[q_spec, kv_spec, bias_spec, q_spec, q_spec, log_spec, q_spec]
        + [pl.BlockSpec((1, rows, HD), lambda b, g: (b, 0, 0))] * 2
        + [pl.BlockSpec((1, HD), lambda b, g: (0, 0))],
        out_specs=[q_spec, kv_spec, pl.BlockSpec((1, HD), lambda b, g: (0, 0))],
        out_shape=[
            jax.ShapeDtypeStruct(query.shape, bf16),
            jax.ShapeDtypeStruct(kv_all.shape, bf16),
            jax.ShapeDtypeStruct((1, HD), f32),
        ],
        scratch_shapes=[pltpu.VMEM((group_len, HD), f32), pltpu.VMEM((group_len, HD), f32)],
        compiler_params=pltpu.CompilerParams(vmem_limit_bytes=VMEM_LIMIT),
        cost_estimate=pl.CostEstimate(
            flops=flops, bytes_accessed=30_000_000, transcendentals=flops // (10 * HD)
        ),
    )(query, kv_all, bias, mixed, grad, logs, raw, cosine, sine, gain)


MESH = pl.DeviceIdType.MESH


def gather_kernel(phases, count, late, *refs):
    ins, outs, sems = refs[:count], refs[count : 2 * count], refs[2 * count :]
    dp = lax.axis_index("dp"); member = lax.axis_index("expert")
    blocks = lax.axis_size("expert")
    core = member % 2; z = member // 2
    depth = blocks // 2
    sibling = (dp, member + 1 - 2 * core)
    by_x = (dp + 1 - 2 * (dp % 2), member)
    by_y = ((dp + 2) % 4, member)
    x_at, y_at, far_at = by_x[0], by_y[0], 3 - dp
    above, below = (dp, member + 2), (dp, member - 2)
    barrier = pltpu.get_barrier_semaphore()
    peers = [(sibling, None), (by_x, None), (by_y, None), (above, z < depth - 1), (below, z > 0)]
    for peer, ok in peers:
        if ok is None:
            pl.semaphore_signal(barrier, inc=1, device_id=peer, device_id_type=MESH)
        else:
            @pl.when(ok)
            def _(peer=peer):
                pl.semaphore_signal(barrier, inc=1, device_id=peer, device_id_type=MESH)
    @pl.when((z == 0) | (z == depth - 1))
    def _(): pl.semaphore_wait(barrier, 4)
    @pl.when((z > 0) & (z < depth - 1))
    def _(): pl.semaphore_wait(barrier, 5)

    def guarded(ok, run):
        if ok is None: run()
        else: pl.when(ok)(run)

    class Item:
        pass

    def make(i):
        src, out = ins[i], outs[i]
        flat = i in late
        rows = src.shape[0]
        half = rows // 2
        (own_sem, sz, rz, sxy, rxy, sc, rc) = sems[i * 7 : (i + 1) * 7]
        def at(d, s, lo=0, n=rows):
            first = s * 2 + core if flat else d * blocks + s * 2 + core
            return out.at[pl.ds(pl.multiple_of(first * rows + lo, 16 if half % 16 == 0 else 8), n)]
        def copy(a, b, ss, rs, to):
            return pltpu.make_async_remote_copy(src_ref=a, dst_ref=b, send_sem=ss, recv_sem=rs, device_id=to, device_id_type=MESH)
        def block(d, s):
            return at(d, s)
        it = Item()
        def local():
            return pltpu.make_async_copy(src, at(dp, z), own_sem)
        def up(s, ref): return copy(ref, at(dp, s), sz.at[0, s], rz.at[s], above)
        def down(s, ref): return copy(ref, at(dp, s), sz.at[1, s], rz.at[s], below)
        def to_x(s, ref): return copy(ref, at(dp, s), sxy.at[0, s], rxy.at[0, s], by_x)
        def to_y(s, ref): return copy(ref, at(dp, s), sxy.at[1, s], rxy.at[1, s], by_y)
        def half_y(s):
            return copy(at(x_at, s, 0, half), at(x_at, s, 0, half), sxy.at[2, s], rxy.at[2, s], by_y)
        def half_x(s):
            return copy(at(y_at, s, half, half), at(y_at, s, half, half), sxy.at[3, s], rxy.at[3, s], by_x)
        def to_core(r, d, s, ref): return copy(ref, at(d, s), sc.at[r, s], rc.at[r, s], sibling)
        def spread(s, ref):
            if not flat:
                to_x(s, ref).start(); to_y(s, ref).start()
            to_core(0, dp, s, ref).start()
        def start():
            local().start()
            guarded(z < depth - 1, lambda: up(z, src).start())
            guarded(z > 0, lambda: down(z, src).start())
            spread(z, src)
        def z_event(s, ok, rising):
            def run():
                up(s, at(dp, s)).wait_recv()
                if rising: guarded(z < depth - 1, lambda: up(s, at(dp, s)).start())
                else: guarded(z > 0, lambda: down(s, at(dp, s)).start())
                spread(s, at(dp, s))
            pl.when(ok)(run)
        def near_event(s, ok):
            def run():
                to_x(s, at(dp, s)).wait_recv()
                half_y(s).start()
                to_core(1, x_at, s, at(x_at, s)).start()
                to_y(s, at(dp, s)).wait_recv()
                half_x(s).start()
                to_core(2, y_at, s, at(y_at, s)).start()
            guarded(ok, run)
        def far_event(s, ok):
            def run():
                half_y(s).wait_recv(); half_x(s).wait_recv()
                to_core(3, far_at, s, at(far_at, s)).start()
            guarded(ok, run)
        owners = (dp,) if flat else (dp, x_at, y_at, far_at)
        def core_wait(s):
            for r, d in enumerate(owners):
                to_core(r, d, s, at(d, s)).wait_recv()
        def finish():
            local().wait()
            for s in range(depth):
                if not flat:
                    for c in (to_x(s, at(dp, s)), to_y(s, at(dp, s)), half_y(s), half_x(s)): c.wait_send()
                for r, d in enumerate(owners): to_core(r, d, s, at(d, s)).wait_send()
                guarded((z >= s) & (z < depth - 1), lambda: up(s, at(dp, s)).wait_send())
                guarded((z <= s) & (z > 0), lambda: down(s, at(dp, s)).wait_send())
        it.start, it.z_event, it.near_event, it.far_event, it.core_wait, it.finish = start, z_event, near_event, far_event, core_wait, finish
        return it
    items = [make(i) for i in range(count)]
    def around(d):
        if d == 0: return [(z, None, True)]
        return [(z - d, z >= d, True), (z + d, z + d < depth, False)]
    for n, phase in enumerate(phases):
        its = [items[i] for i in phase]
        for it in its: it.start()
        lates = [items[i] for i in late]
        for it in lates: it.start()
        for d in range(1, depth + 2):
            if d < depth:
                for s, ok, rising in around(d):
                    for it in its: it.z_event(s, ok, rising)
            if d - 1 < depth:
                for s, ok, _ in around(d - 1):
                    for it in its: it.near_event(s, ok)
            if d < depth:
                for s, ok, rising in around(d):
                    for it in lates: it.z_event(s, ok, rising)
            if d - 2 >= 0:
                for s, ok, _ in around(d - 2):
                    for it in its: it.far_event(s, ok)
    for it in items:
        for s in range(depth): it.core_wait(s)
    for it in items: it.finish()

def gather_rows(arrays, phases, cid, late=()):
    shards = lax.axis_size("dp") * lax.axis_size("expert")
    depth = lax.axis_size("expert") // 2
    D = pltpu.SemaphoreType.DMA
    sems = []
    for _ in arrays:
        sems += [D, D((2, depth)), D((depth,)), D((4, depth)), D((4, depth)), D((4, depth)), D((4, depth))]
    return pl.pallas_call(
        functools.partial(gather_kernel, phases, len(arrays), late),
        out_shape=[
            jax.ShapeDtypeStruct(((2 * depth if i in late else shards) * a.shape[0],) + a.shape[1:], a.dtype)
            for i, a in enumerate(arrays)
        ],
        in_specs=[pl.BlockSpec(memory_space=pl.ANY)] * len(arrays),
        out_specs=[pl.BlockSpec(memory_space=pl.ANY)] * len(arrays),
        scratch_shapes=sems,
        compiler_params=pltpu.CompilerParams(collective_id=cid, has_side_effects=True),
        cost_estimate=pl.CostEstimate(flops=0, bytes_accessed=400_000_000, transcendentals=0),
    )(*arrays)


def reduce_kernel(rows, cuts, a_ref, extra_ref, b_ref, g_ref, o_ref, go_ref, sib, got, own, far, near, plane, got_z,
                  s0, r0, s1, r1, s2, r2, s3, r3, g_acc, g_got, g_z, gs, gr, gsz, grz):
    dp = lax.axis_index("dp"); member = lax.axis_index("expert")
    core = member % 2; z = member // 2
    sibling = (dp, member + 1 - 2 * core)
    by_x = (dp + 1 - 2 * (dp % 2), member)
    by_y = ((dp + 2) % 4, member)
    x_at, y_at = by_x[0], by_y[0]
    far_at = 3 - dp
    half = rows // 2
    depth = lax.axis_size("expert") // 2
    barrier = pltpu.get_barrier_semaphore()
    peers = [sibling, by_x, by_y] + [(dp, ((z + d) % depth) * 2 + core) for d in range(1, depth)]
    for peer in peers:
        pl.semaphore_signal(barrier, inc=1, device_id=peer, device_id_type=MESH)
    pl.semaphore_wait(barrier, len(peers))

    def pick(table):
        at = table[depth-1]
        for i in range(depth - 1):
            at = jnp.where(z == i, table[i], at)
        return at
    orders = [[3, 3, 0, 0], [2, 0, 3, 1], [1, 2, 1, 2], [0, 1, 2, 3]]
    targets = [pick(t) for t in orders]
    cols = b_ref.shape[1] // cuts

    def copy(src, dst, ssem, rsem, to):
        return pltpu.make_async_remote_copy(src_ref=src, dst_ref=dst, send_sem=ssem, recv_sem=rsem, device_id=to, device_id_type=MESH)

    blocks = 2 * depth
    piece = (rows - HD) // 2

    def product(half_of, k, put):
        spot = targets[k] * 2 + half_of

        def step(i, _):
            shard = (i // cuts) * blocks + spot
            at = (i // cuts) * rows
            col = pl.ds(pl.multiple_of((i % cuts) * cols, cols), cols)
            part = mm(a_ref[:, pl.ds(pl.multiple_of(shard * HD, HD), HD)], b_ref[:, col], TN)
            put(pl.ds(pl.multiple_of(at, 16), HD), col, part)
            if piece:
                base = (shard // PER_KV) * (2 * HD) + (shard % PER_KV) * piece
                small = jnp.concatenate(
                    [
                        extra_ref[pl.ds(pl.multiple_of(base, 16), piece), :],
                        extra_ref[pl.ds(pl.multiple_of(base + HD, 16), piece), :],
                    ],
                    axis=0,
                )
                put(pl.ds(pl.multiple_of(at + HD, 16), 2 * piece), col, mm(small, b_ref[:, col]))
            return 0

        lax.fori_loop(0, 4 * cuts, step, 0)

    def gain_hop(i, src, to):
        return copy(src, g_got.at[i, pl.ds(0, src.shape[0])], gs.at[i], gr.at[i], to)
    hops = {}
    def gain_step(i):
        rows4 = lambda at: pl.ds(pl.multiple_of(at * 8, 8), 8)
        if i == 0:
            hops[0] = gain_hop(0, g_ref.at[pl.ds(pl.multiple_of((1 - core) * 32, 32), 32)], sibling)
        elif i == 1:
            hops[0].wait_recv()
            g_acc[...] = g_ref[pl.ds(pl.multiple_of(core * 32, 32), 32)] + g_got[0]
            hops[1] = gain_hop(1, g_acc.at[pl.ds(pl.multiple_of((1 - dp // 2) * 16, 16), 16)], by_y)
        elif i == 2:
            hops[1].wait_recv()
            mine = pl.ds(pl.multiple_of((dp // 2) * 16, 16), 16)
            g_acc[mine] += g_got[1, :16]
            hops[2] = gain_hop(2, g_acc.at[rows4(x_at)], by_x)
        elif i == 3:
            hops[2].wait_recv()
            g_acc[rows4(dp)] += g_got[2, :8]
            for d in range(1, depth):
                to = (z + d) % depth
                hops[2 + d] = copy(g_acc.at[pl.ds(dp * 8 + to, 1)], g_z.at[z], gsz.at[d - 1], grz.at[z], (dp, to * 2 + core))
        if i < 3:
            hops[i].start()
        else:
            for d in range(1, depth):
                hops[2 + d].start()
    def gain_end():
        total = g_acc[pl.ds(dp * 8 + z, 1)]
        for d in range(1, depth):
            src = (z + d) % depth
            copy(g_acc.at[pl.ds(dp * 8, 1)], g_z.at[src], gsz.at[0], grz.at[src], sibling).wait_recv()
            total += g_z[src]
        go_ref[...] = total
        for i in hops:
            hops[i].wait_send()
    sib_copies, far_copies, near_copies, z_copies = {}, {}, {}, {}
    def sib_step(k):
        slot = k % 2
        if k >= 2:
            sib_copies[k - 2].wait_send()
        def put(r, c, part):
            sib[slot, r, c] = part.astype(bf16)
        product(1 - core, k, put)
        sib_copies[k] = copy(sib.at[slot], got.at[k], s0.at[slot], r0.at[k], sibling)
        sib_copies[k].start()
    def blk(at):
        return pl.ds(pl.multiple_of(at * rows, 16), rows)
    def own_step(k):
        sib_copies[k].wait_recv()
        def put(r, c, part):
            own[k, r, c] = (part + got[k, r, c].astype(f32)).astype(bf16)
        product(core, k, put)
        base = pl.multiple_of(far_at * rows, 16)
        far_copies[k] = (
            copy(own.at[k, pl.ds(base, half)], far.at[k, 0], s1.at[k, 0], r1.at[k, 0], by_x),
            copy(own.at[k, pl.ds(pl.multiple_of(base + half, 16), half)], far.at[k, 1], s1.at[k, 1], r1.at[k, 1], by_y),
        )
        for c in far_copies[k]: c.start()
    def near_step(k):
        a, b = far_copies[k]
        a.wait_recv()
        rng = pl.ds(pl.multiple_of(y_at * rows, 16), half)
        own[k, rng] = (own[k, rng].astype(f32) + far[k, 0].astype(f32)).astype(bf16)
        to_y = copy(own.at[k, blk(y_at)], near.at[k, 1], s2.at[k, 1], r2.at[k, 1], by_y)
        to_y.start()
        b.wait_recv()
        rng = pl.ds(pl.multiple_of(x_at * rows + half, 16), half)
        own[k, rng] = (own[k, rng].astype(f32) + far[k, 1].astype(f32)).astype(bf16)
        to_x = copy(own.at[k, blk(x_at)], near.at[k, 0], s2.at[k, 0], r2.at[k, 0], by_x)
        to_x.start()
        near_copies[k] = (to_x, to_y)
    def plane_step(k):
        for c in near_copies[k]: c.wait_recv()
        total = own[k, blk(dp)].astype(f32) + near[k, 0].astype(f32) + near[k, 1].astype(f32)
        if k < depth - 1:
            plane[k] = total.astype(bf16)
            to = (dp, targets[k] * 2 + core)
            z_copies[k] = copy(plane.at[k], got_z.at[z], s3.at[k], r3.at[z], to)
            z_copies[k].start()
        else:
            o_ref[...] = total
    gain_step(0)
    sib_step(0); sib_step(1)
    own_step(0)
    gain_step(1)
    sib_step(2)
    own_step(1)
    gain_step(2)
    near_step(0)
    sib_step(3)
    own_step(2)
    gain_step(3)
    near_step(1)
    plane_step(0)
    own_step(3)
    near_step(2)
    plane_step(1)
    near_step(3)
    plane_step(2)
    plane_step(3)
    for d in range(1, depth):
        src = (z + d) % depth
        copy(plane.at[0], got_z.at[src], s3.at[0], r3.at[src], sibling).wait_recv()
        o_ref[...] += got_z[src].astype(f32)
    gain_end()
    for k in range(depth):
        if k >= 2: sib_copies[k].wait_send()
        for c in far_copies[k]: c.wait_send()
        for c in near_copies[k]: c.wait_send()
        if k < depth - 1: z_copies[k].wait_send()

def reduce_rows(a, extra, b, cid, gains=None):
    tokens, width = b.shape
    depth = 4
    rows = HD + (0 if extra is None else extra.shape[0] // 32)
    if extra is None:
        extra = jnp.zeros((16, 128), bf16)
    D = pltpu.SemaphoreType.DMA
    lanes = 256
    padded = jnp.zeros((32, lanes), f32)
    if gains is not None:
        padded = jnp.pad(gains, ((0, 0), (0, lanes - gains.shape[1])))
    padded = padded.reshape(4, depth, 2, lanes).transpose(2, 0, 1, 3)
    padded = jnp.pad(padded, ((0, 0), (0, 0), (0, 8 - depth), (0, 0))).reshape(64, lanes)
    return pl.pallas_call(
        functools.partial(reduce_kernel, rows, 4),
        out_shape=[jax.ShapeDtypeStruct((rows, width), f32), jax.ShapeDtypeStruct((1, lanes), f32)],
        in_specs=[pl.BlockSpec(memory_space=pltpu.VMEM)] * 4,
        out_specs=[pl.BlockSpec(memory_space=pltpu.VMEM)] * 2,
        scratch_shapes=[
            pltpu.VMEM((2, 4 * rows, width), bf16),
            pltpu.VMEM((depth, 4 * rows, width), bf16),
            pltpu.VMEM((depth, 4 * rows, width), bf16),
            pltpu.VMEM((depth, 2, rows // 2, width), bf16),
            pltpu.VMEM((depth, 2, rows, width), bf16),
            pltpu.VMEM((depth - 1, rows, width), bf16),
            pltpu.VMEM((depth, rows, width), bf16),
            D((2,)), D((depth,)), D((depth, 2)), D((depth, 2)), D((depth, 2)), D((depth, 2)), D((depth - 1,)), D((depth,)),
            pltpu.VMEM((32, lanes), f32), pltpu.VMEM((3, 32, lanes), f32), pltpu.VMEM((depth, 1, lanes), f32),
            D((3,)), D((3,)), D((depth - 1,)), D((depth,)),
        ],
        compiler_params=pltpu.CompilerParams(vmem_limit_bytes=60*1024*1024, collective_id=cid, has_side_effects=True),
        cost_estimate=pl.CostEstimate(flops=2*tokens*32*rows*width, bytes_accessed=10_000_000, transcendentals=0),
    )(a, extra, b, padded)


ROUTE_LANES = 128


def picks_of(routing, first, local_experts, capacity):
    rows = routing.shape[0]
    lanes = lax.broadcasted_iota(jnp.int32, (rows, ROUTE_LANES), 1)
    places = lax.broadcasted_iota(jnp.int32, (rows, local_experts * capacity), 1)
    hit, weighted = None, 0.0
    for e in range(local_experts):

        def column(base):
            return jnp.sum(jnp.where(lanes == base + first + e, routing, 0.0), axis=1, keepdims=True)

        slot = column(0).astype(jnp.int32)
        here = places == jnp.where(slot >= 0, slot + e * capacity, -1)
        hit = here if hit is None else hit | here
        weighted = weighted + jnp.where(here, column(32) + column(64), 0.0)
    return jnp.where(hit, 1.0, 0.0).astype(bf16), weighted.astype(bf16)


def pick_kernel(capacity, local_experts, n_alias, tok_ref, cot_ref, *refs):
    x_ref, dy_ref = refs[n_alias:]
    width = cot_ref.shape[2]
    first = lax.axis_index("expert") * local_experts
    routing = tok_ref[0, :, width:]
    hit, _ = picks_of(routing.astype(f32), first, local_experts, capacity)
    x = mm(hit, tok_ref[0, :, :width], TN).astype(bf16)
    rows = mm(hit, routing, TN)
    lanes = lax.broadcasted_iota(jnp.int32, rows.shape, 1)
    owner = lax.broadcasted_iota(jnp.int32, rows.shape, 0) // capacity
    at = lanes - first - owner
    weight = jnp.sum(jnp.where((at == 32) | (at == 64), rows, 0.0), axis=1, keepdims=True)
    dy = (mm(hit, cot_ref[0], TN) * weight).astype(bf16)
    for e in range(local_experts):
        x_ref[e, 0, 0] = x[e * capacity : (e + 1) * capacity]
        dy_ref[e, 0, 0] = dy[e * capacity : (e + 1) * capacity]


def expert_kernel(n_alias, *refs):
    x_ref, dy_ref = refs[:2]
    parts = (refs[2:7], refs[7:12], refs[12:17])
    z_ref, dg_ref, du_ref, y_ref, dx_ref, wg, wu, wd, sems = refs[17 + n_alias :]
    local_experts, width, _ = wg.shape
    at = lax.axis_index("dp")
    size = width // 4
    places = (at, at + 1 - 2 * (at % 2), (at + 2) % 4, 3 - at, 3 - at)

    def copies(e):
        out = []
        for m, full in enumerate((wg, wu, wd)):
            for p in range(4):
                part = parts[m][p] if p < 3 else parts[m][3 + e]
                src = part.at[e] if p < 3 else part.at[0]
                where = pl.ds(pl.multiple_of(places[p] * size, size), size)
                dst = full.at[e, where, :] if m < 2 else full.at[e, :, where]
                out.append(pltpu.make_async_copy(src, dst, sems.at[e, m, p]))
        return out

    expert, chunk = pl.program_id(0), pl.program_id(1)

    @pl.when((expert == 0) & (chunk == 0))
    def _():
        for e in range(local_experts):
            for c in copies(e):
                c.start()

    for e in range(local_experts):

        @pl.when((expert == e) & (chunk == 0))
        def _(e=e):
            for c in copies(e):
                c.wait()

    x, dy = x_ref[0, 0], dy_ref[0, 0]
    gate = mm(x, wg[expert])
    up = mm(x, wu[expert])
    d_hidden = mm(dy, wd[expert], NT)
    sig = 1.0 / (1.0 + jnp.exp(-gate))
    silu = gate * sig
    z = (silu * up).astype(bf16)
    d_gate = (d_hidden * up * sig * (1.0 + gate * (1.0 - sig))).astype(bf16)
    d_up = (d_hidden * silu).astype(bf16)
    z_ref[0, 0] = z
    dg_ref[0, 0] = d_gate
    du_ref[0, 0] = d_up
    dx_ref[0] = (mm(d_gate, wg[expert], NT) + mm(d_up, wu[expert], NT)).astype(bf16)
    y_ref[0] = mm(z, wd[expert]).astype(bf16)


def sum_kernel(capacity, routing_ref, y_ref, dx_ref, mix_ref, da_ref):
    local_experts, _, _, width = y_ref.shape
    first = lax.axis_index("expert") * local_experts
    hit, weighted = picks_of(routing_ref[0].astype(f32), first, local_experts, capacity)
    da_ref[...] = mm(hit, dx_ref[...].reshape(local_experts * capacity, width)).astype(bf16)
    mix_ref[...] = mm(weighted, y_ref[...].reshape(local_experts * capacity, width)).astype(bf16)


def run_experts(tokens, cot, parts, capacity, batch_at, micro, earlier):
    blocks, rows, width = cot.shape
    local_experts, _, hidden = parts[0][0].shape
    flat = [p for group in parts for p in group]
    any_spec = pl.BlockSpec(memory_space=pl.ANY)
    params = pltpu.CompilerParams(vmem_limit_bytes=VMEM_LIMIT)
    slots = blocks * capacity
    picked_spec = pl.BlockSpec((local_experts, 1, 1, capacity, width), lambda b: (0, batch_at, b, 0, 0))
    picked = jax.ShapeDtypeStruct((local_experts, micro, blocks, capacity, width), bf16)
    x, dy = pl.pallas_call(
        functools.partial(pick_kernel, capacity, local_experts, len(earlier[:2])),
        grid=(blocks,),
        in_specs=[
            pl.BlockSpec((1, rows, tokens.shape[2]), lambda b: (b, 0, 0)),
            pl.BlockSpec((1, rows, width), lambda b: (b, 0, 0)),
        ]
        + [any_spec] * len(earlier[:2]),
        out_specs=[picked_spec] * 2,
        out_shape=[picked] * 2,
        input_output_aliases={2 + i: i for i in range(len(earlier[:2]))},
        compiler_params=params,
        cost_estimate=pl.CostEstimate(
            flops=4 * slots * local_experts * rows * width, bytes_accessed=25_000_000, transcendentals=0
        ),
    )(tokens, cot, *[a.reshape(picked.shape) for a in earlier[:2]])
    x, dy = (a.reshape(local_experts, micro, slots, width) for a in (x, dy))
    chunk = slots // 2
    row_spec = pl.BlockSpec((1, 1, chunk, width), lambda e, i: (e, batch_at, i, 0))
    hid_spec = pl.BlockSpec((1, 1, chunk, hidden), lambda e, i: (e, batch_at, i, 0))
    out_spec = pl.BlockSpec((1, chunk, width), lambda e, i: (e, i, 0))
    hid = jax.ShapeDtypeStruct((local_experts, micro, slots, hidden), bf16)
    out = jax.ShapeDtypeStruct((local_experts, slots, width), bf16)
    z, dg, du, y, dx = pl.pallas_call(
        functools.partial(expert_kernel, len(earlier[2:])),
        grid=(local_experts, 2),
        in_specs=[row_spec, row_spec] + [any_spec] * (len(flat) + len(earlier[2:])),
        out_specs=[hid_spec] * 3 + [out_spec] * 2,
        out_shape=[hid] * 3 + [out] * 2,
        input_output_aliases={2 + len(flat) + i: i for i in range(len(earlier[2:]))},
        scratch_shapes=[
            pltpu.VMEM((local_experts, width, hidden), bf16),
            pltpu.VMEM((local_experts, width, hidden), bf16),
            pltpu.VMEM((local_experts, hidden, width), bf16),
            pltpu.SemaphoreType.DMA((local_experts, 3, 4)),
        ],
        compiler_params=params,
        cost_estimate=pl.CostEstimate(
            flops=12 * local_experts * slots * width * hidden, bytes_accessed=50_000_000, transcendentals=0
        ),
    )(x, dy, *flat, *earlier[2:])
    y, dx = (a.reshape(local_experts, blocks, capacity, width) for a in (y, dx))
    part_spec = pl.BlockSpec((local_experts, 1, capacity, width), lambda b: (0, b, 0, 0))
    sums = jax.ShapeDtypeStruct((blocks * rows, width), bf16)
    sums_spec = pl.BlockSpec((rows, width), lambda b: (b, 0))
    mix, da = pl.pallas_call(
        functools.partial(sum_kernel, capacity),
        grid=(blocks,),
        in_specs=[
            pl.BlockSpec((1, rows, ROUTE_LANES), lambda b: (b, 0, width // ROUTE_LANES)),
            part_spec,
            part_spec,
        ],
        out_specs=[sums_spec] * 2,
        out_shape=[sums] * 2,
        compiler_params=params,
        cost_estimate=pl.CostEstimate(
            flops=4 * slots * local_experts * rows * width, bytes_accessed=25_000_000, transcendentals=0
        ),
    )(tokens, y, dx)
    return [x, dy, z, dg, du], mix, da


def slots_of(route_ids, gate_vals, ranking, capacity, experts):
    rows = route_ids.shape[0]
    pair_experts = route_ids.reshape(-1)
    earlier = (pair_experts[None, :] == pair_experts[:, None]) & (
        ranking[None, :] < ranking[:, None]
    )
    slot = jnp.sum(earlier.astype(jnp.int32), axis=1).reshape(rows, -1)
    kept = slot < capacity
    chosen = route_ids[:, :, None] == jnp.arange(experts, dtype=jnp.int32)[None, None, :]
    chosen = chosen & kept[:, :, None]
    slot_map = jnp.sum(jnp.where(chosen, slot[:, :, None] + 1, 0), axis=1).astype(f32) - 1.0
    weight_map = jnp.sum(jnp.where(chosen, gate_vals[:, :, None], 0.0), axis=1)
    return slot_map, weight_map


def swap(values, bit):
    return lax.ppermute(values, "dp", [(i, i ^ bit) for i in range(lax.axis_size("dp"))])


def scatter_far(total, axis):
    at = lax.axis_index("dp")
    size = total.shape[axis] // 4

    def part(bits):
        return lax.dynamic_slice_in_dim(total, (at ^ bits) * size, size, axis=axis)

    far = part(3)
    return [swap(far[:1], 1), swap(far[1:], 2), part(1), part(2), part(0)]


def scatter_near(for_y, for_x, near_x, near_y, own):
    half_y = (near_y[:1].astype(f32) + for_y.astype(f32)).astype(bf16)
    half_x = (near_x[1:].astype(f32) + for_x.astype(f32)).astype(bf16)
    near_y = jnp.concatenate([half_y, near_y[1:]], axis=0)
    near_x = jnp.concatenate([near_x[:1], half_x], axis=0)
    by_x, by_y = swap(near_x, 1), swap(near_y, 2)
    return own.astype(f32) + by_x.astype(f32) + by_y.astype(f32)


def body_plain(
    inputs,
    cotangent,
    membership,
    routes,
    gate_weights,
    pair_order,
    w_query,
    w_key,
    w_value,
    w_output,
    norm_gains,
    w_gate,
    w_up,
    w_down,
):
    micro = inputs.shape[0]
    rows = inputs.shape[2]
    width = inputs.shape[3]
    group_len = membership.shape[2]
    member = lax.axis_index("expert")
    blocks = lax.axis_size("expert")
    shards = blocks * lax.axis_size("dp")
    shard_at = lax.axis_index("dp") * blocks + member
    local_experts = w_gate.shape[0]
    experts = local_experts * blocks
    capacity = rows * TOPK // experts
    step_heads = max(1, 384 // rows)
    total = micro * rows
    q_part, k_part, v_part = w_query.shape[1], w_key.shape[1], w_value.shape[1]

    gain_len = norm_gains.shape[0]
    gain_shard = jnp.zeros((2048,), bf16).at[:gain_len].set(norm_gains).reshape(16, 128)
    gain_full = lax.all_gather(gain_shard, BOTH, axis=0, tiled=True)
    gains = gain_full.reshape(shards, 2048)[:, :gain_len].reshape(-1).astype(f32)
    gain_in = gains[:width]
    gain_mid = gains[width : 2 * width]
    gain_q = gains[2 * width : 2 * width + HD]
    gain_k = gains[2 * width + HD :]

    qkv_w = lax.all_gather(
        jnp.concatenate([w_query.T, w_key.T, w_value.T], axis=0), BOTH, axis=0, tiled=True
    )
    out_w = lax.all_gather(w_output, BOTH, axis=0, tiled=True)
    wg = lax.all_gather(w_gate, "dp", axis=1, tiled=True)
    wu = lax.all_gather(w_up, "dp", axis=1, tiled=True)
    wd = lax.all_gather(w_down, "dp", axis=2, tiled=True)

    slot_map, weight_map = jax.vmap(
        lambda r, g, o: slots_of(r, g, o, capacity, experts)
    )(routes[:, 0], gate_weights[:, 0], pair_order[:, 0, 0])
    routing = jnp.concatenate([slot_map, weight_map], axis=-1)
    routing = lax.all_gather(routing, "expert", axis=0, tiled=False)
    mine = member * local_experts
    slot_mine = lax.dynamic_slice_in_dim(routing, mine, local_experts, axis=3)
    weight_mine = lax.dynamic_slice_in_dim(routing, experts + mine, local_experts, axis=3)
    slot_mine = jnp.transpose(slot_mine, (1, 3, 0, 2))
    weight_mine = jnp.transpose(weight_mine, (1, 3, 0, 2))
    slot_ids = jnp.arange(capacity, dtype=f32)
    hit = slot_mine[:, :, :, None, :] == slot_ids[None, None, None, :, None]
    pick = hit.astype(bf16)
    weighted = jnp.where(hit, weight_mine[:, :, :, None, :], 0.0)
    slot_weight = jnp.sum(weighted, axis=-1)
    weighted = weighted.astype(bf16)

    key_index = jnp.arange(group_len, dtype=jnp.int32)
    start_row = member * rows
    segment = membership[:, 0]
    row_index = start_row + jnp.arange(rows, dtype=jnp.int32)
    seg_rows = lax.dynamic_slice_in_dim(segment, start_row, rows, axis=1)
    before = jnp.sum((segment[:, None, :] < seg_rows[:, :, None]).astype(jnp.int32), axis=2)
    position = jnp.where(seg_rows == 0, row_index[None], PROMPT + row_index[None] - before)
    allowed = (key_index[None, :, None] <= row_index[None, None, :]) & (
        (segment[:, :, None] == 0) | (segment[:, :, None] == seg_rows[:, None, :])
    )
    bias = jnp.tile(jnp.where(allowed, 0.0, MASKED).astype(f32), (1, 1, step_heads))
    frequency = ROPE_BASE ** (-(jnp.arange(HD // 2, dtype=f32) * 2.0 / HD))
    angles = position.astype(f32).reshape(total)[:, None] * frequency[None, :]
    cosine = jnp.cos(angles)[:, None, :]
    sine_part = jnp.sin(angles)[:, None, :]

    hidden = inputs[:, 0].astype(f32).reshape(total, width)
    scale_in = rms_scale(hidden)
    normed = (hidden * scale_in * gain_in).astype(bf16)
    proj = mm(normed, qkv_w, NT).reshape(total, shards, q_part + k_part + v_part)
    queries = proj[:, :, :q_part].reshape(total, H, HD)
    key_pre = proj[:, :, q_part : q_part + k_part].reshape(total, KVH, HD)
    value = proj[:, :, q_part + k_part :].reshape(total, KVH, HD).astype(bf16)
    scale_q = rms_scale(queries)
    scale_k = rms_scale(key_pre)
    q_low = rotate(queries * scale_q * (gain_q * (SCALE * LOG2E)), cosine, sine_part).astype(bf16)
    q_low = q_low.reshape(micro, rows, H * HD)
    k_low = rotate(key_pre * scale_k * gain_k, cosine, sine_part).astype(bf16)
    kv_own = jnp.concatenate([k_low, value], axis=-1).reshape(micro, rows, KVH * 2 * HD)
    kv_all = lax.all_gather(kv_own, "expert", axis=0, tiled=False)
    chunk = 256
    mixed, logs = run_forward(q_low, kv_all, bias, step_heads, chunk)

    branch = mm(mixed.reshape(total, H * HD), out_w)
    middle = hidden + branch
    scale_mid = rms_scale(middle)
    routed = (middle * scale_mid * gain_mid).astype(bf16).reshape(micro, rows, width)
    middle = middle.reshape(micro, rows, width)
    scale_mid = scale_mid.reshape(micro, rows, 1)

    outputs, d_branches, d_middles = [], [], []
    acc_gate = acc_up = acc_down = 0.0
    grad_mid = 0.0
    slots = blocks * capacity
    for at in range(micro):
        d_out = lax.all_gather(cotangent[at, 0], "expert", axis=0, tiled=False)
        tokens = lax.all_gather(routed[at], "expert", axis=0, tiled=False)
        picked = jnp.einsum("ebst,btd->ebsd", pick[at], tokens, preferred_element_type=f32)
        picked = picked.astype(bf16).reshape(local_experts, slots, width)
        d_result = jnp.einsum("ebst,btd->ebsd", pick[at], d_out, preferred_element_type=f32)
        d_result = (d_result * slot_weight[at][..., None]).astype(bf16)
        d_result = d_result.reshape(local_experts, slots, width)
        gate_pre = jnp.einsum("erd,edf->erf", picked, wg, preferred_element_type=f32)
        up_pre = jnp.einsum("erd,edf->erf", picked, wu, preferred_element_type=f32)
        d_hidden = jnp.einsum("erd,efd->erf", d_result, wd, preferred_element_type=f32)
        sigmoid_g = jax.nn.sigmoid(gate_pre)
        silu_g = gate_pre * sigmoid_g
        hidden_low = (silu_g * up_pre).astype(bf16)
        d_gate = (d_hidden * up_pre * sigmoid_g * (1.0 + gate_pre * (1.0 - sigmoid_g))).astype(bf16)
        d_up = (d_hidden * silu_g).astype(bf16)
        d_rows = jnp.einsum("erf,edf->erd", d_gate, wg, preferred_element_type=f32)
        d_rows = d_rows + jnp.einsum("erf,edf->erd", d_up, wu, preferred_element_type=f32)
        d_rows = d_rows.astype(bf16).reshape(local_experts, blocks, capacity, width)
        d_part = jnp.einsum("ebst,ebsd->btd", pick[at], d_rows, preferred_element_type=f32)
        d_part = d_part.astype(bf16).reshape(group_len, width)
        d_routed = lax.psum_scatter(d_part, "expert", scatter_dimension=0, tiled=True).astype(f32)
        result = jnp.einsum("erf,efd->erd", hidden_low, wd, preferred_element_type=f32)
        result = result.astype(bf16).reshape(local_experts, blocks, capacity, width)
        part = jnp.einsum("ebst,ebsd->btd", weighted[at], result, preferred_element_type=f32)
        part = part.astype(bf16).reshape(group_len, width)
        expert_mix = lax.psum_scatter(part, "expert", scatter_dimension=0, tiled=True).astype(f32)
        outputs.append((middle[at] + expert_mix).astype(bf16))

        acc_down += jnp.einsum("erf,erd->efd", hidden_low, d_result, preferred_element_type=f32)
        acc_gate += jnp.einsum("erd,erf->edf", picked, d_gate, preferred_element_type=f32)
        acc_up += jnp.einsum("erd,erf->edf", picked, d_up, preferred_element_type=f32)

        d_mid_norm, mid_gain_grad = norm_back(d_routed, middle[at], scale_mid[at], gain_mid)
        grad_mid = grad_mid + mid_gain_grad
        d_middle = cotangent[at, 0].astype(f32) + d_mid_norm
        d_middles.append(d_middle)
        d_branches.append(d_middle.astype(bf16))

    grad_gate = lax.psum_scatter(acc_gate.astype(bf16), "dp", scatter_dimension=1, tiled=True)
    grad_up = lax.psum_scatter(acc_up.astype(bf16), "dp", scatter_dimension=1, tiled=True)
    grad_down = lax.psum_scatter(acc_down.astype(bf16), "dp", scatter_dimension=2, tiled=True)

    d_branch = jnp.concatenate(d_branches, axis=0)
    d_middle = jnp.concatenate(d_middles, axis=0)
    grad_output = mm(mixed.reshape(total, H * HD), d_branch, TN).astype(bf16)
    grad_output = lax.psum_scatter(grad_output, BOTH, scatter_dimension=0, tiled=True)
    d_mixed = mm(d_branch, out_w, NT).astype(bf16).reshape(micro, rows, H * HD)
    cos_rows = jnp.concatenate([cosine, cosine], axis=-1).reshape(micro, rows, HD)
    sine_rows = jnp.concatenate([-sine_part, sine_part], axis=-1).reshape(micro, rows, HD)
    q_raw = queries.reshape(micro, rows, H * HD)
    d_query, dkv_all, grad_qn = run_backward(
        q_low, kv_all, bias, mixed, d_mixed, logs, q_raw, cos_rows, sine_rows, gain_q[None, :], step_heads, chunk
    )
    grad_qn = grad_qn[0]
    dkv = lax.psum_scatter(dkv_all, "expert", scatter_dimension=0, tiled=False)
    dkv = dkv.reshape(total, KVH, 2 * HD)
    d_key = rotate(dkv[:, :, :HD].astype(f32), cosine, -sine_part)
    d_key, grad_kn = norm_back(d_key, key_pre, scale_k, gain_k)
    d_proj = jnp.concatenate(
        [
            d_query.reshape(total, shards, q_part),
            d_key.astype(bf16).reshape(total, shards, k_part),
            dkv[:, :, HD:].reshape(total, shards, v_part),
        ],
        axis=-1,
    ).reshape(total, -1)
    grad_qkv = mm(d_proj, normed, TN).astype(bf16)
    grad_qkv = lax.psum_scatter(grad_qkv, BOTH, scatter_dimension=0, tiled=True).astype(f32)
    d_normed = mm(d_proj, qkv_w)
    d_in_norm, grad_in = norm_back(d_normed, hidden, scale_in, gain_in)
    input_grad = d_middle + d_in_norm

    gain_grads = jnp.concatenate([grad_in, grad_mid, grad_qn, grad_kn]).reshape(shards, gain_len)
    gain_grads = jnp.pad(gain_grads, ((0, 0), (0, 256 - gain_len % 256)))
    gain_all = lax.all_gather(gain_grads, BOTH, axis=0, tiled=False)
    grad_gains = jnp.sum(lax.dynamic_index_in_dim(gain_all, shard_at, axis=1, keepdims=False), axis=0)
    return (
        jnp.stack(outputs)[:, None],
        input_grad.reshape(micro, 1, rows, width),
        grad_qkv[:q_part].T,
        grad_qkv[q_part : q_part + k_part].T,
        grad_qkv[q_part + k_part :].T,
        grad_output.astype(f32),
        grad_gains[:gain_len],
        grad_gate.astype(f32),
        grad_up.astype(f32),
        grad_down.astype(f32),
    )


def body_fast(
    inputs,
    cotangent,
    membership,
    routes,
    gate_weights,
    pair_order,
    w_query,
    w_key,
    w_value,
    w_output,
    norm_gains,
    w_gate,
    w_up,
    w_down,
):
    micro = inputs.shape[0]
    rows = inputs.shape[2]
    width = inputs.shape[3]
    group_len = membership.shape[2]
    member = lax.axis_index("expert")
    blocks = lax.axis_size("expert")
    shards = blocks * lax.axis_size("dp")
    local_experts = w_gate.shape[0]
    experts = local_experts * blocks
    capacity = rows * TOPK // experts
    step_heads = max(1, 384 // rows)
    total = micro * rows
    q_part, k_part, v_part = w_query.shape[1], w_key.shape[1], w_value.shape[1]
    tie = lax.optimization_barrier

    slot_map, weight_map = jax.vmap(
        lambda r, g, o: slots_of(r, g, o, capacity, experts)
    )(routes[:, 0], gate_weights[:, 0], pair_order[:, 0, 0])
    weight_high = tie(weight_map.astype(bf16))
    weight_low = (weight_map - weight_high.astype(f32)).astype(bf16)

    def padded(values, lanes):
        return jnp.pad(values, ((0, 0), (0, 0), (0, lanes - experts)))

    routing = jnp.concatenate(
        [
            padded(slot_map.astype(bf16), 32),
            padded(weight_high, 32),
            padded(weight_low, ROUTE_LANES - 64),
        ],
        axis=-1,
    )

    gain_len = norm_gains.shape[0]
    gain_shard = jnp.zeros((2048,), bf16).at[:gain_len].set(norm_gains).reshape(16, 128)
    kv_w = jnp.concatenate([w_key.T, w_value.T], axis=0)
    q_w, kv_w, out_w, gain_full, cot_0 = gather_rows(
        [w_query.T, kv_w, w_output, gain_shard, cotangent[0, 0]], [(3, 0, 1, 2)], 1, (4,)
    )
    cot_0 = cot_0.reshape(blocks, rows, width)
    q_w, w_gate = tie((q_w, w_gate))
    gains = gain_full.reshape(shards, 2048)[:, :gain_len].reshape(-1).astype(f32)
    gain_in = gains[:width]
    gain_mid = gains[width : 2 * width]
    gain_q = gains[2 * width : 2 * width + HD]
    gain_k = gains[2 * width + HD :]
    gate_near = (swap(w_gate, 1), swap(w_gate, 2))

    key_index = jnp.arange(group_len, dtype=jnp.int32)
    start_row = member * rows
    segment = membership[:, 0]
    row_index = start_row + jnp.arange(rows, dtype=jnp.int32)
    seg_rows = lax.dynamic_slice_in_dim(segment, start_row, rows, axis=1)
    before = jnp.sum((segment[:, None, :] < seg_rows[:, :, None]).astype(jnp.int32), axis=2)
    position = jnp.where(seg_rows == 0, row_index[None], PROMPT + row_index[None] - before)
    allowed = (key_index[None, :, None] <= row_index[None, None, :]) & (
        (segment[:, :, None] == 0) | (segment[:, :, None] == seg_rows[:, None, :])
    )
    bias = jnp.tile(jnp.where(allowed, 0.0, MASKED).astype(f32), (1, 1, step_heads))
    frequency = ROPE_BASE ** (-(jnp.arange(HD // 2, dtype=f32) * 2.0 / HD))
    angles = position.astype(f32).reshape(total)[:, None] * frequency[None, :]
    cosine, sine = jnp.cos(angles), jnp.sin(angles)
    cosine = jnp.concatenate([cosine, cosine], axis=-1)
    sine = jnp.concatenate([-sine, sine], axis=-1)
    gain_q, gain_k = gain_q[None, :], gain_k[None, :]

    hidden = inputs[:, 0].astype(f32).reshape(total, width)
    scale_in = rms_scale(hidden)
    normed = (hidden * scale_in * gain_in).astype(bf16)
    q_low, q_raw, kv_own, k_raw, kv_w = run_project(
        normed, q_w, kv_w, cosine, sine, gain_q * (SCALE * LOG2E), gain_k
    )
    q_low, q_raw = (a.reshape(micro, rows, H * HD) for a in (q_low, q_raw))
    kv_own = kv_own.reshape(micro, rows, KVH * 2 * HD)
    kv_own, gate_near = tie((kv_own, gate_near))
    kv_all = lax.all_gather(kv_own, "expert", axis=0, tiled=False)
    kv_all, w_up, w_down, cot_1 = tie((kv_all, w_up, w_down, cotangent[1, 0]))
    cot_1 = lax.all_gather(cot_1, "expert", axis=0, tiled=False)
    up_near, down_near = ((swap(w, 1), swap(w, 2)) for w in (w_up, w_down))
    chunk = 256
    mixed, logs = run_forward(q_low, kv_all, bias, step_heads, chunk)
    mixed, up_near, down_near = tie((mixed, up_near, down_near))
    parts = [
        (own, near[0], near[1], swap(near[0][:1], 2), swap(near[1][1:], 1))
        for own, near in ((w_gate, gate_near), (w_up, up_near), (w_down, down_near))
    ]

    branch = mm(mixed.reshape(total, H * HD), out_w)
    middle = hidden + branch
    scale_mid = rms_scale(middle)
    routed = (middle * scale_mid * gain_mid).astype(bf16).reshape(micro, rows, width)
    routed = jnp.concatenate([routed, routing], axis=-1)
    routed, cot_1 = tie((routed, cot_1))
    middle = middle.reshape(micro, rows, width)
    scale_mid = scale_mid.reshape(micro, rows, 1)

    mix_parts, d_routeds, d_branches, d_middles = [], [], [], []
    kept = []
    for at, cot in enumerate((cot_0, cot_1)):
        tokens = lax.all_gather(routed[at], "expert", axis=0, tiled=False)
        tokens, parts = tie((tokens, parts))
        kept, mix, d_part = run_experts(tokens, cot, parts, capacity, at, micro, kept)
        kept, d_part, mix, d_routeds = tie((kept, d_part, mix, d_routeds))
        mix_parts.append(mix)
        d_routed = lax.psum_scatter(d_part, "expert", scatter_dimension=0, tiled=True)
        d_routeds.append(d_routed)
    picked, d_result, hidden_low, d_gate, d_up = (
        a.reshape(local_experts, -1, a.shape[-1]) for a in kept
    )

    def weight_grad(rows_in, rows_out):
        return jnp.einsum("era,erb->eab", rows_in, rows_out, preferred_element_type=f32).astype(bf16)

    scattering = [
        scatter_far(weight_grad(hidden_low, d_result), 2),
        scatter_far(weight_grad(picked, d_gate), 1),
        scatter_far(weight_grad(picked, d_up), 1),
    ]
    d_routeds[-1], scattering, mix_parts[0] = tie((d_routeds[-1], scattering, mix_parts[0]))
    expert_grads = [scatter_near(*pieces) for pieces in scattering]
    grad_mid = 0.0
    for at in range(micro):
        d_mid_norm, mid_gain_grad = norm_back(
            d_routeds[at].astype(f32), middle[at], scale_mid[at], gain_mid
        )
        grad_mid = grad_mid + mid_gain_grad
        d_middle = cotangent[at, 0].astype(f32) + d_mid_norm
        d_middles.append(d_middle)
        d_branches.append(d_middle.astype(bf16))

    d_branch = jnp.concatenate(d_branches, axis=0)
    d_middle = jnp.concatenate(d_middles, axis=0)
    d_mixed = mm(d_branch, out_w, NT).astype(bf16).reshape(micro, rows, H * HD)
    cos_rows, sine_rows = (a.reshape(micro, rows, HD) for a in (cosine, sine))
    d_query, dkv_all, grad_qn = run_backward(
        q_low, kv_all, bias, mixed, d_mixed, logs, q_raw, cos_rows, sine_rows, gain_q, step_heads, chunk
    )
    mixes = [lax.psum_scatter(mix_parts[0], "expert", scatter_dimension=0, tiled=True)]
    mixed_after, d_query, dkv_all, expert_grads, mixes = tie(
        (mixed, d_query, dkv_all, expert_grads, mixes)
    )
    grad_output, _ = reduce_rows(mixed_after.reshape(total, H * HD), None, d_branch, 2)
    dkv = lax.psum_scatter(dkv_all, "expert", scatter_dimension=0, tiled=False)
    dkv, grad_output, d_query = tie((dkv, grad_output, d_query))
    d_query = d_query.reshape(total, H * HD)
    dkv = dkv.reshape(total, KVH * 2 * HD)
    mix_part, dkv = tie((mix_parts[1], dkv))
    mixes.append(lax.psum_scatter(mix_part, "expert", scatter_dimension=0, tiled=True))
    outputs = [(middle[at] + mixes[at].astype(f32)).astype(bf16) for at in range(micro)]
    dkv, dkv_t, grad_kn = run_key_back(dkv, k_raw, cosine, sine, gain_k)
    d_normed = mm(d_query, q_w) + mm(dkv, kv_w)
    d_in_norm, grad_in = norm_back(d_normed, hidden, scale_in, gain_in)
    input_grad = d_middle + d_in_norm
    gain_grads = jnp.concatenate([grad_in, grad_mid, grad_qn[0], grad_kn[0]]).reshape(shards, gain_len)
    grad_qkv, grad_gains = reduce_rows(d_query, dkv_t, normed, 3, gain_grads)
    return (
        jnp.stack(outputs)[:, None],
        input_grad.reshape(micro, 1, rows, width),
        grad_qkv[:q_part].T,
        grad_qkv[q_part : q_part + k_part].T,
        grad_qkv[q_part + k_part :].T,
        grad_output,
        grad_gains[0, :gain_len],
        expert_grads[1],
        expert_grads[2],
        expert_grads[0],
    )


def solution(mesh):
    fast = mesh.shape["dp"] == 4 and mesh.shape["expert"] == 8
    return jax.shard_map(
        body_fast if fast else body_plain,
        mesh=mesh,
        in_specs=(
            P(None, "dp", "expert", None),
            P(None, "dp", "expert", None),
            P(None, "dp", None),
            P(None, "dp", "expert", None),
            P(None, "dp", "expert", None),
            P(None, "dp", "expert", None),
            P(None, ("dp", "expert")),
            P(None, ("dp", "expert")),
            P(None, ("dp", "expert")),
            P(("dp", "expert"), None),
            P(("dp", "expert")),
            P("expert", "dp", None),
            P("expert", "dp", None),
            P("expert", None, "dp"),
        ),
        out_specs=(
            P(None, "dp", "expert", None),
            P(None, "dp", "expert", None),
            P(None, ("dp", "expert")),
            P(None, ("dp", "expert")),
            P(None, ("dp", "expert")),
            P(("dp", "expert"), None),
            P(("dp", "expert")),
            P("expert", "dp", None),
            P("expert", "dp", None),
            P("expert", None, "dp"),
        ),
        check_vma=False,
    )
```

```python
import functools
import math

import jax
import jax.numpy as jnp
from jax import lax
from jax.experimental import pallas as pl
from jax.experimental.pallas import tpu as pltpu
from jax.sharding import PartitionSpec as P

H = 32
KVH = 4
HD = 128
FF = 768
TOPK = 8
PROMPT = 1024
PER_KV = H // KVH

EPSILON = 1e-06
ROPE_BASE = 1000000.0
MASKED = -1e30
LOG2E = math.log2(math.e)
SCALE = HD ** (-0.5)

bf16 = jnp.bfloat16
f32 = jnp.float32
NT = (((1,), (1,)), ((), ()))
TN = (((0,), (0,)), ((), ()))
NN = (((1,), (0,)), ((), ()))
BOTH = ("dp", "expert")
VMEM_LIMIT = 56 * 1024 * 1024


def mm(a, b, dims=NN):
    return lax.dot_general(a, b, dims, preferred_element_type=f32)


def rms_scale(values):
    return lax.rsqrt(jnp.mean(values * values, axis=-1, keepdims=True) + EPSILON)


def norm_back(upstream, values, inv_rms, norm_gain):
    lifted = upstream * norm_gain
    inner_dot = jnp.mean(lifted * values, axis=-1, keepdims=True)
    back_grad = inv_rms * lifted - values * (inv_rms * inv_rms * inv_rms) * inner_dot
    gain_grad = jnp.sum((upstream * values * inv_rms).reshape(-1, values.shape[-1]), axis=0)
    return (back_grad, gain_grad)


def rotate(values, cosine, sine_part):
    half_dim = values.shape[-1] // 2
    first_half = values[..., :half_dim]
    second_half = values[..., half_dim:]
    return jnp.concatenate(
        [
            first_half * cosine - second_half * sine_part,
            second_half * cosine + first_half * sine_part,
        ],
        axis=-1,
    )


def turn(values, cosine, sine):
    return values * cosine + pltpu.roll(values, HD // 2, 1) * sine


def project(x_ref, wq_ref, wkv_ref, cos_ref, sin_ref, gq_ref, gk_ref, q_ref, qraw_ref, kv_ref, kraw_ref, wkv_out):
    x = x_ref[...]
    cosine, sine = cos_ref[...], sin_ref[...]
    for at in range(0, PER_KV * HD, 2 * HD):
        raw = mm(x, wq_ref[at : at + 2 * HD], NT)
        qraw_ref[:, at : at + 2 * HD] = raw
        for lane in (0, HD):
            head = raw[:, lane : lane + HD]
            normed = head * rms_scale(head) * gq_ref[...]
            q_ref[:, at + lane : at + lane + HD] = turn(normed, cosine, sine).astype(bf16)
    piece = HD // PER_KV
    w_k = [wkv_ref[2 * piece * i : 2 * piece * i + piece] for i in range(PER_KV)]
    w_v = [wkv_ref[2 * piece * i + piece : 2 * piece * (i + 1)] for i in range(PER_KV)]
    w_kv = jnp.concatenate(w_k + w_v, axis=0)
    wkv_out[...] = w_kv
    raw = mm(x, w_kv, NT)
    key = raw[:, :HD]
    kraw_ref[...] = key
    normed = key * rms_scale(key) * gk_ref[...]
    kv_ref[:, :HD] = turn(normed, cosine, sine).astype(bf16)
    kv_ref[:, HD:] = raw[:, HD:].astype(bf16)


def run_project(x, wq, wkv, cosine, sine, gain_q, gain_k):
    tokens, width = x.shape
    wide = PER_KV * HD
    whole = lambda a: pl.BlockSpec(a.shape, lambda g: (0, 0))
    cols = lambda n: pl.BlockSpec((tokens, n), lambda g: (0, g))
    rows = lambda n: pl.BlockSpec((n, width), lambda g: (g, 0))
    return pl.pallas_call(
        project,
        grid=(KVH,),
        in_specs=[whole(x), rows(wide), rows(2 * HD), whole(cosine), whole(sine), whole(gain_q), whole(gain_k)],
        out_specs=[cols(wide), cols(wide), cols(2 * HD), cols(HD), rows(2 * HD)],
        out_shape=[
            jax.ShapeDtypeStruct((tokens, H * HD), bf16),
            jax.ShapeDtypeStruct((tokens, H * HD), f32),
            jax.ShapeDtypeStruct((tokens, KVH * 2 * HD), bf16),
            jax.ShapeDtypeStruct((tokens, KVH * HD), f32),
            jax.ShapeDtypeStruct((KVH * 2 * HD, width), bf16),
        ],
        compiler_params=pltpu.CompilerParams(vmem_limit_bytes=VMEM_LIMIT),
        cost_estimate=pl.CostEstimate(
            flops=2 * tokens * width * (H + 2 * KVH) * HD, bytes_accessed=40_000_000, transcendentals=0
        ),
    )(x, wq, wkv, cosine, sine, gain_q, gain_k)


def norm_turn_back(grad, raw, cosine, sine, gain):
    grad = turn(grad, cosine, -sine)
    scale = rms_scale(raw)
    lifted = grad * gain
    inner = jnp.mean(lifted * raw, axis=-1, keepdims=True)
    back = scale * lifted - raw * (scale * scale * scale) * inner
    return back, jnp.sum(grad * raw * scale, axis=0, keepdims=True)


def key_back(dkv_ref, kraw_ref, cos_ref, sin_ref, gk_ref, out_ref, out_t_ref, gain_ref):
    gain_sum = 0.0
    for g in range(KVH):
        key = slice(2 * g * HD, (2 * g + 1) * HD)
        value = slice((2 * g + 1) * HD, (2 * g + 2) * HD)
        grad = dkv_ref[:, key].astype(f32)
        back, part = norm_turn_back(
            grad, kraw_ref[:, g * HD : (g + 1) * HD], cos_ref[...], sin_ref[...], gk_ref[...]
        )
        gain_sum += part
        low = back.astype(bf16)
        out_ref[:, key] = low
        out_t_ref[key] = low.T
        out_ref[:, value] = dkv_ref[:, value]
        out_t_ref[value] = dkv_ref[:, value].T
    gain_ref[...] = gain_sum


def run_key_back(dkv, key_raw, cosine, sine, gain):
    tokens, wide = dkv.shape
    return pl.pallas_call(
        key_back,
        out_shape=[
            jax.ShapeDtypeStruct((tokens, wide), bf16),
            jax.ShapeDtypeStruct((wide, tokens), bf16),
            jax.ShapeDtypeStruct((1, HD), f32),
        ],
        compiler_params=pltpu.CompilerParams(vmem_limit_bytes=VMEM_LIMIT),
    )(dkv, key_raw, cosine, sine, gain)


def attend_forward(step_heads, chunk, q_ref, kv_ref, bias_ref, o_ref, log_ref):
    group_len = bias_ref.shape[1]
    keys = kv_ref[:, 0, :, :HD].reshape(group_len, HD)
    values_t = kv_ref[:, 0, :, HD:].reshape(group_len, HD).T
    rows = q_ref.shape[1]
    for step in range(PER_KV // step_heads):
        heads = range(step * step_heads, (step + 1) * step_heads)
        query = jnp.concatenate([q_ref[0, :, h * HD : (h + 1) * HD] for h in heads], axis=0)
        mixed, row_sum = 0.0, 0.0
        for at in range(0, group_len, chunk):
            scores = mm(keys[at : at + chunk], query, NT)
            prob = jnp.exp2(scores + bias_ref[0, at : at + chunk, :])
            row_sum += jnp.sum(prob, axis=0, keepdims=True)
            mixed += mm(values_t[:, at : at + chunk], prob.astype(bf16))
        out = (mixed / row_sum).T.astype(bf16)
        for i, h in enumerate(heads):
            o_ref[0, :, h * HD : (h + 1) * HD] = out[i * rows : (i + 1) * rows]
        log_ref[0, 0, step : step + 1, :] = jnp.log2(row_sum)


def attend_backward(
    step_heads, chunk, q_ref, kv_ref, bias_ref, o_ref, do_ref, log_ref, raw_ref, cos_ref, sin_ref, gain_ref,
    dq_ref, dkv_ref, gain_out, dk_acc, dv_acc
):
    group_len = bias_ref.shape[1]
    keys = kv_ref[:, 0, :, :HD].reshape(group_len, HD)
    values = kv_ref[:, 0, :, HD:].reshape(group_len, HD)
    keys_t = keys.T
    rows = q_ref.shape[1]
    cosine, sine, gain = cos_ref[0], sin_ref[0], gain_ref[...]

    @pl.when(pl.program_id(0) == 0)
    def _():
        gain_out[...] = jnp.zeros_like(gain_out)

    gain_sum = 0.0
    dk_acc[...] = jnp.zeros_like(dk_acc)
    dv_acc[...] = jnp.zeros_like(dv_acc)
    for step in range(PER_KV // step_heads):
        heads = range(step * step_heads, (step + 1) * step_heads)
        query = jnp.concatenate([q_ref[0, :, h * HD : (h + 1) * HD] for h in heads], axis=0)
        grad = jnp.concatenate([do_ref[0, :, h * HD : (h + 1) * HD] for h in heads], axis=0)
        mixed = jnp.concatenate([o_ref[0, :, h * HD : (h + 1) * HD] for h in heads], axis=0)
        row_dot = jnp.sum((grad.astype(f32) * mixed.astype(f32)).T, axis=0, keepdims=True)
        log_sum = log_ref[0, 0, step : step + 1, :]
        dq_t = 0.0
        for at in range(0, group_len, chunk):
            part = slice(at, at + chunk)
            scores = mm(keys[part], query, NT)
            prob = jnp.exp2(scores + (bias_ref[0, part, :] - log_sum))
            d_prob = mm(values[part], grad, NT)
            d_score = (prob * (d_prob - row_dot)).astype(bf16)
            dv_acc[part] += mm(prob.astype(bf16), grad)
            dk_acc[part] += mm(d_score, query)
            dq_t += mm(keys_t[:, part], d_score)
        out = (dq_t * SCALE).T.astype(bf16).astype(f32)
        for i, h in enumerate(heads):
            head = slice(h * HD, (h + 1) * HD)
            back, part = norm_turn_back(
                out[i * rows : (i + 1) * rows], raw_ref[0, :, head], cosine, sine, gain
            )
            dq_ref[0, :, head] = back.astype(bf16)
            gain_sum += part
    gain_out[...] += gain_sum
    blocks = dkv_ref.shape[0]
    dkv_ref[:, 0, :, :HD] = (dk_acc[...] * (1.0 / LOG2E)).astype(bf16).reshape(blocks, rows, HD)
    dkv_ref[:, 0, :, HD:] = dv_acc[...].astype(bf16).reshape(blocks, rows, HD)


def attention_specs(rows, group_len, blocks, step_heads, at):
    wide = PER_KV * HD
    q_spec = pl.BlockSpec((1, rows, wide), lambda g: (at, 0, g))
    kv_spec = pl.BlockSpec((blocks, 1, rows, 2 * HD), lambda g: (0, 0, 0, g))
    bias_spec = pl.BlockSpec((1, group_len, step_heads * rows), lambda g: (at, 0, 0))
    log_spec = pl.BlockSpec((1, 1, PER_KV // step_heads, step_heads * rows), lambda g: (at, g, 0, 0))
    return q_spec, kv_spec, bias_spec, log_spec


def run_forward(query, kv_all, bias, step_heads, chunk, at, earlier):
    micro, rows, _ = query.shape
    blocks = kv_all.shape[0]
    group_len = bias.shape[1]
    q_spec, kv_spec, bias_spec, log_spec = attention_specs(rows, group_len, blocks, step_heads, at)
    flops = 4 * rows * H * HD * group_len

    def kernel(*refs):
        attend_forward(step_heads, chunk, *refs[:3], *refs[3 + len(earlier) :])

    return pl.pallas_call(
        kernel,
        grid=(KVH,),
        in_specs=[q_spec, kv_spec, bias_spec] + [pl.BlockSpec(memory_space=pl.ANY)] * len(earlier),
        out_specs=[q_spec, log_spec],
        out_shape=[
            jax.ShapeDtypeStruct(query.shape, bf16),
            jax.ShapeDtypeStruct((micro, KVH, PER_KV // step_heads, step_heads * rows), f32),
        ],
        input_output_aliases={3 + i: i for i in range(len(earlier))},
        compiler_params=pltpu.CompilerParams(vmem_limit_bytes=VMEM_LIMIT),
        cost_estimate=pl.CostEstimate(
            flops=flops, bytes_accessed=20_000_000, transcendentals=flops // (4 * HD)
        ),
    )(query, kv_all, bias, *earlier)


def run_backward(query, kv_all, bias, mixed, grad, logs, raw, cosine, sine, gain, step_heads, chunk, at, earlier):
    micro, rows, _ = query.shape
    blocks = kv_all.shape[0]
    group_len = bias.shape[1]
    q_spec, kv_spec, bias_spec, log_spec = attention_specs(rows, group_len, blocks, step_heads, at)
    flops = 10 * rows * H * HD * group_len
    gain_spec = pl.BlockSpec((1, HD), lambda g: (0, 0))

    def kernel(*refs):
        attend_backward(step_heads, chunk, *refs[:10], *refs[10 + len(earlier) :])

    return pl.pallas_call(
        kernel,
        grid=(KVH,),
        in_specs=[q_spec, kv_spec, bias_spec, q_spec, q_spec, log_spec, q_spec]
        + [pl.BlockSpec((1, rows, HD), lambda g: (at, 0, 0))] * 2
        + [gain_spec]
        + [pl.BlockSpec(memory_space=pl.ANY)] * len(earlier),
        out_specs=[q_spec, kv_spec, gain_spec],
        out_shape=[
            jax.ShapeDtypeStruct(query.shape, bf16),
            jax.ShapeDtypeStruct(kv_all.shape, bf16),
            jax.ShapeDtypeStruct((1, HD), f32),
        ],
        input_output_aliases={10 + i: i for i in range(len(earlier))},
        scratch_shapes=[pltpu.VMEM((group_len, HD), f32), pltpu.VMEM((group_len, HD), f32)],
        compiler_params=pltpu.CompilerParams(vmem_limit_bytes=VMEM_LIMIT),
        cost_estimate=pl.CostEstimate(
            flops=flops, bytes_accessed=30_000_000, transcendentals=flops // (10 * HD)
        ),
    )(query, kv_all, bias, mixed, grad, logs, raw, cosine, sine, gain, *earlier)


def middle_back(r0_ref, r1_ref, mid_ref, cot_ref, gain_ref, w_ref, mix_ref, dmid_ref, low_ref, gain_out):
    @pl.when(pl.program_id(0) == 0)
    def _():
        gain_sum = 0.0
        rows = r0_ref.shape[0]
        for b, ref in enumerate((r0_ref, r1_ref)):
            grad = ref[...].astype(f32)
            middle = mid_ref[b]
            scale = rms_scale(middle)
            lifted = grad * gain_ref[...]
            inner = jnp.mean(lifted * middle, axis=-1, keepdims=True)
            total = cot_ref[b].astype(f32) + scale * lifted - middle * (scale * scale * scale) * inner
            gain_sum += jnp.sum(grad * middle * scale, axis=0, keepdims=True)
            dmid_ref[b * rows : (b + 1) * rows] = total
            low_ref[b * rows : (b + 1) * rows] = total.astype(bf16)
        gain_out[...] = gain_sum

    mix_ref[...] = mm(low_ref[...], w_ref[...], NT).astype(bf16)


def run_middle_back(routed, middle, cot, gain, out_w):
    micro, rows, width = middle.shape
    total = micro * rows
    piece = 512
    whole = lambda *shape: pl.BlockSpec(shape, lambda i: (0,) * len(shape))
    return pl.pallas_call(
        middle_back,
        grid=(out_w.shape[0] // piece,),
        in_specs=[whole(rows, width)] * 2
        + [whole(micro, rows, width)] * 2
        + [whole(1, width), pl.BlockSpec((piece, width), lambda i: (i, 0))],
        out_specs=[
            pl.BlockSpec((total, piece), lambda i: (0, i)),
            whole(total, width),
            whole(total, width),
            whole(1, width),
        ],
        out_shape=[
            jax.ShapeDtypeStruct((total, out_w.shape[0]), bf16),
            jax.ShapeDtypeStruct((total, width), f32),
            jax.ShapeDtypeStruct((total, width), bf16),
            jax.ShapeDtypeStruct((1, width), f32),
        ],
        compiler_params=pltpu.CompilerParams(vmem_limit_bytes=VMEM_LIMIT),
        cost_estimate=pl.CostEstimate(
            flops=2 * total * width * out_w.shape[0], bytes_accessed=35_000_000, transcendentals=0
        ),
    )(*routed, middle, cot, gain, out_w)


MESH = pl.DeviceIdType.MESH


def gather_kernel(phases, count, late, *refs):
    ins, outs, sems = refs[:count], refs[count : 2 * count], refs[2 * count :]
    dp = lax.axis_index("dp"); member = lax.axis_index("expert")
    blocks = lax.axis_size("expert")
    core = member % 2; z = member // 2
    depth = blocks // 2
    sibling = (dp, member + 1 - 2 * core)
    by_x = (dp + 1 - 2 * (dp % 2), member)
    by_y = ((dp + 2) % 4, member)
    x_at, y_at, far_at = by_x[0], by_y[0], 3 - dp
    above, below = (dp, member + 2), (dp, member - 2)
    barrier = pltpu.get_barrier_semaphore()
    peers = [(sibling, None), (by_x, None), (by_y, None), (above, z < depth - 1), (below, z > 0)]
    for peer, ok in peers:
        if ok is None:
            pl.semaphore_signal(barrier, inc=1, device_id=peer, device_id_type=MESH)
        else:
            @pl.when(ok)
            def _(peer=peer):
                pl.semaphore_signal(barrier, inc=1, device_id=peer, device_id_type=MESH)
    @pl.when((z == 0) | (z == depth - 1))
    def _(): pl.semaphore_wait(barrier, 4)
    @pl.when((z > 0) & (z < depth - 1))
    def _(): pl.semaphore_wait(barrier, 5)

    def guarded(ok, run):
        if ok is None: run()
        else: pl.when(ok)(run)

    class Item:
        pass

    def make(i):
        src, out = ins[i], outs[i]
        flat = i in late
        rows = src.shape[0]
        half = rows // 2
        (own_sem, sz, rz, sxy, rxy, sc, rc) = sems[i * 7 : (i + 1) * 7]
        def at(d, s, lo=0, n=rows):
            first = s * 2 + core if flat else d * blocks + s * 2 + core
            return out.at[pl.ds(pl.multiple_of(first * rows + lo, 16 if half % 16 == 0 else 8), n)]
        def copy(a, b, ss, rs, to):
            return pltpu.make_async_remote_copy(src_ref=a, dst_ref=b, send_sem=ss, recv_sem=rs, device_id=to, device_id_type=MESH)
        def block(d, s):
            return at(d, s)
        it = Item()
        def local():
            return pltpu.make_async_copy(src, at(dp, z), own_sem)
        def up(s, ref): return copy(ref, at(dp, s), sz.at[0, s], rz.at[s], above)
        def down(s, ref): return copy(ref, at(dp, s), sz.at[1, s], rz.at[s], below)
        def to_x(s, ref): return copy(ref, at(dp, s), sxy.at[0, s], rxy.at[0, s], by_x)
        def to_y(s, ref): return copy(ref, at(dp, s), sxy.at[1, s], rxy.at[1, s], by_y)
        def half_y(s):
            return copy(at(x_at, s, 0, half), at(x_at, s, 0, half), sxy.at[2, s], rxy.at[2, s], by_y)
        def half_x(s):
            return copy(at(y_at, s, half, half), at(y_at, s, half, half), sxy.at[3, s], rxy.at[3, s], by_x)
        def to_core(r, d, s, ref): return copy(ref, at(d, s), sc.at[r, s], rc.at[r, s], sibling)
        def spread(s, ref):
            if not flat:
                to_x(s, ref).start(); to_y(s, ref).start()
            to_core(0, dp, s, ref).start()
        def start_up():
            up(z, src).start()
        def start_down():
            down(z, src).start()
        def start():
            local().start()
            if not flat:
                guarded(z < depth - 1, start_up)
                guarded(z > 0, start_down)
            spread(z, src)
        def z_event(s, ok, rising):
            def run():
                up(s, at(dp, s)).wait_recv()
                if rising: guarded(z < depth - 1, lambda: up(s, at(dp, s)).start())
                else: guarded(z > 0, lambda: down(s, at(dp, s)).start())
                spread(s, at(dp, s))
            pl.when(ok)(run)
        def near_event(s, ok):
            def run():
                to_x(s, at(dp, s)).wait_recv()
                half_y(s).start()
                to_core(1, x_at, s, at(x_at, s)).start()
                to_y(s, at(dp, s)).wait_recv()
                half_x(s).start()
                to_core(2, y_at, s, at(y_at, s)).start()
            guarded(ok, run)
        def far_event(s, ok):
            def run():
                half_y(s).wait_recv(); half_x(s).wait_recv()
                to_core(3, far_at, s, at(far_at, s)).start()
            guarded(ok, run)
        owners = (dp,) if flat else (dp, x_at, y_at, far_at)
        def core_wait(s):
            for r, d in enumerate(owners):
                to_core(r, d, s, at(d, s)).wait_recv()
        def finish():
            local().wait()
            for s in range(depth):
                if not flat:
                    for c in (to_x(s, at(dp, s)), to_y(s, at(dp, s)), half_y(s), half_x(s)): c.wait_send()
                for r, d in enumerate(owners): to_core(r, d, s, at(d, s)).wait_send()
                guarded((z >= s) & (z < depth - 1), lambda: up(s, at(dp, s)).wait_send())
                guarded((z <= s) & (z > 0), lambda: down(s, at(dp, s)).wait_send())
        it.start_up, it.start_down = start_up, start_down
        it.start, it.z_event, it.near_event, it.far_event, it.core_wait, it.finish = start, z_event, near_event, far_event, core_wait, finish
        return it
    items = [make(i) for i in range(count)]
    def around(d):
        if d == 0: return [(z, None, True)]
        return [(z - d, z >= d, True), (z + d, z + d < depth, False)]
    for n, phase in enumerate(phases):
        its = [items[i] for i in phase]
        for it in its: it.start()
        lates = [items[i] for i in late]
        for it in lates: it.start()
        def late_sends(d):
            for it in lates:
                if d < depth - 1:
                    pl.when(z == d)(it.start_up)
                    pl.when(z == depth - 1 - d)(it.start_down)
        late_sends(0)
        for d in range(1, depth + 2):
            if d < depth:
                for s, ok, rising in around(d):
                    for it in its: it.z_event(s, ok, rising)
                late_sends(d)
            if d - 1 < depth:
                for s, ok, _ in around(d - 1):
                    for it in its: it.near_event(s, ok)
            if d > 2:
                for s, ok, rising in around(d - 2):
                    for it in lates: it.z_event(s, ok, rising)
            if d - 2 >= 0:
                for s, ok, _ in around(d - 2):
                    for it in its: it.far_event(s, ok)
    for it in items:
        for s in range(depth): it.core_wait(s)
    for it in items: it.finish()

def gather_rows(arrays, phases, cid, late=()):
    shards = lax.axis_size("dp") * lax.axis_size("expert")
    depth = lax.axis_size("expert") // 2
    D = pltpu.SemaphoreType.DMA
    sems = []
    for _ in arrays:
        sems += [D, D((2, depth)), D((depth,)), D((4, depth)), D((4, depth)), D((4, depth)), D((4, depth))]
    return pl.pallas_call(
        functools.partial(gather_kernel, phases, len(arrays), late),
        out_shape=[
            jax.ShapeDtypeStruct(((2 * depth if i in late else shards) * a.shape[0],) + a.shape[1:], a.dtype)
            for i, a in enumerate(arrays)
        ],
        in_specs=[pl.BlockSpec(memory_space=pl.ANY)] * len(arrays),
        out_specs=[pl.BlockSpec(memory_space=pl.ANY)] * len(arrays),
        scratch_shapes=sems,
        compiler_params=pltpu.CompilerParams(collective_id=cid, has_side_effects=True),
        cost_estimate=pl.CostEstimate(flops=0, bytes_accessed=400_000_000, transcendentals=0),
    )(*arrays)


def reduce_kernel(rows, cuts, a_ref, extra_ref, b_ref, g_ref, o_ref, go_ref, sib, got, own, far, near, plane, got_z,
                  s0, r0, s1, r1, s2, r2, s3, r3, g_acc, g_got, g_z, gs, gr, gsz, grz):
    dp = lax.axis_index("dp"); member = lax.axis_index("expert")
    core = member % 2; z = member // 2
    sibling = (dp, member + 1 - 2 * core)
    by_x = (dp + 1 - 2 * (dp % 2), member)
    by_y = ((dp + 2) % 4, member)
    x_at, y_at = by_x[0], by_y[0]
    far_at = 3 - dp
    half = rows // 2
    depth = lax.axis_size("expert") // 2
    barrier = pltpu.get_barrier_semaphore()
    peers = [sibling, by_x, by_y] + [(dp, ((z + d) % depth) * 2 + core) for d in range(1, depth)]
    for peer in peers:
        pl.semaphore_signal(barrier, inc=1, device_id=peer, device_id_type=MESH)
    pl.semaphore_wait(barrier, len(peers))

    def pick(table):
        at = table[depth-1]
        for i in range(depth - 1):
            at = jnp.where(z == i, table[i], at)
        return at
    orders = [[3, 3, 0, 0], [2, 0, 3, 1], [1, 2, 1, 2], [0, 1, 2, 3]]
    targets = [pick(t) for t in orders]
    cols = b_ref.shape[1] // cuts

    def copy(src, dst, ssem, rsem, to):
        return pltpu.make_async_remote_copy(src_ref=src, dst_ref=dst, send_sem=ssem, recv_sem=rsem, device_id=to, device_id_type=MESH)

    blocks = 2 * depth
    piece = (rows - HD) // 2

    def product(half_of, k, put):
        spot = targets[k] * 2 + half_of

        def step(i, _):
            shard = (i // cuts) * blocks + spot
            at = (i // cuts) * rows
            col = pl.ds(pl.multiple_of((i % cuts) * cols, cols), cols)
            part = mm(a_ref[:, pl.ds(pl.multiple_of(shard * HD, HD), HD)], b_ref[:, col], TN)
            put(pl.ds(pl.multiple_of(at, 16), HD), col, part)
            if piece:
                base = (shard // PER_KV) * (2 * HD) + (shard % PER_KV) * piece
                small = jnp.concatenate(
                    [
                        extra_ref[pl.ds(pl.multiple_of(base, 16), piece), :],
                        extra_ref[pl.ds(pl.multiple_of(base + HD, 16), piece), :],
                    ],
                    axis=0,
                )
                put(pl.ds(pl.multiple_of(at + HD, 16), 2 * piece), col, mm(small, b_ref[:, col]))
            return 0

        lax.fori_loop(0, 4 * cuts, step, 0)

    def gain_hop(i, src, to):
        return copy(src, g_got.at[i, pl.ds(0, src.shape[0])], gs.at[i], gr.at[i], to)
    hops = {}
    def gain_step(i):
        rows4 = lambda at: pl.ds(pl.multiple_of(at * 8, 8), 8)
        if i == 0:
            hops[0] = gain_hop(0, g_ref.at[pl.ds(pl.multiple_of((1 - core) * 32, 32), 32)], sibling)
        elif i == 1:
            hops[0].wait_recv()
            g_acc[...] = g_ref[pl.ds(pl.multiple_of(core * 32, 32), 32)] + g_got[0]
            hops[1] = gain_hop(1, g_acc.at[pl.ds(pl.multiple_of((1 - dp // 2) * 16, 16), 16)], by_y)
        elif i == 2:
            hops[1].wait_recv()
            mine = pl.ds(pl.multiple_of((dp // 2) * 16, 16), 16)
            g_acc[mine] += g_got[1, :16]
            hops[2] = gain_hop(2, g_acc.at[rows4(x_at)], by_x)
        elif i == 3:
            hops[2].wait_recv()
            g_acc[rows4(dp)] += g_got[2, :8]
            for d in range(1, depth):
                to = (z + d) % depth
                hops[2 + d] = copy(g_acc.at[pl.ds(dp * 8 + to, 1)], g_z.at[z], gsz.at[d - 1], grz.at[z], (dp, to * 2 + core))
        if i < 3:
            hops[i].start()
        else:
            for d in range(1, depth):
                hops[2 + d].start()
    def gain_end():
        total = g_acc[pl.ds(dp * 8 + z, 1)]
        for d in range(1, depth):
            src = (z + d) % depth
            copy(g_acc.at[pl.ds(dp * 8, 1)], g_z.at[src], gsz.at[0], grz.at[src], sibling).wait_recv()
            total += g_z[src]
        go_ref[...] = total
        for i in hops:
            hops[i].wait_send()
    sib_copies, far_copies, near_copies, z_copies = {}, {}, {}, {}
    def sib_step(k):
        slot = k % 2
        if k >= 2:
            sib_copies[k - 2].wait_send()
        def put(r, c, part):
            sib[slot, r, c] = part.astype(bf16)
        product(1 - core, k, put)
        sib_copies[k] = copy(sib.at[slot], got.at[k], s0.at[slot], r0.at[k], sibling)
        sib_copies[k].start()
    def blk(at):
        return pl.ds(pl.multiple_of(at * rows, 16), rows)
    def own_step(k):
        sib_copies[k].wait_recv()
        def put(r, c, part):
            own[k, r, c] = (part + got[k, r, c].astype(f32)).astype(bf16)
        product(core, k, put)
        base = pl.multiple_of(far_at * rows, 16)
        far_copies[k] = (
            copy(own.at[k, pl.ds(base, half)], far.at[k, 0], s1.at[k, 0], r1.at[k, 0], by_x),
            copy(own.at[k, pl.ds(pl.multiple_of(base + half, 16), half)], far.at[k, 1], s1.at[k, 1], r1.at[k, 1], by_y),
        )
        for c in far_copies[k]: c.start()
    def near_step(k):
        a, b = far_copies[k]
        a.wait_recv()
        rng = pl.ds(pl.multiple_of(y_at * rows, 16), half)
        own[k, rng] = (own[k, rng].astype(f32) + far[k, 0].astype(f32)).astype(bf16)
        to_y = copy(own.at[k, blk(y_at)], near.at[k, 1], s2.at[k, 1], r2.at[k, 1], by_y)
        to_y.start()
        b.wait_recv()
        rng = pl.ds(pl.multiple_of(x_at * rows + half, 16), half)
        own[k, rng] = (own[k, rng].astype(f32) + far[k, 1].astype(f32)).astype(bf16)
        to_x = copy(own.at[k, blk(x_at)], near.at[k, 0], s2.at[k, 0], r2.at[k, 0], by_x)
        to_x.start()
        near_copies[k] = (to_x, to_y)
    def plane_step(k):
        for c in near_copies[k]: c.wait_recv()
        total = own[k, blk(dp)].astype(f32) + near[k, 0].astype(f32) + near[k, 1].astype(f32)
        if k < depth - 1:
            plane[k] = total.astype(bf16)
            to = (dp, targets[k] * 2 + core)
            z_copies[k] = copy(plane.at[k], got_z.at[z], s3.at[k], r3.at[z], to)
            z_copies[k].start()
        else:
            o_ref[...] = total
    gain_step(0)
    sib_step(0); sib_step(1)
    own_step(0)
    gain_step(1)
    sib_step(2)
    own_step(1)
    gain_step(2)
    near_step(0)
    sib_step(3)
    own_step(2)
    gain_step(3)
    near_step(1)
    plane_step(0)
    own_step(3)
    near_step(2)
    plane_step(1)
    near_step(3)
    plane_step(2)
    plane_step(3)
    for d in range(1, depth):
        src = (z + d) % depth
        copy(plane.at[0], got_z.at[src], s3.at[0], r3.at[src], sibling).wait_recv()
        o_ref[...] += got_z[src].astype(f32)
    gain_end()
    for k in range(depth):
        if k >= 2: sib_copies[k].wait_send()
        for c in far_copies[k]: c.wait_send()
        for c in near_copies[k]: c.wait_send()
        if k < depth - 1: z_copies[k].wait_send()

def reduce_rows(a, extra, b, cid, gains=None):
    tokens, width = b.shape
    depth = 4
    rows = HD + (0 if extra is None else extra.shape[0] // 32)
    if extra is None:
        extra = jnp.zeros((16, 128), bf16)
    D = pltpu.SemaphoreType.DMA
    lanes = 256
    padded = jnp.zeros((32, lanes), f32)
    if gains is not None:
        padded = jnp.pad(gains, ((0, 0), (0, lanes - gains.shape[1])))
    padded = padded.reshape(4, depth, 2, lanes).transpose(2, 0, 1, 3)
    padded = jnp.pad(padded, ((0, 0), (0, 0), (0, 8 - depth), (0, 0))).reshape(64, lanes)
    return pl.pallas_call(
        functools.partial(reduce_kernel, rows, 4),
        out_shape=[jax.ShapeDtypeStruct((rows, width), f32), jax.ShapeDtypeStruct((1, lanes), f32)],
        in_specs=[pl.BlockSpec(memory_space=pltpu.VMEM)] * 4,
        out_specs=[pl.BlockSpec(memory_space=pltpu.VMEM)] * 2,
        scratch_shapes=[
            pltpu.VMEM((2, 4 * rows, width), bf16),
            pltpu.VMEM((depth, 4 * rows, width), bf16),
            pltpu.VMEM((depth, 4 * rows, width), bf16),
            pltpu.VMEM((depth, 2, rows // 2, width), bf16),
            pltpu.VMEM((depth, 2, rows, width), bf16),
            pltpu.VMEM((depth - 1, rows, width), bf16),
            pltpu.VMEM((depth, rows, width), bf16),
            D((2,)), D((depth,)), D((depth, 2)), D((depth, 2)), D((depth, 2)), D((depth, 2)), D((depth - 1,)), D((depth,)),
            pltpu.VMEM((32, lanes), f32), pltpu.VMEM((3, 32, lanes), f32), pltpu.VMEM((depth, 1, lanes), f32),
            D((3,)), D((3,)), D((depth - 1,)), D((depth,)),
        ],
        compiler_params=pltpu.CompilerParams(vmem_limit_bytes=60*1024*1024, collective_id=cid, has_side_effects=True),
        cost_estimate=pl.CostEstimate(flops=2*tokens*32*rows*width, bytes_accessed=10_000_000, transcendentals=0),
    )(a, extra, b, padded)


ROUTE_LANES = 128


def picks_of(routing, first, local_experts, capacity):
    rows = routing.shape[0]
    lanes = lax.broadcasted_iota(jnp.int32, (rows, ROUTE_LANES), 1)
    places = lax.broadcasted_iota(jnp.int32, (rows, local_experts * capacity), 1)
    hit, weighted = None, 0.0
    for e in range(local_experts):

        def column(base):
            return jnp.sum(jnp.where(lanes == base + first + e, routing, 0.0), axis=1, keepdims=True)

        slot = column(0).astype(jnp.int32)
        here = places == jnp.where(slot >= 0, slot + e * capacity, -1)
        hit = here if hit is None else hit | here
        weighted = weighted + jnp.where(here, column(32) + column(64), 0.0)
    return jnp.where(hit, 1.0, 0.0).astype(bf16), weighted.astype(bf16)


def pick_kernel(capacity, local_experts, n_alias, tok_ref, cot_ref, *refs):
    x_ref, dy_ref = refs[n_alias:]
    width = cot_ref.shape[3]
    first = lax.axis_index("expert") * local_experts
    routing = tok_ref[0, :, width:]
    hit, _ = picks_of(routing.astype(f32), first, local_experts, capacity)
    x = mm(hit, tok_ref[0, :, :width], TN).astype(bf16)
    rows = mm(hit, routing, TN)
    lanes = lax.broadcasted_iota(jnp.int32, rows.shape, 1)
    owner = lax.broadcasted_iota(jnp.int32, rows.shape, 0) // capacity
    at = lanes - first - owner
    weight = jnp.sum(jnp.where((at == 32) | (at == 64), rows, 0.0), axis=1, keepdims=True)
    dy = (mm(hit, cot_ref[0, 0], TN) * weight).astype(bf16)
    for e in range(local_experts):
        x_ref[e, 0, 0] = x[e * capacity : (e + 1) * capacity]
        dy_ref[e, 0, 0] = dy[e * capacity : (e + 1) * capacity]


def expert_kernel(n_alias, *refs):
    x_ref, dy_ref = refs[:2]
    parts = (refs[2:7], refs[7:12], refs[12:17])
    z_ref, dg_ref, du_ref, y_ref, dx_ref, wg, wu, wd, sems = refs[17 + n_alias :]
    local_experts, width, _ = wg.shape
    at = lax.axis_index("dp")
    size = width // 4
    places = (at, at + 1 - 2 * (at % 2), (at + 2) % 4, 3 - at, 3 - at)

    def copies(e):
        out = []
        for m, full in enumerate((wg, wu, wd)):
            for p in range(4):
                part = parts[m][p] if p < 3 else parts[m][3 + e]
                src = part.at[e] if p < 3 else part.at[0]
                where = pl.ds(pl.multiple_of(places[p] * size, size), size)
                dst = full.at[e, where, :] if m < 2 else full.at[e, :, where]
                out.append(pltpu.make_async_copy(src, dst, sems.at[e, m, p]))
        return out

    expert, chunk = pl.program_id(0), pl.program_id(1)

    @pl.when((expert == 0) & (chunk == 0))
    def _():
        for e in range(local_experts):
            for c in copies(e):
                c.start()

    for e in range(local_experts):

        @pl.when((expert == e) & (chunk == 0))
        def _(e=e):
            for c in copies(e):
                c.wait()

    x, dy = x_ref[0, 0], dy_ref[0, 0]
    gate = mm(x, wg[expert])
    up = mm(x, wu[expert])
    d_hidden = mm(dy, wd[expert], NT)
    sig = 1.0 / (1.0 + jnp.exp(-gate))
    silu = gate * sig
    z = (silu * up).astype(bf16)
    d_gate = (d_hidden * up * sig * (1.0 + gate * (1.0 - sig))).astype(bf16)
    d_up = (d_hidden * silu).astype(bf16)
    z_ref[0, 0] = z
    dg_ref[0, 0] = d_gate
    du_ref[0, 0] = d_up
    dx_ref[0] = (mm(d_gate, wg[expert], NT) + mm(d_up, wu[expert], NT)).astype(bf16)
    y_ref[0] = mm(z, wd[expert]).astype(bf16)


def sum_kernel(capacity, routing_ref, y_ref, dx_ref, mix_ref, da_ref):
    local_experts, _, _, width = y_ref.shape
    first = lax.axis_index("expert") * local_experts
    hit, weighted = picks_of(routing_ref[0].astype(f32), first, local_experts, capacity)
    da_ref[...] = mm(hit, dx_ref[...].reshape(local_experts * capacity, width)).astype(bf16)
    mix_ref[...] = mm(weighted, y_ref[...].reshape(local_experts * capacity, width)).astype(bf16)


def run_experts(tokens, cot, parts, capacity, batch_at, micro, earlier):
    blocks, _, rows, width = cot.shape
    local_experts, _, hidden = parts[0][0].shape
    flat = [p for group in parts for p in group]
    any_spec = pl.BlockSpec(memory_space=pl.ANY)
    params = pltpu.CompilerParams(vmem_limit_bytes=VMEM_LIMIT)
    slots = blocks * capacity
    picked_spec = pl.BlockSpec((local_experts, 1, 1, capacity, width), lambda b: (0, batch_at, b, 0, 0))
    picked = jax.ShapeDtypeStruct((local_experts, micro, blocks, capacity, width), bf16)
    x, dy = pl.pallas_call(
        functools.partial(pick_kernel, capacity, local_experts, len(earlier[:2])),
        grid=(blocks,),
        in_specs=[
            pl.BlockSpec((1, rows, tokens.shape[2]), lambda b: (b, 0, 0)),
            pl.BlockSpec((1, 1, rows, width), lambda b: (b, batch_at, 0, 0)),
        ]
        + [any_spec] * len(earlier[:2]),
        out_specs=[picked_spec] * 2,
        out_shape=[picked] * 2,
        input_output_aliases={2 + i: i for i in range(len(earlier[:2]))},
        compiler_params=params,
        cost_estimate=pl.CostEstimate(
            flops=4 * slots * local_experts * rows * width, bytes_accessed=25_000_000, transcendentals=0
        ),
    )(tokens, cot, *[a.reshape(picked.shape) for a in earlier[:2]])
    x, dy = (a.reshape(local_experts, micro, slots, width) for a in (x, dy))
    chunk = slots // 2
    row_spec = pl.BlockSpec((1, 1, chunk, width), lambda e, i: (e, batch_at, i, 0))
    hid_spec = pl.BlockSpec((1, 1, chunk, hidden), lambda e, i: (e, batch_at, i, 0))
    out_spec = pl.BlockSpec((1, chunk, width), lambda e, i: (e, i, 0))
    hid = jax.ShapeDtypeStruct((local_experts, micro, slots, hidden), bf16)
    out = jax.ShapeDtypeStruct((local_experts, slots, width), bf16)
    z, dg, du, y, dx = pl.pallas_call(
        functools.partial(expert_kernel, len(earlier[2:])),
        grid=(local_experts, 2),
        in_specs=[row_spec, row_spec] + [any_spec] * (len(flat) + len(earlier[2:])),
        out_specs=[hid_spec] * 3 + [out_spec] * 2,
        out_shape=[hid] * 3 + [out] * 2,
        input_output_aliases={2 + len(flat) + i: i for i in range(len(earlier[2:]))},
        scratch_shapes=[
            pltpu.VMEM((local_experts, width, hidden), bf16),
            pltpu.VMEM((local_experts, width, hidden), bf16),
            pltpu.VMEM((local_experts, hidden, width), bf16),
            pltpu.SemaphoreType.DMA((local_experts, 3, 4)),
        ],
        compiler_params=params,
        cost_estimate=pl.CostEstimate(
            flops=12 * local_experts * slots * width * hidden, bytes_accessed=50_000_000, transcendentals=0
        ),
    )(x, dy, *flat, *earlier[2:])
    y, dx = (a.reshape(local_experts, blocks, capacity, width) for a in (y, dx))
    part_spec = pl.BlockSpec((local_experts, 1, capacity, width), lambda b: (0, b, 0, 0))
    sums = jax.ShapeDtypeStruct((blocks * rows, width), bf16)
    sums_spec = pl.BlockSpec((rows, width), lambda b: (b, 0))
    mix, da = pl.pallas_call(
        functools.partial(sum_kernel, capacity),
        grid=(blocks,),
        in_specs=[
            pl.BlockSpec((1, rows, ROUTE_LANES), lambda b: (b, 0, width // ROUTE_LANES)),
            part_spec,
            part_spec,
        ],
        out_specs=[sums_spec] * 2,
        out_shape=[sums] * 2,
        compiler_params=params,
        cost_estimate=pl.CostEstimate(
            flops=4 * slots * local_experts * rows * width, bytes_accessed=25_000_000, transcendentals=0
        ),
    )(tokens, y, dx)
    return [x, dy, z, dg, du], mix, da


def slots_of(route_ids, gate_vals, ranking, capacity, experts):
    rows = route_ids.shape[0]
    pair_experts = route_ids.reshape(-1)
    earlier = (pair_experts[None, :] == pair_experts[:, None]) & (
        ranking[None, :] < ranking[:, None]
    )
    slot = jnp.sum(earlier.astype(jnp.int32), axis=1).reshape(rows, -1)
    kept = slot < capacity
    chosen = route_ids[:, :, None] == jnp.arange(experts, dtype=jnp.int32)[None, None, :]
    chosen = chosen & kept[:, :, None]
    slot_map = jnp.sum(jnp.where(chosen, slot[:, :, None] + 1, 0), axis=1).astype(f32) - 1.0
    weight_map = jnp.sum(jnp.where(chosen, gate_vals[:, :, None], 0.0), axis=1)
    return slot_map, weight_map


def swap(values, bit):
    return lax.ppermute(values, "dp", [(i, i ^ bit) for i in range(lax.axis_size("dp"))])


def scatter_far(total, axis):
    at = lax.axis_index("dp")
    size = total.shape[axis] // 4

    def part(bits, expert):
        start, sizes = [expert, 0, 0], list(total.shape)
        start[axis] = (at ^ bits) * size
        sizes[0], sizes[axis] = 1, size
        return lax.dynamic_slice(total, start, sizes)

    return [
        swap(part(3, 0), 1),
        swap(part(3, 1), 2),
        part(1, 0),
        part(2, 1),
        part(2, 0),
        part(1, 1),
        lax.dynamic_slice_in_dim(total, at * size, size, axis=axis),
    ]


def scatter_near(for_y, for_x, by_x, by_y, near_y, near_x, own):
    by_x, by_y = swap(by_x, 1), swap(by_y, 2)
    near_y = swap((near_y.astype(f32) + for_y.astype(f32)).astype(bf16), 2)
    near_x = swap((near_x.astype(f32) + for_x.astype(f32)).astype(bf16), 1)
    return (by_x, by_y, near_y, near_x, own)


def scatter_sum(by_x, by_y, near_y, near_x, own):
    by_x = jnp.concatenate([by_x, near_x], axis=0).astype(f32)
    by_y = jnp.concatenate([near_y, by_y], axis=0).astype(f32)
    return own.astype(f32) + by_x + by_y


def body_plain(
    inputs,
    cotangent,
    membership,
    routes,
    gate_weights,
    pair_order,
    w_query,
    w_key,
    w_value,
    w_output,
    norm_gains,
    w_gate,
    w_up,
    w_down,
):
    micro = inputs.shape[0]
    rows = inputs.shape[2]
    width = inputs.shape[3]
    group_len = membership.shape[2]
    member = lax.axis_index("expert")
    blocks = lax.axis_size("expert")
    shards = blocks * lax.axis_size("dp")
    shard_at = lax.axis_index("dp") * blocks + member
    local_experts = w_gate.shape[0]
    experts = local_experts * blocks
    capacity = rows * TOPK // experts
    step_heads = max(1, 384 // rows)
    total = micro * rows
    q_part, k_part, v_part = w_query.shape[1], w_key.shape[1], w_value.shape[1]

    gain_len = norm_gains.shape[0]
    gain_shard = jnp.zeros((2048,), bf16).at[:gain_len].set(norm_gains).reshape(16, 128)
    gain_full = lax.all_gather(gain_shard, BOTH, axis=0, tiled=True)
    gains = gain_full.reshape(shards, 2048)[:, :gain_len].reshape(-1).astype(f32)
    gain_in = gains[:width]
    gain_mid = gains[width : 2 * width]
    gain_q = gains[2 * width : 2 * width + HD]
    gain_k = gains[2 * width + HD :]

    qkv_w = lax.all_gather(
        jnp.concatenate([w_query.T, w_key.T, w_value.T], axis=0), BOTH, axis=0, tiled=True
    )
    out_w = lax.all_gather(w_output, BOTH, axis=0, tiled=True)
    wg = lax.all_gather(w_gate, "dp", axis=1, tiled=True)
    wu = lax.all_gather(w_up, "dp", axis=1, tiled=True)
    wd = lax.all_gather(w_down, "dp", axis=2, tiled=True)

    slot_map, weight_map = jax.vmap(
        lambda r, g, o: slots_of(r, g, o, capacity, experts)
    )(routes[:, 0], gate_weights[:, 0], pair_order[:, 0, 0])
    routing = jnp.concatenate([slot_map, weight_map], axis=-1)
    routing = lax.all_gather(routing, "expert", axis=0, tiled=False)
    mine = member * local_experts
    slot_mine = lax.dynamic_slice_in_dim(routing, mine, local_experts, axis=3)
    weight_mine = lax.dynamic_slice_in_dim(routing, experts + mine, local_experts, axis=3)
    slot_mine = jnp.transpose(slot_mine, (1, 3, 0, 2))
    weight_mine = jnp.transpose(weight_mine, (1, 3, 0, 2))
    slot_ids = jnp.arange(capacity, dtype=f32)
    hit = slot_mine[:, :, :, None, :] == slot_ids[None, None, None, :, None]
    pick = hit.astype(bf16)
    weighted = jnp.where(hit, weight_mine[:, :, :, None, :], 0.0)
    slot_weight = jnp.sum(weighted, axis=-1)
    weighted = weighted.astype(bf16)

    key_index = jnp.arange(group_len, dtype=jnp.int32)
    start_row = member * rows
    segment = membership[:, 0]
    row_index = start_row + jnp.arange(rows, dtype=jnp.int32)
    seg_rows = lax.dynamic_slice_in_dim(segment, start_row, rows, axis=1)
    before = jnp.sum((segment[:, None, :] < seg_rows[:, :, None]).astype(jnp.int32), axis=2)
    position = jnp.where(seg_rows == 0, row_index[None], PROMPT + row_index[None] - before)
    allowed = (key_index[None, :, None] <= row_index[None, None, :]) & (
        (segment[:, :, None] == 0) | (segment[:, :, None] == seg_rows[:, None, :])
    )
    bias = jnp.tile(jnp.where(allowed, 0.0, MASKED).astype(f32), (1, 1, step_heads))
    frequency = ROPE_BASE ** (-(jnp.arange(HD // 2, dtype=f32) * 2.0 / HD))
    angles = position.astype(f32).reshape(total)[:, None] * frequency[None, :]
    cosine = jnp.cos(angles)[:, None, :]
    sine_part = jnp.sin(angles)[:, None, :]

    hidden = inputs[:, 0].astype(f32).reshape(total, width)
    scale_in = rms_scale(hidden)
    normed = (hidden * scale_in * gain_in).astype(bf16)
    proj = mm(normed, qkv_w, NT).reshape(total, shards, q_part + k_part + v_part)
    queries = proj[:, :, :q_part].reshape(total, H, HD)
    key_pre = proj[:, :, q_part : q_part + k_part].reshape(total, KVH, HD)
    value = proj[:, :, q_part + k_part :].reshape(total, KVH, HD).astype(bf16)
    scale_q = rms_scale(queries)
    scale_k = rms_scale(key_pre)
    q_low = rotate(queries * scale_q * (gain_q * (SCALE * LOG2E)), cosine, sine_part).astype(bf16)
    q_low = q_low.reshape(micro, rows, H * HD)
    k_low = rotate(key_pre * scale_k * gain_k, cosine, sine_part).astype(bf16)
    kv_own = jnp.concatenate([k_low, value], axis=-1).reshape(micro, rows, KVH * 2 * HD)
    kv_all = lax.all_gather(kv_own, "expert", axis=0, tiled=False)
    chunk = 256
    mixed = []
    for at in range(micro):
        mixed = run_forward(q_low, kv_all[:, at : at + 1], bias, step_heads, chunk, at, mixed)
    mixed, logs = mixed

    branch = mm(mixed.reshape(total, H * HD), out_w)
    middle = hidden + branch
    scale_mid = rms_scale(middle)
    routed = (middle * scale_mid * gain_mid).astype(bf16).reshape(micro, rows, width)
    middle = middle.reshape(micro, rows, width)
    scale_mid = scale_mid.reshape(micro, rows, 1)

    outputs, d_branches, d_middles = [], [], []
    acc_gate = acc_up = acc_down = 0.0
    grad_mid = 0.0
    slots = blocks * capacity
    for at in range(micro):
        d_out = lax.all_gather(cotangent[at, 0], "expert", axis=0, tiled=False)
        tokens = lax.all_gather(routed[at], "expert", axis=0, tiled=False)
        picked = jnp.einsum("ebst,btd->ebsd", pick[at], tokens, preferred_element_type=f32)
        picked = picked.astype(bf16).reshape(local_experts, slots, width)
        d_result = jnp.einsum("ebst,btd->ebsd", pick[at], d_out, preferred_element_type=f32)
        d_result = (d_result * slot_weight[at][..., None]).astype(bf16)
        d_result = d_result.reshape(local_experts, slots, width)
        gate_pre = jnp.einsum("erd,edf->erf", picked, wg, preferred_element_type=f32)
        up_pre = jnp.einsum("erd,edf->erf", picked, wu, preferred_element_type=f32)
        d_hidden = jnp.einsum("erd,efd->erf", d_result, wd, preferred_element_type=f32)
        sigmoid_g = jax.nn.sigmoid(gate_pre)
        silu_g = gate_pre * sigmoid_g
        hidden_low = (silu_g * up_pre).astype(bf16)
        d_gate = (d_hidden * up_pre * sigmoid_g * (1.0 + gate_pre * (1.0 - sigmoid_g))).astype(bf16)
        d_up = (d_hidden * silu_g).astype(bf16)
        d_rows = jnp.einsum("erf,edf->erd", d_gate, wg, preferred_element_type=f32)
        d_rows = d_rows + jnp.einsum("erf,edf->erd", d_up, wu, preferred_element_type=f32)
        d_rows = d_rows.astype(bf16).reshape(local_experts, blocks, capacity, width)
        d_part = jnp.einsum("ebst,ebsd->btd", pick[at], d_rows, preferred_element_type=f32)
        d_part = d_part.astype(bf16).reshape(group_len, width)
        d_routed = lax.psum_scatter(d_part, "expert", scatter_dimension=0, tiled=True).astype(f32)
        result = jnp.einsum("erf,efd->erd", hidden_low, wd, preferred_element_type=f32)
        result = result.astype(bf16).reshape(local_experts, blocks, capacity, width)
        part = jnp.einsum("ebst,ebsd->btd", weighted[at], result, preferred_element_type=f32)
        part = part.astype(bf16).reshape(group_len, width)
        expert_mix = lax.psum_scatter(part, "expert", scatter_dimension=0, tiled=True).astype(f32)
        outputs.append((middle[at] + expert_mix).astype(bf16))

        acc_down += jnp.einsum("erf,erd->efd", hidden_low, d_result, preferred_element_type=f32)
        acc_gate += jnp.einsum("erd,erf->edf", picked, d_gate, preferred_element_type=f32)
        acc_up += jnp.einsum("erd,erf->edf", picked, d_up, preferred_element_type=f32)

        d_mid_norm, mid_gain_grad = norm_back(d_routed, middle[at], scale_mid[at], gain_mid)
        grad_mid = grad_mid + mid_gain_grad
        d_middle = cotangent[at, 0].astype(f32) + d_mid_norm
        d_middles.append(d_middle)
        d_branches.append(d_middle.astype(bf16))

    grad_gate = lax.psum_scatter(acc_gate.astype(bf16), "dp", scatter_dimension=1, tiled=True)
    grad_up = lax.psum_scatter(acc_up.astype(bf16), "dp", scatter_dimension=1, tiled=True)
    grad_down = lax.psum_scatter(acc_down.astype(bf16), "dp", scatter_dimension=2, tiled=True)

    d_branch = jnp.concatenate(d_branches, axis=0)
    d_middle = jnp.concatenate(d_middles, axis=0)
    grad_output = mm(mixed.reshape(total, H * HD), d_branch, TN).astype(bf16)
    grad_output = lax.psum_scatter(grad_output, BOTH, scatter_dimension=0, tiled=True)
    d_mixed = mm(d_branch, out_w, NT).astype(bf16).reshape(micro, rows, H * HD)
    cos_rows = jnp.concatenate([cosine, cosine], axis=-1).reshape(micro, rows, HD)
    sine_rows = jnp.concatenate([-sine_part, sine_part], axis=-1).reshape(micro, rows, HD)
    q_raw = queries.reshape(micro, rows, H * HD)
    d_query, dkv_list, grad_qn = [], [], 0.0
    for at in range(micro):
        d_query, dkv_one, part = run_backward(
            q_low, kv_all[:, at : at + 1], bias, mixed, d_mixed, logs, q_raw, cos_rows, sine_rows,
            gain_q[None, :], step_heads, chunk, at, [d_query] if at else []
        )
        dkv_list.append(dkv_one)
        grad_qn += part[0]
    dkv_all = jnp.concatenate(dkv_list, axis=1)
    dkv = lax.psum_scatter(dkv_all, "expert", scatter_dimension=0, tiled=False)
    dkv = dkv.reshape(total, KVH, 2 * HD)
    d_key = rotate(dkv[:, :, :HD].astype(f32), cosine, -sine_part)
    d_key, grad_kn = norm_back(d_key, key_pre, scale_k, gain_k)
    d_proj = jnp.concatenate(
        [
            d_query.reshape(total, shards, q_part),
            d_key.astype(bf16).reshape(total, shards, k_part),
            dkv[:, :, HD:].reshape(total, shards, v_part),
        ],
        axis=-1,
    ).reshape(total, -1)
    grad_qkv = mm(d_proj, normed, TN).astype(bf16)
    grad_qkv = lax.psum_scatter(grad_qkv, BOTH, scatter_dimension=0, tiled=True).astype(f32)
    d_normed = mm(d_proj, qkv_w)
    d_in_norm, grad_in = norm_back(d_normed, hidden, scale_in, gain_in)
    input_grad = d_middle + d_in_norm

    gain_grads = jnp.concatenate([grad_in, grad_mid, grad_qn, grad_kn]).reshape(shards, gain_len)
    gain_grads = jnp.pad(gain_grads, ((0, 0), (0, 256 - gain_len % 256)))
    gain_all = lax.all_gather(gain_grads, BOTH, axis=0, tiled=False)
    grad_gains = jnp.sum(lax.dynamic_index_in_dim(gain_all, shard_at, axis=1, keepdims=False), axis=0)
    return (
        jnp.stack(outputs)[:, None],
        input_grad.reshape(micro, 1, rows, width),
        grad_qkv[:q_part].T,
        grad_qkv[q_part : q_part + k_part].T,
        grad_qkv[q_part + k_part :].T,
        grad_output.astype(f32),
        grad_gains[:gain_len],
        grad_gate.astype(f32),
        grad_up.astype(f32),
        grad_down.astype(f32),
    )


def body_fast(
    inputs,
    cotangent,
    membership,
    routes,
    gate_weights,
    pair_order,
    w_query,
    w_key,
    w_value,
    w_output,
    norm_gains,
    w_gate,
    w_up,
    w_down,
):
    micro = inputs.shape[0]
    rows = inputs.shape[2]
    width = inputs.shape[3]
    group_len = membership.shape[2]
    member = lax.axis_index("expert")
    blocks = lax.axis_size("expert")
    shards = blocks * lax.axis_size("dp")
    local_experts = w_gate.shape[0]
    experts = local_experts * blocks
    capacity = rows * TOPK // experts
    step_heads = max(1, 384 // rows)
    total = micro * rows
    q_part, k_part, v_part = w_query.shape[1], w_key.shape[1], w_value.shape[1]
    tie = lax.optimization_barrier

    slot_map, weight_map = jax.vmap(
        lambda r, g, o: slots_of(r, g, o, capacity, experts)
    )(routes[:, 0], gate_weights[:, 0], pair_order[:, 0, 0])
    weight_high = tie(weight_map.astype(bf16))
    weight_low = (weight_map - weight_high.astype(f32)).astype(bf16)

    def padded(values, lanes):
        return jnp.pad(values, ((0, 0), (0, 0), (0, lanes - experts)))

    routing = jnp.concatenate(
        [
            padded(slot_map.astype(bf16), 32),
            padded(weight_high, 32),
            padded(weight_low, ROUTE_LANES - 64),
        ],
        axis=-1,
    )

    gain_len = norm_gains.shape[0]
    gain_shard = jnp.zeros((2048,), bf16).at[:gain_len].set(norm_gains).reshape(16, 128)
    kv_w = jnp.concatenate([w_key.T, w_value.T], axis=0)
    q_w, kv_w, out_w, gain_full, cot_all = gather_rows(
        [w_query.T, kv_w, w_output, gain_shard, cotangent.reshape(total, width)], [(3, 0, 1, 2)], 1, (4,)
    )
    cot_all = cot_all.reshape(blocks, micro, rows, width)
    q_w, w_gate, w_up, w_down = tie((q_w, w_gate, w_up, w_down))
    gains = gain_full.reshape(shards, 2048)[:, :gain_len].reshape(-1).astype(f32)
    gain_in = gains[:width]
    gain_mid = gains[width : 2 * width]
    gain_q = gains[2 * width : 2 * width + HD]
    gain_k = gains[2 * width + HD :]
    gate_near, up_near, down_near = ((swap(w, 1), swap(w, 2)) for w in (w_gate, w_up, w_down))

    key_index = jnp.arange(group_len, dtype=jnp.int32)
    start_row = member * rows
    segment = membership[:, 0]
    row_index = start_row + jnp.arange(rows, dtype=jnp.int32)
    seg_rows = lax.dynamic_slice_in_dim(segment, start_row, rows, axis=1)
    before = jnp.sum((segment[:, None, :] < seg_rows[:, :, None]).astype(jnp.int32), axis=2)
    position = jnp.where(seg_rows == 0, row_index[None], PROMPT + row_index[None] - before)
    allowed = (key_index[None, :, None] <= row_index[None, None, :]) & (
        (segment[:, :, None] == 0) | (segment[:, :, None] == seg_rows[:, None, :])
    )
    bias = jnp.tile(jnp.where(allowed, 0.0, MASKED).astype(f32), (1, 1, step_heads))
    frequency = ROPE_BASE ** (-(jnp.arange(HD // 2, dtype=f32) * 2.0 / HD))
    angles = position.astype(f32).reshape(total)[:, None] * frequency[None, :]
    cosine, sine = jnp.cos(angles), jnp.sin(angles)
    cosine = jnp.concatenate([cosine, cosine], axis=-1)
    sine = jnp.concatenate([-sine, sine], axis=-1)
    gain_q, gain_k = gain_q[None, :], gain_k[None, :]

    hidden = inputs[:, 0].astype(f32).reshape(total, width)
    scale_in = rms_scale(hidden)
    normed = (hidden * scale_in * gain_in).astype(bf16)
    q_low, q_raw, kv_own, k_raw, kv_w = run_project(
        normed, q_w, kv_w, cosine, sine, gain_q * (SCALE * LOG2E), gain_k
    )
    q_low, q_raw = (a.reshape(micro, rows, H * HD) for a in (q_low, q_raw))
    kv_own = kv_own.reshape(micro, rows, KVH * 2 * HD)
    kv_0 = lax.all_gather(kv_own[0], "expert", axis=0, tiled=False)
    kv_1 = lax.all_gather(kv_own[1], "expert", axis=0, tiled=False)
    kv_0, gate_near = tie((kv_0, gate_near))
    kv_all = [kv_0[:, None], kv_1[:, None]]
    chunk = 256
    mixed = run_forward(q_low, kv_all[0], bias, step_heads, chunk, 0, [])
    mixed, kv_all = tie((mixed, kv_all))
    mixed, logs = run_forward(q_low, kv_all[1], bias, step_heads, chunk, 1, mixed)
    mixed, up_near, down_near = tie((mixed, up_near, down_near))
    parts = [
        (own, near[0], near[1], swap(near[0][:1], 2), swap(near[1][1:], 1))
        for own, near in ((w_gate, gate_near), (w_up, up_near), (w_down, down_near))
    ]

    branch = mm(mixed.reshape(total, H * HD), out_w)
    middle = hidden + branch
    scale_mid = rms_scale(middle)
    routed = (middle * scale_mid * gain_mid).astype(bf16).reshape(micro, rows, width)
    routed = jnp.concatenate([routed, routing], axis=-1)
    middle = middle.reshape(micro, rows, width)
    scale_mid = scale_mid.reshape(micro, rows, 1)

    mix_parts, d_routeds = [], []
    kept = []
    for at in range(micro):
        tokens = lax.all_gather(routed[at], "expert", axis=0, tiled=False)
        tokens, parts = tie((tokens, parts))
        kept, mix, d_part = run_experts(tokens, cot_all, parts, capacity, at, micro, kept)
        kept, d_part, mix, d_routeds = tie((kept, d_part, mix, d_routeds))
        mix_parts.append(mix)
        d_routed = lax.psum_scatter(d_part, "expert", scatter_dimension=0, tiled=True)
        d_routeds.append(d_routed)
    picked, d_result, hidden_low, d_gate, d_up = (
        a.reshape(local_experts, -1, a.shape[-1]) for a in kept
    )

    def weight_grad(rows_in, rows_out):
        return jnp.einsum("era,erb->eab", rows_in, rows_out, preferred_element_type=f32).astype(bf16)

    scattering = [
        scatter_far(weight_grad(hidden_low, d_result), 2),
        scatter_far(weight_grad(picked, d_gate), 1),
        scatter_far(weight_grad(picked, d_up), 1),
    ]
    d_routeds[-1], scattering, mix_parts[0] = tie((d_routeds[-1], scattering, mix_parts[0]))
    expert_grads = [scatter_near(*pieces) for pieces in scattering]
    d_mixed, d_middle, d_branch, grad_mid = run_middle_back(
        d_routeds, middle, cotangent[:, 0], gain_mid[None, :], out_w
    )
    d_mixed = d_mixed.reshape(micro, rows, H * HD)
    cos_rows, sine_rows = (a.reshape(micro, rows, HD) for a in (cosine, sine))
    d_query, dkv_all, grad_qn = [], [], 0.0
    for at in range(micro):
        d_query, dkv_one, part = run_backward(
            q_low, kv_all[at], bias, mixed, d_mixed, logs, q_raw, cos_rows, sine_rows, gain_q,
            step_heads, chunk, at, [d_query] if at else []
        )
        dkv_all.append(dkv_one[:, 0])
        grad_qn += part
    mixes = [lax.psum_scatter(mix_parts[0], "expert", scatter_dimension=0, tiled=True)]
    mixed_after, d_query, dkv_all, expert_grads, mixes = tie(
        (mixed, d_query, dkv_all, expert_grads, mixes)
    )
    grad_output, _ = reduce_rows(mixed_after.reshape(total, H * HD), None, d_branch, 2)
    dkv = jnp.concatenate(
        [lax.psum_scatter(part, "expert", scatter_dimension=0, tiled=False) for part in dkv_all], axis=0
    )
    dkv, grad_output, d_query = tie((dkv, grad_output, d_query))
    d_query = d_query.reshape(total, H * HD)
    dkv = dkv.reshape(total, KVH * 2 * HD)
    mix_part, dkv = tie((mix_parts[1], dkv))
    mixes.append(lax.psum_scatter(mix_part, "expert", scatter_dimension=0, tiled=True))
    outputs = [(middle[at] + mixes[at].astype(f32)).astype(bf16) for at in range(micro)]
    dkv, dkv_t, grad_kn = run_key_back(dkv, k_raw, cosine, sine, gain_k)
    d_normed = mm(d_query, q_w) + mm(dkv, kv_w)
    d_in_norm, grad_in = norm_back(d_normed, hidden, scale_in, gain_in)
    input_grad = d_middle + d_in_norm
    gain_grads = jnp.concatenate([grad_in, grad_mid[0], grad_qn[0], grad_kn[0]]).reshape(shards, gain_len)
    grad_qkv, grad_gains = reduce_rows(d_query, dkv_t, normed, 3, gain_grads)
    expert_grads = [scatter_sum(*pieces) for pieces in expert_grads]
    return (
        jnp.stack(outputs)[:, None],
        input_grad.reshape(micro, 1, rows, width),
        grad_qkv[:q_part].T,
        grad_qkv[q_part : q_part + k_part].T,
        grad_qkv[q_part + k_part :].T,
        grad_output,
        grad_gains[0, :gain_len],
        expert_grads[1],
        expert_grads[2],
        expert_grads[0],
    )


def solution(mesh):
    fast = mesh.shape["dp"] == 4 and mesh.shape["expert"] == 8
    return jax.shard_map(
        body_fast if fast else body_plain,
        mesh=mesh,
        in_specs=(
            P(None, "dp", "expert", None),
            P(None, "dp", "expert", None),
            P(None, "dp", None),
            P(None, "dp", "expert", None),
            P(None, "dp", "expert", None),
            P(None, "dp", "expert", None),
            P(None, ("dp", "expert")),
            P(None, ("dp", "expert")),
            P(None, ("dp", "expert")),
            P(("dp", "expert"), None),
            P(("dp", "expert")),
            P("expert", "dp", None),
            P("expert", "dp", None),
            P("expert", None, "dp"),
        ),
        out_specs=(
            P(None, "dp", "expert", None),
            P(None, "dp", "expert", None),
            P(None, ("dp", "expert")),
            P(None, ("dp", "expert")),
            P(None, ("dp", "expert")),
            P(("dp", "expert"), None),
            P(("dp", "expert")),
            P("expert", "dp", None),
            P("expert", "dp", None),
            P("expert", None, "dp"),
        ),
        check_vma=False,
    )
```

```python
import functools
import math

import jax
import jax.numpy as jnp
from jax import lax
from jax.experimental import pallas as pl
from jax.experimental.pallas import tpu as pltpu
from jax.sharding import PartitionSpec as P

H = 32
KVH = 4
HD = 128
FF = 768
TOPK = 8
PROMPT = 1024
PER_KV = H // KVH

EPSILON = 1e-06
ROPE_BASE = 1000000.0
MASKED = -1e30
LOG2E = math.log2(math.e)
SCALE = HD ** (-0.5)

bf16 = jnp.bfloat16
f32 = jnp.float32
NT = (((1,), (1,)), ((), ()))
TN = (((0,), (0,)), ((), ()))
NN = (((1,), (0,)), ((), ()))
BOTH = ("dp", "expert")
VMEM_LIMIT = 56 * 1024 * 1024


def mm(a, b, dims=NN):
    return lax.dot_general(a, b, dims, preferred_element_type=f32)


def rms_scale(values):
    return lax.rsqrt(jnp.mean(values * values, axis=-1, keepdims=True) + EPSILON)


def norm_back(upstream, values, inv_rms, norm_gain):
    lifted = upstream * norm_gain
    inner_dot = jnp.mean(lifted * values, axis=-1, keepdims=True)
    back_grad = inv_rms * lifted - values * (inv_rms * inv_rms * inv_rms) * inner_dot
    gain_grad = jnp.sum((upstream * values * inv_rms).reshape(-1, values.shape[-1]), axis=0)
    return (back_grad, gain_grad)


def rotate(values, cosine, sine_part):
    half_dim = values.shape[-1] // 2
    first_half = values[..., :half_dim]
    second_half = values[..., half_dim:]
    return jnp.concatenate(
        [
            first_half * cosine - second_half * sine_part,
            second_half * cosine + first_half * sine_part,
        ],
        axis=-1,
    )


def turn(values, cosine, sine):
    return values * cosine + pltpu.roll(values, HD // 2, 1) * sine


def project(x_ref, wq_ref, wkv_ref, cos_ref, sin_ref, gq_ref, gk_ref, q_ref, qraw_ref, kv_ref, kraw_ref, wkv_out):
    x = x_ref[...]
    cosine, sine = cos_ref[...], sin_ref[...]
    for at in range(0, PER_KV * HD, 2 * HD):
        raw = mm(x, wq_ref[at : at + 2 * HD], NT)
        qraw_ref[:, at : at + 2 * HD] = raw
        for lane in (0, HD):
            head = raw[:, lane : lane + HD]
            normed = head * rms_scale(head) * gq_ref[...]
            q_ref[:, at + lane : at + lane + HD] = turn(normed, cosine, sine).astype(bf16)
    piece = HD // PER_KV
    w_k = [wkv_ref[2 * piece * i : 2 * piece * i + piece] for i in range(PER_KV)]
    w_v = [wkv_ref[2 * piece * i + piece : 2 * piece * (i + 1)] for i in range(PER_KV)]
    w_kv = jnp.concatenate(w_k + w_v, axis=0)
    wkv_out[...] = w_kv
    raw = mm(x, w_kv, NT)
    key = raw[:, :HD]
    kraw_ref[...] = key
    normed = key * rms_scale(key) * gk_ref[...]
    kv_ref[:, :HD] = turn(normed, cosine, sine).astype(bf16)
    kv_ref[:, HD:] = raw[:, HD:].astype(bf16)


def run_project(x, wq, wkv, cosine, sine, gain_q, gain_k):
    tokens, width = x.shape
    wide = PER_KV * HD
    whole = lambda a: pl.BlockSpec(a.shape, lambda g: (0, 0))
    cols = lambda n: pl.BlockSpec((tokens, n), lambda g: (0, g))
    rows = lambda n: pl.BlockSpec((n, width), lambda g: (g, 0))
    return pl.pallas_call(
        project,
        grid=(KVH,),
        in_specs=[whole(x), rows(wide), rows(2 * HD), whole(cosine), whole(sine), whole(gain_q), whole(gain_k)],
        out_specs=[cols(wide), cols(wide), cols(2 * HD), cols(HD), rows(2 * HD)],
        out_shape=[
            jax.ShapeDtypeStruct((tokens, H * HD), bf16),
            jax.ShapeDtypeStruct((tokens, H * HD), f32),
            jax.ShapeDtypeStruct((tokens, KVH * 2 * HD), bf16),
            jax.ShapeDtypeStruct((tokens, KVH * HD), f32),
            jax.ShapeDtypeStruct((KVH * 2 * HD, width), bf16),
        ],
        compiler_params=pltpu.CompilerParams(vmem_limit_bytes=VMEM_LIMIT),
        cost_estimate=pl.CostEstimate(
            flops=2 * tokens * width * (H + 2 * KVH) * HD, bytes_accessed=40_000_000, transcendentals=0
        ),
    )(x, wq, wkv, cosine, sine, gain_q, gain_k)


def norm_turn_back(grad, raw, cosine, sine, gain):
    grad = turn(grad, cosine, -sine)
    scale = rms_scale(raw)
    lifted = grad * gain
    inner = jnp.mean(lifted * raw, axis=-1, keepdims=True)
    back = scale * lifted - raw * (scale * scale * scale) * inner
    return back, jnp.sum(grad * raw * scale, axis=0, keepdims=True)


def key_back(dkv_ref, kraw_ref, cos_ref, sin_ref, gk_ref, out_ref, out_t_ref, gain_ref):
    gain_sum = 0.0
    for g in range(KVH):
        key = slice(2 * g * HD, (2 * g + 1) * HD)
        value = slice((2 * g + 1) * HD, (2 * g + 2) * HD)
        grad = dkv_ref[:, key].astype(f32)
        back, part = norm_turn_back(
            grad, kraw_ref[:, g * HD : (g + 1) * HD], cos_ref[...], sin_ref[...], gk_ref[...]
        )
        gain_sum += part
        low = back.astype(bf16)
        out_ref[:, key] = low
        out_t_ref[key] = low.T
        out_ref[:, value] = dkv_ref[:, value]
        out_t_ref[value] = dkv_ref[:, value].T
    gain_ref[...] = gain_sum


def run_key_back(dkv, key_raw, cosine, sine, gain):
    tokens, wide = dkv.shape
    return pl.pallas_call(
        key_back,
        out_shape=[
            jax.ShapeDtypeStruct((tokens, wide), bf16),
            jax.ShapeDtypeStruct((wide, tokens), bf16),
            jax.ShapeDtypeStruct((1, HD), f32),
        ],
        compiler_params=pltpu.CompilerParams(vmem_limit_bytes=VMEM_LIMIT),
    )(dkv, key_raw, cosine, sine, gain)


def attend_forward(step_heads, chunk, q_ref, kv_ref, bias_ref, o_ref, log_ref):
    group_len = bias_ref.shape[1]
    keys = kv_ref[:, 0, :, :HD].reshape(group_len, HD)
    values_t = kv_ref[:, 0, :, HD:].reshape(group_len, HD).T
    rows = q_ref.shape[1]
    for step in range(PER_KV // step_heads):
        heads = range(step * step_heads, (step + 1) * step_heads)
        query = jnp.concatenate([q_ref[0, :, h * HD : (h + 1) * HD] for h in heads], axis=0)
        mixed, row_sum = 0.0, 0.0
        for at in range(0, group_len, chunk):
            scores = mm(keys[at : at + chunk], query, NT)
            prob = jnp.exp2(scores + bias_ref[0, at : at + chunk, :])
            row_sum += jnp.sum(prob, axis=0, keepdims=True)
            mixed += mm(values_t[:, at : at + chunk], prob.astype(bf16))
        out = (mixed / row_sum).T.astype(bf16)
        for i, h in enumerate(heads):
            o_ref[0, :, h * HD : (h + 1) * HD] = out[i * rows : (i + 1) * rows]
        log_ref[0, 0, step : step + 1, :] = jnp.log2(row_sum)


def attend_backward(
    step_heads, chunk, q_ref, kv_ref, bias_ref, o_ref, do_ref, log_ref, raw_ref, cos_ref, sin_ref, gain_ref,
    dq_ref, dkv_ref, gain_out, dk_acc, dv_acc
):
    group_len = bias_ref.shape[1]
    keys = kv_ref[:, 0, :, :HD].reshape(group_len, HD)
    values = kv_ref[:, 0, :, HD:].reshape(group_len, HD)
    keys_t = keys.T
    rows = q_ref.shape[1]
    cosine, sine, gain = cos_ref[0], sin_ref[0], gain_ref[...]

    @pl.when(pl.program_id(0) == 0)
    def _():
        gain_out[...] = jnp.zeros_like(gain_out)

    gain_sum = 0.0
    dk_acc[...] = jnp.zeros_like(dk_acc)
    dv_acc[...] = jnp.zeros_like(dv_acc)
    for step in range(PER_KV // step_heads):
        heads = range(step * step_heads, (step + 1) * step_heads)
        query = jnp.concatenate([q_ref[0, :, h * HD : (h + 1) * HD] for h in heads], axis=0)
        grad = jnp.concatenate([do_ref[0, :, h * HD : (h + 1) * HD] for h in heads], axis=0)
        mixed = jnp.concatenate([o_ref[0, :, h * HD : (h + 1) * HD] for h in heads], axis=0)
        row_dot = jnp.sum((grad.astype(f32) * mixed.astype(f32)).T, axis=0, keepdims=True)
        log_sum = log_ref[0, 0, step : step + 1, :]
        dq_t = 0.0
        for at in range(0, group_len, chunk):
            part = slice(at, at + chunk)
            scores = mm(keys[part], query, NT)
            prob = jnp.exp2(scores + (bias_ref[0, part, :] - log_sum))
            d_prob = mm(values[part], grad, NT)
            d_score = (prob * (d_prob - row_dot)).astype(bf16)
            dv_acc[part] += mm(prob.astype(bf16), grad)
            dk_acc[part] += mm(d_score, query)
            dq_t += mm(keys_t[:, part], d_score)
        out = (dq_t * SCALE).T.astype(bf16).astype(f32)
        for i, h in enumerate(heads):
            head = slice(h * HD, (h + 1) * HD)
            back, part = norm_turn_back(
                out[i * rows : (i + 1) * rows], raw_ref[0, :, head], cosine, sine, gain
            )
            dq_ref[0, :, head] = back.astype(bf16)
            gain_sum += part
    gain_out[...] += gain_sum
    blocks = dkv_ref.shape[0]
    dkv_ref[:, 0, :, :HD] = (dk_acc[...] * (1.0 / LOG2E)).astype(bf16).reshape(blocks, rows, HD)
    dkv_ref[:, 0, :, HD:] = dv_acc[...].astype(bf16).reshape(blocks, rows, HD)


def attention_specs(rows, group_len, blocks, step_heads, at):
    wide = PER_KV * HD
    q_spec = pl.BlockSpec((1, rows, wide), lambda g: (at, 0, g))
    kv_spec = pl.BlockSpec((blocks, 1, rows, 2 * HD), lambda g: (0, 0, 0, g))
    bias_spec = pl.BlockSpec((1, group_len, step_heads * rows), lambda g: (at, 0, 0))
    log_spec = pl.BlockSpec((1, 1, PER_KV // step_heads, step_heads * rows), lambda g: (at, g, 0, 0))
    return q_spec, kv_spec, bias_spec, log_spec


def run_forward(query, kv_all, bias, step_heads, chunk, at, earlier):
    micro, rows, _ = query.shape
    blocks = kv_all.shape[0]
    group_len = bias.shape[1]
    q_spec, kv_spec, bias_spec, log_spec = attention_specs(rows, group_len, blocks, step_heads, at)
    flops = 4 * rows * H * HD * group_len

    def kernel(*refs):
        attend_forward(step_heads, chunk, *refs[:3], *refs[3 + len(earlier) :])

    return pl.pallas_call(
        kernel,
        grid=(KVH,),
        in_specs=[q_spec, kv_spec, bias_spec] + [pl.BlockSpec(memory_space=pl.ANY)] * len(earlier),
        out_specs=[q_spec, log_spec],
        out_shape=[
            jax.ShapeDtypeStruct(query.shape, bf16),
            jax.ShapeDtypeStruct((micro, KVH, PER_KV // step_heads, step_heads * rows), f32),
        ],
        input_output_aliases={3 + i: i for i in range(len(earlier))},
        compiler_params=pltpu.CompilerParams(vmem_limit_bytes=VMEM_LIMIT),
        cost_estimate=pl.CostEstimate(
            flops=flops, bytes_accessed=20_000_000, transcendentals=flops // (4 * HD)
        ),
    )(query, kv_all, bias, *earlier)


def run_backward(query, kv_all, bias, mixed, grad, logs, raw, cosine, sine, gain, step_heads, chunk, at, earlier):
    micro, rows, _ = query.shape
    blocks = kv_all.shape[0]
    group_len = bias.shape[1]
    q_spec, kv_spec, bias_spec, log_spec = attention_specs(rows, group_len, blocks, step_heads, at)
    flops = 10 * rows * H * HD * group_len
    gain_spec = pl.BlockSpec((1, HD), lambda g: (0, 0))

    def kernel(*refs):
        attend_backward(step_heads, chunk, *refs[:10], *refs[10 + len(earlier) :])

    return pl.pallas_call(
        kernel,
        grid=(KVH,),
        in_specs=[q_spec, kv_spec, bias_spec, q_spec, q_spec, log_spec, q_spec]
        + [pl.BlockSpec((1, rows, HD), lambda g: (at, 0, 0))] * 2
        + [gain_spec]
        + [pl.BlockSpec(memory_space=pl.ANY)] * len(earlier),
        out_specs=[q_spec, kv_spec, gain_spec],
        out_shape=[
            jax.ShapeDtypeStruct(query.shape, bf16),
            jax.ShapeDtypeStruct(kv_all.shape, bf16),
            jax.ShapeDtypeStruct((1, HD), f32),
        ],
        input_output_aliases={10 + i: i for i in range(len(earlier))},
        scratch_shapes=[pltpu.VMEM((group_len, HD), f32), pltpu.VMEM((group_len, HD), f32)],
        compiler_params=pltpu.CompilerParams(vmem_limit_bytes=VMEM_LIMIT),
        cost_estimate=pl.CostEstimate(
            flops=flops, bytes_accessed=30_000_000, transcendentals=flops // (10 * HD)
        ),
    )(query, kv_all, bias, mixed, grad, logs, raw, cosine, sine, gain, *earlier)


def middle_back(r0_ref, r1_ref, mid_ref, cot_ref, gain_ref, w_ref, mix_ref, dmid_ref, low_ref, gain_out):
    @pl.when(pl.program_id(0) == 0)
    def _():
        gain_sum = 0.0
        rows = r0_ref.shape[0]
        for b, ref in enumerate((r0_ref, r1_ref)):
            grad = ref[...].astype(f32)
            middle = mid_ref[b]
            scale = rms_scale(middle)
            lifted = grad * gain_ref[...]
            inner = jnp.mean(lifted * middle, axis=-1, keepdims=True)
            total = cot_ref[b].astype(f32) + scale * lifted - middle * (scale * scale * scale) * inner
            gain_sum += jnp.sum(grad * middle * scale, axis=0, keepdims=True)
            dmid_ref[b * rows : (b + 1) * rows] = total
            low_ref[b * rows : (b + 1) * rows] = total.astype(bf16)
        gain_out[...] = gain_sum

    mix_ref[...] = mm(low_ref[...], w_ref[...], NT).astype(bf16)


def run_middle_back(routed, middle, cot, gain, out_w):
    micro, rows, width = middle.shape
    total = micro * rows
    piece = 512
    whole = lambda *shape: pl.BlockSpec(shape, lambda i: (0,) * len(shape))
    return pl.pallas_call(
        middle_back,
        grid=(out_w.shape[0] // piece,),
        in_specs=[whole(rows, width)] * 2
        + [whole(micro, rows, width)] * 2
        + [whole(1, width), pl.BlockSpec((piece, width), lambda i: (i, 0))],
        out_specs=[
            pl.BlockSpec((total, piece), lambda i: (0, i)),
            whole(total, width),
            whole(total, width),
            whole(1, width),
        ],
        out_shape=[
            jax.ShapeDtypeStruct((total, out_w.shape[0]), bf16),
            jax.ShapeDtypeStruct((total, width), f32),
            jax.ShapeDtypeStruct((total, width), bf16),
            jax.ShapeDtypeStruct((1, width), f32),
        ],
        compiler_params=pltpu.CompilerParams(vmem_limit_bytes=VMEM_LIMIT),
        cost_estimate=pl.CostEstimate(
            flops=2 * total * width * out_w.shape[0], bytes_accessed=35_000_000, transcendentals=0
        ),
    )(*routed, middle, cot, gain, out_w)


MESH = pl.DeviceIdType.MESH


def gather_kernel(phases, count, late, *refs):
    ins, outs, sems = refs[:count], refs[count : 2 * count], refs[2 * count :]
    dp = lax.axis_index("dp"); member = lax.axis_index("expert")
    blocks = lax.axis_size("expert")
    core = member % 2; z = member // 2
    depth = blocks // 2
    sibling = (dp, member + 1 - 2 * core)
    by_x = (dp + 1 - 2 * (dp % 2), member)
    by_y = ((dp + 2) % 4, member)
    x_at, y_at, far_at = by_x[0], by_y[0], 3 - dp
    above, below = (dp, member + 2), (dp, member - 2)
    barrier = pltpu.get_barrier_semaphore()
    peers = [(sibling, None), (by_x, None), (by_y, None), (above, z < depth - 1), (below, z > 0)]
    for peer, ok in peers:
        if ok is None:
            pl.semaphore_signal(barrier, inc=1, device_id=peer, device_id_type=MESH)
        else:
            @pl.when(ok)
            def _(peer=peer):
                pl.semaphore_signal(barrier, inc=1, device_id=peer, device_id_type=MESH)
    @pl.when((z == 0) | (z == depth - 1))
    def _(): pl.semaphore_wait(barrier, 4)
    @pl.when((z > 0) & (z < depth - 1))
    def _(): pl.semaphore_wait(barrier, 5)

    def guarded(ok, run):
        if ok is None: run()
        else: pl.when(ok)(run)

    class Item:
        pass

    def make(i):
        src, out = ins[i], outs[i]
        flat = i in late
        rows = src.shape[0]
        half = rows // 2
        (own_sem, sz, rz, sxy, rxy, sc, rc) = sems[i * 7 : (i + 1) * 7]
        def at(d, s, lo=0, n=rows):
            first = s * 2 + core if flat else d * blocks + s * 2 + core
            return out.at[pl.ds(pl.multiple_of(first * rows + lo, 16 if half % 16 == 0 else 8), n)]
        def copy(a, b, ss, rs, to):
            return pltpu.make_async_remote_copy(src_ref=a, dst_ref=b, send_sem=ss, recv_sem=rs, device_id=to, device_id_type=MESH)
        def block(d, s):
            return at(d, s)
        it = Item()
        def local():
            return pltpu.make_async_copy(src, at(dp, z), own_sem)
        def up(s, ref): return copy(ref, at(dp, s), sz.at[0, s], rz.at[s], above)
        def down(s, ref): return copy(ref, at(dp, s), sz.at[1, s], rz.at[s], below)
        def to_x(s, ref): return copy(ref, at(dp, s), sxy.at[0, s], rxy.at[0, s], by_x)
        def to_y(s, ref): return copy(ref, at(dp, s), sxy.at[1, s], rxy.at[1, s], by_y)
        def half_y(s):
            return copy(at(x_at, s, 0, half), at(x_at, s, 0, half), sxy.at[2, s], rxy.at[2, s], by_y)
        def half_x(s):
            return copy(at(y_at, s, half, half), at(y_at, s, half, half), sxy.at[3, s], rxy.at[3, s], by_x)
        def to_core(r, d, s, ref): return copy(ref, at(d, s), sc.at[r, s], rc.at[r, s], sibling)
        def spread(s, ref):
            if not flat:
                to_x(s, ref).start(); to_y(s, ref).start()
            to_core(0, dp, s, ref).start()
        def start_up():
            up(z, src).start()
        def start_down():
            down(z, src).start()
        def start():
            local().start()
            if not flat:
                guarded(z < depth - 1, start_up)
                guarded(z > 0, start_down)
            spread(z, src)
        def z_event(s, ok, rising):
            def run():
                up(s, at(dp, s)).wait_recv()
                if rising: guarded(z < depth - 1, lambda: up(s, at(dp, s)).start())
                else: guarded(z > 0, lambda: down(s, at(dp, s)).start())
                spread(s, at(dp, s))
            pl.when(ok)(run)
        def near_event(s, ok):
            def run():
                to_x(s, at(dp, s)).wait_recv()
                half_y(s).start()
                to_core(1, x_at, s, at(x_at, s)).start()
                to_y(s, at(dp, s)).wait_recv()
                half_x(s).start()
                to_core(2, y_at, s, at(y_at, s)).start()
            guarded(ok, run)
        def far_event(s, ok):
            def run():
                half_y(s).wait_recv(); half_x(s).wait_recv()
                to_core(3, far_at, s, at(far_at, s)).start()
            guarded(ok, run)
        owners = (dp,) if flat else (dp, x_at, y_at, far_at)
        def core_wait(s):
            for r, d in enumerate(owners):
                to_core(r, d, s, at(d, s)).wait_recv()
        def finish():
            local().wait()
            for s in range(depth):
                if not flat:
                    for c in (to_x(s, at(dp, s)), to_y(s, at(dp, s)), half_y(s), half_x(s)): c.wait_send()
                for r, d in enumerate(owners): to_core(r, d, s, at(d, s)).wait_send()
                guarded((z >= s) & (z < depth - 1), lambda: up(s, at(dp, s)).wait_send())
                guarded((z <= s) & (z > 0), lambda: down(s, at(dp, s)).wait_send())
        it.start_up, it.start_down = start_up, start_down
        it.start, it.z_event, it.near_event, it.far_event, it.core_wait, it.finish = start, z_event, near_event, far_event, core_wait, finish
        return it
    items = [make(i) for i in range(count)]
    def around(d):
        if d == 0: return [(z, None, True)]
        return [(z - d, z >= d, True), (z + d, z + d < depth, False)]
    for n, phase in enumerate(phases):
        its = [items[i] for i in phase]
        for it in its: it.start()
        lates = [items[i] for i in late]
        for it in lates: it.start()
        def late_sends(d):
            for it in lates:
                if d < depth - 1:
                    pl.when(z == d)(it.start_up)
                    pl.when(z == depth - 1 - d)(it.start_down)
        late_sends(0)
        for d in range(1, depth + 2):
            if d < depth:
                for s, ok, rising in around(d):
                    for it in its: it.z_event(s, ok, rising)
                late_sends(d)
            if d - 1 < depth:
                for s, ok, _ in around(d - 1):
                    for it in its: it.near_event(s, ok)
            if d > 2:
                for s, ok, rising in around(d - 2):
                    for it in lates: it.z_event(s, ok, rising)
            if d - 2 >= 0:
                for s, ok, _ in around(d - 2):
                    for it in its: it.far_event(s, ok)
    for it in items:
        for s in range(depth): it.core_wait(s)
    for it in items: it.finish()

def gather_rows(arrays, phases, cid, late=()):
    shards = lax.axis_size("dp") * lax.axis_size("expert")
    depth = lax.axis_size("expert") // 2
    D = pltpu.SemaphoreType.DMA
    sems = []
    for _ in arrays:
        sems += [D, D((2, depth)), D((depth,)), D((4, depth)), D((4, depth)), D((4, depth)), D((4, depth))]
    return pl.pallas_call(
        functools.partial(gather_kernel, phases, len(arrays), late),
        out_shape=[
            jax.ShapeDtypeStruct(((2 * depth if i in late else shards) * a.shape[0],) + a.shape[1:], a.dtype)
            for i, a in enumerate(arrays)
        ],
        in_specs=[pl.BlockSpec(memory_space=pl.ANY)] * len(arrays),
        out_specs=[pl.BlockSpec(memory_space=pl.ANY)] * len(arrays),
        scratch_shapes=sems,
        compiler_params=pltpu.CompilerParams(collective_id=cid, has_side_effects=True),
        cost_estimate=pl.CostEstimate(flops=0, bytes_accessed=400_000_000, transcendentals=0),
    )(*arrays)


def reduce_kernel(rows, cuts, a_ref, extra_ref, b_ref, g_ref, o_ref, go_ref, sib, got, own, far, near, plane, got_z,
                  s0, r0, s1, r1, s2, r2, s3, r3, g_acc, g_got, g_z, gs, gr, gsz, grz):
    dp = lax.axis_index("dp"); member = lax.axis_index("expert")
    core = member % 2; z = member // 2
    sibling = (dp, member + 1 - 2 * core)
    by_x = (dp + 1 - 2 * (dp % 2), member)
    by_y = ((dp + 2) % 4, member)
    x_at, y_at = by_x[0], by_y[0]
    far_at = 3 - dp
    half = rows // 2
    depth = lax.axis_size("expert") // 2
    barrier = pltpu.get_barrier_semaphore()
    peers = [sibling, by_x, by_y] + [(dp, ((z + d) % depth) * 2 + core) for d in range(1, depth)]
    for peer in peers:
        pl.semaphore_signal(barrier, inc=1, device_id=peer, device_id_type=MESH)
    pl.semaphore_wait(barrier, len(peers))

    def pick(table):
        at = table[depth-1]
        for i in range(depth - 1):
            at = jnp.where(z == i, table[i], at)
        return at
    orders = [[3, 3, 0, 0], [2, 0, 3, 1], [1, 2, 1, 2], [0, 1, 2, 3]]
    targets = [pick(t) for t in orders]
    cols = b_ref.shape[1] // cuts

    def copy(src, dst, ssem, rsem, to):
        return pltpu.make_async_remote_copy(src_ref=src, dst_ref=dst, send_sem=ssem, recv_sem=rsem, device_id=to, device_id_type=MESH)

    blocks = 2 * depth
    piece = (rows - HD) // 2

    def product(half_of, k, put):
        spot = targets[k] * 2 + half_of

        def step(i, _):
            shard = (i // cuts) * blocks + spot
            at = (i // cuts) * rows
            col = pl.ds(pl.multiple_of((i % cuts) * cols, cols), cols)
            part = mm(a_ref[:, pl.ds(pl.multiple_of(shard * HD, HD), HD)], b_ref[:, col], TN)
            put(pl.ds(pl.multiple_of(at, 16), HD), col, part)
            if piece:
                base = (shard // PER_KV) * (2 * HD) + (shard % PER_KV) * piece
                small = jnp.concatenate(
                    [
                        extra_ref[pl.ds(pl.multiple_of(base, 16), piece), :],
                        extra_ref[pl.ds(pl.multiple_of(base + HD, 16), piece), :],
                    ],
                    axis=0,
                )
                put(pl.ds(pl.multiple_of(at + HD, 16), 2 * piece), col, mm(small, b_ref[:, col]))
            return 0

        lax.fori_loop(0, 4 * cuts, step, 0)

    def gain_hop(i, src, to):
        return copy(src, g_got.at[i, pl.ds(0, src.shape[0])], gs.at[i], gr.at[i], to)
    hops = {}
    def gain_step(i):
        rows4 = lambda at: pl.ds(pl.multiple_of(at * 8, 8), 8)
        if i == 0:
            hops[0] = gain_hop(0, g_ref.at[pl.ds(pl.multiple_of((1 - core) * 32, 32), 32)], sibling)
        elif i == 1:
            hops[0].wait_recv()
            g_acc[...] = g_ref[pl.ds(pl.multiple_of(core * 32, 32), 32)] + g_got[0]
            hops[1] = gain_hop(1, g_acc.at[pl.ds(pl.multiple_of((1 - dp // 2) * 16, 16), 16)], by_y)
        elif i == 2:
            hops[1].wait_recv()
            mine = pl.ds(pl.multiple_of((dp // 2) * 16, 16), 16)
            g_acc[mine] += g_got[1, :16]
            hops[2] = gain_hop(2, g_acc.at[rows4(x_at)], by_x)
        elif i == 3:
            hops[2].wait_recv()
            g_acc[rows4(dp)] += g_got[2, :8]
            for d in range(1, depth):
                to = (z + d) % depth
                hops[2 + d] = copy(g_acc.at[pl.ds(dp * 8 + to, 1)], g_z.at[z], gsz.at[d - 1], grz.at[z], (dp, to * 2 + core))
        if i < 3:
            hops[i].start()
        else:
            for d in range(1, depth):
                hops[2 + d].start()
    def gain_end():
        total = g_acc[pl.ds(dp * 8 + z, 1)]
        for d in range(1, depth):
            src = (z + d) % depth
            copy(g_acc.at[pl.ds(dp * 8, 1)], g_z.at[src], gsz.at[0], grz.at[src], sibling).wait_recv()
            total += g_z[src]
        go_ref[...] = total
        for i in hops:
            hops[i].wait_send()
    sib_copies, far_copies, near_copies, z_copies = {}, {}, {}, {}
    def sib_step(k):
        slot = k % 2
        if k >= 2:
            sib_copies[k - 2].wait_send()
        def put(r, c, part):
            sib[slot, r, c] = part.astype(bf16)
        product(1 - core, k, put)
        sib_copies[k] = copy(sib.at[slot], got.at[k], s0.at[slot], r0.at[k], sibling)
        sib_copies[k].start()
    def blk(at):
        return pl.ds(pl.multiple_of(at * rows, 16), rows)
    def own_step(k):
        sib_copies[k].wait_recv()
        def put(r, c, part):
            own[k, r, c] = (part + got[k, r, c].astype(f32)).astype(bf16)
        product(core, k, put)
        base = pl.multiple_of(far_at * rows, 16)
        far_copies[k] = (
            copy(own.at[k, pl.ds(base, half)], far.at[k, 0], s1.at[k, 0], r1.at[k, 0], by_x),
            copy(own.at[k, pl.ds(pl.multiple_of(base + half, 16), half)], far.at[k, 1], s1.at[k, 1], r1.at[k, 1], by_y),
        )
        for c in far_copies[k]: c.start()
    def near_step(k):
        a, b = far_copies[k]
        a.wait_recv()
        rng = pl.ds(pl.multiple_of(y_at * rows, 16), half)
        own[k, rng] = (own[k, rng].astype(f32) + far[k, 0].astype(f32)).astype(bf16)
        to_y = copy(own.at[k, blk(y_at)], near.at[k, 1], s2.at[k, 1], r2.at[k, 1], by_y)
        to_y.start()
        b.wait_recv()
        rng = pl.ds(pl.multiple_of(x_at * rows + half, 16), half)
        own[k, rng] = (own[k, rng].astype(f32) + far[k, 1].astype(f32)).astype(bf16)
        to_x = copy(own.at[k, blk(x_at)], near.at[k, 0], s2.at[k, 0], r2.at[k, 0], by_x)
        to_x.start()
        near_copies[k] = (to_x, to_y)
    def plane_step(k):
        for c in near_copies[k]: c.wait_recv()
        total = own[k, blk(dp)].astype(f32) + near[k, 0].astype(f32) + near[k, 1].astype(f32)
        if k < depth - 1:
            plane[k] = total.astype(bf16)
            to = (dp, targets[k] * 2 + core)
            z_copies[k] = copy(plane.at[k], got_z.at[z], s3.at[k], r3.at[z], to)
            z_copies[k].start()
        else:
            o_ref[...] = total
    gain_step(0)
    sib_step(0); sib_step(1)
    own_step(0)
    gain_step(1)
    sib_step(2)
    own_step(1)
    gain_step(2)
    near_step(0)
    sib_step(3)
    own_step(2)
    gain_step(3)
    near_step(1)
    plane_step(0)
    own_step(3)
    near_step(2)
    plane_step(1)
    near_step(3)
    plane_step(2)
    plane_step(3)
    for d in range(1, depth):
        src = (z + d) % depth
        copy(plane.at[0], got_z.at[src], s3.at[0], r3.at[src], sibling).wait_recv()
        o_ref[...] += got_z[src].astype(f32)
    gain_end()
    for k in range(depth):
        if k >= 2: sib_copies[k].wait_send()
        for c in far_copies[k]: c.wait_send()
        for c in near_copies[k]: c.wait_send()
        if k < depth - 1: z_copies[k].wait_send()

def reduce_rows(a, extra, b, cid, gains=None):
    tokens, width = b.shape
    depth = 4
    rows = HD + (0 if extra is None else extra.shape[0] // 32)
    if extra is None:
        extra = jnp.zeros((16, 128), bf16)
    D = pltpu.SemaphoreType.DMA
    lanes = 256
    padded = jnp.zeros((32, lanes), f32)
    if gains is not None:
        padded = jnp.pad(gains, ((0, 0), (0, lanes - gains.shape[1])))
    padded = padded.reshape(4, depth, 2, lanes).transpose(2, 0, 1, 3)
    padded = jnp.pad(padded, ((0, 0), (0, 0), (0, 8 - depth), (0, 0))).reshape(64, lanes)
    return pl.pallas_call(
        functools.partial(reduce_kernel, rows, 4),
        out_shape=[jax.ShapeDtypeStruct((rows, width), f32), jax.ShapeDtypeStruct((1, lanes), f32)],
        in_specs=[pl.BlockSpec(memory_space=pltpu.VMEM)] * 4,
        out_specs=[pl.BlockSpec(memory_space=pltpu.VMEM)] * 2,
        scratch_shapes=[
            pltpu.VMEM((2, 4 * rows, width), bf16),
            pltpu.VMEM((depth, 4 * rows, width), bf16),
            pltpu.VMEM((depth, 4 * rows, width), bf16),
            pltpu.VMEM((depth, 2, rows // 2, width), bf16),
            pltpu.VMEM((depth, 2, rows, width), bf16),
            pltpu.VMEM((depth - 1, rows, width), bf16),
            pltpu.VMEM((depth, rows, width), bf16),
            D((2,)), D((depth,)), D((depth, 2)), D((depth, 2)), D((depth, 2)), D((depth, 2)), D((depth - 1,)), D((depth,)),
            pltpu.VMEM((32, lanes), f32), pltpu.VMEM((3, 32, lanes), f32), pltpu.VMEM((depth, 1, lanes), f32),
            D((3,)), D((3,)), D((depth - 1,)), D((depth,)),
        ],
        compiler_params=pltpu.CompilerParams(vmem_limit_bytes=60*1024*1024, collective_id=cid, has_side_effects=True),
        cost_estimate=pl.CostEstimate(flops=2*tokens*32*rows*width, bytes_accessed=10_000_000, transcendentals=0),
    )(a, extra, b, padded)


ROUTE_LANES = 128


def picks_of(routing, first, local_experts, capacity):
    rows = routing.shape[0]
    lanes = lax.broadcasted_iota(jnp.int32, (rows, ROUTE_LANES), 1)
    places = lax.broadcasted_iota(jnp.int32, (rows, local_experts * capacity), 1)
    hit, weighted = None, 0.0
    for e in range(local_experts):

        def column(base):
            return jnp.sum(jnp.where(lanes == base + first + e, routing, 0.0), axis=1, keepdims=True)

        slot = column(0).astype(jnp.int32)
        here = places == jnp.where(slot >= 0, slot + e * capacity, -1)
        hit = here if hit is None else hit | here
        weighted = weighted + jnp.where(here, column(32) + column(64), 0.0)
    return jnp.where(hit, 1.0, 0.0).astype(bf16), weighted.astype(bf16)


def pick_kernel(capacity, local_experts, n_alias, tok_ref, cot_ref, *refs):
    x_ref, dy_ref = refs[n_alias:]
    width = cot_ref.shape[3]
    first = lax.axis_index("expert") * local_experts
    routing = tok_ref[0, :, width:]
    hit, _ = picks_of(routing.astype(f32), first, local_experts, capacity)
    x = mm(hit, tok_ref[0, :, :width], TN).astype(bf16)
    rows = mm(hit, routing, TN)
    lanes = lax.broadcasted_iota(jnp.int32, rows.shape, 1)
    owner = lax.broadcasted_iota(jnp.int32, rows.shape, 0) // capacity
    at = lanes - first - owner
    weight = jnp.sum(jnp.where((at == 32) | (at == 64), rows, 0.0), axis=1, keepdims=True)
    dy = (mm(hit, cot_ref[0, 0], TN) * weight).astype(bf16)
    for e in range(local_experts):
        x_ref[e, 0, 0] = x[e * capacity : (e + 1) * capacity]
        dy_ref[e, 0, 0] = dy[e * capacity : (e + 1) * capacity]


def expert_kernel(n_alias, *refs):
    x_ref, dy_ref = refs[:2]
    parts = (refs[2:7], refs[7:12], refs[12:17])
    z_ref, dg_ref, du_ref, y_ref, dx_ref, wg, wu, wd, sems = refs[17 + n_alias :]
    local_experts, width, _ = wg.shape
    at = lax.axis_index("dp")
    size = width // 4
    places = (at, at + 1 - 2 * (at % 2), (at + 2) % 4, 3 - at, 3 - at)

    def copies(e):
        out = []
        for m, full in enumerate((wg, wu, wd)):
            for p in range(4):
                part = parts[m][p] if p < 3 else parts[m][3 + e]
                src = part.at[e] if p < 3 else part.at[0]
                where = pl.ds(pl.multiple_of(places[p] * size, size), size)
                dst = full.at[e, where, :] if m < 2 else full.at[e, :, where]
                out.append(pltpu.make_async_copy(src, dst, sems.at[e, m, p]))
        return out

    expert, chunk = pl.program_id(0), pl.program_id(1)

    @pl.when((expert == 0) & (chunk == 0))
    def _():
        for e in range(local_experts):
            for c in copies(e):
                c.start()

    for e in range(local_experts):

        @pl.when((expert == e) & (chunk == 0))
        def _(e=e):
            for c in copies(e):
                c.wait()

    x, dy = x_ref[0, 0], dy_ref[0, 0]
    gate = mm(x, wg[expert])
    up = mm(x, wu[expert])
    d_hidden = mm(dy, wd[expert], NT)
    sig = 1.0 / (1.0 + jnp.exp(-gate))
    silu = gate * sig
    z = (silu * up).astype(bf16)
    d_gate = (d_hidden * up * sig * (1.0 + gate * (1.0 - sig))).astype(bf16)
    d_up = (d_hidden * silu).astype(bf16)
    z_ref[0, 0] = z
    dg_ref[0, 0] = d_gate
    du_ref[0, 0] = d_up
    dx_ref[0] = (mm(d_gate, wg[expert], NT) + mm(d_up, wu[expert], NT)).astype(bf16)
    y_ref[0] = mm(z, wd[expert]).astype(bf16)


def sum_kernel(capacity, routing_ref, y_ref, dx_ref, mix_ref, da_ref):
    local_experts, _, _, width = y_ref.shape
    first = lax.axis_index("expert") * local_experts
    hit, weighted = picks_of(routing_ref[0].astype(f32), first, local_experts, capacity)
    da_ref[...] = mm(hit, dx_ref[...].reshape(local_experts * capacity, width)).astype(bf16)
    mix_ref[...] = mm(weighted, y_ref[...].reshape(local_experts * capacity, width)).astype(bf16)


def run_experts(tokens, cot, parts, capacity, batch_at, micro, earlier):
    blocks, _, rows, width = cot.shape
    local_experts, _, hidden = parts[0][0].shape
    flat = [p for group in parts for p in group]
    any_spec = pl.BlockSpec(memory_space=pl.ANY)
    params = pltpu.CompilerParams(vmem_limit_bytes=VMEM_LIMIT)
    slots = blocks * capacity
    picked_spec = pl.BlockSpec((local_experts, 1, 1, capacity, width), lambda b: (0, batch_at, b, 0, 0))
    picked = jax.ShapeDtypeStruct((local_experts, micro, blocks, capacity, width), bf16)
    x, dy = pl.pallas_call(
        functools.partial(pick_kernel, capacity, local_experts, len(earlier[:2])),
        grid=(blocks,),
        in_specs=[
            pl.BlockSpec((1, rows, tokens.shape[2]), lambda b: (b, 0, 0)),
            pl.BlockSpec((1, 1, rows, width), lambda b: (b, 0, 0, 0)),
        ]
        + [any_spec] * len(earlier[:2]),
        out_specs=[picked_spec] * 2,
        out_shape=[picked] * 2,
        input_output_aliases={2 + i: i for i in range(len(earlier[:2]))},
        compiler_params=params,
        cost_estimate=pl.CostEstimate(
            flops=4 * slots * local_experts * rows * width, bytes_accessed=25_000_000, transcendentals=0
        ),
    )(tokens, cot, *[a.reshape(picked.shape) for a in earlier[:2]])
    x, dy = (a.reshape(local_experts, micro, slots, width) for a in (x, dy))
    chunk = slots // 2
    row_spec = pl.BlockSpec((1, 1, chunk, width), lambda e, i: (e, batch_at, i, 0))
    hid_spec = pl.BlockSpec((1, 1, chunk, hidden), lambda e, i: (e, batch_at, i, 0))
    out_spec = pl.BlockSpec((1, chunk, width), lambda e, i: (e, i, 0))
    hid = jax.ShapeDtypeStruct((local_experts, micro, slots, hidden), bf16)
    out = jax.ShapeDtypeStruct((local_experts, slots, width), bf16)
    z, dg, du, y, dx = pl.pallas_call(
        functools.partial(expert_kernel, len(earlier[2:])),
        grid=(local_experts, 2),
        in_specs=[row_spec, row_spec] + [any_spec] * (len(flat) + len(earlier[2:])),
        out_specs=[hid_spec] * 3 + [out_spec] * 2,
        out_shape=[hid] * 3 + [out] * 2,
        input_output_aliases={2 + len(flat) + i: i for i in range(len(earlier[2:]))},
        scratch_shapes=[
            pltpu.VMEM((local_experts, width, hidden), bf16),
            pltpu.VMEM((local_experts, width, hidden), bf16),
            pltpu.VMEM((local_experts, hidden, width), bf16),
            pltpu.SemaphoreType.DMA((local_experts, 3, 4)),
        ],
        compiler_params=params,
        cost_estimate=pl.CostEstimate(
            flops=12 * local_experts * slots * width * hidden, bytes_accessed=50_000_000, transcendentals=0
        ),
    )(x, dy, *flat, *earlier[2:])
    y, dx = (a.reshape(local_experts, blocks, capacity, width) for a in (y, dx))
    part_spec = pl.BlockSpec((local_experts, 1, capacity, width), lambda b: (0, b, 0, 0))
    sums = jax.ShapeDtypeStruct((blocks * rows, width), bf16)
    sums_spec = pl.BlockSpec((rows, width), lambda b: (b, 0))
    mix, da = pl.pallas_call(
        functools.partial(sum_kernel, capacity),
        grid=(blocks,),
        in_specs=[
            pl.BlockSpec((1, rows, ROUTE_LANES), lambda b: (b, 0, width // ROUTE_LANES)),
            part_spec,
            part_spec,
        ],
        out_specs=[sums_spec] * 2,
        out_shape=[sums] * 2,
        compiler_params=params,
        cost_estimate=pl.CostEstimate(
            flops=4 * slots * local_experts * rows * width, bytes_accessed=25_000_000, transcendentals=0
        ),
    )(tokens, y, dx)
    return [x, dy, z, dg, du], mix, da


def slots_of(route_ids, gate_vals, ranking, capacity, experts):
    rows = route_ids.shape[0]
    pair_experts = route_ids.reshape(-1)
    earlier = (pair_experts[None, :] == pair_experts[:, None]) & (
        ranking[None, :] < ranking[:, None]
    )
    slot = jnp.sum(earlier.astype(jnp.int32), axis=1).reshape(rows, -1)
    kept = slot < capacity
    chosen = route_ids[:, :, None] == jnp.arange(experts, dtype=jnp.int32)[None, None, :]
    chosen = chosen & kept[:, :, None]
    slot_map = jnp.sum(jnp.where(chosen, slot[:, :, None] + 1, 0), axis=1).astype(f32) - 1.0
    weight_map = jnp.sum(jnp.where(chosen, gate_vals[:, :, None], 0.0), axis=1)
    return slot_map, weight_map


def swap(values, bit):
    return lax.ppermute(values, "dp", [(i, i ^ bit) for i in range(lax.axis_size("dp"))])


def scatter_far(total, axis):
    at = lax.axis_index("dp")
    size = total.shape[axis] // 4

    def part(bits, expert):
        start, sizes = [expert, 0, 0], list(total.shape)
        start[axis] = (at ^ bits) * size
        sizes[0], sizes[axis] = 1, size
        return lax.dynamic_slice(total, start, sizes)

    return [
        swap(part(3, 0), 1),
        swap(part(3, 1), 2),
        part(1, 0),
        part(2, 1),
        part(2, 0),
        part(1, 1),
        lax.dynamic_slice_in_dim(total, at * size, size, axis=axis),
    ]


def scatter_near(for_y, for_x, by_x, by_y, near_y, near_x, own):
    by_x, by_y = swap(by_x, 1), swap(by_y, 2)
    near_y = swap((near_y.astype(f32) + for_y.astype(f32)).astype(bf16), 2)
    near_x = swap((near_x.astype(f32) + for_x.astype(f32)).astype(bf16), 1)
    return (by_x, by_y, near_y, near_x, own)


def scatter_sum(by_x, by_y, near_y, near_x, own):
    by_x = jnp.concatenate([by_x, near_x], axis=0).astype(f32)
    by_y = jnp.concatenate([near_y, by_y], axis=0).astype(f32)
    return own.astype(f32) + by_x + by_y


def body_plain(
    inputs,
    cotangent,
    membership,
    routes,
    gate_weights,
    pair_order,
    w_query,
    w_key,
    w_value,
    w_output,
    norm_gains,
    w_gate,
    w_up,
    w_down,
):
    micro = inputs.shape[0]
    rows = inputs.shape[2]
    width = inputs.shape[3]
    group_len = membership.shape[2]
    member = lax.axis_index("expert")
    blocks = lax.axis_size("expert")
    shards = blocks * lax.axis_size("dp")
    shard_at = lax.axis_index("dp") * blocks + member
    local_experts = w_gate.shape[0]
    experts = local_experts * blocks
    capacity = rows * TOPK // experts
    step_heads = max(1, 384 // rows)
    total = micro * rows
    q_part, k_part, v_part = w_query.shape[1], w_key.shape[1], w_value.shape[1]

    gain_len = norm_gains.shape[0]
    gain_shard = jnp.zeros((2048,), bf16).at[:gain_len].set(norm_gains).reshape(16, 128)
    gain_full = lax.all_gather(gain_shard, BOTH, axis=0, tiled=True)
    gains = gain_full.reshape(shards, 2048)[:, :gain_len].reshape(-1).astype(f32)
    gain_in = gains[:width]
    gain_mid = gains[width : 2 * width]
    gain_q = gains[2 * width : 2 * width + HD]
    gain_k = gains[2 * width + HD :]

    qkv_w = lax.all_gather(
        jnp.concatenate([w_query.T, w_key.T, w_value.T], axis=0), BOTH, axis=0, tiled=True
    )
    out_w = lax.all_gather(w_output, BOTH, axis=0, tiled=True)
    wg = lax.all_gather(w_gate, "dp", axis=1, tiled=True)
    wu = lax.all_gather(w_up, "dp", axis=1, tiled=True)
    wd = lax.all_gather(w_down, "dp", axis=2, tiled=True)

    slot_map, weight_map = jax.vmap(
        lambda r, g, o: slots_of(r, g, o, capacity, experts)
    )(routes[:, 0], gate_weights[:, 0], pair_order[:, 0, 0])
    routing = jnp.concatenate([slot_map, weight_map], axis=-1)
    routing = lax.all_gather(routing, "expert", axis=0, tiled=False)
    mine = member * local_experts
    slot_mine = lax.dynamic_slice_in_dim(routing, mine, local_experts, axis=3)
    weight_mine = lax.dynamic_slice_in_dim(routing, experts + mine, local_experts, axis=3)
    slot_mine = jnp.transpose(slot_mine, (1, 3, 0, 2))
    weight_mine = jnp.transpose(weight_mine, (1, 3, 0, 2))
    slot_ids = jnp.arange(capacity, dtype=f32)
    hit = slot_mine[:, :, :, None, :] == slot_ids[None, None, None, :, None]
    pick = hit.astype(bf16)
    weighted = jnp.where(hit, weight_mine[:, :, :, None, :], 0.0)
    slot_weight = jnp.sum(weighted, axis=-1)
    weighted = weighted.astype(bf16)

    key_index = jnp.arange(group_len, dtype=jnp.int32)
    start_row = member * rows
    segment = membership[:, 0]
    row_index = start_row + jnp.arange(rows, dtype=jnp.int32)
    seg_rows = lax.dynamic_slice_in_dim(segment, start_row, rows, axis=1)
    before = jnp.sum((segment[:, None, :] < seg_rows[:, :, None]).astype(jnp.int32), axis=2)
    position = jnp.where(seg_rows == 0, row_index[None], PROMPT + row_index[None] - before)
    allowed = (key_index[None, :, None] <= row_index[None, None, :]) & (
        (segment[:, :, None] == 0) | (segment[:, :, None] == seg_rows[:, None, :])
    )
    bias = jnp.tile(jnp.where(allowed, 0.0, MASKED).astype(f32), (1, 1, step_heads))
    frequency = ROPE_BASE ** (-(jnp.arange(HD // 2, dtype=f32) * 2.0 / HD))
    angles = position.astype(f32).reshape(total)[:, None] * frequency[None, :]
    cosine = jnp.cos(angles)[:, None, :]
    sine_part = jnp.sin(angles)[:, None, :]

    hidden = inputs[:, 0].astype(f32).reshape(total, width)
    scale_in = rms_scale(hidden)
    normed = (hidden * scale_in * gain_in).astype(bf16)
    proj = mm(normed, qkv_w, NT).reshape(total, shards, q_part + k_part + v_part)
    queries = proj[:, :, :q_part].reshape(total, H, HD)
    key_pre = proj[:, :, q_part : q_part + k_part].reshape(total, KVH, HD)
    value = proj[:, :, q_part + k_part :].reshape(total, KVH, HD).astype(bf16)
    scale_q = rms_scale(queries)
    scale_k = rms_scale(key_pre)
    q_low = rotate(queries * scale_q * (gain_q * (SCALE * LOG2E)), cosine, sine_part).astype(bf16)
    q_low = q_low.reshape(micro, rows, H * HD)
    k_low = rotate(key_pre * scale_k * gain_k, cosine, sine_part).astype(bf16)
    kv_own = jnp.concatenate([k_low, value], axis=-1).reshape(micro, rows, KVH * 2 * HD)
    kv_all = lax.all_gather(kv_own, "expert", axis=0, tiled=False)
    chunk = 256
    mixed = []
    for at in range(micro):
        mixed = run_forward(q_low, kv_all[:, at : at + 1], bias, step_heads, chunk, at, mixed)
    mixed, logs = mixed

    branch = mm(mixed.reshape(total, H * HD), out_w)
    middle = hidden + branch
    scale_mid = rms_scale(middle)
    routed = (middle * scale_mid * gain_mid).astype(bf16).reshape(micro, rows, width)
    middle = middle.reshape(micro, rows, width)
    scale_mid = scale_mid.reshape(micro, rows, 1)

    outputs, d_branches, d_middles = [], [], []
    acc_gate = acc_up = acc_down = 0.0
    grad_mid = 0.0
    slots = blocks * capacity
    for at in range(micro):
        d_out = lax.all_gather(cotangent[at, 0], "expert", axis=0, tiled=False)
        tokens = lax.all_gather(routed[at], "expert", axis=0, tiled=False)
        picked = jnp.einsum("ebst,btd->ebsd", pick[at], tokens, preferred_element_type=f32)
        picked = picked.astype(bf16).reshape(local_experts, slots, width)
        d_result = jnp.einsum("ebst,btd->ebsd", pick[at], d_out, preferred_element_type=f32)
        d_result = (d_result * slot_weight[at][..., None]).astype(bf16)
        d_result = d_result.reshape(local_experts, slots, width)
        gate_pre = jnp.einsum("erd,edf->erf", picked, wg, preferred_element_type=f32)
        up_pre = jnp.einsum("erd,edf->erf", picked, wu, preferred_element_type=f32)
        d_hidden = jnp.einsum("erd,efd->erf", d_result, wd, preferred_element_type=f32)
        sigmoid_g = jax.nn.sigmoid(gate_pre)
        silu_g = gate_pre * sigmoid_g
        hidden_low = (silu_g * up_pre).astype(bf16)
        d_gate = (d_hidden * up_pre * sigmoid_g * (1.0 + gate_pre * (1.0 - sigmoid_g))).astype(bf16)
        d_up = (d_hidden * silu_g).astype(bf16)
        d_rows = jnp.einsum("erf,edf->erd", d_gate, wg, preferred_element_type=f32)
        d_rows = d_rows + jnp.einsum("erf,edf->erd", d_up, wu, preferred_element_type=f32)
        d_rows = d_rows.astype(bf16).reshape(local_experts, blocks, capacity, width)
        d_part = jnp.einsum("ebst,ebsd->btd", pick[at], d_rows, preferred_element_type=f32)
        d_part = d_part.astype(bf16).reshape(group_len, width)
        d_routed = lax.psum_scatter(d_part, "expert", scatter_dimension=0, tiled=True).astype(f32)
        result = jnp.einsum("erf,efd->erd", hidden_low, wd, preferred_element_type=f32)
        result = result.astype(bf16).reshape(local_experts, blocks, capacity, width)
        part = jnp.einsum("ebst,ebsd->btd", weighted[at], result, preferred_element_type=f32)
        part = part.astype(bf16).reshape(group_len, width)
        expert_mix = lax.psum_scatter(part, "expert", scatter_dimension=0, tiled=True).astype(f32)
        outputs.append((middle[at] + expert_mix).astype(bf16))

        acc_down += jnp.einsum("erf,erd->efd", hidden_low, d_result, preferred_element_type=f32)
        acc_gate += jnp.einsum("erd,erf->edf", picked, d_gate, preferred_element_type=f32)
        acc_up += jnp.einsum("erd,erf->edf", picked, d_up, preferred_element_type=f32)

        d_mid_norm, mid_gain_grad = norm_back(d_routed, middle[at], scale_mid[at], gain_mid)
        grad_mid = grad_mid + mid_gain_grad
        d_middle = cotangent[at, 0].astype(f32) + d_mid_norm
        d_middles.append(d_middle)
        d_branches.append(d_middle.astype(bf16))

    grad_gate = lax.psum_scatter(acc_gate.astype(bf16), "dp", scatter_dimension=1, tiled=True)
    grad_up = lax.psum_scatter(acc_up.astype(bf16), "dp", scatter_dimension=1, tiled=True)
    grad_down = lax.psum_scatter(acc_down.astype(bf16), "dp", scatter_dimension=2, tiled=True)

    d_branch = jnp.concatenate(d_branches, axis=0)
    d_middle = jnp.concatenate(d_middles, axis=0)
    grad_output = mm(mixed.reshape(total, H * HD), d_branch, TN).astype(bf16)
    grad_output = lax.psum_scatter(grad_output, BOTH, scatter_dimension=0, tiled=True)
    d_mixed = mm(d_branch, out_w, NT).astype(bf16).reshape(micro, rows, H * HD)
    cos_rows = jnp.concatenate([cosine, cosine], axis=-1).reshape(micro, rows, HD)
    sine_rows = jnp.concatenate([-sine_part, sine_part], axis=-1).reshape(micro, rows, HD)
    q_raw = queries.reshape(micro, rows, H * HD)
    d_query, dkv_list, grad_qn = [], [], 0.0
    for at in range(micro):
        d_query, dkv_one, part = run_backward(
            q_low, kv_all[:, at : at + 1], bias, mixed, d_mixed, logs, q_raw, cos_rows, sine_rows,
            gain_q[None, :], step_heads, chunk, at, [d_query] if at else []
        )
        dkv_list.append(dkv_one)
        grad_qn += part[0]
    dkv_all = jnp.concatenate(dkv_list, axis=1)
    dkv = lax.psum_scatter(dkv_all, "expert", scatter_dimension=0, tiled=False)
    dkv = dkv.reshape(total, KVH, 2 * HD)
    d_key = rotate(dkv[:, :, :HD].astype(f32), cosine, -sine_part)
    d_key, grad_kn = norm_back(d_key, key_pre, scale_k, gain_k)
    d_proj = jnp.concatenate(
        [
            d_query.reshape(total, shards, q_part),
            d_key.astype(bf16).reshape(total, shards, k_part),
            dkv[:, :, HD:].reshape(total, shards, v_part),
        ],
        axis=-1,
    ).reshape(total, -1)
    grad_qkv = mm(d_proj, normed, TN).astype(bf16)
    grad_qkv = lax.psum_scatter(grad_qkv, BOTH, scatter_dimension=0, tiled=True).astype(f32)
    d_normed = mm(d_proj, qkv_w)
    d_in_norm, grad_in = norm_back(d_normed, hidden, scale_in, gain_in)
    input_grad = d_middle + d_in_norm

    gain_grads = jnp.concatenate([grad_in, grad_mid, grad_qn, grad_kn]).reshape(shards, gain_len)
    gain_grads = jnp.pad(gain_grads, ((0, 0), (0, 256 - gain_len % 256)))
    gain_all = lax.all_gather(gain_grads, BOTH, axis=0, tiled=False)
    grad_gains = jnp.sum(lax.dynamic_index_in_dim(gain_all, shard_at, axis=1, keepdims=False), axis=0)
    return (
        jnp.stack(outputs)[:, None],
        input_grad.reshape(micro, 1, rows, width),
        grad_qkv[:q_part].T,
        grad_qkv[q_part : q_part + k_part].T,
        grad_qkv[q_part + k_part :].T,
        grad_output.astype(f32),
        grad_gains[:gain_len],
        grad_gate.astype(f32),
        grad_up.astype(f32),
        grad_down.astype(f32),
    )


def body_fast(
    inputs,
    cotangent,
    membership,
    routes,
    gate_weights,
    pair_order,
    w_query,
    w_key,
    w_value,
    w_output,
    norm_gains,
    w_gate,
    w_up,
    w_down,
):
    micro = inputs.shape[0]
    rows = inputs.shape[2]
    width = inputs.shape[3]
    group_len = membership.shape[2]
    member = lax.axis_index("expert")
    blocks = lax.axis_size("expert")
    shards = blocks * lax.axis_size("dp")
    local_experts = w_gate.shape[0]
    experts = local_experts * blocks
    capacity = rows * TOPK // experts
    step_heads = max(1, 384 // rows)
    total = micro * rows
    q_part, k_part, v_part = w_query.shape[1], w_key.shape[1], w_value.shape[1]
    tie = lax.optimization_barrier

    slot_map, weight_map = jax.vmap(
        lambda r, g, o: slots_of(r, g, o, capacity, experts)
    )(routes[:, 0], gate_weights[:, 0], pair_order[:, 0, 0])
    weight_high = tie(weight_map.astype(bf16))
    weight_low = (weight_map - weight_high.astype(f32)).astype(bf16)

    def padded(values, lanes):
        return jnp.pad(values, ((0, 0), (0, 0), (0, lanes - experts)))

    routing = jnp.concatenate(
        [
            padded(slot_map.astype(bf16), 32),
            padded(weight_high, 32),
            padded(weight_low, ROUTE_LANES - 64),
        ],
        axis=-1,
    )

    gain_len = norm_gains.shape[0]
    gain_shard = jnp.zeros((2048,), bf16).at[:gain_len].set(norm_gains).reshape(16, 128)
    kv_w = jnp.concatenate([w_key.T, w_value.T], axis=0)
    q_w, kv_w, out_w, gain_full, cot_0 = gather_rows(
        [w_query.T, kv_w, w_output, gain_shard, cotangent[0, 0]], [(3, 0, 1, 2)], 1, (4,)
    )
    cot_0 = cot_0.reshape(blocks, 1, rows, width)
    q_w, w_gate, w_up, w_down = tie((q_w, w_gate, w_up, w_down))
    gains = gain_full.reshape(shards, 2048)[:, :gain_len].reshape(-1).astype(f32)
    gain_in = gains[:width]
    gain_mid = gains[width : 2 * width]
    gain_q = gains[2 * width : 2 * width + HD]
    gain_k = gains[2 * width + HD :]
    gate_near, up_near, down_near = ((swap(w, 1), swap(w, 2)) for w in (w_gate, w_up, w_down))

    key_index = jnp.arange(group_len, dtype=jnp.int32)
    start_row = member * rows
    segment = membership[:, 0]
    row_index = start_row + jnp.arange(rows, dtype=jnp.int32)
    seg_rows = lax.dynamic_slice_in_dim(segment, start_row, rows, axis=1)
    before = jnp.sum((segment[:, None, :] < seg_rows[:, :, None]).astype(jnp.int32), axis=2)
    position = jnp.where(seg_rows == 0, row_index[None], PROMPT + row_index[None] - before)
    allowed = (key_index[None, :, None] <= row_index[None, None, :]) & (
        (segment[:, :, None] == 0) | (segment[:, :, None] == seg_rows[:, None, :])
    )
    bias = jnp.tile(jnp.where(allowed, 0.0, MASKED).astype(f32), (1, 1, step_heads))
    frequency = ROPE_BASE ** (-(jnp.arange(HD // 2, dtype=f32) * 2.0 / HD))
    angles = position.astype(f32).reshape(total)[:, None] * frequency[None, :]
    cosine, sine = jnp.cos(angles), jnp.sin(angles)
    cosine = jnp.concatenate([cosine, cosine], axis=-1)
    sine = jnp.concatenate([-sine, sine], axis=-1)
    gain_q, gain_k = gain_q[None, :], gain_k[None, :]

    hidden = inputs[:, 0].astype(f32).reshape(total, width)
    scale_in = rms_scale(hidden)
    normed = (hidden * scale_in * gain_in).astype(bf16)
    q_low, q_raw, kv_own, k_raw, kv_w = run_project(
        normed, q_w, kv_w, cosine, sine, gain_q * (SCALE * LOG2E), gain_k
    )
    q_low, q_raw = (a.reshape(micro, rows, H * HD) for a in (q_low, q_raw))
    kv_own = kv_own.reshape(micro, rows, KVH * 2 * HD)
    kv_0 = lax.all_gather(kv_own[0], "expert", axis=0, tiled=False)
    kv_1 = lax.all_gather(kv_own[1], "expert", axis=0, tiled=False)
    kv_0, gate_near = tie((kv_0, gate_near))
    kv_1, cot_1 = tie((kv_1, cotangent[1, 0]))
    cot_1 = lax.all_gather(cot_1, "expert", axis=0, tiled=False)
    kv_all = [kv_0[:, None], kv_1[:, None]]
    cots = [cot_0, cot_1[:, None]]
    chunk = 256
    mixed = run_forward(q_low, kv_all[0], bias, step_heads, chunk, 0, [])
    mixed, kv_all = tie((mixed, kv_all))
    mixed, logs = run_forward(q_low, kv_all[1], bias, step_heads, chunk, 1, mixed)
    mixed, up_near, down_near = tie((mixed, up_near, down_near))
    parts = [
        (own, near[0], near[1], swap(near[0][:1], 2), swap(near[1][1:], 1))
        for own, near in ((w_gate, gate_near), (w_up, up_near), (w_down, down_near))
    ]

    branch = mm(mixed.reshape(total, H * HD), out_w)
    middle = hidden + branch
    scale_mid = rms_scale(middle)
    routed = (middle * scale_mid * gain_mid).astype(bf16).reshape(micro, rows, width)
    routed = jnp.concatenate([routed, routing], axis=-1)
    routed, cots[1] = tie((routed, cots[1]))
    middle = middle.reshape(micro, rows, width)
    scale_mid = scale_mid.reshape(micro, rows, 1)

    mix_parts, d_routeds = [], []
    kept = []
    for at in range(micro):
        tokens = lax.all_gather(routed[at], "expert", axis=0, tiled=False)
        tokens, parts = tie((tokens, parts))
        kept, mix, d_part = run_experts(tokens, cots[at], parts, capacity, at, micro, kept)
        kept, d_part, mix, d_routeds = tie((kept, d_part, mix, d_routeds))
        mix_parts.append(mix)
        d_routed = lax.psum_scatter(d_part, "expert", scatter_dimension=0, tiled=True)
        d_routeds.append(d_routed)
    picked, d_result, hidden_low, d_gate, d_up = (
        a.reshape(local_experts, -1, a.shape[-1]) for a in kept
    )

    def weight_grad(rows_in, rows_out):
        return jnp.einsum("era,erb->eab", rows_in, rows_out, preferred_element_type=f32).astype(bf16)

    first = scatter_far(weight_grad(picked, d_gate), 1)
    second = scatter_far(weight_grad(picked, d_up), 1)
    first, hidden_low = tie((first, hidden_low))
    first = scatter_near(*first)
    third = scatter_far(weight_grad(hidden_low, d_result), 2)
    d_routeds[-1], second, mix_parts[0] = tie((d_routeds[-1], second, mix_parts[0]))
    second = scatter_near(*second)
    d_mixed, d_middle, d_branch, grad_mid = run_middle_back(
        d_routeds, middle, cotangent[:, 0], gain_mid[None, :], out_w
    )
    d_mixed, d_branch, first, third = tie((d_mixed, d_branch, first, third))
    third = scatter_near(*third)
    d_mixed = d_mixed.reshape(micro, rows, H * HD)
    cos_rows, sine_rows = (a.reshape(micro, rows, HD) for a in (cosine, sine))
    heads = mixed.reshape(total, 4, 2, 2, 2, HD)

    def share(core):
        part = lax.dynamic_index_in_dim(heads, core, axis=4, keepdims=False)
        return part.transpose(0, 2, 1, 3, 4).reshape(total, -1)

    core = member % 2
    pairs = [(i, i ^ 1) for i in range(blocks)]
    got = lax.ppermute(mm(share(1 - core), d_branch, TN).astype(bf16), "expert", pairs)
    mixes = [lax.psum_scatter(mix_parts[0], "expert", scatter_dimension=0, tiled=True)]

    def backward(at, earlier):
        d_query, dkv_one, part = run_backward(
            q_low, kv_all[at], bias, mixed, d_mixed, logs, q_raw, cos_rows, sine_rows, gain_q,
            step_heads, chunk, at, earlier
        )
        return d_query, dkv_one[:, 0], part

    d_query, dkv_0, gain_0 = backward(0, [])
    d_query, dkv_0, got, second = tie((d_query, dkv_0, got, second))
    dkv_0 = lax.psum_scatter(dkv_0, "expert", scatter_dimension=0, tiled=False)
    out_grad = tie(mm(share(core), d_branch, TN).astype(bf16))
    out_grad = (out_grad.astype(f32) + got.astype(f32)).astype(bf16)
    d_query, out_grad = tie((d_query, out_grad))
    out_grad = scatter_far(out_grad.reshape(2, -1, width), 1)
    d_query, dkv_1, gain_1 = backward(1, [d_query])
    grad_qn = gain_0 + gain_1
    d_query, dkv_1, out_grad, mixes, third = tie((d_query, dkv_1, out_grad, mixes, third))
    dkv_1 = lax.psum_scatter(dkv_1, "expert", scatter_dimension=0, tiled=False)
    out_grad = scatter_sum(*scatter_near(*out_grad)).astype(bf16).reshape(-1, width)
    d_query = d_query.reshape(total, H * HD)
    dkv = jnp.concatenate([dkv_0, dkv_1], axis=0)
    dkv = dkv.reshape(total, KVH * 2 * HD)
    mix_part, dkv = tie((mix_parts[1], dkv))
    mixes.append(lax.psum_scatter(mix_part, "expert", scatter_dimension=0, tiled=True))
    outputs = [(middle[at] + mixes[at].astype(f32)).astype(bf16) for at in range(micro)]
    dkv, dkv_t, grad_kn = run_key_back(dkv, k_raw, cosine, sine, gain_k)
    dkv, out_grad = tie((dkv, out_grad))
    d_normed = mm(d_query, q_w) + mm(dkv, kv_w)
    grad_output = lax.psum_scatter(
        out_grad,
        "expert",
        scatter_dimension=0,
        tiled=True,
        axis_index_groups=[list(range(c, blocks, 2)) for c in range(2)],
    ).astype(f32)
    d_in_norm, grad_in = norm_back(d_normed, hidden, scale_in, gain_in)
    input_grad = d_middle + d_in_norm
    gain_grads = jnp.concatenate([grad_in, grad_mid[0], grad_qn[0], grad_kn[0]]).reshape(shards, gain_len)
    grad_qkv, grad_gains = reduce_rows(d_query, dkv_t, normed, 3, gain_grads)
    expert_grads = [scatter_sum(*pieces) for pieces in (first, second, third)]
    return (
        jnp.stack(outputs)[:, None],
        input_grad.reshape(micro, 1, rows, width),
        grad_qkv[:q_part].T,
        grad_qkv[q_part : q_part + k_part].T,
        grad_qkv[q_part + k_part :].T,
        grad_output,
        grad_gains[0, :gain_len],
        *expert_grads,
    )


def solution(mesh):
    fast = mesh.shape["dp"] == 4 and mesh.shape["expert"] == 8
    return jax.shard_map(
        body_fast if fast else body_plain,
        mesh=mesh,
        in_specs=(
            P(None, "dp", "expert", None),
            P(None, "dp", "expert", None),
            P(None, "dp", None),
            P(None, "dp", "expert", None),
            P(None, "dp", "expert", None),
            P(None, "dp", "expert", None),
            P(None, ("dp", "expert")),
            P(None, ("dp", "expert")),
            P(None, ("dp", "expert")),
            P(("dp", "expert"), None),
            P(("dp", "expert")),
            P("expert", "dp", None),
            P("expert", "dp", None),
            P("expert", None, "dp"),
        ),
        out_specs=(
            P(None, "dp", "expert", None),
            P(None, "dp", "expert", None),
            P(None, ("dp", "expert")),
            P(None, ("dp", "expert")),
            P(None, ("dp", "expert")),
            P(("dp", "expert"), None),
            P(("dp", "expert")),
            P("expert", "dp", None),
            P("expert", "dp", None),
            P("expert", None, "dp"),
        ),
        check_vma=False,
    )
```

```python
import functools
import math

import jax
import jax.numpy as jnp
from jax import lax
from jax.experimental import pallas as pl
from jax.experimental.pallas import tpu as pltpu
from jax.sharding import PartitionSpec as P

H = 32
KVH = 4
HD = 128
FF = 768
TOPK = 8
PROMPT = 1024
PER_KV = H // KVH

EPSILON = 1e-06
ROPE_BASE = 1000000.0
MASKED = -1e30
LOG2E = math.log2(math.e)
SCALE = HD ** (-0.5)

bf16 = jnp.bfloat16
f32 = jnp.float32
NT = (((1,), (1,)), ((), ()))
TN = (((0,), (0,)), ((), ()))
NN = (((1,), (0,)), ((), ()))
BOTH = ("dp", "expert")
VMEM_LIMIT = 56 * 1024 * 1024


def mm(a, b, dims=NN):
    return lax.dot_general(a, b, dims, preferred_element_type=f32)


def rms_scale(values):
    return lax.rsqrt(jnp.mean(values * values, axis=-1, keepdims=True) + EPSILON)


def norm_back(upstream, values, inv_rms, norm_gain):
    lifted = upstream * norm_gain
    inner_dot = jnp.mean(lifted * values, axis=-1, keepdims=True)
    back_grad = inv_rms * lifted - values * (inv_rms * inv_rms * inv_rms) * inner_dot
    gain_grad = jnp.sum((upstream * values * inv_rms).reshape(-1, values.shape[-1]), axis=0)
    return (back_grad, gain_grad)


def rotate(values, cosine, sine_part):
    half_dim = values.shape[-1] // 2
    first_half = values[..., :half_dim]
    second_half = values[..., half_dim:]
    return jnp.concatenate(
        [
            first_half * cosine - second_half * sine_part,
            second_half * cosine + first_half * sine_part,
        ],
        axis=-1,
    )


def turn(values, cosine, sine):
    return values * cosine + pltpu.roll(values, HD // 2, 1) * sine


def project(x_ref, wq_ref, wkv_ref, cos_ref, sin_ref, gq_ref, gk_ref, q_ref, qraw_ref, kv_ref, kraw_ref, wkv_out):
    x = x_ref[...]
    cosine, sine = cos_ref[...], sin_ref[...]
    for at in range(0, PER_KV * HD, 2 * HD):
        raw = mm(x, wq_ref[at : at + 2 * HD], NT)
        qraw_ref[:, at : at + 2 * HD] = raw
        for lane in (0, HD):
            head = raw[:, lane : lane + HD]
            normed = head * rms_scale(head) * gq_ref[...]
            q_ref[:, at + lane : at + lane + HD] = turn(normed, cosine, sine).astype(bf16)
    piece = HD // PER_KV
    w_k = [wkv_ref[2 * piece * i : 2 * piece * i + piece] for i in range(PER_KV)]
    w_v = [wkv_ref[2 * piece * i + piece : 2 * piece * (i + 1)] for i in range(PER_KV)]
    w_kv = jnp.concatenate(w_k + w_v, axis=0)
    wkv_out[...] = w_kv
    raw = mm(x, w_kv, NT)
    key = raw[:, :HD]
    kraw_ref[...] = key
    normed = key * rms_scale(key) * gk_ref[...]
    kv_ref[:, :HD] = turn(normed, cosine, sine).astype(bf16)
    kv_ref[:, HD:] = raw[:, HD:].astype(bf16)


def run_project(x, wq, wkv, cosine, sine, gain_q, gain_k):
    tokens, width = x.shape
    wide = PER_KV * HD
    whole = lambda a: pl.BlockSpec(a.shape, lambda g: (0, 0))
    cols = lambda n: pl.BlockSpec((tokens, n), lambda g: (0, g))
    rows = lambda n: pl.BlockSpec((n, width), lambda g: (g, 0))
    return pl.pallas_call(
        project,
        grid=(KVH,),
        in_specs=[whole(x), rows(wide), rows(2 * HD), whole(cosine), whole(sine), whole(gain_q), whole(gain_k)],
        out_specs=[cols(wide), cols(wide), cols(2 * HD), cols(HD), rows(2 * HD)],
        out_shape=[
            jax.ShapeDtypeStruct((tokens, H * HD), bf16),
            jax.ShapeDtypeStruct((tokens, H * HD), f32),
            jax.ShapeDtypeStruct((tokens, KVH * 2 * HD), bf16),
            jax.ShapeDtypeStruct((tokens, KVH * HD), f32),
            jax.ShapeDtypeStruct((KVH * 2 * HD, width), bf16),
        ],
        compiler_params=pltpu.CompilerParams(vmem_limit_bytes=VMEM_LIMIT),
        cost_estimate=pl.CostEstimate(
            flops=2 * tokens * width * (H + 2 * KVH) * HD, bytes_accessed=40_000_000, transcendentals=0
        ),
    )(x, wq, wkv, cosine, sine, gain_q, gain_k)


def norm_turn_back(grad, raw, cosine, sine, gain):
    grad = turn(grad, cosine, -sine)
    scale = rms_scale(raw)
    lifted = grad * gain
    inner = jnp.mean(lifted * raw, axis=-1, keepdims=True)
    back = scale * lifted - raw * (scale * scale * scale) * inner
    return back, jnp.sum(grad * raw * scale, axis=0, keepdims=True)


def key_back(dkv_ref, kraw_ref, cos_ref, sin_ref, gk_ref, out_ref, out_t_ref, gain_ref):
    gain_sum = 0.0
    for g in range(KVH):
        key = slice(2 * g * HD, (2 * g + 1) * HD)
        value = slice((2 * g + 1) * HD, (2 * g + 2) * HD)
        grad = dkv_ref[:, key].astype(f32)
        back, part = norm_turn_back(
            grad, kraw_ref[:, g * HD : (g + 1) * HD], cos_ref[...], sin_ref[...], gk_ref[...]
        )
        gain_sum += part
        low = back.astype(bf16)
        out_ref[:, key] = low
        out_t_ref[key] = low.T
        out_ref[:, value] = dkv_ref[:, value]
        out_t_ref[value] = dkv_ref[:, value].T
    gain_ref[...] = gain_sum


def run_key_back(dkv, key_raw, cosine, sine, gain):
    tokens, wide = dkv.shape
    return pl.pallas_call(
        key_back,
        out_shape=[
            jax.ShapeDtypeStruct((tokens, wide), bf16),
            jax.ShapeDtypeStruct((wide, tokens), bf16),
            jax.ShapeDtypeStruct((1, HD), f32),
        ],
        compiler_params=pltpu.CompilerParams(vmem_limit_bytes=VMEM_LIMIT),
    )(dkv, key_raw, cosine, sine, gain)


def attend_forward(step_heads, chunk, q_ref, kv_ref, bias_ref, o_ref, log_ref, o2_ref=None):
    group_len = bias_ref.shape[1]
    keys = kv_ref[:, 0, :, :HD].reshape(group_len, HD)
    values_t = kv_ref[:, 0, :, HD:].reshape(group_len, HD).T
    rows = q_ref.shape[1]
    for step in range(PER_KV // step_heads):
        heads = range(step * step_heads, (step + 1) * step_heads)
        query = jnp.concatenate([q_ref[0, :, h * HD : (h + 1) * HD] for h in heads], axis=0)
        mixed, row_sum = 0.0, 0.0
        for at in range(0, group_len, chunk):
            scores = mm(keys[at : at + chunk], query, NT)
            prob = jnp.exp2(scores + bias_ref[0, at : at + chunk, :])
            row_sum += jnp.sum(prob, axis=0, keepdims=True)
            mixed += mm(values_t[:, at : at + chunk], prob.astype(bf16))
        out = (mixed / row_sum).T.astype(bf16)
        for i, h in enumerate(heads):
            part = out[i * rows : (i + 1) * rows]
            o_ref[0, :, h * HD : (h + 1) * HD] = part
            if o2_ref is not None:
                lane = (h // 2) % 2 * HD
                o2_ref[h % 2, h // 4, 0, :, lane : lane + HD] = part
        log_ref[0, 0, step : step + 1, :] = jnp.log2(row_sum)


def attend_backward(
    step_heads, chunk, q_ref, kv_ref, bias_ref, o_ref, do_ref, log_ref, raw_ref, cos_ref, sin_ref, gain_ref,
    dq_ref, dkv_ref, gain_out, dk_acc, dv_acc
):
    group_len = bias_ref.shape[1]
    keys = kv_ref[:, 0, :, :HD].reshape(group_len, HD)
    values = kv_ref[:, 0, :, HD:].reshape(group_len, HD)
    keys_t = keys.T
    rows = q_ref.shape[1]
    cosine, sine, gain = cos_ref[0], sin_ref[0], gain_ref[...]

    @pl.when(pl.program_id(0) == 0)
    def _():
        gain_out[...] = jnp.zeros_like(gain_out)

    gain_sum = 0.0
    dk_acc[...] = jnp.zeros_like(dk_acc)
    dv_acc[...] = jnp.zeros_like(dv_acc)
    for step in range(PER_KV // step_heads):
        heads = range(step * step_heads, (step + 1) * step_heads)
        query = jnp.concatenate([q_ref[0, :, h * HD : (h + 1) * HD] for h in heads], axis=0)
        grad = jnp.concatenate([do_ref[0, :, h * HD : (h + 1) * HD] for h in heads], axis=0)
        mixed = jnp.concatenate([o_ref[0, :, h * HD : (h + 1) * HD] for h in heads], axis=0)
        row_dot = jnp.sum((grad.astype(f32) * mixed.astype(f32)).T, axis=0, keepdims=True)
        log_sum = log_ref[0, 0, step : step + 1, :]
        dq_t = 0.0
        for at in range(0, group_len, chunk):
            part = slice(at, at + chunk)
            scores = mm(keys[part], query, NT)
            prob = jnp.exp2(scores + (bias_ref[0, part, :] - log_sum))
            d_prob = mm(values[part], grad, NT)
            d_score = (prob * (d_prob - row_dot)).astype(bf16)
            dv_acc[part] += mm(prob.astype(bf16), grad)
            dk_acc[part] += mm(d_score, query)
            dq_t += mm(keys_t[:, part], d_score)
        out = (dq_t * SCALE).T.astype(bf16).astype(f32)
        for i, h in enumerate(heads):
            head = slice(h * HD, (h + 1) * HD)
            back, part = norm_turn_back(
                out[i * rows : (i + 1) * rows], raw_ref[0, :, head], cosine, sine, gain
            )
            dq_ref[0, :, head] = back.astype(bf16)
            gain_sum += part
    gain_out[...] += gain_sum
    blocks = dkv_ref.shape[0]
    dkv_ref[:, 0, :, :HD] = (dk_acc[...] * (1.0 / LOG2E)).astype(bf16).reshape(blocks, rows, HD)
    dkv_ref[:, 0, :, HD:] = dv_acc[...].astype(bf16).reshape(blocks, rows, HD)


def attention_specs(rows, group_len, blocks, step_heads, at):
    wide = PER_KV * HD
    q_spec = pl.BlockSpec((1, rows, wide), lambda g: (at, 0, g))
    kv_spec = pl.BlockSpec((blocks, 1, rows, 2 * HD), lambda g: (0, 0, 0, g))
    bias_spec = pl.BlockSpec((1, group_len, step_heads * rows), lambda g: (at, 0, 0))
    log_spec = pl.BlockSpec((1, 1, PER_KV // step_heads, step_heads * rows), lambda g: (at, g, 0, 0))
    return q_spec, kv_spec, bias_spec, log_spec


def run_forward(query, kv_all, bias, step_heads, chunk, at, earlier, again=False):
    micro, rows, _ = query.shape
    blocks = kv_all.shape[0]
    group_len = bias.shape[1]
    q_spec, kv_spec, bias_spec, log_spec = attention_specs(rows, group_len, blocks, step_heads, at)
    flops = 4 * rows * H * HD * group_len

    def kernel(*refs):
        attend_forward(step_heads, chunk, *refs[:3], *refs[3 + len(earlier) :])

    return pl.pallas_call(
        kernel,
        grid=(KVH,),
        in_specs=[q_spec, kv_spec, bias_spec] + [pl.BlockSpec(memory_space=pl.ANY)] * len(earlier),
        out_specs=[q_spec, log_spec]
        + again * [pl.BlockSpec((2, 2, 1, rows, 2 * HD), lambda g: (0, 0, at, 0, g))],
        out_shape=[
            jax.ShapeDtypeStruct(query.shape, bf16),
            jax.ShapeDtypeStruct((micro, KVH, PER_KV // step_heads, step_heads * rows), f32),
        ]
        + again * [jax.ShapeDtypeStruct((2, 2, micro, rows, KVH * 2 * HD), bf16)],
        input_output_aliases={3 + i: i for i in range(len(earlier))},
        compiler_params=pltpu.CompilerParams(vmem_limit_bytes=VMEM_LIMIT),
        cost_estimate=pl.CostEstimate(
            flops=flops, bytes_accessed=20_000_000, transcendentals=flops // (4 * HD)
        ),
    )(query, kv_all, bias, *earlier)


def run_backward(query, kv_all, bias, mixed, grad, logs, raw, cosine, sine, gain, step_heads, chunk, at, earlier):
    micro, rows, _ = query.shape
    blocks = kv_all.shape[0]
    group_len = bias.shape[1]
    q_spec, kv_spec, bias_spec, log_spec = attention_specs(rows, group_len, blocks, step_heads, at)
    flops = 10 * rows * H * HD * group_len
    gain_spec = pl.BlockSpec((1, HD), lambda g: (0, 0))

    def kernel(*refs):
        attend_backward(step_heads, chunk, *refs[:10], *refs[10 + len(earlier) :])

    return pl.pallas_call(
        kernel,
        grid=(KVH,),
        in_specs=[q_spec, kv_spec, bias_spec, q_spec, q_spec, log_spec, q_spec]
        + [pl.BlockSpec((1, rows, HD), lambda g: (at, 0, 0))] * 2
        + [gain_spec]
        + [pl.BlockSpec(memory_space=pl.ANY)] * len(earlier),
        out_specs=[q_spec, kv_spec, gain_spec],
        out_shape=[
            jax.ShapeDtypeStruct(query.shape, bf16),
            jax.ShapeDtypeStruct(kv_all.shape, bf16),
            jax.ShapeDtypeStruct((1, HD), f32),
        ],
        input_output_aliases={10 + i: i for i in range(len(earlier))},
        scratch_shapes=[pltpu.VMEM((group_len, HD), f32), pltpu.VMEM((group_len, HD), f32)],
        compiler_params=pltpu.CompilerParams(vmem_limit_bytes=VMEM_LIMIT),
        cost_estimate=pl.CostEstimate(
            flops=flops, bytes_accessed=30_000_000, transcendentals=flops // (10 * HD)
        ),
    )(query, kv_all, bias, mixed, grad, logs, raw, cosine, sine, gain, *earlier)


def middle_back(r0_ref, r1_ref, mid_ref, cot_ref, gain_ref, w_ref, mix_ref, dmid_ref, low_ref, gain_out):
    @pl.when(pl.program_id(0) == 0)
    def _():
        gain_sum = 0.0
        rows = r0_ref.shape[0]
        for b, ref in enumerate((r0_ref, r1_ref)):
            grad = ref[...].astype(f32)
            middle = mid_ref[b]
            scale = rms_scale(middle)
            lifted = grad * gain_ref[...]
            inner = jnp.mean(lifted * middle, axis=-1, keepdims=True)
            total = cot_ref[b].astype(f32) + scale * lifted - middle * (scale * scale * scale) * inner
            gain_sum += jnp.sum(grad * middle * scale, axis=0, keepdims=True)
            dmid_ref[b * rows : (b + 1) * rows] = total
            low_ref[b * rows : (b + 1) * rows] = total.astype(bf16)
        gain_out[...] = gain_sum

    mix_ref[...] = mm(low_ref[...], w_ref[...], NT).astype(bf16)


def run_middle_back(routed, middle, cot, gain, out_w):
    micro, rows, width = middle.shape
    total = micro * rows
    piece = 512
    whole = lambda *shape: pl.BlockSpec(shape, lambda i: (0,) * len(shape))
    return pl.pallas_call(
        middle_back,
        grid=(out_w.shape[0] // piece,),
        in_specs=[whole(rows, width)] * 2
        + [whole(micro, rows, width)] * 2
        + [whole(1, width), pl.BlockSpec((piece, width), lambda i: (i, 0))],
        out_specs=[
            pl.BlockSpec((total, piece), lambda i: (0, i)),
            whole(total, width),
            whole(total, width),
            whole(1, width),
        ],
        out_shape=[
            jax.ShapeDtypeStruct((total, out_w.shape[0]), bf16),
            jax.ShapeDtypeStruct((total, width), f32),
            jax.ShapeDtypeStruct((total, width), bf16),
            jax.ShapeDtypeStruct((1, width), f32),
        ],
        compiler_params=pltpu.CompilerParams(vmem_limit_bytes=VMEM_LIMIT),
        cost_estimate=pl.CostEstimate(
            flops=2 * total * width * out_w.shape[0], bytes_accessed=35_000_000, transcendentals=0
        ),
    )(*routed, middle, cot, gain, out_w)


MESH = pl.DeviceIdType.MESH


def gather_kernel(phases, count, late, *refs):
    ins, outs, sems = refs[:count], refs[count : 2 * count], refs[2 * count :]
    dp = lax.axis_index("dp"); member = lax.axis_index("expert")
    blocks = lax.axis_size("expert")
    core = member % 2; z = member // 2
    depth = blocks // 2
    sibling = (dp, member + 1 - 2 * core)
    by_x = (dp + 1 - 2 * (dp % 2), member)
    by_y = ((dp + 2) % 4, member)
    x_at, y_at, far_at = by_x[0], by_y[0], 3 - dp
    above, below = (dp, member + 2), (dp, member - 2)
    barrier = pltpu.get_barrier_semaphore()
    peers = [(sibling, None), (by_x, None), (by_y, None), (above, z < depth - 1), (below, z > 0)]
    for peer, ok in peers:
        if ok is None:
            pl.semaphore_signal(barrier, inc=1, device_id=peer, device_id_type=MESH)
        else:
            @pl.when(ok)
            def _(peer=peer):
                pl.semaphore_signal(barrier, inc=1, device_id=peer, device_id_type=MESH)
    @pl.when((z == 0) | (z == depth - 1))
    def _(): pl.semaphore_wait(barrier, 4)
    @pl.when((z > 0) & (z < depth - 1))
    def _(): pl.semaphore_wait(barrier, 5)

    def guarded(ok, run):
        if ok is None: run()
        else: pl.when(ok)(run)

    class Item:
        pass

    def make(i):
        src, out = ins[i], outs[i]
        flat = i in late
        rows = src.shape[0]
        half = rows // 2
        (own_sem, sz, rz, sxy, rxy, sc, rc) = sems[i * 7 : (i + 1) * 7]
        def at(d, s, lo=0, n=rows):
            first = s * 2 + core if flat else d * blocks + s * 2 + core
            return out.at[pl.ds(pl.multiple_of(first * rows + lo, 16 if half % 16 == 0 else 8), n)]
        def copy(a, b, ss, rs, to):
            return pltpu.make_async_remote_copy(src_ref=a, dst_ref=b, send_sem=ss, recv_sem=rs, device_id=to, device_id_type=MESH)
        def block(d, s):
            return at(d, s)
        it = Item()
        def local():
            return pltpu.make_async_copy(src, at(dp, z), own_sem)
        def up(s, ref): return copy(ref, at(dp, s), sz.at[0, s], rz.at[s], above)
        def down(s, ref): return copy(ref, at(dp, s), sz.at[1, s], rz.at[s], below)
        def to_x(s, ref): return copy(ref, at(dp, s), sxy.at[0, s], rxy.at[0, s], by_x)
        def to_y(s, ref): return copy(ref, at(dp, s), sxy.at[1, s], rxy.at[1, s], by_y)
        def half_y(s):
            return copy(at(x_at, s, 0, half), at(x_at, s, 0, half), sxy.at[2, s], rxy.at[2, s], by_y)
        def half_x(s):
            return copy(at(y_at, s, half, half), at(y_at, s, half, half), sxy.at[3, s], rxy.at[3, s], by_x)
        def to_core(r, d, s, ref): return copy(ref, at(d, s), sc.at[r, s], rc.at[r, s], sibling)
        def spread(s, ref):
            if not flat:
                to_x(s, ref).start(); to_y(s, ref).start()
            to_core(0, dp, s, ref).start()
        def start_up():
            up(z, src).start()
        def start_down():
            down(z, src).start()
        def start():
            local().start()
            if not flat:
                guarded(z < depth - 1, start_up)
                guarded(z > 0, start_down)
            spread(z, src)
        def z_event(s, ok, rising):
            def run():
                up(s, at(dp, s)).wait_recv()
                if rising: guarded(z < depth - 1, lambda: up(s, at(dp, s)).start())
                else: guarded(z > 0, lambda: down(s, at(dp, s)).start())
                spread(s, at(dp, s))
            pl.when(ok)(run)
        def near_event(s, ok):
            def run():
                to_x(s, at(dp, s)).wait_recv()
                half_y(s).start()
                to_core(1, x_at, s, at(x_at, s)).start()
                to_y(s, at(dp, s)).wait_recv()
                half_x(s).start()
                to_core(2, y_at, s, at(y_at, s)).start()
            guarded(ok, run)
        def far_event(s, ok):
            def run():
                half_y(s).wait_recv(); half_x(s).wait_recv()
                to_core(3, far_at, s, at(far_at, s)).start()
            guarded(ok, run)
        owners = (dp,) if flat else (dp, x_at, y_at, far_at)
        def core_wait(s):
            for r, d in enumerate(owners):
                to_core(r, d, s, at(d, s)).wait_recv()
        def finish():
            local().wait()
            for s in range(depth):
                if not flat:
                    for c in (to_x(s, at(dp, s)), to_y(s, at(dp, s)), half_y(s), half_x(s)): c.wait_send()
                for r, d in enumerate(owners): to_core(r, d, s, at(d, s)).wait_send()
                guarded((z >= s) & (z < depth - 1), lambda: up(s, at(dp, s)).wait_send())
                guarded((z <= s) & (z > 0), lambda: down(s, at(dp, s)).wait_send())
        it.start_up, it.start_down = start_up, start_down
        it.start, it.z_event, it.near_event, it.far_event, it.core_wait, it.finish = start, z_event, near_event, far_event, core_wait, finish
        return it
    items = [make(i) for i in range(count)]
    def around(d):
        if d == 0: return [(z, None, True)]
        return [(z - d, z >= d, True), (z + d, z + d < depth, False)]
    for n, phase in enumerate(phases):
        its = [items[i] for i in phase]
        for it in its: it.start()
        lates = [items[i] for i in late]
        for it in lates: it.start()
        def late_sends(d):
            for it in lates:
                if d < depth - 1:
                    pl.when(z == d)(it.start_up)
                    pl.when(z == depth - 1 - d)(it.start_down)
        late_sends(0)
        for d in range(1, depth + 2):
            if d < depth:
                for s, ok, rising in around(d):
                    for it in its: it.z_event(s, ok, rising)
                late_sends(d)
            if d - 1 < depth:
                for s, ok, _ in around(d - 1):
                    for it in its: it.near_event(s, ok)
            if d > 2:
                for s, ok, rising in around(d - 2):
                    for it in lates: it.z_event(s, ok, rising)
            if d - 2 >= 0:
                for s, ok, _ in around(d - 2):
                    for it in its: it.far_event(s, ok)
    for it in items:
        for s in range(depth): it.core_wait(s)
    for it in items: it.finish()

def gather_rows(arrays, phases, cid, late=()):
    shards = lax.axis_size("dp") * lax.axis_size("expert")
    depth = lax.axis_size("expert") // 2
    D = pltpu.SemaphoreType.DMA
    sems = []
    for _ in arrays:
        sems += [D, D((2, depth)), D((depth,)), D((4, depth)), D((4, depth)), D((4, depth)), D((4, depth))]
    return pl.pallas_call(
        functools.partial(gather_kernel, phases, len(arrays), late),
        out_shape=[
            jax.ShapeDtypeStruct(((2 * depth if i in late else shards) * a.shape[0],) + a.shape[1:], a.dtype)
            for i, a in enumerate(arrays)
        ],
        in_specs=[pl.BlockSpec(memory_space=pl.ANY)] * len(arrays),
        out_specs=[pl.BlockSpec(memory_space=pl.ANY)] * len(arrays),
        scratch_shapes=sems,
        compiler_params=pltpu.CompilerParams(collective_id=cid, has_side_effects=True),
        cost_estimate=pl.CostEstimate(flops=0, bytes_accessed=400_000_000, transcendentals=0),
    )(*arrays)


def reduce_kernel(rows, cuts, a_ref, extra_ref, b_ref, g_ref, o_ref, go_ref, sib, got, own, far, near, plane, got_z,
                  s0, r0, s1, r1, s2, r2, s3, r3, g_acc, g_got, g_z, gs, gr, gsz, grz):
    dp = lax.axis_index("dp"); member = lax.axis_index("expert")
    core = member % 2; z = member // 2
    sibling = (dp, member + 1 - 2 * core)
    by_x = (dp + 1 - 2 * (dp % 2), member)
    by_y = ((dp + 2) % 4, member)
    x_at, y_at = by_x[0], by_y[0]
    far_at = 3 - dp
    half = rows // 2
    depth = lax.axis_size("expert") // 2
    barrier = pltpu.get_barrier_semaphore()
    peers = [sibling, by_x, by_y] + [(dp, ((z + d) % depth) * 2 + core) for d in range(1, depth)]
    for peer in peers:
        pl.semaphore_signal(barrier, inc=1, device_id=peer, device_id_type=MESH)
    pl.semaphore_wait(barrier, len(peers))

    def pick(table):
        at = table[depth-1]
        for i in range(depth - 1):
            at = jnp.where(z == i, table[i], at)
        return at
    orders = [[3, 3, 0, 0], [2, 0, 3, 1], [1, 2, 1, 2], [0, 1, 2, 3]]
    targets = [pick(t) for t in orders]
    cols = b_ref.shape[1] // cuts

    def copy(src, dst, ssem, rsem, to):
        return pltpu.make_async_remote_copy(src_ref=src, dst_ref=dst, send_sem=ssem, recv_sem=rsem, device_id=to, device_id_type=MESH)

    blocks = 2 * depth
    piece = (rows - HD) // 2

    def product(half_of, k, put):
        spot = targets[k] * 2 + half_of

        def step(i, _):
            shard = (i // cuts) * blocks + spot
            at = (i // cuts) * rows
            col = pl.ds(pl.multiple_of((i % cuts) * cols, cols), cols)
            part = mm(a_ref[:, pl.ds(pl.multiple_of(shard * HD, HD), HD)], b_ref[:, col], TN)
            put(pl.ds(pl.multiple_of(at, 16), HD), col, part)
            if piece:
                base = (shard // PER_KV) * (2 * HD) + (shard % PER_KV) * piece
                small = jnp.concatenate(
                    [
                        extra_ref[pl.ds(pl.multiple_of(base, 16), piece), :],
                        extra_ref[pl.ds(pl.multiple_of(base + HD, 16), piece), :],
                    ],
                    axis=0,
                )
                put(pl.ds(pl.multiple_of(at + HD, 16), 2 * piece), col, mm(small, b_ref[:, col]))
            return 0

        lax.fori_loop(0, 4 * cuts, step, 0)

    def gain_hop(i, src, to):
        return copy(src, g_got.at[i, pl.ds(0, src.shape[0])], gs.at[i], gr.at[i], to)
    hops = {}
    def gain_step(i):
        rows4 = lambda at: pl.ds(pl.multiple_of(at * 8, 8), 8)
        if i == 0:
            hops[0] = gain_hop(0, g_ref.at[pl.ds(pl.multiple_of((1 - core) * 32, 32), 32)], sibling)
        elif i == 1:
            hops[0].wait_recv()
            g_acc[...] = g_ref[pl.ds(pl.multiple_of(core * 32, 32), 32)] + g_got[0]
            hops[1] = gain_hop(1, g_acc.at[pl.ds(pl.multiple_of((1 - dp // 2) * 16, 16), 16)], by_y)
        elif i == 2:
            hops[1].wait_recv()
            mine = pl.ds(pl.multiple_of((dp // 2) * 16, 16), 16)
            g_acc[mine] += g_got[1, :16]
            hops[2] = gain_hop(2, g_acc.at[rows4(x_at)], by_x)
        elif i == 3:
            hops[2].wait_recv()
            g_acc[rows4(dp)] += g_got[2, :8]
            for d in range(1, depth):
                to = (z + d) % depth
                hops[2 + d] = copy(g_acc.at[pl.ds(dp * 8 + to, 1)], g_z.at[z], gsz.at[d - 1], grz.at[z], (dp, to * 2 + core))
        if i < 3:
            hops[i].start()
        else:
            for d in range(1, depth):
                hops[2 + d].start()
    def gain_end():
        total = g_acc[pl.ds(dp * 8 + z, 1)]
        for d in range(1, depth):
            src = (z + d) % depth
            copy(g_acc.at[pl.ds(dp * 8, 1)], g_z.at[src], gsz.at[0], grz.at[src], sibling).wait_recv()
            total += g_z[src]
        go_ref[...] = total
        for i in hops:
            hops[i].wait_send()
    sib_copies, far_copies, near_copies, z_copies = {}, {}, {}, {}
    def sib_step(k):
        slot = k % 2
        if k >= 2:
            sib_copies[k - 2].wait_send()
        def put(r, c, part):
            sib[slot, r, c] = part.astype(bf16)
        product(1 - core, k, put)
        sib_copies[k] = copy(sib.at[slot], got.at[k], s0.at[slot], r0.at[k], sibling)
        sib_copies[k].start()
    def blk(at):
        return pl.ds(pl.multiple_of(at * rows, 16), rows)
    def own_step(k):
        sib_copies[k].wait_recv()
        def put(r, c, part):
            own[k, r, c] = (part + got[k, r, c].astype(f32)).astype(bf16)
        product(core, k, put)
        base = pl.multiple_of(far_at * rows, 16)
        far_copies[k] = (
            copy(own.at[k, pl.ds(base, half)], far.at[k, 0], s1.at[k, 0], r1.at[k, 0], by_x),
            copy(own.at[k, pl.ds(pl.multiple_of(base + half, 16), half)], far.at[k, 1], s1.at[k, 1], r1.at[k, 1], by_y),
        )
        for c in far_copies[k]: c.start()
    def near_step(k):
        a, b = far_copies[k]
        a.wait_recv()
        rng = pl.ds(pl.multiple_of(y_at * rows, 16), half)
        own[k, rng] = (own[k, rng].astype(f32) + far[k, 0].astype(f32)).astype(bf16)
        to_y = copy(own.at[k, blk(y_at)], near.at[k, 1], s2.at[k, 1], r2.at[k, 1], by_y)
        to_y.start()
        b.wait_recv()
        rng = pl.ds(pl.multiple_of(x_at * rows + half, 16), half)
        own[k, rng] = (own[k, rng].astype(f32) + far[k, 1].astype(f32)).astype(bf16)
        to_x = copy(own.at[k, blk(x_at)], near.at[k, 0], s2.at[k, 0], r2.at[k, 0], by_x)
        to_x.start()
        near_copies[k] = (to_x, to_y)
    def plane_step(k):
        for c in near_copies[k]: c.wait_recv()
        total = own[k, blk(dp)].astype(f32) + near[k, 0].astype(f32) + near[k, 1].astype(f32)
        if k < depth - 1:
            plane[k] = total.astype(bf16)
            to = (dp, targets[k] * 2 + core)
            z_copies[k] = copy(plane.at[k], got_z.at[z], s3.at[k], r3.at[z], to)
            z_copies[k].start()
        else:
            o_ref[...] = total
    gain_step(0)
    sib_step(0); sib_step(1)
    own_step(0)
    gain_step(1)
    sib_step(2)
    own_step(1)
    gain_step(2)
    near_step(0)
    sib_step(3)
    own_step(2)
    gain_step(3)
    near_step(1)
    plane_step(0)
    own_step(3)
    near_step(2)
    plane_step(1)
    near_step(3)
    plane_step(2)
    plane_step(3)
    for d in range(1, depth):
        src = (z + d) % depth
        copy(plane.at[0], got_z.at[src], s3.at[0], r3.at[src], sibling).wait_recv()
        o_ref[...] += got_z[src].astype(f32)
    gain_end()
    for k in range(depth):
        if k >= 2: sib_copies[k].wait_send()
        for c in far_copies[k]: c.wait_send()
        for c in near_copies[k]: c.wait_send()
        if k < depth - 1: z_copies[k].wait_send()

def reduce_rows(a, extra, b, cid, gains=None):
    tokens, width = b.shape
    depth = 4
    rows = HD + (0 if extra is None else extra.shape[0] // 32)
    if extra is None:
        extra = jnp.zeros((16, 128), bf16)
    D = pltpu.SemaphoreType.DMA
    lanes = 256
    padded = jnp.zeros((32, lanes), f32)
    if gains is not None:
        padded = jnp.pad(gains, ((0, 0), (0, lanes - gains.shape[1])))
    padded = padded.reshape(4, depth, 2, lanes).transpose(2, 0, 1, 3)
    padded = jnp.pad(padded, ((0, 0), (0, 0), (0, 8 - depth), (0, 0))).reshape(64, lanes)
    return pl.pallas_call(
        functools.partial(reduce_kernel, rows, 4),
        out_shape=[jax.ShapeDtypeStruct((rows, width), f32), jax.ShapeDtypeStruct((1, lanes), f32)],
        in_specs=[pl.BlockSpec(memory_space=pltpu.VMEM)] * 4,
        out_specs=[pl.BlockSpec(memory_space=pltpu.VMEM)] * 2,
        scratch_shapes=[
            pltpu.VMEM((2, 4 * rows, width), bf16),
            pltpu.VMEM((depth, 4 * rows, width), bf16),
            pltpu.VMEM((depth, 4 * rows, width), bf16),
            pltpu.VMEM((depth, 2, rows // 2, width), bf16),
            pltpu.VMEM((depth, 2, rows, width), bf16),
            pltpu.VMEM((depth - 1, rows, width), bf16),
            pltpu.VMEM((depth, rows, width), bf16),
            D((2,)), D((depth,)), D((depth, 2)), D((depth, 2)), D((depth, 2)), D((depth, 2)), D((depth - 1,)), D((depth,)),
            pltpu.VMEM((32, lanes), f32), pltpu.VMEM((3, 32, lanes), f32), pltpu.VMEM((depth, 1, lanes), f32),
            D((3,)), D((3,)), D((depth - 1,)), D((depth,)),
        ],
        compiler_params=pltpu.CompilerParams(vmem_limit_bytes=60*1024*1024, collective_id=cid, has_side_effects=True),
        cost_estimate=pl.CostEstimate(flops=2*tokens*32*rows*width, bytes_accessed=10_000_000, transcendentals=0),
    )(a, extra, b, padded)


ROUTE_LANES = 128


def picks_of(routing, first, local_experts, capacity):
    rows = routing.shape[0]
    lanes = lax.broadcasted_iota(jnp.int32, (rows, ROUTE_LANES), 1)
    places = lax.broadcasted_iota(jnp.int32, (rows, local_experts * capacity), 1)
    hit, weighted = None, 0.0
    for e in range(local_experts):

        def column(base):
            return jnp.sum(jnp.where(lanes == base + first + e, routing, 0.0), axis=1, keepdims=True)

        slot = column(0).astype(jnp.int32)
        here = places == jnp.where(slot >= 0, slot + e * capacity, -1)
        hit = here if hit is None else hit | here
        weighted = weighted + jnp.where(here, column(32) + column(64), 0.0)
    return jnp.where(hit, 1.0, 0.0).astype(bf16), weighted.astype(bf16)


def pick_kernel(capacity, local_experts, n_alias, tok_ref, cot_a, cot_b, *refs):
    x_ref, dy_ref = refs[n_alias:]
    width = cot_a.shape[3]
    cot = jnp.concatenate([cot_a[0, 0], cot_b[0, 0]], axis=0)
    first = lax.axis_index("expert") * local_experts
    routing = tok_ref[0, :, width:]
    hit, _ = picks_of(routing.astype(f32), first, local_experts, capacity)
    x = mm(hit, tok_ref[0, :, :width], TN).astype(bf16)
    rows = mm(hit, routing, TN)
    lanes = lax.broadcasted_iota(jnp.int32, rows.shape, 1)
    owner = lax.broadcasted_iota(jnp.int32, rows.shape, 0) // capacity
    at = lanes - first - owner
    weight = jnp.sum(jnp.where((at == 32) | (at == 64), rows, 0.0), axis=1, keepdims=True)
    dy = (mm(hit, cot, TN) * weight).astype(bf16)
    for e in range(local_experts):
        x_ref[e, 0, 0] = x[e * capacity : (e + 1) * capacity]
        dy_ref[e, 0, 0] = dy[e * capacity : (e + 1) * capacity]


def expert_kernel(n_alias, *refs):
    x_ref, dy_ref = refs[:2]
    parts = (refs[2:7], refs[7:12], refs[12:17])
    z_ref, dg_ref, du_ref, y_ref, dx_ref, wg, wu, wd, sems = refs[17 + n_alias :]
    local_experts, width, _ = wg.shape
    at = lax.axis_index("dp")
    size = width // 4
    places = (at, at + 1 - 2 * (at % 2), (at + 2) % 4, 3 - at, 3 - at)

    def copies(e):
        out = []
        for m, full in enumerate((wg, wu, wd)):
            for p in range(4):
                part = parts[m][p] if p < 3 else parts[m][3 + e]
                src = part.at[e] if p < 3 else part.at[0]
                where = pl.ds(pl.multiple_of(places[p] * size, size), size)
                dst = full.at[e, where, :] if m < 2 else full.at[e, :, where]
                out.append(pltpu.make_async_copy(src, dst, sems.at[e, m, p]))
        return out

    expert, chunk = pl.program_id(0), pl.program_id(1)

    @pl.when((expert == 0) & (chunk == 0))
    def _():
        for e in range(local_experts):
            for c in copies(e):
                c.start()

    for e in range(local_experts):

        @pl.when((expert == e) & (chunk == 0))
        def _(e=e):
            for c in copies(e):
                c.wait()

    x, dy = x_ref[0, 0], dy_ref[0, 0]
    gate = mm(x, wg[expert])
    up = mm(x, wu[expert])
    d_hidden = mm(dy, wd[expert], NT)
    sig = 1.0 / (1.0 + jnp.exp(-gate))
    silu = gate * sig
    z = (silu * up).astype(bf16)
    d_gate = (d_hidden * up * sig * (1.0 + gate * (1.0 - sig))).astype(bf16)
    d_up = (d_hidden * silu).astype(bf16)
    z_ref[0, 0] = z
    dg_ref[0, 0] = d_gate
    du_ref[0, 0] = d_up
    dx_ref[0] = (mm(d_gate, wg[expert], NT) + mm(d_up, wu[expert], NT)).astype(bf16)
    y_ref[0] = mm(z, wd[expert]).astype(bf16)


def sum_kernel(capacity, routing_ref, y_ref, dx_ref, mix_ref, da_ref):
    local_experts, _, _, width = y_ref.shape
    first = lax.axis_index("expert") * local_experts
    hit, weighted = picks_of(routing_ref[0].astype(f32), first, local_experts, capacity)
    da_ref[...] = mm(hit, dx_ref[...].reshape(local_experts * capacity, width)).astype(bf16)
    mix_ref[...] = mm(weighted, y_ref[...].reshape(local_experts * capacity, width)).astype(bf16)


def run_experts(tokens, cot, parts, capacity, batch_at, micro, earlier):
    blocks, rows, _ = tokens.shape
    width = cot[0][0].shape[3]
    local_experts, _, hidden = parts[0][0].shape
    flat = [p for group in parts for p in group]
    any_spec = pl.BlockSpec(memory_space=pl.ANY)
    params = pltpu.CompilerParams(vmem_limit_bytes=VMEM_LIMIT)
    slots = blocks * capacity
    picked_spec = pl.BlockSpec((local_experts, 1, 1, capacity, width), lambda b: (0, batch_at, b, 0, 0))
    picked = jax.ShapeDtypeStruct((local_experts, micro, blocks, capacity, width), bf16)
    x, dy = pl.pallas_call(
        functools.partial(pick_kernel, capacity, local_experts, len(earlier[:2])),
        grid=(blocks,),
        in_specs=[
            pl.BlockSpec((1, rows, tokens.shape[2]), lambda b: (b, 0, 0)),
        ]
        + [pl.BlockSpec((1, 1, rows // 2, width), lambda b, i=i: (b, i, 0, 0)) for _, i in cot]
        + [any_spec] * len(earlier[:2]),
        out_specs=[picked_spec] * 2,
        out_shape=[picked] * 2,
        input_output_aliases={3 + i: i for i in range(len(earlier[:2]))},
        compiler_params=params,
        cost_estimate=pl.CostEstimate(
            flops=4 * slots * local_experts * rows * width, bytes_accessed=25_000_000, transcendentals=0
        ),
    )(tokens, cot[0][0], cot[1][0], *[a.reshape(picked.shape) for a in earlier[:2]])
    x, dy = (a.reshape(local_experts, micro, slots, width) for a in (x, dy))
    chunk = slots // 2
    row_spec = pl.BlockSpec((1, 1, chunk, width), lambda e, i: (e, batch_at, i, 0))
    hid_spec = pl.BlockSpec((1, 1, chunk, hidden), lambda e, i: (e, batch_at, i, 0))
    out_spec = pl.BlockSpec((1, chunk, width), lambda e, i: (e, i, 0))
    hid = jax.ShapeDtypeStruct((local_experts, micro, slots, hidden), bf16)
    out = jax.ShapeDtypeStruct((local_experts, slots, width), bf16)
    z, dg, du, y, dx = pl.pallas_call(
        functools.partial(expert_kernel, len(earlier[2:])),
        grid=(local_experts, 2),
        in_specs=[row_spec, row_spec] + [any_spec] * (len(flat) + len(earlier[2:])),
        out_specs=[hid_spec] * 3 + [out_spec] * 2,
        out_shape=[hid] * 3 + [out] * 2,
        input_output_aliases={2 + len(flat) + i: i for i in range(len(earlier[2:]))},
        scratch_shapes=[
            pltpu.VMEM((local_experts, width, hidden), bf16),
            pltpu.VMEM((local_experts, width, hidden), bf16),
            pltpu.VMEM((local_experts, hidden, width), bf16),
            pltpu.SemaphoreType.DMA((local_experts, 3, 4)),
        ],
        compiler_params=params,
        cost_estimate=pl.CostEstimate(
            flops=12 * local_experts * slots * width * hidden, bytes_accessed=50_000_000, transcendentals=0
        ),
    )(x, dy, *flat, *earlier[2:])
    y, dx = (a.reshape(local_experts, blocks, capacity, width) for a in (y, dx))
    part_spec = pl.BlockSpec((local_experts, 1, capacity, width), lambda b: (0, b, 0, 0))
    sums = jax.ShapeDtypeStruct((blocks * rows, width), bf16)
    sums_spec = pl.BlockSpec((rows, width), lambda b: (b, 0))
    mix, da = pl.pallas_call(
        functools.partial(sum_kernel, capacity),
        grid=(blocks,),
        in_specs=[
            pl.BlockSpec((1, rows, ROUTE_LANES), lambda b: (b, 0, width // ROUTE_LANES)),
            part_spec,
            part_spec,
        ],
        out_specs=[sums_spec] * 2,
        out_shape=[sums] * 2,
        compiler_params=params,
        cost_estimate=pl.CostEstimate(
            flops=4 * slots * local_experts * rows * width, bytes_accessed=25_000_000, transcendentals=0
        ),
    )(tokens, y, dx)
    return [x, dy, z, dg, du], mix, da


def slots_of(route_ids, gate_vals, ranking, capacity, experts):
    rows = route_ids.shape[0]
    pair_experts = route_ids.reshape(-1)
    earlier = (pair_experts[None, :] == pair_experts[:, None]) & (
        ranking[None, :] < ranking[:, None]
    )
    slot = jnp.sum(earlier.astype(jnp.int32), axis=1).reshape(rows, -1)
    kept = slot < capacity
    chosen = route_ids[:, :, None] == jnp.arange(experts, dtype=jnp.int32)[None, None, :]
    chosen = chosen & kept[:, :, None]
    slot_map = jnp.sum(jnp.where(chosen, slot[:, :, None] + 1, 0), axis=1).astype(f32) - 1.0
    weight_map = jnp.sum(jnp.where(chosen, gate_vals[:, :, None], 0.0), axis=1)
    return slot_map, weight_map


def swap(values, bit):
    return lax.ppermute(values, "dp", [(i, i ^ bit) for i in range(lax.axis_size("dp"))])


def dp_part(total, axis, bits, expert, count=1):
    size = total.shape[axis] // 4
    start, sizes = [expert, 0, 0], list(total.shape)
    start[axis] = (lax.axis_index("dp") ^ bits) * size
    sizes[0], sizes[axis] = count, size
    return lax.dynamic_slice(total, start, sizes)


def scatter_far(total, axis):
    return swap(dp_part(total, axis, 3, 0), 1), swap(dp_part(total, axis, 3, 1), 2), total


def scatter_near(pieces, axis):
    for_y, for_x, total = pieces
    by_x, by_y = swap(dp_part(total, axis, 1, 0), 1), swap(dp_part(total, axis, 2, 1), 2)
    near_y = dp_part(total, axis, 2, 0).astype(f32) + for_y.astype(f32)
    near_x = dp_part(total, axis, 1, 1).astype(f32) + for_x.astype(f32)
    return by_x, by_y, swap(near_y.astype(bf16), 2), swap(near_x.astype(bf16), 1), total


def scatter_sum(pieces, axis):
    by_x, by_y, near_y, near_x, total = pieces
    by_x = jnp.concatenate([by_x, near_x], axis=0).astype(f32)
    by_y = jnp.concatenate([near_y, by_y], axis=0).astype(f32)
    return dp_part(total, axis, 0, 0, total.shape[0]).astype(f32) + by_x + by_y


def body_plain(
    inputs,
    cotangent,
    membership,
    routes,
    gate_weights,
    pair_order,
    w_query,
    w_key,
    w_value,
    w_output,
    norm_gains,
    w_gate,
    w_up,
    w_down,
):
    micro = inputs.shape[0]
    rows = inputs.shape[2]
    width = inputs.shape[3]
    group_len = membership.shape[2]
    member = lax.axis_index("expert")
    blocks = lax.axis_size("expert")
    shards = blocks * lax.axis_size("dp")
    shard_at = lax.axis_index("dp") * blocks + member
    local_experts = w_gate.shape[0]
    experts = local_experts * blocks
    capacity = rows * TOPK // experts
    step_heads = max(1, 384 // rows)
    total = micro * rows
    q_part, k_part, v_part = w_query.shape[1], w_key.shape[1], w_value.shape[1]

    gain_len = norm_gains.shape[0]
    gain_shard = jnp.zeros((2048,), bf16).at[:gain_len].set(norm_gains).reshape(16, 128)
    gain_full = lax.all_gather(gain_shard, BOTH, axis=0, tiled=True)
    gains = gain_full.reshape(shards, 2048)[:, :gain_len].reshape(-1).astype(f32)
    gain_in = gains[:width]
    gain_mid = gains[width : 2 * width]
    gain_q = gains[2 * width : 2 * width + HD]
    gain_k = gains[2 * width + HD :]

    qkv_w = lax.all_gather(
        jnp.concatenate([w_query.T, w_key.T, w_value.T], axis=0), BOTH, axis=0, tiled=True
    )
    out_w = lax.all_gather(w_output, BOTH, axis=0, tiled=True)
    wg = lax.all_gather(w_gate, "dp", axis=1, tiled=True)
    wu = lax.all_gather(w_up, "dp", axis=1, tiled=True)
    wd = lax.all_gather(w_down, "dp", axis=2, tiled=True)

    slot_map, weight_map = jax.vmap(
        lambda r, g, o: slots_of(r, g, o, capacity, experts)
    )(routes[:, 0], gate_weights[:, 0], pair_order[:, 0, 0])
    routing = jnp.concatenate([slot_map, weight_map], axis=-1)
    routing = lax.all_gather(routing, "expert", axis=0, tiled=False)
    mine = member * local_experts
    slot_mine = lax.dynamic_slice_in_dim(routing, mine, local_experts, axis=3)
    weight_mine = lax.dynamic_slice_in_dim(routing, experts + mine, local_experts, axis=3)
    slot_mine = jnp.transpose(slot_mine, (1, 3, 0, 2))
    weight_mine = jnp.transpose(weight_mine, (1, 3, 0, 2))
    slot_ids = jnp.arange(capacity, dtype=f32)
    hit = slot_mine[:, :, :, None, :] == slot_ids[None, None, None, :, None]
    pick = hit.astype(bf16)
    weighted = jnp.where(hit, weight_mine[:, :, :, None, :], 0.0)
    slot_weight = jnp.sum(weighted, axis=-1)
    weighted = weighted.astype(bf16)

    key_index = jnp.arange(group_len, dtype=jnp.int32)
    start_row = member * rows
    segment = membership[:, 0]
    row_index = start_row + jnp.arange(rows, dtype=jnp.int32)
    seg_rows = lax.dynamic_slice_in_dim(segment, start_row, rows, axis=1)
    before = jnp.sum((segment[:, None, :] < seg_rows[:, :, None]).astype(jnp.int32), axis=2)
    position = jnp.where(seg_rows == 0, row_index[None], PROMPT + row_index[None] - before)
    allowed = (key_index[None, :, None] <= row_index[None, None, :]) & (
        (segment[:, :, None] == 0) | (segment[:, :, None] == seg_rows[:, None, :])
    )
    bias = jnp.tile(jnp.where(allowed, 0.0, MASKED).astype(f32), (1, 1, step_heads))
    frequency = ROPE_BASE ** (-(jnp.arange(HD // 2, dtype=f32) * 2.0 / HD))
    angles = position.astype(f32).reshape(total)[:, None] * frequency[None, :]
    cosine = jnp.cos(angles)[:, None, :]
    sine_part = jnp.sin(angles)[:, None, :]

    hidden = inputs[:, 0].astype(f32).reshape(total, width)
    scale_in = rms_scale(hidden)
    normed = (hidden * scale_in * gain_in).astype(bf16)
    proj = mm(normed, qkv_w, NT).reshape(total, shards, q_part + k_part + v_part)
    queries = proj[:, :, :q_part].reshape(total, H, HD)
    key_pre = proj[:, :, q_part : q_part + k_part].reshape(total, KVH, HD)
    value = proj[:, :, q_part + k_part :].reshape(total, KVH, HD).astype(bf16)
    scale_q = rms_scale(queries)
    scale_k = rms_scale(key_pre)
    q_low = rotate(queries * scale_q * (gain_q * (SCALE * LOG2E)), cosine, sine_part).astype(bf16)
    q_low = q_low.reshape(micro, rows, H * HD)
    k_low = rotate(key_pre * scale_k * gain_k, cosine, sine_part).astype(bf16)
    kv_own = jnp.concatenate([k_low, value], axis=-1).reshape(micro, rows, KVH * 2 * HD)
    kv_all = lax.all_gather(kv_own, "expert", axis=0, tiled=False)
    chunk = 256
    mixed = []
    for at in range(micro):
        mixed = run_forward(q_low, kv_all[:, at : at + 1], bias, step_heads, chunk, at, mixed)
    mixed, logs = mixed

    branch = mm(mixed.reshape(total, H * HD), out_w)
    middle = hidden + branch
    scale_mid = rms_scale(middle)
    routed = (middle * scale_mid * gain_mid).astype(bf16).reshape(micro, rows, width)
    middle = middle.reshape(micro, rows, width)
    scale_mid = scale_mid.reshape(micro, rows, 1)

    outputs, d_branches, d_middles = [], [], []
    acc_gate = acc_up = acc_down = 0.0
    grad_mid = 0.0
    slots = blocks * capacity
    for at in range(micro):
        d_out = lax.all_gather(cotangent[at, 0], "expert", axis=0, tiled=False)
        tokens = lax.all_gather(routed[at], "expert", axis=0, tiled=False)
        picked = jnp.einsum("ebst,btd->ebsd", pick[at], tokens, preferred_element_type=f32)
        picked = picked.astype(bf16).reshape(local_experts, slots, width)
        d_result = jnp.einsum("ebst,btd->ebsd", pick[at], d_out, preferred_element_type=f32)
        d_result = (d_result * slot_weight[at][..., None]).astype(bf16)
        d_result = d_result.reshape(local_experts, slots, width)
        gate_pre = jnp.einsum("erd,edf->erf", picked, wg, preferred_element_type=f32)
        up_pre = jnp.einsum("erd,edf->erf", picked, wu, preferred_element_type=f32)
        d_hidden = jnp.einsum("erd,efd->erf", d_result, wd, preferred_element_type=f32)
        sigmoid_g = jax.nn.sigmoid(gate_pre)
        silu_g = gate_pre * sigmoid_g
        hidden_low = (silu_g * up_pre).astype(bf16)
        d_gate = (d_hidden * up_pre * sigmoid_g * (1.0 + gate_pre * (1.0 - sigmoid_g))).astype(bf16)
        d_up = (d_hidden * silu_g).astype(bf16)
        d_rows = jnp.einsum("erf,edf->erd", d_gate, wg, preferred_element_type=f32)
        d_rows = d_rows + jnp.einsum("erf,edf->erd", d_up, wu, preferred_element_type=f32)
        d_rows = d_rows.astype(bf16).reshape(local_experts, blocks, capacity, width)
        d_part = jnp.einsum("ebst,ebsd->btd", pick[at], d_rows, preferred_element_type=f32)
        d_part = d_part.astype(bf16).reshape(group_len, width)
        d_routed = lax.psum_scatter(d_part, "expert", scatter_dimension=0, tiled=True).astype(f32)
        result = jnp.einsum("erf,efd->erd", hidden_low, wd, preferred_element_type=f32)
        result = result.astype(bf16).reshape(local_experts, blocks, capacity, width)
        part = jnp.einsum("ebst,ebsd->btd", weighted[at], result, preferred_element_type=f32)
        part = part.astype(bf16).reshape(group_len, width)
        expert_mix = lax.psum_scatter(part, "expert", scatter_dimension=0, tiled=True).astype(f32)
        outputs.append((middle[at] + expert_mix).astype(bf16))

        acc_down += jnp.einsum("erf,erd->efd", hidden_low, d_result, preferred_element_type=f32)
        acc_gate += jnp.einsum("erd,erf->edf", picked, d_gate, preferred_element_type=f32)
        acc_up += jnp.einsum("erd,erf->edf", picked, d_up, preferred_element_type=f32)

        d_mid_norm, mid_gain_grad = norm_back(d_routed, middle[at], scale_mid[at], gain_mid)
        grad_mid = grad_mid + mid_gain_grad
        d_middle = cotangent[at, 0].astype(f32) + d_mid_norm
        d_middles.append(d_middle)
        d_branches.append(d_middle.astype(bf16))

    grad_gate = lax.psum_scatter(acc_gate.astype(bf16), "dp", scatter_dimension=1, tiled=True)
    grad_up = lax.psum_scatter(acc_up.astype(bf16), "dp", scatter_dimension=1, tiled=True)
    grad_down = lax.psum_scatter(acc_down.astype(bf16), "dp", scatter_dimension=2, tiled=True)

    d_branch = jnp.concatenate(d_branches, axis=0)
    d_middle = jnp.concatenate(d_middles, axis=0)
    grad_output = mm(mixed.reshape(total, H * HD), d_branch, TN).astype(bf16)
    grad_output = lax.psum_scatter(grad_output, BOTH, scatter_dimension=0, tiled=True)
    d_mixed = mm(d_branch, out_w, NT).astype(bf16).reshape(micro, rows, H * HD)
    cos_rows = jnp.concatenate([cosine, cosine], axis=-1).reshape(micro, rows, HD)
    sine_rows = jnp.concatenate([-sine_part, sine_part], axis=-1).reshape(micro, rows, HD)
    q_raw = queries.reshape(micro, rows, H * HD)
    d_query, dkv_list, grad_qn = [], [], 0.0
    for at in range(micro):
        d_query, dkv_one, part = run_backward(
            q_low, kv_all[:, at : at + 1], bias, mixed, d_mixed, logs, q_raw, cos_rows, sine_rows,
            gain_q[None, :], step_heads, chunk, at, [d_query] if at else []
        )
        dkv_list.append(dkv_one)
        grad_qn += part[0]
    dkv_all = jnp.concatenate(dkv_list, axis=1)
    dkv = lax.psum_scatter(dkv_all, "expert", scatter_dimension=0, tiled=False)
    dkv = dkv.reshape(total, KVH, 2 * HD)
    d_key = rotate(dkv[:, :, :HD].astype(f32), cosine, -sine_part)
    d_key, grad_kn = norm_back(d_key, key_pre, scale_k, gain_k)
    d_proj = jnp.concatenate(
        [
            d_query.reshape(total, shards, q_part),
            d_key.astype(bf16).reshape(total, shards, k_part),
            dkv[:, :, HD:].reshape(total, shards, v_part),
        ],
        axis=-1,
    ).reshape(total, -1)
    grad_qkv = mm(d_proj, normed, TN).astype(bf16)
    grad_qkv = lax.psum_scatter(grad_qkv, BOTH, scatter_dimension=0, tiled=True).astype(f32)
    d_normed = mm(d_proj, qkv_w)
    d_in_norm, grad_in = norm_back(d_normed, hidden, scale_in, gain_in)
    input_grad = d_middle + d_in_norm

    gain_grads = jnp.concatenate([grad_in, grad_mid, grad_qn, grad_kn]).reshape(shards, gain_len)
    gain_grads = jnp.pad(gain_grads, ((0, 0), (0, 256 - gain_len % 256)))
    gain_all = lax.all_gather(gain_grads, BOTH, axis=0, tiled=False)
    grad_gains = jnp.sum(lax.dynamic_index_in_dim(gain_all, shard_at, axis=1, keepdims=False), axis=0)
    return (
        jnp.stack(outputs)[:, None],
        input_grad.reshape(micro, 1, rows, width),
        grad_qkv[:q_part].T,
        grad_qkv[q_part : q_part + k_part].T,
        grad_qkv[q_part + k_part :].T,
        grad_output.astype(f32),
        grad_gains[:gain_len],
        grad_gate.astype(f32),
        grad_up.astype(f32),
        grad_down.astype(f32),
    )


def body_fast(
    inputs,
    cotangent,
    membership,
    routes,
    gate_weights,
    pair_order,
    w_query,
    w_key,
    w_value,
    w_output,
    norm_gains,
    w_gate,
    w_up,
    w_down,
):
    micro = inputs.shape[0]
    rows = inputs.shape[2]
    width = inputs.shape[3]
    group_len = membership.shape[2]
    member = lax.axis_index("expert")
    blocks = lax.axis_size("expert")
    shards = blocks * lax.axis_size("dp")
    local_experts = w_gate.shape[0]
    experts = local_experts * blocks
    capacity = rows * TOPK // experts
    step_heads = max(1, 384 // rows)
    total = micro * rows
    q_part, k_part, v_part = w_query.shape[1], w_key.shape[1], w_value.shape[1]
    tie = lax.optimization_barrier

    slot_map, weight_map = jax.vmap(
        lambda r, g, o: slots_of(r, g, o, capacity, experts)
    )(routes[:, 0], gate_weights[:, 0], pair_order[:, 0, 0])
    weight_high = tie(weight_map.astype(bf16))
    weight_low = (weight_map - weight_high.astype(f32)).astype(bf16)

    def padded(values, lanes):
        return jnp.pad(values, ((0, 0), (0, 0), (0, lanes - experts)))

    routing = jnp.concatenate(
        [
            padded(slot_map.astype(bf16), 32),
            padded(weight_high, 32),
            padded(weight_low, ROUTE_LANES - 64),
        ],
        axis=-1,
    )

    gain_len = norm_gains.shape[0]
    gain_shard = jnp.zeros((2048,), bf16).at[:gain_len].set(norm_gains).reshape(16, 128)
    kv_w = jnp.concatenate([w_key.T, w_value.T], axis=0)
    halves = cotangent.reshape(2 * micro, rows // 2, width)
    cot_first = halves[:3].reshape(-1, width)
    q_w, kv_w, out_w, gain_full, cot_first = gather_rows(
        [w_query.T, kv_w, w_output, gain_shard, cot_first], [(3, 0, 1, 2)], 1, (4,)
    )
    cot_first = cot_first.reshape(blocks, 3, rows // 2, width)
    q_w, w_gate = tie((q_w, w_gate))
    gains = gain_full.reshape(shards, 2048)[:, :gain_len].reshape(-1).astype(f32)
    gain_in = gains[:width]
    gain_mid = gains[width : 2 * width]
    gain_q = gains[2 * width : 2 * width + HD]
    gain_k = gains[2 * width + HD :]
    gate_near = (swap(w_gate, 1), swap(w_gate, 2))

    key_index = jnp.arange(group_len, dtype=jnp.int32)
    start_row = member * rows
    segment = membership[:, 0]
    row_index = start_row + jnp.arange(rows, dtype=jnp.int32)
    seg_rows = lax.dynamic_slice_in_dim(segment, start_row, rows, axis=1)
    before = jnp.sum((segment[:, None, :] < seg_rows[:, :, None]).astype(jnp.int32), axis=2)
    position = jnp.where(seg_rows == 0, row_index[None], PROMPT + row_index[None] - before)
    allowed = (key_index[None, :, None] <= row_index[None, None, :]) & (
        (segment[:, :, None] == 0) | (segment[:, :, None] == seg_rows[:, None, :])
    )
    bias = jnp.tile(jnp.where(allowed, 0.0, MASKED).astype(f32), (1, 1, step_heads))
    frequency = ROPE_BASE ** (-(jnp.arange(HD // 2, dtype=f32) * 2.0 / HD))
    angles = position.astype(f32).reshape(total)[:, None] * frequency[None, :]
    cosine, sine = jnp.cos(angles), jnp.sin(angles)
    cosine = jnp.concatenate([cosine, cosine], axis=-1)
    sine = jnp.concatenate([-sine, sine], axis=-1)
    gain_q, gain_k = gain_q[None, :], gain_k[None, :]

    hidden = inputs[:, 0].astype(f32).reshape(total, width)
    scale_in = rms_scale(hidden)
    normed = (hidden * scale_in * gain_in).astype(bf16)
    q_low, q_raw, kv_own, k_raw, kv_w = run_project(
        normed, q_w, kv_w, cosine, sine, gain_q * (SCALE * LOG2E), gain_k
    )
    q_low, q_raw = (a.reshape(micro, rows, H * HD) for a in (q_low, q_raw))
    kv_own = kv_own.reshape(micro, rows, KVH * 2 * HD)
    kv_own, gate_near, w_up = tie((kv_own, gate_near, w_up))
    up_near = (swap(w_up, 1), swap(w_up, 2))
    kv_0 = lax.all_gather(kv_own[0], "expert", axis=0, tiled=False)
    kv_1 = lax.all_gather(kv_own[1], "expert", axis=0, tiled=False)
    kv_0, up_near, w_down = tie((kv_0, up_near, w_down))
    down_near = (swap(w_down, 1), swap(w_down, 2))
    kv_1, cot_last = tie((kv_1, halves[3]))
    cot_last = lax.all_gather(cot_last, "expert", axis=0, tiled=False)[:, None]
    kv_all = [kv_0[:, None], kv_1[:, None]]
    chunk = 256
    mixed = run_forward(q_low, kv_all[0], bias, step_heads, chunk, 0, [], True)
    mixed, kv_all = tie((mixed, kv_all))
    mixed, logs, shares = run_forward(q_low, kv_all[1], bias, step_heads, chunk, 1, mixed, True)
    mixed, down_near = tie((mixed, down_near))
    parts = [
        (own, near[0], near[1], swap(near[0][:1], 2), swap(near[1][1:], 1))
        for own, near in ((w_gate, gate_near), (w_up, up_near), (w_down, down_near))
    ]

    branch = mm(mixed.reshape(total, H * HD), out_w)
    middle = hidden + branch
    scale_mid = rms_scale(middle)
    routed = (middle * scale_mid * gain_mid).astype(bf16).reshape(micro, rows, width)
    routed = jnp.concatenate([routed, routing], axis=-1)
    routed, cot_last = tie((routed, cot_last))
    cots = [((cot_first, 0), (cot_first, 1)), ((cot_first, 2), (cot_last, 0))]
    middle = middle.reshape(micro, rows, width)
    scale_mid = scale_mid.reshape(micro, rows, 1)

    mix_parts, d_routeds = [], []
    kept = []
    for at in range(micro):
        tokens = lax.all_gather(routed[at], "expert", axis=0, tiled=False)
        tokens, parts = tie((tokens, parts))
        kept, mix, d_part = run_experts(tokens, cots[at], parts, capacity, at, micro, kept)
        kept, d_part, mix, d_routeds = tie((kept, d_part, mix, d_routeds))
        mix_parts.append(mix)
        d_routed = lax.psum_scatter(d_part, "expert", scatter_dimension=0, tiled=True)
        d_routeds.append(d_routed)
    picked, d_result, hidden_low, d_gate, d_up = (
        a.reshape(local_experts, -1, a.shape[-1]) for a in kept
    )

    def weight_grad(rows_in, rows_out):
        return jnp.einsum("era,erb->eab", rows_in, rows_out, preferred_element_type=f32).astype(bf16)

    first = scatter_far(weight_grad(picked, d_gate), 1)
    second = scatter_far(weight_grad(picked, d_up), 1)
    first, hidden_low = tie((first, hidden_low))
    first = scatter_near(first, 1)
    third = weight_grad(hidden_low, d_result)
    d_routeds[-1], first, second, third, mix_parts[0] = tie(
        (d_routeds[-1], first, second, third, mix_parts[0])
    )
    second = scatter_near(second, 1)
    third = scatter_far(third, 2)
    d_mixed, d_middle, d_branch, grad_mid = run_middle_back(
        d_routeds, middle, cotangent[:, 0], gain_mid[None, :], out_w
    )
    d_mixed, d_branch, third = tie((d_mixed, d_branch, third))
    third = scatter_near(third, 2)
    d_mixed = d_mixed.reshape(micro, rows, H * HD)
    cos_rows, sine_rows = (a.reshape(micro, rows, HD) for a in (cosine, sine))
    def share(core):
        part = lax.dynamic_index_in_dim(shares, core, axis=0, keepdims=False)
        part = part.reshape(2, total, -1)
        return jnp.einsum("zta,td->zad", part, d_branch, preferred_element_type=f32).astype(bf16)

    core = member % 2
    pairs = [(i, i ^ 1) for i in range(blocks)]
    got = lax.ppermute(share(1 - core), "expert", pairs)
    mixes = [lax.psum_scatter(mix_parts[0], "expert", scatter_dimension=0, tiled=True)]

    def backward(at, earlier):
        d_query, dkv_one, part = run_backward(
            q_low, kv_all[at], bias, mixed, d_mixed, logs, q_raw, cos_rows, sine_rows, gain_q,
            step_heads, chunk, at, earlier
        )
        return d_query, dkv_one[:, 0], part

    d_query, dkv_0, gain_0 = backward(0, [])
    d_query, dkv_0, got, second = tie((d_query, dkv_0, got, second))
    dkv_0 = lax.psum_scatter(dkv_0, "expert", scatter_dimension=0, tiled=False)
    out_grad = tie(share(core))
    out_grad = (out_grad.astype(f32) + got.astype(f32)).astype(bf16)
    d_query, out_grad = tie((d_query, out_grad))
    out_grad = scatter_far(out_grad, 1)
    d_query, dkv_1, gain_1 = backward(1, [d_query])
    grad_qn = gain_0 + gain_1
    d_query, dkv_1, out_grad, mixes, third = tie((d_query, dkv_1, out_grad, mixes, third))
    dkv_1 = lax.psum_scatter(dkv_1, "expert", scatter_dimension=0, tiled=False)
    out_grad = scatter_sum(scatter_near(out_grad, 1), 1).astype(bf16).reshape(-1, width)
    d_query = d_query.reshape(total, H * HD)
    dkv = jnp.concatenate([dkv_0, dkv_1], axis=0)
    dkv = dkv.reshape(total, KVH * 2 * HD)
    mix_part, dkv = tie((mix_parts[1], dkv))
    mixes.append(lax.psum_scatter(mix_part, "expert", scatter_dimension=0, tiled=True))
    outputs = [(middle[at] + mixes[at].astype(f32)).astype(bf16) for at in range(micro)]
    dkv, dkv_t, grad_kn = run_key_back(dkv, k_raw, cosine, sine, gain_k)
    dkv, out_grad = tie((dkv, out_grad))
    d_normed = mm(d_query, q_w) + mm(dkv, kv_w)
    grad_output = lax.psum_scatter(
        out_grad,
        "expert",
        scatter_dimension=0,
        tiled=True,
        axis_index_groups=[list(range(c, blocks, 2)) for c in range(2)],
    ).astype(f32)
    d_in_norm, grad_in = norm_back(d_normed, hidden, scale_in, gain_in)
    input_grad = d_middle + d_in_norm
    gain_grads = jnp.concatenate([grad_in, grad_mid[0], grad_qn[0], grad_kn[0]]).reshape(shards, gain_len)
    grad_qkv, grad_gains = reduce_rows(d_query, dkv_t, normed, 3, gain_grads)
    expert_grads = [scatter_sum(first, 1), scatter_sum(second, 1), scatter_sum(third, 2)]
    return (
        jnp.stack(outputs)[:, None],
        input_grad.reshape(micro, 1, rows, width),
        grad_qkv[:q_part].T,
        grad_qkv[q_part : q_part + k_part].T,
        grad_qkv[q_part + k_part :].T,
        grad_output,
        grad_gains[0, :gain_len],
        *expert_grads,
    )


def solution(mesh):
    fast = mesh.shape["dp"] == 4 and mesh.shape["expert"] == 8
    return jax.shard_map(
        body_fast if fast else body_plain,
        mesh=mesh,
        in_specs=(
            P(None, "dp", "expert", None),
            P(None, "dp", "expert", None),
            P(None, "dp", None),
            P(None, "dp", "expert", None),
            P(None, "dp", "expert", None),
            P(None, "dp", "expert", None),
            P(None, ("dp", "expert")),
            P(None, ("dp", "expert")),
            P(None, ("dp", "expert")),
            P(("dp", "expert"), None),
            P(("dp", "expert")),
            P("expert", "dp", None),
            P("expert", "dp", None),
            P("expert", None, "dp"),
        ),
        out_specs=(
            P(None, "dp", "expert", None),
            P(None, "dp", "expert", None),
            P(None, ("dp", "expert")),
            P(None, ("dp", "expert")),
            P(None, ("dp", "expert")),
            P(("dp", "expert"), None),
            P(("dp", "expert")),
            P("expert", "dp", None),
            P("expert", "dp", None),
            P("expert", None, "dp"),
        ),
        check_vma=False,
    )
```

```python
import functools
import math

import jax
import jax.numpy as jnp
from jax import lax
from jax.experimental import pallas as pl
from jax.experimental.pallas import tpu as pltpu
from jax.sharding import PartitionSpec as P

H = 32
KVH = 4
HD = 128
FF = 768
TOPK = 8
PROMPT = 1024
PER_KV = H // KVH

EPSILON = 1e-06
ROPE_BASE = 1000000.0
MASKED = -1e30
LOG2E = math.log2(math.e)
SCALE = HD ** (-0.5)

bf16 = jnp.bfloat16
f32 = jnp.float32
NT = (((1,), (1,)), ((), ()))
TN = (((0,), (0,)), ((), ()))
NN = (((1,), (0,)), ((), ()))
BOTH = ("dp", "expert")
VMEM_LIMIT = 56 * 1024 * 1024


def mm(a, b, dims=NN):
    return lax.dot_general(a, b, dims, preferred_element_type=f32)


def rms_scale(values):
    return lax.rsqrt(jnp.mean(values * values, axis=-1, keepdims=True) + EPSILON)


def norm_back(upstream, values, inv_rms, norm_gain):
    lifted = upstream * norm_gain
    inner_dot = jnp.mean(lifted * values, axis=-1, keepdims=True)
    back_grad = inv_rms * lifted - values * (inv_rms * inv_rms * inv_rms) * inner_dot
    gain_grad = jnp.sum((upstream * values * inv_rms).reshape(-1, values.shape[-1]), axis=0)
    return (back_grad, gain_grad)


def rotate(values, cosine, sine_part):
    half_dim = values.shape[-1] // 2
    first_half = values[..., :half_dim]
    second_half = values[..., half_dim:]
    return jnp.concatenate(
        [
            first_half * cosine - second_half * sine_part,
            second_half * cosine + first_half * sine_part,
        ],
        axis=-1,
    )


def turn(values, cosine, sine):
    return values * cosine + pltpu.roll(values, HD // 2, 1) * sine


def project(x_ref, wq_ref, wkv_ref, cos_ref, sin_ref, gq_ref, gk_ref, q_ref, qraw_ref, kv_ref, kraw_ref, wkv_out):
    x = x_ref[...]
    cosine, sine = cos_ref[...], sin_ref[...]
    for at in range(0, PER_KV * HD, 2 * HD):
        raw = mm(x, wq_ref[at : at + 2 * HD], NT)
        qraw_ref[:, at : at + 2 * HD] = raw
        for lane in (0, HD):
            head = raw[:, lane : lane + HD]
            normed = head * rms_scale(head) * gq_ref[...]
            q_ref[:, at + lane : at + lane + HD] = turn(normed, cosine, sine).astype(bf16)
    piece = HD // PER_KV
    w_k = [wkv_ref[2 * piece * i : 2 * piece * i + piece] for i in range(PER_KV)]
    w_v = [wkv_ref[2 * piece * i + piece : 2 * piece * (i + 1)] for i in range(PER_KV)]
    w_kv = jnp.concatenate(w_k + w_v, axis=0)
    wkv_out[...] = w_kv
    raw = mm(x, w_kv, NT)
    key = raw[:, :HD]
    kraw_ref[...] = key
    normed = key * rms_scale(key) * gk_ref[...]
    kv_ref[:, :HD] = turn(normed, cosine, sine).astype(bf16)
    kv_ref[:, HD:] = raw[:, HD:].astype(bf16)


def run_project(x, wq, wkv, cosine, sine, gain_q, gain_k):
    tokens, width = x.shape
    wide = PER_KV * HD
    whole = lambda a: pl.BlockSpec(a.shape, lambda g: (0, 0))
    cols = lambda n: pl.BlockSpec((tokens, n), lambda g: (0, g))
    rows = lambda n: pl.BlockSpec((n, width), lambda g: (g, 0))
    return pl.pallas_call(
        project,
        grid=(KVH,),
        in_specs=[whole(x), rows(wide), rows(2 * HD), whole(cosine), whole(sine), whole(gain_q), whole(gain_k)],
        out_specs=[cols(wide), cols(wide), cols(2 * HD), cols(HD), rows(2 * HD)],
        out_shape=[
            jax.ShapeDtypeStruct((tokens, H * HD), bf16),
            jax.ShapeDtypeStruct((tokens, H * HD), f32),
            jax.ShapeDtypeStruct((tokens, KVH * 2 * HD), bf16),
            jax.ShapeDtypeStruct((tokens, KVH * HD), f32),
            jax.ShapeDtypeStruct((KVH * 2 * HD, width), bf16),
        ],
        compiler_params=pltpu.CompilerParams(vmem_limit_bytes=VMEM_LIMIT),
        cost_estimate=pl.CostEstimate(
            flops=2 * tokens * width * (H + 2 * KVH) * HD, bytes_accessed=40_000_000, transcendentals=0
        ),
    )(x, wq, wkv, cosine, sine, gain_q, gain_k)


def norm_turn_back(grad, raw, cosine, sine, gain):
    grad = turn(grad, cosine, -sine)
    scale = rms_scale(raw)
    lifted = grad * gain
    inner = jnp.mean(lifted * raw, axis=-1, keepdims=True)
    back = scale * lifted - raw * (scale * scale * scale) * inner
    return back, jnp.sum(grad * raw * scale, axis=0, keepdims=True)


def key_back(dkv_ref, kraw_ref, cos_ref, sin_ref, gk_ref, out_ref, out_t_ref, gain_ref):
    gain_sum = 0.0
    for g in range(KVH):
        key = slice(2 * g * HD, (2 * g + 1) * HD)
        value = slice((2 * g + 1) * HD, (2 * g + 2) * HD)
        grad = dkv_ref[:, key].astype(f32)
        back, part = norm_turn_back(
            grad, kraw_ref[:, g * HD : (g + 1) * HD], cos_ref[...], sin_ref[...], gk_ref[...]
        )
        gain_sum += part
        low = back.astype(bf16)
        out_ref[:, key] = low
        out_t_ref[key] = low.T
        out_ref[:, value] = dkv_ref[:, value]
        out_t_ref[value] = dkv_ref[:, value].T
    gain_ref[...] = gain_sum


def run_key_back(dkv, key_raw, cosine, sine, gain):
    tokens, wide = dkv.shape
    return pl.pallas_call(
        key_back,
        out_shape=[
            jax.ShapeDtypeStruct((tokens, wide), bf16),
            jax.ShapeDtypeStruct((wide, tokens), bf16),
            jax.ShapeDtypeStruct((1, HD), f32),
        ],
        compiler_params=pltpu.CompilerParams(vmem_limit_bytes=VMEM_LIMIT),
    )(dkv, key_raw, cosine, sine, gain)


def attend_forward(step_heads, chunk, q_ref, kv_ref, bias_ref, o_ref, log_ref, o2_ref=None):
    group_len = bias_ref.shape[1]
    keys = kv_ref[:, 0, :, :HD].reshape(group_len, HD)
    values_t = kv_ref[:, 0, :, HD:].reshape(group_len, HD).T
    rows = q_ref.shape[1]
    for step in range(PER_KV // step_heads):
        heads = range(step * step_heads, (step + 1) * step_heads)
        query = jnp.concatenate([q_ref[0, :, h * HD : (h + 1) * HD] for h in heads], axis=0)
        mixed, row_sum = 0.0, 0.0
        for at in range(0, group_len, chunk):
            scores = mm(keys[at : at + chunk], query, NT)
            prob = jnp.exp2(scores + bias_ref[0, at : at + chunk, :])
            row_sum += jnp.sum(prob, axis=0, keepdims=True)
            mixed += mm(values_t[:, at : at + chunk], prob.astype(bf16))
        out = (mixed / row_sum).T.astype(bf16)
        for i, h in enumerate(heads):
            part = out[i * rows : (i + 1) * rows]
            o_ref[0, :, h * HD : (h + 1) * HD] = part
            if o2_ref is not None:
                lane = (h // 2) % 2 * HD
                o2_ref[h % 2, h // 4, 0, :, lane : lane + HD] = part
        log_ref[0, 0, step : step + 1, :] = jnp.log2(row_sum)


def attend_backward(
    step_heads, chunk, q_ref, kv_ref, bias_ref, o_ref, do_ref, log_ref, raw_ref, cos_ref, sin_ref, gain_ref,
    dq_ref, dkv_ref, gain_out, dk_acc, dv_acc
):
    group_len = bias_ref.shape[1]
    keys = kv_ref[:, 0, :, :HD].reshape(group_len, HD)
    values = kv_ref[:, 0, :, HD:].reshape(group_len, HD)
    keys_t = keys.T
    rows = q_ref.shape[1]
    cosine, sine, gain = cos_ref[0], sin_ref[0], gain_ref[...]

    @pl.when(pl.program_id(0) == 0)
    def _():
        gain_out[...] = jnp.zeros_like(gain_out)

    gain_sum = 0.0
    dk_acc[...] = jnp.zeros_like(dk_acc)
    dv_acc[...] = jnp.zeros_like(dv_acc)
    for step in range(PER_KV // step_heads):
        heads = range(step * step_heads, (step + 1) * step_heads)
        query = jnp.concatenate([q_ref[0, :, h * HD : (h + 1) * HD] for h in heads], axis=0)
        grad = jnp.concatenate([do_ref[0, :, h * HD : (h + 1) * HD] for h in heads], axis=0)
        mixed = jnp.concatenate([o_ref[0, :, h * HD : (h + 1) * HD] for h in heads], axis=0)
        row_dot = jnp.sum((grad.astype(f32) * mixed.astype(f32)).T, axis=0, keepdims=True)
        log_sum = log_ref[0, 0, step : step + 1, :]
        dq_t = 0.0
        for at in range(0, group_len, chunk):
            part = slice(at, at + chunk)
            scores = mm(keys[part], query, NT)
            prob = jnp.exp2(scores + (bias_ref[0, part, :] - log_sum))
            d_prob = mm(values[part], grad, NT)
            d_score = (prob * (d_prob - row_dot)).astype(bf16)
            dv_acc[part] += mm(prob.astype(bf16), grad)
            dk_acc[part] += mm(d_score, query)
            dq_t += mm(keys_t[:, part], d_score)
        out = (dq_t * SCALE).T.astype(bf16).astype(f32)
        for i, h in enumerate(heads):
            head = slice(h * HD, (h + 1) * HD)
            back, part = norm_turn_back(
                out[i * rows : (i + 1) * rows], raw_ref[0, :, head], cosine, sine, gain
            )
            dq_ref[0, :, head] = back.astype(bf16)
            gain_sum += part
    gain_out[...] += gain_sum
    blocks = dkv_ref.shape[0]
    dkv_ref[:, 0, :, :HD] = (dk_acc[...] * (1.0 / LOG2E)).astype(bf16).reshape(blocks, rows, HD)
    dkv_ref[:, 0, :, HD:] = dv_acc[...].astype(bf16).reshape(blocks, rows, HD)


def attention_specs(rows, group_len, blocks, step_heads, at):
    wide = PER_KV * HD
    q_spec = pl.BlockSpec((1, rows, wide), lambda g: (at, 0, g))
    kv_spec = pl.BlockSpec((blocks, 1, rows, 2 * HD), lambda g: (0, 0, 0, g))
    bias_spec = pl.BlockSpec((1, group_len, step_heads * rows), lambda g: (at, 0, 0))
    log_spec = pl.BlockSpec((1, 1, PER_KV // step_heads, step_heads * rows), lambda g: (at, g, 0, 0))
    return q_spec, kv_spec, bias_spec, log_spec


def run_forward(query, kv_all, bias, step_heads, chunk, at, earlier, again=False):
    micro, rows, _ = query.shape
    blocks = kv_all.shape[0]
    group_len = bias.shape[1]
    q_spec, kv_spec, bias_spec, log_spec = attention_specs(rows, group_len, blocks, step_heads, at)
    flops = 4 * rows * H * HD * group_len

    def kernel(*refs):
        attend_forward(step_heads, chunk, *refs[:3], *refs[3 + len(earlier) :])

    return pl.pallas_call(
        kernel,
        grid=(KVH,),
        in_specs=[q_spec, kv_spec, bias_spec] + [pl.BlockSpec(memory_space=pl.ANY)] * len(earlier),
        out_specs=[q_spec, log_spec]
        + again * [pl.BlockSpec((2, 2, 1, rows, 2 * HD), lambda g: (0, 0, at, 0, g))],
        out_shape=[
            jax.ShapeDtypeStruct(query.shape, bf16),
            jax.ShapeDtypeStruct((micro, KVH, PER_KV // step_heads, step_heads * rows), f32),
        ]
        + again * [jax.ShapeDtypeStruct((2, 2, micro, rows, KVH * 2 * HD), bf16)],
        input_output_aliases={3 + i: i for i in range(len(earlier))},
        compiler_params=pltpu.CompilerParams(vmem_limit_bytes=VMEM_LIMIT),
        cost_estimate=pl.CostEstimate(
            flops=flops, bytes_accessed=20_000_000, transcendentals=flops // (4 * HD)
        ),
    )(query, kv_all, bias, *earlier)


def run_backward(query, kv_all, bias, mixed, grad, logs, raw, cosine, sine, gain, step_heads, chunk, at, earlier):
    micro, rows, _ = query.shape
    blocks = kv_all.shape[0]
    group_len = bias.shape[1]
    q_spec, kv_spec, bias_spec, log_spec = attention_specs(rows, group_len, blocks, step_heads, at)
    flops = 10 * rows * H * HD * group_len
    gain_spec = pl.BlockSpec((1, HD), lambda g: (0, 0))

    def kernel(*refs):
        attend_backward(step_heads, chunk, *refs[:10], *refs[10 + len(earlier) :])

    return pl.pallas_call(
        kernel,
        grid=(KVH,),
        in_specs=[q_spec, kv_spec, bias_spec, q_spec, q_spec, log_spec, q_spec]
        + [pl.BlockSpec((1, rows, HD), lambda g: (at, 0, 0))] * 2
        + [gain_spec]
        + [pl.BlockSpec(memory_space=pl.ANY)] * len(earlier),
        out_specs=[q_spec, kv_spec, gain_spec],
        out_shape=[
            jax.ShapeDtypeStruct(query.shape, bf16),
            jax.ShapeDtypeStruct(kv_all.shape, bf16),
            jax.ShapeDtypeStruct((1, HD), f32),
        ],
        input_output_aliases={10 + i: i for i in range(len(earlier))},
        scratch_shapes=[pltpu.VMEM((group_len, HD), f32), pltpu.VMEM((group_len, HD), f32)],
        compiler_params=pltpu.CompilerParams(vmem_limit_bytes=VMEM_LIMIT),
        cost_estimate=pl.CostEstimate(
            flops=flops, bytes_accessed=30_000_000, transcendentals=flops // (10 * HD)
        ),
    )(query, kv_all, bias, mixed, grad, logs, raw, cosine, sine, gain, *earlier)


def middle_back(r0_ref, r1_ref, mid_ref, cot_ref, gain_ref, w_ref, mix_ref, dmid_ref, low_ref, gain_out):
    @pl.when(pl.program_id(0) == 0)
    def _():
        gain_sum = 0.0
        rows = r0_ref.shape[0]
        for b, ref in enumerate((r0_ref, r1_ref)):
            grad = ref[...].astype(f32)
            middle = mid_ref[b]
            scale = rms_scale(middle)
            lifted = grad * gain_ref[...]
            inner = jnp.mean(lifted * middle, axis=-1, keepdims=True)
            total = cot_ref[b].astype(f32) + scale * lifted - middle * (scale * scale * scale) * inner
            gain_sum += jnp.sum(grad * middle * scale, axis=0, keepdims=True)
            dmid_ref[b * rows : (b + 1) * rows] = total
            low_ref[b * rows : (b + 1) * rows] = total.astype(bf16)
        gain_out[...] = gain_sum

    mix_ref[...] = mm(low_ref[...], w_ref[...], NT).astype(bf16)


def run_middle_back(routed, middle, cot, gain, out_w):
    micro, rows, width = middle.shape
    total = micro * rows
    piece = 512
    whole = lambda *shape: pl.BlockSpec(shape, lambda i: (0,) * len(shape))
    return pl.pallas_call(
        middle_back,
        grid=(out_w.shape[0] // piece,),
        in_specs=[whole(rows, width)] * 2
        + [whole(micro, rows, width)] * 2
        + [whole(1, width), pl.BlockSpec((piece, width), lambda i: (i, 0))],
        out_specs=[
            pl.BlockSpec((total, piece), lambda i: (0, i)),
            whole(total, width),
            whole(total, width),
            whole(1, width),
        ],
        out_shape=[
            jax.ShapeDtypeStruct((total, out_w.shape[0]), bf16),
            jax.ShapeDtypeStruct((total, width), f32),
            jax.ShapeDtypeStruct((total, width), bf16),
            jax.ShapeDtypeStruct((1, width), f32),
        ],
        compiler_params=pltpu.CompilerParams(vmem_limit_bytes=VMEM_LIMIT),
        cost_estimate=pl.CostEstimate(
            flops=2 * total * width * out_w.shape[0], bytes_accessed=35_000_000, transcendentals=0
        ),
    )(*routed, middle, cot, gain, out_w)


MESH = pl.DeviceIdType.MESH


def gather_kernel(phases, count, late, *refs):
    ins, outs, sems = refs[:count], refs[count : 2 * count], refs[2 * count :]
    dp = lax.axis_index("dp"); member = lax.axis_index("expert")
    blocks = lax.axis_size("expert")
    core = member % 2; z = member // 2
    depth = blocks // 2
    sibling = (dp, member + 1 - 2 * core)
    by_x = (dp + 1 - 2 * (dp % 2), member)
    by_y = ((dp + 2) % 4, member)
    x_at, y_at, far_at = by_x[0], by_y[0], 3 - dp
    above, below = (dp, member + 2), (dp, member - 2)
    barrier = pltpu.get_barrier_semaphore()
    peers = [(sibling, None), (by_x, None), (by_y, None), (above, z < depth - 1), (below, z > 0)]
    for peer, ok in peers:
        if ok is None:
            pl.semaphore_signal(barrier, inc=1, device_id=peer, device_id_type=MESH)
        else:
            @pl.when(ok)
            def _(peer=peer):
                pl.semaphore_signal(barrier, inc=1, device_id=peer, device_id_type=MESH)
    @pl.when((z == 0) | (z == depth - 1))
    def _(): pl.semaphore_wait(barrier, 4)
    @pl.when((z > 0) & (z < depth - 1))
    def _(): pl.semaphore_wait(barrier, 5)

    def guarded(ok, run):
        if ok is None: run()
        else: pl.when(ok)(run)

    class Item:
        pass

    def make(i):
        src, out = ins[i], outs[i]
        flat = i in late
        rows = src.shape[0]
        half = rows // 2
        (own_sem, sz, rz, sxy, rxy, sc, rc) = sems[i * 7 : (i + 1) * 7]
        def at(d, s, lo=0, n=rows):
            first = s * 2 + core if flat else d * blocks + s * 2 + core
            return out.at[pl.ds(pl.multiple_of(first * rows + lo, 16 if half % 16 == 0 else 8), n)]
        def copy(a, b, ss, rs, to):
            return pltpu.make_async_remote_copy(src_ref=a, dst_ref=b, send_sem=ss, recv_sem=rs, device_id=to, device_id_type=MESH)
        def block(d, s):
            return at(d, s)
        it = Item()
        def local():
            return pltpu.make_async_copy(src, at(dp, z), own_sem)
        def up(s, ref): return copy(ref, at(dp, s), sz.at[0, s], rz.at[s], above)
        def down(s, ref): return copy(ref, at(dp, s), sz.at[1, s], rz.at[s], below)
        def to_x(s, ref): return copy(ref, at(dp, s), sxy.at[0, s], rxy.at[0, s], by_x)
        def to_y(s, ref): return copy(ref, at(dp, s), sxy.at[1, s], rxy.at[1, s], by_y)
        def half_y(s):
            return copy(at(x_at, s, 0, half), at(x_at, s, 0, half), sxy.at[2, s], rxy.at[2, s], by_y)
        def half_x(s):
            return copy(at(y_at, s, half, half), at(y_at, s, half, half), sxy.at[3, s], rxy.at[3, s], by_x)
        def to_core(r, d, s, ref): return copy(ref, at(d, s), sc.at[r, s], rc.at[r, s], sibling)
        def spread(s, ref):
            if not flat:
                to_x(s, ref).start(); to_y(s, ref).start()
            to_core(0, dp, s, ref).start()
        def start_up():
            up(z, src).start()
        def start_down():
            down(z, src).start()
        def start():
            local().start()
            if not flat:
                guarded(z < depth - 1, start_up)
                guarded(z > 0, start_down)
            spread(z, src)
        def z_event(s, ok, rising):
            def run():
                up(s, at(dp, s)).wait_recv()
                if rising: guarded(z < depth - 1, lambda: up(s, at(dp, s)).start())
                else: guarded(z > 0, lambda: down(s, at(dp, s)).start())
                spread(s, at(dp, s))
            pl.when(ok)(run)
        def near_event(s, ok):
            def run():
                to_x(s, at(dp, s)).wait_recv()
                half_y(s).start()
                to_core(1, x_at, s, at(x_at, s)).start()
                to_y(s, at(dp, s)).wait_recv()
                half_x(s).start()
                to_core(2, y_at, s, at(y_at, s)).start()
            guarded(ok, run)
        def far_event(s, ok):
            def run():
                half_y(s).wait_recv(); half_x(s).wait_recv()
                to_core(3, far_at, s, at(far_at, s)).start()
            guarded(ok, run)
        owners = (dp,) if flat else (dp, x_at, y_at, far_at)
        def core_wait(s):
            for r, d in enumerate(owners):
                to_core(r, d, s, at(d, s)).wait_recv()
        def finish():
            local().wait()
            for s in range(depth):
                if not flat:
                    for c in (to_x(s, at(dp, s)), to_y(s, at(dp, s)), half_y(s), half_x(s)): c.wait_send()
                for r, d in enumerate(owners): to_core(r, d, s, at(d, s)).wait_send()
                guarded((z >= s) & (z < depth - 1), lambda: up(s, at(dp, s)).wait_send())
                guarded((z <= s) & (z > 0), lambda: down(s, at(dp, s)).wait_send())
        it.start_up, it.start_down = start_up, start_down
        it.start, it.z_event, it.near_event, it.far_event, it.core_wait, it.finish = start, z_event, near_event, far_event, core_wait, finish
        return it
    items = [make(i) for i in range(count)]
    def around(d):
        if d == 0: return [(z, None, True)]
        return [(z - d, z >= d, True), (z + d, z + d < depth, False)]
    for n, phase in enumerate(phases):
        its = [items[i] for i in phase]
        for it in its: it.start()
        lates = [items[i] for i in late]
        for it in lates: it.start()
        def late_sends(d):
            for it in lates:
                if d < depth - 1:
                    pl.when(z == d)(it.start_up)
                    pl.when(z == depth - 1 - d)(it.start_down)
        late_sends(0)
        for d in range(1, depth + 2):
            if d < depth:
                for s, ok, rising in around(d):
                    for it in its: it.z_event(s, ok, rising)
                late_sends(d)
            if d - 1 < depth:
                for s, ok, _ in around(d - 1):
                    for it in its: it.near_event(s, ok)
            if d > 2:
                for s, ok, rising in around(d - 2):
                    for it in lates: it.z_event(s, ok, rising)
            if d - 2 >= 0:
                for s, ok, _ in around(d - 2):
                    for it in its: it.far_event(s, ok)
    for it in items:
        for s in range(depth): it.core_wait(s)
    for it in items: it.finish()

def gather_rows(arrays, phases, cid, late=()):
    shards = lax.axis_size("dp") * lax.axis_size("expert")
    depth = lax.axis_size("expert") // 2
    D = pltpu.SemaphoreType.DMA
    sems = []
    for _ in arrays:
        sems += [D, D((2, depth)), D((depth,)), D((4, depth)), D((4, depth)), D((4, depth)), D((4, depth))]
    return pl.pallas_call(
        functools.partial(gather_kernel, phases, len(arrays), late),
        out_shape=[
            jax.ShapeDtypeStruct(((2 * depth if i in late else shards) * a.shape[0],) + a.shape[1:], a.dtype)
            for i, a in enumerate(arrays)
        ],
        in_specs=[pl.BlockSpec(memory_space=pl.ANY)] * len(arrays),
        out_specs=[pl.BlockSpec(memory_space=pl.ANY)] * len(arrays),
        scratch_shapes=sems,
        compiler_params=pltpu.CompilerParams(collective_id=cid, has_side_effects=True),
        cost_estimate=pl.CostEstimate(flops=0, bytes_accessed=400_000_000, transcendentals=0),
    )(*arrays)


def reduce_kernel(rows, cuts, a_ref, extra_ref, b_ref, g_ref, o_ref, go_ref, sib, got, own, far, near, plane, got_z,
                  s0, r0, s1, r1, s2, r2, s3, r3, g_acc, g_got, g_z, gs, gr, gsz, grz):
    dp = lax.axis_index("dp"); member = lax.axis_index("expert")
    core = member % 2; z = member // 2
    sibling = (dp, member + 1 - 2 * core)
    by_x = (dp + 1 - 2 * (dp % 2), member)
    by_y = ((dp + 2) % 4, member)
    x_at, y_at = by_x[0], by_y[0]
    far_at = 3 - dp
    half = rows // 2
    depth = lax.axis_size("expert") // 2
    barrier = pltpu.get_barrier_semaphore()
    peers = [sibling, by_x, by_y] + [(dp, ((z + d) % depth) * 2 + core) for d in range(1, depth)]
    for peer in peers:
        pl.semaphore_signal(barrier, inc=1, device_id=peer, device_id_type=MESH)
    pl.semaphore_wait(barrier, len(peers))

    def pick(table):
        at = table[depth-1]
        for i in range(depth - 1):
            at = jnp.where(z == i, table[i], at)
        return at
    orders = [[3, 3, 0, 0], [2, 0, 3, 1], [1, 2, 1, 2], [0, 1, 2, 3]]
    targets = [pick(t) for t in orders]
    cols = b_ref.shape[1] // cuts

    def copy(src, dst, ssem, rsem, to):
        return pltpu.make_async_remote_copy(src_ref=src, dst_ref=dst, send_sem=ssem, recv_sem=rsem, device_id=to, device_id_type=MESH)

    blocks = 2 * depth
    piece = (rows - HD) // 2

    def product(half_of, k, put):
        spot = targets[k] * 2 + half_of

        def step(i, _):
            shard = (i // cuts) * blocks + spot
            at = (i // cuts) * rows
            col = pl.ds(pl.multiple_of((i % cuts) * cols, cols), cols)
            part = mm(a_ref[:, pl.ds(pl.multiple_of(shard * HD, HD), HD)], b_ref[:, col], TN)
            put(pl.ds(pl.multiple_of(at, 16), HD), col, part)
            if piece:
                base = (shard // PER_KV) * (2 * HD) + (shard % PER_KV) * piece
                small = jnp.concatenate(
                    [
                        extra_ref[pl.ds(pl.multiple_of(base, 16), piece), :],
                        extra_ref[pl.ds(pl.multiple_of(base + HD, 16), piece), :],
                    ],
                    axis=0,
                )
                put(pl.ds(pl.multiple_of(at + HD, 16), 2 * piece), col, mm(small, b_ref[:, col]))
            return 0

        lax.fori_loop(0, 4 * cuts, step, 0)

    def gain_hop(i, src, to):
        return copy(src, g_got.at[i, pl.ds(0, src.shape[0])], gs.at[i], gr.at[i], to)
    hops = {}
    def gain_step(i):
        rows4 = lambda at: pl.ds(pl.multiple_of(at * 8, 8), 8)
        if i == 0:
            hops[0] = gain_hop(0, g_ref.at[pl.ds(pl.multiple_of((1 - core) * 32, 32), 32)], sibling)
        elif i == 1:
            hops[0].wait_recv()
            g_acc[...] = g_ref[pl.ds(pl.multiple_of(core * 32, 32), 32)] + g_got[0]
            hops[1] = gain_hop(1, g_acc.at[pl.ds(pl.multiple_of((1 - dp // 2) * 16, 16), 16)], by_y)
        elif i == 2:
            hops[1].wait_recv()
            mine = pl.ds(pl.multiple_of((dp // 2) * 16, 16), 16)
            g_acc[mine] += g_got[1, :16]
            hops[2] = gain_hop(2, g_acc.at[rows4(x_at)], by_x)
        elif i == 3:
            hops[2].wait_recv()
            g_acc[rows4(dp)] += g_got[2, :8]
            for d in range(1, depth):
                to = (z + d) % depth
                hops[2 + d] = copy(g_acc.at[pl.ds(dp * 8 + to, 1)], g_z.at[z], gsz.at[d - 1], grz.at[z], (dp, to * 2 + core))
        if i < 3:
            hops[i].start()
        else:
            for d in range(1, depth):
                hops[2 + d].start()
    def gain_end():
        total = g_acc[pl.ds(dp * 8 + z, 1)]
        for d in range(1, depth):
            src = (z + d) % depth
            copy(g_acc.at[pl.ds(dp * 8, 1)], g_z.at[src], gsz.at[0], grz.at[src], sibling).wait_recv()
            total += g_z[src]
        go_ref[...] = total
        for i in hops:
            hops[i].wait_send()
    sib_copies, far_copies, near_copies, z_copies = {}, {}, {}, {}
    def sib_step(k):
        slot = k % 2
        if k >= 2:
            sib_copies[k - 2].wait_send()
        def put(r, c, part):
            sib[slot, r, c] = part.astype(bf16)
        product(1 - core, k, put)
        sib_copies[k] = copy(sib.at[slot], got.at[k], s0.at[slot], r0.at[k], sibling)
        sib_copies[k].start()
    def blk(at):
        return pl.ds(pl.multiple_of(at * rows, 16), rows)
    def own_step(k):
        sib_copies[k].wait_recv()
        def put(r, c, part):
            own[k, r, c] = (part + got[k, r, c].astype(f32)).astype(bf16)
        product(core, k, put)
        base = pl.multiple_of(far_at * rows, 16)
        far_copies[k] = (
            copy(own.at[k, pl.ds(base, half)], far.at[k, 0], s1.at[k, 0], r1.at[k, 0], by_x),
            copy(own.at[k, pl.ds(pl.multiple_of(base + half, 16), half)], far.at[k, 1], s1.at[k, 1], r1.at[k, 1], by_y),
        )
        for c in far_copies[k]: c.start()
    def near_step(k):
        a, b = far_copies[k]
        a.wait_recv()
        rng = pl.ds(pl.multiple_of(y_at * rows, 16), half)
        own[k, rng] = (own[k, rng].astype(f32) + far[k, 0].astype(f32)).astype(bf16)
        to_y = copy(own.at[k, blk(y_at)], near.at[k, 1], s2.at[k, 1], r2.at[k, 1], by_y)
        to_y.start()
        b.wait_recv()
        rng = pl.ds(pl.multiple_of(x_at * rows + half, 16), half)
        own[k, rng] = (own[k, rng].astype(f32) + far[k, 1].astype(f32)).astype(bf16)
        to_x = copy(own.at[k, blk(x_at)], near.at[k, 0], s2.at[k, 0], r2.at[k, 0], by_x)
        to_x.start()
        near_copies[k] = (to_x, to_y)
    def plane_step(k):
        for c in near_copies[k]: c.wait_recv()
        total = own[k, blk(dp)].astype(f32) + near[k, 0].astype(f32) + near[k, 1].astype(f32)
        if k < depth - 1:
            plane[k] = total.astype(bf16)
            to = (dp, targets[k] * 2 + core)
            z_copies[k] = copy(plane.at[k], got_z.at[z], s3.at[k], r3.at[z], to)
            z_copies[k].start()
        else:
            o_ref[...] = total
    gain_step(0)
    sib_step(0); sib_step(1)
    own_step(0)
    gain_step(1)
    sib_step(2)
    own_step(1)
    gain_step(2)
    near_step(0)
    sib_step(3)
    own_step(2)
    gain_step(3)
    near_step(1)
    plane_step(0)
    own_step(3)
    near_step(2)
    plane_step(1)
    near_step(3)
    plane_step(2)
    plane_step(3)
    for d in range(1, depth):
        src = (z + d) % depth
        copy(plane.at[0], got_z.at[src], s3.at[0], r3.at[src], sibling).wait_recv()
        o_ref[...] += got_z[src].astype(f32)
    gain_end()
    for k in range(depth):
        if k >= 2: sib_copies[k].wait_send()
        for c in far_copies[k]: c.wait_send()
        for c in near_copies[k]: c.wait_send()
        if k < depth - 1: z_copies[k].wait_send()

def reduce_rows(a, extra, b, cid, gains=None):
    tokens, width = b.shape
    depth = 4
    rows = HD + (0 if extra is None else extra.shape[0] // 32)
    if extra is None:
        extra = jnp.zeros((16, 128), bf16)
    D = pltpu.SemaphoreType.DMA
    lanes = 256
    padded = jnp.zeros((32, lanes), f32)
    if gains is not None:
        padded = jnp.pad(gains, ((0, 0), (0, lanes - gains.shape[1])))
    padded = padded.reshape(4, depth, 2, lanes).transpose(2, 0, 1, 3)
    padded = jnp.pad(padded, ((0, 0), (0, 0), (0, 8 - depth), (0, 0))).reshape(64, lanes)
    return pl.pallas_call(
        functools.partial(reduce_kernel, rows, 4),
        out_shape=[jax.ShapeDtypeStruct((rows, width), f32), jax.ShapeDtypeStruct((1, lanes), f32)],
        in_specs=[pl.BlockSpec(memory_space=pltpu.VMEM)] * 4,
        out_specs=[pl.BlockSpec(memory_space=pltpu.VMEM)] * 2,
        scratch_shapes=[
            pltpu.VMEM((2, 4 * rows, width), bf16),
            pltpu.VMEM((depth, 4 * rows, width), bf16),
            pltpu.VMEM((depth, 4 * rows, width), bf16),
            pltpu.VMEM((depth, 2, rows // 2, width), bf16),
            pltpu.VMEM((depth, 2, rows, width), bf16),
            pltpu.VMEM((depth - 1, rows, width), bf16),
            pltpu.VMEM((depth, rows, width), bf16),
            D((2,)), D((depth,)), D((depth, 2)), D((depth, 2)), D((depth, 2)), D((depth, 2)), D((depth - 1,)), D((depth,)),
            pltpu.VMEM((32, lanes), f32), pltpu.VMEM((3, 32, lanes), f32), pltpu.VMEM((depth, 1, lanes), f32),
            D((3,)), D((3,)), D((depth - 1,)), D((depth,)),
        ],
        compiler_params=pltpu.CompilerParams(vmem_limit_bytes=60*1024*1024, collective_id=cid, has_side_effects=True),
        cost_estimate=pl.CostEstimate(flops=2*tokens*32*rows*width, bytes_accessed=10_000_000, transcendentals=0),
    )(a, extra, b, padded)


ROUTE_LANES = 128


def picks_of(routing, first, local_experts, capacity):
    rows = routing.shape[0]
    lanes = lax.broadcasted_iota(jnp.int32, (rows, ROUTE_LANES), 1)
    places = lax.broadcasted_iota(jnp.int32, (rows, local_experts * capacity), 1)
    hit, weighted = None, 0.0
    for e in range(local_experts):

        def column(base):
            return jnp.sum(jnp.where(lanes == base + first + e, routing, 0.0), axis=1, keepdims=True)

        slot = column(0).astype(jnp.int32)
        here = places == jnp.where(slot >= 0, slot + e * capacity, -1)
        hit = here if hit is None else hit | here
        weighted = weighted + jnp.where(here, column(32) + column(64), 0.0)
    return jnp.where(hit, 1.0, 0.0).astype(bf16), weighted.astype(bf16)


def pick_kernel(capacity, local_experts, n_alias, tok_ref, cot_a, cot_b, *refs):
    x_ref, dy_ref = refs[n_alias:]
    width = cot_a.shape[3]
    cot = jnp.concatenate([cot_a[0, 0], cot_b[0, 0]], axis=0)
    first = lax.axis_index("expert") * local_experts
    routing = tok_ref[0, :, width:]
    hit, _ = picks_of(routing.astype(f32), first, local_experts, capacity)
    x = mm(hit, tok_ref[0, :, :width], TN).astype(bf16)
    rows = mm(hit, routing, TN)
    lanes = lax.broadcasted_iota(jnp.int32, rows.shape, 1)
    owner = lax.broadcasted_iota(jnp.int32, rows.shape, 0) // capacity
    at = lanes - first - owner
    weight = jnp.sum(jnp.where((at == 32) | (at == 64), rows, 0.0), axis=1, keepdims=True)
    dy = (mm(hit, cot, TN) * weight).astype(bf16)
    for e in range(local_experts):
        x_ref[e, 0, 0] = x[e * capacity : (e + 1) * capacity]
        dy_ref[e, 0, 0] = dy[e * capacity : (e + 1) * capacity]


def expert_kernel(n_alias, *refs):
    x_ref, dy_ref = refs[:2]
    parts = (refs[2:7], refs[7:12], refs[12:17])
    z_ref, dg_ref, du_ref, y_ref, dx_ref, wg, wu, wd, sems = refs[17 + n_alias :]
    local_experts, width, _ = wg.shape
    at = lax.axis_index("dp")
    size = width // 4
    places = (at, at + 1 - 2 * (at % 2), (at + 2) % 4, 3 - at, 3 - at)

    def copies(e):
        out = []
        for m, full in enumerate((wg, wu, wd)):
            for p in range(4):
                part = parts[m][p] if p < 3 else parts[m][3 + e]
                src = part.at[e] if p < 3 else part.at[0]
                where = pl.ds(pl.multiple_of(places[p] * size, size), size)
                dst = full.at[e, where, :] if m < 2 else full.at[e, :, where]
                out.append(pltpu.make_async_copy(src, dst, sems.at[e, m, p]))
        return out

    expert, chunk = pl.program_id(0), pl.program_id(1)

    @pl.when((expert == 0) & (chunk == 0))
    def _():
        for e in range(local_experts):
            for c in copies(e):
                c.start()

    for e in range(local_experts):

        @pl.when((expert == e) & (chunk == 0))
        def _(e=e):
            for c in copies(e):
                c.wait()

    x, dy = x_ref[0, 0], dy_ref[0, 0]
    gate = mm(x, wg[expert])
    up = mm(x, wu[expert])
    d_hidden = mm(dy, wd[expert], NT)
    sig = 1.0 / (1.0 + jnp.exp(-gate))
    silu = gate * sig
    z = (silu * up).astype(bf16)
    d_gate = (d_hidden * up * sig * (1.0 + gate * (1.0 - sig))).astype(bf16)
    d_up = (d_hidden * silu).astype(bf16)
    z_ref[0, 0] = z
    dg_ref[0, 0] = d_gate
    du_ref[0, 0] = d_up
    dx_ref[0] = (mm(d_gate, wg[expert], NT) + mm(d_up, wu[expert], NT)).astype(bf16)
    y_ref[0] = mm(z, wd[expert]).astype(bf16)


def sum_kernel(capacity, routing_ref, y_ref, dx_ref, mix_ref, da_ref):
    local_experts, _, _, width = y_ref.shape
    first = lax.axis_index("expert") * local_experts
    hit, weighted = picks_of(routing_ref[0].astype(f32), first, local_experts, capacity)
    da_ref[...] = mm(hit, dx_ref[...].reshape(local_experts * capacity, width)).astype(bf16)
    mix_ref[...] = mm(weighted, y_ref[...].reshape(local_experts * capacity, width)).astype(bf16)


def run_experts(tokens, cot, parts, capacity, batch_at, micro, earlier):
    blocks, rows, _ = tokens.shape
    width = cot[0][0].shape[3]
    local_experts, _, hidden = parts[0][0].shape
    flat = [p for group in parts for p in group]
    any_spec = pl.BlockSpec(memory_space=pl.ANY)
    params = pltpu.CompilerParams(vmem_limit_bytes=VMEM_LIMIT)
    slots = blocks * capacity
    picked_spec = pl.BlockSpec((local_experts, 1, 1, capacity, width), lambda b: (0, batch_at, b, 0, 0))
    picked = jax.ShapeDtypeStruct((local_experts, micro, blocks, capacity, width), bf16)
    x, dy = pl.pallas_call(
        functools.partial(pick_kernel, capacity, local_experts, len(earlier[:2])),
        grid=(blocks,),
        in_specs=[
            pl.BlockSpec((1, rows, tokens.shape[2]), lambda b: (b, 0, 0)),
        ]
        + [pl.BlockSpec((1, 1, rows // 2, width), lambda b, i=i: (b, i, 0, 0)) for _, i in cot]
        + [any_spec] * len(earlier[:2]),
        out_specs=[picked_spec] * 2,
        out_shape=[picked] * 2,
        input_output_aliases={3 + i: i for i in range(len(earlier[:2]))},
        compiler_params=params,
        cost_estimate=pl.CostEstimate(
            flops=4 * slots * local_experts * rows * width, bytes_accessed=25_000_000, transcendentals=0
        ),
    )(tokens, cot[0][0], cot[1][0], *[a.reshape(picked.shape) for a in earlier[:2]])
    x, dy = (a.reshape(local_experts, micro, slots, width) for a in (x, dy))
    chunk = slots // 2
    row_spec = pl.BlockSpec((1, 1, chunk, width), lambda e, i: (e, batch_at, i, 0))
    hid_spec = pl.BlockSpec((1, 1, chunk, hidden), lambda e, i: (e, batch_at, i, 0))
    out_spec = pl.BlockSpec((1, chunk, width), lambda e, i: (e, i, 0))
    hid = jax.ShapeDtypeStruct((local_experts, micro, slots, hidden), bf16)
    out = jax.ShapeDtypeStruct((local_experts, slots, width), bf16)
    z, dg, du, y, dx = pl.pallas_call(
        functools.partial(expert_kernel, len(earlier[2:])),
        grid=(local_experts, 2),
        in_specs=[row_spec, row_spec] + [any_spec] * (len(flat) + len(earlier[2:])),
        out_specs=[hid_spec] * 3 + [out_spec] * 2,
        out_shape=[hid] * 3 + [out] * 2,
        input_output_aliases={2 + len(flat) + i: i for i in range(len(earlier[2:]))},
        scratch_shapes=[
            pltpu.VMEM((local_experts, width, hidden), bf16),
            pltpu.VMEM((local_experts, width, hidden), bf16),
            pltpu.VMEM((local_experts, hidden, width), bf16),
            pltpu.SemaphoreType.DMA((local_experts, 3, 4)),
        ],
        compiler_params=params,
        cost_estimate=pl.CostEstimate(
            flops=12 * local_experts * slots * width * hidden, bytes_accessed=50_000_000, transcendentals=0
        ),
    )(x, dy, *flat, *earlier[2:])
    y, dx = (a.reshape(local_experts, blocks, capacity, width) for a in (y, dx))
    part_spec = pl.BlockSpec((local_experts, 1, capacity, width), lambda b: (0, b, 0, 0))
    sums = jax.ShapeDtypeStruct((blocks * rows, width), bf16)
    sums_spec = pl.BlockSpec((rows, width), lambda b: (b, 0))
    mix, da = pl.pallas_call(
        functools.partial(sum_kernel, capacity),
        grid=(blocks,),
        in_specs=[
            pl.BlockSpec((1, rows, ROUTE_LANES), lambda b: (b, 0, width // ROUTE_LANES)),
            part_spec,
            part_spec,
        ],
        out_specs=[sums_spec] * 2,
        out_shape=[sums] * 2,
        compiler_params=params,
        cost_estimate=pl.CostEstimate(
            flops=4 * slots * local_experts * rows * width, bytes_accessed=25_000_000, transcendentals=0
        ),
    )(tokens, y, dx)
    return [x, dy, z, dg, du], mix, da


def slots_of(route_ids, gate_vals, ranking, capacity, experts):
    rows = route_ids.shape[0]
    pair_experts = route_ids.reshape(-1)
    earlier = (pair_experts[None, :] == pair_experts[:, None]) & (
        ranking[None, :] < ranking[:, None]
    )
    slot = jnp.sum(earlier.astype(jnp.int32), axis=1).reshape(rows, -1)
    kept = slot < capacity
    chosen = route_ids[:, :, None] == jnp.arange(experts, dtype=jnp.int32)[None, None, :]
    chosen = chosen & kept[:, :, None]
    slot_map = jnp.sum(jnp.where(chosen, slot[:, :, None] + 1, 0), axis=1).astype(f32) - 1.0
    weight_map = jnp.sum(jnp.where(chosen, gate_vals[:, :, None], 0.0), axis=1)
    return slot_map, weight_map


def swap(values, bit):
    return lax.ppermute(values, "dp", [(i, i ^ bit) for i in range(lax.axis_size("dp"))])


def dp_part(total, axis, bits, expert, count=1):
    size = total.shape[axis] // 4
    start, sizes = [expert, 0, 0], list(total.shape)
    start[axis] = (lax.axis_index("dp") ^ bits) * size
    sizes[0], sizes[axis] = count, size
    return lax.dynamic_slice(total, start, sizes)


def scatter_far(total, axis):
    return swap(dp_part(total, axis, 3, 0), 1), swap(dp_part(total, axis, 3, 1), 2), total


def scatter_add(pieces, axis):
    for_y, for_x, total = pieces
    near_x = dp_part(total, axis, 1, 0, 2).astype(f32) + jnp.pad(for_x.astype(f32), ((1, 0), (0, 0), (0, 0)))
    near_y = dp_part(total, axis, 2, 0, 2).astype(f32) + jnp.pad(for_y.astype(f32), ((0, 1), (0, 0), (0, 0)))
    return near_x.astype(bf16), near_y.astype(bf16), total


def scatter_near(pieces, axis):
    near_x, near_y, total = scatter_add(pieces, axis)
    return swap(near_x, 1), swap(near_y, 2), total


def scatter_sum(pieces, axis):
    by_x, by_y, total = pieces
    return dp_part(total, axis, 0, 0, total.shape[0]).astype(f32) + by_x.astype(f32) + by_y.astype(f32)


def body_plain(
    inputs,
    cotangent,
    membership,
    routes,
    gate_weights,
    pair_order,
    w_query,
    w_key,
    w_value,
    w_output,
    norm_gains,
    w_gate,
    w_up,
    w_down,
):
    micro = inputs.shape[0]
    rows = inputs.shape[2]
    width = inputs.shape[3]
    group_len = membership.shape[2]
    member = lax.axis_index("expert")
    blocks = lax.axis_size("expert")
    shards = blocks * lax.axis_size("dp")
    shard_at = lax.axis_index("dp") * blocks + member
    local_experts = w_gate.shape[0]
    experts = local_experts * blocks
    capacity = rows * TOPK // experts
    step_heads = max(1, 384 // rows)
    total = micro * rows
    q_part, k_part, v_part = w_query.shape[1], w_key.shape[1], w_value.shape[1]

    gain_len = norm_gains.shape[0]
    gain_shard = jnp.zeros((2048,), bf16).at[:gain_len].set(norm_gains).reshape(16, 128)
    gain_full = lax.all_gather(gain_shard, BOTH, axis=0, tiled=True)
    gains = gain_full.reshape(shards, 2048)[:, :gain_len].reshape(-1).astype(f32)
    gain_in = gains[:width]
    gain_mid = gains[width : 2 * width]
    gain_q = gains[2 * width : 2 * width + HD]
    gain_k = gains[2 * width + HD :]

    qkv_w = lax.all_gather(
        jnp.concatenate([w_query.T, w_key.T, w_value.T], axis=0), BOTH, axis=0, tiled=True
    )
    out_w = lax.all_gather(w_output, BOTH, axis=0, tiled=True)
    wg = lax.all_gather(w_gate, "dp", axis=1, tiled=True)
    wu = lax.all_gather(w_up, "dp", axis=1, tiled=True)
    wd = lax.all_gather(w_down, "dp", axis=2, tiled=True)

    slot_map, weight_map = jax.vmap(
        lambda r, g, o: slots_of(r, g, o, capacity, experts)
    )(routes[:, 0], gate_weights[:, 0], pair_order[:, 0, 0])
    routing = jnp.concatenate([slot_map, weight_map], axis=-1)
    routing = lax.all_gather(routing, "expert", axis=0, tiled=False)
    mine = member * local_experts
    slot_mine = lax.dynamic_slice_in_dim(routing, mine, local_experts, axis=3)
    weight_mine = lax.dynamic_slice_in_dim(routing, experts + mine, local_experts, axis=3)
    slot_mine = jnp.transpose(slot_mine, (1, 3, 0, 2))
    weight_mine = jnp.transpose(weight_mine, (1, 3, 0, 2))
    slot_ids = jnp.arange(capacity, dtype=f32)
    hit = slot_mine[:, :, :, None, :] == slot_ids[None, None, None, :, None]
    pick = hit.astype(bf16)
    weighted = jnp.where(hit, weight_mine[:, :, :, None, :], 0.0)
    slot_weight = jnp.sum(weighted, axis=-1)
    weighted = weighted.astype(bf16)

    key_index = jnp.arange(group_len, dtype=jnp.int32)
    start_row = member * rows
    segment = membership[:, 0]
    row_index = start_row + jnp.arange(rows, dtype=jnp.int32)
    seg_rows = lax.dynamic_slice_in_dim(segment, start_row, rows, axis=1)
    before = jnp.sum((segment[:, None, :] < seg_rows[:, :, None]).astype(jnp.int32), axis=2)
    position = jnp.where(seg_rows == 0, row_index[None], PROMPT + row_index[None] - before)
    allowed = (key_index[None, :, None] <= row_index[None, None, :]) & (
        (segment[:, :, None] == 0) | (segment[:, :, None] == seg_rows[:, None, :])
    )
    bias = jnp.tile(jnp.where(allowed, 0.0, MASKED).astype(f32), (1, 1, step_heads))
    frequency = ROPE_BASE ** (-(jnp.arange(HD // 2, dtype=f32) * 2.0 / HD))
    angles = position.astype(f32).reshape(total)[:, None] * frequency[None, :]
    cosine = jnp.cos(angles)[:, None, :]
    sine_part = jnp.sin(angles)[:, None, :]

    hidden = inputs[:, 0].astype(f32).reshape(total, width)
    scale_in = rms_scale(hidden)
    normed = (hidden * scale_in * gain_in).astype(bf16)
    proj = mm(normed, qkv_w, NT).reshape(total, shards, q_part + k_part + v_part)
    queries = proj[:, :, :q_part].reshape(total, H, HD)
    key_pre = proj[:, :, q_part : q_part + k_part].reshape(total, KVH, HD)
    value = proj[:, :, q_part + k_part :].reshape(total, KVH, HD).astype(bf16)
    scale_q = rms_scale(queries)
    scale_k = rms_scale(key_pre)
    q_low = rotate(queries * scale_q * (gain_q * (SCALE * LOG2E)), cosine, sine_part).astype(bf16)
    q_low = q_low.reshape(micro, rows, H * HD)
    k_low = rotate(key_pre * scale_k * gain_k, cosine, sine_part).astype(bf16)
    kv_own = jnp.concatenate([k_low, value], axis=-1).reshape(micro, rows, KVH * 2 * HD)
    kv_all = lax.all_gather(kv_own, "expert", axis=0, tiled=False)
    chunk = 256
    mixed = []
    for at in range(micro):
        mixed = run_forward(q_low, kv_all[:, at : at + 1], bias, step_heads, chunk, at, mixed)
    mixed, logs = mixed

    branch = mm(mixed.reshape(total, H * HD), out_w)
    middle = hidden + branch
    scale_mid = rms_scale(middle)
    routed = (middle * scale_mid * gain_mid).astype(bf16).reshape(micro, rows, width)
    middle = middle.reshape(micro, rows, width)
    scale_mid = scale_mid.reshape(micro, rows, 1)

    outputs, d_branches, d_middles = [], [], []
    acc_gate = acc_up = acc_down = 0.0
    grad_mid = 0.0
    slots = blocks * capacity
    for at in range(micro):
        d_out = lax.all_gather(cotangent[at, 0], "expert", axis=0, tiled=False)
        tokens = lax.all_gather(routed[at], "expert", axis=0, tiled=False)
        picked = jnp.einsum("ebst,btd->ebsd", pick[at], tokens, preferred_element_type=f32)
        picked = picked.astype(bf16).reshape(local_experts, slots, width)
        d_result = jnp.einsum("ebst,btd->ebsd", pick[at], d_out, preferred_element_type=f32)
        d_result = (d_result * slot_weight[at][..., None]).astype(bf16)
        d_result = d_result.reshape(local_experts, slots, width)
        gate_pre = jnp.einsum("erd,edf->erf", picked, wg, preferred_element_type=f32)
        up_pre = jnp.einsum("erd,edf->erf", picked, wu, preferred_element_type=f32)
        d_hidden = jnp.einsum("erd,efd->erf", d_result, wd, preferred_element_type=f32)
        sigmoid_g = jax.nn.sigmoid(gate_pre)
        silu_g = gate_pre * sigmoid_g
        hidden_low = (silu_g * up_pre).astype(bf16)
        d_gate = (d_hidden * up_pre * sigmoid_g * (1.0 + gate_pre * (1.0 - sigmoid_g))).astype(bf16)
        d_up = (d_hidden * silu_g).astype(bf16)
        d_rows = jnp.einsum("erf,edf->erd", d_gate, wg, preferred_element_type=f32)
        d_rows = d_rows + jnp.einsum("erf,edf->erd", d_up, wu, preferred_element_type=f32)
        d_rows = d_rows.astype(bf16).reshape(local_experts, blocks, capacity, width)
        d_part = jnp.einsum("ebst,ebsd->btd", pick[at], d_rows, preferred_element_type=f32)
        d_part = d_part.astype(bf16).reshape(group_len, width)
        d_routed = lax.psum_scatter(d_part, "expert", scatter_dimension=0, tiled=True).astype(f32)
        result = jnp.einsum("erf,efd->erd", hidden_low, wd, preferred_element_type=f32)
        result = result.astype(bf16).reshape(local_experts, blocks, capacity, width)
        part = jnp.einsum("ebst,ebsd->btd", weighted[at], result, preferred_element_type=f32)
        part = part.astype(bf16).reshape(group_len, width)
        expert_mix = lax.psum_scatter(part, "expert", scatter_dimension=0, tiled=True).astype(f32)
        outputs.append((middle[at] + expert_mix).astype(bf16))

        acc_down += jnp.einsum("erf,erd->efd", hidden_low, d_result, preferred_element_type=f32)
        acc_gate += jnp.einsum("erd,erf->edf", picked, d_gate, preferred_element_type=f32)
        acc_up += jnp.einsum("erd,erf->edf", picked, d_up, preferred_element_type=f32)

        d_mid_norm, mid_gain_grad = norm_back(d_routed, middle[at], scale_mid[at], gain_mid)
        grad_mid = grad_mid + mid_gain_grad
        d_middle = cotangent[at, 0].astype(f32) + d_mid_norm
        d_middles.append(d_middle)
        d_branches.append(d_middle.astype(bf16))

    grad_gate = lax.psum_scatter(acc_gate.astype(bf16), "dp", scatter_dimension=1, tiled=True)
    grad_up = lax.psum_scatter(acc_up.astype(bf16), "dp", scatter_dimension=1, tiled=True)
    grad_down = lax.psum_scatter(acc_down.astype(bf16), "dp", scatter_dimension=2, tiled=True)

    d_branch = jnp.concatenate(d_branches, axis=0)
    d_middle = jnp.concatenate(d_middles, axis=0)
    grad_output = mm(mixed.reshape(total, H * HD), d_branch, TN).astype(bf16)
    grad_output = lax.psum_scatter(grad_output, BOTH, scatter_dimension=0, tiled=True)
    d_mixed = mm(d_branch, out_w, NT).astype(bf16).reshape(micro, rows, H * HD)
    cos_rows = jnp.concatenate([cosine, cosine], axis=-1).reshape(micro, rows, HD)
    sine_rows = jnp.concatenate([-sine_part, sine_part], axis=-1).reshape(micro, rows, HD)
    q_raw = queries.reshape(micro, rows, H * HD)
    d_query, dkv_list, grad_qn = [], [], 0.0
    for at in range(micro):
        d_query, dkv_one, part = run_backward(
            q_low, kv_all[:, at : at + 1], bias, mixed, d_mixed, logs, q_raw, cos_rows, sine_rows,
            gain_q[None, :], step_heads, chunk, at, [d_query] if at else []
        )
        dkv_list.append(dkv_one)
        grad_qn += part[0]
    dkv_all = jnp.concatenate(dkv_list, axis=1)
    dkv = lax.psum_scatter(dkv_all, "expert", scatter_dimension=0, tiled=False)
    dkv = dkv.reshape(total, KVH, 2 * HD)
    d_key = rotate(dkv[:, :, :HD].astype(f32), cosine, -sine_part)
    d_key, grad_kn = norm_back(d_key, key_pre, scale_k, gain_k)
    d_proj = jnp.concatenate(
        [
            d_query.reshape(total, shards, q_part),
            d_key.astype(bf16).reshape(total, shards, k_part),
            dkv[:, :, HD:].reshape(total, shards, v_part),
        ],
        axis=-1,
    ).reshape(total, -1)
    grad_qkv = mm(d_proj, normed, TN).astype(bf16)
    grad_qkv = lax.psum_scatter(grad_qkv, BOTH, scatter_dimension=0, tiled=True).astype(f32)
    d_normed = mm(d_proj, qkv_w)
    d_in_norm, grad_in = norm_back(d_normed, hidden, scale_in, gain_in)
    input_grad = d_middle + d_in_norm

    gain_grads = jnp.concatenate([grad_in, grad_mid, grad_qn, grad_kn]).reshape(shards, gain_len)
    gain_grads = jnp.pad(gain_grads, ((0, 0), (0, 256 - gain_len % 256)))
    gain_all = lax.all_gather(gain_grads, BOTH, axis=0, tiled=False)
    grad_gains = jnp.sum(lax.dynamic_index_in_dim(gain_all, shard_at, axis=1, keepdims=False), axis=0)
    return (
        jnp.stack(outputs)[:, None],
        input_grad.reshape(micro, 1, rows, width),
        grad_qkv[:q_part].T,
        grad_qkv[q_part : q_part + k_part].T,
        grad_qkv[q_part + k_part :].T,
        grad_output.astype(f32),
        grad_gains[:gain_len],
        grad_gate.astype(f32),
        grad_up.astype(f32),
        grad_down.astype(f32),
    )


def body_fast(
    inputs,
    cotangent,
    membership,
    routes,
    gate_weights,
    pair_order,
    w_query,
    w_key,
    w_value,
    w_output,
    norm_gains,
    w_gate,
    w_up,
    w_down,
):
    micro = inputs.shape[0]
    rows = inputs.shape[2]
    width = inputs.shape[3]
    group_len = membership.shape[2]
    member = lax.axis_index("expert")
    blocks = lax.axis_size("expert")
    shards = blocks * lax.axis_size("dp")
    local_experts = w_gate.shape[0]
    experts = local_experts * blocks
    capacity = rows * TOPK // experts
    step_heads = max(1, 384 // rows)
    total = micro * rows
    q_part, k_part, v_part = w_query.shape[1], w_key.shape[1], w_value.shape[1]
    tie = lax.optimization_barrier

    slot_map, weight_map = jax.vmap(
        lambda r, g, o: slots_of(r, g, o, capacity, experts)
    )(routes[:, 0], gate_weights[:, 0], pair_order[:, 0, 0])
    weight_high = tie(weight_map.astype(bf16))
    weight_low = (weight_map - weight_high.astype(f32)).astype(bf16)

    def padded(values, lanes):
        return jnp.pad(values, ((0, 0), (0, 0), (0, lanes - experts)))

    routing = jnp.concatenate(
        [
            padded(slot_map.astype(bf16), 32),
            padded(weight_high, 32),
            padded(weight_low, ROUTE_LANES - 64),
        ],
        axis=-1,
    )

    gain_len = norm_gains.shape[0]
    gain_shard = jnp.pad(norm_gains[None], ((0, 15), (0, 256 - gain_len)))
    kv_w = jnp.concatenate([w_key.T, w_value.T], axis=0)
    halves = cotangent.reshape(2 * micro, rows // 2, width)
    cot_first = halves[:3].reshape(-1, width)
    q_w, kv_w, out_w, gain_full, cot_first = gather_rows(
        [w_query.T, kv_w, w_output, gain_shard, cot_first], [(3, 0, 1, 2)], 1, (4,)
    )
    cot_first = cot_first.reshape(blocks, 3, rows // 2, width)
    q_w, w_gate = tie((q_w, w_gate))
    gains = gain_full.reshape(shards, 16, 256)[:, 0, :gain_len].reshape(-1).astype(f32)
    gain_in = gains[:width]
    gain_mid = gains[width : 2 * width]
    gain_q = gains[2 * width : 2 * width + HD]
    gain_k = gains[2 * width + HD :]
    gate_near = (swap(w_gate, 1), swap(w_gate, 2))

    key_index = jnp.arange(group_len, dtype=jnp.int32)
    start_row = member * rows
    segment = membership[:, 0]
    row_index = start_row + jnp.arange(rows, dtype=jnp.int32)
    seg_rows = lax.dynamic_slice_in_dim(segment, start_row, rows, axis=1)
    before = jnp.sum((segment[:, None, :] < seg_rows[:, :, None]).astype(jnp.int32), axis=2)
    position = jnp.where(seg_rows == 0, row_index[None], PROMPT + row_index[None] - before)
    allowed = (key_index[None, :, None] <= row_index[None, None, :]) & (
        (segment[:, :, None] == 0) | (segment[:, :, None] == seg_rows[:, None, :])
    )
    bias = jnp.tile(jnp.where(allowed, 0.0, MASKED).astype(f32), (1, 1, step_heads))
    frequency = ROPE_BASE ** (-(jnp.arange(HD // 2, dtype=f32) * 2.0 / HD))
    angles = position.astype(f32).reshape(total)[:, None] * frequency[None, :]
    cosine, sine = jnp.cos(angles), jnp.sin(angles)
    cosine = jnp.concatenate([cosine, cosine], axis=-1)
    sine = jnp.concatenate([-sine, sine], axis=-1)
    gain_q, gain_k = gain_q[None, :], gain_k[None, :]

    hidden = inputs[:, 0].astype(f32).reshape(total, width)
    scale_in = rms_scale(hidden)
    normed = (hidden * scale_in * gain_in).astype(bf16)
    q_low, q_raw, kv_own, k_raw, kv_w = run_project(
        normed, q_w, kv_w, cosine, sine, gain_q * (SCALE * LOG2E), gain_k
    )
    q_low, q_raw = (a.reshape(micro, rows, H * HD) for a in (q_low, q_raw))
    kv_own = kv_own.reshape(micro, rows, KVH * 2 * HD)
    kv_own, gate_near, w_up = tie((kv_own, gate_near, w_up))
    up_near = (swap(w_up, 1), swap(w_up, 2))
    kv_0 = lax.all_gather(kv_own[0], "expert", axis=0, tiled=False)
    kv_1 = lax.all_gather(kv_own[1], "expert", axis=0, tiled=False)
    kv_0, up_near, w_down = tie((kv_0, up_near, w_down))
    down_near = (swap(w_down, 1), swap(w_down, 2))
    chunk = 256
    mixed = run_forward(q_low, kv_0[:, None], bias, step_heads, chunk, 0, [], True)
    mixed, kv_1, cot_last = tie((mixed, kv_1, halves[3]))
    cot_last = lax.all_gather(cot_last, "expert", axis=0, tiled=False)[:, None]
    kv_all = [kv_0[:, None], kv_1[:, None]]
    mixed, logs, shares = run_forward(q_low, kv_all[1], bias, step_heads, chunk, 1, mixed, True)
    mixed, down_near = tie((mixed, down_near))
    parts = [
        (own, near[0], near[1], swap(near[0][:1], 2), swap(near[1][1:], 1))
        for own, near in ((w_gate, gate_near), (w_up, up_near), (w_down, down_near))
    ]

    branch = mm(mixed.reshape(total, H * HD), out_w)
    middle = hidden + branch
    scale_mid = rms_scale(middle)
    routed = (middle * scale_mid * gain_mid).astype(bf16).reshape(micro, rows, width)
    routed = jnp.concatenate([routed, routing], axis=-1)
    routed, cot_last = tie((routed, cot_last))
    cots = [((cot_first, 0), (cot_first, 1)), ((cot_first, 2), (cot_last, 0))]
    middle = middle.reshape(micro, rows, width)
    scale_mid = scale_mid.reshape(micro, rows, 1)

    mix_parts, d_routeds = [], []
    kept = []
    for at in range(micro):
        tokens = lax.all_gather(routed[at], "expert", axis=0, tiled=False)
        tokens, parts = tie((tokens, parts))
        kept, mix, d_part = run_experts(tokens, cots[at], parts, capacity, at, micro, kept)
        kept, d_part, mix, d_routeds = tie((kept, d_part, mix, d_routeds))
        mix_parts.append(mix)
        d_routed = lax.psum_scatter(d_part, "expert", scatter_dimension=0, tiled=True)
        d_routeds.append(d_routed)
    picked, d_result, hidden_low, d_gate, d_up = (
        a.reshape(local_experts, -1, a.shape[-1]) for a in kept
    )

    def weight_grad(rows_in, rows_out):
        return jnp.einsum("era,erb->eab", rows_in, rows_out, preferred_element_type=f32).astype(bf16)

    first = scatter_far(weight_grad(picked, d_gate), 1)
    second = scatter_far(weight_grad(picked, d_up), 1)
    first, hidden_low = tie((first, hidden_low))
    first = scatter_near(first, 1)
    third = weight_grad(hidden_low, d_result)
    d_routeds[-1], first, second, third, mix_parts[0] = tie(
        (d_routeds[-1], first, second, third, mix_parts[0])
    )
    second = scatter_near(second, 1)
    third = scatter_far(third, 2)
    d_mixed, d_middle, d_branch, grad_mid = run_middle_back(
        d_routeds, middle, cotangent[:, 0], gain_mid[None, :], out_w
    )
    d_mixed, d_branch, third = tie((d_mixed, d_branch, third))
    third = scatter_near(third, 2)
    d_mixed = d_mixed.reshape(micro, rows, H * HD)
    cos_rows, sine_rows = (a.reshape(micro, rows, HD) for a in (cosine, sine))
    def share(core):
        part = lax.dynamic_index_in_dim(shares, core, axis=0, keepdims=False)
        part = part.reshape(2, total, -1)
        return jnp.einsum("zta,td->zad", part, d_branch, preferred_element_type=f32).astype(bf16)

    core = member % 2
    pairs = [(i, i ^ 1) for i in range(blocks)]
    got = lax.ppermute(share(1 - core), "expert", pairs)
    mixes = [lax.psum_scatter(mix_parts[0], "expert", scatter_dimension=0, tiled=True)]

    def backward(at, earlier):
        d_query, dkv_one, part = run_backward(
            q_low, kv_all[at], bias, mixed, d_mixed, logs, q_raw, cos_rows, sine_rows, gain_q,
            step_heads, chunk, at, earlier
        )
        return d_query, dkv_one[:, 0], part

    d_query, dkv_0, gain_0 = backward(0, [])
    d_query, dkv_0, got, second = tie((d_query, dkv_0, got, second))
    dkv_0 = lax.psum_scatter(dkv_0, "expert", scatter_dimension=0, tiled=False)
    out_grad = tie(share(core))
    out_grad = (out_grad.astype(f32) + got.astype(f32)).astype(bf16)
    d_query, out_grad = tie((d_query, out_grad))
    out_grad = scatter_far(out_grad, 1)
    d_query, dkv_1, gain_1 = backward(1, [d_query])
    grad_qn = gain_0 + gain_1
    d_query, dkv_1, out_grad, mixes, third = tie((d_query, dkv_1, out_grad, mixes, third))
    dkv_1 = lax.psum_scatter(dkv_1, "expert", scatter_dimension=0, tiled=False)
    out_grad = scatter_add(out_grad, 1)
    out_grad, first, second, third, d_query = tie((out_grad, first, second, third, d_query))
    out_grad = (swap(out_grad[0], 1), swap(out_grad[1], 2), out_grad[2])
    out_grad = scatter_sum(out_grad, 1).astype(bf16).reshape(-1, width)
    d_query = d_query.reshape(total, H * HD)
    dkv = jnp.concatenate([dkv_0, dkv_1], axis=0)
    dkv = dkv.reshape(total, KVH * 2 * HD)
    mix_part, dkv = tie((mix_parts[1], dkv))
    mixes.append(lax.psum_scatter(mix_part, "expert", scatter_dimension=0, tiled=True))
    outputs = [(middle[at] + mixes[at].astype(f32)).astype(bf16) for at in range(micro)]
    expert_grads = [scatter_sum(first, 1), scatter_sum(second, 1), scatter_sum(third, 2)]
    d_normed = mm(d_query, q_w)
    dkv, out_grad, expert_grads, d_normed = tie((dkv, out_grad, expert_grads, d_normed))
    dkv, dkv_t, grad_kn = run_key_back(dkv, k_raw, cosine, sine, gain_k)
    d_normed = d_normed + mm(dkv, kv_w)
    grad_output = lax.psum_scatter(
        out_grad,
        "expert",
        scatter_dimension=0,
        tiled=True,
        axis_index_groups=[list(range(c, blocks, 2)) for c in range(2)],
    ).astype(f32)
    d_in_norm, grad_in = norm_back(d_normed, hidden, scale_in, gain_in)
    input_grad = d_middle + d_in_norm
    gain_grads = jnp.concatenate([grad_in, grad_mid[0], grad_qn[0], grad_kn[0]]).reshape(shards, gain_len)
    grad_qkv, grad_gains = reduce_rows(d_query, dkv_t, normed, 3, gain_grads)
    return (
        jnp.stack(outputs)[:, None],
        input_grad.reshape(micro, 1, rows, width),
        grad_qkv[:q_part].T,
        grad_qkv[q_part : q_part + k_part].T,
        grad_qkv[q_part + k_part :].T,
        grad_output,
        grad_gains[0, :gain_len],
        *expert_grads,
    )


def solution(mesh):
    fast = mesh.shape["dp"] == 4 and mesh.shape["expert"] == 8
    return jax.shard_map(
        body_fast if fast else body_plain,
        mesh=mesh,
        in_specs=(
            P(None, "dp", "expert", None),
            P(None, "dp", "expert", None),
            P(None, "dp", None),
            P(None, "dp", "expert", None),
            P(None, "dp", "expert", None),
            P(None, "dp", "expert", None),
            P(None, ("dp", "expert")),
            P(None, ("dp", "expert")),
            P(None, ("dp", "expert")),
            P(("dp", "expert"), None),
            P(("dp", "expert")),
            P("expert", "dp", None),
            P("expert", "dp", None),
            P("expert", None, "dp"),
        ),
        out_specs=(
            P(None, "dp", "expert", None),
            P(None, "dp", "expert", None),
            P(None, ("dp", "expert")),
            P(None, ("dp", "expert")),
            P(None, ("dp", "expert")),
            P(("dp", "expert"), None),
            P(("dp", "expert")),
            P("expert", "dp", None),
            P("expert", "dp", None),
            P("expert", None, "dp"),
        ),
        check_vma=False,
    )
```

```python
import functools
import math

import jax
import jax.numpy as jnp
from jax import lax
from jax.experimental import pallas as pl
from jax.experimental.pallas import tpu as pltpu
from jax.sharding import PartitionSpec as P

H = 32
KVH = 4
HD = 128
FF = 768
TOPK = 8
PROMPT = 1024
PER_KV = H // KVH

EPSILON = 1e-06
ROPE_BASE = 1000000.0
MASKED = -1e30
LOG2E = math.log2(math.e)
SCALE = HD ** (-0.5)

bf16 = jnp.bfloat16
f32 = jnp.float32
NT = (((1,), (1,)), ((), ()))
TN = (((0,), (0,)), ((), ()))
NN = (((1,), (0,)), ((), ()))
BOTH = ("dp", "expert")
VMEM_LIMIT = 56 * 1024 * 1024


def mm(a, b, dims=NN):
    return lax.dot_general(a, b, dims, preferred_element_type=f32)


def rms_scale(values):
    return lax.rsqrt(jnp.mean(values * values, axis=-1, keepdims=True) + EPSILON)


def norm_back(upstream, values, inv_rms, norm_gain):
    lifted = upstream * norm_gain
    inner_dot = jnp.mean(lifted * values, axis=-1, keepdims=True)
    back_grad = inv_rms * lifted - values * (inv_rms * inv_rms * inv_rms) * inner_dot
    gain_grad = jnp.sum((upstream * values * inv_rms).reshape(-1, values.shape[-1]), axis=0)
    return (back_grad, gain_grad)


def rotate(values, cosine, sine_part):
    half_dim = values.shape[-1] // 2
    first_half = values[..., :half_dim]
    second_half = values[..., half_dim:]
    return jnp.concatenate(
        [
            first_half * cosine - second_half * sine_part,
            second_half * cosine + first_half * sine_part,
        ],
        axis=-1,
    )


def turn(values, cosine, sine):
    return values * cosine + pltpu.roll(values, HD // 2, 1) * sine


def project(x_ref, wq_ref, wkv_ref, cos_ref, sin_ref, gq_ref, gk_ref, q_ref, qraw_ref, kv_ref, kraw_ref, wkv_out):
    x = x_ref[...]
    cosine, sine = cos_ref[...], sin_ref[...]
    for at in range(0, PER_KV * HD, 2 * HD):
        raw = mm(x, wq_ref[at : at + 2 * HD], NT)
        qraw_ref[:, at : at + 2 * HD] = raw
        for lane in (0, HD):
            head = raw[:, lane : lane + HD]
            normed = head * rms_scale(head) * gq_ref[...]
            q_ref[:, at + lane : at + lane + HD] = turn(normed, cosine, sine).astype(bf16)
    piece = HD // PER_KV
    w_k = [wkv_ref[2 * piece * i : 2 * piece * i + piece] for i in range(PER_KV)]
    w_v = [wkv_ref[2 * piece * i + piece : 2 * piece * (i + 1)] for i in range(PER_KV)]
    w_kv = jnp.concatenate(w_k + w_v, axis=0)
    wkv_out[...] = w_kv
    raw = mm(x, w_kv, NT)
    key = raw[:, :HD]
    kraw_ref[...] = key
    normed = key * rms_scale(key) * gk_ref[...]
    kv_ref[:, :HD] = turn(normed, cosine, sine).astype(bf16)
    kv_ref[:, HD:] = raw[:, HD:].astype(bf16)


def run_project(x, wq, wkv, cosine, sine, gain_q, gain_k):
    tokens, width = x.shape
    wide = PER_KV * HD
    whole = lambda a: pl.BlockSpec(a.shape, lambda g: (0, 0))
    cols = lambda n: pl.BlockSpec((tokens, n), lambda g: (0, g))
    rows = lambda n: pl.BlockSpec((n, width), lambda g: (g, 0))
    return pl.pallas_call(
        project,
        grid=(KVH,),
        in_specs=[whole(x), rows(wide), rows(2 * HD), whole(cosine), whole(sine), whole(gain_q), whole(gain_k)],
        out_specs=[cols(wide), cols(wide), cols(2 * HD), cols(HD), rows(2 * HD)],
        out_shape=[
            jax.ShapeDtypeStruct((tokens, H * HD), bf16),
            jax.ShapeDtypeStruct((tokens, H * HD), f32),
            jax.ShapeDtypeStruct((tokens, KVH * 2 * HD), bf16),
            jax.ShapeDtypeStruct((tokens, KVH * HD), f32),
            jax.ShapeDtypeStruct((KVH * 2 * HD, width), bf16),
        ],
        compiler_params=pltpu.CompilerParams(vmem_limit_bytes=VMEM_LIMIT),
        cost_estimate=pl.CostEstimate(
            flops=2 * tokens * width * (H + 2 * KVH) * HD, bytes_accessed=40_000_000, transcendentals=0
        ),
    )(x, wq, wkv, cosine, sine, gain_q, gain_k)


def norm_turn_back(grad, raw, cosine, sine, gain):
    grad = turn(grad, cosine, -sine)
    scale = rms_scale(raw)
    lifted = grad * gain
    inner = jnp.mean(lifted * raw, axis=-1, keepdims=True)
    back = scale * lifted - raw * (scale * scale * scale) * inner
    return back, jnp.sum(grad * raw * scale, axis=0, keepdims=True)


def key_back(dkv_ref, kraw_ref, cos_ref, sin_ref, gk_ref, out_ref, out_t_ref, gain_ref):
    gain_sum = 0.0
    for g in range(KVH):
        key = slice(2 * g * HD, (2 * g + 1) * HD)
        value = slice((2 * g + 1) * HD, (2 * g + 2) * HD)
        grad = dkv_ref[:, key].astype(f32)
        back, part = norm_turn_back(
            grad, kraw_ref[:, g * HD : (g + 1) * HD], cos_ref[...], sin_ref[...], gk_ref[...]
        )
        gain_sum += part
        low = back.astype(bf16)
        out_ref[:, key] = low
        out_t_ref[key] = low.T
        out_ref[:, value] = dkv_ref[:, value]
        out_t_ref[value] = dkv_ref[:, value].T
    gain_ref[...] = gain_sum


def run_key_back(dkv, key_raw, cosine, sine, gain):
    tokens, wide = dkv.shape
    return pl.pallas_call(
        key_back,
        out_shape=[
            jax.ShapeDtypeStruct((tokens, wide), bf16),
            jax.ShapeDtypeStruct((wide, tokens), bf16),
            jax.ShapeDtypeStruct((1, HD), f32),
        ],
        compiler_params=pltpu.CompilerParams(vmem_limit_bytes=VMEM_LIMIT),
    )(dkv, key_raw, cosine, sine, gain)


def attend_forward(step_heads, chunk, q_ref, kv_ref, bias_ref, o_ref, log_ref, o2_ref=None):
    group_len = bias_ref.shape[1]
    keys = kv_ref[:, 0, :, :HD].reshape(group_len, HD)
    values_t = kv_ref[:, 0, :, HD:].reshape(group_len, HD).T
    rows = q_ref.shape[1]
    for step in range(PER_KV // step_heads):
        heads = range(step * step_heads, (step + 1) * step_heads)
        query = jnp.concatenate([q_ref[0, :, h * HD : (h + 1) * HD] for h in heads], axis=0)
        mixed, row_sum = 0.0, 0.0
        for at in range(0, group_len, chunk):
            scores = mm(keys[at : at + chunk], query, NT)
            prob = jnp.exp2(scores + bias_ref[0, at : at + chunk, :])
            row_sum += jnp.sum(prob, axis=0, keepdims=True)
            mixed += mm(values_t[:, at : at + chunk], prob.astype(bf16))
        out = (mixed / row_sum).T.astype(bf16)
        for i, h in enumerate(heads):
            part = out[i * rows : (i + 1) * rows]
            o_ref[0, :, h * HD : (h + 1) * HD] = part
            if o2_ref is not None:
                lane = (h // 2) % 2 * HD
                o2_ref[h % 2, h // 4, 0, :, lane : lane + HD] = part
        log_ref[0, 0, step : step + 1, :] = jnp.log2(row_sum)


def attend_backward(
    step_heads, chunk, q_ref, kv_ref, bias_ref, o_ref, do_ref, log_ref, raw_ref, cos_ref, sin_ref, gain_ref,
    dq_ref, dkv_ref, gain_out, dk_acc, dv_acc
):
    group_len = bias_ref.shape[1]
    keys = kv_ref[:, 0, :, :HD].reshape(group_len, HD)
    values = kv_ref[:, 0, :, HD:].reshape(group_len, HD)
    keys_t = keys.T
    rows = q_ref.shape[1]
    cosine, sine, gain = cos_ref[0], sin_ref[0], gain_ref[...]

    @pl.when(pl.program_id(0) == 0)
    def _():
        gain_out[...] = jnp.zeros_like(gain_out)

    gain_sum = 0.0
    dk_acc[...] = jnp.zeros_like(dk_acc)
    dv_acc[...] = jnp.zeros_like(dv_acc)
    for step in range(PER_KV // step_heads):
        heads = range(step * step_heads, (step + 1) * step_heads)
        query = jnp.concatenate([q_ref[0, :, h * HD : (h + 1) * HD] for h in heads], axis=0)
        grad = jnp.concatenate([do_ref[0, :, h * HD : (h + 1) * HD] for h in heads], axis=0)
        mixed = jnp.concatenate([o_ref[0, :, h * HD : (h + 1) * HD] for h in heads], axis=0)
        row_dot = jnp.sum((grad.astype(f32) * mixed.astype(f32)).T, axis=0, keepdims=True)
        log_sum = log_ref[0, 0, step : step + 1, :]
        dq_t = 0.0
        for at in range(0, group_len, chunk):
            part = slice(at, at + chunk)
            scores = mm(keys[part], query, NT)
            prob = jnp.exp2(scores + (bias_ref[0, part, :] - log_sum))
            d_prob = mm(values[part], grad, NT)
            d_score = (prob * (d_prob - row_dot)).astype(bf16)
            dv_acc[part] += mm(prob.astype(bf16), grad)
            dk_acc[part] += mm(d_score, query)
            dq_t += mm(keys_t[:, part], d_score)
        out = (dq_t * SCALE).T.astype(bf16).astype(f32)
        for i, h in enumerate(heads):
            head = slice(h * HD, (h + 1) * HD)
            back, part = norm_turn_back(
                out[i * rows : (i + 1) * rows], raw_ref[0, :, head], cosine, sine, gain
            )
            dq_ref[0, :, head] = back.astype(bf16)
            gain_sum += part
    gain_out[...] += gain_sum
    blocks = dkv_ref.shape[0]
    dkv_ref[:, 0, :, :HD] = (dk_acc[...] * (1.0 / LOG2E)).astype(bf16).reshape(blocks, rows, HD)
    dkv_ref[:, 0, :, HD:] = dv_acc[...].astype(bf16).reshape(blocks, rows, HD)


def attention_specs(rows, group_len, blocks, step_heads, at):
    wide = PER_KV * HD
    q_spec = pl.BlockSpec((1, rows, wide), lambda g: (at, 0, g))
    kv_spec = pl.BlockSpec((blocks, 1, rows, 2 * HD), lambda g: (0, 0, 0, g))
    bias_spec = pl.BlockSpec((1, group_len, step_heads * rows), lambda g: (at, 0, 0))
    log_spec = pl.BlockSpec((1, 1, PER_KV // step_heads, step_heads * rows), lambda g: (at, g, 0, 0))
    return q_spec, kv_spec, bias_spec, log_spec


def run_forward(query, kv_all, bias, step_heads, chunk, at, earlier, again=False):
    micro, rows, _ = query.shape
    blocks = kv_all.shape[0]
    group_len = bias.shape[1]
    q_spec, kv_spec, bias_spec, log_spec = attention_specs(rows, group_len, blocks, step_heads, at)
    flops = 4 * rows * H * HD * group_len

    def kernel(*refs):
        attend_forward(step_heads, chunk, *refs[:3], *refs[3 + len(earlier) :])

    return pl.pallas_call(
        kernel,
        grid=(KVH,),
        in_specs=[q_spec, kv_spec, bias_spec] + [pl.BlockSpec(memory_space=pl.ANY)] * len(earlier),
        out_specs=[q_spec, log_spec]
        + again * [pl.BlockSpec((2, 2, 1, rows, 2 * HD), lambda g: (0, 0, at, 0, g))],
        out_shape=[
            jax.ShapeDtypeStruct(query.shape, bf16),
            jax.ShapeDtypeStruct((micro, KVH, PER_KV // step_heads, step_heads * rows), f32),
        ]
        + again * [jax.ShapeDtypeStruct((2, 2, micro, rows, KVH * 2 * HD), bf16)],
        input_output_aliases={3 + i: i for i in range(len(earlier))},
        compiler_params=pltpu.CompilerParams(vmem_limit_bytes=VMEM_LIMIT),
        cost_estimate=pl.CostEstimate(
            flops=flops, bytes_accessed=20_000_000, transcendentals=flops // (4 * HD)
        ),
    )(query, kv_all, bias, *earlier)


def run_backward(query, kv_all, bias, mixed, grad, logs, raw, cosine, sine, gain, step_heads, chunk, at, earlier):
    micro, rows, _ = query.shape
    blocks = kv_all.shape[0]
    group_len = bias.shape[1]
    q_spec, kv_spec, bias_spec, log_spec = attention_specs(rows, group_len, blocks, step_heads, at)
    flops = 10 * rows * H * HD * group_len
    gain_spec = pl.BlockSpec((1, HD), lambda g: (0, 0))

    def kernel(*refs):
        attend_backward(step_heads, chunk, *refs[:10], *refs[10 + len(earlier) :])

    return pl.pallas_call(
        kernel,
        grid=(KVH,),
        in_specs=[q_spec, kv_spec, bias_spec, q_spec, q_spec, log_spec, q_spec]
        + [pl.BlockSpec((1, rows, HD), lambda g: (at, 0, 0))] * 2
        + [gain_spec]
        + [pl.BlockSpec(memory_space=pl.ANY)] * len(earlier),
        out_specs=[q_spec, kv_spec, gain_spec],
        out_shape=[
            jax.ShapeDtypeStruct(query.shape, bf16),
            jax.ShapeDtypeStruct(kv_all.shape, bf16),
            jax.ShapeDtypeStruct((1, HD), f32),
        ],
        input_output_aliases={10 + i: i for i in range(len(earlier))},
        scratch_shapes=[pltpu.VMEM((group_len, HD), f32), pltpu.VMEM((group_len, HD), f32)],
        compiler_params=pltpu.CompilerParams(vmem_limit_bytes=VMEM_LIMIT),
        cost_estimate=pl.CostEstimate(
            flops=flops, bytes_accessed=30_000_000, transcendentals=flops // (10 * HD)
        ),
    )(query, kv_all, bias, mixed, grad, logs, raw, cosine, sine, gain, *earlier)


def middle_back(r0_ref, r1_ref, mid_ref, cot_ref, gain_ref, w_ref, mix_ref, dmid_ref, low_ref, gain_out):
    @pl.when(pl.program_id(0) == 0)
    def _():
        gain_sum = 0.0
        rows = r0_ref.shape[0]
        for b, ref in enumerate((r0_ref, r1_ref)):
            grad = ref[...].astype(f32)
            middle = mid_ref[b]
            scale = rms_scale(middle)
            lifted = grad * gain_ref[...]
            inner = jnp.mean(lifted * middle, axis=-1, keepdims=True)
            total = cot_ref[b].astype(f32) + scale * lifted - middle * (scale * scale * scale) * inner
            gain_sum += jnp.sum(grad * middle * scale, axis=0, keepdims=True)
            dmid_ref[b * rows : (b + 1) * rows] = total
            low_ref[b * rows : (b + 1) * rows] = total.astype(bf16)
        gain_out[...] = gain_sum

    mix_ref[...] = mm(low_ref[...], w_ref[...], NT).astype(bf16)


def run_middle_back(routed, middle, cot, gain, out_w):
    micro, rows, width = middle.shape
    total = micro * rows
    piece = 512
    whole = lambda *shape: pl.BlockSpec(shape, lambda i: (0,) * len(shape))
    return pl.pallas_call(
        middle_back,
        grid=(out_w.shape[0] // piece,),
        in_specs=[whole(rows, width)] * 2
        + [whole(micro, rows, width)] * 2
        + [whole(1, width), pl.BlockSpec((piece, width), lambda i: (i, 0))],
        out_specs=[
            pl.BlockSpec((total, piece), lambda i: (0, i)),
            whole(total, width),
            whole(total, width),
            whole(1, width),
        ],
        out_shape=[
            jax.ShapeDtypeStruct((total, out_w.shape[0]), bf16),
            jax.ShapeDtypeStruct((total, width), f32),
            jax.ShapeDtypeStruct((total, width), bf16),
            jax.ShapeDtypeStruct((1, width), f32),
        ],
        compiler_params=pltpu.CompilerParams(vmem_limit_bytes=VMEM_LIMIT),
        cost_estimate=pl.CostEstimate(
            flops=2 * total * width * out_w.shape[0], bytes_accessed=35_000_000, transcendentals=0
        ),
    )(*routed, middle, cot, gain, out_w)


MESH = pl.DeviceIdType.MESH


def gather_kernel(phases, count, late, *refs):
    ins, outs, sems = refs[:count], refs[count : 2 * count], refs[2 * count :]
    dp = lax.axis_index("dp"); member = lax.axis_index("expert")
    blocks = lax.axis_size("expert")
    core = member % 2; z = member // 2
    depth = blocks // 2
    sibling = (dp, member + 1 - 2 * core)
    by_x = (dp + 1 - 2 * (dp % 2), member)
    by_y = ((dp + 2) % 4, member)
    x_at, y_at, far_at = by_x[0], by_y[0], 3 - dp
    above, below = (dp, member + 2), (dp, member - 2)
    barrier = pltpu.get_barrier_semaphore()
    peers = [(sibling, None), (by_x, None), (by_y, None), (above, z < depth - 1), (below, z > 0)]
    for peer, ok in peers:
        if ok is None:
            pl.semaphore_signal(barrier, inc=1, device_id=peer, device_id_type=MESH)
        else:
            @pl.when(ok)
            def _(peer=peer):
                pl.semaphore_signal(barrier, inc=1, device_id=peer, device_id_type=MESH)
    @pl.when((z == 0) | (z == depth - 1))
    def _(): pl.semaphore_wait(barrier, 4)
    @pl.when((z > 0) & (z < depth - 1))
    def _(): pl.semaphore_wait(barrier, 5)

    def guarded(ok, run):
        if ok is None: run()
        else: pl.when(ok)(run)

    class Item:
        pass

    def make(i):
        src, out = ins[i], outs[i]
        flat = i in late
        rows = src.shape[0]
        half = rows // 2
        (own_sem, sz, rz, sxy, rxy, sc, rc) = sems[i * 7 : (i + 1) * 7]
        def at(d, s, lo=0, n=rows):
            first = s * 2 + core if flat else d * blocks + s * 2 + core
            return out.at[pl.ds(pl.multiple_of(first * rows + lo, 16 if half % 16 == 0 else 8), n)]
        def copy(a, b, ss, rs, to):
            return pltpu.make_async_remote_copy(src_ref=a, dst_ref=b, send_sem=ss, recv_sem=rs, device_id=to, device_id_type=MESH)
        def block(d, s):
            return at(d, s)
        it = Item()
        def local():
            return pltpu.make_async_copy(src, at(dp, z), own_sem)
        def up(s, ref): return copy(ref, at(dp, s), sz.at[0, s], rz.at[s], above)
        def down(s, ref): return copy(ref, at(dp, s), sz.at[1, s], rz.at[s], below)
        def to_x(s, ref): return copy(ref, at(dp, s), sxy.at[0, s], rxy.at[0, s], by_x)
        def to_y(s, ref): return copy(ref, at(dp, s), sxy.at[1, s], rxy.at[1, s], by_y)
        def half_y(s):
            return copy(at(x_at, s, 0, half), at(x_at, s, 0, half), sxy.at[2, s], rxy.at[2, s], by_y)
        def half_x(s):
            return copy(at(y_at, s, half, half), at(y_at, s, half, half), sxy.at[3, s], rxy.at[3, s], by_x)
        def to_core(r, d, s, ref): return copy(ref, at(d, s), sc.at[r, s], rc.at[r, s], sibling)
        def spread(s, ref):
            if not flat:
                to_x(s, ref).start(); to_y(s, ref).start()
            to_core(0, dp, s, ref).start()
        def start_up():
            up(z, src).start()
        def start_down():
            down(z, src).start()
        def start():
            local().start()
            if not flat:
                guarded(z < depth - 1, start_up)
                guarded(z > 0, start_down)
            spread(z, src)
        def z_event(s, ok, rising):
            def run():
                up(s, at(dp, s)).wait_recv()
                if rising: guarded(z < depth - 1, lambda: up(s, at(dp, s)).start())
                else: guarded(z > 0, lambda: down(s, at(dp, s)).start())
                spread(s, at(dp, s))
            pl.when(ok)(run)
        def near_event(s, ok):
            def run():
                to_x(s, at(dp, s)).wait_recv()
                half_y(s).start()
                to_core(1, x_at, s, at(x_at, s)).start()
                to_y(s, at(dp, s)).wait_recv()
                half_x(s).start()
                to_core(2, y_at, s, at(y_at, s)).start()
            guarded(ok, run)
        def far_event(s, ok):
            def run():
                half_y(s).wait_recv(); half_x(s).wait_recv()
                to_core(3, far_at, s, at(far_at, s)).start()
            guarded(ok, run)
        owners = (dp,) if flat else (dp, x_at, y_at, far_at)
        def core_wait(s):
            for r, d in enumerate(owners):
                to_core(r, d, s, at(d, s)).wait_recv()
        def finish():
            local().wait()
            for s in range(depth):
                if not flat:
                    for c in (to_x(s, at(dp, s)), to_y(s, at(dp, s)), half_y(s), half_x(s)): c.wait_send()
                for r, d in enumerate(owners): to_core(r, d, s, at(d, s)).wait_send()
                guarded((z >= s) & (z < depth - 1), lambda: up(s, at(dp, s)).wait_send())
                guarded((z <= s) & (z > 0), lambda: down(s, at(dp, s)).wait_send())
        it.start_up, it.start_down = start_up, start_down
        it.start, it.z_event, it.near_event, it.far_event, it.core_wait, it.finish = start, z_event, near_event, far_event, core_wait, finish
        return it
    items = [make(i) for i in range(count)]
    def around(d):
        if d == 0: return [(z, None, True)]
        return [(z - d, z >= d, True), (z + d, z + d < depth, False)]
    for n, phase in enumerate(phases):
        its = [items[i] for i in phase]
        for it in its: it.start()
        lates = [items[i] for i in late]
        for it in lates: it.start()
        def late_sends(d):
            for it in lates:
                if d < depth - 1:
                    pl.when(z == d)(it.start_up)
                    pl.when(z == depth - 1 - d)(it.start_down)
        late_sends(0)
        for d in range(1, depth + 2):
            if d < depth:
                for s, ok, rising in around(d):
                    for it in its: it.z_event(s, ok, rising)
                late_sends(d)
            if d - 1 < depth:
                for s, ok, _ in around(d - 1):
                    for it in its: it.near_event(s, ok)
            if d > 2:
                for s, ok, rising in around(d - 2):
                    for it in lates: it.z_event(s, ok, rising)
            if d - 2 >= 0:
                for s, ok, _ in around(d - 2):
                    for it in its: it.far_event(s, ok)
    for it in items:
        for s in range(depth): it.core_wait(s)
    for it in items: it.finish()

def gather_rows(arrays, phases, cid, late=()):
    shards = lax.axis_size("dp") * lax.axis_size("expert")
    depth = lax.axis_size("expert") // 2
    D = pltpu.SemaphoreType.DMA
    sems = []
    for _ in arrays:
        sems += [D, D((2, depth)), D((depth,)), D((4, depth)), D((4, depth)), D((4, depth)), D((4, depth))]
    return pl.pallas_call(
        functools.partial(gather_kernel, phases, len(arrays), late),
        out_shape=[
            jax.ShapeDtypeStruct(((2 * depth if i in late else shards) * a.shape[0],) + a.shape[1:], a.dtype)
            for i, a in enumerate(arrays)
        ],
        in_specs=[pl.BlockSpec(memory_space=pl.ANY)] * len(arrays),
        out_specs=[pl.BlockSpec(memory_space=pl.ANY)] * len(arrays),
        scratch_shapes=sems,
        compiler_params=pltpu.CompilerParams(collective_id=cid, has_side_effects=True),
        cost_estimate=pl.CostEstimate(flops=0, bytes_accessed=400_000_000, transcendentals=0),
    )(*arrays)


def reduce_kernel(rows, cuts, a_ref, extra_ref, b_ref, g_ref, o_ref, go_ref, sib, got, own, far, near, plane, got_z,
                  s0, r0, s1, r1, s2, r2, s3, r3, g_acc, g_got, g_z, gs, gr, gsz, grz):
    dp = lax.axis_index("dp"); member = lax.axis_index("expert")
    core = member % 2; z = member // 2
    sibling = (dp, member + 1 - 2 * core)
    by_x = (dp + 1 - 2 * (dp % 2), member)
    by_y = ((dp + 2) % 4, member)
    x_at, y_at = by_x[0], by_y[0]
    far_at = 3 - dp
    half = rows // 2
    depth = lax.axis_size("expert") // 2
    barrier = pltpu.get_barrier_semaphore()
    peers = [sibling, by_x, by_y] + [(dp, ((z + d) % depth) * 2 + core) for d in range(1, depth)]
    for peer in peers:
        pl.semaphore_signal(barrier, inc=1, device_id=peer, device_id_type=MESH)
    pl.semaphore_wait(barrier, len(peers))

    def pick(table):
        at = table[depth-1]
        for i in range(depth - 1):
            at = jnp.where(z == i, table[i], at)
        return at
    orders = [[3, 3, 0, 0], [2, 0, 3, 1], [1, 2, 1, 2], [0, 1, 2, 3]]
    targets = [pick(t) for t in orders]
    cols = b_ref.shape[1] // cuts

    def copy(src, dst, ssem, rsem, to):
        return pltpu.make_async_remote_copy(src_ref=src, dst_ref=dst, send_sem=ssem, recv_sem=rsem, device_id=to, device_id_type=MESH)

    blocks = 2 * depth
    piece = (rows - HD) // 2

    def product(half_of, k, put):
        spot = targets[k] * 2 + half_of

        def step(i, _):
            shard = (i // cuts) * blocks + spot
            at = (i // cuts) * rows
            col = pl.ds(pl.multiple_of((i % cuts) * cols, cols), cols)
            part = mm(a_ref[:, pl.ds(pl.multiple_of(shard * HD, HD), HD)], b_ref[:, col], TN)
            put(pl.ds(pl.multiple_of(at, 16), HD), col, part)
            if piece:
                base = (shard // PER_KV) * (2 * HD) + (shard % PER_KV) * piece
                small = jnp.concatenate(
                    [
                        extra_ref[pl.ds(pl.multiple_of(base, 16), piece), :],
                        extra_ref[pl.ds(pl.multiple_of(base + HD, 16), piece), :],
                    ],
                    axis=0,
                )
                put(pl.ds(pl.multiple_of(at + HD, 16), 2 * piece), col, mm(small, b_ref[:, col]))
            return 0

        lax.fori_loop(0, 4 * cuts, step, 0)

    def gain_hop(i, src, to):
        return copy(src, g_got.at[i, pl.ds(0, src.shape[0])], gs.at[i], gr.at[i], to)
    hops = {}
    def gain_step(i):
        rows4 = lambda at: pl.ds(pl.multiple_of(at * 8, 8), 8)
        if i == 0:
            hops[0] = gain_hop(0, g_ref.at[pl.ds(pl.multiple_of((1 - core) * 32, 32), 32)], sibling)
        elif i == 1:
            hops[0].wait_recv()
            g_acc[...] = g_ref[pl.ds(pl.multiple_of(core * 32, 32), 32)] + g_got[0]
            hops[1] = gain_hop(1, g_acc.at[pl.ds(pl.multiple_of((1 - dp // 2) * 16, 16), 16)], by_y)
        elif i == 2:
            hops[1].wait_recv()
            mine = pl.ds(pl.multiple_of((dp // 2) * 16, 16), 16)
            g_acc[mine] += g_got[1, :16]
            hops[2] = gain_hop(2, g_acc.at[rows4(x_at)], by_x)
        elif i == 3:
            hops[2].wait_recv()
            g_acc[rows4(dp)] += g_got[2, :8]
            for d in range(1, depth):
                to = (z + d) % depth
                hops[2 + d] = copy(g_acc.at[pl.ds(dp * 8 + to, 1)], g_z.at[z], gsz.at[d - 1], grz.at[z], (dp, to * 2 + core))
        if i < 3:
            hops[i].start()
        else:
            for d in range(1, depth):
                hops[2 + d].start()
    def gain_end():
        total = g_acc[pl.ds(dp * 8 + z, 1)]
        for d in range(1, depth):
            src = (z + d) % depth
            copy(g_acc.at[pl.ds(dp * 8, 1)], g_z.at[src], gsz.at[0], grz.at[src], sibling).wait_recv()
            total += g_z[src]
        go_ref[...] = total
        for i in hops:
            hops[i].wait_send()
    sib_copies, far_copies, near_copies, z_copies = {}, {}, {}, {}
    def sib_step(k):
        slot = k % 2
        if k >= 2:
            sib_copies[k - 2].wait_send()
        def put(r, c, part):
            sib[slot, r, c] = part.astype(bf16)
        product(1 - core, k, put)
        sib_copies[k] = copy(sib.at[slot], got.at[k], s0.at[slot], r0.at[k], sibling)
        sib_copies[k].start()
    def blk(at):
        return pl.ds(pl.multiple_of(at * rows, 16), rows)
    def own_step(k):
        sib_copies[k].wait_recv()
        def put(r, c, part):
            own[k, r, c] = (part + got[k, r, c].astype(f32)).astype(bf16)
        product(core, k, put)
        base = pl.multiple_of(far_at * rows, 16)
        far_copies[k] = (
            copy(own.at[k, pl.ds(base, half)], far.at[k, 0], s1.at[k, 0], r1.at[k, 0], by_x),
            copy(own.at[k, pl.ds(pl.multiple_of(base + half, 16), half)], far.at[k, 1], s1.at[k, 1], r1.at[k, 1], by_y),
        )
        for c in far_copies[k]: c.start()
    def near_step(k):
        a, b = far_copies[k]
        a.wait_recv()
        rng = pl.ds(pl.multiple_of(y_at * rows, 16), half)
        own[k, rng] = (own[k, rng].astype(f32) + far[k, 0].astype(f32)).astype(bf16)
        to_y = copy(own.at[k, blk(y_at)], near.at[k, 1], s2.at[k, 1], r2.at[k, 1], by_y)
        to_y.start()
        b.wait_recv()
        rng = pl.ds(pl.multiple_of(x_at * rows + half, 16), half)
        own[k, rng] = (own[k, rng].astype(f32) + far[k, 1].astype(f32)).astype(bf16)
        to_x = copy(own.at[k, blk(x_at)], near.at[k, 0], s2.at[k, 0], r2.at[k, 0], by_x)
        to_x.start()
        near_copies[k] = (to_x, to_y)
    def plane_step(k):
        for c in near_copies[k]: c.wait_recv()
        total = own[k, blk(dp)].astype(f32) + near[k, 0].astype(f32) + near[k, 1].astype(f32)
        if k < depth - 1:
            plane[k] = total.astype(bf16)
            to = (dp, targets[k] * 2 + core)
            z_copies[k] = copy(plane.at[k], got_z.at[z], s3.at[k], r3.at[z], to)
            z_copies[k].start()
        else:
            o_ref[...] = total
    gain_step(0)
    sib_step(0); sib_step(1)
    own_step(0)
    gain_step(1)
    sib_step(2)
    own_step(1)
    gain_step(2)
    near_step(0)
    sib_step(3)
    own_step(2)
    gain_step(3)
    near_step(1)
    plane_step(0)
    own_step(3)
    near_step(2)
    plane_step(1)
    near_step(3)
    plane_step(2)
    plane_step(3)
    for d in range(1, depth):
        src = (z + d) % depth
        copy(plane.at[0], got_z.at[src], s3.at[0], r3.at[src], sibling).wait_recv()
        o_ref[...] += got_z[src].astype(f32)
    gain_end()
    for k in range(depth):
        if k >= 2: sib_copies[k].wait_send()
        for c in far_copies[k]: c.wait_send()
        for c in near_copies[k]: c.wait_send()
        if k < depth - 1: z_copies[k].wait_send()

def reduce_rows(a, extra, b, cid, gains=None):
    tokens, width = b.shape
    depth = 4
    rows = HD + (0 if extra is None else extra.shape[0] // 32)
    if extra is None:
        extra = jnp.zeros((16, 128), bf16)
    D = pltpu.SemaphoreType.DMA
    lanes = 256
    padded = jnp.zeros((32, lanes), f32)
    if gains is not None:
        padded = jnp.pad(gains, ((0, 0), (0, lanes - gains.shape[1])))
    padded = padded.reshape(4, depth, 2, lanes).transpose(2, 0, 1, 3)
    padded = jnp.pad(padded, ((0, 0), (0, 0), (0, 8 - depth), (0, 0))).reshape(64, lanes)
    return pl.pallas_call(
        functools.partial(reduce_kernel, rows, 4),
        out_shape=[jax.ShapeDtypeStruct((rows, width), f32), jax.ShapeDtypeStruct((1, lanes), f32)],
        in_specs=[pl.BlockSpec(memory_space=pltpu.VMEM)] * 4,
        out_specs=[pl.BlockSpec(memory_space=pltpu.VMEM)] * 2,
        scratch_shapes=[
            pltpu.VMEM((2, 4 * rows, width), bf16),
            pltpu.VMEM((depth, 4 * rows, width), bf16),
            pltpu.VMEM((depth, 4 * rows, width), bf16),
            pltpu.VMEM((depth, 2, rows // 2, width), bf16),
            pltpu.VMEM((depth, 2, rows, width), bf16),
            pltpu.VMEM((depth - 1, rows, width), bf16),
            pltpu.VMEM((depth, rows, width), bf16),
            D((2,)), D((depth,)), D((depth, 2)), D((depth, 2)), D((depth, 2)), D((depth, 2)), D((depth - 1,)), D((depth,)),
            pltpu.VMEM((32, lanes), f32), pltpu.VMEM((3, 32, lanes), f32), pltpu.VMEM((depth, 1, lanes), f32),
            D((3,)), D((3,)), D((depth - 1,)), D((depth,)),
        ],
        compiler_params=pltpu.CompilerParams(vmem_limit_bytes=60*1024*1024, collective_id=cid, has_side_effects=True),
        cost_estimate=pl.CostEstimate(flops=2*tokens*32*rows*width, bytes_accessed=10_000_000, transcendentals=0),
    )(a, extra, b, padded)


ROUTE_LANES = 128


def picks_of(routing, first, local_experts, capacity):
    rows = routing.shape[0]
    lanes = lax.broadcasted_iota(jnp.int32, (rows, ROUTE_LANES), 1)
    places = lax.broadcasted_iota(jnp.int32, (rows, local_experts * capacity), 1)
    hit, weighted = None, 0.0
    for e in range(local_experts):

        def column(base):
            return jnp.sum(jnp.where(lanes == base + first + e, routing, 0.0), axis=1, keepdims=True)

        slot = column(0).astype(jnp.int32)
        here = places == jnp.where(slot >= 0, slot + e * capacity, -1)
        hit = here if hit is None else hit | here
        weighted = weighted + jnp.where(here, column(32) + column(64), 0.0)
    return jnp.where(hit, 1.0, 0.0).astype(bf16), weighted.astype(bf16)


def pick_kernel(capacity, local_experts, n_alias, tok_ref, cot_a, cot_b, *refs):
    x_ref, dy_ref = refs[n_alias:]
    width = cot_a.shape[3]
    cot = jnp.concatenate([cot_a[0, 0], cot_b[0, 0]], axis=0)
    first = lax.axis_index("expert") * local_experts
    routing = tok_ref[0, :, width:]
    hit, _ = picks_of(routing.astype(f32), first, local_experts, capacity)
    x = mm(hit, tok_ref[0, :, :width], TN).astype(bf16)
    rows = mm(hit, routing, TN)
    lanes = lax.broadcasted_iota(jnp.int32, rows.shape, 1)
    owner = lax.broadcasted_iota(jnp.int32, rows.shape, 0) // capacity
    at = lanes - first - owner
    weight = jnp.sum(jnp.where((at == 32) | (at == 64), rows, 0.0), axis=1, keepdims=True)
    dy = (mm(hit, cot, TN) * weight).astype(bf16)
    for e in range(local_experts):
        x_ref[e, 0, 0] = x[e * capacity : (e + 1) * capacity]
        dy_ref[e, 0, 0] = dy[e * capacity : (e + 1) * capacity]


def expert_kernel(n_alias, *refs):
    x_ref, dy_ref = refs[:2]
    parts = (refs[2:7], refs[7:12], refs[12:17])
    z_ref, dg_ref, du_ref, y_ref, dx_ref, wg, wu, wd, sems = refs[17 + n_alias :]
    local_experts, width, _ = wg.shape
    at = lax.axis_index("dp")
    size = width // 4
    places = (at, at + 1 - 2 * (at % 2), (at + 2) % 4, 3 - at, 3 - at)

    def copies(e):
        out = []
        for m, full in enumerate((wg, wu, wd)):
            for p in range(4):
                part = parts[m][p] if p < 3 else parts[m][3 + e]
                src = part.at[e] if p < 3 else part.at[0]
                where = pl.ds(pl.multiple_of(places[p] * size, size), size)
                dst = full.at[e, where, :] if m < 2 else full.at[e, :, where]
                out.append(pltpu.make_async_copy(src, dst, sems.at[e, m, p]))
        return out

    expert, chunk = pl.program_id(0), pl.program_id(1)

    @pl.when((expert == 0) & (chunk == 0))
    def _():
        for e in range(local_experts):
            for c in copies(e):
                c.start()

    for e in range(local_experts):

        @pl.when((expert == e) & (chunk == 0))
        def _(e=e):
            for c in copies(e):
                c.wait()

    x, dy = x_ref[0, 0], dy_ref[0, 0]
    gate = mm(x, wg[expert])
    up = mm(x, wu[expert])
    d_hidden = mm(dy, wd[expert], NT)
    sig = 1.0 / (1.0 + jnp.exp(-gate))
    silu = gate * sig
    z = (silu * up).astype(bf16)
    d_gate = (d_hidden * up * sig * (1.0 + gate * (1.0 - sig))).astype(bf16)
    d_up = (d_hidden * silu).astype(bf16)
    z_ref[0, 0] = z
    dg_ref[0, 0] = d_gate
    du_ref[0, 0] = d_up
    dx_ref[0] = (mm(d_gate, wg[expert], NT) + mm(d_up, wu[expert], NT)).astype(bf16)
    y_ref[0] = mm(z, wd[expert]).astype(bf16)


def sum_kernel(capacity, routing_ref, y_ref, dx_ref, mix_ref, da_ref):
    local_experts, _, _, width = y_ref.shape
    first = lax.axis_index("expert") * local_experts
    hit, weighted = picks_of(routing_ref[0].astype(f32), first, local_experts, capacity)
    da_ref[...] = mm(hit, dx_ref[...].reshape(local_experts * capacity, width)).astype(bf16)
    mix_ref[...] = mm(weighted, y_ref[...].reshape(local_experts * capacity, width)).astype(bf16)


def run_experts(tokens, cot, parts, capacity, batch_at, micro, earlier):
    blocks, rows, _ = tokens.shape
    width = cot[0][0].shape[3]
    local_experts, _, hidden = parts[0][0].shape
    flat = [p for group in parts for p in group]
    any_spec = pl.BlockSpec(memory_space=pl.ANY)
    params = pltpu.CompilerParams(vmem_limit_bytes=VMEM_LIMIT)
    slots = blocks * capacity
    picked_spec = pl.BlockSpec((local_experts, 1, 1, capacity, width), lambda b: (0, batch_at, b, 0, 0))
    picked = jax.ShapeDtypeStruct((local_experts, micro, blocks, capacity, width), bf16)
    x, dy = pl.pallas_call(
        functools.partial(pick_kernel, capacity, local_experts, len(earlier[:2])),
        grid=(blocks,),
        in_specs=[
            pl.BlockSpec((1, rows, tokens.shape[2]), lambda b: (b, 0, 0)),
        ]
        + [pl.BlockSpec((1, 1, rows // 2, width), lambda b, i=i: (b, i, 0, 0)) for _, i in cot]
        + [any_spec] * len(earlier[:2]),
        out_specs=[picked_spec] * 2,
        out_shape=[picked] * 2,
        input_output_aliases={3 + i: i for i in range(len(earlier[:2]))},
        compiler_params=params,
        cost_estimate=pl.CostEstimate(
            flops=4 * slots * local_experts * rows * width, bytes_accessed=25_000_000, transcendentals=0
        ),
    )(tokens, cot[0][0], cot[1][0], *[a.reshape(picked.shape) for a in earlier[:2]])
    x, dy = (a.reshape(local_experts, micro, slots, width) for a in (x, dy))
    chunk = slots // 2
    row_spec = pl.BlockSpec((1, 1, chunk, width), lambda e, i: (e, batch_at, i, 0))
    hid_spec = pl.BlockSpec((1, 1, chunk, hidden), lambda e, i: (e, batch_at, i, 0))
    out_spec = pl.BlockSpec((1, chunk, width), lambda e, i: (e, i, 0))
    hid = jax.ShapeDtypeStruct((local_experts, micro, slots, hidden), bf16)
    out = jax.ShapeDtypeStruct((local_experts, slots, width), bf16)
    z, dg, du, y, dx = pl.pallas_call(
        functools.partial(expert_kernel, len(earlier[2:])),
        grid=(local_experts, 2),
        in_specs=[row_spec, row_spec] + [any_spec] * (len(flat) + len(earlier[2:])),
        out_specs=[hid_spec] * 3 + [out_spec] * 2,
        out_shape=[hid] * 3 + [out] * 2,
        input_output_aliases={2 + len(flat) + i: i for i in range(len(earlier[2:]))},
        scratch_shapes=[
            pltpu.VMEM((local_experts, width, hidden), bf16),
            pltpu.VMEM((local_experts, width, hidden), bf16),
            pltpu.VMEM((local_experts, hidden, width), bf16),
            pltpu.SemaphoreType.DMA((local_experts, 3, 4)),
        ],
        compiler_params=params,
        cost_estimate=pl.CostEstimate(
            flops=12 * local_experts * slots * width * hidden, bytes_accessed=50_000_000, transcendentals=0
        ),
    )(x, dy, *flat, *earlier[2:])
    y, dx = (a.reshape(local_experts, blocks, capacity, width) for a in (y, dx))
    part_spec = pl.BlockSpec((local_experts, 1, capacity, width), lambda b: (0, b, 0, 0))
    sums = jax.ShapeDtypeStruct((blocks * rows, width), bf16)
    sums_spec = pl.BlockSpec((rows, width), lambda b: (b, 0))
    mix, da = pl.pallas_call(
        functools.partial(sum_kernel, capacity),
        grid=(blocks,),
        in_specs=[
            pl.BlockSpec((1, rows, ROUTE_LANES), lambda b: (b, 0, width // ROUTE_LANES)),
            part_spec,
            part_spec,
        ],
        out_specs=[sums_spec] * 2,
        out_shape=[sums] * 2,
        compiler_params=params,
        cost_estimate=pl.CostEstimate(
            flops=4 * slots * local_experts * rows * width, bytes_accessed=25_000_000, transcendentals=0
        ),
    )(tokens, y, dx)
    return [x, dy, z, dg, du], mix, da


def slots_of(route_ids, gate_vals, ranking, capacity, experts):
    rows = route_ids.shape[0]
    pair_experts = route_ids.reshape(-1)
    earlier = (pair_experts[None, :] == pair_experts[:, None]) & (
        ranking[None, :] < ranking[:, None]
    )
    slot = jnp.sum(earlier.astype(jnp.int32), axis=1).reshape(rows, -1)
    kept = slot < capacity
    chosen = route_ids[:, :, None] == jnp.arange(experts, dtype=jnp.int32)[None, None, :]
    chosen = chosen & kept[:, :, None]
    slot_map = jnp.sum(jnp.where(chosen, slot[:, :, None] + 1, 0), axis=1).astype(f32) - 1.0
    weight_map = jnp.sum(jnp.where(chosen, gate_vals[:, :, None], 0.0), axis=1)
    return slot_map, weight_map


def swap(values, bit):
    return lax.ppermute(values, "dp", [(i, i ^ bit) for i in range(lax.axis_size("dp"))])


def dp_part(total, axis, bits, expert, count=1):
    size = total.shape[axis] // 4
    start, sizes = [expert, 0, 0], list(total.shape)
    start[axis] = (lax.axis_index("dp") ^ bits) * size
    sizes[0], sizes[axis] = count, size
    return lax.dynamic_slice(total, start, sizes)


def scatter_far(total, axis):
    return swap(dp_part(total, axis, 3, 0), 1), swap(dp_part(total, axis, 3, 1), 2), total


def scatter_add(pieces, axis):
    for_y, for_x, total = pieces
    near_x = dp_part(total, axis, 1, 0, 2).astype(f32) + jnp.pad(for_x.astype(f32), ((1, 0), (0, 0), (0, 0)))
    near_y = dp_part(total, axis, 2, 0, 2).astype(f32) + jnp.pad(for_y.astype(f32), ((0, 1), (0, 0), (0, 0)))
    return near_x.astype(bf16), near_y.astype(bf16), total


def scatter_near(pieces, axis):
    near_x, near_y, total = scatter_add(pieces, axis)
    return swap(near_x, 1), swap(near_y, 2), total


def scatter_sum(pieces, axis):
    by_x, by_y, total = pieces
    return dp_part(total, axis, 0, 0, total.shape[0]).astype(f32) + by_x.astype(f32) + by_y.astype(f32)


def body_plain(
    inputs,
    cotangent,
    membership,
    routes,
    gate_weights,
    pair_order,
    w_query,
    w_key,
    w_value,
    w_output,
    norm_gains,
    w_gate,
    w_up,
    w_down,
):
    micro = inputs.shape[0]
    rows = inputs.shape[2]
    width = inputs.shape[3]
    group_len = membership.shape[2]
    member = lax.axis_index("expert")
    blocks = lax.axis_size("expert")
    shards = blocks * lax.axis_size("dp")
    shard_at = lax.axis_index("dp") * blocks + member
    local_experts = w_gate.shape[0]
    experts = local_experts * blocks
    capacity = rows * TOPK // experts
    step_heads = max(1, 384 // rows)
    total = micro * rows
    q_part, k_part, v_part = w_query.shape[1], w_key.shape[1], w_value.shape[1]

    gain_len = norm_gains.shape[0]
    gain_shard = jnp.zeros((2048,), bf16).at[:gain_len].set(norm_gains).reshape(16, 128)
    gain_full = lax.all_gather(gain_shard, BOTH, axis=0, tiled=True)
    gains = gain_full.reshape(shards, 2048)[:, :gain_len].reshape(-1).astype(f32)
    gain_in = gains[:width]
    gain_mid = gains[width : 2 * width]
    gain_q = gains[2 * width : 2 * width + HD]
    gain_k = gains[2 * width + HD :]

    qkv_w = lax.all_gather(
        jnp.concatenate([w_query.T, w_key.T, w_value.T], axis=0), BOTH, axis=0, tiled=True
    )
    out_w = lax.all_gather(w_output, BOTH, axis=0, tiled=True)
    wg = lax.all_gather(w_gate, "dp", axis=1, tiled=True)
    wu = lax.all_gather(w_up, "dp", axis=1, tiled=True)
    wd = lax.all_gather(w_down, "dp", axis=2, tiled=True)

    slot_map, weight_map = jax.vmap(
        lambda r, g, o: slots_of(r, g, o, capacity, experts)
    )(routes[:, 0], gate_weights[:, 0], pair_order[:, 0, 0])
    routing = jnp.concatenate([slot_map, weight_map], axis=-1)
    routing = lax.all_gather(routing, "expert", axis=0, tiled=False)
    mine = member * local_experts
    slot_mine = lax.dynamic_slice_in_dim(routing, mine, local_experts, axis=3)
    weight_mine = lax.dynamic_slice_in_dim(routing, experts + mine, local_experts, axis=3)
    slot_mine = jnp.transpose(slot_mine, (1, 3, 0, 2))
    weight_mine = jnp.transpose(weight_mine, (1, 3, 0, 2))
    slot_ids = jnp.arange(capacity, dtype=f32)
    hit = slot_mine[:, :, :, None, :] == slot_ids[None, None, None, :, None]
    pick = hit.astype(bf16)
    weighted = jnp.where(hit, weight_mine[:, :, :, None, :], 0.0)
    slot_weight = jnp.sum(weighted, axis=-1)
    weighted = weighted.astype(bf16)

    key_index = jnp.arange(group_len, dtype=jnp.int32)
    start_row = member * rows
    segment = membership[:, 0]
    row_index = start_row + jnp.arange(rows, dtype=jnp.int32)
    seg_rows = lax.dynamic_slice_in_dim(segment, start_row, rows, axis=1)
    before = jnp.sum((segment[:, None, :] < seg_rows[:, :, None]).astype(jnp.int32), axis=2)
    position = jnp.where(seg_rows == 0, row_index[None], PROMPT + row_index[None] - before)
    allowed = (key_index[None, :, None] <= row_index[None, None, :]) & (
        (segment[:, :, None] == 0) | (segment[:, :, None] == seg_rows[:, None, :])
    )
    bias = jnp.tile(jnp.where(allowed, 0.0, MASKED).astype(f32), (1, 1, step_heads))
    frequency = ROPE_BASE ** (-(jnp.arange(HD // 2, dtype=f32) * 2.0 / HD))
    angles = position.astype(f32).reshape(total)[:, None] * frequency[None, :]
    cosine = jnp.cos(angles)[:, None, :]
    sine_part = jnp.sin(angles)[:, None, :]

    hidden = inputs[:, 0].astype(f32).reshape(total, width)
    scale_in = rms_scale(hidden)
    normed = (hidden * scale_in * gain_in).astype(bf16)
    proj = mm(normed, qkv_w, NT).reshape(total, shards, q_part + k_part + v_part)
    queries = proj[:, :, :q_part].reshape(total, H, HD)
    key_pre = proj[:, :, q_part : q_part + k_part].reshape(total, KVH, HD)
    value = proj[:, :, q_part + k_part :].reshape(total, KVH, HD).astype(bf16)
    scale_q = rms_scale(queries)
    scale_k = rms_scale(key_pre)
    q_low = rotate(queries * scale_q * (gain_q * (SCALE * LOG2E)), cosine, sine_part).astype(bf16)
    q_low = q_low.reshape(micro, rows, H * HD)
    k_low = rotate(key_pre * scale_k * gain_k, cosine, sine_part).astype(bf16)
    kv_own = jnp.concatenate([k_low, value], axis=-1).reshape(micro, rows, KVH * 2 * HD)
    kv_all = lax.all_gather(kv_own, "expert", axis=0, tiled=False)
    chunk = 256
    mixed = []
    for at in range(micro):
        mixed = run_forward(q_low, kv_all[:, at : at + 1], bias, step_heads, chunk, at, mixed)
    mixed, logs = mixed

    branch = mm(mixed.reshape(total, H * HD), out_w)
    middle = hidden + branch
    scale_mid = rms_scale(middle)
    routed = (middle * scale_mid * gain_mid).astype(bf16).reshape(micro, rows, width)
    middle = middle.reshape(micro, rows, width)
    scale_mid = scale_mid.reshape(micro, rows, 1)

    outputs, d_branches, d_middles = [], [], []
    acc_gate = acc_up = acc_down = 0.0
    grad_mid = 0.0
    slots = blocks * capacity
    for at in range(micro):
        d_out = lax.all_gather(cotangent[at, 0], "expert", axis=0, tiled=False)
        tokens = lax.all_gather(routed[at], "expert", axis=0, tiled=False)
        picked = jnp.einsum("ebst,btd->ebsd", pick[at], tokens, preferred_element_type=f32)
        picked = picked.astype(bf16).reshape(local_experts, slots, width)
        d_result = jnp.einsum("ebst,btd->ebsd", pick[at], d_out, preferred_element_type=f32)
        d_result = (d_result * slot_weight[at][..., None]).astype(bf16)
        d_result = d_result.reshape(local_experts, slots, width)
        gate_pre = jnp.einsum("erd,edf->erf", picked, wg, preferred_element_type=f32)
        up_pre = jnp.einsum("erd,edf->erf", picked, wu, preferred_element_type=f32)
        d_hidden = jnp.einsum("erd,efd->erf", d_result, wd, preferred_element_type=f32)
        sigmoid_g = jax.nn.sigmoid(gate_pre)
        silu_g = gate_pre * sigmoid_g
        hidden_low = (silu_g * up_pre).astype(bf16)
        d_gate = (d_hidden * up_pre * sigmoid_g * (1.0 + gate_pre * (1.0 - sigmoid_g))).astype(bf16)
        d_up = (d_hidden * silu_g).astype(bf16)
        d_rows = jnp.einsum("erf,edf->erd", d_gate, wg, preferred_element_type=f32)
        d_rows = d_rows + jnp.einsum("erf,edf->erd", d_up, wu, preferred_element_type=f32)
        d_rows = d_rows.astype(bf16).reshape(local_experts, blocks, capacity, width)
        d_part = jnp.einsum("ebst,ebsd->btd", pick[at], d_rows, preferred_element_type=f32)
        d_part = d_part.astype(bf16).reshape(group_len, width)
        d_routed = lax.psum_scatter(d_part, "expert", scatter_dimension=0, tiled=True).astype(f32)
        result = jnp.einsum("erf,efd->erd", hidden_low, wd, preferred_element_type=f32)
        result = result.astype(bf16).reshape(local_experts, blocks, capacity, width)
        part = jnp.einsum("ebst,ebsd->btd", weighted[at], result, preferred_element_type=f32)
        part = part.astype(bf16).reshape(group_len, width)
        expert_mix = lax.psum_scatter(part, "expert", scatter_dimension=0, tiled=True).astype(f32)
        outputs.append((middle[at] + expert_mix).astype(bf16))

        acc_down += jnp.einsum("erf,erd->efd", hidden_low, d_result, preferred_element_type=f32)
        acc_gate += jnp.einsum("erd,erf->edf", picked, d_gate, preferred_element_type=f32)
        acc_up += jnp.einsum("erd,erf->edf", picked, d_up, preferred_element_type=f32)

        d_mid_norm, mid_gain_grad = norm_back(d_routed, middle[at], scale_mid[at], gain_mid)
        grad_mid = grad_mid + mid_gain_grad
        d_middle = cotangent[at, 0].astype(f32) + d_mid_norm
        d_middles.append(d_middle)
        d_branches.append(d_middle.astype(bf16))

    grad_gate = lax.psum_scatter(acc_gate.astype(bf16), "dp", scatter_dimension=1, tiled=True)
    grad_up = lax.psum_scatter(acc_up.astype(bf16), "dp", scatter_dimension=1, tiled=True)
    grad_down = lax.psum_scatter(acc_down.astype(bf16), "dp", scatter_dimension=2, tiled=True)

    d_branch = jnp.concatenate(d_branches, axis=0)
    d_middle = jnp.concatenate(d_middles, axis=0)
    grad_output = mm(mixed.reshape(total, H * HD), d_branch, TN).astype(bf16)
    grad_output = lax.psum_scatter(grad_output, BOTH, scatter_dimension=0, tiled=True)
    d_mixed = mm(d_branch, out_w, NT).astype(bf16).reshape(micro, rows, H * HD)
    cos_rows = jnp.concatenate([cosine, cosine], axis=-1).reshape(micro, rows, HD)
    sine_rows = jnp.concatenate([-sine_part, sine_part], axis=-1).reshape(micro, rows, HD)
    q_raw = queries.reshape(micro, rows, H * HD)
    d_query, dkv_list, grad_qn = [], [], 0.0
    for at in range(micro):
        d_query, dkv_one, part = run_backward(
            q_low, kv_all[:, at : at + 1], bias, mixed, d_mixed, logs, q_raw, cos_rows, sine_rows,
            gain_q[None, :], step_heads, chunk, at, [d_query] if at else []
        )
        dkv_list.append(dkv_one)
        grad_qn += part[0]
    dkv_all = jnp.concatenate(dkv_list, axis=1)
    dkv = lax.psum_scatter(dkv_all, "expert", scatter_dimension=0, tiled=False)
    dkv = dkv.reshape(total, KVH, 2 * HD)
    d_key = rotate(dkv[:, :, :HD].astype(f32), cosine, -sine_part)
    d_key, grad_kn = norm_back(d_key, key_pre, scale_k, gain_k)
    d_proj = jnp.concatenate(
        [
            d_query.reshape(total, shards, q_part),
            d_key.astype(bf16).reshape(total, shards, k_part),
            dkv[:, :, HD:].reshape(total, shards, v_part),
        ],
        axis=-1,
    ).reshape(total, -1)
    grad_qkv = mm(d_proj, normed, TN).astype(bf16)
    grad_qkv = lax.psum_scatter(grad_qkv, BOTH, scatter_dimension=0, tiled=True).astype(f32)
    d_normed = mm(d_proj, qkv_w)
    d_in_norm, grad_in = norm_back(d_normed, hidden, scale_in, gain_in)
    input_grad = d_middle + d_in_norm

    gain_grads = jnp.concatenate([grad_in, grad_mid, grad_qn, grad_kn]).reshape(shards, gain_len)
    gain_grads = jnp.pad(gain_grads, ((0, 0), (0, 256 - gain_len % 256)))
    gain_all = lax.all_gather(gain_grads, BOTH, axis=0, tiled=False)
    grad_gains = jnp.sum(lax.dynamic_index_in_dim(gain_all, shard_at, axis=1, keepdims=False), axis=0)
    return (
        jnp.stack(outputs)[:, None],
        input_grad.reshape(micro, 1, rows, width),
        grad_qkv[:q_part].T,
        grad_qkv[q_part : q_part + k_part].T,
        grad_qkv[q_part + k_part :].T,
        grad_output.astype(f32),
        grad_gains[:gain_len],
        grad_gate.astype(f32),
        grad_up.astype(f32),
        grad_down.astype(f32),
    )


def body_fast(
    inputs,
    cotangent,
    membership,
    routes,
    gate_weights,
    pair_order,
    w_query,
    w_key,
    w_value,
    w_output,
    norm_gains,
    w_gate,
    w_up,
    w_down,
):
    micro = inputs.shape[0]
    rows = inputs.shape[2]
    width = inputs.shape[3]
    group_len = membership.shape[2]
    member = lax.axis_index("expert")
    blocks = lax.axis_size("expert")
    shards = blocks * lax.axis_size("dp")
    local_experts = w_gate.shape[0]
    experts = local_experts * blocks
    capacity = rows * TOPK // experts
    step_heads = max(1, 384 // rows)
    total = micro * rows
    q_part, k_part, v_part = w_query.shape[1], w_key.shape[1], w_value.shape[1]
    tie = lax.optimization_barrier

    slot_map, weight_map = jax.vmap(
        lambda r, g, o: slots_of(r, g, o, capacity, experts)
    )(routes[:, 0], gate_weights[:, 0], pair_order[:, 0, 0])
    weight_high = tie(weight_map.astype(bf16))
    weight_low = (weight_map - weight_high.astype(f32)).astype(bf16)

    def padded(values, lanes):
        return jnp.pad(values, ((0, 0), (0, 0), (0, lanes - experts)))

    routing = jnp.concatenate(
        [
            padded(slot_map.astype(bf16), 32),
            padded(weight_high, 32),
            padded(weight_low, ROUTE_LANES - 64),
        ],
        axis=-1,
    )

    gain_len = norm_gains.shape[0]
    gain_shard = jnp.pad(norm_gains[None], ((0, 15), (0, 256 - gain_len)))
    kv_w = jnp.concatenate([w_key.T, w_value.T], axis=0)
    halves = cotangent.reshape(2 * micro, rows // 2, width)
    cot_first = halves[:3].reshape(-1, width)
    q_w, kv_w, out_w, gain_full, cot_first = gather_rows(
        [w_query.T, kv_w, w_output, gain_shard, cot_first], [(3, 0, 1, 2)], 1, (4,)
    )
    cot_first = cot_first.reshape(blocks, 3, rows // 2, width)
    q_w, w_gate = tie((q_w, w_gate))
    gains = gain_full.reshape(shards, 16, 256)[:, 0, :gain_len].reshape(-1).astype(f32)
    gain_in = gains[:width]
    gain_mid = gains[width : 2 * width]
    gain_q = gains[2 * width : 2 * width + HD]
    gain_k = gains[2 * width + HD :]
    gate_near = (swap(w_gate, 1), swap(w_gate, 2))

    key_index = jnp.arange(group_len, dtype=jnp.int32)
    start_row = member * rows
    segment = membership[:, 0]
    row_index = start_row + jnp.arange(rows, dtype=jnp.int32)
    seg_rows = lax.dynamic_slice_in_dim(segment, start_row, rows, axis=1)
    before = jnp.sum((segment[:, None, :] < seg_rows[:, :, None]).astype(jnp.int32), axis=2)
    position = jnp.where(seg_rows == 0, row_index[None], PROMPT + row_index[None] - before)
    allowed = (key_index[None, :, None] <= row_index[None, None, :]) & (
        (segment[:, :, None] == 0) | (segment[:, :, None] == seg_rows[:, None, :])
    )
    bias = jnp.tile(jnp.where(allowed, 0.0, MASKED).astype(f32), (1, 1, step_heads))
    frequency = ROPE_BASE ** (-(jnp.arange(HD // 2, dtype=f32) * 2.0 / HD))
    angles = position.astype(f32).reshape(total)[:, None] * frequency[None, :]
    cosine, sine = jnp.cos(angles), jnp.sin(angles)
    cosine = jnp.concatenate([cosine, cosine], axis=-1)
    sine = jnp.concatenate([-sine, sine], axis=-1)
    gain_q, gain_k = gain_q[None, :], gain_k[None, :]

    hidden = inputs[:, 0].astype(f32).reshape(total, width)
    scale_in = rms_scale(hidden)
    normed = (hidden * scale_in * gain_in).astype(bf16)
    q_low, q_raw, kv_own, k_raw, kv_w = run_project(
        normed, q_w, kv_w, cosine, sine, gain_q * (SCALE * LOG2E), gain_k
    )
    q_low, q_raw = (a.reshape(micro, rows, H * HD) for a in (q_low, q_raw))
    kv_own = kv_own.reshape(micro, rows, KVH * 2 * HD)
    kv_own, gate_near, w_up = tie((kv_own, gate_near, w_up))
    up_near = (swap(w_up, 1), swap(w_up, 2))
    kv_0 = lax.all_gather(kv_own[0], "expert", axis=0, tiled=False)
    kv_1 = lax.all_gather(kv_own[1], "expert", axis=0, tiled=False)
    kv_0, up_near, w_down = tie((kv_0, up_near, w_down))
    down_near = (swap(w_down, 1), swap(w_down, 2))
    chunk = 256

    def middle_of(mixed, at):
        part = hidden[at * rows : (at + 1) * rows]
        middle = part + mm(mixed[at], out_w)
        routed = (middle * rms_scale(middle) * gain_mid).astype(bf16)
        return middle, jnp.concatenate([routed, routing[at]], axis=-1)

    mixed, logs, shares = run_forward(q_low, kv_0[:, None], bias, step_heads, chunk, 0, [], True)
    middle_0, routed_0 = middle_of(mixed, 0)
    mixed, kv_1, routed_0 = tie((mixed, kv_1, routed_0))
    kv_all = [kv_0[:, None], kv_1[:, None]]
    mixed, logs, shares = run_forward(
        q_low, kv_all[1], bias, step_heads, chunk, 1, [mixed, logs, shares], True
    )
    middle_1, routed_1 = middle_of(mixed, 1)
    routed_1, down_near, cot_last = tie((routed_1, down_near, halves[3]))
    cot_last = lax.all_gather(cot_last, "expert", axis=0, tiled=False)[:, None]
    parts = [
        (own, near[0], near[1], swap(near[0][:1], 2), swap(near[1][1:], 1))
        for own, near in ((w_gate, gate_near), (w_up, up_near), (w_down, down_near))
    ]
    cots = [((cot_first, 0), (cot_first, 1)), ((cot_first, 2), (cot_last, 0))]
    routed = [routed_0, routed_1]
    middle = jnp.stack([middle_0, middle_1])

    mix_parts, d_routeds = [], []
    kept = []
    for at in range(micro):
        tokens = lax.all_gather(routed[at], "expert", axis=0, tiled=False)
        tokens, parts = tie((tokens, parts))
        kept, mix, d_part = run_experts(tokens, cots[at], parts, capacity, at, micro, kept)
        kept, d_part, mix, d_routeds = tie((kept, d_part, mix, d_routeds))
        mix_parts.append(mix)
        d_routed = lax.psum_scatter(d_part, "expert", scatter_dimension=0, tiled=True)
        d_routeds.append(d_routed)
    picked, d_result, hidden_low, d_gate, d_up = (
        a.reshape(local_experts, -1, a.shape[-1]) for a in kept
    )

    def weight_grad(rows_in, rows_out):
        return jnp.einsum("era,erb->eab", rows_in, rows_out, preferred_element_type=f32).astype(bf16)

    first = scatter_far(weight_grad(picked, d_gate), 1)
    second = scatter_far(weight_grad(picked, d_up), 1)
    first, hidden_low = tie((first, hidden_low))
    first = scatter_near(first, 1)
    third = weight_grad(hidden_low, d_result)
    d_routeds[-1], first, second, third, mix_parts[0] = tie(
        (d_routeds[-1], first, second, third, mix_parts[0])
    )
    second = scatter_near(second, 1)
    third = scatter_far(third, 2)
    d_mixed, d_middle, d_branch, grad_mid = run_middle_back(
        d_routeds, middle, cotangent[:, 0], gain_mid[None, :], out_w
    )
    d_mixed, d_branch, third = tie((d_mixed, d_branch, third))
    third = scatter_near(third, 2)
    d_mixed = d_mixed.reshape(micro, rows, H * HD)
    cos_rows, sine_rows = (a.reshape(micro, rows, HD) for a in (cosine, sine))
    def share(core):
        part = lax.dynamic_index_in_dim(shares, core, axis=0, keepdims=False)
        part = part.reshape(2, total, -1)
        return jnp.einsum("zta,td->zad", part, d_branch, preferred_element_type=f32).astype(bf16)

    core = member % 2
    pairs = [(i, i ^ 1) for i in range(blocks)]
    got = lax.ppermute(share(1 - core), "expert", pairs)
    mixes = [lax.psum_scatter(mix_parts[0], "expert", scatter_dimension=0, tiled=True)]

    def backward(at, earlier):
        d_query, dkv_one, part = run_backward(
            q_low, kv_all[at], bias, mixed, d_mixed, logs, q_raw, cos_rows, sine_rows, gain_q,
            step_heads, chunk, at, earlier
        )
        return d_query, dkv_one[:, 0], part

    d_query, dkv_0, gain_0 = backward(0, [])
    d_query, dkv_0, got, second = tie((d_query, dkv_0, got, second))
    dkv_0 = lax.psum_scatter(dkv_0, "expert", scatter_dimension=0, tiled=False)
    out_grad = tie(share(core))
    out_grad = (out_grad.astype(f32) + got.astype(f32)).astype(bf16)
    d_query, out_grad = tie((d_query, out_grad))
    out_grad = scatter_far(out_grad, 1)
    d_query, dkv_1, gain_1 = backward(1, [d_query])
    grad_qn = gain_0 + gain_1
    d_query, dkv_1, out_grad, mixes, third = tie((d_query, dkv_1, out_grad, mixes, third))
    dkv_1 = lax.psum_scatter(dkv_1, "expert", scatter_dimension=0, tiled=False)
    out_grad = scatter_add(out_grad, 1)
    out_grad, first, second, third, d_query = tie((out_grad, first, second, third, d_query))
    out_grad = (swap(out_grad[0], 1), swap(out_grad[1], 2), out_grad[2])
    out_grad = scatter_sum(out_grad, 1).astype(bf16).reshape(-1, width)
    d_query = d_query.reshape(total, H * HD)
    dkv = jnp.concatenate([dkv_0, dkv_1], axis=0)
    dkv = dkv.reshape(total, KVH * 2 * HD)
    mix_part, dkv = tie((mix_parts[1], dkv))
    mixes.append(lax.psum_scatter(mix_part, "expert", scatter_dimension=0, tiled=True))
    outputs = [(middle[at] + mixes[at].astype(f32)).astype(bf16) for at in range(micro)]
    expert_grads = [scatter_sum(first, 1), scatter_sum(second, 1), scatter_sum(third, 2)]
    d_normed = mm(d_query, q_w)
    dkv, out_grad, expert_grads, d_normed = tie((dkv, out_grad, expert_grads, d_normed))
    dkv, dkv_t, grad_kn = run_key_back(dkv, k_raw, cosine, sine, gain_k)
    d_normed = d_normed + mm(dkv, kv_w)
    grad_output = lax.psum_scatter(
        out_grad,
        "expert",
        scatter_dimension=0,
        tiled=True,
        axis_index_groups=[list(range(c, blocks, 2)) for c in range(2)],
    ).astype(f32)
    d_in_norm, grad_in = norm_back(d_normed, hidden, scale_in, gain_in)
    input_grad = d_middle + d_in_norm
    gain_grads = jnp.concatenate([grad_in, grad_mid[0], grad_qn[0], grad_kn[0]]).reshape(shards, gain_len)
    grad_qkv, grad_gains = reduce_rows(d_query, dkv_t, normed, 3, gain_grads)
    return (
        jnp.stack(outputs)[:, None],
        input_grad.reshape(micro, 1, rows, width),
        grad_qkv[:q_part].T,
        grad_qkv[q_part : q_part + k_part].T,
        grad_qkv[q_part + k_part :].T,
        grad_output,
        grad_gains[0, :gain_len],
        *expert_grads,
    )


def solution(mesh):
    fast = mesh.shape["dp"] == 4 and mesh.shape["expert"] == 8
    return jax.shard_map(
        body_fast if fast else body_plain,
        mesh=mesh,
        in_specs=(
            P(None, "dp", "expert", None),
            P(None, "dp", "expert", None),
            P(None, "dp", None),
            P(None, "dp", "expert", None),
            P(None, "dp", "expert", None),
            P(None, "dp", "expert", None),
            P(None, ("dp", "expert")),
            P(None, ("dp", "expert")),
            P(None, ("dp", "expert")),
            P(("dp", "expert"), None),
            P(("dp", "expert")),
            P("expert", "dp", None),
            P("expert", "dp", None),
            P("expert", None, "dp"),
        ),
        out_specs=(
            P(None, "dp", "expert", None),
            P(None, "dp", "expert", None),
            P(None, ("dp", "expert")),
            P(None, ("dp", "expert")),
            P(None, ("dp", "expert")),
            P(("dp", "expert"), None),
            P(("dp", "expert")),
            P("expert", "dp", None),
            P("expert", "dp", None),
            P("expert", None, "dp"),
        ),
        check_vma=False,
    )
```

```python
import functools
import math

import jax
import jax.numpy as jnp
from jax import lax
from jax.experimental import pallas as pl
from jax.experimental.pallas import tpu as pltpu
from jax.sharding import PartitionSpec as P

H = 32
KVH = 4
HD = 128
FF = 768
TOPK = 8
PROMPT = 1024
PER_KV = H // KVH

EPSILON = 1e-06
ROPE_BASE = 1000000.0
MASKED = -1e30
LOG2E = math.log2(math.e)
SCALE = HD ** (-0.5)

bf16 = jnp.bfloat16
f32 = jnp.float32
NT = (((1,), (1,)), ((), ()))
TN = (((0,), (0,)), ((), ()))
NN = (((1,), (0,)), ((), ()))
BOTH = ("dp", "expert")
VMEM_LIMIT = 56 * 1024 * 1024
LIGHT = pl.CostEstimate(flops=1_000_000, bytes_accessed=1_000_000, transcendentals=0)


def mm(a, b, dims=NN):
    return lax.dot_general(a, b, dims, preferred_element_type=f32)


def rms_scale(values):
    return lax.rsqrt(jnp.mean(values * values, axis=-1, keepdims=True) + EPSILON)


def norm_back(upstream, values, inv_rms, norm_gain):
    lifted = upstream * norm_gain
    inner_dot = jnp.mean(lifted * values, axis=-1, keepdims=True)
    back_grad = inv_rms * lifted - values * (inv_rms * inv_rms * inv_rms) * inner_dot
    gain_grad = jnp.sum((upstream * values * inv_rms).reshape(-1, values.shape[-1]), axis=0)
    return (back_grad, gain_grad)


def rotate(values, cosine, sine_part):
    half_dim = values.shape[-1] // 2
    first_half = values[..., :half_dim]
    second_half = values[..., half_dim:]
    return jnp.concatenate(
        [
            first_half * cosine - second_half * sine_part,
            second_half * cosine + first_half * sine_part,
        ],
        axis=-1,
    )


def turn(values, cosine, sine):
    return values * cosine + pltpu.roll(values, HD // 2, 1) * sine


def project(x_ref, wq_ref, wkv_ref, cos_ref, sin_ref, gq_ref, gk_ref, q_ref, qraw_ref, kraw_ref, wkv_out, *kv_refs):
    x = x_ref[...]
    cosine, sine = cos_ref[...], sin_ref[...]
    for at in range(0, PER_KV * HD, 2 * HD):
        raw = mm(x, wq_ref[at : at + 2 * HD], NT)
        qraw_ref[:, at : at + 2 * HD] = raw
        for lane in (0, HD):
            head = raw[:, lane : lane + HD]
            normed = head * rms_scale(head) * gq_ref[...]
            q_ref[:, at + lane : at + lane + HD] = turn(normed, cosine, sine).astype(bf16)
    piece = HD // PER_KV
    w_k = [wkv_ref[2 * piece * i : 2 * piece * i + piece] for i in range(PER_KV)]
    w_v = [wkv_ref[2 * piece * i + piece : 2 * piece * (i + 1)] for i in range(PER_KV)]
    w_kv = jnp.concatenate(w_k + w_v, axis=0)
    wkv_out[...] = w_kv
    raw = mm(x, w_kv, NT)
    key = raw[:, :HD]
    kraw_ref[...] = key
    normed = key * rms_scale(key) * gk_ref[...]
    key, value = turn(normed, cosine, sine).astype(bf16), raw[:, HD:].astype(bf16)
    rows = x.shape[0] // len(kv_refs)
    for b, kv_ref in enumerate(kv_refs):
        kv_ref[:, :HD] = key[b * rows : (b + 1) * rows]
        kv_ref[:, HD:] = value[b * rows : (b + 1) * rows]


def run_project(x, wq, wkv, cosine, sine, gain_q, gain_k, micro):
    tokens, width = x.shape
    wide = PER_KV * HD
    whole = lambda a: pl.BlockSpec(a.shape, lambda g: (0, 0))
    cols = lambda n: pl.BlockSpec((tokens, n), lambda g: (0, g))
    rows = lambda n: pl.BlockSpec((n, width), lambda g: (g, 0))
    return pl.pallas_call(
        project,
        grid=(KVH,),
        in_specs=[whole(x), rows(wide), rows(2 * HD), whole(cosine), whole(sine), whole(gain_q), whole(gain_k)],
        out_specs=[cols(wide), cols(wide), cols(HD), rows(2 * HD)]
        + [pl.BlockSpec((tokens // micro, 2 * HD), lambda g: (0, g))] * micro,
        out_shape=[
            jax.ShapeDtypeStruct((tokens, H * HD), bf16),
            jax.ShapeDtypeStruct((tokens, H * HD), f32),
            jax.ShapeDtypeStruct((tokens, KVH * HD), f32),
            jax.ShapeDtypeStruct((KVH * 2 * HD, width), bf16),
        ]
        + [jax.ShapeDtypeStruct((tokens // micro, KVH * 2 * HD), bf16)] * micro,
        compiler_params=pltpu.CompilerParams(vmem_limit_bytes=VMEM_LIMIT),
        cost_estimate=LIGHT,
    )(x, wq, wkv, cosine, sine, gain_q, gain_k)


def norm_turn_back(grad, raw, cosine, sine, gain):
    grad = turn(grad, cosine, -sine)
    scale = rms_scale(raw)
    lifted = grad * gain
    inner = jnp.mean(lifted * raw, axis=-1, keepdims=True)
    back = scale * lifted - raw * (scale * scale * scale) * inner
    return back, jnp.sum(grad * raw * scale, axis=0, keepdims=True)


def key_back(dkv_ref, kraw_ref, cos_ref, sin_ref, gk_ref, out_ref, out_t_ref, gain_ref):
    gain_sum = 0.0
    for g in range(KVH):
        key = slice(2 * g * HD, (2 * g + 1) * HD)
        value = slice((2 * g + 1) * HD, (2 * g + 2) * HD)
        grad = dkv_ref[:, key].astype(f32)
        back, part = norm_turn_back(
            grad, kraw_ref[:, g * HD : (g + 1) * HD], cos_ref[...], sin_ref[...], gk_ref[...]
        )
        gain_sum += part
        low = back.astype(bf16)
        out_ref[:, key] = low
        out_t_ref[key] = low.T
        out_ref[:, value] = dkv_ref[:, value]
        out_t_ref[value] = dkv_ref[:, value].T
    gain_ref[...] = gain_sum


def run_key_back(dkv, key_raw, cosine, sine, gain):
    tokens, wide = dkv.shape
    return pl.pallas_call(
        key_back,
        out_shape=[
            jax.ShapeDtypeStruct((tokens, wide), bf16),
            jax.ShapeDtypeStruct((wide, tokens), bf16),
            jax.ShapeDtypeStruct((1, HD), f32),
        ],
        compiler_params=pltpu.CompilerParams(vmem_limit_bytes=VMEM_LIMIT),
    )(dkv, key_raw, cosine, sine, gain)


def attend_forward(step_heads, chunk, q_ref, kv_ref, bias_ref, o_ref, log_ref, o2_ref=None):
    group_len = bias_ref.shape[1]
    keys = kv_ref[:, 0, :, :HD].reshape(group_len, HD)
    values_t = kv_ref[:, 0, :, HD:].reshape(group_len, HD).T
    rows = q_ref.shape[1]
    for step in range(PER_KV // step_heads):
        heads = range(step * step_heads, (step + 1) * step_heads)
        query = jnp.concatenate([q_ref[0, :, h * HD : (h + 1) * HD] for h in heads], axis=0)
        mixed, row_sum = 0.0, 0.0
        for at in range(0, group_len, chunk):
            scores = mm(keys[at : at + chunk], query, NT)
            prob = jnp.exp2(scores + bias_ref[0, at : at + chunk, :])
            row_sum += jnp.sum(prob, axis=0, keepdims=True)
            mixed += mm(values_t[:, at : at + chunk], prob.astype(bf16))
        out = (mixed / row_sum).T.astype(bf16)
        for i, h in enumerate(heads):
            part = out[i * rows : (i + 1) * rows]
            o_ref[0, :, h * HD : (h + 1) * HD] = part
            if o2_ref is not None:
                lane = (h // 2) % 2 * HD
                o2_ref[h % 2, h // 4, 0, :, lane : lane + HD] = part
        log_ref[0, 0, step : step + 1, :] = jnp.log2(row_sum)


def attend_backward(
    step_heads, chunk, q_ref, kv_ref, bias_ref, o_ref, do_ref, log_ref, raw_ref, cos_ref, sin_ref, gain_ref,
    dq_ref, dkv_ref, gain_out, dk_acc, dv_acc
):
    group_len = bias_ref.shape[1]
    keys = kv_ref[:, 0, :, :HD].reshape(group_len, HD)
    values = kv_ref[:, 0, :, HD:].reshape(group_len, HD)
    keys_t = keys.T
    rows = q_ref.shape[1]
    cosine, sine, gain = cos_ref[0], sin_ref[0], gain_ref[...]

    @pl.when(pl.program_id(0) == 0)
    def _():
        gain_out[...] = jnp.zeros_like(gain_out)

    gain_sum = 0.0
    dk_acc[...] = jnp.zeros_like(dk_acc)
    dv_acc[...] = jnp.zeros_like(dv_acc)
    for step in range(PER_KV // step_heads):
        heads = range(step * step_heads, (step + 1) * step_heads)
        query = jnp.concatenate([q_ref[0, :, h * HD : (h + 1) * HD] for h in heads], axis=0)
        grad = jnp.concatenate([do_ref[0, :, h * HD : (h + 1) * HD] for h in heads], axis=0)
        mixed = jnp.concatenate([o_ref[0, :, h * HD : (h + 1) * HD] for h in heads], axis=0)
        row_dot = jnp.sum((grad.astype(f32) * mixed.astype(f32)).T, axis=0, keepdims=True)
        log_sum = log_ref[0, 0, step : step + 1, :]
        dq_t = 0.0
        for at in range(0, group_len, chunk):
            part = slice(at, at + chunk)
            scores = mm(keys[part], query, NT)
            prob = jnp.exp2(scores + (bias_ref[0, part, :] - log_sum))
            d_prob = mm(values[part], grad, NT)
            d_score = (prob * (d_prob - row_dot)).astype(bf16)
            dv_acc[part] += mm(prob.astype(bf16), grad)
            dk_acc[part] += mm(d_score, query)
            dq_t += mm(keys_t[:, part], d_score)
        out = (dq_t * SCALE).T.astype(bf16).astype(f32)
        for i, h in enumerate(heads):
            head = slice(h * HD, (h + 1) * HD)
            back, part = norm_turn_back(
                out[i * rows : (i + 1) * rows], raw_ref[0, :, head], cosine, sine, gain
            )
            dq_ref[0, :, head] = back.astype(bf16)
            gain_sum += part
    gain_out[...] += gain_sum
    blocks = dkv_ref.shape[0]
    dkv_ref[:, 0, :, :HD] = (dk_acc[...] * (1.0 / LOG2E)).astype(bf16).reshape(blocks, rows, HD)
    dkv_ref[:, 0, :, HD:] = dv_acc[...].astype(bf16).reshape(blocks, rows, HD)


def attention_specs(rows, group_len, blocks, step_heads, at):
    wide = PER_KV * HD
    q_spec = pl.BlockSpec((1, rows, wide), lambda g: (at, 0, g))
    kv_spec = pl.BlockSpec((blocks, 1, rows, 2 * HD), lambda g: (0, 0, 0, g))
    bias_spec = pl.BlockSpec((1, group_len, step_heads * rows), lambda g: (at, 0, 0))
    log_spec = pl.BlockSpec((1, 1, PER_KV // step_heads, step_heads * rows), lambda g: (at, g, 0, 0))
    return q_spec, kv_spec, bias_spec, log_spec


def run_forward(query, kv_all, bias, step_heads, chunk, at, earlier, again=False):
    micro, rows, _ = query.shape
    blocks = kv_all.shape[0]
    group_len = bias.shape[1]
    q_spec, kv_spec, bias_spec, log_spec = attention_specs(rows, group_len, blocks, step_heads, at)
    flops = 4 * rows * H * HD * group_len

    def kernel(*refs):
        attend_forward(step_heads, chunk, *refs[:3], *refs[3 + len(earlier) :])

    return pl.pallas_call(
        kernel,
        grid=(KVH,),
        in_specs=[q_spec, kv_spec, bias_spec] + [pl.BlockSpec(memory_space=pl.ANY)] * len(earlier),
        out_specs=[q_spec, log_spec]
        + again * [pl.BlockSpec((2, 2, 1, rows, 2 * HD), lambda g: (0, 0, at, 0, g))],
        out_shape=[
            jax.ShapeDtypeStruct(query.shape, bf16),
            jax.ShapeDtypeStruct((micro, KVH, PER_KV // step_heads, step_heads * rows), f32),
        ]
        + again * [jax.ShapeDtypeStruct((2, 2, micro, rows, KVH * 2 * HD), bf16)],
        input_output_aliases={3 + i: i for i in range(len(earlier))},
        compiler_params=pltpu.CompilerParams(vmem_limit_bytes=VMEM_LIMIT),
        cost_estimate=LIGHT,
    )(query, kv_all, bias, *earlier)


def run_backward(query, kv_all, bias, mixed, grad, logs, raw, cosine, sine, gain, step_heads, chunk, at, earlier):
    micro, rows, _ = query.shape
    blocks = kv_all.shape[0]
    group_len = bias.shape[1]
    q_spec, kv_spec, bias_spec, log_spec = attention_specs(rows, group_len, blocks, step_heads, at)
    flops = 10 * rows * H * HD * group_len
    gain_spec = pl.BlockSpec((1, HD), lambda g: (0, 0))

    def kernel(*refs):
        attend_backward(step_heads, chunk, *refs[:10], *refs[10 + len(earlier) :])

    return pl.pallas_call(
        kernel,
        grid=(KVH,),
        in_specs=[q_spec, kv_spec, bias_spec, q_spec, q_spec, log_spec, q_spec]
        + [pl.BlockSpec((1, rows, HD), lambda g: (at, 0, 0))] * 2
        + [gain_spec]
        + [pl.BlockSpec(memory_space=pl.ANY)] * len(earlier),
        out_specs=[q_spec, kv_spec, gain_spec],
        out_shape=[
            jax.ShapeDtypeStruct(query.shape, bf16),
            jax.ShapeDtypeStruct(kv_all.shape, bf16),
            jax.ShapeDtypeStruct((1, HD), f32),
        ],
        input_output_aliases={10 + i: i for i in range(len(earlier))},
        scratch_shapes=[pltpu.VMEM((group_len, HD), f32), pltpu.VMEM((group_len, HD), f32)],
        compiler_params=pltpu.CompilerParams(vmem_limit_bytes=VMEM_LIMIT),
        cost_estimate=LIGHT,
    )(query, kv_all, bias, mixed, grad, logs, raw, cosine, sine, gain, *earlier)


def middle_back(r0_ref, r1_ref, mid_ref, cot_ref, gain_ref, w_ref, mix_ref, dmid_ref, low_ref, gain_out):
    @pl.when(pl.program_id(0) == 0)
    def _():
        gain_sum = 0.0
        rows = r0_ref.shape[0]
        for b, ref in enumerate((r0_ref, r1_ref)):
            grad = ref[...].astype(f32)
            middle = mid_ref[b]
            scale = rms_scale(middle)
            lifted = grad * gain_ref[...]
            inner = jnp.mean(lifted * middle, axis=-1, keepdims=True)
            total = cot_ref[b].astype(f32) + scale * lifted - middle * (scale * scale * scale) * inner
            gain_sum += jnp.sum(grad * middle * scale, axis=0, keepdims=True)
            dmid_ref[b * rows : (b + 1) * rows] = total
            low_ref[b * rows : (b + 1) * rows] = total.astype(bf16)
        gain_out[...] = gain_sum

    mix_ref[...] = mm(low_ref[...], w_ref[...], NT).astype(bf16)


def run_middle_back(routed, middle, cot, gain, out_w):
    micro, rows, width = middle.shape
    total = micro * rows
    piece = 512
    whole = lambda *shape: pl.BlockSpec(shape, lambda i: (0,) * len(shape))
    return pl.pallas_call(
        middle_back,
        grid=(out_w.shape[0] // piece,),
        in_specs=[whole(rows, width)] * 2
        + [whole(micro, rows, width)] * 2
        + [whole(1, width), pl.BlockSpec((piece, width), lambda i: (i, 0))],
        out_specs=[
            pl.BlockSpec((total, piece), lambda i: (0, i)),
            whole(total, width),
            whole(total, width),
            whole(1, width),
        ],
        out_shape=[
            jax.ShapeDtypeStruct((total, out_w.shape[0]), bf16),
            jax.ShapeDtypeStruct((total, width), f32),
            jax.ShapeDtypeStruct((total, width), bf16),
            jax.ShapeDtypeStruct((1, width), f32),
        ],
        compiler_params=pltpu.CompilerParams(vmem_limit_bytes=VMEM_LIMIT),
        cost_estimate=LIGHT,
    )(*routed, middle, cot, gain, out_w)


MESH = pl.DeviceIdType.MESH


def gather_kernel(phases, count, late, *refs):
    ins, outs, sems = refs[:count], refs[count : 2 * count], refs[2 * count :]
    dp = lax.axis_index("dp"); member = lax.axis_index("expert")
    blocks = lax.axis_size("expert")
    core = member % 2; z = member // 2
    depth = blocks // 2
    sibling = (dp, member + 1 - 2 * core)
    by_x = (dp + 1 - 2 * (dp % 2), member)
    by_y = ((dp + 2) % 4, member)
    x_at, y_at, far_at = by_x[0], by_y[0], 3 - dp
    above, below = (dp, member + 2), (dp, member - 2)
    barrier = pltpu.get_barrier_semaphore()
    peers = [(sibling, None), (by_x, None), (by_y, None), (above, z < depth - 1), (below, z > 0)]
    for peer, ok in peers:
        if ok is None:
            pl.semaphore_signal(barrier, inc=1, device_id=peer, device_id_type=MESH)
        else:
            @pl.when(ok)
            def _(peer=peer):
                pl.semaphore_signal(barrier, inc=1, device_id=peer, device_id_type=MESH)
    @pl.when((z == 0) | (z == depth - 1))
    def _(): pl.semaphore_wait(barrier, 4)
    @pl.when((z > 0) & (z < depth - 1))
    def _(): pl.semaphore_wait(barrier, 5)

    def guarded(ok, run):
        if ok is None: run()
        else: pl.when(ok)(run)

    class Item:
        pass

    def make(i):
        src, out = ins[i], outs[i]
        flat = i in late
        rows = src.shape[0]
        half = rows // 2
        (own_sem, sz, rz, sxy, rxy, sc, rc) = sems[i * 7 : (i + 1) * 7]
        def at(d, s, lo=0, n=rows):
            first = s * 2 + core if flat else d * blocks + s * 2 + core
            return out.at[pl.ds(pl.multiple_of(first * rows + lo, 16 if half % 16 == 0 else 8), n)]
        def copy(a, b, ss, rs, to):
            return pltpu.make_async_remote_copy(src_ref=a, dst_ref=b, send_sem=ss, recv_sem=rs, device_id=to, device_id_type=MESH)
        def block(d, s):
            return at(d, s)
        it = Item()
        def local():
            return pltpu.make_async_copy(src, at(dp, z), own_sem)
        def up(s, ref): return copy(ref, at(dp, s), sz.at[0, s], rz.at[s], above)
        def down(s, ref): return copy(ref, at(dp, s), sz.at[1, s], rz.at[s], below)
        def to_x(s, ref): return copy(ref, at(dp, s), sxy.at[0, s], rxy.at[0, s], by_x)
        def to_y(s, ref): return copy(ref, at(dp, s), sxy.at[1, s], rxy.at[1, s], by_y)
        def half_y(s):
            return copy(at(x_at, s, 0, half), at(x_at, s, 0, half), sxy.at[2, s], rxy.at[2, s], by_y)
        def half_x(s):
            return copy(at(y_at, s, half, half), at(y_at, s, half, half), sxy.at[3, s], rxy.at[3, s], by_x)
        def to_core(r, d, s, ref): return copy(ref, at(d, s), sc.at[r, s], rc.at[r, s], sibling)
        def spread(s, ref):
            if not flat:
                to_x(s, ref).start(); to_y(s, ref).start()
            to_core(0, dp, s, ref).start()
        def start_up():
            up(z, src).start()
        def start_down():
            down(z, src).start()
        def start():
            local().start()
            if not flat:
                guarded(z < depth - 1, start_up)
                guarded(z > 0, start_down)
            spread(z, src)
        def z_event(s, ok, rising):
            def run():
                up(s, at(dp, s)).wait_recv()
                if rising: guarded(z < depth - 1, lambda: up(s, at(dp, s)).start())
                else: guarded(z > 0, lambda: down(s, at(dp, s)).start())
                spread(s, at(dp, s))
            pl.when(ok)(run)
        def near_event(s, ok):
            def run():
                to_x(s, at(dp, s)).wait_recv()
                half_y(s).start()
                to_core(1, x_at, s, at(x_at, s)).start()
                to_y(s, at(dp, s)).wait_recv()
                half_x(s).start()
                to_core(2, y_at, s, at(y_at, s)).start()
            guarded(ok, run)
        def far_event(s, ok):
            def run():
                half_y(s).wait_recv(); half_x(s).wait_recv()
                to_core(3, far_at, s, at(far_at, s)).start()
            guarded(ok, run)
        owners = (dp,) if flat else (dp, x_at, y_at, far_at)
        def core_wait(s):
            for r, d in enumerate(owners):
                to_core(r, d, s, at(d, s)).wait_recv()
        def finish():
            local().wait()
            for s in range(depth):
                if not flat:
                    for c in (to_x(s, at(dp, s)), to_y(s, at(dp, s)), half_y(s), half_x(s)): c.wait_send()
                for r, d in enumerate(owners): to_core(r, d, s, at(d, s)).wait_send()
                guarded((z >= s) & (z < depth - 1), lambda: up(s, at(dp, s)).wait_send())
                guarded((z <= s) & (z > 0), lambda: down(s, at(dp, s)).wait_send())
        it.start_up, it.start_down = start_up, start_down
        it.start, it.z_event, it.near_event, it.far_event, it.core_wait, it.finish = start, z_event, near_event, far_event, core_wait, finish
        return it
    items = [make(i) for i in range(count)]
    def around(d):
        if d == 0: return [(z, None, True)]
        return [(z - d, z >= d, True), (z + d, z + d < depth, False)]
    for n, phase in enumerate(phases):
        its = [items[i] for i in phase]
        for it in its: it.start()
        lates = [items[i] for i in late]
        for it in lates: it.start()
        def late_sends(d):
            for it in lates:
                if d < depth - 1:
                    pl.when(z == d)(it.start_up)
                    pl.when(z == depth - 1 - d)(it.start_down)
        late_sends(0)
        for d in range(1, depth + 2):
            if d < depth:
                for s, ok, rising in around(d):
                    for it in its: it.z_event(s, ok, rising)
                late_sends(d)
            if d - 1 < depth:
                for s, ok, _ in around(d - 1):
                    for it in its: it.near_event(s, ok)
            if d > 2:
                for s, ok, rising in around(d - 2):
                    for it in lates: it.z_event(s, ok, rising)
            if d - 2 >= 0:
                for s, ok, _ in around(d - 2):
                    for it in its: it.far_event(s, ok)
    for it in items:
        for s in range(depth): it.core_wait(s)
    for it in items: it.finish()

def gather_rows(arrays, phases, cid, late=()):
    shards = lax.axis_size("dp") * lax.axis_size("expert")
    depth = lax.axis_size("expert") // 2
    D = pltpu.SemaphoreType.DMA
    sems = []
    for _ in arrays:
        sems += [D, D((2, depth)), D((depth,)), D((4, depth)), D((4, depth)), D((4, depth)), D((4, depth))]
    return pl.pallas_call(
        functools.partial(gather_kernel, phases, len(arrays), late),
        out_shape=[
            jax.ShapeDtypeStruct(((2 * depth if i in late else shards) * a.shape[0],) + a.shape[1:], a.dtype)
            for i, a in enumerate(arrays)
        ],
        in_specs=[pl.BlockSpec(memory_space=pl.ANY)] * len(arrays),
        out_specs=[pl.BlockSpec(memory_space=pl.ANY)] * len(arrays),
        scratch_shapes=sems,
        compiler_params=pltpu.CompilerParams(collective_id=cid, has_side_effects=True),
        cost_estimate=pl.CostEstimate(flops=0, bytes_accessed=400_000_000, transcendentals=0),
    )(*arrays)


def reduce_kernel(rows, cuts, a_ref, extra_ref, b_ref, g_ref, q_out, k_out, v_out, go_ref, o_ref, sib, got, own, far, near, plane, got_z,
                  s0, r0, s1, r1, s2, r2, s3, r3, g_acc, g_got, g_z, gs, gr, gsz, grz):
    dp = lax.axis_index("dp"); member = lax.axis_index("expert")
    core = member % 2; z = member // 2
    sibling = (dp, member + 1 - 2 * core)
    by_x = (dp + 1 - 2 * (dp % 2), member)
    by_y = ((dp + 2) % 4, member)
    x_at, y_at = by_x[0], by_y[0]
    far_at = 3 - dp
    half = rows // 2
    depth = lax.axis_size("expert") // 2
    barrier = pltpu.get_barrier_semaphore()
    peers = [sibling, by_x, by_y] + [(dp, ((z + d) % depth) * 2 + core) for d in range(1, depth)]
    for peer in peers:
        pl.semaphore_signal(barrier, inc=1, device_id=peer, device_id_type=MESH)
    pl.semaphore_wait(barrier, len(peers))

    def pick(table):
        at = table[depth-1]
        for i in range(depth - 1):
            at = jnp.where(z == i, table[i], at)
        return at
    orders = [[3, 3, 0, 0], [2, 0, 3, 1], [1, 2, 1, 2], [0, 1, 2, 3]]
    targets = [pick(t) for t in orders]
    cols = b_ref.shape[1] // cuts

    def copy(src, dst, ssem, rsem, to):
        return pltpu.make_async_remote_copy(src_ref=src, dst_ref=dst, send_sem=ssem, recv_sem=rsem, device_id=to, device_id_type=MESH)

    blocks = 2 * depth
    piece = (rows - HD) // 2

    def product(half_of, k, put):
        spot = targets[k] * 2 + half_of

        def step(i, _):
            shard = (i // cuts) * blocks + spot
            at = (i // cuts) * rows
            col = pl.ds(pl.multiple_of((i % cuts) * cols, cols), cols)
            part = mm(a_ref[:, pl.ds(pl.multiple_of(shard * HD, HD), HD)], b_ref[:, col], TN)
            put(pl.ds(pl.multiple_of(at, 16), HD), col, part)
            if piece:
                base = (shard // PER_KV) * (2 * HD) + (shard % PER_KV) * piece
                small = jnp.concatenate(
                    [
                        extra_ref[pl.ds(pl.multiple_of(base, 16), piece), :],
                        extra_ref[pl.ds(pl.multiple_of(base + HD, 16), piece), :],
                    ],
                    axis=0,
                )
                put(pl.ds(pl.multiple_of(at + HD, 16), 2 * piece), col, mm(small, b_ref[:, col]))
            return 0

        lax.fori_loop(0, 4 * cuts, step, 0)

    def gain_hop(i, src, to):
        return copy(src, g_got.at[i, pl.ds(0, src.shape[0])], gs.at[i], gr.at[i], to)
    hops = {}
    def gain_step(i):
        rows4 = lambda at: pl.ds(pl.multiple_of(at * 8, 8), 8)
        if i == 0:
            hops[0] = gain_hop(0, g_ref.at[pl.ds(pl.multiple_of((1 - core) * 32, 32), 32)], sibling)
        elif i == 1:
            hops[0].wait_recv()
            g_acc[...] = g_ref[pl.ds(pl.multiple_of(core * 32, 32), 32)] + g_got[0]
            hops[1] = gain_hop(1, g_acc.at[pl.ds(pl.multiple_of((1 - dp // 2) * 16, 16), 16)], by_y)
        elif i == 2:
            hops[1].wait_recv()
            mine = pl.ds(pl.multiple_of((dp // 2) * 16, 16), 16)
            g_acc[mine] += g_got[1, :16]
            hops[2] = gain_hop(2, g_acc.at[rows4(x_at)], by_x)
        elif i == 3:
            hops[2].wait_recv()
            g_acc[rows4(dp)] += g_got[2, :8]
            for d in range(1, depth):
                to = (z + d) % depth
                hops[2 + d] = copy(g_acc.at[pl.ds(dp * 8 + to, 1)], g_z.at[z], gsz.at[d - 1], grz.at[z], (dp, to * 2 + core))
        if i < 3:
            hops[i].start()
        else:
            for d in range(1, depth):
                hops[2 + d].start()
    def gain_end():
        total = g_acc[pl.ds(dp * 8 + z, 1)]
        for d in range(1, depth):
            src = (z + d) % depth
            copy(g_acc.at[pl.ds(dp * 8, 1)], g_z.at[src], gsz.at[0], grz.at[src], sibling).wait_recv()
            total += g_z[src]
        go_ref[...] = total
        for i in hops:
            hops[i].wait_send()
    sib_copies, far_copies, near_copies, z_copies = {}, {}, {}, {}
    def sib_step(k):
        slot = k % 2
        if k >= 2:
            sib_copies[k - 2].wait_send()
        def put(r, c, part):
            sib[slot, r, c] = part.astype(bf16)
        product(1 - core, k, put)
        sib_copies[k] = copy(sib.at[slot], got.at[k], s0.at[slot], r0.at[k], sibling)
        sib_copies[k].start()
    def blk(at):
        return pl.ds(pl.multiple_of(at * rows, 16), rows)
    def own_step(k):
        sib_copies[k].wait_recv()
        def put(r, c, part):
            own[k, r, c] = (part + got[k, r, c].astype(f32)).astype(bf16)
        product(core, k, put)
        base = pl.multiple_of(far_at * rows, 16)
        far_copies[k] = (
            copy(own.at[k, pl.ds(base, half)], far.at[k, 0], s1.at[k, 0], r1.at[k, 0], by_x),
            copy(own.at[k, pl.ds(pl.multiple_of(base + half, 16), half)], far.at[k, 1], s1.at[k, 1], r1.at[k, 1], by_y),
        )
        for c in far_copies[k]: c.start()
    def near_step(k):
        a, b = far_copies[k]
        a.wait_recv()
        rng = pl.ds(pl.multiple_of(y_at * rows, 16), half)
        own[k, rng] = (own[k, rng].astype(f32) + far[k, 0].astype(f32)).astype(bf16)
        to_y = copy(own.at[k, blk(y_at)], near.at[k, 1], s2.at[k, 1], r2.at[k, 1], by_y)
        to_y.start()
        b.wait_recv()
        rng = pl.ds(pl.multiple_of(x_at * rows + half, 16), half)
        own[k, rng] = (own[k, rng].astype(f32) + far[k, 1].astype(f32)).astype(bf16)
        to_x = copy(own.at[k, blk(x_at)], near.at[k, 0], s2.at[k, 0], r2.at[k, 0], by_x)
        to_x.start()
        near_copies[k] = (to_x, to_y)
    def plane_step(k):
        for c in near_copies[k]: c.wait_recv()
        total = own[k, blk(dp)].astype(f32) + near[k, 0].astype(f32) + near[k, 1].astype(f32)
        if k < depth - 1:
            plane[k] = total.astype(bf16)
            to = (dp, targets[k] * 2 + core)
            z_copies[k] = copy(plane.at[k], got_z.at[z], s3.at[k], r3.at[z], to)
            z_copies[k].start()
        else:
            o_ref[...] = total
    gain_step(0)
    sib_step(0); sib_step(1)
    own_step(0)
    gain_step(1)
    sib_step(2)
    own_step(1)
    gain_step(2)
    near_step(0)
    sib_step(3)
    own_step(2)
    gain_step(3)
    near_step(1)
    plane_step(0)
    own_step(3)
    near_step(2)
    plane_step(1)
    near_step(3)
    plane_step(2)
    plane_step(3)
    for d in range(1, depth):
        src = (z + d) % depth
        copy(plane.at[0], got_z.at[src], s3.at[0], r3.at[src], sibling).wait_recv()
        o_ref[...] += got_z[src].astype(f32)
    q_out[...] = o_ref[:HD].T
    k_out[...] = o_ref[HD : HD + piece].T
    v_out[...] = o_ref[HD + piece :].T
    gain_end()
    for k in range(depth):
        if k >= 2: sib_copies[k].wait_send()
        for c in far_copies[k]: c.wait_send()
        for c in near_copies[k]: c.wait_send()
        if k < depth - 1: z_copies[k].wait_send()

def reduce_rows(a, extra, b, cid, gains=None):
    tokens, width = b.shape
    depth = 4
    rows = HD + extra.shape[0] // 32
    D = pltpu.SemaphoreType.DMA
    lanes = 256
    padded = jnp.zeros((32, lanes), f32)
    if gains is not None:
        padded = jnp.pad(gains, ((0, 0), (0, lanes - gains.shape[1])))
    padded = padded.reshape(4, depth, 2, lanes).transpose(2, 0, 1, 3)
    padded = jnp.pad(padded, ((0, 0), (0, 0), (0, 8 - depth), (0, 0))).reshape(64, lanes)
    return pl.pallas_call(
        functools.partial(reduce_kernel, rows, 4),
        out_shape=[
            jax.ShapeDtypeStruct((width, HD), f32),
            jax.ShapeDtypeStruct((width, (rows - HD) // 2), f32),
            jax.ShapeDtypeStruct((width, (rows - HD) // 2), f32),
            jax.ShapeDtypeStruct((1, lanes), f32),
        ],
        in_specs=[pl.BlockSpec(memory_space=pltpu.VMEM)] * 4,
        out_specs=[pl.BlockSpec(memory_space=pltpu.VMEM)] * 4,
        scratch_shapes=[
            pltpu.VMEM((rows, width), f32),
            pltpu.VMEM((2, 4 * rows, width), bf16),
            pltpu.VMEM((depth, 4 * rows, width), bf16),
            pltpu.VMEM((depth, 4 * rows, width), bf16),
            pltpu.VMEM((depth, 2, rows // 2, width), bf16),
            pltpu.VMEM((depth, 2, rows, width), bf16),
            pltpu.VMEM((depth - 1, rows, width), bf16),
            pltpu.VMEM((depth, rows, width), bf16),
            D((2,)), D((depth,)), D((depth, 2)), D((depth, 2)), D((depth, 2)), D((depth, 2)), D((depth - 1,)), D((depth,)),
            pltpu.VMEM((32, lanes), f32), pltpu.VMEM((3, 32, lanes), f32), pltpu.VMEM((depth, 1, lanes), f32),
            D((3,)), D((3,)), D((depth - 1,)), D((depth,)),
        ],
        compiler_params=pltpu.CompilerParams(vmem_limit_bytes=60*1024*1024, collective_id=cid, has_side_effects=True),
        cost_estimate=pl.CostEstimate(flops=2*tokens*32*rows*width, bytes_accessed=10_000_000, transcendentals=0),
    )(a, extra, b, padded)


ROUTE_LANES = 128


def picks_of(routing, first, local_experts, capacity):
    rows = routing.shape[0]
    lanes = lax.broadcasted_iota(jnp.int32, (rows, ROUTE_LANES), 1)
    places = lax.broadcasted_iota(jnp.int32, (rows, local_experts * capacity), 1)
    hit, weighted = None, 0.0
    for e in range(local_experts):

        def column(base):
            return jnp.sum(jnp.where(lanes == base + first + e, routing, 0.0), axis=1, keepdims=True)

        slot = column(0).astype(jnp.int32)
        here = places == jnp.where(slot >= 0, slot + e * capacity, -1)
        hit = here if hit is None else hit | here
        weighted = weighted + jnp.where(here, column(32) + column(64), 0.0)
    return jnp.where(hit, 1.0, 0.0).astype(bf16), weighted.astype(bf16)


def pick_kernel(capacity, local_experts, n_alias, tok_ref, cot_a, cot_b, *refs):
    x_ref, dy_ref = refs[n_alias:]
    width = cot_a.shape[3]
    cot = jnp.concatenate([cot_a[0, 0], cot_b[0, 0]], axis=0)
    first = lax.axis_index("expert") * local_experts
    routing = tok_ref[0, :, width:]
    hit, _ = picks_of(routing.astype(f32), first, local_experts, capacity)
    x = mm(hit, tok_ref[0, :, :width], TN).astype(bf16)
    rows = mm(hit, routing, TN)
    lanes = lax.broadcasted_iota(jnp.int32, rows.shape, 1)
    owner = lax.broadcasted_iota(jnp.int32, rows.shape, 0) // capacity
    at = lanes - first - owner
    weight = jnp.sum(jnp.where((at == 32) | (at == 64), rows, 0.0), axis=1, keepdims=True)
    dy = (mm(hit, cot, TN) * weight).astype(bf16)
    for e in range(local_experts):
        x_ref[e, 0, 0] = x[e * capacity : (e + 1) * capacity]
        dy_ref[e, 0, 0] = dy[e * capacity : (e + 1) * capacity]


def expert_kernel(n_alias, *refs):
    x_ref, dy_ref = refs[:2]
    parts = (refs[2:7], refs[7:12], refs[12:17])
    z_ref, dg_ref, du_ref, y_ref, dx_ref, wg, wu, wd, sems = refs[17 + n_alias :]
    local_experts, width, _ = wg.shape
    at = lax.axis_index("dp")
    size = width // 4
    places = (at, at + 1 - 2 * (at % 2), (at + 2) % 4, 3 - at, 3 - at)

    def copies(e):
        out = []
        for m, full in enumerate((wg, wu, wd)):
            for p in range(4):
                part = parts[m][p] if p < 3 else parts[m][3 + e]
                src = part.at[e] if p < 3 else part.at[0]
                where = pl.ds(pl.multiple_of(places[p] * size, size), size)
                dst = full.at[e, where, :] if m < 2 else full.at[e, :, where]
                out.append(pltpu.make_async_copy(src, dst, sems.at[e, m, p]))
        return out

    expert, chunk = pl.program_id(0), pl.program_id(1)

    @pl.when((expert == 0) & (chunk == 0))
    def _():
        for e in range(local_experts):
            for c in copies(e):
                c.start()

    for e in range(local_experts):

        @pl.when((expert == e) & (chunk == 0))
        def _(e=e):
            for c in copies(e):
                c.wait()

    x, dy = x_ref[0, 0], dy_ref[0, 0]
    gate = mm(x, wg[expert])
    up = mm(x, wu[expert])
    d_hidden = mm(dy, wd[expert], NT)
    sig = 1.0 / (1.0 + jnp.exp(-gate))
    silu = gate * sig
    z = (silu * up).astype(bf16)
    d_gate = (d_hidden * up * sig * (1.0 + gate * (1.0 - sig))).astype(bf16)
    d_up = (d_hidden * silu).astype(bf16)
    z_ref[0, 0] = z
    dg_ref[0, 0] = d_gate
    du_ref[0, 0] = d_up
    dx_ref[0] = (mm(d_gate, wg[expert], NT) + mm(d_up, wu[expert], NT)).astype(bf16)
    y_ref[0] = mm(z, wd[expert]).astype(bf16)


def sum_kernel(capacity, routing_ref, y_ref, dx_ref, mix_ref, da_ref):
    local_experts, _, _, width = y_ref.shape
    first = lax.axis_index("expert") * local_experts
    hit, weighted = picks_of(routing_ref[0].astype(f32), first, local_experts, capacity)
    da_ref[...] = mm(hit, dx_ref[...].reshape(local_experts * capacity, width)).astype(bf16)
    mix_ref[...] = mm(weighted, y_ref[...].reshape(local_experts * capacity, width)).astype(bf16)


def run_experts(tokens, cot, parts, capacity, batch_at, micro, earlier):
    blocks, rows, _ = tokens.shape
    width = cot[0][0].shape[3]
    local_experts, _, hidden = parts[0][0].shape
    flat = [p for group in parts for p in group]
    any_spec = pl.BlockSpec(memory_space=pl.ANY)
    params = pltpu.CompilerParams(vmem_limit_bytes=VMEM_LIMIT)
    slots = blocks * capacity
    picked_spec = pl.BlockSpec((local_experts, 1, 1, capacity, width), lambda b: (0, batch_at, b, 0, 0))
    picked = jax.ShapeDtypeStruct((local_experts, micro, blocks, capacity, width), bf16)
    x, dy = pl.pallas_call(
        functools.partial(pick_kernel, capacity, local_experts, len(earlier[:2])),
        grid=(blocks,),
        in_specs=[
            pl.BlockSpec((1, rows, tokens.shape[2]), lambda b: (b, 0, 0)),
        ]
        + [pl.BlockSpec((1, 1, rows // 2, width), lambda b, i=i: (b, i, 0, 0)) for _, i in cot]
        + [any_spec] * len(earlier[:2]),
        out_specs=[picked_spec] * 2,
        out_shape=[picked] * 2,
        input_output_aliases={3 + i: i for i in range(len(earlier[:2]))},
        compiler_params=params,
        cost_estimate=LIGHT,
    )(tokens, cot[0][0], cot[1][0], *[a.reshape(picked.shape) for a in earlier[:2]])
    x, dy = (a.reshape(local_experts, micro, slots, width) for a in (x, dy))
    chunk = slots // 2
    row_spec = pl.BlockSpec((1, 1, chunk, width), lambda e, i: (e, batch_at, i, 0))
    hid_spec = pl.BlockSpec((1, 1, chunk, hidden), lambda e, i: (e, batch_at, i, 0))
    out_spec = pl.BlockSpec((1, chunk, width), lambda e, i: (e, i, 0))
    hid = jax.ShapeDtypeStruct((local_experts, micro, slots, hidden), bf16)
    out = jax.ShapeDtypeStruct((local_experts, slots, width), bf16)
    z, dg, du, y, dx = pl.pallas_call(
        functools.partial(expert_kernel, len(earlier[2:])),
        grid=(local_experts, 2),
        in_specs=[row_spec, row_spec] + [any_spec] * (len(flat) + len(earlier[2:])),
        out_specs=[hid_spec] * 3 + [out_spec] * 2,
        out_shape=[hid] * 3 + [out] * 2,
        input_output_aliases={2 + len(flat) + i: i for i in range(len(earlier[2:]))},
        scratch_shapes=[
            pltpu.VMEM((local_experts, width, hidden), bf16),
            pltpu.VMEM((local_experts, width, hidden), bf16),
            pltpu.VMEM((local_experts, hidden, width), bf16),
            pltpu.SemaphoreType.DMA((local_experts, 3, 4)),
        ],
        compiler_params=params,
        cost_estimate=LIGHT,
    )(x, dy, *flat, *earlier[2:])
    y, dx = (a.reshape(local_experts, blocks, capacity, width) for a in (y, dx))
    part_spec = pl.BlockSpec((local_experts, 1, capacity, width), lambda b: (0, b, 0, 0))
    sums = jax.ShapeDtypeStruct((blocks * rows, width), bf16)
    sums_spec = pl.BlockSpec((rows, width), lambda b: (b, 0))
    mix, da = pl.pallas_call(
        functools.partial(sum_kernel, capacity),
        grid=(blocks,),
        in_specs=[
            pl.BlockSpec((1, rows, ROUTE_LANES), lambda b: (b, 0, width // ROUTE_LANES)),
            part_spec,
            part_spec,
        ],
        out_specs=[sums_spec] * 2,
        out_shape=[sums] * 2,
        compiler_params=params,
        cost_estimate=LIGHT,
    )(tokens, y, dx)
    return [x, dy, z, dg, du], mix, da


def slots_of(route_ids, gate_vals, ranking, capacity, experts):
    rows = route_ids.shape[0]
    pair_experts = route_ids.reshape(-1)
    earlier = (pair_experts[None, :] == pair_experts[:, None]) & (
        ranking[None, :] < ranking[:, None]
    )
    slot = jnp.sum(earlier.astype(jnp.int32), axis=1).reshape(rows, -1)
    kept = slot < capacity
    chosen = route_ids[:, :, None] == jnp.arange(experts, dtype=jnp.int32)[None, None, :]
    chosen = chosen & kept[:, :, None]
    slot_map = jnp.sum(jnp.where(chosen, slot[:, :, None] + 1, 0), axis=1).astype(f32) - 1.0
    weight_map = jnp.sum(jnp.where(chosen, gate_vals[:, :, None], 0.0), axis=1)
    return slot_map, weight_map


def swap(values, bit):
    return lax.ppermute(values, "dp", [(i, i ^ bit) for i in range(lax.axis_size("dp"))])


def dp_part(total, axis, bits, expert, count=1):
    size = total.shape[axis] // 4
    start, sizes = [expert, 0, 0], list(total.shape)
    start[axis] = (lax.axis_index("dp") ^ bits) * size
    sizes[0], sizes[axis] = count, size
    return lax.dynamic_slice(total, start, sizes)


def scatter_far(total, axis):
    return swap(dp_part(total, axis, 3, 0), 1), swap(dp_part(total, axis, 3, 1), 2), total


def scatter_add(pieces, axis):
    for_y, for_x, total = pieces
    near_x = dp_part(total, axis, 1, 0, 2).astype(f32) + jnp.pad(for_x.astype(f32), ((1, 0), (0, 0), (0, 0)))
    near_y = dp_part(total, axis, 2, 0, 2).astype(f32) + jnp.pad(for_y.astype(f32), ((0, 1), (0, 0), (0, 0)))
    return near_x.astype(bf16), near_y.astype(bf16), total


def scatter_near(pieces, axis):
    near_x, near_y, total = scatter_add(pieces, axis)
    return swap(near_x, 1), swap(near_y, 2), total


def scatter_sum(pieces, axis):
    by_x, by_y, total = pieces
    return dp_part(total, axis, 0, 0, total.shape[0]).astype(f32) + by_x.astype(f32) + by_y.astype(f32)


def body_plain(
    inputs,
    cotangent,
    membership,
    routes,
    gate_weights,
    pair_order,
    w_query,
    w_key,
    w_value,
    w_output,
    norm_gains,
    w_gate,
    w_up,
    w_down,
):
    micro = inputs.shape[0]
    rows = inputs.shape[2]
    width = inputs.shape[3]
    group_len = membership.shape[2]
    member = lax.axis_index("expert")
    blocks = lax.axis_size("expert")
    shards = blocks * lax.axis_size("dp")
    shard_at = lax.axis_index("dp") * blocks + member
    local_experts = w_gate.shape[0]
    experts = local_experts * blocks
    capacity = rows * TOPK // experts
    step_heads = max(1, 384 // rows)
    total = micro * rows
    q_part, k_part, v_part = w_query.shape[1], w_key.shape[1], w_value.shape[1]

    gain_len = norm_gains.shape[0]
    gain_shard = jnp.zeros((2048,), bf16).at[:gain_len].set(norm_gains).reshape(16, 128)
    gain_full = lax.all_gather(gain_shard, BOTH, axis=0, tiled=True)
    gains = gain_full.reshape(shards, 2048)[:, :gain_len].reshape(-1).astype(f32)
    gain_in = gains[:width]
    gain_mid = gains[width : 2 * width]
    gain_q = gains[2 * width : 2 * width + HD]
    gain_k = gains[2 * width + HD :]

    qkv_w = lax.all_gather(
        jnp.concatenate([w_query.T, w_key.T, w_value.T], axis=0), BOTH, axis=0, tiled=True
    )
    out_w = lax.all_gather(w_output, BOTH, axis=0, tiled=True)
    wg = lax.all_gather(w_gate, "dp", axis=1, tiled=True)
    wu = lax.all_gather(w_up, "dp", axis=1, tiled=True)
    wd = lax.all_gather(w_down, "dp", axis=2, tiled=True)

    slot_map, weight_map = jax.vmap(
        lambda r, g, o: slots_of(r, g, o, capacity, experts)
    )(routes[:, 0], gate_weights[:, 0], pair_order[:, 0, 0])
    routing = jnp.concatenate([slot_map, weight_map], axis=-1)
    routing = lax.all_gather(routing, "expert", axis=0, tiled=False)
    mine = member * local_experts
    slot_mine = lax.dynamic_slice_in_dim(routing, mine, local_experts, axis=3)
    weight_mine = lax.dynamic_slice_in_dim(routing, experts + mine, local_experts, axis=3)
    slot_mine = jnp.transpose(slot_mine, (1, 3, 0, 2))
    weight_mine = jnp.transpose(weight_mine, (1, 3, 0, 2))
    slot_ids = jnp.arange(capacity, dtype=f32)
    hit = slot_mine[:, :, :, None, :] == slot_ids[None, None, None, :, None]
    pick = hit.astype(bf16)
    weighted = jnp.where(hit, weight_mine[:, :, :, None, :], 0.0)
    slot_weight = jnp.sum(weighted, axis=-1)
    weighted = weighted.astype(bf16)

    key_index = jnp.arange(group_len, dtype=jnp.int32)
    start_row = member * rows
    segment = membership[:, 0]
    row_index = start_row + jnp.arange(rows, dtype=jnp.int32)
    seg_rows = lax.dynamic_slice_in_dim(segment, start_row, rows, axis=1)
    before = jnp.sum((segment[:, None, :] < seg_rows[:, :, None]).astype(jnp.int32), axis=2)
    position = jnp.where(seg_rows == 0, row_index[None], PROMPT + row_index[None] - before)
    allowed = (key_index[None, :, None] <= row_index[None, None, :]) & (
        (segment[:, :, None] == 0) | (segment[:, :, None] == seg_rows[:, None, :])
    )
    bias = jnp.tile(jnp.where(allowed, 0.0, MASKED).astype(f32), (1, 1, step_heads))
    frequency = ROPE_BASE ** (-(jnp.arange(HD // 2, dtype=f32) * 2.0 / HD))
    angles = position.astype(f32).reshape(total)[:, None] * frequency[None, :]
    cosine = jnp.cos(angles)[:, None, :]
    sine_part = jnp.sin(angles)[:, None, :]

    hidden = inputs[:, 0].astype(f32).reshape(total, width)
    scale_in = rms_scale(hidden)
    normed = (hidden * scale_in * gain_in).astype(bf16)
    proj = mm(normed, qkv_w, NT).reshape(total, shards, q_part + k_part + v_part)
    queries = proj[:, :, :q_part].reshape(total, H, HD)
    key_pre = proj[:, :, q_part : q_part + k_part].reshape(total, KVH, HD)
    value = proj[:, :, q_part + k_part :].reshape(total, KVH, HD).astype(bf16)
    scale_q = rms_scale(queries)
    scale_k = rms_scale(key_pre)
    q_low = rotate(queries * scale_q * (gain_q * (SCALE * LOG2E)), cosine, sine_part).astype(bf16)
    q_low = q_low.reshape(micro, rows, H * HD)
    k_low = rotate(key_pre * scale_k * gain_k, cosine, sine_part).astype(bf16)
    kv_own = jnp.concatenate([k_low, value], axis=-1).reshape(micro, rows, KVH * 2 * HD)
    kv_all = lax.all_gather(kv_own, "expert", axis=0, tiled=False)
    chunk = 256
    mixed = []
    for at in range(micro):
        mixed = run_forward(q_low, kv_all[:, at : at + 1], bias, step_heads, chunk, at, mixed)
    mixed, logs = mixed

    branch = mm(mixed.reshape(total, H * HD), out_w)
    middle = hidden + branch
    scale_mid = rms_scale(middle)
    routed = (middle * scale_mid * gain_mid).astype(bf16).reshape(micro, rows, width)
    middle = middle.reshape(micro, rows, width)
    scale_mid = scale_mid.reshape(micro, rows, 1)

    outputs, d_branches, d_middles = [], [], []
    acc_gate = acc_up = acc_down = 0.0
    grad_mid = 0.0
    slots = blocks * capacity
    for at in range(micro):
        d_out = lax.all_gather(cotangent[at, 0], "expert", axis=0, tiled=False)
        tokens = lax.all_gather(routed[at], "expert", axis=0, tiled=False)
        picked = jnp.einsum("ebst,btd->ebsd", pick[at], tokens, preferred_element_type=f32)
        picked = picked.astype(bf16).reshape(local_experts, slots, width)
        d_result = jnp.einsum("ebst,btd->ebsd", pick[at], d_out, preferred_element_type=f32)
        d_result = (d_result * slot_weight[at][..., None]).astype(bf16)
        d_result = d_result.reshape(local_experts, slots, width)
        gate_pre = jnp.einsum("erd,edf->erf", picked, wg, preferred_element_type=f32)
        up_pre = jnp.einsum("erd,edf->erf", picked, wu, preferred_element_type=f32)
        d_hidden = jnp.einsum("erd,efd->erf", d_result, wd, preferred_element_type=f32)
        sigmoid_g = jax.nn.sigmoid(gate_pre)
        silu_g = gate_pre * sigmoid_g
        hidden_low = (silu_g * up_pre).astype(bf16)
        d_gate = (d_hidden * up_pre * sigmoid_g * (1.0 + gate_pre * (1.0 - sigmoid_g))).astype(bf16)
        d_up = (d_hidden * silu_g).astype(bf16)
        d_rows = jnp.einsum("erf,edf->erd", d_gate, wg, preferred_element_type=f32)
        d_rows = d_rows + jnp.einsum("erf,edf->erd", d_up, wu, preferred_element_type=f32)
        d_rows = d_rows.astype(bf16).reshape(local_experts, blocks, capacity, width)
        d_part = jnp.einsum("ebst,ebsd->btd", pick[at], d_rows, preferred_element_type=f32)
        d_part = d_part.astype(bf16).reshape(group_len, width)
        d_routed = lax.psum_scatter(d_part, "expert", scatter_dimension=0, tiled=True).astype(f32)
        result = jnp.einsum("erf,efd->erd", hidden_low, wd, preferred_element_type=f32)
        result = result.astype(bf16).reshape(local_experts, blocks, capacity, width)
        part = jnp.einsum("ebst,ebsd->btd", weighted[at], result, preferred_element_type=f32)
        part = part.astype(bf16).reshape(group_len, width)
        expert_mix = lax.psum_scatter(part, "expert", scatter_dimension=0, tiled=True).astype(f32)
        outputs.append((middle[at] + expert_mix).astype(bf16))

        acc_down += jnp.einsum("erf,erd->efd", hidden_low, d_result, preferred_element_type=f32)
        acc_gate += jnp.einsum("erd,erf->edf", picked, d_gate, preferred_element_type=f32)
        acc_up += jnp.einsum("erd,erf->edf", picked, d_up, preferred_element_type=f32)

        d_mid_norm, mid_gain_grad = norm_back(d_routed, middle[at], scale_mid[at], gain_mid)
        grad_mid = grad_mid + mid_gain_grad
        d_middle = cotangent[at, 0].astype(f32) + d_mid_norm
        d_middles.append(d_middle)
        d_branches.append(d_middle.astype(bf16))

    grad_gate = lax.psum_scatter(acc_gate.astype(bf16), "dp", scatter_dimension=1, tiled=True)
    grad_up = lax.psum_scatter(acc_up.astype(bf16), "dp", scatter_dimension=1, tiled=True)
    grad_down = lax.psum_scatter(acc_down.astype(bf16), "dp", scatter_dimension=2, tiled=True)

    d_branch = jnp.concatenate(d_branches, axis=0)
    d_middle = jnp.concatenate(d_middles, axis=0)
    grad_output = mm(mixed.reshape(total, H * HD), d_branch, TN).astype(bf16)
    grad_output = lax.psum_scatter(grad_output, BOTH, scatter_dimension=0, tiled=True)
    d_mixed = mm(d_branch, out_w, NT).astype(bf16).reshape(micro, rows, H * HD)
    cos_rows = jnp.concatenate([cosine, cosine], axis=-1).reshape(micro, rows, HD)
    sine_rows = jnp.concatenate([-sine_part, sine_part], axis=-1).reshape(micro, rows, HD)
    q_raw = queries.reshape(micro, rows, H * HD)
    d_query, dkv_list, grad_qn = [], [], 0.0
    for at in range(micro):
        d_query, dkv_one, part = run_backward(
            q_low, kv_all[:, at : at + 1], bias, mixed, d_mixed, logs, q_raw, cos_rows, sine_rows,
            gain_q[None, :], step_heads, chunk, at, [d_query] if at else []
        )
        dkv_list.append(dkv_one)
        grad_qn += part[0]
    dkv_all = jnp.concatenate(dkv_list, axis=1)
    dkv = lax.psum_scatter(dkv_all, "expert", scatter_dimension=0, tiled=False)
    dkv = dkv.reshape(total, KVH, 2 * HD)
    d_key = rotate(dkv[:, :, :HD].astype(f32), cosine, -sine_part)
    d_key, grad_kn = norm_back(d_key, key_pre, scale_k, gain_k)
    d_proj = jnp.concatenate(
        [
            d_query.reshape(total, shards, q_part),
            d_key.astype(bf16).reshape(total, shards, k_part),
            dkv[:, :, HD:].reshape(total, shards, v_part),
        ],
        axis=-1,
    ).reshape(total, -1)
    grad_qkv = mm(d_proj, normed, TN).astype(bf16)
    grad_qkv = lax.psum_scatter(grad_qkv, BOTH, scatter_dimension=0, tiled=True).astype(f32)
    d_normed = mm(d_proj, qkv_w)
    d_in_norm, grad_in = norm_back(d_normed, hidden, scale_in, gain_in)
    input_grad = d_middle + d_in_norm

    gain_grads = jnp.concatenate([grad_in, grad_mid, grad_qn, grad_kn]).reshape(shards, gain_len)
    gain_grads = jnp.pad(gain_grads, ((0, 0), (0, 256 - gain_len % 256)))
    gain_all = lax.all_gather(gain_grads, BOTH, axis=0, tiled=False)
    grad_gains = jnp.sum(lax.dynamic_index_in_dim(gain_all, shard_at, axis=1, keepdims=False), axis=0)
    return (
        jnp.stack(outputs)[:, None],
        input_grad.reshape(micro, 1, rows, width),
        grad_qkv[:q_part].T,
        grad_qkv[q_part : q_part + k_part].T,
        grad_qkv[q_part + k_part :].T,
        grad_output.astype(f32),
        grad_gains[:gain_len],
        grad_gate.astype(f32),
        grad_up.astype(f32),
        grad_down.astype(f32),
    )


def body_fast(
    inputs,
    cotangent,
    membership,
    routes,
    gate_weights,
    pair_order,
    w_query,
    w_key,
    w_value,
    w_output,
    norm_gains,
    w_gate,
    w_up,
    w_down,
):
    micro = inputs.shape[0]
    rows = inputs.shape[2]
    width = inputs.shape[3]
    group_len = membership.shape[2]
    member = lax.axis_index("expert")
    blocks = lax.axis_size("expert")
    shards = blocks * lax.axis_size("dp")
    local_experts = w_gate.shape[0]
    experts = local_experts * blocks
    capacity = rows * TOPK // experts
    step_heads = max(1, 384 // rows)
    total = micro * rows
    q_part, k_part, v_part = w_query.shape[1], w_key.shape[1], w_value.shape[1]
    tie = lax.optimization_barrier

    slot_map, weight_map = jax.vmap(
        lambda r, g, o: slots_of(r, g, o, capacity, experts)
    )(routes[:, 0], gate_weights[:, 0], pair_order[:, 0, 0])
    weight_high = tie(weight_map.astype(bf16))
    weight_low = (weight_map - weight_high.astype(f32)).astype(bf16)

    def padded(values, lanes):
        return jnp.pad(values, ((0, 0), (0, 0), (0, lanes - experts)))

    routing = jnp.concatenate(
        [
            padded(slot_map.astype(bf16), 32),
            padded(weight_high, 32),
            padded(weight_low, ROUTE_LANES - 64),
        ],
        axis=-1,
    )

    gain_len = norm_gains.shape[0]
    gain_shard = jnp.pad(norm_gains[None], ((0, 15), (0, 256 - gain_len)))
    kv_w = jnp.concatenate([w_key.T, w_value.T], axis=0)
    halves = cotangent.reshape(2 * micro, rows // 2, width)
    cot_first = halves[:3].reshape(-1, width)
    q_w, kv_w, out_w, gain_full, cot_first = gather_rows(
        [w_query.T, kv_w, w_output, gain_shard, cot_first], [(3, 0, 1, 2)], 1, (4,)
    )
    cot_first = cot_first.reshape(blocks, 3, rows // 2, width)
    q_w, w_gate = tie((q_w, w_gate))
    gains = gain_full.reshape(shards, 16, 256)[:, 0, :gain_len].reshape(-1).astype(f32)
    gain_in = gains[:width]
    gain_mid = gains[width : 2 * width]
    gain_q = gains[2 * width : 2 * width + HD]
    gain_k = gains[2 * width + HD :]

    key_index = jnp.arange(group_len, dtype=jnp.int32)
    start_row = member * rows
    segment = membership[:, 0]
    row_index = start_row + jnp.arange(rows, dtype=jnp.int32)
    seg_rows = lax.dynamic_slice_in_dim(segment, start_row, rows, axis=1)
    before = jnp.sum((segment[:, None, :] < seg_rows[:, :, None]).astype(jnp.int32), axis=2)
    position = jnp.where(seg_rows == 0, row_index[None], PROMPT + row_index[None] - before)
    allowed = (key_index[None, :, None] <= row_index[None, None, :]) & (
        (segment[:, :, None] == 0) | (segment[:, :, None] == seg_rows[:, None, :])
    )
    bias = jnp.tile(jnp.where(allowed, 0.0, MASKED).astype(f32), (1, 1, step_heads))
    frequency = ROPE_BASE ** (-(jnp.arange(HD // 2, dtype=f32) * 2.0 / HD))
    angles = position.astype(f32).reshape(total)[:, None] * frequency[None, :]
    cosine, sine = jnp.cos(angles), jnp.sin(angles)
    cosine = jnp.concatenate([cosine, cosine], axis=-1)
    sine = jnp.concatenate([-sine, sine], axis=-1)
    gain_q, gain_k = gain_q[None, :], gain_k[None, :]

    hidden = inputs[:, 0].astype(f32).reshape(total, width)
    scale_in = rms_scale(hidden)
    normed = (hidden * scale_in * gain_in).astype(bf16)
    q_low, q_raw, k_raw, kv_w, kv_0, kv_1 = run_project(
        normed, q_w, kv_w, cosine, sine, gain_q * (SCALE * LOG2E), gain_k, micro
    )
    q_low, q_raw = (a.reshape(micro, rows, H * HD) for a in (q_low, q_raw))
    gate_near = (swap(w_gate, 1), swap(w_gate, 2))
    kv_0, gate_near, w_up, w_down = tie((kv_0, gate_near, w_up, w_down))
    kv_0 = lax.all_gather(kv_0, "expert", axis=0, tiled=False)
    kv_1 = lax.all_gather(kv_1, "expert", axis=0, tiled=False)
    up_near, down_near = ((swap(w, 1), swap(w, 2)) for w in (w_up, w_down))
    chunk = 256

    def middle_of(mixed, at):
        part = hidden[at * rows : (at + 1) * rows]
        middle = part + mm(mixed[at], out_w)
        routed = (middle * rms_scale(middle) * gain_mid).astype(bf16)
        return middle, jnp.concatenate([routed, routing[at]], axis=-1)

    mixed, logs, shares = run_forward(q_low, kv_0[:, None], bias, step_heads, chunk, 0, [], True)
    middle_0, routed_0 = middle_of(mixed, 0)
    mixed, kv_1, routed_0, up_near, down_near = tie((mixed, kv_1, routed_0, up_near, down_near))
    kv_all = [kv_0[:, None], kv_1[:, None]]
    mixed, logs, shares = run_forward(
        q_low, kv_all[1], bias, step_heads, chunk, 1, [mixed, logs, shares], True
    )
    middle_1, routed_1 = middle_of(mixed, 1)
    parts = [
        (own, near[0], near[1], swap(near[0][:1], 2), swap(near[1][1:], 1))
        for own, near in ((w_gate, gate_near), (w_up, up_near), (w_down, down_near))
    ]
    routed_1, parts, cot_last = tie((routed_1, parts, halves[3]))
    cot_last = lax.all_gather(cot_last, "expert", axis=0, tiled=False)[:, None]
    cots = [((cot_first, 0), (cot_first, 1)), ((cot_first, 2), (cot_last, 0))]
    routed = [routed_0, routed_1]
    middle = jnp.stack([middle_0, middle_1])

    mix_parts, d_routeds = [], []
    kept = []
    for at in range(micro):
        tokens = lax.all_gather(routed[at], "expert", axis=0, tiled=False)
        tokens, parts = tie((tokens, parts))
        kept, mix, d_part = run_experts(tokens, cots[at], parts, capacity, at, micro, kept)
        kept, d_part, mix, d_routeds = tie((kept, d_part, mix, d_routeds))
        mix_parts.append(mix)
        d_routed = lax.psum_scatter(d_part, "expert", scatter_dimension=0, tiled=True)
        d_routeds.append(d_routed)
    picked, d_result, hidden_low, d_gate, d_up = (
        a.reshape(local_experts, -1, a.shape[-1]) for a in kept
    )

    def weight_grad(rows_in, rows_out):
        return jnp.einsum("era,erb->eab", rows_in, rows_out, preferred_element_type=f32).astype(bf16)

    first = scatter_far(weight_grad(picked, d_gate), 1)
    second = scatter_far(weight_grad(picked, d_up), 1)
    first, hidden_low = tie((first, hidden_low))
    first = scatter_near(first, 1)
    third = weight_grad(hidden_low, d_result)
    d_routeds[-1], first, second, third, mix_parts[0] = tie(
        (d_routeds[-1], first, second, third, mix_parts[0])
    )
    second = scatter_add(second, 1)
    d_routeds[-1], second, third = tie((d_routeds[-1], second, third))
    second = (swap(second[0], 1), swap(second[1], 2), second[2])
    third = scatter_far(third, 2)
    d_mixed, d_middle, d_branch, grad_mid = run_middle_back(
        d_routeds, middle, cotangent[:, 0], gain_mid[None, :], out_w
    )
    d_mixed, d_branch, third = tie((d_mixed, d_branch, third))
    third = scatter_near(third, 2)
    d_mixed = d_mixed.reshape(micro, rows, H * HD)
    cos_rows, sine_rows = (a.reshape(micro, rows, HD) for a in (cosine, sine))
    def share(core):
        part = lax.dynamic_index_in_dim(shares, core, axis=0, keepdims=False)
        part = part.reshape(2, total, -1)
        return jnp.einsum("zta,td->zad", part, d_branch, preferred_element_type=f32).astype(bf16)

    core = member % 2
    pairs = [(i, i ^ 1) for i in range(blocks)]
    got = lax.ppermute(share(1 - core), "expert", pairs)
    mixes = [lax.psum_scatter(mix_parts[0], "expert", scatter_dimension=0, tiled=True)]

    def backward(at, earlier):
        d_query, dkv_one, part = run_backward(
            q_low, kv_all[at], bias, mixed, d_mixed, logs, q_raw, cos_rows, sine_rows, gain_q,
            step_heads, chunk, at, earlier
        )
        return d_query, dkv_one[:, 0], part

    d_query, dkv_0, gain_0 = backward(0, [])
    d_query, dkv_0, got, second = tie((d_query, dkv_0, got, second))
    dkv_0 = lax.psum_scatter(dkv_0, "expert", scatter_dimension=0, tiled=False)
    out_grad = tie(share(core))
    out_grad = (out_grad.astype(f32) + got.astype(f32)).astype(bf16)
    d_query, out_grad = tie((d_query, out_grad))
    out_grad = scatter_far(out_grad, 1)
    d_query, dkv_1, gain_1 = backward(1, [d_query])
    grad_qn = gain_0 + gain_1
    d_query, dkv_1, out_grad, mixes, third = tie((d_query, dkv_1, out_grad, mixes, third))
    dkv_1 = lax.psum_scatter(dkv_1, "expert", scatter_dimension=0, tiled=False)
    out_grad = scatter_add(out_grad, 1)
    out_grad, first, second, third, d_query = tie((out_grad, first, second, third, d_query))
    out_grad = (swap(out_grad[0], 1), swap(out_grad[1], 2), out_grad[2])
    out_grad = scatter_sum(out_grad, 1).astype(bf16).reshape(-1, width)
    d_query = d_query.reshape(total, H * HD)
    dkv = jnp.concatenate([dkv_0, dkv_1], axis=0)
    dkv = dkv.reshape(total, KVH * 2 * HD)
    mix_part, dkv = tie((mix_parts[1], dkv))
    mixes.append(lax.psum_scatter(mix_part, "expert", scatter_dimension=0, tiled=True))
    outputs = [(middle[at] + mixes[at].astype(f32)).astype(bf16) for at in range(micro)]
    expert_grads = [scatter_sum(first, 1), scatter_sum(second, 1), scatter_sum(third, 2)]
    d_normed = mm(d_query, q_w)
    dkv, out_grad, expert_grads, d_normed = tie((dkv, out_grad, expert_grads, d_normed))
    dkv, dkv_t, grad_kn = run_key_back(dkv, k_raw, cosine, sine, gain_k)
    d_normed = d_normed + mm(dkv, kv_w)
    grad_output = lax.psum_scatter(
        out_grad,
        "expert",
        scatter_dimension=0,
        tiled=True,
        axis_index_groups=[list(range(c, blocks, 2)) for c in range(2)],
    ).astype(f32)
    d_in_norm, grad_in = norm_back(d_normed, hidden, scale_in, gain_in)
    input_grad = d_middle + d_in_norm
    gain_grads = jnp.concatenate([grad_in, grad_mid[0], grad_qn[0], grad_kn[0]]).reshape(shards, gain_len)
    grad_query, grad_key, grad_value, grad_gains = reduce_rows(d_query, dkv_t, normed, 3, gain_grads)
    return (
        jnp.stack(outputs)[:, None],
        input_grad.reshape(micro, 1, rows, width),
        grad_query,
        grad_key,
        grad_value,
        grad_output,
        grad_gains[0, :gain_len],
        *expert_grads,
    )


def solution(mesh):
    fast = mesh.shape["dp"] == 4 and mesh.shape["expert"] == 8
    return jax.shard_map(
        body_fast if fast else body_plain,
        mesh=mesh,
        in_specs=(
            P(None, "dp", "expert", None),
            P(None, "dp", "expert", None),
            P(None, "dp", None),
            P(None, "dp", "expert", None),
            P(None, "dp", "expert", None),
            P(None, "dp", "expert", None),
            P(None, ("dp", "expert")),
            P(None, ("dp", "expert")),
            P(None, ("dp", "expert")),
            P(("dp", "expert"), None),
            P(("dp", "expert")),
            P("expert", "dp", None),
            P("expert", "dp", None),
            P("expert", None, "dp"),
        ),
        out_specs=(
            P(None, "dp", "expert", None),
            P(None, "dp", "expert", None),
            P(None, ("dp", "expert")),
            P(None, ("dp", "expert")),
            P(None, ("dp", "expert")),
            P(("dp", "expert"), None),
            P(("dp", "expert")),
            P("expert", "dp", None),
            P("expert", "dp", None),
            P("expert", None, "dp"),
        ),
        check_vma=False,
    )
```

```python
import functools
import math

import jax
import jax.numpy as jnp
from jax import lax
from jax.experimental import pallas as pl
from jax.experimental.pallas import tpu as pltpu
from jax.sharding import PartitionSpec as P

H = 32
KVH = 4
HD = 128
FF = 768
TOPK = 8
PROMPT = 1024
PER_KV = H // KVH

EPSILON = 1e-06
ROPE_BASE = 1000000.0
MASKED = -1e30
LOG2E = math.log2(math.e)
SCALE = HD ** (-0.5)

bf16 = jnp.bfloat16
f32 = jnp.float32
NT = (((1,), (1,)), ((), ()))
TN = (((0,), (0,)), ((), ()))
NN = (((1,), (0,)), ((), ()))
BOTH = ("dp", "expert")
VMEM_LIMIT = 56 * 1024 * 1024
LIGHT = pl.CostEstimate(flops=1_000_000, bytes_accessed=1_000_000, transcendentals=0)


def mm(a, b, dims=NN):
    return lax.dot_general(a, b, dims, preferred_element_type=f32)


def rms_scale(values):
    return lax.rsqrt(jnp.mean(values * values, axis=-1, keepdims=True) + EPSILON)


def norm_back(upstream, values, inv_rms, norm_gain):
    lifted = upstream * norm_gain
    inner_dot = jnp.mean(lifted * values, axis=-1, keepdims=True)
    back_grad = inv_rms * lifted - values * (inv_rms * inv_rms * inv_rms) * inner_dot
    gain_grad = jnp.sum((upstream * values * inv_rms).reshape(-1, values.shape[-1]), axis=0)
    return (back_grad, gain_grad)


def rotate(values, cosine, sine_part):
    half_dim = values.shape[-1] // 2
    first_half = values[..., :half_dim]
    second_half = values[..., half_dim:]
    return jnp.concatenate(
        [
            first_half * cosine - second_half * sine_part,
            second_half * cosine + first_half * sine_part,
        ],
        axis=-1,
    )


def turn(values, cosine, sine):
    return values * cosine + pltpu.roll(values, HD // 2, 1) * sine


def project(x_ref, wq_ref, wkv_ref, cos_ref, sin_ref, gq_ref, gk_ref, q_ref, qraw_ref, kraw_ref, wkv_out, *kv_refs):
    x = x_ref[...]
    cosine, sine = cos_ref[...], sin_ref[...]
    for at in range(0, PER_KV * HD, 2 * HD):
        raw = mm(x, wq_ref[at : at + 2 * HD], NT)
        qraw_ref[:, at : at + 2 * HD] = raw
        for lane in (0, HD):
            head = raw[:, lane : lane + HD]
            normed = head * rms_scale(head) * gq_ref[...]
            q_ref[:, at + lane : at + lane + HD] = turn(normed, cosine, sine).astype(bf16)
    piece = HD // PER_KV
    w_k = [wkv_ref[2 * piece * i : 2 * piece * i + piece] for i in range(PER_KV)]
    w_v = [wkv_ref[2 * piece * i + piece : 2 * piece * (i + 1)] for i in range(PER_KV)]
    w_kv = jnp.concatenate(w_k + w_v, axis=0)
    wkv_out[...] = w_kv
    raw = mm(x, w_kv, NT)
    key = raw[:, :HD]
    kraw_ref[...] = key
    normed = key * rms_scale(key) * gk_ref[...]
    key, value = turn(normed, cosine, sine).astype(bf16), raw[:, HD:].astype(bf16)
    rows = x.shape[0] // len(kv_refs)
    for b, kv_ref in enumerate(kv_refs):
        kv_ref[:, :HD] = key[b * rows : (b + 1) * rows]
        kv_ref[:, HD:] = value[b * rows : (b + 1) * rows]


def run_project(x, wq, wkv, cosine, sine, gain_q, gain_k, micro):
    tokens, width = x.shape
    wide = PER_KV * HD
    whole = lambda a: pl.BlockSpec(a.shape, lambda g: (0, 0))
    cols = lambda n: pl.BlockSpec((tokens, n), lambda g: (0, g))
    rows = lambda n: pl.BlockSpec((n, width), lambda g: (g, 0))
    return pl.pallas_call(
        project,
        grid=(KVH,),
        in_specs=[whole(x), rows(wide), rows(2 * HD), whole(cosine), whole(sine), whole(gain_q), whole(gain_k)],
        out_specs=[cols(wide), cols(wide), cols(HD), rows(2 * HD)]
        + [pl.BlockSpec((tokens // micro, 2 * HD), lambda g: (0, g))] * micro,
        out_shape=[
            jax.ShapeDtypeStruct((tokens, H * HD), bf16),
            jax.ShapeDtypeStruct((tokens, H * HD), f32),
            jax.ShapeDtypeStruct((tokens, KVH * HD), f32),
            jax.ShapeDtypeStruct((KVH * 2 * HD, width), bf16),
        ]
        + [jax.ShapeDtypeStruct((tokens // micro, KVH * 2 * HD), bf16)] * micro,
        compiler_params=pltpu.CompilerParams(vmem_limit_bytes=VMEM_LIMIT),
        cost_estimate=LIGHT,
    )(x, wq, wkv, cosine, sine, gain_q, gain_k)


def norm_turn_back(grad, raw, cosine, sine, gain):
    grad = turn(grad, cosine, -sine)
    scale = rms_scale(raw)
    lifted = grad * gain
    inner = jnp.mean(lifted * raw, axis=-1, keepdims=True)
    back = scale * lifted - raw * (scale * scale * scale) * inner
    return back, jnp.sum(grad * raw * scale, axis=0, keepdims=True)


def key_back(dkv_ref, kraw_ref, cos_ref, sin_ref, gk_ref, out_ref, out_t_ref, gain_ref):
    gain_sum = 0.0
    for g in range(KVH):
        key = slice(2 * g * HD, (2 * g + 1) * HD)
        value = slice((2 * g + 1) * HD, (2 * g + 2) * HD)
        grad = dkv_ref[:, key].astype(f32)
        back, part = norm_turn_back(
            grad, kraw_ref[:, g * HD : (g + 1) * HD], cos_ref[...], sin_ref[...], gk_ref[...]
        )
        gain_sum += part
        low = back.astype(bf16)
        out_ref[:, key] = low
        out_t_ref[key] = low.T
        out_ref[:, value] = dkv_ref[:, value]
        out_t_ref[value] = dkv_ref[:, value].T
    gain_ref[...] = gain_sum


def run_key_back(dkv, key_raw, cosine, sine, gain):
    tokens, wide = dkv.shape
    return pl.pallas_call(
        key_back,
        out_shape=[
            jax.ShapeDtypeStruct((tokens, wide), bf16),
            jax.ShapeDtypeStruct((wide, tokens), bf16),
            jax.ShapeDtypeStruct((1, HD), f32),
        ],
        compiler_params=pltpu.CompilerParams(vmem_limit_bytes=VMEM_LIMIT),
    )(dkv, key_raw, cosine, sine, gain)


def attend_forward(step_heads, chunk, q_ref, kv_ref, bias_ref, o_ref, log_ref, o2_ref=None):
    group_len = bias_ref.shape[1]
    keys = kv_ref[:, 0, :, :HD].reshape(group_len, HD)
    values_t = kv_ref[:, 0, :, HD:].reshape(group_len, HD).T
    rows = q_ref.shape[1]
    for step in range(PER_KV // step_heads):
        heads = range(step * step_heads, (step + 1) * step_heads)
        query = jnp.concatenate([q_ref[0, :, h * HD : (h + 1) * HD] for h in heads], axis=0)
        mixed, row_sum = 0.0, 0.0
        for at in range(0, group_len, chunk):
            scores = mm(keys[at : at + chunk], query, NT)
            prob = jnp.exp2(scores + bias_ref[0, at : at + chunk, :])
            row_sum += jnp.sum(prob, axis=0, keepdims=True)
            mixed += mm(values_t[:, at : at + chunk], prob.astype(bf16))
        out = (mixed / row_sum).T.astype(bf16)
        for i, h in enumerate(heads):
            part = out[i * rows : (i + 1) * rows]
            o_ref[0, :, h * HD : (h + 1) * HD] = part
            if o2_ref is not None:
                lane = (h // 2) % 2 * HD
                o2_ref[h % 2, h // 4, 0, :, lane : lane + HD] = part
        log_ref[0, 0, step : step + 1, :] = jnp.log2(row_sum)


def attend_backward(
    step_heads, chunk, q_ref, kv_ref, bias_ref, o_ref, do_ref, log_ref, raw_ref, cos_ref, sin_ref, gain_ref,
    dq_ref, dkv_ref, gain_out, dk_acc, dv_acc
):
    group_len = bias_ref.shape[1]
    keys = kv_ref[:, 0, :, :HD].reshape(group_len, HD)
    values = kv_ref[:, 0, :, HD:].reshape(group_len, HD)
    keys_t = keys.T
    rows = q_ref.shape[1]
    cosine, sine, gain = cos_ref[0], sin_ref[0], gain_ref[...]

    @pl.when(pl.program_id(0) == 0)
    def _():
        gain_out[...] = jnp.zeros_like(gain_out)

    gain_sum = 0.0
    dk_acc[...] = jnp.zeros_like(dk_acc)
    dv_acc[...] = jnp.zeros_like(dv_acc)
    for step in range(PER_KV // step_heads):
        heads = range(step * step_heads, (step + 1) * step_heads)
        query = jnp.concatenate([q_ref[0, :, h * HD : (h + 1) * HD] for h in heads], axis=0)
        grad = jnp.concatenate([do_ref[0, :, h * HD : (h + 1) * HD] for h in heads], axis=0)
        mixed = jnp.concatenate([o_ref[0, :, h * HD : (h + 1) * HD] for h in heads], axis=0)
        row_dot = jnp.sum((grad.astype(f32) * mixed.astype(f32)).T, axis=0, keepdims=True)
        log_sum = log_ref[0, 0, step : step + 1, :]
        dq_t = 0.0
        for at in range(0, group_len, chunk):
            part = slice(at, at + chunk)
            scores = mm(keys[part], query, NT)
            prob = jnp.exp2(scores + (bias_ref[0, part, :] - log_sum))
            d_prob = mm(values[part], grad, NT)
            d_score = (prob * (d_prob - row_dot)).astype(bf16)
            dv_acc[part] += mm(prob.astype(bf16), grad)
            dk_acc[part] += mm(d_score, query)
            dq_t += mm(keys_t[:, part], d_score)
        out = (dq_t * SCALE).T.astype(bf16).astype(f32)
        for i, h in enumerate(heads):
            head = slice(h * HD, (h + 1) * HD)
            back, part = norm_turn_back(
                out[i * rows : (i + 1) * rows], raw_ref[0, :, head], cosine, sine, gain
            )
            dq_ref[0, :, head] = back.astype(bf16)
            gain_sum += part
    gain_out[...] += gain_sum
    blocks = dkv_ref.shape[0]
    dkv_ref[:, 0, :, :HD] = (dk_acc[...] * (1.0 / LOG2E)).astype(bf16).reshape(blocks, rows, HD)
    dkv_ref[:, 0, :, HD:] = dv_acc[...].astype(bf16).reshape(blocks, rows, HD)


def attention_specs(rows, group_len, blocks, step_heads, at):
    wide = PER_KV * HD
    q_spec = pl.BlockSpec((1, rows, wide), lambda g: (at, 0, g))
    kv_spec = pl.BlockSpec((blocks, 1, rows, 2 * HD), lambda g: (0, 0, 0, g))
    bias_spec = pl.BlockSpec((1, group_len, step_heads * rows), lambda g: (at, 0, 0))
    log_spec = pl.BlockSpec((1, 1, PER_KV // step_heads, step_heads * rows), lambda g: (at, g, 0, 0))
    return q_spec, kv_spec, bias_spec, log_spec


def run_forward(query, kv_all, bias, step_heads, chunk, at, earlier, again=False):
    micro, rows, _ = query.shape
    blocks = kv_all.shape[0]
    group_len = bias.shape[1]
    q_spec, kv_spec, bias_spec, log_spec = attention_specs(rows, group_len, blocks, step_heads, at)
    flops = 4 * rows * H * HD * group_len

    def kernel(*refs):
        attend_forward(step_heads, chunk, *refs[:3], *refs[3 + len(earlier) :])

    return pl.pallas_call(
        kernel,
        grid=(KVH,),
        in_specs=[q_spec, kv_spec, bias_spec] + [pl.BlockSpec(memory_space=pl.ANY)] * len(earlier),
        out_specs=[q_spec, log_spec]
        + again * [pl.BlockSpec((2, 2, 1, rows, 2 * HD), lambda g: (0, 0, at, 0, g))],
        out_shape=[
            jax.ShapeDtypeStruct(query.shape, bf16),
            jax.ShapeDtypeStruct((micro, KVH, PER_KV // step_heads, step_heads * rows), f32),
        ]
        + again * [jax.ShapeDtypeStruct((2, 2, micro, rows, KVH * 2 * HD), bf16)],
        input_output_aliases={3 + i: i for i in range(len(earlier))},
        compiler_params=pltpu.CompilerParams(vmem_limit_bytes=VMEM_LIMIT),
        cost_estimate=LIGHT,
    )(query, kv_all, bias, *earlier)


def run_backward(query, kv_all, bias, mixed, grad, logs, raw, cosine, sine, gain, step_heads, chunk, at, earlier):
    micro, rows, _ = query.shape
    blocks = kv_all.shape[0]
    group_len = bias.shape[1]
    q_spec, kv_spec, bias_spec, log_spec = attention_specs(rows, group_len, blocks, step_heads, at)
    flops = 10 * rows * H * HD * group_len
    gain_spec = pl.BlockSpec((1, HD), lambda g: (0, 0))

    def kernel(*refs):
        attend_backward(step_heads, chunk, *refs[:10], *refs[10 + len(earlier) :])

    return pl.pallas_call(
        kernel,
        grid=(KVH,),
        in_specs=[q_spec, kv_spec, bias_spec, q_spec, q_spec, log_spec, q_spec]
        + [pl.BlockSpec((1, rows, HD), lambda g: (at, 0, 0))] * 2
        + [gain_spec]
        + [pl.BlockSpec(memory_space=pl.ANY)] * len(earlier),
        out_specs=[q_spec, kv_spec, gain_spec],
        out_shape=[
            jax.ShapeDtypeStruct(query.shape, bf16),
            jax.ShapeDtypeStruct(kv_all.shape, bf16),
            jax.ShapeDtypeStruct((1, HD), f32),
        ],
        input_output_aliases={10 + i: i for i in range(len(earlier))},
        scratch_shapes=[pltpu.VMEM((group_len, HD), f32), pltpu.VMEM((group_len, HD), f32)],
        compiler_params=pltpu.CompilerParams(vmem_limit_bytes=VMEM_LIMIT),
        cost_estimate=LIGHT,
    )(query, kv_all, bias, mixed, grad, logs, raw, cosine, sine, gain, *earlier)


def middle_back(r0_ref, r1_ref, mid_ref, cot_ref, gain_ref, w_ref, mix_ref, dmid_ref, low_ref, gain_out):
    @pl.when(pl.program_id(0) == 0)
    def _():
        gain_sum = 0.0
        rows = r0_ref.shape[0]
        for b, ref in enumerate((r0_ref, r1_ref)):
            grad = ref[...].astype(f32)
            middle = mid_ref[b]
            scale = rms_scale(middle)
            lifted = grad * gain_ref[...]
            inner = jnp.mean(lifted * middle, axis=-1, keepdims=True)
            total = cot_ref[b].astype(f32) + scale * lifted - middle * (scale * scale * scale) * inner
            gain_sum += jnp.sum(grad * middle * scale, axis=0, keepdims=True)
            dmid_ref[b * rows : (b + 1) * rows] = total
            low_ref[b * rows : (b + 1) * rows] = total.astype(bf16)
        gain_out[...] = gain_sum

    mix_ref[...] = mm(low_ref[...], w_ref[...], NT).astype(bf16)


def run_middle_back(routed, middle, cot, gain, out_w):
    micro, rows, width = middle.shape
    total = micro * rows
    piece = 512
    whole = lambda *shape: pl.BlockSpec(shape, lambda i: (0,) * len(shape))
    return pl.pallas_call(
        middle_back,
        grid=(out_w.shape[0] // piece,),
        in_specs=[whole(rows, width)] * 2
        + [whole(micro, rows, width)] * 2
        + [whole(1, width), pl.BlockSpec((piece, width), lambda i: (i, 0))],
        out_specs=[
            pl.BlockSpec((total, piece), lambda i: (0, i)),
            whole(total, width),
            whole(total, width),
            whole(1, width),
        ],
        out_shape=[
            jax.ShapeDtypeStruct((total, out_w.shape[0]), bf16),
            jax.ShapeDtypeStruct((total, width), f32),
            jax.ShapeDtypeStruct((total, width), bf16),
            jax.ShapeDtypeStruct((1, width), f32),
        ],
        compiler_params=pltpu.CompilerParams(vmem_limit_bytes=VMEM_LIMIT),
        cost_estimate=LIGHT,
    )(*routed, middle, cot, gain, out_w)


MESH = pl.DeviceIdType.MESH


def gather_kernel(phases, count, late, *refs):
    ins, outs, sems = refs[:count], refs[count : 2 * count], refs[2 * count :]
    dp = lax.axis_index("dp"); member = lax.axis_index("expert")
    blocks = lax.axis_size("expert")
    core = member % 2; z = member // 2
    depth = blocks // 2
    sibling = (dp, member + 1 - 2 * core)
    by_x = (dp + 1 - 2 * (dp % 2), member)
    by_y = ((dp + 2) % 4, member)
    x_at, y_at, far_at = by_x[0], by_y[0], 3 - dp
    above, below = (dp, member + 2), (dp, member - 2)
    barrier = pltpu.get_barrier_semaphore()
    peers = [(sibling, None), (by_x, None), (by_y, None), (above, z < depth - 1), (below, z > 0)]
    for peer, ok in peers:
        if ok is None:
            pl.semaphore_signal(barrier, inc=1, device_id=peer, device_id_type=MESH)
        else:
            @pl.when(ok)
            def _(peer=peer):
                pl.semaphore_signal(barrier, inc=1, device_id=peer, device_id_type=MESH)
    @pl.when((z == 0) | (z == depth - 1))
    def _(): pl.semaphore_wait(barrier, 4)
    @pl.when((z > 0) & (z < depth - 1))
    def _(): pl.semaphore_wait(barrier, 5)

    def guarded(ok, run):
        if ok is None: run()
        else: pl.when(ok)(run)

    class Item:
        pass

    def make(i):
        src, out = ins[i], outs[i]
        flat = i in late
        rows = src.shape[0]
        half = rows // 2
        (own_sem, sz, rz, sxy, rxy, sc, rc) = sems[i * 7 : (i + 1) * 7]
        def at(d, s, lo=0, n=rows):
            first = s * 2 + core if flat else d * blocks + s * 2 + core
            return out.at[pl.ds(pl.multiple_of(first * rows + lo, 16 if half % 16 == 0 else 8), n)]
        def copy(a, b, ss, rs, to):
            return pltpu.make_async_remote_copy(src_ref=a, dst_ref=b, send_sem=ss, recv_sem=rs, device_id=to, device_id_type=MESH)
        def block(d, s):
            return at(d, s)
        it = Item()
        def local():
            return pltpu.make_async_copy(src, at(dp, z), own_sem)
        def up(s, ref): return copy(ref, at(dp, s), sz.at[0, s], rz.at[s], above)
        def down(s, ref): return copy(ref, at(dp, s), sz.at[1, s], rz.at[s], below)
        def to_x(s, ref): return copy(ref, at(dp, s), sxy.at[0, s], rxy.at[0, s], by_x)
        def to_y(s, ref): return copy(ref, at(dp, s), sxy.at[1, s], rxy.at[1, s], by_y)
        def half_y(s):
            return copy(at(x_at, s, 0, half), at(x_at, s, 0, half), sxy.at[2, s], rxy.at[2, s], by_y)
        def half_x(s):
            return copy(at(y_at, s, half, half), at(y_at, s, half, half), sxy.at[3, s], rxy.at[3, s], by_x)
        def to_core(r, d, s, ref): return copy(ref, at(d, s), sc.at[r, s], rc.at[r, s], sibling)
        def spread(s, ref):
            if not flat:
                to_x(s, ref).start(); to_y(s, ref).start()
            to_core(0, dp, s, ref).start()
        def start_up():
            up(z, src).start()
        def start_down():
            down(z, src).start()
        def start():
            local().start()
            if not flat:
                guarded(z < depth - 1, start_up)
                guarded(z > 0, start_down)
            spread(z, src)
        def z_event(s, ok, rising):
            def run():
                up(s, at(dp, s)).wait_recv()
                if rising: guarded(z < depth - 1, lambda: up(s, at(dp, s)).start())
                else: guarded(z > 0, lambda: down(s, at(dp, s)).start())
                spread(s, at(dp, s))
            pl.when(ok)(run)
        def near_event(s, ok):
            def run():
                to_x(s, at(dp, s)).wait_recv()
                half_y(s).start()
                to_core(1, x_at, s, at(x_at, s)).start()
                to_y(s, at(dp, s)).wait_recv()
                half_x(s).start()
                to_core(2, y_at, s, at(y_at, s)).start()
            guarded(ok, run)
        def far_event(s, ok):
            def run():
                half_y(s).wait_recv(); half_x(s).wait_recv()
                to_core(3, far_at, s, at(far_at, s)).start()
            guarded(ok, run)
        owners = (dp,) if flat else (dp, x_at, y_at, far_at)
        def core_wait(s):
            for r, d in enumerate(owners):
                to_core(r, d, s, at(d, s)).wait_recv()
        def finish():
            local().wait()
            for s in range(depth):
                if not flat:
                    for c in (to_x(s, at(dp, s)), to_y(s, at(dp, s)), half_y(s), half_x(s)): c.wait_send()
                for r, d in enumerate(owners): to_core(r, d, s, at(d, s)).wait_send()
                guarded((z >= s) & (z < depth - 1), lambda: up(s, at(dp, s)).wait_send())
                guarded((z <= s) & (z > 0), lambda: down(s, at(dp, s)).wait_send())
        it.start_up, it.start_down = start_up, start_down
        it.start, it.z_event, it.near_event, it.far_event, it.core_wait, it.finish = start, z_event, near_event, far_event, core_wait, finish
        return it
    items = [make(i) for i in range(count)]
    def around(d):
        if d == 0: return [(z, None, True)]
        return [(z - d, z >= d, True), (z + d, z + d < depth, False)]
    for n, phase in enumerate(phases):
        its = [items[i] for i in phase]
        for it in its: it.start()
        lates = [items[i] for i in late]
        for it in lates: it.start()
        def late_sends(d):
            for it in lates:
                if d < depth - 1:
                    pl.when(z == d)(it.start_up)
                    pl.when(z == depth - 1 - d)(it.start_down)
        late_sends(0)
        for d in range(1, depth + 2):
            if d < depth:
                for s, ok, rising in around(d):
                    for it in its: it.z_event(s, ok, rising)
                late_sends(d)
            if d - 1 < depth:
                for s, ok, _ in around(d - 1):
                    for it in its: it.near_event(s, ok)
            if d > 2:
                for s, ok, rising in around(d - 2):
                    for it in lates: it.z_event(s, ok, rising)
            if d - 2 >= 0:
                for s, ok, _ in around(d - 2):
                    for it in its: it.far_event(s, ok)
    for it in items:
        for s in range(depth): it.core_wait(s)
    for it in items: it.finish()

def gather_rows(arrays, phases, cid, late=()):
    shards = lax.axis_size("dp") * lax.axis_size("expert")
    depth = lax.axis_size("expert") // 2
    D = pltpu.SemaphoreType.DMA
    sems = []
    for _ in arrays:
        sems += [D, D((2, depth)), D((depth,)), D((4, depth)), D((4, depth)), D((4, depth)), D((4, depth))]
    return pl.pallas_call(
        functools.partial(gather_kernel, phases, len(arrays), late),
        out_shape=[
            jax.ShapeDtypeStruct(((2 * depth if i in late else shards) * a.shape[0],) + a.shape[1:], a.dtype)
            for i, a in enumerate(arrays)
        ],
        in_specs=[pl.BlockSpec(memory_space=pl.ANY)] * len(arrays),
        out_specs=[pl.BlockSpec(memory_space=pl.ANY)] * len(arrays),
        scratch_shapes=sems,
        compiler_params=pltpu.CompilerParams(collective_id=cid, has_side_effects=True),
        cost_estimate=pl.CostEstimate(flops=0, bytes_accessed=400_000_000, transcendentals=0),
    )(*arrays)


def reduce_kernel(rows, cuts, a_ref, extra_ref, b_ref, g_ref, q_out, k_out, v_out, go_ref, o_ref, sib, got, own, far, near, plane, got_z,
                  s0, r0, s1, r1, s2, r2, s3, r3, g_acc, g_got, g_z, gs, gr, gsz, grz):
    dp = lax.axis_index("dp"); member = lax.axis_index("expert")
    core = member % 2; z = member // 2
    sibling = (dp, member + 1 - 2 * core)
    by_x = (dp + 1 - 2 * (dp % 2), member)
    by_y = ((dp + 2) % 4, member)
    x_at, y_at = by_x[0], by_y[0]
    far_at = 3 - dp
    half = rows // 2
    depth = lax.axis_size("expert") // 2
    barrier = pltpu.get_barrier_semaphore()
    peers = [sibling, by_x, by_y] + [(dp, ((z + d) % depth) * 2 + core) for d in range(1, depth)]
    for peer in peers:
        pl.semaphore_signal(barrier, inc=1, device_id=peer, device_id_type=MESH)
    pl.semaphore_wait(barrier, len(peers))

    def pick(table):
        at = table[depth-1]
        for i in range(depth - 1):
            at = jnp.where(z == i, table[i], at)
        return at
    orders = [[3, 3, 0, 0], [2, 0, 3, 1], [1, 2, 1, 2], [0, 1, 2, 3]]
    targets = [pick(t) for t in orders]
    cols = b_ref.shape[1] // cuts

    def copy(src, dst, ssem, rsem, to):
        return pltpu.make_async_remote_copy(src_ref=src, dst_ref=dst, send_sem=ssem, recv_sem=rsem, device_id=to, device_id_type=MESH)

    blocks = 2 * depth
    piece = (rows - HD) // 2

    def product(half_of, k, put):
        spot = targets[k] * 2 + half_of

        def step(i, _):
            shard = (i // cuts) * blocks + spot
            at = (i // cuts) * rows
            col = pl.ds(pl.multiple_of((i % cuts) * cols, cols), cols)
            part = mm(a_ref[:, pl.ds(pl.multiple_of(shard * HD, HD), HD)], b_ref[:, col], TN)
            put(pl.ds(pl.multiple_of(at, 16), HD), col, part)
            if piece:
                base = (shard // PER_KV) * (2 * HD) + (shard % PER_KV) * piece
                small = jnp.concatenate(
                    [
                        extra_ref[pl.ds(pl.multiple_of(base, 16), piece), :],
                        extra_ref[pl.ds(pl.multiple_of(base + HD, 16), piece), :],
                    ],
                    axis=0,
                )
                put(pl.ds(pl.multiple_of(at + HD, 16), 2 * piece), col, mm(small, b_ref[:, col]))
            return 0

        lax.fori_loop(0, 4 * cuts, step, 0)

    def gain_hop(i, src, to):
        return copy(src, g_got.at[i, pl.ds(0, src.shape[0])], gs.at[i], gr.at[i], to)
    hops = {}
    def gain_step(i):
        rows4 = lambda at: pl.ds(pl.multiple_of(at * 8, 8), 8)
        if i == 0:
            hops[0] = gain_hop(0, g_ref.at[pl.ds(pl.multiple_of((1 - core) * 32, 32), 32)], sibling)
        elif i == 1:
            hops[0].wait_recv()
            g_acc[...] = g_ref[pl.ds(pl.multiple_of(core * 32, 32), 32)] + g_got[0]
            hops[1] = gain_hop(1, g_acc.at[pl.ds(pl.multiple_of((1 - dp // 2) * 16, 16), 16)], by_y)
        elif i == 2:
            hops[1].wait_recv()
            mine = pl.ds(pl.multiple_of((dp // 2) * 16, 16), 16)
            g_acc[mine] += g_got[1, :16]
            hops[2] = gain_hop(2, g_acc.at[rows4(x_at)], by_x)
        elif i == 3:
            hops[2].wait_recv()
            g_acc[rows4(dp)] += g_got[2, :8]
            for d in range(1, depth):
                to = (z + d) % depth
                hops[2 + d] = copy(g_acc.at[pl.ds(dp * 8 + to, 1)], g_z.at[z], gsz.at[d - 1], grz.at[z], (dp, to * 2 + core))
        if i < 3:
            hops[i].start()
        else:
            for d in range(1, depth):
                hops[2 + d].start()
    def gain_end():
        total = g_acc[pl.ds(dp * 8 + z, 1)]
        for d in range(1, depth):
            src = (z + d) % depth
            copy(g_acc.at[pl.ds(dp * 8, 1)], g_z.at[src], gsz.at[0], grz.at[src], sibling).wait_recv()
            total += g_z[src]
        go_ref[...] = total
        for i in hops:
            hops[i].wait_send()
    sib_copies, far_copies, near_copies, z_copies = {}, {}, {}, {}
    def sib_step(k):
        slot = k % 2
        if k >= 2:
            sib_copies[k - 2].wait_send()
        def put(r, c, part):
            sib[slot, r, c] = part.astype(bf16)
        product(1 - core, k, put)
        sib_copies[k] = copy(sib.at[slot], got.at[k], s0.at[slot], r0.at[k], sibling)
        sib_copies[k].start()
    def blk(at):
        return pl.ds(pl.multiple_of(at * rows, 16), rows)
    def own_step(k):
        sib_copies[k].wait_recv()
        def put(r, c, part):
            own[k, r, c] = (part + got[k, r, c].astype(f32)).astype(bf16)
        product(core, k, put)
        base = pl.multiple_of(far_at * rows, 16)
        far_copies[k] = (
            copy(own.at[k, pl.ds(base, half)], far.at[k, 0], s1.at[k, 0], r1.at[k, 0], by_x),
            copy(own.at[k, pl.ds(pl.multiple_of(base + half, 16), half)], far.at[k, 1], s1.at[k, 1], r1.at[k, 1], by_y),
        )
        for c in far_copies[k]: c.start()
    def near_step(k):
        a, b = far_copies[k]
        a.wait_recv()
        rng = pl.ds(pl.multiple_of(y_at * rows, 16), half)
        own[k, rng] = (own[k, rng].astype(f32) + far[k, 0].astype(f32)).astype(bf16)
        to_y = copy(own.at[k, blk(y_at)], near.at[k, 1], s2.at[k, 1], r2.at[k, 1], by_y)
        to_y.start()
        b.wait_recv()
        rng = pl.ds(pl.multiple_of(x_at * rows + half, 16), half)
        own[k, rng] = (own[k, rng].astype(f32) + far[k, 1].astype(f32)).astype(bf16)
        to_x = copy(own.at[k, blk(x_at)], near.at[k, 0], s2.at[k, 0], r2.at[k, 0], by_x)
        to_x.start()
        near_copies[k] = (to_x, to_y)
    def plane_step(k):
        for c in near_copies[k]: c.wait_recv()
        total = own[k, blk(dp)].astype(f32) + near[k, 0].astype(f32) + near[k, 1].astype(f32)
        if k < depth - 1:
            plane[k] = total.astype(bf16)
            to = (dp, targets[k] * 2 + core)
            z_copies[k] = copy(plane.at[k], got_z.at[z], s3.at[k], r3.at[z], to)
            z_copies[k].start()
        else:
            o_ref[...] = total
    gain_step(0)
    sib_step(0); sib_step(1)
    own_step(0)
    gain_step(1)
    sib_step(2)
    own_step(1)
    gain_step(2)
    near_step(0)
    sib_step(3)
    own_step(2)
    gain_step(3)
    near_step(1)
    plane_step(0)
    own_step(3)
    near_step(2)
    plane_step(1)
    near_step(3)
    plane_step(2)
    plane_step(3)
    for d in range(1, depth):
        src = (z + d) % depth
        copy(plane.at[0], got_z.at[src], s3.at[0], r3.at[src], sibling).wait_recv()
        o_ref[...] += got_z[src].astype(f32)
    q_out[...] = o_ref[:HD].T
    k_out[...] = o_ref[HD : HD + piece].T
    v_out[...] = o_ref[HD + piece :].T
    gain_end()
    for k in range(depth):
        if k >= 2: sib_copies[k].wait_send()
        for c in far_copies[k]: c.wait_send()
        for c in near_copies[k]: c.wait_send()
        if k < depth - 1: z_copies[k].wait_send()

def reduce_rows(a, extra, b, cid, gains=None):
    tokens, width = b.shape
    depth = 4
    rows = HD + extra.shape[0] // 32
    D = pltpu.SemaphoreType.DMA
    lanes = 256
    padded = jnp.zeros((32, lanes), f32)
    if gains is not None:
        padded = jnp.pad(gains, ((0, 0), (0, lanes - gains.shape[1])))
    padded = padded.reshape(4, depth, 2, lanes).transpose(2, 0, 1, 3)
    padded = jnp.pad(padded, ((0, 0), (0, 0), (0, 8 - depth), (0, 0))).reshape(64, lanes)
    return pl.pallas_call(
        functools.partial(reduce_kernel, rows, 4),
        out_shape=[
            jax.ShapeDtypeStruct((width, HD), f32),
            jax.ShapeDtypeStruct((width, (rows - HD) // 2), f32),
            jax.ShapeDtypeStruct((width, (rows - HD) // 2), f32),
            jax.ShapeDtypeStruct((1, lanes), f32),
        ],
        in_specs=[pl.BlockSpec(memory_space=pltpu.VMEM)] * 4,
        out_specs=[pl.BlockSpec(memory_space=pltpu.VMEM)] * 4,
        scratch_shapes=[
            pltpu.VMEM((rows, width), f32),
            pltpu.VMEM((2, 4 * rows, width), bf16),
            pltpu.VMEM((depth, 4 * rows, width), bf16),
            pltpu.VMEM((depth, 4 * rows, width), bf16),
            pltpu.VMEM((depth, 2, rows // 2, width), bf16),
            pltpu.VMEM((depth, 2, rows, width), bf16),
            pltpu.VMEM((depth - 1, rows, width), bf16),
            pltpu.VMEM((depth, rows, width), bf16),
            D((2,)), D((depth,)), D((depth, 2)), D((depth, 2)), D((depth, 2)), D((depth, 2)), D((depth - 1,)), D((depth,)),
            pltpu.VMEM((32, lanes), f32), pltpu.VMEM((3, 32, lanes), f32), pltpu.VMEM((depth, 1, lanes), f32),
            D((3,)), D((3,)), D((depth - 1,)), D((depth,)),
        ],
        compiler_params=pltpu.CompilerParams(vmem_limit_bytes=60*1024*1024, collective_id=cid, has_side_effects=True),
        cost_estimate=pl.CostEstimate(flops=2*tokens*32*rows*width, bytes_accessed=10_000_000, transcendentals=0),
    )(a, extra, b, padded)


ROUTE_LANES = 128


def picks_of(routing, first, local_experts, capacity):
    rows = routing.shape[0]
    lanes = lax.broadcasted_iota(jnp.int32, (rows, ROUTE_LANES), 1)
    places = lax.broadcasted_iota(jnp.int32, (rows, local_experts * capacity), 1)
    hit, weighted = None, 0.0
    for e in range(local_experts):

        def column(base):
            return jnp.sum(jnp.where(lanes == base + first + e, routing, 0.0), axis=1, keepdims=True)

        slot = column(0).astype(jnp.int32)
        here = places == jnp.where(slot >= 0, slot + e * capacity, -1)
        hit = here if hit is None else hit | here
        weighted = weighted + jnp.where(here, column(32) + column(64), 0.0)
    return jnp.where(hit, 1.0, 0.0).astype(bf16), weighted.astype(bf16)


def pick_kernel(capacity, local_experts, n_alias, tok_ref, cot_a, cot_b, *refs):
    x_ref, dy_ref = refs[n_alias:]
    width = cot_a.shape[3]
    cot = jnp.concatenate([cot_a[0, 0], cot_b[0, 0]], axis=0)
    first = lax.axis_index("expert") * local_experts
    routing = tok_ref[0, :, width:]
    hit, _ = picks_of(routing.astype(f32), first, local_experts, capacity)
    x = mm(hit, tok_ref[0, :, :width], TN).astype(bf16)
    rows = mm(hit, routing, TN)
    lanes = lax.broadcasted_iota(jnp.int32, rows.shape, 1)
    owner = lax.broadcasted_iota(jnp.int32, rows.shape, 0) // capacity
    at = lanes - first - owner
    weight = jnp.sum(jnp.where((at == 32) | (at == 64), rows, 0.0), axis=1, keepdims=True)
    dy = (mm(hit, cot, TN) * weight).astype(bf16)
    for e in range(local_experts):
        x_ref[e, 0, 0] = x[e * capacity : (e + 1) * capacity]
        dy_ref[e, 0, 0] = dy[e * capacity : (e + 1) * capacity]


def expert_kernel(n_alias, *refs):
    x_ref, dy_ref = refs[:2]
    parts = (refs[2:7], refs[7:12], refs[12:17])
    z_ref, dg_ref, du_ref, y_ref, dx_ref, wg, wu, wd, sems = refs[17 + n_alias :]
    local_experts, width, _ = wg.shape
    at = lax.axis_index("dp")
    size = width // 4
    places = (at, at + 1 - 2 * (at % 2), (at + 2) % 4, 3 - at, 3 - at)

    def copies(e):
        out = []
        for m, full in enumerate((wg, wu, wd)):
            for p in range(4):
                part = parts[m][p] if p < 3 else parts[m][3 + e]
                src = part.at[e] if p < 3 else part.at[0]
                where = pl.ds(pl.multiple_of(places[p] * size, size), size)
                dst = full.at[e, where, :] if m < 2 else full.at[e, :, where]
                out.append(pltpu.make_async_copy(src, dst, sems.at[e, m, p]))
        return out

    expert, chunk = pl.program_id(0), pl.program_id(1)

    @pl.when((expert == 0) & (chunk == 0))
    def _():
        for e in range(local_experts):
            for c in copies(e):
                c.start()

    for e in range(local_experts):

        @pl.when((expert == e) & (chunk == 0))
        def _(e=e):
            for c in copies(e):
                c.wait()

    x, dy = x_ref[0, 0], dy_ref[0, 0]
    gate = mm(x, wg[expert])
    up = mm(x, wu[expert])
    d_hidden = mm(dy, wd[expert], NT)
    sig = 1.0 / (1.0 + jnp.exp(-gate))
    silu = gate * sig
    z = (silu * up).astype(bf16)
    d_gate = (d_hidden * up * sig * (1.0 + gate * (1.0 - sig))).astype(bf16)
    d_up = (d_hidden * silu).astype(bf16)
    z_ref[0, 0] = z
    dg_ref[0, 0] = d_gate
    du_ref[0, 0] = d_up
    dx_ref[0] = (mm(d_gate, wg[expert], NT) + mm(d_up, wu[expert], NT)).astype(bf16)
    y_ref[0] = mm(z, wd[expert]).astype(bf16)


def sum_kernel(capacity, routing_ref, y_ref, dx_ref, mix_ref, da_ref):
    local_experts, _, _, width = y_ref.shape
    first = lax.axis_index("expert") * local_experts
    hit, weighted = picks_of(routing_ref[0].astype(f32), first, local_experts, capacity)
    da_ref[...] = mm(hit, dx_ref[...].reshape(local_experts * capacity, width)).astype(bf16)
    mix_ref[...] = mm(weighted, y_ref[...].reshape(local_experts * capacity, width)).astype(bf16)


def run_experts(tokens, cot, parts, capacity, batch_at, micro, earlier):
    blocks, rows, _ = tokens.shape
    width = cot[0][0].shape[3]
    local_experts, _, hidden = parts[0][0].shape
    flat = [p for group in parts for p in group]
    any_spec = pl.BlockSpec(memory_space=pl.ANY)
    params = pltpu.CompilerParams(vmem_limit_bytes=VMEM_LIMIT)
    slots = blocks * capacity
    picked_spec = pl.BlockSpec((local_experts, 1, 1, capacity, width), lambda b: (0, batch_at, b, 0, 0))
    picked = jax.ShapeDtypeStruct((local_experts, micro, blocks, capacity, width), bf16)
    x, dy = pl.pallas_call(
        functools.partial(pick_kernel, capacity, local_experts, len(earlier[:2])),
        grid=(blocks,),
        in_specs=[
            pl.BlockSpec((1, rows, tokens.shape[2]), lambda b: (b, 0, 0)),
        ]
        + [pl.BlockSpec((1, 1, rows // 2, width), lambda b, i=i: (b, i, 0, 0)) for _, i in cot]
        + [any_spec] * len(earlier[:2]),
        out_specs=[picked_spec] * 2,
        out_shape=[picked] * 2,
        input_output_aliases={3 + i: i for i in range(len(earlier[:2]))},
        compiler_params=params,
        cost_estimate=LIGHT,
    )(tokens, cot[0][0], cot[1][0], *[a.reshape(picked.shape) for a in earlier[:2]])
    x, dy = (a.reshape(local_experts, micro, slots, width) for a in (x, dy))
    chunk = slots // 2
    row_spec = pl.BlockSpec((1, 1, chunk, width), lambda e, i: (e, batch_at, i, 0))
    hid_spec = pl.BlockSpec((1, 1, chunk, hidden), lambda e, i: (e, batch_at, i, 0))
    out_spec = pl.BlockSpec((1, chunk, width), lambda e, i: (e, i, 0))
    hid = jax.ShapeDtypeStruct((local_experts, micro, slots, hidden), bf16)
    out = jax.ShapeDtypeStruct((local_experts, slots, width), bf16)
    z, dg, du, y, dx = pl.pallas_call(
        functools.partial(expert_kernel, len(earlier[2:])),
        grid=(local_experts, 2),
        in_specs=[row_spec, row_spec] + [any_spec] * (len(flat) + len(earlier[2:])),
        out_specs=[hid_spec] * 3 + [out_spec] * 2,
        out_shape=[hid] * 3 + [out] * 2,
        input_output_aliases={2 + len(flat) + i: i for i in range(len(earlier[2:]))},
        scratch_shapes=[
            pltpu.VMEM((local_experts, width, hidden), bf16),
            pltpu.VMEM((local_experts, width, hidden), bf16),
            pltpu.VMEM((local_experts, hidden, width), bf16),
            pltpu.SemaphoreType.DMA((local_experts, 3, 4)),
        ],
        compiler_params=params,
        cost_estimate=LIGHT,
    )(x, dy, *flat, *earlier[2:])
    y, dx = (a.reshape(local_experts, blocks, capacity, width) for a in (y, dx))
    part_spec = pl.BlockSpec((local_experts, 1, capacity, width), lambda b: (0, b, 0, 0))
    sums = jax.ShapeDtypeStruct((blocks * rows, width), bf16)
    sums_spec = pl.BlockSpec((rows, width), lambda b: (b, 0))
    mix, da = pl.pallas_call(
        functools.partial(sum_kernel, capacity),
        grid=(blocks,),
        in_specs=[
            pl.BlockSpec((1, rows, ROUTE_LANES), lambda b: (b, 0, width // ROUTE_LANES)),
            part_spec,
            part_spec,
        ],
        out_specs=[sums_spec] * 2,
        out_shape=[sums] * 2,
        compiler_params=params,
        cost_estimate=LIGHT,
    )(tokens, y, dx)
    return [x, dy, z, dg, du], mix, da


def slots_of(route_ids, gate_vals, ranking, capacity, experts):
    rows = route_ids.shape[0]
    pair_experts = route_ids.reshape(-1)
    earlier = (pair_experts[None, :] == pair_experts[:, None]) & (
        ranking[None, :] < ranking[:, None]
    )
    slot = jnp.sum(earlier.astype(jnp.int32), axis=1).reshape(rows, -1)
    kept = slot < capacity
    chosen = route_ids[:, :, None] == jnp.arange(experts, dtype=jnp.int32)[None, None, :]
    chosen = chosen & kept[:, :, None]
    slot_map = jnp.sum(jnp.where(chosen, slot[:, :, None] + 1, 0), axis=1).astype(f32) - 1.0
    weight_map = jnp.sum(jnp.where(chosen, gate_vals[:, :, None], 0.0), axis=1)
    return slot_map, weight_map


def swap(values, bit):
    return lax.ppermute(values, "dp", [(i, i ^ bit) for i in range(lax.axis_size("dp"))])


def dp_part(total, axis, bits, expert, count=1):
    size = total.shape[axis] // 4
    start, sizes = [expert, 0, 0], list(total.shape)
    start[axis] = (lax.axis_index("dp") ^ bits) * size
    sizes[0], sizes[axis] = count, size
    return lax.dynamic_slice(total, start, sizes)


def scatter_far(total, axis):
    return swap(dp_part(total, axis, 3, 0), 1), swap(dp_part(total, axis, 3, 1), 2), total


def scatter_add(pieces, axis):
    for_y, for_x, total = pieces
    near_x = dp_part(total, axis, 1, 0, 2).astype(f32) + jnp.pad(for_x.astype(f32), ((1, 0), (0, 0), (0, 0)))
    near_y = dp_part(total, axis, 2, 0, 2).astype(f32) + jnp.pad(for_y.astype(f32), ((0, 1), (0, 0), (0, 0)))
    return near_x.astype(bf16), near_y.astype(bf16), total


def scatter_near(pieces, axis):
    near_x, near_y, total = scatter_add(pieces, axis)
    return swap(near_x, 1), swap(near_y, 2), total


def scatter_sum(pieces, axis):
    by_x, by_y, total = pieces
    return dp_part(total, axis, 0, 0, total.shape[0]).astype(f32) + by_x.astype(f32) + by_y.astype(f32)


def body_plain(
    inputs,
    cotangent,
    membership,
    routes,
    gate_weights,
    pair_order,
    w_query,
    w_key,
    w_value,
    w_output,
    norm_gains,
    w_gate,
    w_up,
    w_down,
):
    micro = inputs.shape[0]
    rows = inputs.shape[2]
    width = inputs.shape[3]
    group_len = membership.shape[2]
    member = lax.axis_index("expert")
    blocks = lax.axis_size("expert")
    shards = blocks * lax.axis_size("dp")
    shard_at = lax.axis_index("dp") * blocks + member
    local_experts = w_gate.shape[0]
    experts = local_experts * blocks
    capacity = rows * TOPK // experts
    step_heads = max(1, 384 // rows)
    total = micro * rows
    q_part, k_part, v_part = w_query.shape[1], w_key.shape[1], w_value.shape[1]

    gain_len = norm_gains.shape[0]
    gain_shard = jnp.zeros((2048,), bf16).at[:gain_len].set(norm_gains).reshape(16, 128)
    gain_full = lax.all_gather(gain_shard, BOTH, axis=0, tiled=True)
    gains = gain_full.reshape(shards, 2048)[:, :gain_len].reshape(-1).astype(f32)
    gain_in = gains[:width]
    gain_mid = gains[width : 2 * width]
    gain_q = gains[2 * width : 2 * width + HD]
    gain_k = gains[2 * width + HD :]

    qkv_w = lax.all_gather(
        jnp.concatenate([w_query.T, w_key.T, w_value.T], axis=0), BOTH, axis=0, tiled=True
    )
    out_w = lax.all_gather(w_output, BOTH, axis=0, tiled=True)
    wg = lax.all_gather(w_gate, "dp", axis=1, tiled=True)
    wu = lax.all_gather(w_up, "dp", axis=1, tiled=True)
    wd = lax.all_gather(w_down, "dp", axis=2, tiled=True)

    slot_map, weight_map = jax.vmap(
        lambda r, g, o: slots_of(r, g, o, capacity, experts)
    )(routes[:, 0], gate_weights[:, 0], pair_order[:, 0, 0])
    routing = jnp.concatenate([slot_map, weight_map], axis=-1)
    routing = lax.all_gather(routing, "expert", axis=0, tiled=False)
    mine = member * local_experts
    slot_mine = lax.dynamic_slice_in_dim(routing, mine, local_experts, axis=3)
    weight_mine = lax.dynamic_slice_in_dim(routing, experts + mine, local_experts, axis=3)
    slot_mine = jnp.transpose(slot_mine, (1, 3, 0, 2))
    weight_mine = jnp.transpose(weight_mine, (1, 3, 0, 2))
    slot_ids = jnp.arange(capacity, dtype=f32)
    hit = slot_mine[:, :, :, None, :] == slot_ids[None, None, None, :, None]
    pick = hit.astype(bf16)
    weighted = jnp.where(hit, weight_mine[:, :, :, None, :], 0.0)
    slot_weight = jnp.sum(weighted, axis=-1)
    weighted = weighted.astype(bf16)

    key_index = jnp.arange(group_len, dtype=jnp.int32)
    start_row = member * rows
    segment = membership[:, 0]
    row_index = start_row + jnp.arange(rows, dtype=jnp.int32)
    seg_rows = lax.dynamic_slice_in_dim(segment, start_row, rows, axis=1)
    before = jnp.sum((segment[:, None, :] < seg_rows[:, :, None]).astype(jnp.int32), axis=2)
    position = jnp.where(seg_rows == 0, row_index[None], PROMPT + row_index[None] - before)
    allowed = (key_index[None, :, None] <= row_index[None, None, :]) & (
        (segment[:, :, None] == 0) | (segment[:, :, None] == seg_rows[:, None, :])
    )
    bias = jnp.tile(jnp.where(allowed, 0.0, MASKED).astype(f32), (1, 1, step_heads))
    frequency = ROPE_BASE ** (-(jnp.arange(HD // 2, dtype=f32) * 2.0 / HD))
    angles = position.astype(f32).reshape(total)[:, None] * frequency[None, :]
    cosine = jnp.cos(angles)[:, None, :]
    sine_part = jnp.sin(angles)[:, None, :]

    hidden = inputs[:, 0].astype(f32).reshape(total, width)
    scale_in = rms_scale(hidden)
    normed = (hidden * scale_in * gain_in).astype(bf16)
    proj = mm(normed, qkv_w, NT).reshape(total, shards, q_part + k_part + v_part)
    queries = proj[:, :, :q_part].reshape(total, H, HD)
    key_pre = proj[:, :, q_part : q_part + k_part].reshape(total, KVH, HD)
    value = proj[:, :, q_part + k_part :].reshape(total, KVH, HD).astype(bf16)
    scale_q = rms_scale(queries)
    scale_k = rms_scale(key_pre)
    q_low = rotate(queries * scale_q * (gain_q * (SCALE * LOG2E)), cosine, sine_part).astype(bf16)
    q_low = q_low.reshape(micro, rows, H * HD)
    k_low = rotate(key_pre * scale_k * gain_k, cosine, sine_part).astype(bf16)
    kv_own = jnp.concatenate([k_low, value], axis=-1).reshape(micro, rows, KVH * 2 * HD)
    kv_all = lax.all_gather(kv_own, "expert", axis=0, tiled=False)
    chunk = 256
    mixed = []
    for at in range(micro):
        mixed = run_forward(q_low, kv_all[:, at : at + 1], bias, step_heads, chunk, at, mixed)
    mixed, logs = mixed

    branch = mm(mixed.reshape(total, H * HD), out_w)
    middle = hidden + branch
    scale_mid = rms_scale(middle)
    routed = (middle * scale_mid * gain_mid).astype(bf16).reshape(micro, rows, width)
    middle = middle.reshape(micro, rows, width)
    scale_mid = scale_mid.reshape(micro, rows, 1)

    outputs, d_branches, d_middles = [], [], []
    acc_gate = acc_up = acc_down = 0.0
    grad_mid = 0.0
    slots = blocks * capacity
    for at in range(micro):
        d_out = lax.all_gather(cotangent[at, 0], "expert", axis=0, tiled=False)
        tokens = lax.all_gather(routed[at], "expert", axis=0, tiled=False)
        picked = jnp.einsum("ebst,btd->ebsd", pick[at], tokens, preferred_element_type=f32)
        picked = picked.astype(bf16).reshape(local_experts, slots, width)
        d_result = jnp.einsum("ebst,btd->ebsd", pick[at], d_out, preferred_element_type=f32)
        d_result = (d_result * slot_weight[at][..., None]).astype(bf16)
        d_result = d_result.reshape(local_experts, slots, width)
        gate_pre = jnp.einsum("erd,edf->erf", picked, wg, preferred_element_type=f32)
        up_pre = jnp.einsum("erd,edf->erf", picked, wu, preferred_element_type=f32)
        d_hidden = jnp.einsum("erd,efd->erf", d_result, wd, preferred_element_type=f32)
        sigmoid_g = jax.nn.sigmoid(gate_pre)
        silu_g = gate_pre * sigmoid_g
        hidden_low = (silu_g * up_pre).astype(bf16)
        d_gate = (d_hidden * up_pre * sigmoid_g * (1.0 + gate_pre * (1.0 - sigmoid_g))).astype(bf16)
        d_up = (d_hidden * silu_g).astype(bf16)
        d_rows = jnp.einsum("erf,edf->erd", d_gate, wg, preferred_element_type=f32)
        d_rows = d_rows + jnp.einsum("erf,edf->erd", d_up, wu, preferred_element_type=f32)
        d_rows = d_rows.astype(bf16).reshape(local_experts, blocks, capacity, width)
        d_part = jnp.einsum("ebst,ebsd->btd", pick[at], d_rows, preferred_element_type=f32)
        d_part = d_part.astype(bf16).reshape(group_len, width)
        d_routed = lax.psum_scatter(d_part, "expert", scatter_dimension=0, tiled=True).astype(f32)
        result = jnp.einsum("erf,efd->erd", hidden_low, wd, preferred_element_type=f32)
        result = result.astype(bf16).reshape(local_experts, blocks, capacity, width)
        part = jnp.einsum("ebst,ebsd->btd", weighted[at], result, preferred_element_type=f32)
        part = part.astype(bf16).reshape(group_len, width)
        expert_mix = lax.psum_scatter(part, "expert", scatter_dimension=0, tiled=True).astype(f32)
        outputs.append((middle[at] + expert_mix).astype(bf16))

        acc_down += jnp.einsum("erf,erd->efd", hidden_low, d_result, preferred_element_type=f32)
        acc_gate += jnp.einsum("erd,erf->edf", picked, d_gate, preferred_element_type=f32)
        acc_up += jnp.einsum("erd,erf->edf", picked, d_up, preferred_element_type=f32)

        d_mid_norm, mid_gain_grad = norm_back(d_routed, middle[at], scale_mid[at], gain_mid)
        grad_mid = grad_mid + mid_gain_grad
        d_middle = cotangent[at, 0].astype(f32) + d_mid_norm
        d_middles.append(d_middle)
        d_branches.append(d_middle.astype(bf16))

    grad_gate = lax.psum_scatter(acc_gate.astype(bf16), "dp", scatter_dimension=1, tiled=True)
    grad_up = lax.psum_scatter(acc_up.astype(bf16), "dp", scatter_dimension=1, tiled=True)
    grad_down = lax.psum_scatter(acc_down.astype(bf16), "dp", scatter_dimension=2, tiled=True)

    d_branch = jnp.concatenate(d_branches, axis=0)
    d_middle = jnp.concatenate(d_middles, axis=0)
    grad_output = mm(mixed.reshape(total, H * HD), d_branch, TN).astype(bf16)
    grad_output = lax.psum_scatter(grad_output, BOTH, scatter_dimension=0, tiled=True)
    d_mixed = mm(d_branch, out_w, NT).astype(bf16).reshape(micro, rows, H * HD)
    cos_rows = jnp.concatenate([cosine, cosine], axis=-1).reshape(micro, rows, HD)
    sine_rows = jnp.concatenate([-sine_part, sine_part], axis=-1).reshape(micro, rows, HD)
    q_raw = queries.reshape(micro, rows, H * HD)
    d_query, dkv_list, grad_qn = [], [], 0.0
    for at in range(micro):
        d_query, dkv_one, part = run_backward(
            q_low, kv_all[:, at : at + 1], bias, mixed, d_mixed, logs, q_raw, cos_rows, sine_rows,
            gain_q[None, :], step_heads, chunk, at, [d_query] if at else []
        )
        dkv_list.append(dkv_one)
        grad_qn += part[0]
    dkv_all = jnp.concatenate(dkv_list, axis=1)
    dkv = lax.psum_scatter(dkv_all, "expert", scatter_dimension=0, tiled=False)
    dkv = dkv.reshape(total, KVH, 2 * HD)
    d_key = rotate(dkv[:, :, :HD].astype(f32), cosine, -sine_part)
    d_key, grad_kn = norm_back(d_key, key_pre, scale_k, gain_k)
    d_proj = jnp.concatenate(
        [
            d_query.reshape(total, shards, q_part),
            d_key.astype(bf16).reshape(total, shards, k_part),
            dkv[:, :, HD:].reshape(total, shards, v_part),
        ],
        axis=-1,
    ).reshape(total, -1)
    grad_qkv = mm(d_proj, normed, TN).astype(bf16)
    grad_qkv = lax.psum_scatter(grad_qkv, BOTH, scatter_dimension=0, tiled=True).astype(f32)
    d_normed = mm(d_proj, qkv_w)
    d_in_norm, grad_in = norm_back(d_normed, hidden, scale_in, gain_in)
    input_grad = d_middle + d_in_norm

    gain_grads = jnp.concatenate([grad_in, grad_mid, grad_qn, grad_kn]).reshape(shards, gain_len)
    gain_grads = jnp.pad(gain_grads, ((0, 0), (0, 256 - gain_len % 256)))
    gain_all = lax.all_gather(gain_grads, BOTH, axis=0, tiled=False)
    grad_gains = jnp.sum(lax.dynamic_index_in_dim(gain_all, shard_at, axis=1, keepdims=False), axis=0)
    return (
        jnp.stack(outputs)[:, None],
        input_grad.reshape(micro, 1, rows, width),
        grad_qkv[:q_part].T,
        grad_qkv[q_part : q_part + k_part].T,
        grad_qkv[q_part + k_part :].T,
        grad_output.astype(f32),
        grad_gains[:gain_len],
        grad_gate.astype(f32),
        grad_up.astype(f32),
        grad_down.astype(f32),
    )


def body_fast(
    inputs,
    cotangent,
    membership,
    routes,
    gate_weights,
    pair_order,
    w_query,
    w_key,
    w_value,
    w_output,
    norm_gains,
    w_gate,
    w_up,
    w_down,
):
    micro = inputs.shape[0]
    rows = inputs.shape[2]
    width = inputs.shape[3]
    group_len = membership.shape[2]
    member = lax.axis_index("expert")
    blocks = lax.axis_size("expert")
    shards = blocks * lax.axis_size("dp")
    local_experts = w_gate.shape[0]
    experts = local_experts * blocks
    capacity = rows * TOPK // experts
    step_heads = max(1, 384 // rows)
    total = micro * rows
    q_part, k_part, v_part = w_query.shape[1], w_key.shape[1], w_value.shape[1]
    tie = lax.optimization_barrier

    slot_map, weight_map = jax.vmap(
        lambda r, g, o: slots_of(r, g, o, capacity, experts)
    )(routes[:, 0], gate_weights[:, 0], pair_order[:, 0, 0])
    weight_high = tie(weight_map.astype(bf16))
    weight_low = (weight_map - weight_high.astype(f32)).astype(bf16)

    def padded(values, lanes):
        return jnp.pad(values, ((0, 0), (0, 0), (0, lanes - experts)))

    routing = jnp.concatenate(
        [
            padded(slot_map.astype(bf16), 32),
            padded(weight_high, 32),
            padded(weight_low, ROUTE_LANES - 64),
        ],
        axis=-1,
    )

    gain_len = norm_gains.shape[0]
    gain_shard = jnp.pad(norm_gains[None], ((0, 15), (0, 256 - gain_len)))
    kv_w = jnp.concatenate([w_key.T, w_value.T], axis=0)
    q_w, kv_w, out_w, gain_full, cot_all = gather_rows(
        [w_query.T, kv_w, w_output, gain_shard, cotangent.reshape(total, width)], [(3, 0, 1, 2)], 1, (4,)
    )
    cot_all = cot_all.reshape(blocks, 2 * micro, rows // 2, width)
    q_w, w_gate = tie((q_w, w_gate))
    gains = gain_full.reshape(shards, 16, 256)[:, 0, :gain_len].reshape(-1).astype(f32)
    gain_in = gains[:width]
    gain_mid = gains[width : 2 * width]
    gain_q = gains[2 * width : 2 * width + HD]
    gain_k = gains[2 * width + HD :]

    key_index = jnp.arange(group_len, dtype=jnp.int32)
    start_row = member * rows
    segment = membership[:, 0]
    row_index = start_row + jnp.arange(rows, dtype=jnp.int32)
    seg_rows = lax.dynamic_slice_in_dim(segment, start_row, rows, axis=1)
    before = jnp.sum((segment[:, None, :] < seg_rows[:, :, None]).astype(jnp.int32), axis=2)
    position = jnp.where(seg_rows == 0, row_index[None], PROMPT + row_index[None] - before)
    allowed = (key_index[None, :, None] <= row_index[None, None, :]) & (
        (segment[:, :, None] == 0) | (segment[:, :, None] == seg_rows[:, None, :])
    )
    bias = jnp.tile(jnp.where(allowed, 0.0, MASKED).astype(f32), (1, 1, step_heads))
    frequency = ROPE_BASE ** (-(jnp.arange(HD // 2, dtype=f32) * 2.0 / HD))
    angles = position.astype(f32).reshape(total)[:, None] * frequency[None, :]
    cosine, sine = jnp.cos(angles), jnp.sin(angles)
    cosine = jnp.concatenate([cosine, cosine], axis=-1)
    sine = jnp.concatenate([-sine, sine], axis=-1)
    gain_q, gain_k = gain_q[None, :], gain_k[None, :]

    hidden = inputs[:, 0].astype(f32).reshape(total, width)
    scale_in = rms_scale(hidden)
    normed = (hidden * scale_in * gain_in).astype(bf16)
    q_low, q_raw, k_raw, kv_w, kv_0, kv_1 = run_project(
        normed, q_w, kv_w, cosine, sine, gain_q * (SCALE * LOG2E), gain_k, micro
    )
    q_low, q_raw = (a.reshape(micro, rows, H * HD) for a in (q_low, q_raw))
    gate_near = (swap(w_gate, 1), swap(w_gate, 2))
    kv_0, gate_near, w_up, w_down = tie((kv_0, gate_near, w_up, w_down))
    kv_0 = lax.all_gather(kv_0, "expert", axis=0, tiled=False)
    kv_1 = lax.all_gather(kv_1, "expert", axis=0, tiled=False)
    gate_far = (swap(gate_near[0][:1], 2), swap(gate_near[1][1:], 1))
    up_near = (swap(w_up, 1), swap(w_up, 2))
    chunk = 256

    def middle_of(mixed, at):
        part = hidden[at * rows : (at + 1) * rows]
        middle = part + mm(mixed[at], out_w)
        routed = (middle * rms_scale(middle) * gain_mid).astype(bf16)
        return middle, jnp.concatenate([routed, routing[at]], axis=-1)

    mixed, logs, shares = run_forward(q_low, kv_0[:, None], bias, step_heads, chunk, 0, [], True)
    mixed, up_near, gate_far = tie((mixed, up_near, gate_far))
    up_far = (swap(up_near[0][:1], 2), swap(up_near[1][1:], 1))
    middle_0, routed_0 = middle_of(mixed, 0)
    mixed, routed_0 = tie((mixed, routed_0))
    mixed, kv_1, up_far, w_down = tie((mixed, kv_1, up_far, w_down))
    down_near = (swap(w_down, 1), swap(w_down, 2))
    kv_all = [kv_0[:, None], kv_1[:, None]]
    mixed, logs, shares = run_forward(
        q_low, kv_all[1], bias, step_heads, chunk, 1, [mixed, logs, shares], True
    )
    mixed, down_near = tie((mixed, down_near))
    down_far = (swap(down_near[0][:1], 2), swap(down_near[1][1:], 1))
    middle_1, routed_1 = middle_of(mixed, 1)
    parts = [
        (w_gate, *gate_near, *gate_far),
        (w_up, *up_near, *up_far),
        (w_down, *down_near, *down_far),
    ]
    cots = [[(cot_all, 2 * b), (cot_all, 2 * b + 1)] for b in range(micro)]
    routed = [routed_0, routed_1]
    middle = jnp.stack([middle_0, middle_1])

    mix_parts, d_routeds = [], []
    kept = []
    for at in range(micro):
        tokens = lax.all_gather(routed[at], "expert", axis=0, tiled=False)
        tokens, parts = tie((tokens, parts))
        kept, mix, d_part = run_experts(tokens, cots[at], parts, capacity, at, micro, kept)
        kept, d_part, mix, d_routeds = tie((kept, d_part, mix, d_routeds))
        mix_parts.append(mix)
        d_routed = lax.psum_scatter(d_part, "expert", scatter_dimension=0, tiled=True)
        d_routeds.append(d_routed)
    picked, d_result, hidden_low, d_gate, d_up = (
        a.reshape(local_experts, -1, a.shape[-1]) for a in kept
    )

    def weight_grad(rows_in, rows_out):
        return jnp.einsum("era,erb->eab", rows_in, rows_out, preferred_element_type=f32).astype(bf16)

    first = scatter_far(weight_grad(picked, d_gate), 1)
    second = scatter_far(weight_grad(picked, d_up), 1)
    first, hidden_low = tie((first, hidden_low))
    first = scatter_near(first, 1)
    third = weight_grad(hidden_low, d_result)
    d_routeds[-1], first, second, third, mix_parts[0] = tie(
        (d_routeds[-1], first, second, third, mix_parts[0])
    )
    second = scatter_near(second, 1)
    third = scatter_far(third, 2)
    d_mixed, d_middle, d_branch, grad_mid = run_middle_back(
        d_routeds, middle, cotangent[:, 0], gain_mid[None, :], out_w
    )
    d_mixed, d_branch, third = tie((d_mixed, d_branch, third))
    third = scatter_near(third, 2)
    d_mixed = d_mixed.reshape(micro, rows, H * HD)
    cos_rows, sine_rows = (a.reshape(micro, rows, HD) for a in (cosine, sine))
    def share(core):
        part = lax.dynamic_index_in_dim(shares, core, axis=0, keepdims=False)
        part = part.reshape(2, total, -1)
        return jnp.einsum("zta,td->zad", part, d_branch, preferred_element_type=f32).astype(bf16)

    core = member % 2
    pairs = [(i, i ^ 1) for i in range(blocks)]
    got = lax.ppermute(share(1 - core), "expert", pairs)
    mixes = [lax.psum_scatter(mix_parts[0], "expert", scatter_dimension=0, tiled=True)]

    def backward(at, earlier):
        d_query, dkv_one, part = run_backward(
            q_low, kv_all[at], bias, mixed, d_mixed, logs, q_raw, cos_rows, sine_rows, gain_q,
            step_heads, chunk, at, earlier
        )
        return d_query, dkv_one[:, 0], part

    d_query, dkv_0, gain_0 = backward(0, [])
    d_query, dkv_0, got, second = tie((d_query, dkv_0, got, second))
    dkv_0 = lax.psum_scatter(dkv_0, "expert", scatter_dimension=0, tiled=False)
    out_grad = tie(share(core))
    out_grad = (out_grad.astype(f32) + got.astype(f32)).astype(bf16)
    d_query, out_grad = tie((d_query, out_grad))
    out_grad = scatter_far(out_grad, 1)
    d_query, dkv_1, gain_1 = backward(1, [d_query])
    grad_qn = gain_0 + gain_1
    d_query, dkv_1, out_grad, mixes, third = tie((d_query, dkv_1, out_grad, mixes, third))
    dkv_1 = lax.psum_scatter(dkv_1, "expert", scatter_dimension=0, tiled=False)
    out_grad = scatter_add(out_grad, 1)
    out_grad, first, second, third, d_query = tie((out_grad, first, second, third, d_query))
    out_grad = (swap(out_grad[0], 1), swap(out_grad[1], 2), out_grad[2])
    out_grad = scatter_sum(out_grad, 1).astype(bf16).reshape(-1, width)
    d_query = d_query.reshape(total, H * HD)
    dkv = jnp.concatenate([dkv_0, dkv_1], axis=0)
    dkv = dkv.reshape(total, KVH * 2 * HD)
    mix_part, dkv = tie((mix_parts[1], dkv))
    mixes.append(lax.psum_scatter(mix_part, "expert", scatter_dimension=0, tiled=True))
    outputs = [(middle[at] + mixes[at].astype(f32)).astype(bf16) for at in range(micro)]
    expert_grads = [scatter_sum(first, 1), scatter_sum(second, 1), scatter_sum(third, 2)]
    d_normed = mm(d_query, q_w)
    dkv, out_grad, expert_grads, d_normed = tie((dkv, out_grad, expert_grads, d_normed))
    dkv, dkv_t, grad_kn = run_key_back(dkv, k_raw, cosine, sine, gain_k)
    d_normed = d_normed + mm(dkv, kv_w)
    grad_output = lax.psum_scatter(
        out_grad,
        "expert",
        scatter_dimension=0,
        tiled=True,
        axis_index_groups=[list(range(c, blocks, 2)) for c in range(2)],
    ).astype(f32)
    d_in_norm, grad_in = norm_back(d_normed, hidden, scale_in, gain_in)
    input_grad = d_middle + d_in_norm
    gain_grads = jnp.concatenate([grad_in, grad_mid[0], grad_qn[0], grad_kn[0]]).reshape(shards, gain_len)
    grad_query, grad_key, grad_value, grad_gains = reduce_rows(d_query, dkv_t, normed, 3, gain_grads)
    return (
        jnp.stack(outputs)[:, None],
        input_grad.reshape(micro, 1, rows, width),
        grad_query,
        grad_key,
        grad_value,
        grad_output,
        grad_gains[0, :gain_len],
        *expert_grads,
    )


def solution(mesh):
    fast = mesh.shape["dp"] == 4 and mesh.shape["expert"] == 8
    return jax.shard_map(
        body_fast if fast else body_plain,
        mesh=mesh,
        in_specs=(
            P(None, "dp", "expert", None),
            P(None, "dp", "expert", None),
            P(None, "dp", None),
            P(None, "dp", "expert", None),
            P(None, "dp", "expert", None),
            P(None, "dp", "expert", None),
            P(None, ("dp", "expert")),
            P(None, ("dp", "expert")),
            P(None, ("dp", "expert")),
            P(("dp", "expert"), None),
            P(("dp", "expert")),
            P("expert", "dp", None),
            P("expert", "dp", None),
            P("expert", None, "dp"),
        ),
        out_specs=(
            P(None, "dp", "expert", None),
            P(None, "dp", "expert", None),
            P(None, ("dp", "expert")),
            P(None, ("dp", "expert")),
            P(None, ("dp", "expert")),
            P(("dp", "expert"), None),
            P(("dp", "expert")),
            P("expert", "dp", None),
            P("expert", "dp", None),
            P("expert", None, "dp"),
        ),
        check_vma=False,
    )
```

```python
import functools
import math

import jax
import jax.numpy as jnp
from jax import lax
from jax.experimental import pallas as pl
from jax.experimental.pallas import tpu as pltpu
from jax.sharding import PartitionSpec as P

H = 32
KVH = 4
HD = 128
FF = 768
TOPK = 8
PROMPT = 1024
PER_KV = H // KVH

EPSILON = 1e-06
ROPE_BASE = 1000000.0
MASKED = -1e30
LOG2E = math.log2(math.e)
SCALE = HD ** (-0.5)

bf16 = jnp.bfloat16
f32 = jnp.float32
NT = (((1,), (1,)), ((), ()))
TN = (((0,), (0,)), ((), ()))
NN = (((1,), (0,)), ((), ()))
BOTH = ("dp", "expert")
VMEM_LIMIT = 56 * 1024 * 1024
LIGHT = pl.CostEstimate(flops=1_000_000, bytes_accessed=1_000_000, transcendentals=0)


def mm(a, b, dims=NN):
    return lax.dot_general(a, b, dims, preferred_element_type=f32)


def rms_scale(values):
    return lax.rsqrt(jnp.mean(values * values, axis=-1, keepdims=True) + EPSILON)


def norm_back(upstream, values, inv_rms, norm_gain):
    lifted = upstream * norm_gain
    inner_dot = jnp.mean(lifted * values, axis=-1, keepdims=True)
    back_grad = inv_rms * lifted - values * (inv_rms * inv_rms * inv_rms) * inner_dot
    gain_grad = jnp.sum((upstream * values * inv_rms).reshape(-1, values.shape[-1]), axis=0)
    return (back_grad, gain_grad)


def rotate(values, cosine, sine_part):
    half_dim = values.shape[-1] // 2
    first_half = values[..., :half_dim]
    second_half = values[..., half_dim:]
    return jnp.concatenate(
        [
            first_half * cosine - second_half * sine_part,
            second_half * cosine + first_half * sine_part,
        ],
        axis=-1,
    )


def turn(values, cosine, sine):
    return values * cosine + pltpu.roll(values, HD // 2, 1) * sine


def project(x_ref, wq_ref, wkv_ref, cos_ref, sin_ref, gq_ref, gk_ref, q_ref, qraw_ref, kraw_ref, wkv_out, *kv_refs):
    x = x_ref[...]
    cosine, sine = cos_ref[...], sin_ref[...]
    for at in range(0, PER_KV * HD, 2 * HD):
        raw = mm(x, wq_ref[at : at + 2 * HD], NT)
        qraw_ref[:, at : at + 2 * HD] = raw
        for lane in (0, HD):
            head = raw[:, lane : lane + HD]
            normed = head * rms_scale(head) * gq_ref[...]
            q_ref[:, at + lane : at + lane + HD] = turn(normed, cosine, sine).astype(bf16)
    piece = HD // PER_KV
    w_k = [wkv_ref[2 * piece * i : 2 * piece * i + piece] for i in range(PER_KV)]
    w_v = [wkv_ref[2 * piece * i + piece : 2 * piece * (i + 1)] for i in range(PER_KV)]
    w_kv = jnp.concatenate(w_k + w_v, axis=0)
    wkv_out[...] = w_kv
    raw = mm(x, w_kv, NT)
    key = raw[:, :HD]
    kraw_ref[...] = key
    normed = key * rms_scale(key) * gk_ref[...]
    key, value = turn(normed, cosine, sine).astype(bf16), raw[:, HD:].astype(bf16)
    rows = x.shape[0] // len(kv_refs)
    for b, kv_ref in enumerate(kv_refs):
        kv_ref[:, :HD] = key[b * rows : (b + 1) * rows]
        kv_ref[:, HD:] = value[b * rows : (b + 1) * rows]


def run_project(x, wq, wkv, cosine, sine, gain_q, gain_k, micro):
    tokens, width = x.shape
    wide = PER_KV * HD
    whole = lambda a: pl.BlockSpec(a.shape, lambda g: (0, 0))
    cols = lambda n: pl.BlockSpec((tokens, n), lambda g: (0, g))
    rows = lambda n: pl.BlockSpec((n, width), lambda g: (g, 0))
    return pl.pallas_call(
        project,
        grid=(KVH,),
        in_specs=[whole(x), rows(wide), rows(2 * HD), whole(cosine), whole(sine), whole(gain_q), whole(gain_k)],
        out_specs=[cols(wide), cols(wide), cols(HD), rows(2 * HD)]
        + [pl.BlockSpec((tokens // micro, 2 * HD), lambda g: (0, g))] * micro,
        out_shape=[
            jax.ShapeDtypeStruct((tokens, H * HD), bf16),
            jax.ShapeDtypeStruct((tokens, H * HD), f32),
            jax.ShapeDtypeStruct((tokens, KVH * HD), f32),
            jax.ShapeDtypeStruct((KVH * 2 * HD, width), bf16),
        ]
        + [jax.ShapeDtypeStruct((tokens // micro, KVH * 2 * HD), bf16)] * micro,
        compiler_params=pltpu.CompilerParams(vmem_limit_bytes=VMEM_LIMIT),
        cost_estimate=LIGHT,
    )(x, wq, wkv, cosine, sine, gain_q, gain_k)


def norm_turn_back(grad, raw, cosine, sine, gain):
    grad = turn(grad, cosine, -sine)
    scale = rms_scale(raw)
    lifted = grad * gain
    inner = jnp.mean(lifted * raw, axis=-1, keepdims=True)
    back = scale * lifted - raw * (scale * scale * scale) * inner
    return back, jnp.sum(grad * raw * scale, axis=0, keepdims=True)


def key_back(dkv_ref, kraw_ref, cos_ref, sin_ref, gk_ref, out_ref, out_t_ref, gain_ref):
    gain_sum = 0.0
    for g in range(KVH):
        key = slice(2 * g * HD, (2 * g + 1) * HD)
        value = slice((2 * g + 1) * HD, (2 * g + 2) * HD)
        grad = dkv_ref[:, key].astype(f32)
        back, part = norm_turn_back(
            grad, kraw_ref[:, g * HD : (g + 1) * HD], cos_ref[...], sin_ref[...], gk_ref[...]
        )
        gain_sum += part
        low = back.astype(bf16)
        out_ref[:, key] = low
        out_t_ref[key] = low.T
        out_ref[:, value] = dkv_ref[:, value]
        out_t_ref[value] = dkv_ref[:, value].T
    gain_ref[...] = gain_sum


def run_key_back(dkv, key_raw, cosine, sine, gain):
    tokens, wide = dkv.shape
    return pl.pallas_call(
        key_back,
        out_shape=[
            jax.ShapeDtypeStruct((tokens, wide), bf16),
            jax.ShapeDtypeStruct((wide, tokens), bf16),
            jax.ShapeDtypeStruct((1, HD), f32),
        ],
        compiler_params=pltpu.CompilerParams(vmem_limit_bytes=VMEM_LIMIT),
    )(dkv, key_raw, cosine, sine, gain)


def attend_forward(step_heads, chunk, q_ref, kv_ref, bias_ref, o_ref, log_ref, o2_ref=None):
    group_len = bias_ref.shape[1]
    keys = kv_ref[:, 0, :, :HD].reshape(group_len, HD)
    values_t = kv_ref[:, 0, :, HD:].reshape(group_len, HD).T
    rows = q_ref.shape[1]
    for step in range(PER_KV // step_heads):
        heads = range(step * step_heads, (step + 1) * step_heads)
        query = jnp.concatenate([q_ref[0, :, h * HD : (h + 1) * HD] for h in heads], axis=0)
        mixed, row_sum = 0.0, 0.0
        for at in range(0, group_len, chunk):
            scores = mm(keys[at : at + chunk], query, NT)
            prob = jnp.exp2(scores + bias_ref[0, at : at + chunk, :])
            row_sum += jnp.sum(prob, axis=0, keepdims=True)
            mixed += mm(values_t[:, at : at + chunk], prob.astype(bf16))
        out = (mixed / row_sum).T.astype(bf16)
        for i, h in enumerate(heads):
            part = out[i * rows : (i + 1) * rows]
            o_ref[0, :, h * HD : (h + 1) * HD] = part
            if o2_ref is not None:
                lane = (h // 2) % 2 * HD
                o2_ref[h % 2, h // 4, 0, :, lane : lane + HD] = part
        log_ref[0, 0, step : step + 1, :] = jnp.log2(row_sum)


def attend_backward(
    step_heads, chunk, q_ref, kv_ref, bias_ref, o_ref, do_ref, log_ref, raw_ref, cos_ref, sin_ref, gain_ref,
    dq_ref, dkv_ref, gain_out, dk_acc, dv_acc
):
    group_len = bias_ref.shape[1]
    keys = kv_ref[:, 0, :, :HD].reshape(group_len, HD)
    values = kv_ref[:, 0, :, HD:].reshape(group_len, HD)
    keys_t = keys.T
    rows = q_ref.shape[1]
    cosine, sine, gain = cos_ref[0], sin_ref[0], gain_ref[...]

    @pl.when(pl.program_id(0) == 0)
    def _():
        gain_out[...] = jnp.zeros_like(gain_out)

    gain_sum = 0.0
    dk_acc[...] = jnp.zeros_like(dk_acc)
    dv_acc[...] = jnp.zeros_like(dv_acc)
    for step in range(PER_KV // step_heads):
        heads = range(step * step_heads, (step + 1) * step_heads)
        query = jnp.concatenate([q_ref[0, :, h * HD : (h + 1) * HD] for h in heads], axis=0)
        grad = jnp.concatenate([do_ref[0, :, h * HD : (h + 1) * HD] for h in heads], axis=0)
        mixed = jnp.concatenate([o_ref[0, :, h * HD : (h + 1) * HD] for h in heads], axis=0)
        row_dot = jnp.sum((grad.astype(f32) * mixed.astype(f32)).T, axis=0, keepdims=True)
        log_sum = log_ref[0, 0, step : step + 1, :]
        dq_t = 0.0
        for at in range(0, group_len, chunk):
            part = slice(at, at + chunk)
            scores = mm(keys[part], query, NT)
            prob = jnp.exp2(scores + (bias_ref[0, part, :] - log_sum))
            d_prob = mm(values[part], grad, NT)
            d_score = (prob * (d_prob - row_dot)).astype(bf16)
            dv_acc[part] += mm(prob.astype(bf16), grad)
            dk_acc[part] += mm(d_score, query)
            dq_t += mm(keys_t[:, part], d_score)
        out = (dq_t * SCALE).T.astype(bf16).astype(f32)
        for i, h in enumerate(heads):
            head = slice(h * HD, (h + 1) * HD)
            back, part = norm_turn_back(
                out[i * rows : (i + 1) * rows], raw_ref[0, :, head], cosine, sine, gain
            )
            dq_ref[0, :, head] = back.astype(bf16)
            gain_sum += part
    gain_out[...] += gain_sum
    blocks = dkv_ref.shape[0]
    dkv_ref[:, 0, :, :HD] = (dk_acc[...] * (1.0 / LOG2E)).astype(bf16).reshape(blocks, rows, HD)
    dkv_ref[:, 0, :, HD:] = dv_acc[...].astype(bf16).reshape(blocks, rows, HD)


def attention_specs(rows, group_len, blocks, step_heads, at):
    wide = PER_KV * HD
    q_spec = pl.BlockSpec((1, rows, wide), lambda g: (at, 0, g))
    kv_spec = pl.BlockSpec((blocks, 1, rows, 2 * HD), lambda g: (0, 0, 0, g))
    bias_spec = pl.BlockSpec((1, group_len, step_heads * rows), lambda g: (at, 0, 0))
    log_spec = pl.BlockSpec((1, 1, PER_KV // step_heads, step_heads * rows), lambda g: (at, g, 0, 0))
    return q_spec, kv_spec, bias_spec, log_spec


def run_forward(query, kv_all, bias, step_heads, chunk, at, earlier, again=False):
    micro, rows, _ = query.shape
    blocks = kv_all.shape[0]
    group_len = bias.shape[1]
    q_spec, kv_spec, bias_spec, log_spec = attention_specs(rows, group_len, blocks, step_heads, at)
    flops = 4 * rows * H * HD * group_len

    def kernel(*refs):
        attend_forward(step_heads, chunk, *refs[:3], *refs[3 + len(earlier) :])

    return pl.pallas_call(
        kernel,
        grid=(KVH,),
        in_specs=[q_spec, kv_spec, bias_spec] + [pl.BlockSpec(memory_space=pl.ANY)] * len(earlier),
        out_specs=[q_spec, log_spec]
        + again * [pl.BlockSpec((2, 2, 1, rows, 2 * HD), lambda g: (0, 0, at, 0, g))],
        out_shape=[
            jax.ShapeDtypeStruct(query.shape, bf16),
            jax.ShapeDtypeStruct((micro, KVH, PER_KV // step_heads, step_heads * rows), f32),
        ]
        + again * [jax.ShapeDtypeStruct((2, 2, micro, rows, KVH * 2 * HD), bf16)],
        input_output_aliases={3 + i: i for i in range(len(earlier))},
        compiler_params=pltpu.CompilerParams(vmem_limit_bytes=VMEM_LIMIT),
        cost_estimate=LIGHT,
    )(query, kv_all, bias, *earlier)


def run_backward(query, kv_all, bias, mixed, grad, logs, raw, cosine, sine, gain, step_heads, chunk, at, earlier):
    micro, rows, _ = query.shape
    blocks = kv_all.shape[0]
    group_len = bias.shape[1]
    q_spec, kv_spec, bias_spec, log_spec = attention_specs(rows, group_len, blocks, step_heads, at)
    flops = 10 * rows * H * HD * group_len
    gain_spec = pl.BlockSpec((1, HD), lambda g: (0, 0))

    def kernel(*refs):
        attend_backward(step_heads, chunk, *refs[:10], *refs[10 + len(earlier) :])

    return pl.pallas_call(
        kernel,
        grid=(KVH,),
        in_specs=[q_spec, kv_spec, bias_spec, q_spec, q_spec, log_spec, q_spec]
        + [pl.BlockSpec((1, rows, HD), lambda g: (at, 0, 0))] * 2
        + [gain_spec]
        + [pl.BlockSpec(memory_space=pl.ANY)] * len(earlier),
        out_specs=[q_spec, kv_spec, gain_spec],
        out_shape=[
            jax.ShapeDtypeStruct(query.shape, bf16),
            jax.ShapeDtypeStruct(kv_all.shape, bf16),
            jax.ShapeDtypeStruct((1, HD), f32),
        ],
        input_output_aliases={10 + i: i for i in range(len(earlier))},
        scratch_shapes=[pltpu.VMEM((group_len, HD), f32), pltpu.VMEM((group_len, HD), f32)],
        compiler_params=pltpu.CompilerParams(vmem_limit_bytes=VMEM_LIMIT),
        cost_estimate=LIGHT,
    )(query, kv_all, bias, mixed, grad, logs, raw, cosine, sine, gain, *earlier)


def middle_back(r0_ref, r1_ref, mid_ref, cot_ref, gain_ref, w_ref, mix_ref, dmid_ref, low_ref, gain_out):
    @pl.when(pl.program_id(0) == 0)
    def _():
        gain_sum = 0.0
        rows = r0_ref.shape[0]
        for b, ref in enumerate((r0_ref, r1_ref)):
            grad = ref[...].astype(f32)
            middle = mid_ref[b]
            scale = rms_scale(middle)
            lifted = grad * gain_ref[...]
            inner = jnp.mean(lifted * middle, axis=-1, keepdims=True)
            total = cot_ref[b].astype(f32) + scale * lifted - middle * (scale * scale * scale) * inner
            gain_sum += jnp.sum(grad * middle * scale, axis=0, keepdims=True)
            dmid_ref[b * rows : (b + 1) * rows] = total
            low_ref[b * rows : (b + 1) * rows] = total.astype(bf16)
        gain_out[...] = gain_sum

    mix_ref[...] = mm(low_ref[...], w_ref[...], NT).astype(bf16)


def run_middle_back(routed, middle, cot, gain, out_w):
    micro, rows, width = middle.shape
    total = micro * rows
    piece = 512
    whole = lambda *shape: pl.BlockSpec(shape, lambda i: (0,) * len(shape))
    return pl.pallas_call(
        middle_back,
        grid=(out_w.shape[0] // piece,),
        in_specs=[whole(rows, width)] * 2
        + [whole(micro, rows, width)] * 2
        + [whole(1, width), pl.BlockSpec((piece, width), lambda i: (i, 0))],
        out_specs=[
            pl.BlockSpec((total, piece), lambda i: (0, i)),
            whole(total, width),
            whole(total, width),
            whole(1, width),
        ],
        out_shape=[
            jax.ShapeDtypeStruct((total, out_w.shape[0]), bf16),
            jax.ShapeDtypeStruct((total, width), f32),
            jax.ShapeDtypeStruct((total, width), bf16),
            jax.ShapeDtypeStruct((1, width), f32),
        ],
        compiler_params=pltpu.CompilerParams(vmem_limit_bytes=VMEM_LIMIT),
        cost_estimate=LIGHT,
    )(*routed, middle, cot, gain, out_w)


MESH = pl.DeviceIdType.MESH


def gather_kernel(phases, count, late, *refs):
    ins, outs, sems = refs[:count], refs[count : 2 * count], refs[2 * count :]
    dp = lax.axis_index("dp"); member = lax.axis_index("expert")
    blocks = lax.axis_size("expert")
    core = member % 2; z = member // 2
    depth = blocks // 2
    sibling = (dp, member + 1 - 2 * core)
    by_x = (dp + 1 - 2 * (dp % 2), member)
    by_y = ((dp + 2) % 4, member)
    x_at, y_at, far_at = by_x[0], by_y[0], 3 - dp
    above, below = (dp, member + 2), (dp, member - 2)
    barrier = pltpu.get_barrier_semaphore()
    peers = [(sibling, None), (by_x, None), (by_y, None), (above, z < depth - 1), (below, z > 0)]
    for peer, ok in peers:
        if ok is None:
            pl.semaphore_signal(barrier, inc=1, device_id=peer, device_id_type=MESH)
        else:
            @pl.when(ok)
            def _(peer=peer):
                pl.semaphore_signal(barrier, inc=1, device_id=peer, device_id_type=MESH)
    @pl.when((z == 0) | (z == depth - 1))
    def _(): pl.semaphore_wait(barrier, 4)
    @pl.when((z > 0) & (z < depth - 1))
    def _(): pl.semaphore_wait(barrier, 5)

    def guarded(ok, run):
        if ok is None: run()
        else: pl.when(ok)(run)

    class Item:
        pass

    def make(i):
        src, out = ins[i], outs[i]
        flat = i in late
        rows = src.shape[0]
        half = rows // 2
        (own_sem, sz, rz, sxy, rxy, sc, rc) = sems[i * 7 : (i + 1) * 7]
        def at(d, s, lo=0, n=rows):
            first = s * 2 + core if flat else d * blocks + s * 2 + core
            return out.at[pl.ds(pl.multiple_of(first * rows + lo, 16 if half % 16 == 0 else 8), n)]
        def copy(a, b, ss, rs, to):
            return pltpu.make_async_remote_copy(src_ref=a, dst_ref=b, send_sem=ss, recv_sem=rs, device_id=to, device_id_type=MESH)
        def block(d, s):
            return at(d, s)
        it = Item()
        def local():
            return pltpu.make_async_copy(src, at(dp, z), own_sem)
        def up(s, ref): return copy(ref, at(dp, s), sz.at[0, s], rz.at[s], above)
        def down(s, ref): return copy(ref, at(dp, s), sz.at[1, s], rz.at[s], below)
        def to_x(s, ref): return copy(ref, at(dp, s), sxy.at[0, s], rxy.at[0, s], by_x)
        def to_y(s, ref): return copy(ref, at(dp, s), sxy.at[1, s], rxy.at[1, s], by_y)
        def half_y(s):
            return copy(at(x_at, s, 0, half), at(x_at, s, 0, half), sxy.at[2, s], rxy.at[2, s], by_y)
        def half_x(s):
            return copy(at(y_at, s, half, half), at(y_at, s, half, half), sxy.at[3, s], rxy.at[3, s], by_x)
        def to_core(r, d, s, ref): return copy(ref, at(d, s), sc.at[r, s], rc.at[r, s], sibling)
        def spread(s, ref):
            if not flat:
                to_x(s, ref).start(); to_y(s, ref).start()
            to_core(0, dp, s, ref).start()
        def start_up():
            up(z, src).start()
        def start_down():
            down(z, src).start()
        def start():
            local().start()
            if not flat:
                guarded(z < depth - 1, start_up)
                guarded(z > 0, start_down)
            spread(z, src)
        def z_event(s, ok, rising):
            def run():
                up(s, at(dp, s)).wait_recv()
                if rising: guarded(z < depth - 1, lambda: up(s, at(dp, s)).start())
                else: guarded(z > 0, lambda: down(s, at(dp, s)).start())
                spread(s, at(dp, s))
            pl.when(ok)(run)
        def near_event(s, ok):
            def run():
                to_x(s, at(dp, s)).wait_recv()
                half_y(s).start()
                to_core(1, x_at, s, at(x_at, s)).start()
                to_y(s, at(dp, s)).wait_recv()
                half_x(s).start()
                to_core(2, y_at, s, at(y_at, s)).start()
            guarded(ok, run)
        def far_event(s, ok):
            def run():
                half_y(s).wait_recv(); half_x(s).wait_recv()
                to_core(3, far_at, s, at(far_at, s)).start()
            guarded(ok, run)
        owners = (dp,) if flat else (dp, x_at, y_at, far_at)
        def core_wait(s):
            for r, d in enumerate(owners):
                to_core(r, d, s, at(d, s)).wait_recv()
        def finish():
            local().wait()
            for s in range(depth):
                if not flat:
                    for c in (to_x(s, at(dp, s)), to_y(s, at(dp, s)), half_y(s), half_x(s)): c.wait_send()
                for r, d in enumerate(owners): to_core(r, d, s, at(d, s)).wait_send()
                guarded((z >= s) & (z < depth - 1), lambda: up(s, at(dp, s)).wait_send())
                guarded((z <= s) & (z > 0), lambda: down(s, at(dp, s)).wait_send())
        it.start_up, it.start_down = start_up, start_down
        it.start, it.z_event, it.near_event, it.far_event, it.core_wait, it.finish = start, z_event, near_event, far_event, core_wait, finish
        return it
    items = [make(i) for i in range(count)]
    def around(d):
        if d == 0: return [(z, None, True)]
        return [(z - d, z >= d, True), (z + d, z + d < depth, False)]
    for n, phase in enumerate(phases):
        its = [items[i] for i in phase]
        for it in its: it.start()
        lates = [items[i] for i in late]
        for it in lates: it.start()
        def late_sends(d):
            for it in lates:
                if d < depth - 1:
                    pl.when(z == d)(it.start_up)
                    pl.when(z == depth - 1 - d)(it.start_down)
        late_sends(0)
        for d in range(1, depth + 2):
            if d < depth:
                for s, ok, rising in around(d):
                    for it in its: it.z_event(s, ok, rising)
                late_sends(d)
            if d - 1 < depth:
                for s, ok, _ in around(d - 1):
                    for it in its: it.near_event(s, ok)
            if d > 2:
                for s, ok, rising in around(d - 2):
                    for it in lates: it.z_event(s, ok, rising)
            if d - 2 >= 0:
                for s, ok, _ in around(d - 2):
                    for it in its: it.far_event(s, ok)
    for it in items:
        for s in range(depth): it.core_wait(s)
    for it in items: it.finish()

def gather_rows(arrays, phases, cid, late=()):
    shards = lax.axis_size("dp") * lax.axis_size("expert")
    depth = lax.axis_size("expert") // 2
    D = pltpu.SemaphoreType.DMA
    sems = []
    for _ in arrays:
        sems += [D, D((2, depth)), D((depth,)), D((4, depth)), D((4, depth)), D((4, depth)), D((4, depth))]
    return pl.pallas_call(
        functools.partial(gather_kernel, phases, len(arrays), late),
        out_shape=[
            jax.ShapeDtypeStruct(((2 * depth if i in late else shards) * a.shape[0],) + a.shape[1:], a.dtype)
            for i, a in enumerate(arrays)
        ],
        in_specs=[pl.BlockSpec(memory_space=pl.ANY)] * len(arrays),
        out_specs=[pl.BlockSpec(memory_space=pl.ANY)] * len(arrays),
        scratch_shapes=sems,
        compiler_params=pltpu.CompilerParams(collective_id=cid, has_side_effects=True),
        cost_estimate=pl.CostEstimate(flops=0, bytes_accessed=400_000_000, transcendentals=0),
    )(*arrays)


def reduce_kernel(rows, cuts, a_ref, extra_ref, b_ref, g_ref, q_out, k_out, v_out, go_ref, o_ref, sib, got, own, far, near, plane, got_z,
                  s0, r0, s1, r1, s2, r2, s3, r3, g_acc, g_got, g_z, gs, gr, gsz, grz):
    dp = lax.axis_index("dp"); member = lax.axis_index("expert")
    core = member % 2; z = member // 2
    sibling = (dp, member + 1 - 2 * core)
    by_x = (dp + 1 - 2 * (dp % 2), member)
    by_y = ((dp + 2) % 4, member)
    x_at, y_at = by_x[0], by_y[0]
    far_at = 3 - dp
    half = rows // 2
    depth = lax.axis_size("expert") // 2
    barrier = pltpu.get_barrier_semaphore()
    peers = [sibling, by_x, by_y] + [(dp, ((z + d) % depth) * 2 + core) for d in range(1, depth)]
    for peer in peers:
        pl.semaphore_signal(barrier, inc=1, device_id=peer, device_id_type=MESH)
    pl.semaphore_wait(barrier, len(peers))

    def pick(table):
        at = table[depth-1]
        for i in range(depth - 1):
            at = jnp.where(z == i, table[i], at)
        return at
    orders = [[3, 3, 0, 0], [2, 0, 3, 1], [1, 2, 1, 2], [0, 1, 2, 3]]
    targets = [pick(t) for t in orders]
    cols = b_ref.shape[1] // cuts

    def copy(src, dst, ssem, rsem, to):
        return pltpu.make_async_remote_copy(src_ref=src, dst_ref=dst, send_sem=ssem, recv_sem=rsem, device_id=to, device_id_type=MESH)

    blocks = 2 * depth
    piece = (rows - HD) // 2

    def product(half_of, k, put):
        spot = targets[k] * 2 + half_of

        def step(i, _):
            shard = (i // cuts) * blocks + spot
            at = (i // cuts) * rows
            col = pl.ds(pl.multiple_of((i % cuts) * cols, cols), cols)
            part = mm(a_ref[:, pl.ds(pl.multiple_of(shard * HD, HD), HD)], b_ref[:, col], TN)
            put(pl.ds(pl.multiple_of(at, 16), HD), col, part)
            if piece:
                base = (shard // PER_KV) * (2 * HD) + (shard % PER_KV) * piece
                small = jnp.concatenate(
                    [
                        extra_ref[pl.ds(pl.multiple_of(base, 16), piece), :],
                        extra_ref[pl.ds(pl.multiple_of(base + HD, 16), piece), :],
                    ],
                    axis=0,
                )
                put(pl.ds(pl.multiple_of(at + HD, 16), 2 * piece), col, mm(small, b_ref[:, col]))
            return 0

        lax.fori_loop(0, 4 * cuts, step, 0)

    def gain_hop(i, src, to):
        return copy(src, g_got.at[i, pl.ds(0, src.shape[0])], gs.at[i], gr.at[i], to)
    hops = {}
    def gain_step(i):
        rows4 = lambda at: pl.ds(pl.multiple_of(at * 8, 8), 8)
        if i == 0:
            hops[0] = gain_hop(0, g_ref.at[pl.ds(pl.multiple_of((1 - core) * 32, 32), 32)], sibling)
        elif i == 1:
            hops[0].wait_recv()
            g_acc[...] = g_ref[pl.ds(pl.multiple_of(core * 32, 32), 32)] + g_got[0]
            hops[1] = gain_hop(1, g_acc.at[pl.ds(pl.multiple_of((1 - dp // 2) * 16, 16), 16)], by_y)
        elif i == 2:
            hops[1].wait_recv()
            mine = pl.ds(pl.multiple_of((dp // 2) * 16, 16), 16)
            g_acc[mine] += g_got[1, :16]
            hops[2] = gain_hop(2, g_acc.at[rows4(x_at)], by_x)
        elif i == 3:
            hops[2].wait_recv()
            g_acc[rows4(dp)] += g_got[2, :8]
            for d in range(1, depth):
                to = (z + d) % depth
                hops[2 + d] = copy(g_acc.at[pl.ds(dp * 8 + to, 1)], g_z.at[z], gsz.at[d - 1], grz.at[z], (dp, to * 2 + core))
        if i < 3:
            hops[i].start()
        else:
            for d in range(1, depth):
                hops[2 + d].start()
    def gain_end():
        total = g_acc[pl.ds(dp * 8 + z, 1)]
        for d in range(1, depth):
            src = (z + d) % depth
            copy(g_acc.at[pl.ds(dp * 8, 1)], g_z.at[src], gsz.at[0], grz.at[src], sibling).wait_recv()
            total += g_z[src]
        go_ref[...] = total
        for i in hops:
            hops[i].wait_send()
    sib_copies, far_copies, near_copies, z_copies = {}, {}, {}, {}
    def sib_step(k):
        slot = k % 2
        if k >= 2:
            sib_copies[k - 2].wait_send()
        def put(r, c, part):
            sib[slot, r, c] = part.astype(bf16)
        product(1 - core, k, put)
        sib_copies[k] = copy(sib.at[slot], got.at[k], s0.at[slot], r0.at[k], sibling)
        sib_copies[k].start()
    def blk(at):
        return pl.ds(pl.multiple_of(at * rows, 16), rows)
    def own_step(k):
        sib_copies[k].wait_recv()
        def put(r, c, part):
            own[k, r, c] = (part + got[k, r, c].astype(f32)).astype(bf16)
        product(core, k, put)
        base = pl.multiple_of(far_at * rows, 16)
        far_copies[k] = (
            copy(own.at[k, pl.ds(base, half)], far.at[k, 0], s1.at[k, 0], r1.at[k, 0], by_x),
            copy(own.at[k, pl.ds(pl.multiple_of(base + half, 16), half)], far.at[k, 1], s1.at[k, 1], r1.at[k, 1], by_y),
        )
        for c in far_copies[k]: c.start()
    def near_step(k):
        a, b = far_copies[k]
        a.wait_recv()
        rng = pl.ds(pl.multiple_of(y_at * rows, 16), half)
        own[k, rng] = (own[k, rng].astype(f32) + far[k, 0].astype(f32)).astype(bf16)
        to_y = copy(own.at[k, blk(y_at)], near.at[k, 1], s2.at[k, 1], r2.at[k, 1], by_y)
        to_y.start()
        b.wait_recv()
        rng = pl.ds(pl.multiple_of(x_at * rows + half, 16), half)
        own[k, rng] = (own[k, rng].astype(f32) + far[k, 1].astype(f32)).astype(bf16)
        to_x = copy(own.at[k, blk(x_at)], near.at[k, 0], s2.at[k, 0], r2.at[k, 0], by_x)
        to_x.start()
        near_copies[k] = (to_x, to_y)
    def plane_step(k):
        for c in near_copies[k]: c.wait_recv()
        total = own[k, blk(dp)].astype(f32) + near[k, 0].astype(f32) + near[k, 1].astype(f32)
        if k < depth - 1:
            plane[k] = total.astype(bf16)
            to = (dp, targets[k] * 2 + core)
            z_copies[k] = copy(plane.at[k], got_z.at[z], s3.at[k], r3.at[z], to)
            z_copies[k].start()
        else:
            o_ref[...] = total
    gain_step(0)
    sib_step(0); sib_step(1)
    own_step(0)
    gain_step(1)
    sib_step(2)
    own_step(1)
    gain_step(2)
    near_step(0)
    sib_step(3)
    own_step(2)
    gain_step(3)
    near_step(1)
    plane_step(0)
    own_step(3)
    near_step(2)
    plane_step(1)
    near_step(3)
    plane_step(2)
    plane_step(3)
    for d in range(1, depth):
        src = (z + d) % depth
        copy(plane.at[0], got_z.at[src], s3.at[0], r3.at[src], sibling).wait_recv()
        o_ref[...] += got_z[src].astype(f32)
    q_out[...] = o_ref[:HD].T
    k_out[...] = o_ref[HD : HD + piece].T
    v_out[...] = o_ref[HD + piece :].T
    gain_end()
    for k in range(depth):
        if k >= 2: sib_copies[k].wait_send()
        for c in far_copies[k]: c.wait_send()
        for c in near_copies[k]: c.wait_send()
        if k < depth - 1: z_copies[k].wait_send()

def reduce_rows(a, extra, b, cid, gains=None):
    tokens, width = b.shape
    depth = 4
    rows = HD + extra.shape[0] // 32
    D = pltpu.SemaphoreType.DMA
    lanes = 256
    padded = jnp.zeros((32, lanes), f32)
    if gains is not None:
        padded = jnp.pad(gains, ((0, 0), (0, lanes - gains.shape[1])))
    padded = padded.reshape(4, depth, 2, lanes).transpose(2, 0, 1, 3)
    padded = jnp.pad(padded, ((0, 0), (0, 0), (0, 8 - depth), (0, 0))).reshape(64, lanes)
    return pl.pallas_call(
        functools.partial(reduce_kernel, rows, 4),
        out_shape=[
            jax.ShapeDtypeStruct((width, HD), f32),
            jax.ShapeDtypeStruct((width, (rows - HD) // 2), f32),
            jax.ShapeDtypeStruct((width, (rows - HD) // 2), f32),
            jax.ShapeDtypeStruct((1, lanes), f32),
        ],
        in_specs=[pl.BlockSpec(memory_space=pltpu.VMEM)] * 4,
        out_specs=[pl.BlockSpec(memory_space=pltpu.VMEM)] * 4,
        scratch_shapes=[
            pltpu.VMEM((rows, width), f32),
            pltpu.VMEM((2, 4 * rows, width), bf16),
            pltpu.VMEM((depth, 4 * rows, width), bf16),
            pltpu.VMEM((depth, 4 * rows, width), bf16),
            pltpu.VMEM((depth, 2, rows // 2, width), bf16),
            pltpu.VMEM((depth, 2, rows, width), bf16),
            pltpu.VMEM((depth - 1, rows, width), bf16),
            pltpu.VMEM((depth, rows, width), bf16),
            D((2,)), D((depth,)), D((depth, 2)), D((depth, 2)), D((depth, 2)), D((depth, 2)), D((depth - 1,)), D((depth,)),
            pltpu.VMEM((32, lanes), f32), pltpu.VMEM((3, 32, lanes), f32), pltpu.VMEM((depth, 1, lanes), f32),
            D((3,)), D((3,)), D((depth - 1,)), D((depth,)),
        ],
        compiler_params=pltpu.CompilerParams(vmem_limit_bytes=60*1024*1024, collective_id=cid, has_side_effects=True),
        cost_estimate=pl.CostEstimate(flops=2*tokens*32*rows*width, bytes_accessed=10_000_000, transcendentals=0),
    )(a, extra, b, padded)


ROUTE_LANES = 128


def picks_of(routing, first, local_experts, capacity):
    rows = routing.shape[0]
    lanes = lax.broadcasted_iota(jnp.int32, (rows, ROUTE_LANES), 1)
    places = lax.broadcasted_iota(jnp.int32, (rows, local_experts * capacity), 1)
    hit, weighted = None, 0.0
    for e in range(local_experts):

        def column(base):
            return jnp.sum(jnp.where(lanes == base + first + e, routing, 0.0), axis=1, keepdims=True)

        slot = column(0).astype(jnp.int32)
        here = places == jnp.where(slot >= 0, slot + e * capacity, -1)
        hit = here if hit is None else hit | here
        weighted = weighted + jnp.where(here, column(32) + column(64), 0.0)
    return jnp.where(hit, 1.0, 0.0).astype(bf16), weighted.astype(bf16)


def pick_kernel(capacity, local_experts, n_alias, tok_ref, cot_a, cot_b, *refs):
    x_ref, dy_ref = refs[n_alias:]
    width = cot_a.shape[3]
    cot = jnp.concatenate([cot_a[0, 0], cot_b[0, 0]], axis=0)
    first = lax.axis_index("expert") * local_experts
    routing = tok_ref[0, :, width:]
    hit, _ = picks_of(routing.astype(f32), first, local_experts, capacity)
    x = mm(hit, tok_ref[0, :, :width], TN).astype(bf16)
    rows = mm(hit, routing, TN)
    lanes = lax.broadcasted_iota(jnp.int32, rows.shape, 1)
    owner = lax.broadcasted_iota(jnp.int32, rows.shape, 0) // capacity
    at = lanes - first - owner
    weight = jnp.sum(jnp.where((at == 32) | (at == 64), rows, 0.0), axis=1, keepdims=True)
    dy = (mm(hit, cot, TN) * weight).astype(bf16)
    for e in range(local_experts):
        x_ref[e, 0, 0] = x[e * capacity : (e + 1) * capacity]
        dy_ref[e, 0, 0] = dy[e * capacity : (e + 1) * capacity]


def expert_kernel(n_alias, *refs):
    x_ref, dy_ref = refs[:2]
    parts = (refs[2:7], refs[7:12], refs[12:17])
    z_ref, dg_ref, du_ref, y_ref, dx_ref, wg, wu, wd, sems = refs[17 + n_alias :]
    local_experts, width, _ = wg.shape
    at = lax.axis_index("dp")
    size = width // 4
    places = (at, at + 1 - 2 * (at % 2), (at + 2) % 4, 3 - at, 3 - at)

    def copies(e):
        out = []
        for m, full in enumerate((wg, wu, wd)):
            for p in range(4):
                part = parts[m][p] if p < 3 else parts[m][3 + e]
                src = part.at[e] if p < 3 else part.at[0]
                where = pl.ds(pl.multiple_of(places[p] * size, size), size)
                dst = full.at[e, where, :] if m < 2 else full.at[e, :, where]
                out.append(pltpu.make_async_copy(src, dst, sems.at[e, m, p]))
        return out

    expert, chunk = pl.program_id(0), pl.program_id(1)

    @pl.when((expert == 0) & (chunk == 0))
    def _():
        for e in range(local_experts):
            for c in copies(e):
                c.start()

    for e in range(local_experts):

        @pl.when((expert == e) & (chunk == 0))
        def _(e=e):
            for c in copies(e):
                c.wait()

    x, dy = x_ref[0, 0], dy_ref[0, 0]
    gate = mm(x, wg[expert])
    up = mm(x, wu[expert])
    d_hidden = mm(dy, wd[expert], NT)
    sig = 1.0 / (1.0 + jnp.exp(-gate))
    silu = gate * sig
    z = (silu * up).astype(bf16)
    d_gate = (d_hidden * up * sig * (1.0 + gate * (1.0 - sig))).astype(bf16)
    d_up = (d_hidden * silu).astype(bf16)
    z_ref[0, 0] = z
    dg_ref[0, 0] = d_gate
    du_ref[0, 0] = d_up
    dx_ref[0] = (mm(d_gate, wg[expert], NT) + mm(d_up, wu[expert], NT)).astype(bf16)
    y_ref[0] = mm(z, wd[expert]).astype(bf16)


def sum_kernel(capacity, routing_ref, y_ref, dx_ref, mix_ref, da_ref):
    local_experts, _, _, width = y_ref.shape
    first = lax.axis_index("expert") * local_experts
    hit, weighted = picks_of(routing_ref[0].astype(f32), first, local_experts, capacity)
    da_ref[...] = mm(hit, dx_ref[...].reshape(local_experts * capacity, width)).astype(bf16)
    mix_ref[...] = mm(weighted, y_ref[...].reshape(local_experts * capacity, width)).astype(bf16)


def run_experts(tokens, cot, parts, capacity, batch_at, micro, earlier):
    blocks, rows, _ = tokens.shape
    width = cot[0][0].shape[3]
    local_experts, _, hidden = parts[0][0].shape
    flat = [p for group in parts for p in group]
    any_spec = pl.BlockSpec(memory_space=pl.ANY)
    params = pltpu.CompilerParams(vmem_limit_bytes=VMEM_LIMIT)
    slots = blocks * capacity
    picked_spec = pl.BlockSpec((local_experts, 1, 1, capacity, width), lambda b: (0, batch_at, b, 0, 0))
    picked = jax.ShapeDtypeStruct((local_experts, micro, blocks, capacity, width), bf16)
    x, dy = pl.pallas_call(
        functools.partial(pick_kernel, capacity, local_experts, len(earlier[:2])),
        grid=(blocks,),
        in_specs=[
            pl.BlockSpec((1, rows, tokens.shape[2]), lambda b: (b, 0, 0)),
        ]
        + [pl.BlockSpec((1, 1, rows // 2, width), lambda b, i=i: (b, i, 0, 0)) for _, i in cot]
        + [any_spec] * len(earlier[:2]),
        out_specs=[picked_spec] * 2,
        out_shape=[picked] * 2,
        input_output_aliases={3 + i: i for i in range(len(earlier[:2]))},
        compiler_params=params,
        cost_estimate=LIGHT,
    )(tokens, cot[0][0], cot[1][0], *[a.reshape(picked.shape) for a in earlier[:2]])
    x, dy = (a.reshape(local_experts, micro, slots, width) for a in (x, dy))
    chunk = slots // 2
    row_spec = pl.BlockSpec((1, 1, chunk, width), lambda e, i: (e, batch_at, i, 0))
    hid_spec = pl.BlockSpec((1, 1, chunk, hidden), lambda e, i: (e, batch_at, i, 0))
    out_spec = pl.BlockSpec((1, chunk, width), lambda e, i: (e, i, 0))
    hid = jax.ShapeDtypeStruct((local_experts, micro, slots, hidden), bf16)
    out = jax.ShapeDtypeStruct((local_experts, slots, width), bf16)
    z, dg, du, y, dx = pl.pallas_call(
        functools.partial(expert_kernel, len(earlier[2:])),
        grid=(local_experts, 2),
        in_specs=[row_spec, row_spec] + [any_spec] * (len(flat) + len(earlier[2:])),
        out_specs=[hid_spec] * 3 + [out_spec] * 2,
        out_shape=[hid] * 3 + [out] * 2,
        input_output_aliases={2 + len(flat) + i: i for i in range(len(earlier[2:]))},
        scratch_shapes=[
            pltpu.VMEM((local_experts, width, hidden), bf16),
            pltpu.VMEM((local_experts, width, hidden), bf16),
            pltpu.VMEM((local_experts, hidden, width), bf16),
            pltpu.SemaphoreType.DMA((local_experts, 3, 4)),
        ],
        compiler_params=params,
        cost_estimate=LIGHT,
    )(x, dy, *flat, *earlier[2:])
    y, dx = (a.reshape(local_experts, blocks, capacity, width) for a in (y, dx))
    part_spec = pl.BlockSpec((local_experts, 1, capacity, width), lambda b: (0, b, 0, 0))
    sums = jax.ShapeDtypeStruct((blocks * rows, width), bf16)
    sums_spec = pl.BlockSpec((rows, width), lambda b: (b, 0))
    mix, da = pl.pallas_call(
        functools.partial(sum_kernel, capacity),
        grid=(blocks,),
        in_specs=[
            pl.BlockSpec((1, rows, ROUTE_LANES), lambda b: (b, 0, width // ROUTE_LANES)),
            part_spec,
            part_spec,
        ],
        out_specs=[sums_spec] * 2,
        out_shape=[sums] * 2,
        compiler_params=params,
        cost_estimate=LIGHT,
    )(tokens, y, dx)
    return [x, dy, z, dg, du], mix, da


def slots_of(route_ids, gate_vals, ranking, capacity, experts):
    rows = route_ids.shape[0]
    pair_experts = route_ids.reshape(-1)
    earlier = (pair_experts[None, :] == pair_experts[:, None]) & (
        ranking[None, :] < ranking[:, None]
    )
    slot = jnp.sum(earlier.astype(jnp.int32), axis=1).reshape(rows, -1)
    kept = slot < capacity
    chosen = route_ids[:, :, None] == jnp.arange(experts, dtype=jnp.int32)[None, None, :]
    chosen = chosen & kept[:, :, None]
    slot_map = jnp.sum(jnp.where(chosen, slot[:, :, None] + 1, 0), axis=1).astype(f32) - 1.0
    weight_map = jnp.sum(jnp.where(chosen, gate_vals[:, :, None], 0.0), axis=1)
    return slot_map, weight_map


def swap(values, bit):
    return lax.ppermute(values, "dp", [(i, i ^ bit) for i in range(lax.axis_size("dp"))])


def dp_part(total, axis, bits, expert, count=1):
    size = total.shape[axis] // 4
    start, sizes = [expert, 0, 0], list(total.shape)
    start[axis] = (lax.axis_index("dp") ^ bits) * size
    sizes[0], sizes[axis] = count, size
    return lax.dynamic_slice(total, start, sizes)


def scatter_far(total, axis):
    return swap(dp_part(total, axis, 3, 0), 1), swap(dp_part(total, axis, 3, 1), 2), total


def scatter_add(pieces, axis):
    for_y, for_x, total = pieces
    near_x = dp_part(total, axis, 1, 0, 2).astype(f32) + jnp.pad(for_x.astype(f32), ((1, 0), (0, 0), (0, 0)))
    near_y = dp_part(total, axis, 2, 0, 2).astype(f32) + jnp.pad(for_y.astype(f32), ((0, 1), (0, 0), (0, 0)))
    return near_x.astype(bf16), near_y.astype(bf16), total


def scatter_near(pieces, axis):
    near_x, near_y, total = scatter_add(pieces, axis)
    return swap(near_x, 1), swap(near_y, 2), total


def scatter_sum(pieces, axis):
    by_x, by_y, total = pieces
    return dp_part(total, axis, 0, 0, total.shape[0]).astype(f32) + by_x.astype(f32) + by_y.astype(f32)


def body_plain(
    inputs,
    cotangent,
    membership,
    routes,
    gate_weights,
    pair_order,
    w_query,
    w_key,
    w_value,
    w_output,
    norm_gains,
    w_gate,
    w_up,
    w_down,
):
    micro = inputs.shape[0]
    rows = inputs.shape[2]
    width = inputs.shape[3]
    group_len = membership.shape[2]
    member = lax.axis_index("expert")
    blocks = lax.axis_size("expert")
    shards = blocks * lax.axis_size("dp")
    shard_at = lax.axis_index("dp") * blocks + member
    local_experts = w_gate.shape[0]
    experts = local_experts * blocks
    capacity = rows * TOPK // experts
    step_heads = max(1, 384 // rows)
    total = micro * rows
    q_part, k_part, v_part = w_query.shape[1], w_key.shape[1], w_value.shape[1]

    gain_len = norm_gains.shape[0]
    gain_shard = jnp.zeros((2048,), bf16).at[:gain_len].set(norm_gains).reshape(16, 128)
    gain_full = lax.all_gather(gain_shard, BOTH, axis=0, tiled=True)
    gains = gain_full.reshape(shards, 2048)[:, :gain_len].reshape(-1).astype(f32)
    gain_in = gains[:width]
    gain_mid = gains[width : 2 * width]
    gain_q = gains[2 * width : 2 * width + HD]
    gain_k = gains[2 * width + HD :]

    qkv_w = lax.all_gather(
        jnp.concatenate([w_query.T, w_key.T, w_value.T], axis=0), BOTH, axis=0, tiled=True
    )
    out_w = lax.all_gather(w_output, BOTH, axis=0, tiled=True)
    wg = lax.all_gather(w_gate, "dp", axis=1, tiled=True)
    wu = lax.all_gather(w_up, "dp", axis=1, tiled=True)
    wd = lax.all_gather(w_down, "dp", axis=2, tiled=True)

    slot_map, weight_map = jax.vmap(
        lambda r, g, o: slots_of(r, g, o, capacity, experts)
    )(routes[:, 0], gate_weights[:, 0], pair_order[:, 0, 0])
    routing = jnp.concatenate([slot_map, weight_map], axis=-1)
    routing = lax.all_gather(routing, "expert", axis=0, tiled=False)
    mine = member * local_experts
    slot_mine = lax.dynamic_slice_in_dim(routing, mine, local_experts, axis=3)
    weight_mine = lax.dynamic_slice_in_dim(routing, experts + mine, local_experts, axis=3)
    slot_mine = jnp.transpose(slot_mine, (1, 3, 0, 2))
    weight_mine = jnp.transpose(weight_mine, (1, 3, 0, 2))
    slot_ids = jnp.arange(capacity, dtype=f32)
    hit = slot_mine[:, :, :, None, :] == slot_ids[None, None, None, :, None]
    pick = hit.astype(bf16)
    weighted = jnp.where(hit, weight_mine[:, :, :, None, :], 0.0)
    slot_weight = jnp.sum(weighted, axis=-1)
    weighted = weighted.astype(bf16)

    key_index = jnp.arange(group_len, dtype=jnp.int32)
    start_row = member * rows
    segment = membership[:, 0]
    row_index = start_row + jnp.arange(rows, dtype=jnp.int32)
    seg_rows = lax.dynamic_slice_in_dim(segment, start_row, rows, axis=1)
    before = jnp.sum((segment[:, None, :] < seg_rows[:, :, None]).astype(jnp.int32), axis=2)
    position = jnp.where(seg_rows == 0, row_index[None], PROMPT + row_index[None] - before)
    allowed = (key_index[None, :, None] <= row_index[None, None, :]) & (
        (segment[:, :, None] == 0) | (segment[:, :, None] == seg_rows[:, None, :])
    )
    bias = jnp.tile(jnp.where(allowed, 0.0, MASKED).astype(f32), (1, 1, step_heads))
    frequency = ROPE_BASE ** (-(jnp.arange(HD // 2, dtype=f32) * 2.0 / HD))
    angles = position.astype(f32).reshape(total)[:, None] * frequency[None, :]
    cosine = jnp.cos(angles)[:, None, :]
    sine_part = jnp.sin(angles)[:, None, :]

    hidden = inputs[:, 0].astype(f32).reshape(total, width)
    scale_in = rms_scale(hidden)
    normed = (hidden * scale_in * gain_in).astype(bf16)
    proj = mm(normed, qkv_w, NT).reshape(total, shards, q_part + k_part + v_part)
    queries = proj[:, :, :q_part].reshape(total, H, HD)
    key_pre = proj[:, :, q_part : q_part + k_part].reshape(total, KVH, HD)
    value = proj[:, :, q_part + k_part :].reshape(total, KVH, HD).astype(bf16)
    scale_q = rms_scale(queries)
    scale_k = rms_scale(key_pre)
    q_low = rotate(queries * scale_q * (gain_q * (SCALE * LOG2E)), cosine, sine_part).astype(bf16)
    q_low = q_low.reshape(micro, rows, H * HD)
    k_low = rotate(key_pre * scale_k * gain_k, cosine, sine_part).astype(bf16)
    kv_own = jnp.concatenate([k_low, value], axis=-1).reshape(micro, rows, KVH * 2 * HD)
    kv_all = lax.all_gather(kv_own, "expert", axis=0, tiled=False)
    chunk = 256
    mixed = []
    for at in range(micro):
        mixed = run_forward(q_low, kv_all[:, at : at + 1], bias, step_heads, chunk, at, mixed)
    mixed, logs = mixed

    branch = mm(mixed.reshape(total, H * HD), out_w)
    middle = hidden + branch
    scale_mid = rms_scale(middle)
    routed = (middle * scale_mid * gain_mid).astype(bf16).reshape(micro, rows, width)
    middle = middle.reshape(micro, rows, width)
    scale_mid = scale_mid.reshape(micro, rows, 1)

    outputs, d_branches, d_middles = [], [], []
    acc_gate = acc_up = acc_down = 0.0
    grad_mid = 0.0
    slots = blocks * capacity
    for at in range(micro):
        d_out = lax.all_gather(cotangent[at, 0], "expert", axis=0, tiled=False)
        tokens = lax.all_gather(routed[at], "expert", axis=0, tiled=False)
        picked = jnp.einsum("ebst,btd->ebsd", pick[at], tokens, preferred_element_type=f32)
        picked = picked.astype(bf16).reshape(local_experts, slots, width)
        d_result = jnp.einsum("ebst,btd->ebsd", pick[at], d_out, preferred_element_type=f32)
        d_result = (d_result * slot_weight[at][..., None]).astype(bf16)
        d_result = d_result.reshape(local_experts, slots, width)
        gate_pre = jnp.einsum("erd,edf->erf", picked, wg, preferred_element_type=f32)
        up_pre = jnp.einsum("erd,edf->erf", picked, wu, preferred_element_type=f32)
        d_hidden = jnp.einsum("erd,efd->erf", d_result, wd, preferred_element_type=f32)
        sigmoid_g = jax.nn.sigmoid(gate_pre)
        silu_g = gate_pre * sigmoid_g
        hidden_low = (silu_g * up_pre).astype(bf16)
        d_gate = (d_hidden * up_pre * sigmoid_g * (1.0 + gate_pre * (1.0 - sigmoid_g))).astype(bf16)
        d_up = (d_hidden * silu_g).astype(bf16)
        d_rows = jnp.einsum("erf,edf->erd", d_gate, wg, preferred_element_type=f32)
        d_rows = d_rows + jnp.einsum("erf,edf->erd", d_up, wu, preferred_element_type=f32)
        d_rows = d_rows.astype(bf16).reshape(local_experts, blocks, capacity, width)
        d_part = jnp.einsum("ebst,ebsd->btd", pick[at], d_rows, preferred_element_type=f32)
        d_part = d_part.astype(bf16).reshape(group_len, width)
        d_routed = lax.psum_scatter(d_part, "expert", scatter_dimension=0, tiled=True).astype(f32)
        result = jnp.einsum("erf,efd->erd", hidden_low, wd, preferred_element_type=f32)
        result = result.astype(bf16).reshape(local_experts, blocks, capacity, width)
        part = jnp.einsum("ebst,ebsd->btd", weighted[at], result, preferred_element_type=f32)
        part = part.astype(bf16).reshape(group_len, width)
        expert_mix = lax.psum_scatter(part, "expert", scatter_dimension=0, tiled=True).astype(f32)
        outputs.append((middle[at] + expert_mix).astype(bf16))

        acc_down += jnp.einsum("erf,erd->efd", hidden_low, d_result, preferred_element_type=f32)
        acc_gate += jnp.einsum("erd,erf->edf", picked, d_gate, preferred_element_type=f32)
        acc_up += jnp.einsum("erd,erf->edf", picked, d_up, preferred_element_type=f32)

        d_mid_norm, mid_gain_grad = norm_back(d_routed, middle[at], scale_mid[at], gain_mid)
        grad_mid = grad_mid + mid_gain_grad
        d_middle = cotangent[at, 0].astype(f32) + d_mid_norm
        d_middles.append(d_middle)
        d_branches.append(d_middle.astype(bf16))

    grad_gate = lax.psum_scatter(acc_gate.astype(bf16), "dp", scatter_dimension=1, tiled=True)
    grad_up = lax.psum_scatter(acc_up.astype(bf16), "dp", scatter_dimension=1, tiled=True)
    grad_down = lax.psum_scatter(acc_down.astype(bf16), "dp", scatter_dimension=2, tiled=True)

    d_branch = jnp.concatenate(d_branches, axis=0)
    d_middle = jnp.concatenate(d_middles, axis=0)
    grad_output = mm(mixed.reshape(total, H * HD), d_branch, TN).astype(bf16)
    grad_output = lax.psum_scatter(grad_output, BOTH, scatter_dimension=0, tiled=True)
    d_mixed = mm(d_branch, out_w, NT).astype(bf16).reshape(micro, rows, H * HD)
    cos_rows = jnp.concatenate([cosine, cosine], axis=-1).reshape(micro, rows, HD)
    sine_rows = jnp.concatenate([-sine_part, sine_part], axis=-1).reshape(micro, rows, HD)
    q_raw = queries.reshape(micro, rows, H * HD)
    d_query, dkv_list, grad_qn = [], [], 0.0
    for at in range(micro):
        d_query, dkv_one, part = run_backward(
            q_low, kv_all[:, at : at + 1], bias, mixed, d_mixed, logs, q_raw, cos_rows, sine_rows,
            gain_q[None, :], step_heads, chunk, at, [d_query] if at else []
        )
        dkv_list.append(dkv_one)
        grad_qn += part[0]
    dkv_all = jnp.concatenate(dkv_list, axis=1)
    dkv = lax.psum_scatter(dkv_all, "expert", scatter_dimension=0, tiled=False)
    dkv = dkv.reshape(total, KVH, 2 * HD)
    d_key = rotate(dkv[:, :, :HD].astype(f32), cosine, -sine_part)
    d_key, grad_kn = norm_back(d_key, key_pre, scale_k, gain_k)
    d_proj = jnp.concatenate(
        [
            d_query.reshape(total, shards, q_part),
            d_key.astype(bf16).reshape(total, shards, k_part),
            dkv[:, :, HD:].reshape(total, shards, v_part),
        ],
        axis=-1,
    ).reshape(total, -1)
    grad_qkv = mm(d_proj, normed, TN).astype(bf16)
    grad_qkv = lax.psum_scatter(grad_qkv, BOTH, scatter_dimension=0, tiled=True).astype(f32)
    d_normed = mm(d_proj, qkv_w)
    d_in_norm, grad_in = norm_back(d_normed, hidden, scale_in, gain_in)
    input_grad = d_middle + d_in_norm

    gain_grads = jnp.concatenate([grad_in, grad_mid, grad_qn, grad_kn]).reshape(shards, gain_len)
    gain_grads = jnp.pad(gain_grads, ((0, 0), (0, 256 - gain_len % 256)))
    gain_all = lax.all_gather(gain_grads, BOTH, axis=0, tiled=False)
    grad_gains = jnp.sum(lax.dynamic_index_in_dim(gain_all, shard_at, axis=1, keepdims=False), axis=0)
    return (
        jnp.stack(outputs)[:, None],
        input_grad.reshape(micro, 1, rows, width),
        grad_qkv[:q_part].T,
        grad_qkv[q_part : q_part + k_part].T,
        grad_qkv[q_part + k_part :].T,
        grad_output.astype(f32),
        grad_gains[:gain_len],
        grad_gate.astype(f32),
        grad_up.astype(f32),
        grad_down.astype(f32),
    )


def body_fast(
    inputs,
    cotangent,
    membership,
    routes,
    gate_weights,
    pair_order,
    w_query,
    w_key,
    w_value,
    w_output,
    norm_gains,
    w_gate,
    w_up,
    w_down,
):
    micro = inputs.shape[0]
    rows = inputs.shape[2]
    width = inputs.shape[3]
    group_len = membership.shape[2]
    member = lax.axis_index("expert")
    blocks = lax.axis_size("expert")
    shards = blocks * lax.axis_size("dp")
    local_experts = w_gate.shape[0]
    experts = local_experts * blocks
    capacity = rows * TOPK // experts
    step_heads = max(1, 384 // rows)
    total = micro * rows
    q_part, k_part, v_part = w_query.shape[1], w_key.shape[1], w_value.shape[1]
    tie = lax.optimization_barrier

    slot_map, weight_map = jax.vmap(
        lambda r, g, o: slots_of(r, g, o, capacity, experts)
    )(routes[:, 0], gate_weights[:, 0], pair_order[:, 0, 0])
    weight_high = tie(weight_map.astype(bf16))
    weight_low = (weight_map - weight_high.astype(f32)).astype(bf16)

    def padded(values, lanes):
        return jnp.pad(values, ((0, 0), (0, 0), (0, lanes - experts)))

    routing = jnp.concatenate(
        [
            padded(slot_map.astype(bf16), 32),
            padded(weight_high, 32),
            padded(weight_low, ROUTE_LANES - 64),
        ],
        axis=-1,
    )

    gain_len = norm_gains.shape[0]
    gain_shard = jnp.pad(norm_gains[None], ((0, 15), (0, 256 - gain_len)))
    kv_w = jnp.concatenate([w_key.T, w_value.T], axis=0)
    q_w, kv_w, out_w, gain_full, cot_all = gather_rows(
        [w_query.T, kv_w, w_output, gain_shard, cotangent.reshape(total, width)], [(3, 0, 1, 2)], 1, (4,)
    )
    cot_all = cot_all.reshape(blocks, 2 * micro, rows // 2, width)
    q_w, w_gate = tie((q_w, w_gate))
    gains = gain_full.reshape(shards, 16, 256)[:, 0, :gain_len].reshape(-1).astype(f32)
    gain_in = gains[:width]
    gain_mid = gains[width : 2 * width]
    gain_q = gains[2 * width : 2 * width + HD]
    gain_k = gains[2 * width + HD :]

    key_index = jnp.arange(group_len, dtype=jnp.int32)
    start_row = member * rows
    segment = membership[:, 0]
    row_index = start_row + jnp.arange(rows, dtype=jnp.int32)
    seg_rows = lax.dynamic_slice_in_dim(segment, start_row, rows, axis=1)
    before = jnp.sum((segment[:, None, :] < seg_rows[:, :, None]).astype(jnp.int32), axis=2)
    position = jnp.where(seg_rows == 0, row_index[None], PROMPT + row_index[None] - before)
    allowed = (key_index[None, :, None] <= row_index[None, None, :]) & (
        (segment[:, :, None] == 0) | (segment[:, :, None] == seg_rows[:, None, :])
    )
    bias = jnp.tile(jnp.where(allowed, 0.0, MASKED).astype(f32), (1, 1, step_heads))
    frequency = ROPE_BASE ** (-(jnp.arange(HD // 2, dtype=f32) * 2.0 / HD))
    angles = position.astype(f32).reshape(total)[:, None] * frequency[None, :]
    cosine, sine = jnp.cos(angles), jnp.sin(angles)
    cosine = jnp.concatenate([cosine, cosine], axis=-1)
    sine = jnp.concatenate([-sine, sine], axis=-1)
    gain_q, gain_k = gain_q[None, :], gain_k[None, :]

    hidden = inputs[:, 0].astype(f32).reshape(total, width)
    scale_in = rms_scale(hidden)
    normed = (hidden * scale_in * gain_in).astype(bf16)
    q_low, q_raw, k_raw, kv_w, kv_0, kv_1 = run_project(
        normed, q_w, kv_w, cosine, sine, gain_q * (SCALE * LOG2E), gain_k, micro
    )
    q_low, q_raw = (a.reshape(micro, rows, H * HD) for a in (q_low, q_raw))
    gate_near = (swap(w_gate, 1), swap(w_gate, 2))
    kv_0, gate_near, w_up, w_down = tie((kv_0, gate_near, w_up, w_down))
    kv_0 = lax.all_gather(kv_0, "expert", axis=0, tiled=False)
    kv_1 = lax.all_gather(kv_1, "expert", axis=0, tiled=False)
    gate_far = (swap(gate_near[0][:1], 2), swap(gate_near[1][1:], 1))
    up_near = (swap(w_up, 1), swap(w_up, 2))
    chunk = 256

    def middle_of(mixed, at):
        part = hidden[at * rows : (at + 1) * rows]
        middle = part + mm(mixed[at], out_w)
        routed = (middle * rms_scale(middle) * gain_mid).astype(bf16)
        return middle, jnp.concatenate([routed, routing[at]], axis=-1)

    mixed, logs, shares = run_forward(q_low, kv_0[:, None], bias, step_heads, chunk, 0, [], True)
    mixed, up_near, gate_far = tie((mixed, up_near, gate_far))
    up_far = (swap(up_near[0][:1], 2), swap(up_near[1][1:], 1))
    middle_0, routed_0 = middle_of(mixed, 0)
    mixed, routed_0 = tie((mixed, routed_0))
    mixed, kv_1, up_far, w_down = tie((mixed, kv_1, up_far, w_down))
    down_near = (swap(w_down, 1), swap(w_down, 2))
    kv_all = [kv_0[:, None], kv_1[:, None]]
    mixed, logs, shares = run_forward(
        q_low, kv_all[1], bias, step_heads, chunk, 1, [mixed, logs, shares], True
    )
    mixed, down_near = tie((mixed, down_near))
    down_far = (swap(down_near[0][:1], 2), swap(down_near[1][1:], 1))
    middle_1, routed_1 = middle_of(mixed, 1)
    parts = [
        (w_gate, *gate_near, *gate_far),
        (w_up, *up_near, *up_far),
        (w_down, *down_near, *down_far),
    ]
    cots = [[(cot_all, 2 * b), (cot_all, 2 * b + 1)] for b in range(micro)]
    routed = [routed_0, routed_1]
    middle = jnp.stack([middle_0, middle_1])

    mix_parts, d_routeds = [], []
    kept = []
    for at in range(micro):
        tokens = lax.all_gather(routed[at], "expert", axis=0, tiled=False)
        kept, mix, d_part = run_experts(tokens, cots[at], parts, capacity, at, micro, kept)
        kept, d_part, mix, d_routeds = tie((kept, d_part, mix, d_routeds))
        mix_parts.append(mix)
        d_routed = lax.psum_scatter(d_part, "expert", scatter_dimension=0, tiled=True)
        d_routeds.append(d_routed)
    picked, d_result, hidden_low, d_gate, d_up = (
        a.reshape(local_experts, -1, a.shape[-1]) for a in kept
    )

    def weight_grad(rows_in, rows_out):
        return jnp.einsum("era,erb->eab", rows_in, rows_out, preferred_element_type=f32).astype(bf16)

    first = scatter_far(weight_grad(picked, d_gate), 1)
    second = scatter_far(weight_grad(picked, d_up), 1)
    first, hidden_low = tie((first, hidden_low))
    first = scatter_near(first, 1)
    third = weight_grad(hidden_low, d_result)
    d_routeds[-1], first, second, third, mix_parts[0] = tie(
        (d_routeds[-1], first, second, third, mix_parts[0])
    )
    second = scatter_near(second, 1)
    third = scatter_far(third, 2)
    d_mixed, d_middle, d_branch, grad_mid = run_middle_back(
        d_routeds, middle, cotangent[:, 0], gain_mid[None, :], out_w
    )
    d_mixed, d_branch, third = tie((d_mixed, d_branch, third))
    third = scatter_near(third, 2)
    d_mixed = d_mixed.reshape(micro, rows, H * HD)
    cos_rows, sine_rows = (a.reshape(micro, rows, HD) for a in (cosine, sine))
    def share(core):
        part = lax.dynamic_index_in_dim(shares, core, axis=0, keepdims=False)
        part = part.reshape(2, total, -1)
        return jnp.einsum("zta,td->zad", part, d_branch, preferred_element_type=f32).astype(bf16)

    core = member % 2
    pairs = [(i, i ^ 1) for i in range(blocks)]
    got = lax.ppermute(share(1 - core), "expert", pairs)
    mixes = [lax.psum_scatter(mix_parts[0], "expert", scatter_dimension=0, tiled=True)]

    def backward(at, earlier):
        d_query, dkv_one, part = run_backward(
            q_low, kv_all[at], bias, mixed, d_mixed, logs, q_raw, cos_rows, sine_rows, gain_q,
            step_heads, chunk, at, earlier
        )
        return d_query, dkv_one[:, 0], part

    d_query, dkv_0, gain_0 = backward(0, [])
    d_query, dkv_0, got, second = tie((d_query, dkv_0, got, second))
    dkv_0 = lax.psum_scatter(dkv_0, "expert", scatter_dimension=0, tiled=False)
    out_grad = tie(share(core))
    out_grad = (out_grad.astype(f32) + got.astype(f32)).astype(bf16)
    d_query, out_grad = tie((d_query, out_grad))
    out_grad = scatter_far(out_grad, 1)
    d_query, dkv_1, gain_1 = backward(1, [d_query])
    grad_qn = gain_0 + gain_1
    d_query, dkv_1, out_grad, mixes, third = tie((d_query, dkv_1, out_grad, mixes, third))
    dkv_1 = lax.psum_scatter(dkv_1, "expert", scatter_dimension=0, tiled=False)
    out_grad = scatter_add(out_grad, 1)
    out_grad, first, second, third, d_query = tie((out_grad, first, second, third, d_query))
    out_grad = (swap(out_grad[0], 1), swap(out_grad[1], 2), out_grad[2])
    out_grad = scatter_sum(out_grad, 1).astype(bf16).reshape(-1, width)
    d_query = d_query.reshape(total, H * HD)
    dkv = jnp.concatenate([dkv_0, dkv_1], axis=0)
    dkv = dkv.reshape(total, KVH * 2 * HD)
    mix_part, dkv = tie((mix_parts[1], dkv))
    mixes.append(lax.psum_scatter(mix_part, "expert", scatter_dimension=0, tiled=True))
    outputs = [(middle[at] + mixes[at].astype(f32)).astype(bf16) for at in range(micro)]
    expert_grads = [scatter_sum(first, 1), scatter_sum(second, 1), scatter_sum(third, 2)]
    d_normed = mm(d_query, q_w)
    dkv, out_grad, expert_grads, d_normed = tie((dkv, out_grad, expert_grads, d_normed))
    dkv, dkv_t, grad_kn = run_key_back(dkv, k_raw, cosine, sine, gain_k)
    d_normed = d_normed + mm(dkv, kv_w)
    grad_output = lax.psum_scatter(
        out_grad,
        "expert",
        scatter_dimension=0,
        tiled=True,
        axis_index_groups=[list(range(c, blocks, 2)) for c in range(2)],
    ).astype(f32)
    d_in_norm, grad_in = norm_back(d_normed, hidden, scale_in, gain_in)
    input_grad = d_middle + d_in_norm
    gain_grads = jnp.concatenate([grad_in, grad_mid[0], grad_qn[0], grad_kn[0]]).reshape(shards, gain_len)
    grad_query, grad_key, grad_value, grad_gains = reduce_rows(d_query, dkv_t, normed, 3, gain_grads)
    return (
        jnp.stack(outputs)[:, None],
        input_grad.reshape(micro, 1, rows, width),
        grad_query,
        grad_key,
        grad_value,
        grad_output,
        grad_gains[0, :gain_len],
        *expert_grads,
    )


def solution(mesh):
    fast = mesh.shape["dp"] == 4 and mesh.shape["expert"] == 8
    return jax.shard_map(
        body_fast if fast else body_plain,
        mesh=mesh,
        in_specs=(
            P(None, "dp", "expert", None),
            P(None, "dp", "expert", None),
            P(None, "dp", None),
            P(None, "dp", "expert", None),
            P(None, "dp", "expert", None),
            P(None, "dp", "expert", None),
            P(None, ("dp", "expert")),
            P(None, ("dp", "expert")),
            P(None, ("dp", "expert")),
            P(("dp", "expert"), None),
            P(("dp", "expert")),
            P("expert", "dp", None),
            P("expert", "dp", None),
            P("expert", None, "dp"),
        ),
        out_specs=(
            P(None, "dp", "expert", None),
            P(None, "dp", "expert", None),
            P(None, ("dp", "expert")),
            P(None, ("dp", "expert")),
            P(None, ("dp", "expert")),
            P(("dp", "expert"), None),
            P(("dp", "expert")),
            P("expert", "dp", None),
            P("expert", "dp", None),
            P("expert", None, "dp"),
        ),
        check_vma=False,
    )
```
